32 devices in a mesh: seq: 8 (over y, x, core), mp: 4 (over z).
Axes of the slice: x: 2, y: 2, z: 4, core: 2. Of those that a mesh axis runs over, the one named last changes fastest.
Arguments:
- tokens: bfloat16 [2, 4096, 1024], P(None, 'seq'), may hold values from -6 to 6
- cotangent: bfloat16 [2, 4096, 1024], P(None, 'seq'), may hold values from -6 to 6
- w_qkv: float32 [3, 1024, 1024], P(None, 'seq', 'mp'), may hold values from -0.1875 to 0.1875
- w_out: float32 [1024, 1024], P('mp', 'seq'), may hold values from -3 to 3
- w_up: float32 [1024, 4096], P('seq', 'mp'), may hold values from -0.1875 to 0.1875
- w_down: float32 [4096, 1024], P('mp', 'seq'), may hold values from -0.09375 to 0.09375
- norm_gains: float32 [2, 1024], P(None, ('seq', 'mp'))
- ssm_param: float32 [2, 16, 1024], P(None, None, ('seq', 'mp'))
- first_qkv: float32 [3, 1024, 1024], P(None, 'seq', 'mp'), may hold values from -32 to 32
- second_qkv: float32 [3, 1024, 1024], P(None, 'seq', 'mp'), may hold values from 2.048 to 8.192
- first_out: float32 [1024, 1024], P('mp', 'seq'), may hold values from -4 to 4
- second_out: float32 [1024, 1024], P('mp', 'seq'), may hold values from 0.032 to 0.128
- first_up: float32 [1024, 4096], P('seq', 'mp'), may hold values from -16 to 16
- second_up: float32 [1024, 4096], P('seq', 'mp'), may hold values from 0.73728 to 2.94912
- first_down: float32 [4096, 1024], P('mp', 'seq'), may hold values from -32 to 32
- second_down: float32 [4096, 1024], P('mp', 'seq'), may hold values from 2.94912 to 11.79648
- first_gain: float32 [2, 1024], P(None, ('seq', 'mp')), may hold values from -64 to 64
- second_gain: float32 [2, 1024], P(None, ('seq', 'mp')), may hold values from 8.192 to 32.768
- first_ssm: float32 [2, 16, 1024], P(None, None, ('seq', 'mp')), may hold values from -32 to 32
- second_ssm: float32 [2, 16, 1024], P(None, None, ('seq', 'mp')), may hold values from 2.048 to 8.192
Outputs:
- layer_out: bfloat16 [2, 4096, 1024], P(None, 'seq')
- input_grad: float32 [2, 4096, 1024], P(None, 'seq')
- new_qkv: float32 [3, 1024, 1024], P(None, 'seq', 'mp')
- next_first_qkv: float32 [3, 1024, 1024], P(None, 'seq', 'mp')
- next_second_qkv: float32 [3, 1024, 1024], P(None, 'seq', 'mp')
- new_out: float32 [1024, 1024], P('mp', 'seq')
- next_first_out: float32 [1024, 1024], P('mp', 'seq')
- next_second_out: float32 [1024, 1024], P('mp', 'seq')
- new_up: float32 [1024, 4096], P('seq', 'mp')
- next_first_up: float32 [1024, 4096], P('seq', 'mp')
- next_second_up: float32 [1024, 4096], P('seq', 'mp')
- new_down: float32 [4096, 1024], P('mp', 'seq')
- next_first_down: float32 [4096, 1024], P('mp', 'seq')
- next_second_down: float32 [4096, 1024], P('mp', 'seq')
- new_gains: float32 [2, 1024], P(None, ('seq', 'mp'))
- next_first_gain: float32 [2, 1024], P(None, ('seq', 'mp'))
- next_second_gain: float32 [1024], P(('seq', 'mp'))
- next_second_gain_two: float32 [1024], P(('seq', 'mp'))
- new_ssm: float32 [2, 16, 1024], P(None, None, ('seq', 'mp'))
- next_first_ssm: float32 [2, 16, 1024], P(None, None, ('seq', 'mp'))
- next_second_ssm: float32 [2, 16, 1024], P(None, None, ('seq', 'mp'))
- lamb_norms: float32 [2, 10], replicated
The draws below stay inside these ranges and needn't reach their ends.
All inputs are finite; a program needn't handle non-finite values.
Results may differ from the reference program's by a relative error of at most 0.035.
Values may be sent and summed in bfloat16 or wider, within the bound.
No kernel may reach another device: no remote copies, remote signals or barrier semaphores. Data moves between devices by JAX's collectives and lax.ppermute only.
A program may use at most 128 MiB of HBM per device.

```python
import math
import jax
import jax.numpy as jnp
from jax import lax

D = 1024
HEADS = 8
HD = 128
FF = 4096
STATES = 16
BLK = 512
SEQS = 2
STEP = 10
LENGTH = 4096


def draw_norm_gains(key, part):
    key = jax.random.fold_in(key, 5)
    base_level = 0.6
    rise_span = 1.2
    ramp_line = base_level + rise_span * lax.iota(jnp.float32, D) / D
    jitter = jax.random.uniform(key, (2, D), jnp.float32, 0.8, 1.2)
    return ramp_line[None, :] * jitter


def draw_ssm_param(key, part):
    key = jax.random.fold_in(key, 9)
    coef_key, rate_key = jax.random.split(key)
    coefficients = jax.random.normal(coef_key, (STATES, D), jnp.float32) * STATES ** (-0.5)
    slowest = math.log(0.3 / LENGTH)
    fastest = math.log(0.08)
    log_rates = jax.random.uniform(rate_key, (STATES, D), jnp.float32, slowest, fastest)
    return jnp.stack([coefficients, log_rates])


def block_levels(stream_key, shape, pieces, least, high):
    loudness = 1.0
    for position, blocks in pieces:
        steps = jax.random.uniform(jax.random.fold_in(jax.random.fold_in(stream_key, 6), position), (blocks,), jnp.float32, least / len(pieces), high / len(pieces))
        loudness = loudness * jnp.repeat(jnp.exp(steps), shape[position] // blocks).reshape((-1,) + (1,) * (len(shape) - 1 - position))
    return loudness


def normal_values(stream_key, extent, scale, bound, cuts=(), kind=jnp.bfloat16):
    drawn = jax.random.normal(stream_key, extent, jnp.float32) * scale
    if len(cuts) > 0:
        drawn = block_levels(stream_key, extent, cuts, -0.22, 0.18) * drawn
    return jnp.clip(drawn, min=-bound, max=bound).astype(kind)


def setup_inputs(seed: int = 0) -> dict:
    splits = jax.random.split(jax.random.key(seed), 21)
    return {
        "tokens": normal_values(splits[0], (SEQS, LENGTH, D), 1.0, 6.0, ((1, 8),)),
        "cotangent": normal_values(splits[1], (SEQS, LENGTH, D), 1.0, 6.0, ((1, 8),)),
        "w_qkv": normal_values(splits[2], (3, D, D), D ** -0.5, 0.1875, ((1, 8), (2, 4)), jnp.float32),
        "w_out": normal_values(splits[3], (D, D), (2 * D // BLK) ** -0.5, 3.0, ((0, 4), (1, 8)), jnp.float32),
        "w_up": normal_values(splits[4], (D, FF), D ** -0.5, 0.1875, ((0, 8), (1, 4)), jnp.float32),
        "w_down": normal_values(splits[5], (FF, D), FF ** -0.5, 0.09375, ((0, 4), (1, 8)), jnp.float32),
        "norm_gains": draw_norm_gains(jax.random.fold_in(splits[20], 71), 0),
        "ssm_param": draw_ssm_param(jax.random.fold_in(splits[20], 71), 0),
        "first_qkv": normal_values(splits[8], (3, D, D), (0.055 * (SEQS * LENGTH) ** 0.5), 32.0, ((1, 8), (2, 4)), jnp.float32),
        "second_qkv": jnp.clip(jnp.exp(math.log(8.192) - 1.3862944 * jax.random.uniform(splits[9], (3, D, D), jnp.float32) ** block_levels(splits[9], (3, D, D), ((1, 8), (2, 4)), -0.2, 0.2)), 2.048, 8.192),
        "first_out": normal_values(splits[10], (D, D), (0.11 * (2 * SEQS * LENGTH // BLK) ** 0.5), 4.0, ((0, 4), (1, 8)), jnp.float32),
        "second_out": jnp.clip(jnp.exp(math.log(0.128) - 1.3862944 * jax.random.uniform(splits[11], (D, D), jnp.float32) ** block_levels(splits[11], (D, D), ((0, 4), (1, 8)), -0.2, 0.2)), 0.032, 0.128),
        "first_up": normal_values(splits[12], (D, FF), (0.033 * (SEQS * LENGTH) ** 0.5), 16.0, ((0, 8), (1, 4)), jnp.float32),
        "second_up": jnp.clip(jnp.exp(math.log(2.94912) - 1.3862944 * jax.random.uniform(splits[13], (D, FF), jnp.float32) ** block_levels(splits[13], (D, FF), ((0, 8), (1, 4)), -0.2, 0.2)), 0.73728, 2.94912),
        "first_down": normal_values(splits[14], (FF, D), (0.066 * (SEQS * LENGTH) ** 0.5), 32.0, ((0, 4), (1, 8)), jnp.float32),
        "second_down": jnp.clip(jnp.exp(math.log(11.79648) - 1.3862944 * jax.random.uniform(splits[15], (FF, D), jnp.float32) ** block_levels(splits[15], (FF, D), ((0, 4), (1, 8)), -0.2, 0.2)), 2.94912, 11.79648),
        "first_gain": normal_values(splits[16], (2, D), (0.11 * (SEQS * LENGTH) ** 0.5), 64.0, ((1, 32),), jnp.float32),
        "second_gain": jnp.clip(jnp.exp(math.log(32.768) - 1.3862944 * jax.random.uniform(splits[17], (2, D), jnp.float32) ** block_levels(splits[17], (2, D), ((1, 32),), -0.2, 0.2)), 8.192, 32.768),
        "first_ssm": normal_values(splits[18], (2, STATES, D), (0.055 * (SEQS * LENGTH) ** 0.5), 32.0, ((2, 32),), jnp.float32),
        "second_ssm": jnp.clip(jnp.exp(math.log(8.192) - 1.3862944 * jax.random.uniform(splits[19], (2, STATES, D), jnp.float32) ** block_levels(splits[19], (2, STATES, D), ((2, 32),), -0.2, 0.2)), 2.048, 8.192),
    }


@jax.custom_vjp
def low(v):
    return lax.optimization_barrier(v.astype(jnp.bfloat16)).astype(jnp.float32)

@jax.custom_vjp
def low_back(v):
    return v

def low_keep(v):
    return (low(v), None)

def low_pass(kept, grad):
    return (grad,)

def back_keep(v):
    return (v, None)

def back_low(kept, grad):
    return (low(grad),)
low.defvjp(low_keep, low_pass)
low_back.defvjp(back_keep, back_low)
norm_eps = 1e-05
beta_first = 0.9
beta_second = 0.999
lamb_eps = 1e-06
weight_decay = 0.01
learn_rate = 0.5
highest = lax.Precision.HIGHEST

def layer_norm(values, gain_row):
    centred = values - lax.optimization_barrier(jnp.mean(values, axis=-1, keepdims=True))
    spread = lax.optimization_barrier(jnp.mean(centred * centred, axis=-1, keepdims=True))
    return centred * lax.rsqrt(spread + norm_eps) * gain_row

def ssm_kernel(ssm_param):
    positions = jnp.arange(LENGTH).astype(ssm_param.dtype)
    decay_rate = jnp.exp(ssm_param[1])
    scaled = ssm_param[0] * jnp.sqrt(2.0 * decay_rate)

    def add_state(kernel_sum, state_pair):
        scaled_row, rate_row = state_pair
        return (kernel_sum + scaled_row[None, :] * jnp.exp(-positions[:, None] * rate_row[None, :]), None)
    kernel_sum, unused = lax.scan(add_state, jnp.zeros((LENGTH, D), ssm_param.dtype), (scaled, decay_rate))
    return kernel_sum

def causal_conv(signal, spectrum):
    product = jnp.fft.rfft(signal, n=2 * LENGTH, axis=0) * spectrum
    return jnp.fft.irfft(product, n=2 * LENGTH, axis=0)[:LENGTH]

def attend(query_rows, key_rows, value_rows):
    block_count = LENGTH // BLK
    score_scale = HD ** (-0.5)
    causal_mask = jnp.arange(BLK)[:, None] >= jnp.arange(BLK)[None, :]

    def one_block(block_parts):
        query_block, key_block, value_block = [part_item.reshape(BLK, HEADS, HD) for part_item in block_parts]
        scores = jnp.einsum('qhd,khd->hqk', query_block, key_block, precision=highest) * score_scale
        scores = low_back(scores)
        scores = jnp.where(causal_mask[None], scores, -1e+30)
        row_top = lax.optimization_barrier(jnp.max(scores, axis=-1, keepdims=True))
        shifted = jnp.exp(scores - row_top)
        soft_weights = low(shifted / lax.optimization_barrier(jnp.sum(shifted, axis=-1, keepdims=True)))
        return jnp.einsum('hqk,khd->qhd', soft_weights, value_block, precision=highest).reshape(BLK, D)
    stacked = tuple((part_item.reshape(block_count, BLK, D) for part_item in (query_rows, key_rows, value_rows)))
    return lax.map(jax.checkpoint(one_block), stacked).reshape(LENGTH, D)

def one_sequence(inputs, query_w, key_w, value_w, out_w, up_w, down_w, norm_gains, spectrum):
    normed_one = layer_norm(inputs, norm_gains[0])
    normed_low = low(normed_one)
    conv_in = low_back(normed_low)
    context = low(low_back(causal_conv(conv_in, spectrum)))
    query_rows = low(low_back(jnp.dot(normed_low, query_w, precision=highest)))
    key_rows = low(low_back(jnp.dot(context, key_w, precision=highest)))
    value_rows = low(low_back(jnp.dot(context, value_w, precision=highest)))
    attended = low(low_back(attend(query_rows, key_rows, value_rows)))
    middle = inputs + jnp.dot(attended, out_w, precision=highest)
    normed_two = low(layer_norm(middle, norm_gains[1]))
    hidden_pre = low_back(jnp.dot(normed_two, up_w, precision=highest))
    activated = low(jax.nn.gelu(hidden_pre, approximate=False))
    return middle + jnp.dot(activated, down_w, precision=highest)

def forward(inputs, w_qkv, w_out, w_up, w_down, norm_gains, ssm_param):
    spectrum = jnp.fft.rfft(ssm_kernel(ssm_param), n=2 * LENGTH, axis=0)
    query_w = low(w_qkv[0])
    key_w = low(w_qkv[1])
    value_w = low(w_qkv[2])
    out_w = low(w_out)
    up_w = low(w_up)
    down_w = low(w_down)
    layers = []
    for seq_index in range(SEQS):
        layers.append(one_sequence(inputs[seq_index], query_w, key_w, value_w, out_w, up_w, down_w, norm_gains, spectrum))
    return jnp.stack(layers)

def lamb(weight, grad_item, first_old, second_old, stacked):
    first_new = beta_first * first_old + (1.0 - beta_first) * grad_item
    second_new = beta_second * second_old + (1.0 - beta_second) * grad_item * grad_item
    direction = first_new / (1.0 - beta_first ** STEP) / (jnp.sqrt(second_new / (1.0 - beta_second ** STEP)) + lamb_eps) + weight_decay * weight
    if stacked:
        sum_axes = tuple(range(1, weight.ndim))
        weight_norm = jnp.sqrt(lax.optimization_barrier(jnp.sum(weight * weight, axis=sum_axes)))
        update_norm = jnp.sqrt(lax.optimization_barrier(jnp.sum(direction * direction, axis=sum_axes)))
    else:
        weight_norm = jnp.sqrt(jnp.sum(weight * weight)).reshape(1)
        update_norm = jnp.sqrt(jnp.sum(direction * direction)).reshape(1)
    ratio = (weight_norm / update_norm).reshape((-1,) + (1,) * (weight.ndim - 1))
    return (weight - learn_rate * ratio * direction, first_new, second_new, weight_norm, update_norm)

def reference(tokens, cotangent, w_qkv, w_out, w_up, w_down, norm_gains, ssm_param, first_qkv, second_qkv, first_out, second_out, first_up, second_up, first_down, second_down, first_gain, second_gain, first_ssm, second_ssm):
    masters = (w_qkv, w_out, w_up, w_down, norm_gains, ssm_param)
    layer_value, pull_back = jax.vjp(forward, tokens.astype(jnp.float32), *masters)
    grads = pull_back(cotangent.astype(jnp.float32))
    firsts = (first_qkv, first_out, first_up, first_down, first_gain, first_ssm)
    seconds = (second_qkv, second_out, second_up, second_down, second_gain, second_ssm)
    stacked_flags = (True, False, False, False, True, True)
    results = []
    weight_norms = []
    update_norms = []
    for item_index in range(6):
        new_weight, first_new, second_new, weight_norm, update_norm = lamb(masters[item_index], grads[item_index + 1], firsts[item_index], seconds[item_index], stacked_flags[item_index])
        results.append((new_weight, first_new, second_new))
        weight_norms.append(weight_norm)
        update_norms.append(update_norm)
    lamb_norms = jnp.stack([jnp.concatenate(weight_norms), jnp.concatenate(update_norms)])
    return (layer_value.astype(jnp.bfloat16), grads[0], results[0][0], results[0][1], results[0][2], results[1][0], results[1][1], results[1][2], results[2][0], results[2][1], results[2][2], results[3][0], results[3][1], results[3][2], results[4][0], results[4][1], results[4][2][0], results[4][2][1], results[5][0], results[5][1], results[5][2], lamb_norms)
```

```python
import functools
import math

import jax
import jax.numpy as jnp
from jax import lax
from jax.experimental import pallas as pl
from jax.experimental.pallas import tpu as pltpu
from jax.sharding import Mesh
from jax.sharding import PartitionSpec as P

HD = 128
HEADS = 8
BLK = 512
STEP = 10
SEQS = 2
LANES = 128
SUBS = 8

norm_eps = 1e-05
beta_first = 0.9
beta_second = 0.999
lamb_eps = 1e-06
weight_decay = 0.01
learn_rate = 0.5
score_scale = HD ** (-0.5)

f32 = jnp.float32
bf16 = jnp.bfloat16
VMEM_BYTES = 56 * 1024 * 1024

ALL = ("sh", "sl", "mb", "mq", "ml")
COPIES = ("sh", "mb", "mq")
TEAM = ("sl", "ml")


def dot(left, right):
    return lax.dot_general(left, right, (((1,), (0,)), ((), ())), preferred_element_type=f32)


def dot_t(left, right):
    return lax.dot_general(left, right, (((1,), (1,)), ((), ())), preferred_element_type=f32)


def normalise(values):
    centred = values - jnp.mean(values, axis=-1, keepdims=True)
    inverse = lax.rsqrt(jnp.mean(centred * centred, axis=-1, keepdims=True) + norm_eps)
    return centred * inverse, inverse


def normalise_back(unit, inverse, grad_unit):
    mean_one = jnp.mean(grad_unit, axis=-1, keepdims=True)
    mean_two = jnp.mean(grad_unit * unit, axis=-1, keepdims=True)
    return inverse * (grad_unit - mean_one - unit * mean_two)


def sub_index():
    return lax.broadcasted_iota(jnp.int32, (SUBS, LANES), 0)


def spread(row):
    return jnp.broadcast_to(row, (SUBS, LANES))


def lane_tile(index):
    return slice(index * LANES, (index + 1) * LANES)


def no_state(tiles):
    rows = tiles[0, :SUBS, :]
    return rows - rows


def fill_tiles(scratch, ref, start):
    for tile in range(scratch.shape[0]):
        lanes = pl.ds(pl.multiple_of(start + tile * LANES, LANES), LANES)
        scratch[tile] = ref[:, lanes].astype(f32)


def norm_kernel(place, x_ref, gain_ref, logr_ref, normed_ref, ends_ref, total_ref, u_tiles):
    unit, unused = normalise(x_ref[...].astype(f32))
    normed_ref[...] = (unit * gain_ref[...]).astype(bf16)
    tiles, length, unused = u_tiles.shape
    states = logr_ref.shape[0]
    span = length // SUBS
    fill_tiles(u_tiles, normed_ref, place[0] * (tiles * LANES))
    left = ((SUBS - 1 - sub_index()) * span).astype(f32)
    for tile in range(tiles):
        rate = jnp.exp(logr_ref[:, lane_tile(tile)])
        decay = jnp.exp(-rate)
        decays = [spread(decay[n : n + 1]) for n in range(states)]

        def step(i, held):
            u = u_tiles[tile, pl.ds(i, SUBS, stride=span), :]
            return tuple(d * h + u for d, h in zip(decays, held))

        zero = no_state(u_tiles)
        held = lax.fori_loop(0, span, step, (zero,) * states, unroll=4)
        for n in range(states):
            ends_ref[n, :, lane_tile(tile)] = held[n]
            total_ref[n : n + 1, lane_tile(tile)] = jnp.sum(
                held[n] * jnp.exp(-left * rate[n : n + 1]), axis=0, keepdims=True
            )


def context_kernel(
    place, normed_ref, ends_ref, all_ref, logr_ref, coef_ref, context_ref, u_tiles, y_tiles
):
    tiles, length, unused = u_tiles.shape
    states = logr_ref.shape[0]
    span = length // SUBS
    fill_tiles(u_tiles, normed_ref, place[0] * (tiles * LANES))
    index = sub_index()
    before = (index * span).astype(f32)
    for tile in range(tiles):
        rate = jnp.exp(logr_ref[:, lane_tile(tile)])
        decay = jnp.exp(-rate)
        scale = coef_ref[:, lane_tile(tile)] * jnp.sqrt(2.0 * rate)
        incoming = jnp.zeros((states, LANES), f32)
        for j in range(all_ref.shape[0]):
            gap = place[1] - 1 - j
            distance = (jnp.maximum(gap, 0) * length).astype(f32)
            term = jnp.exp(-distance * rate) * all_ref[j, :, lane_tile(tile)]
            incoming = incoming + jnp.where(gap >= 0, term, 0.0)
        starts = []
        for n in range(states):
            row = rate[n : n + 1]
            run = ends_ref[n, :, lane_tile(tile)]
            for d in (1, 2, 4):
                moved = jnp.exp(-(d * span) * row) * pltpu.roll(run, d, 0)
                run = run + jnp.where(index >= d, moved, 0.0)
            run = jnp.where(index >= 1, pltpu.roll(run, 1, 0), 0.0)
            starts.append(run + jnp.exp(-before * row) * incoming[n : n + 1])
        decays = [spread(decay[n : n + 1]) for n in range(states)]
        scales = [spread(scale[n : n + 1]) for n in range(states)]

        def step(i, held):
            u = u_tiles[tile, pl.ds(i, SUBS, stride=span), :]
            held = tuple(d * h + u for d, h in zip(decays, held))
            parts = [s * h for s, h in zip(scales, held)]
            while len(parts) > 1:
                parts = [a + b for a, b in zip(parts[::2], parts[1::2])]
            y_tiles[tile, pl.ds(i, SUBS, stride=span), :] = parts[0]
            return held

        lax.fori_loop(0, span, step, tuple(starts), unroll=2)
        context_ref[:, lane_tile(tile)] = y_tiles[tile].astype(bf16)


def masked_scores(q, k):
    scores = dot_t(q, k) * score_scale
    rows = lax.broadcasted_iota(jnp.int32, scores.shape, 0)
    cols = lax.broadcasted_iota(jnp.int32, scores.shape, 1)
    return jnp.where(rows >= cols, scores, -1e30)


def probabilities(q, k):
    scores = masked_scores(q, k)
    shifted = jnp.exp(scores - jnp.max(scores, axis=-1, keepdims=True))
    return shifted / jnp.sum(shifted, axis=-1, keepdims=True)


def whole_rows(block):
    return block.reshape(block.shape[0] * block.shape[1], block.shape[2])


def attend_kernel(team, place, normed_ref, *refs):
    pieces, (w_ref, context_ref, part_ref, kept_ref, total) = refs[:team], refs[team:]
    z = pl.program_id(0)
    width = pieces[0].shape[1]

    @pl.when(z == 0)
    def start():
        total[...] = jnp.zeros_like(total)
        for k in range(team):
            lanes = pl.ds(pl.multiple_of((place[0] ^ k) * width, LANES), width)
            context_ref[:, lanes] = pieces[k][...]

    weights = whole_rows(w_ref[:, 0])
    q = dot(normed_ref[...], weights[:, :HD]).astype(bf16)
    kv = dot(context_ref[...], weights[:, HD : 3 * HD]).astype(bf16)
    k, v = kv[:, :HD], kv[:, HD:]
    probs = probabilities(q, k).astype(bf16)
    attended = dot(probs, v).astype(bf16)
    kept_ref[0, :, :HD] = q
    kept_ref[0, :, HD : 3 * HD] = kv
    kept_ref[0, :, 3 * HD :] = attended
    total[...] += dot_t(attended, weights[:, 3 * HD :])

    @pl.when(z == pl.num_programs(0) - 1)
    def finish():
        part_ref[...] = total[...].astype(bf16)


def feed_kernel(team, x_ref, cot_ref, gain_ref, *refs):
    parts = refs[:team]
    (
        up_ref,
        down_ref,
        middle_ref,
        out_ref,
        two_ref,
        grad_up_ref,
        grad_down_ref,
        normed,
        normed_t,
        cot_t,
        out_total,
        two_total,
    ) = refs[team:]
    z = pl.program_id(0)

    @pl.when(z == 0)
    def start():
        attn = parts[0][...].astype(f32)
        for part in parts[1:]:
            attn = attn + part[...].astype(f32)
        middle = x_ref[...].astype(f32) + attn
        middle_ref[...] = middle
        unit, unused = normalise(middle)
        low = (unit * gain_ref[...]).astype(bf16)
        normed[...] = low
        normed_t[...] = low.T
        cot_t[...] = cot_ref[...].T
        out_total[...] = jnp.zeros_like(out_total)
        two_total[...] = jnp.zeros_like(two_total)

    up = whole_rows(up_ref[:, 0])
    down = whole_rows(down_ref[:, 0])
    hidden = dot(normed[...], up)
    grad_act = dot(cot_ref[...], down)
    cdf = 0.5 * (1.0 + lax.erf(hidden * math.sqrt(0.5)))
    activated = (hidden * cdf).astype(bf16)
    slope = cdf + hidden * jnp.exp(-0.5 * hidden * hidden) * (1.0 / math.sqrt(2.0 * math.pi))
    grad_pre = (grad_act * slope).astype(bf16)
    out_total[...] += dot_t(activated, down)
    two_total[...] += dot_t(grad_pre, up)
    shape = grad_up_ref[:, 0].shape
    grad_up_ref[:, 0] = dot(normed_t[...], grad_pre).astype(bf16).reshape(shape)
    grad_down_ref[:, 0] = dot(cot_t[...], activated).astype(bf16).reshape(shape)

    @pl.when(z == pl.num_programs(0) - 1)
    def finish():
        out_ref[...] = out_total[...].astype(bf16)
        two_ref[...] = two_total[...].astype(bf16)


def attend_back_kernel(team, place, middle_ref, gain_ref, cot_ref, *refs):
    parts = refs[:team]
    normed_ref, context_ref, kept_ref, w_ref, middle_grad_ref, gain_grad_ref, grad_w_ref, one_ref = refs[
        team : team + 8
    ]
    pieces = refs[team + 8 : 2 * team + 8]
    low, low_t, normed_t, context_t, one_total, context_total = refs[2 * team + 8 :]
    z = pl.program_id(0)
    own_rows = middle_ref.shape[0] // team

    @pl.when(z == 0)
    def start():
        grad_two = parts[0][...].astype(f32)
        for part in parts[1:]:
            grad_two = grad_two + part[...].astype(f32)
        unit, inverse = normalise(middle_ref[...])
        grad_gain = grad_two * unit
        rows = lax.broadcasted_iota(jnp.int32, grad_gain.shape, 0)
        first = place[0] * own_rows
        mine = (rows >= first) & (rows < first + own_rows)
        gain_grad_ref[...] = jnp.sum(jnp.where(mine, grad_gain, 0.0), axis=0, keepdims=True)
        grad = cot_ref[...].astype(f32) + normalise_back(unit, inverse, grad_two * gain_ref[...])
        middle_grad_ref[...] = grad
        low[...] = grad.astype(bf16)
        low_t[...] = low[...].T
        normed_t[...] = normed_ref[...].T
        context_t[...] = context_ref[...].T
        one_total[...] = jnp.zeros_like(one_total)
        context_total[...] = jnp.zeros_like(context_total)

    weights = whole_rows(w_ref[:, 0])
    q, k, v = kept_ref[0, :, :HD], kept_ref[0, :, HD : 2 * HD], kept_ref[0, :, 2 * HD : 3 * HD]
    attended = kept_ref[0, :, 3 * HD :]
    grad_attended = dot(low[...], weights[:, 3 * HD :]).astype(bf16)
    probs = probabilities(q, k)
    grad_probs = dot_t(grad_attended, v)
    inner = jnp.sum(grad_probs * probs, axis=-1, keepdims=True)
    grad_scores = (probs * (grad_probs - inner)).astype(bf16)
    grad_q = (dot(grad_scores, k) * score_scale).astype(bf16)
    grad_k = (dot(grad_scores.T, q) * score_scale).astype(bf16)
    grad_v = dot(probs.astype(bf16).T, grad_attended).astype(bf16)
    grad_kv = jnp.concatenate([grad_k, grad_v], axis=1)
    one_total[...] += dot_t(grad_q, weights[:, :HD])
    context_total[...] += dot_t(grad_kv, weights[:, HD : 3 * HD])
    shape = grad_w_ref.shape
    shape = (shape[0], shape[2])
    grad_w_ref[:, 0, :, :HD] = dot(normed_t[...], grad_q).astype(bf16).reshape(*shape, HD)
    grad_w_ref[:, 0, :, HD : 3 * HD] = dot(context_t[...], grad_kv).astype(bf16).reshape(*shape, 2 * HD)
    grad_w_ref[:, 0, :, 3 * HD :] = dot(low_t[...], attended).astype(bf16).reshape(*shape, HD)

    @pl.when(z == pl.num_programs(0) - 1)
    def finish():
        one_ref[...] = one_total[...]
        width = pieces[0].shape[1]
        for k in range(team):
            lanes = pl.ds(pl.multiple_of((place[0] ^ k) * width, LANES), width)
            pieces[k][...] = context_total[:, lanes].astype(bf16)


def adjoint_kernel(team, logr_ref, *refs):
    parts = refs[:team]
    grad_ref, ends_ref, total_ref, g_tiles = refs[team:]
    grad = parts[0][...].astype(f32)
    for part in parts[1:]:
        grad = grad + part[...].astype(f32)
    grad_ref[...] = grad.astype(bf16)
    tiles, length, unused = g_tiles.shape
    states = logr_ref.shape[0]
    span = length // SUBS
    fill_tiles(g_tiles, grad_ref, 0)
    before = (sub_index() * span).astype(f32)
    for tile in range(tiles):
        rate = jnp.exp(logr_ref[:, lane_tile(tile)])
        decay = jnp.exp(-rate)
        decays = [spread(decay[n : n + 1]) for n in range(states)]

        def step(i, held):
            g = g_tiles[tile, pl.ds(span - 1 - i, SUBS, stride=span), :]
            later = []
            for d, (b, w) in zip(decays, held):
                shrunk = d * b
                later.append((g + shrunk, d * w + shrunk))
            return tuple(later)

        zero = no_state(g_tiles)
        held = lax.fori_loop(0, span, step, ((zero, zero),) * states, unroll=2)
        for n in range(states):
            b, w = held[n]
            ends_ref[0, n, :, lane_tile(tile)] = b
            ends_ref[1, n, :, lane_tile(tile)] = w
            shrink = jnp.exp(-before * rate[n : n + 1])
            total_ref[0, n : n + 1, lane_tile(tile)] = jnp.sum(shrink * b, axis=0, keepdims=True)
            total_ref[1, n : n + 1, lane_tile(tile)] = jnp.sum(
                shrink * (w + before * b), axis=0, keepdims=True
            )


def context_back_kernel(
    team, place, grad_ref, normed_ref, ends_ref, all_ref, logr_ref, coef_ref, one_ref, *refs
):
    pieces = refs[:team]
    grad_ssm_ref, u_tiles, g_tiles, y_tiles, full = refs[team:]
    tiles, length, unused = u_tiles.shape
    states = logr_ref.shape[0]
    span = length // SUBS
    width = tiles * LANES
    fill_tiles(u_tiles, normed_ref, place[0] * width)
    fill_tiles(g_tiles, grad_ref, 0)
    index = sub_index()
    after = ((SUBS - 1 - index) * span).astype(f32)
    full[...] = one_ref[...]
    group = 8
    for tile in range(tiles):
        lanes = lane_tile(tile)
        rate = jnp.exp(logr_ref[:, lanes])
        decay = jnp.exp(-rate)
        root = jnp.sqrt(2.0 * rate)
        scale = coef_ref[:, lanes] * root
        in_b = jnp.zeros((states, LANES), f32)
        in_w = jnp.zeros((states, LANES), f32)
        for j in range(all_ref.shape[0]):
            gap = j - place[1] - 1
            distance = (jnp.maximum(gap, 0) * length).astype(f32)
            shrink = jnp.exp(-distance * rate)
            b, w = all_ref[j, 0, :, lanes], all_ref[j, 1, :, lanes]
            in_b = in_b + jnp.where(gap >= 0, shrink * b, 0.0)
            in_w = in_w + jnp.where(gap >= 0, shrink * (w + distance * b), 0.0)
        for first in range(0, states, group):
            chosen = range(first, first + group)
            starts = []
            for n in chosen:
                row = rate[n : n + 1]
                b, w = ends_ref[0, n, :, lanes], ends_ref[1, n, :, lanes]
                for d in (1, 2, 4):
                    shrink = jnp.exp(-(d * span) * row)
                    next_b = pltpu.roll(b, SUBS - d, 0)
                    next_w = pltpu.roll(w, SUBS - d, 0)
                    inside = index < SUBS - d
                    b, w = (
                        b + jnp.where(inside, shrink * next_b, 0.0),
                        w + jnp.where(inside, shrink * (next_w + (d * span) * next_b), 0.0),
                    )
                inside = index < SUBS - 1
                b = jnp.where(inside, pltpu.roll(b, SUBS - 1, 0), 0.0)
                w = jnp.where(inside, pltpu.roll(w, SUBS - 1, 0), 0.0)
                shrink = jnp.exp(-after * row)
                b_row, w_row = in_b[n : n + 1], in_w[n : n + 1]
                b = b + shrink * b_row
                w = w + shrink * (w_row + after * b_row)
                zero = no_state(u_tiles)
                starts.append((b, w, zero, zero))
            decays = [spread(decay[n : n + 1]) for n in chosen]
            scales = [spread(scale[n : n + 1]) for n in chosen]

            def step(i, held):
                at = pl.ds(span - 1 - i, SUBS, stride=span)
                g = g_tiles[tile, at, :]
                u = u_tiles[tile, at, :]
                later, parts = [], []
                for d, s, (b, w, sum_b, sum_w) in zip(decays, scales, held):
                    shrunk = d * b
                    w = d * w + shrunk
                    b = g + shrunk
                    later.append((b, w, sum_b + u * b, sum_w + u * w))
                    parts.append(s * b)
                while len(parts) > 1:
                    parts = [p + q for p, q in zip(parts[::2], parts[1::2])]
                if first > 0:
                    parts[0] = parts[0] + y_tiles[tile, at, :]
                y_tiles[tile, at, :] = parts[0]
                return tuple(later)

            held = lax.fori_loop(0, span, step, tuple(starts), unroll=2)
            for n, (unused_b, unused_w, sum_b, sum_w) in zip(chosen, held):
                sum_b = jnp.sum(sum_b, axis=0, keepdims=True)
                sum_w = jnp.sum(sum_w, axis=0, keepdims=True)
                row = slice(n, n + 1)
                grad_ssm_ref[0, row, lanes] = root[row] * sum_b
                grad_ssm_ref[1, row, lanes] = scale[row] * (0.5 * sum_b - rate[row] * sum_w)
        at_lanes = pl.ds(pl.multiple_of(place[0] * width + tile * LANES, LANES), LANES)
        full[:, at_lanes] += y_tiles[tile].astype(bf16).astype(f32)
    rows = pieces[0].shape[0]
    for k in range(team):
        at_rows = pl.ds(pl.multiple_of((place[0] ^ k) * rows, rows), rows)
        pieces[k][...] = full[at_rows, :].astype(bf16)


def input_grad_kernel(team, place, x_ref, gain_ref, middle_grad_ref, *refs):
    parts, (out_ref, gain_grad_ref) = refs[:team], refs[team:]
    rows = out_ref.shape[0]
    at_rows = pl.ds(pl.multiple_of(place[0] * rows, rows), rows)
    grad_one = parts[0][...].astype(f32)
    for part in parts[1:]:
        grad_one = grad_one + part[...].astype(f32)
    unit, inverse = normalise(x_ref[at_rows, :].astype(f32))
    gain_grad_ref[...] = jnp.sum(grad_one * unit, axis=0, keepdims=True)
    back = normalise_back(unit, inverse, grad_one * gain_ref[...])
    out_ref[...] = (middle_grad_ref[at_rows, :] + back).astype(bf16)


def call(body, ins, outs, scratch=(), grid=None, in_specs=None, out_specs=None, flops=0):
    moved = sum(a.size * a.dtype.itemsize for a in list(ins) + list(outs))
    params = pltpu.CompilerParams(vmem_limit_bytes=VMEM_BYTES)
    cost = pl.CostEstimate(flops=flops, bytes_accessed=moved, transcendentals=0)
    whole = pl.BlockSpec(memory_space=pltpu.VMEM)
    extra = {}
    if grid is not None:
        extra["grid"] = grid
    return pl.pallas_call(
        body,
        out_shape=tuple(outs),
        in_specs=in_specs or [whole for unused in ins],
        out_specs=tuple(out_specs or [whole for unused in outs]),
        scratch_shapes=list(scratch),
        compiler_params=params,
        cost_estimate=cost,
        **extra,
    )(*ins)


def shaped(shape, kind):
    return jax.ShapeDtypeStruct(tuple(shape), kind)


def square_sums(arrays, stacked_flags):
    pieces = []
    for array_item, stacked in zip(arrays, stacked_flags):
        if stacked:
            pieces.append(jnp.sum(array_item * array_item, axis=tuple(range(1, array_item.ndim))))
        else:
            pieces.append(jnp.sum(array_item * array_item).reshape(1))
    return jnp.concatenate(pieces)


def lamb_moments(weight, grad_item, first_old, second_old):
    first_new = beta_first * first_old + (1.0 - beta_first) * grad_item
    second_new = beta_second * second_old + (1.0 - beta_second) * grad_item * grad_item
    direction = (
        first_new
        / (1.0 - beta_first**STEP)
        / (jnp.sqrt(second_new / (1.0 - beta_second**STEP)) + lamb_eps)
        + weight_decay * weight
    )
    return (first_new, second_new, direction)


def on_device(
    tokens,
    cotangent,
    w_qkv,
    w_out,
    w_up,
    w_down,
    norm_gains,
    ssm_param,
    first_qkv,
    second_qkv,
    first_out,
    second_out,
    first_up,
    second_up,
    first_down,
    second_down,
    first_gain,
    second_gain,
    first_ssm,
    second_ssm,
):
    halves = lax.axis_size("sl")
    low_count = lax.axis_size("ml")
    row_parts = lax.axis_size("sh")
    col_parts = lax.axis_size("mb") * lax.axis_size("mq")
    team = halves * low_count
    sl, ml, mb, mq = (lax.axis_index(name) for name in ("sl", "ml", "mb", "mq"))
    rank = sl * low_count + ml
    block_index = lax.axis_index("sh") * halves + mq
    block_count = row_parts * halves
    seq_total, length, width = tokens.shape
    assert length == BLK and seq_total == lax.axis_size("mb")
    states = ssm_param.shape[1]
    channels = width // team
    tiles = channels // LANES
    row_count = width // row_parts
    own_rows = length // team
    place = jnp.stack([rank, block_index]).astype(jnp.int32)
    smem = pl.BlockSpec(memory_space=pltpu.SMEM)
    vmem = pl.BlockSpec(memory_space=pltpu.VMEM)

    def swap(value):
        return lax.ppermute(value, "sl", [(0, 1), (1, 0)])

    def in_order(own, other, axis):
        return jnp.where(
            sl == 0, jnp.concatenate([own, other], axis), jnp.concatenate([other, own], axis)
        )

    def team_send(pieces):
        moved = [pieces[0]]
        for k in range(1, team):
            moved.append(lax.ppermute(pieces[k], TEAM, [(i, i ^ k) for i in range(team)]))
        return moved

    def pick_block(array):
        own = lax.dynamic_index_in_dim(array, mb, 0, keepdims=False)
        if halves == 1:
            return own
        moves = [(p * 2 + p, (1 - p) * 2 + p) for p in range(2)]
        other = lax.ppermute(own, ("sl", "mq"), moves)
        return jnp.where(sl == mq, own, other)

    small = jnp.concatenate([ssm_param.reshape(2 * states, -1), norm_gains], 0)
    small = lax.all_gather(small, ALL, axis=1, tiled=True)
    own_ssm = lax.dynamic_slice_in_dim(
        small[: 2 * states].reshape(2, states, width), rank * channels, channels, 2
    )
    coef, logr = own_ssm[0], own_ssm[1]
    gain_one = small[2 * states : 2 * states + 1]
    gain_two = small[2 * states + 1 : 2 * states + 2]

    rows_dev = w_up.shape[0]

    def in_halves(matrix):
        return jnp.transpose(matrix.reshape(rows_dev, halves, -1), (1, 0, 2))

    packed = jnp.concatenate(
        [in_halves(w_qkv[i].astype(bf16)) for i in range(3)]
        + [in_halves(matrix.astype(bf16)) for matrix in (w_out.T, w_up, w_down.T)],
        axis=2,
    )
    head_cols = packed.shape[2] - 2 * (w_up.shape[1] // halves)
    hidden_cols = w_up.shape[1] // halves
    if halves == 2:
        packed = in_order(
            lax.dynamic_index_in_dim(packed, sl, 0, keepdims=False),
            swap(lax.dynamic_index_in_dim(packed, 1 - sl, 0, keepdims=False)),
            0,
        )
    else:
        packed = packed[0]

    def gather_weight(shard):
        full = lax.all_gather(shard, COPIES, axis=0, tiled=False)
        return full.reshape(row_parts, col_parts, row_count, shard.shape[1])

    attn_w = gather_weight(packed[:, :head_cols])
    up_w = gather_weight(packed[:, head_cols : head_cols + hidden_cols])
    down_w = gather_weight(packed[:, head_cols + hidden_cols :])

    x = pick_block(tokens)
    cot = pick_block(cotangent)

    def slab(cols):
        return pl.BlockSpec((row_parts, 1, row_count, cols), lambda z: (0, z, 0, 0))

    def fixed(*shape):
        return pl.BlockSpec(shape, lambda z: (0,) * len(shape))

    wide = fixed(length, width)
    row = fixed(1, width)

    normed_one, ends, total = call(
        norm_kernel,
        (place, x, gain_one, logr),
        (
            shaped((length, width), bf16),
            shaped((states, SUBS, channels), f32),
            shaped((states, channels), f32),
        ),
        scratch=[pltpu.VMEM((tiles, length, LANES), f32)],
        in_specs=[smem, vmem, vmem, vmem],
        flops=length * channels * states * 64,
    )
    totals = lax.all_gather(total, ("sh", "mq"), axis=0, tiled=False)
    totals = totals.reshape(block_count, states, channels)
    (context_own,) = call(
        context_kernel,
        (place, normed_one, ends, totals, logr, coef),
        (shaped((length, channels), bf16),),
        scratch=[pltpu.VMEM((tiles, length, LANES), f32)] * 2,
        in_specs=[smem] + [vmem] * 5,
        flops=length * channels * states * 128,
    )
    contexts = team_send([context_own] * team)

    piece = fixed(length, channels)
    context, attn_part, kept = call(
        functools.partial(attend_kernel, team),
        (place, normed_one, *contexts, attn_w),
        (
            shaped((length, width), bf16),
            shaped((length, width), bf16),
            shaped((col_parts, length, 4 * HD), bf16),
        ),
        scratch=[pltpu.VMEM((length, width), f32)],
        grid=(col_parts,),
        in_specs=[smem, wide] + [piece] * team + [slab(head_cols)],
        out_specs=[wide, wide, pl.BlockSpec((1, length, 4 * HD), lambda z: (z, 0, 0))],
        flops=2 * length * width * head_cols * col_parts,
    )
    attn_parts = team_send([attn_part] * team)

    hidden_shape = shaped((row_parts, col_parts, row_count, hidden_cols), bf16)
    middle, out_part, two_part, grad_up, grad_down = call(
        functools.partial(feed_kernel, team),
        (x, cot, gain_two, *attn_parts, up_w, down_w),
        (
            shaped((length, width), f32),
            shaped((length, width), bf16),
            shaped((length, width), bf16),
            hidden_shape,
            hidden_shape,
        ),
        scratch=[
            pltpu.VMEM((length, width), bf16),
            pltpu.VMEM((width, length), bf16),
            pltpu.VMEM((width, length), bf16),
            pltpu.VMEM((length, width), f32),
            pltpu.VMEM((length, width), f32),
        ],
        grid=(col_parts,),
        in_specs=[wide, wide, row] + [wide] * team + [slab(hidden_cols)] * 2,
        out_specs=[wide, wide, wide, slab(hidden_cols), slab(hidden_cols)],
        flops=12 * length * width * hidden_cols * col_parts,
    )
    two_parts = team_send([two_part] * team)

    def rows_of(array, member):
        return lax.dynamic_slice_in_dim(array, member * own_rows, own_rows, 0)

    def share_rows(own_piece):
        full = lax.all_gather(own_piece, ("mb", "mq", "ml"), axis=0, tiled=False)
        full = full.reshape(seq_total, halves, 1, low_count * own_rows, width)
        if halves == 2:
            own = lax.dynamic_index_in_dim(full, sl, 1, keepdims=False)
            other = swap(lax.dynamic_index_in_dim(full, 1 - sl, 1, keepdims=False))
            full = in_order(own, other, 1)
        return full.reshape(seq_total, length, width)

    out_pieces = team_send([rows_of(out_part, rank ^ k) for k in range(team)])
    result = rows_of(middle, rank) + sum(item.astype(f32) for item in out_pieces)
    layer_out = share_rows(result.astype(bf16))

    def scatter_weight(grad):
        grad = grad.reshape(row_parts * col_parts, row_count, grad.shape[3])
        own = lax.psum_scatter(grad, COPIES, scatter_dimension=0, tiled=False)
        own = own.reshape(halves, rows_dev, -1)
        if halves == 1:
            return own
        keep = lax.dynamic_index_in_dim(own, sl, 0, keepdims=True)
        other = swap(lax.dynamic_index_in_dim(own, 1 - sl, 0, keepdims=True))
        return in_order(keep, other, 0)

    def out_of_halves(parts):
        return jnp.transpose(parts, (1, 0, 2)).reshape(rows_dev, -1).astype(f32)

    summed_up = out_of_halves(scatter_weight(grad_up))
    summed_down = out_of_halves(scatter_weight(grad_down)).T

    middle_grad, gain_two_grad, grad_attn, one_part, *context_grads = call(
        functools.partial(attend_back_kernel, team),
        (place, middle, gain_two, cot, *two_parts, normed_one, context, kept, attn_w),
        (
            shaped((length, width), f32),
            shaped((1, width), f32),
            shaped((row_parts, col_parts, row_count, head_cols), bf16),
            shaped((length, width), f32),
            *[shaped((length, channels), bf16)] * team,
        ),
        scratch=[
            pltpu.VMEM((length, width), bf16),
            pltpu.VMEM((width, length), bf16),
            pltpu.VMEM((width, length), bf16),
            pltpu.VMEM((width, length), bf16),
            pltpu.VMEM((length, width), f32),
            pltpu.VMEM((length, width), f32),
        ],
        grid=(col_parts,),
        in_specs=[smem, wide, row, wide]
        + [wide] * team
        + [wide, wide, pl.BlockSpec((1, length, 4 * HD), lambda z: (z, 0, 0)), slab(head_cols)],
        out_specs=[wide, row, slab(head_cols), wide] + [piece] * team,
        flops=4 * length * width * head_cols * col_parts,
    )
    context_grads = team_send(context_grads)
    halves_attn = scatter_weight(grad_attn)
    split_attn = halves_attn.reshape(halves, rows_dev, 4, -1)
    summed_qkv = jnp.stack([out_of_halves(split_attn[:, :, i]) for i in range(3)])
    summed_out = out_of_halves(split_attn[:, :, 3]).T

    context_grad, adjoint_ends, adjoint_total = call(
        functools.partial(adjoint_kernel, team),
        (logr, *context_grads),
        (
            shaped((length, channels), bf16),
            shaped((2, states, SUBS, channels), f32),
            shaped((2, states, channels), f32),
        ),
        scratch=[pltpu.VMEM((tiles, length, LANES), f32)],
        flops=length * channels * states * 128,
    )
    adjoint_totals = lax.all_gather(adjoint_total, ("sh", "mq"), axis=0, tiled=False)
    adjoint_totals = adjoint_totals.reshape(block_count, 2, states, channels)
    *one_pieces, grad_ssm = call(
        functools.partial(context_back_kernel, team),
        (place, context_grad, normed_one, adjoint_ends, adjoint_totals, logr, coef, one_part),
        (
            *[shaped((own_rows, width), bf16)] * team,
            shaped((2, states, channels), f32),
        ),
        scratch=[pltpu.VMEM((tiles, length, LANES), f32)] * 3 + [pltpu.VMEM((length, width), f32)],
        in_specs=[smem] + [vmem] * 7,
        flops=length * channels * states * 256,
    )
    one_pieces = team_send(one_pieces)
    grad_rows, gain_one_grad = call(
        functools.partial(input_grad_kernel, team),
        (place, x, gain_one, middle_grad, *one_pieces),
        (shaped((own_rows, width), bf16), shaped((1, width), f32)),
        in_specs=[smem] + [vmem] * (3 + team),
    )
    input_grad = share_rows(grad_rows).astype(f32)

    placed_ssm = lax.dynamic_update_slice_in_dim(
        jnp.zeros((2 * states, width), f32),
        grad_ssm.reshape(2 * states, channels),
        rank * channels,
        1,
    )
    small_grads = jnp.concatenate([placed_ssm, gain_one_grad, gain_two_grad], 0)
    small_grads = lax.psum_scatter(small_grads, ALL, scatter_dimension=1, tiled=True)
    summed_ssm = small_grads[: 2 * states].reshape(ssm_param.shape)
    summed_gain = small_grads[2 * states :]

    masters = (w_qkv, w_out, w_up, w_down, norm_gains, ssm_param)
    stacked_flags = (True, False, False, False, True, True)
    grads_all = (summed_qkv, summed_out, summed_up, summed_down, summed_gain, summed_ssm)
    firsts = (first_qkv, first_out, first_up, first_down, first_gain, first_ssm)
    seconds = (second_qkv, second_out, second_up, second_down, second_gain, second_ssm)
    moments = [lamb_moments(*items) for items in zip(masters, grads_all, firsts, seconds)]
    update_sq = square_sums([moment_item[2] for moment_item in moments], stacked_flags)
    weight_sq = square_sums(masters, stacked_flags)
    norms = jnp.sqrt(lax.psum(jnp.stack([weight_sq, update_sq]), ALL))
    ratios = norms[0] / norms[1]
    offsets = (0, 3, 4, 5, 6, 8, 10)
    outputs = [layer_out, input_grad]
    for item_index in range(6):
        master = masters[item_index]
        ratio = ratios[offsets[item_index] : offsets[item_index + 1]].reshape(
            (-1,) + (1,) * (master.ndim - 1)
        )
        first_new, second_new, direction = moments[item_index]
        outputs.append(master - learn_rate * ratio * direction)
        outputs.append(first_new)
        if item_index == 4:
            outputs.append(second_new[0])
            outputs.append(second_new[1])
        else:
            outputs.append(second_new)
    outputs.append(norms)
    return tuple(outputs)


def solution(mesh):
    seq_count, model_count = mesh.shape["seq"], mesh.shape["mp"]
    halves = 2 if HEADS // model_count >= 2 else 1
    sizes = (seq_count // halves, halves, SEQS, halves, model_count // (SEQS * halves))
    fine = Mesh(mesh.devices.reshape(sizes), ALL)
    seq, model = ("sh", "sl"), ("mb", "mq", "ml")
    rows_cols, cols_rows = P(seq, model), P(model, seq)
    token = P(None, seq, None)
    stack = P(None, seq, model)
    gains = P(None, ALL)
    ssm = P(None, None, ALL)
    return jax.shard_map(
        on_device,
        mesh=fine,
        in_specs=(token, token, stack, cols_rows, rows_cols, cols_rows, gains, ssm)
        + (stack,) * 2
        + (cols_rows,) * 2
        + (rows_cols,) * 2
        + (cols_rows,) * 2
        + (gains,) * 2
        + (ssm,) * 2,
        out_specs=(token, token)
        + (stack,) * 3
        + (cols_rows,) * 3
        + (rows_cols,) * 3
        + (cols_rows,) * 3
        + (gains, gains, P(ALL), P(ALL))
        + (ssm,) * 3
        + (P(),),
        check_vma=False,
    )
```

```python
import functools
import math

import jax
import jax.numpy as jnp
from jax import lax
from jax.experimental import pallas as pl
from jax.experimental.pallas import tpu as pltpu
from jax.sharding import Mesh
from jax.sharding import PartitionSpec as P

HD = 128
HEADS = 8
BLK = 512
STEP = 10
SEQS = 2
LANES = 128
SUBS = 8

norm_eps = 1e-05
beta_first = 0.9
beta_second = 0.999
lamb_eps = 1e-06
weight_decay = 0.01
learn_rate = 0.5
score_scale = HD ** (-0.5)

f32 = jnp.float32
bf16 = jnp.bfloat16
VMEM_BYTES = 56 * 1024 * 1024

ALL = ("sh", "sl", "mb", "mq", "ml")
MODEL = ("mb", "mq", "ml")
TEAM = ("sl", "ml")


def dot(left, right):
    return lax.dot_general(left, right, (((1,), (0,)), ((), ())), preferred_element_type=f32)


def dot_t(left, right):
    return lax.dot_general(left, right, (((1,), (1,)), ((), ())), preferred_element_type=f32)


def normalise(values):
    centred = values - jnp.mean(values, axis=-1, keepdims=True)
    inverse = lax.rsqrt(jnp.mean(centred * centred, axis=-1, keepdims=True) + norm_eps)
    return centred * inverse, inverse


def normalise_back(unit, inverse, grad_unit):
    mean_one = jnp.mean(grad_unit, axis=-1, keepdims=True)
    mean_two = jnp.mean(grad_unit * unit, axis=-1, keepdims=True)
    return inverse * (grad_unit - mean_one - unit * mean_two)


def sub_index():
    return lax.broadcasted_iota(jnp.int32, (SUBS, LANES), 0)


def spread(row):
    return jnp.broadcast_to(row, (SUBS, LANES))


def lane_tile(index):
    return slice(index * LANES, (index + 1) * LANES)


def no_state(tiles):
    rows = tiles[0, :SUBS, :]
    return rows - rows


def fill_tiles(scratch, ref, start):
    for tile in range(scratch.shape[0]):
        lanes = pl.ds(pl.multiple_of(start + tile * LANES, LANES), LANES)
        scratch[tile] = ref[:, lanes].astype(f32)


def norm_kernel(place, x_ref, gain_ref, logr_ref, normed_ref, ends_ref, total_ref, u_tiles):
    unit, unused = normalise(x_ref[...].astype(f32))
    normed_ref[...] = (unit * gain_ref[...]).astype(bf16)
    tiles, length, unused = u_tiles.shape
    states = logr_ref.shape[0]
    span = length // SUBS
    fill_tiles(u_tiles, normed_ref, place[0] * (tiles * LANES))
    left = ((SUBS - 1 - sub_index()) * span).astype(f32)
    for tile in range(tiles):
        rate = jnp.exp(logr_ref[:, lane_tile(tile)])
        decay = jnp.exp(-rate)
        decays = [spread(decay[n : n + 1]) for n in range(states)]

        def step(i, held):
            u = u_tiles[tile, pl.ds(i, SUBS, stride=span), :]
            return tuple(d * h + u for d, h in zip(decays, held))

        zero = no_state(u_tiles)
        held = lax.fori_loop(0, span, step, (zero,) * states, unroll=4)
        for n in range(states):
            ends_ref[n, :, lane_tile(tile)] = held[n]
            total_ref[n : n + 1, lane_tile(tile)] = jnp.sum(
                held[n] * jnp.exp(-left * rate[n : n + 1]), axis=0, keepdims=True
            )


def context_kernel(
    place, normed_ref, ends_ref, all_ref, logr_ref, coef_ref, context_ref, u_tiles, y_tiles
):
    tiles, length, unused = u_tiles.shape
    states = logr_ref.shape[0]
    span = length // SUBS
    fill_tiles(u_tiles, normed_ref, place[0] * (tiles * LANES))
    index = sub_index()
    before = (index * span).astype(f32)
    for tile in range(tiles):
        rate = jnp.exp(logr_ref[:, lane_tile(tile)])
        decay = jnp.exp(-rate)
        scale = coef_ref[:, lane_tile(tile)] * jnp.sqrt(2.0 * rate)
        incoming = jnp.zeros((states, LANES), f32)
        for j in range(all_ref.shape[0]):
            gap = place[1] - 1 - j
            distance = (jnp.maximum(gap, 0) * length).astype(f32)
            term = jnp.exp(-distance * rate) * all_ref[j, :, lane_tile(tile)]
            incoming = incoming + jnp.where(gap >= 0, term, 0.0)
        starts = []
        for n in range(states):
            row = rate[n : n + 1]
            run = ends_ref[n, :, lane_tile(tile)]
            for d in (1, 2, 4):
                moved = jnp.exp(-(d * span) * row) * pltpu.roll(run, d, 0)
                run = run + jnp.where(index >= d, moved, 0.0)
            run = jnp.where(index >= 1, pltpu.roll(run, 1, 0), 0.0)
            starts.append(run + jnp.exp(-before * row) * incoming[n : n + 1])
        decays = [spread(decay[n : n + 1]) for n in range(states)]
        scales = [spread(scale[n : n + 1]) for n in range(states)]

        def step(i, held):
            u = u_tiles[tile, pl.ds(i, SUBS, stride=span), :]
            held = tuple(d * h + u for d, h in zip(decays, held))
            parts = [s * h for s, h in zip(scales, held)]
            while len(parts) > 1:
                parts = [a + b for a, b in zip(parts[::2], parts[1::2])]
            y_tiles[tile, pl.ds(i, SUBS, stride=span), :] = parts[0]
            return held

        lax.fori_loop(0, span, step, tuple(starts), unroll=2)
        context_ref[:, lane_tile(tile)] = y_tiles[tile].astype(bf16)


def whole_rows(block):
    return block.reshape(block.shape[0] * block.shape[1], block.shape[2])


def head(index):
    return slice(index * HD, (index + 1) * HD)


def split_pieces(refs, col_parts, row_parts):
    return [refs[k * row_parts : (k + 1) * row_parts] for k in range(col_parts)]


def head_copies(pieces, buffer, place, sems, inward):
    copies = []
    for k, group in enumerate(pieces):
        for r, piece in enumerate(group):
            for i in range(4):
                outside = piece.at[:, pl.ds(i * HD, HD)]
                inside = buffer.at[i, place[2] ^ r, :, pl.ds(k * HD, HD)]
                ends = (outside, inside) if inward else (inside, outside)
                copies.append(pltpu.make_async_copy(*ends, sems.at[k, r, i]))
    return copies


def attend_kernel(team, col_parts, row_parts, place, normed_ref, *refs):
    contexts, refs = refs[:team], refs[team:]
    count = col_parts * row_parts
    pieces, refs = split_pieces(refs[:count], col_parts, row_parts), refs[count:]
    context_ref, part_ref, kept_ref, probs_ref, weights, sems = refs
    copies = head_copies(pieces, weights, place, sems, True)
    for copy in copies:
        copy.start()
    width = contexts[0].shape[1]
    for k in range(team):
        lanes = pl.ds(pl.multiple_of((place[0] ^ k) * width, LANES), width)
        context_ref[:, lanes] = contexts[k][...]
    for copy in copies:
        copy.wait()
    kept_ref[0] = dot(normed_ref[...], whole_rows(weights[0])).astype(bf16)
    kept_ref[1] = dot(context_ref[...], whole_rows(weights[1])).astype(bf16)
    kept_ref[2] = dot(context_ref[...], whole_rows(weights[2])).astype(bf16)
    length = normed_ref.shape[0]
    rows = lax.broadcasted_iota(jnp.int32, (length, length), 0)
    cols = lax.broadcasted_iota(jnp.int32, (length, length), 1)
    for h in range(col_parts):
        scores = dot_t(kept_ref[0, :, head(h)], kept_ref[1, :, head(h)]) * score_scale
        scores = jnp.where(rows >= cols, scores, -1e30)
        shifted = jnp.exp(scores - jnp.max(scores, axis=-1, keepdims=True))
        inverse = 1.0 / jnp.sum(shifted, axis=-1, keepdims=True)
        probs = (shifted * inverse).astype(bf16)
        probs_ref[h] = probs
        kept_ref[3, :, head(h)] = dot(probs, kept_ref[2, :, head(h)]).astype(bf16)
    part_ref[...] = dot_t(kept_ref[3], whole_rows(weights[3])).astype(bf16)


def feed_kernel(team, col_parts, row_parts, place, x_ref, cot_ref, gain_ref, *refs):
    parts, refs = refs[:team], refs[team:]
    count = col_parts * row_parts
    groups = []
    for unused in range(2):
        groups.append(split_pieces(refs[:count], col_parts, row_parts))
        refs = refs[count:]
    middle_ref, out_ref, two_ref = refs[:3]
    refs = refs[3:]
    for unused in range(2):
        groups.append(split_pieces(refs[:count], col_parts, row_parts))
        refs = refs[count:]
    up_all, down_all, grad_up, grad_down, normed, normed_t, cot_t, out_total, two_total, sems = refs
    buffers = (up_all, down_all, grad_up, grad_down)
    z = pl.program_id(0)

    def copies(which, k):
        found = []
        for r, piece in enumerate(groups[which][k]):
            inside = buffers[which].at[k, place[2] ^ r]
            ends = (piece, inside) if which < 2 else (inside, piece)
            found.append(pltpu.make_async_copy(*ends, sems.at[which, k, r]))
        return found

    @pl.when(z == 0)
    def start():
        for k in range(col_parts):
            for copy in copies(0, k) + copies(1, k):
                copy.start()
        attn = parts[0][...].astype(f32)
        for part in parts[1:]:
            attn = attn + part[...].astype(f32)
        middle = x_ref[...].astype(f32) + attn
        middle_ref[...] = middle
        unit, unused = normalise(middle)
        low = (unit * gain_ref[...]).astype(bf16)
        normed[...] = low
        normed_t[...] = low.T
        cot_t[...] = cot_ref[...].T
        out_total[...] = jnp.zeros_like(out_total)
        two_total[...] = jnp.zeros_like(two_total)

    for k in range(col_parts):

        @pl.when(z == k)
        def arrive():
            for copy in copies(0, k) + copies(1, k):
                copy.wait()

    up = whole_rows(up_all[z])
    down = whole_rows(down_all[z])
    hidden = dot(normed[...], up)
    grad_act = dot(cot_ref[...], down)
    cdf = 0.5 * (1.0 + lax.erf(hidden * math.sqrt(0.5)))
    activated = (hidden * cdf).astype(bf16)
    slope = cdf + hidden * jnp.exp(-0.5 * hidden * hidden) * (1.0 / math.sqrt(2.0 * math.pi))
    grad_pre = (grad_act * slope).astype(bf16)
    out_total[...] += dot_t(activated, down)
    two_total[...] += dot_t(grad_pre, up)
    shape = grad_up.shape[1:]
    grad_up[z] = dot(normed_t[...], grad_pre).astype(bf16).reshape(shape)
    grad_down[z] = dot(cot_t[...], activated).astype(bf16).reshape(shape)

    for k in range(col_parts):

        @pl.when(z == k)
        def leave():
            for copy in copies(2, k) + copies(3, k):
                copy.start()

    @pl.when(z == col_parts - 1)
    def finish():
        out_ref[...] = out_total[...].astype(bf16)
        two_ref[...] = two_total[...].astype(bf16)
        for k in range(col_parts):
            for copy in copies(2, k) + copies(3, k):
                copy.wait()


def attend_back_kernel(team, col_parts, row_parts, place, middle_ref, gain_ref, cot_ref, *refs):
    parts, refs = refs[:team], refs[team:]
    normed_ref, context_ref, kept_ref, probs_ref = refs[:4]
    refs = refs[4:]
    count = col_parts * row_parts
    pieces, refs = split_pieces(refs[:count], col_parts, row_parts), refs[count:]
    middle_grad_ref, gain_grad_ref, one_ref = refs[:3]
    refs = refs[3:]
    context_grads, refs = refs[:team], refs[team:]
    grad_pieces, refs = split_pieces(refs[:count], col_parts, row_parts), refs[count:]
    weights, grads, low, grad_out, grad_q, grad_k, grad_v, sems, out_sems = refs
    copies = head_copies(pieces, weights, place, sems, True)
    for copy in copies:
        copy.start()
    own_rows = middle_ref.shape[0] // team
    grad_two = parts[0][...].astype(f32)
    for part in parts[1:]:
        grad_two = grad_two + part[...].astype(f32)
    unit, inverse = normalise(middle_ref[...])
    grad_gain = grad_two * unit
    rows = lax.broadcasted_iota(jnp.int32, grad_gain.shape, 0)
    first = place[0] * own_rows
    mine = (rows >= first) & (rows < first + own_rows)
    gain_grad_ref[...] = jnp.sum(jnp.where(mine, grad_gain, 0.0), axis=0, keepdims=True)
    grad = cot_ref[...].astype(f32) + normalise_back(unit, inverse, grad_two * gain_ref[...])
    middle_grad_ref[...] = grad
    low[...] = grad.astype(bf16)
    for copy in copies:
        copy.wait()
    grad_out[...] = dot(low[...], whole_rows(weights[3])).astype(bf16)
    for h in range(col_parts):
        q, k, v = (kept_ref[i, :, head(h)] for i in range(3))
        probs = probs_ref[h]
        grad_heads = grad_out[:, head(h)]
        grad_v[:, head(h)] = dot(probs.T, grad_heads).astype(bf16)
        probs = probs.astype(f32)
        grad_probs = dot_t(grad_heads, v)
        inner = jnp.sum(grad_probs * probs, axis=-1, keepdims=True)
        grad_scores = (probs * (grad_probs - inner)).astype(bf16)
        grad_q[:, head(h)] = (dot(grad_scores, k) * score_scale).astype(bf16)
        grad_k[:, head(h)] = (dot(grad_scores.T, q) * score_scale).astype(bf16)
    shape = grads.shape[1:]
    normed_t = normed_ref[...].T
    context_t = context_ref[...].T
    grads[3] = dot(low[...].T, kept_ref[3]).astype(bf16).reshape(shape)
    grads[0] = dot(normed_t, grad_q[...]).astype(bf16).reshape(shape)
    grads[1] = dot(context_t, grad_k[...]).astype(bf16).reshape(shape)
    grads[2] = dot(context_t, grad_v[...]).astype(bf16).reshape(shape)
    copies = head_copies(grad_pieces, grads, place, out_sems, False)
    for copy in copies:
        copy.start()
    total = dot_t(grad_k[...], whole_rows(weights[1])) + dot_t(grad_v[...], whole_rows(weights[2]))
    middle_total = total.astype(bf16)
    low[...] = middle_total
    width = context_grads[0].shape[1]
    for k in range(team):
        lanes = pl.ds(pl.multiple_of((place[0] ^ k) * width, LANES), width)
        context_grads[k][...] = low[:, lanes]
    one_ref[...] = dot_t(grad_q[...], whole_rows(weights[0]))
    for copy in copies:
        copy.wait()


def adjoint_kernel(team, logr_ref, *refs):
    parts = refs[:team]
    grad_ref, ends_ref, total_ref, g_tiles = refs[team:]
    grad = parts[0][...].astype(f32)
    for part in parts[1:]:
        grad = grad + part[...].astype(f32)
    grad_ref[...] = grad.astype(bf16)
    tiles, length, unused = g_tiles.shape
    states = logr_ref.shape[0]
    span = length // SUBS
    fill_tiles(g_tiles, grad_ref, 0)
    before = (sub_index() * span).astype(f32)
    for tile in range(tiles):
        rate = jnp.exp(logr_ref[:, lane_tile(tile)])
        decay = jnp.exp(-rate)
        decays = [spread(decay[n : n + 1]) for n in range(states)]

        def step(i, held):
            g = g_tiles[tile, pl.ds(span - 1 - i, SUBS, stride=span), :]
            later = []
            for d, (b, w) in zip(decays, held):
                shrunk = d * b
                later.append((g + shrunk, d * w + shrunk))
            return tuple(later)

        zero = no_state(g_tiles)
        held = lax.fori_loop(0, span, step, ((zero, zero),) * states, unroll=2)
        for n in range(states):
            b, w = held[n]
            ends_ref[0, n, :, lane_tile(tile)] = b
            ends_ref[1, n, :, lane_tile(tile)] = w
            shrink = jnp.exp(-before * rate[n : n + 1])
            total_ref[0, n : n + 1, lane_tile(tile)] = jnp.sum(shrink * b, axis=0, keepdims=True)
            total_ref[1, n : n + 1, lane_tile(tile)] = jnp.sum(
                shrink * (w + before * b), axis=0, keepdims=True
            )


def context_back_kernel(
    team, place, grad_ref, normed_ref, ends_ref, all_ref, logr_ref, coef_ref, one_ref, *refs
):
    pieces = refs[:team]
    grad_ssm_ref, u_tiles, g_tiles, y_tiles, full = refs[team:]
    tiles, length, unused = u_tiles.shape
    states = logr_ref.shape[0]
    span = length // SUBS
    width = tiles * LANES
    fill_tiles(u_tiles, normed_ref, place[0] * width)
    fill_tiles(g_tiles, grad_ref, 0)
    index = sub_index()
    after = ((SUBS - 1 - index) * span).astype(f32)
    full[...] = one_ref[...]
    group = 8
    for tile in range(tiles):
        lanes = lane_tile(tile)
        rate = jnp.exp(logr_ref[:, lanes])
        decay = jnp.exp(-rate)
        root = jnp.sqrt(2.0 * rate)
        scale = coef_ref[:, lanes] * root
        in_b = jnp.zeros((states, LANES), f32)
        in_w = jnp.zeros((states, LANES), f32)
        for j in range(all_ref.shape[0]):
            gap = j - place[1] - 1
            distance = (jnp.maximum(gap, 0) * length).astype(f32)
            shrink = jnp.exp(-distance * rate)
            b, w = all_ref[j, 0, :, lanes], all_ref[j, 1, :, lanes]
            in_b = in_b + jnp.where(gap >= 0, shrink * b, 0.0)
            in_w = in_w + jnp.where(gap >= 0, shrink * (w + distance * b), 0.0)
        for first in range(0, states, group):
            chosen = range(first, first + group)
            starts = []
            for n in chosen:
                row = rate[n : n + 1]
                b, w = ends_ref[0, n, :, lanes], ends_ref[1, n, :, lanes]
                for d in (1, 2, 4):
                    shrink = jnp.exp(-(d * span) * row)
                    next_b = pltpu.roll(b, SUBS - d, 0)
                    next_w = pltpu.roll(w, SUBS - d, 0)
                    inside = index < SUBS - d
                    b, w = (
                        b + jnp.where(inside, shrink * next_b, 0.0),
                        w + jnp.where(inside, shrink * (next_w + (d * span) * next_b), 0.0),
                    )
                inside = index < SUBS - 1
                b = jnp.where(inside, pltpu.roll(b, SUBS - 1, 0), 0.0)
                w = jnp.where(inside, pltpu.roll(w, SUBS - 1, 0), 0.0)
                shrink = jnp.exp(-after * row)
                b_row, w_row = in_b[n : n + 1], in_w[n : n + 1]
                b = b + shrink * b_row
                w = w + shrink * (w_row + after * b_row)
                zero = no_state(u_tiles)
                starts.append((b, w, zero, zero))
            decays = [spread(decay[n : n + 1]) for n in chosen]
            scales = [spread(scale[n : n + 1]) for n in chosen]

            def step(i, held):
                at = pl.ds(span - 1 - i, SUBS, stride=span)
                g = g_tiles[tile, at, :]
                u = u_tiles[tile, at, :]
                later, parts = [], []
                for d, s, (b, w, sum_b, sum_w) in zip(decays, scales, held):
                    shrunk = d * b
                    w = d * w + shrunk
                    b = g + shrunk
                    later.append((b, w, sum_b + u * b, sum_w + u * w))
                    parts.append(s * b)
                while len(parts) > 1:
                    parts = [p + q for p, q in zip(parts[::2], parts[1::2])]
                if first > 0:
                    parts[0] = parts[0] + y_tiles[tile, at, :]
                y_tiles[tile, at, :] = parts[0]
                return tuple(later)

            held = lax.fori_loop(0, span, step, tuple(starts), unroll=2)
            for n, (unused_b, unused_w, sum_b, sum_w) in zip(chosen, held):
                sum_b = jnp.sum(sum_b, axis=0, keepdims=True)
                sum_w = jnp.sum(sum_w, axis=0, keepdims=True)
                row = slice(n, n + 1)
                grad_ssm_ref[0, row, lanes] = root[row] * sum_b
                grad_ssm_ref[1, row, lanes] = scale[row] * (0.5 * sum_b - rate[row] * sum_w)
        at_lanes = pl.ds(pl.multiple_of(place[0] * width + tile * LANES, LANES), LANES)
        full[:, at_lanes] += y_tiles[tile].astype(bf16).astype(f32)
    rows = pieces[0].shape[0]
    for k in range(team):
        at_rows = pl.ds(pl.multiple_of((place[0] ^ k) * rows, rows), rows)
        pieces[k][...] = full[at_rows, :].astype(bf16)


def input_grad_kernel(team, place, x_ref, gain_ref, middle_grad_ref, *refs):
    parts, (out_ref, gain_grad_ref) = refs[:team], refs[team:]
    rows = out_ref.shape[0]
    at_rows = pl.ds(pl.multiple_of(place[0] * rows, rows), rows)
    grad_one = parts[0][...].astype(f32)
    for part in parts[1:]:
        grad_one = grad_one + part[...].astype(f32)
    unit, inverse = normalise(x_ref[at_rows, :].astype(f32))
    gain_grad_ref[...] = jnp.sum(grad_one * unit, axis=0, keepdims=True)
    back = normalise_back(unit, inverse, grad_one * gain_ref[...])
    out_ref[...] = (middle_grad_ref[at_rows, :] + back).astype(bf16)


def assemble_kernel(halves, low_count, count, place, *refs):
    own, refs = refs[:count], refs[count:]
    others, out_ref = refs[:-1], refs[-1]
    rows = own[0].shape[0]
    index, half, swapped = place[3], place[4], place[5]

    def put(piece, steps, which):
        source = lax.rem(index + count - steps, count)
        member = lax.rem(source, low_count)
        sequence = source // (halves * low_count)
        at_rows = pl.ds(pl.multiple_of((which * low_count + member) * rows, rows), rows)
        out_ref[sequence, at_rows, :] = piece[...].astype(out_ref.dtype)

    if halves == 1:
        for k in range(count):
            put(own[k], k, 0)
        return
    for j in range(count // 2):
        put(others[j], 2 * j + swapped, 1 - half)
        for odd in range(2):

            @pl.when(swapped == odd)
            def keep():
                put(own[2 * j + odd], 2 * j + odd, half)


def call(body, ins, outs, scratch=(), grid=None, in_specs=None, out_specs=None, flops=0):
    moved = sum(a.size * a.dtype.itemsize for a in list(ins) + list(outs))
    params = pltpu.CompilerParams(vmem_limit_bytes=VMEM_BYTES)
    cost = pl.CostEstimate(flops=flops, bytes_accessed=moved, transcendentals=0)
    whole = pl.BlockSpec(memory_space=pltpu.VMEM)
    extra = {}
    if grid is not None:
        extra["grid"] = grid
    return pl.pallas_call(
        body,
        out_shape=tuple(outs),
        in_specs=in_specs or [whole for unused in ins],
        out_specs=tuple(out_specs or [whole for unused in outs]),
        scratch_shapes=list(scratch),
        compiler_params=params,
        cost_estimate=cost,
        **extra,
    )(*ins)


def shaped(shape, kind):
    return jax.ShapeDtypeStruct(tuple(shape), kind)


def square_sums(arrays, stacked_flags):
    sums = []
    for array_item, stacked in zip(arrays, stacked_flags):
        for matrix in array_item if stacked else [array_item]:
            sums.append(jnp.sum(matrix * matrix))
    places = lax.iota(jnp.int32, len(sums))
    return sum(jnp.where(places == index, value, 0.0) for index, value in enumerate(sums))


def lamb_moments(weight, grad_item, first_old, second_old):
    first_new = beta_first * first_old + (1.0 - beta_first) * grad_item
    second_new = beta_second * second_old + (1.0 - beta_second) * grad_item * grad_item
    direction = (
        first_new
        / (1.0 - beta_first**STEP)
        / (jnp.sqrt(second_new / (1.0 - beta_second**STEP)) + lamb_eps)
        + weight_decay * weight
    )
    return (first_new, second_new, direction)


def on_device(
    tokens,
    cotangent,
    w_qkv,
    w_out,
    w_up,
    w_down,
    norm_gains,
    ssm_param,
    first_qkv,
    second_qkv,
    first_out,
    second_out,
    first_up,
    second_up,
    first_down,
    second_down,
    first_gain,
    second_gain,
    first_ssm,
    second_ssm,
):
    halves = lax.axis_size("sl")
    low_count = lax.axis_size("ml")
    row_parts = lax.axis_size("sh")
    col_parts = lax.axis_size("mb") * lax.axis_size("mq")
    team = halves * low_count
    sl, ml, mb, mq = (lax.axis_index(name) for name in ("sl", "ml", "mb", "mq"))
    rank = sl * low_count + ml
    block_index = lax.axis_index("sh") * halves + mq
    seq_total, length, width = tokens.shape
    assert length == BLK and seq_total == lax.axis_size("mb")
    states = ssm_param.shape[1]
    channels = width // team
    tiles = channels // LANES
    row_count = width // row_parts
    own_rows = length // team
    place = [rank, block_index, lax.axis_index("sh"), lax.axis_index(MODEL), sl, sl ^ mq]
    place = jnp.stack(place).astype(jnp.int32)
    smem = pl.BlockSpec(memory_space=pltpu.SMEM)
    vmem = pl.BlockSpec(memory_space=pltpu.VMEM)

    def permute(value, axes, moves):
        return lax.ppermute(value, axes, moves)

    def swap(value):
        return permute(value, "sl", [(0, 1), (1, 0)])

    def in_order(own, other, axis):
        return jnp.where(
            sl == 0, jnp.concatenate([own, other], axis), jnp.concatenate([other, own], axis)
        )

    def team_send(pieces):
        moved = [pieces[0]]
        for k in range(1, team):
            moved.append(permute(pieces[k], TEAM, [(i, i ^ k) for i in range(team)]))
        return moved

    def pick_block(array):
        own = lax.dynamic_index_in_dim(array, mb, 0, keepdims=False)
        if halves == 1:
            return own
        return jnp.where(sl == mq, own, swap(own))

    def across(value, bit):
        return permute(value, "sh", [(i, i ^ bit) for i in range(row_parts)])

    def along(value, axes, step):
        count = lax.axis_size(axes)
        return permute(value, axes, [(i, (i + step) % count) for i in range(count)])

    bits = [1 << i for i in range(row_parts.bit_length() - 1)]

    def bit_order(k):
        return bits if k % 2 == 0 else bits[::-1]

    def gather_weight(shard):
        pieces, held = [], shard
        for k in range(col_parts):
            if k > 0:
                held = along(held, ("mb", "mq"), 1)
            found = {0: held}
            for bit in bit_order(k):
                for r in list(found):
                    found[r | bit] = across(found[r], bit)
            pieces.append([found[r] for r in range(row_parts)])
        return pieces

    def add(*items):
        return sum(item.astype(f32) for item in items).astype(bf16)

    def scatter_weight(pieces):
        held = None
        for k in reversed(range(col_parts)):
            sums = {r: [piece] for r, piece in enumerate(pieces[k])}
            for bit in reversed(bit_order(k)):
                for r in [r for r in sums if r & bit]:
                    sums[r ^ bit].append(across(add(*sums.pop(r)), bit))
            items = sums[0]
            if held is not None:
                items = items + [along(held, ("mb", "mq"), -1)]
            held = add(*items)
        return held

    def everywhere(value, axes):
        count = lax.axis_size(axes)
        copies = jnp.broadcast_to(value[None], (count, *value.shape))
        return lax.all_to_all(copies, axes, 0, 0, tiled=True)

    small = jnp.concatenate([ssm_param.reshape(2 * states, -1), norm_gains], 0)
    small = jnp.transpose(everywhere(small, ALL), (1, 0, 2)).reshape(2 * states + 2, width)
    own_ssm = lax.dynamic_slice_in_dim(
        small[: 2 * states].reshape(2, states, width), rank * channels, channels, 2
    )
    coef, logr = own_ssm[0], own_ssm[1]
    gain_one = small[2 * states : 2 * states + 1]
    gain_two = small[2 * states + 1 : 2 * states + 2]

    rows_dev = w_up.shape[0]

    def in_halves(matrix):
        return jnp.transpose(matrix.reshape(rows_dev, halves, -1), (1, 0, 2))

    packed = jnp.concatenate(
        [in_halves(w_qkv[i].astype(bf16)) for i in range(3)]
        + [in_halves(matrix.astype(bf16)) for matrix in (w_out.T, w_up, w_down.T)],
        axis=2,
    )
    head_cols = packed.shape[2] - 2 * (w_up.shape[1] // halves)
    hidden_cols = w_up.shape[1] // halves
    if halves == 2:
        packed = in_order(
            lax.dynamic_index_in_dim(packed, sl, 0, keepdims=False),
            swap(lax.dynamic_index_in_dim(packed, 1 - sl, 0, keepdims=False)),
            0,
        )
    else:
        packed = packed[0]

    attn_w = gather_weight(packed[:, :head_cols])
    up_w = gather_weight(packed[:, head_cols : head_cols + hidden_cols])
    down_w = gather_weight(packed[:, head_cols + hidden_cols :])

    x = pick_block(tokens)
    cot = pick_block(cotangent)

    def flat(pieces):
        return [piece for group in pieces for piece in group]

    def nested(pieces):
        return split_pieces(pieces, col_parts, row_parts)

    piece_count = row_parts * col_parts
    anywhere = [pl.BlockSpec(memory_space=pl.ANY)] * piece_count

    def fixed(*shape):
        return pl.BlockSpec(shape, lambda z: (0,) * len(shape))

    wide = fixed(length, width)
    row = fixed(1, width)

    normed_one, ends, total = call(
        norm_kernel,
        (place, x, gain_one, logr),
        (
            shaped((length, width), bf16),
            shaped((states, SUBS, channels), f32),
            shaped((states, channels), f32),
        ),
        scratch=[pltpu.VMEM((tiles, length, LANES), f32)],
        in_specs=[smem, vmem, vmem, vmem],
        flops=length * channels * states * 64,
    )
    totals = everywhere(total, ("sh", "mq"))
    (context_own,) = call(
        context_kernel,
        (place, normed_one, ends, totals, logr, coef),
        (shaped((length, channels), bf16),),
        scratch=[pltpu.VMEM((tiles, length, LANES), f32)] * 2,
        in_specs=[smem] + [vmem] * 5,
        flops=length * channels * states * 128,
    )
    contexts = team_send([context_own] * team)

    head_piece = shaped((row_count, head_cols), bf16)
    hidden_piece = shaped((row_count, hidden_cols), bf16)
    sizes = (team, col_parts, row_parts)
    head_buffer = pltpu.VMEM((4, row_parts, row_count, col_parts * HD), bf16)
    head_sems = pltpu.SemaphoreType.DMA((col_parts, row_parts, 4))
    kept_shape = shaped((4, length, col_parts * HD), bf16)
    context, attn_part, kept, probs = call(
        functools.partial(attend_kernel, *sizes),
        (place, normed_one, *contexts, *flat(attn_w)),
        (
            shaped((length, width), bf16),
            shaped((length, width), bf16),
            kept_shape,
            shaped((col_parts, length, length), bf16),
        ),
        scratch=[head_buffer, head_sems],
        in_specs=[smem] + [vmem] * (1 + team) + anywhere,
        flops=2 * length * width * head_cols * col_parts,
    )
    attn_parts = team_send([attn_part] * team)

    hidden_buffer = pltpu.VMEM((col_parts, row_parts, row_count, hidden_cols), bf16)
    middle, out_part, two_part, *hidden_grads = call(
        functools.partial(feed_kernel, *sizes),
        (place, x, cot, gain_two, *attn_parts, *flat(up_w), *flat(down_w)),
        (
            shaped((length, width), f32),
            shaped((length, width), bf16),
            shaped((length, width), bf16),
            *[hidden_piece] * (2 * piece_count),
        ),
        scratch=[
            *[hidden_buffer] * 4,
            pltpu.VMEM((length, width), bf16),
            pltpu.VMEM((width, length), bf16),
            pltpu.VMEM((width, length), bf16),
            pltpu.VMEM((length, width), f32),
            pltpu.VMEM((length, width), f32),
            pltpu.SemaphoreType.DMA((4, col_parts, row_parts)),
        ],
        grid=(col_parts,),
        in_specs=[smem, wide, wide, row] + [wide] * team + anywhere * 2,
        out_specs=[wide, wide, wide] + anywhere * 2,
        flops=12 * length * width * hidden_cols * col_parts,
    )
    two_parts = team_send([two_part] * team)

    def rows_of(array, member):
        return lax.dynamic_slice_in_dim(array, member * own_rows, own_rows, 0)

    def share_rows(own_piece, kind):
        pieces = [own_piece]
        count = lax.axis_size(MODEL)
        for unused in range(count - 1):
            pieces.append(along(pieces[-1], MODEL, 1))
        others = []
        if halves == 2:
            for even, odd in zip(pieces[::2], pieces[1::2]):
                others.append(swap(jnp.where(sl == mq, odd, even)))
        (blocks,) = call(
            functools.partial(assemble_kernel, halves, low_count, count),
            (place, *pieces, *others),
            (shaped((seq_total, length, width), kind),),
            in_specs=[smem] + [vmem] * (len(pieces) + len(others)),
        )
        return blocks

    out_pieces = team_send([rows_of(out_part, rank ^ k) for k in range(team)])
    result = rows_of(middle, rank) + sum(item.astype(f32) for item in out_pieces)
    layer_out = share_rows(result.astype(bf16), bf16)

    def own_weight(pieces):
        own = scatter_weight(pieces).reshape(halves, rows_dev, -1)
        if halves == 1:
            return own
        keep = lax.dynamic_index_in_dim(own, sl, 0, keepdims=True)
        other = swap(lax.dynamic_index_in_dim(own, 1 - sl, 0, keepdims=True))
        return in_order(keep, other, 0)

    def out_of_halves(parts):
        return jnp.transpose(parts, (1, 0, 2)).reshape(rows_dev, -1).astype(f32)

    summed_down = out_of_halves(own_weight(nested(hidden_grads[piece_count:]))).T
    summed_up = out_of_halves(own_weight(nested(hidden_grads[:piece_count])))

    middle_grad, gain_two_grad, one_part, *rest = call(
        functools.partial(attend_back_kernel, *sizes),
        (place, middle, gain_two, cot, *two_parts, normed_one, context, kept, probs, *flat(attn_w)),
        (
            shaped((length, width), f32),
            shaped((1, width), f32),
            shaped((length, width), f32),
            *[shaped((length, channels), bf16)] * team,
            *[head_piece] * piece_count,
        ),
        scratch=[
            head_buffer,
            head_buffer,
            pltpu.VMEM((length, width), bf16),
            *[pltpu.VMEM((length, col_parts * HD), bf16)] * 4,
            head_sems,
            head_sems,
        ],
        in_specs=[smem] + [vmem] * (3 + team + 4) + anywhere,
        out_specs=[vmem] * (3 + team) + anywhere,
        flops=4 * length * width * head_cols * col_parts,
    )
    context_grads = team_send(rest[:team])
    halves_attn = own_weight(nested(rest[team:]))
    split_attn = halves_attn.reshape(halves, rows_dev, 4, -1)
    summed_qkv = jnp.stack([out_of_halves(split_attn[:, :, i]) for i in range(3)])
    summed_out = out_of_halves(split_attn[:, :, 3]).T

    context_grad, adjoint_ends, adjoint_total = call(
        functools.partial(adjoint_kernel, team),
        (logr, *context_grads),
        (
            shaped((length, channels), bf16),
            shaped((2, states, SUBS, channels), f32),
            shaped((2, states, channels), f32),
        ),
        scratch=[pltpu.VMEM((tiles, length, LANES), f32)],
        flops=length * channels * states * 128,
    )
    adjoint_totals = everywhere(adjoint_total, ("sh", "mq"))
    *one_pieces, grad_ssm = call(
        functools.partial(context_back_kernel, team),
        (place, context_grad, normed_one, adjoint_ends, adjoint_totals, logr, coef, one_part),
        (
            *[shaped((own_rows, width), bf16)] * team,
            shaped((2, states, channels), f32),
        ),
        scratch=[pltpu.VMEM((tiles, length, LANES), f32)] * 3 + [pltpu.VMEM((length, width), f32)],
        in_specs=[smem] + [vmem] * 7,
        flops=length * channels * states * 256,
    )
    one_pieces = team_send(one_pieces)
    grad_rows, gain_one_grad = call(
        functools.partial(input_grad_kernel, team),
        (place, x, gain_one, middle_grad, *one_pieces),
        (shaped((own_rows, width), bf16), shaped((1, width), f32)),
        in_specs=[smem] + [vmem] * (3 + team),
    )
    input_grad = share_rows(grad_rows, f32)

    placed_ssm = lax.dynamic_update_slice_in_dim(
        jnp.zeros((2 * states, width), f32),
        grad_ssm.reshape(2 * states, channels),
        rank * channels,
        1,
    )
    small_grads = jnp.concatenate([placed_ssm, gain_one_grad, gain_two_grad], 0)
    small_grads = small_grads.reshape(2 * states + 2, lax.axis_size(ALL), -1)
    small_grads = lax.all_to_all(jnp.transpose(small_grads, (1, 0, 2)), ALL, 0, 0, tiled=True)
    small_grads = jnp.sum(small_grads, axis=0)
    summed_ssm = small_grads[: 2 * states].reshape(ssm_param.shape)
    summed_gain = small_grads[2 * states :]

    masters = (w_qkv, w_out, w_up, w_down, norm_gains, ssm_param)
    stacked_flags = (True, False, False, False, True, True)
    grads_all = (summed_qkv, summed_out, summed_up, summed_down, summed_gain, summed_ssm)
    firsts = (first_qkv, first_out, first_up, first_down, first_gain, first_ssm)
    seconds = (second_qkv, second_out, second_up, second_down, second_gain, second_ssm)
    moments = [lamb_moments(*items) for items in zip(masters, grads_all, firsts, seconds)]
    update_sq = square_sums([moment_item[2] for moment_item in moments], stacked_flags)
    weight_sq = square_sums(masters, stacked_flags)
    norms = jnp.sqrt(jnp.sum(everywhere(jnp.stack([weight_sq, update_sq]), ALL), axis=0))
    ratios = norms[0] / norms[1]
    offsets = (0, 3, 4, 5, 6, 8, 10)
    outputs = [layer_out, input_grad]
    for item_index in range(6):
        master = masters[item_index]
        ratio = ratios[offsets[item_index] : offsets[item_index + 1]].reshape(
            (-1,) + (1,) * (master.ndim - 1)
        )
        first_new, second_new, direction = moments[item_index]
        outputs.append(master - learn_rate * ratio * direction)
        outputs.append(first_new)
        if item_index == 4:
            outputs.append(second_new[0])
            outputs.append(second_new[1])
        else:
            outputs.append(second_new)
    outputs.append(norms)
    return tuple(outputs)


def solution(mesh):
    seq_count, model_count = mesh.shape["seq"], mesh.shape["mp"]
    halves = 2 if HEADS // model_count >= 2 else 1
    sizes = (seq_count // halves, halves, SEQS, halves, model_count // (SEQS * halves))
    fine = Mesh(mesh.devices.reshape(sizes), ALL)
    seq, model = ("sh", "sl"), ("mb", "mq", "ml")
    rows_cols, cols_rows = P(seq, model), P(model, seq)
    token = P(None, seq, None)
    stack = P(None, seq, model)
    gains = P(None, ALL)
    ssm = P(None, None, ALL)
    return jax.shard_map(
        on_device,
        mesh=fine,
        in_specs=(token, token, stack, cols_rows, rows_cols, cols_rows, gains, ssm)
        + (stack,) * 2
        + (cols_rows,) * 2
        + (rows_cols,) * 2
        + (cols_rows,) * 2
        + (gains,) * 2
        + (ssm,) * 2,
        out_specs=(token, token)
        + (stack,) * 3
        + (cols_rows,) * 3
        + (rows_cols,) * 3
        + (cols_rows,) * 3
        + (gains, gains, P(ALL), P(ALL))
        + (ssm,) * 3
        + (P(),),
        check_vma=False,
    )
```

```python
import functools
import math

import jax
import jax.numpy as jnp
from jax import lax
from jax.experimental import pallas as pl
from jax.experimental.pallas import tpu as pltpu
from jax.sharding import Mesh
from jax.sharding import PartitionSpec as P

HD = 128
HEADS = 8
BLK = 512
STEP = 10
SEQS = 2
LANES = 128
SUBS = 8

norm_eps = 1e-05
beta_first = 0.9
beta_second = 0.999
lamb_eps = 1e-06
weight_decay = 0.01
learn_rate = 0.5
score_scale = HD ** (-0.5)

f32 = jnp.float32
bf16 = jnp.bfloat16
VMEM_BYTES = 56 * 1024 * 1024

ALL = ("sh", "sl", "mb", "mq", "ml")
MODEL = ("mb", "mq", "ml")
COLS = ("mb", "mq")
TEAM = ("sl", "ml")


def dot(left, right):
    return lax.dot_general(left, right, (((1,), (0,)), ((), ())), preferred_element_type=f32)


def dot_t(left, right):
    return lax.dot_general(left, right, (((1,), (1,)), ((), ())), preferred_element_type=f32)


def normalise(values):
    centred = values - jnp.mean(values, axis=-1, keepdims=True)
    inverse = lax.rsqrt(jnp.mean(centred * centred, axis=-1, keepdims=True) + norm_eps)
    return centred * inverse, inverse


def normalise_back(unit, inverse, grad_unit):
    mean_one = jnp.mean(grad_unit, axis=-1, keepdims=True)
    mean_two = jnp.mean(grad_unit * unit, axis=-1, keepdims=True)
    return inverse * (grad_unit - mean_one - unit * mean_two)


def sub_index():
    return lax.broadcasted_iota(jnp.int32, (SUBS, LANES), 0)


def spread(row):
    return jnp.broadcast_to(row, (SUBS, LANES))


def lane_tile(index):
    return slice(index * LANES, (index + 1) * LANES)


def no_state(tiles):
    rows = tiles[0, :SUBS, :]
    return rows - rows


def fill_tiles(scratch, ref, start):
    for tile in range(scratch.shape[0]):
        lanes = pl.ds(pl.multiple_of(start + tile * LANES, LANES), LANES)
        scratch[tile] = ref[:, lanes].astype(f32)


def norm_kernel(place, x_ref, gain_ref, logr_ref, normed_ref, ends_ref, total_ref, u_tiles):
    unit, unused = normalise(x_ref[...].astype(f32))
    normed_ref[...] = (unit * gain_ref[...]).astype(bf16)
    tiles, length, unused = u_tiles.shape
    states = logr_ref.shape[0]
    span = length // SUBS
    fill_tiles(u_tiles, normed_ref, place[0] * (tiles * LANES))
    left = ((SUBS - 1 - sub_index()) * span).astype(f32)
    for tile in range(tiles):
        rate = jnp.exp(logr_ref[:, lane_tile(tile)])
        decay = jnp.exp(-rate)
        decays = [spread(decay[n : n + 1]) for n in range(states)]

        def step(i, held):
            u = u_tiles[tile, pl.ds(i, SUBS, stride=span), :]
            return tuple(d * h + u for d, h in zip(decays, held))

        zero = no_state(u_tiles)
        held = lax.fori_loop(0, span, step, (zero,) * states, unroll=4)
        for n in range(states):
            ends_ref[n, :, lane_tile(tile)] = held[n]
            total_ref[n : n + 1, lane_tile(tile)] = jnp.sum(
                held[n] * jnp.exp(-left * rate[n : n + 1]), axis=0, keepdims=True
            )


def context_kernel(
    place, normed_ref, ends_ref, all_ref, logr_ref, coef_ref, context_ref, u_tiles, y_tiles
):
    tiles, length, unused = u_tiles.shape
    states = logr_ref.shape[0]
    span = length // SUBS
    fill_tiles(u_tiles, normed_ref, place[0] * (tiles * LANES))
    index = sub_index()
    before = (index * span).astype(f32)
    for tile in range(tiles):
        rate = jnp.exp(logr_ref[:, lane_tile(tile)])
        decay = jnp.exp(-rate)
        scale = coef_ref[:, lane_tile(tile)] * jnp.sqrt(2.0 * rate)
        incoming = jnp.zeros((states, LANES), f32)
        for j in range(all_ref.shape[0]):
            gap = place[1] - 1 - j
            distance = (jnp.maximum(gap, 0) * length).astype(f32)
            term = jnp.exp(-distance * rate) * all_ref[j, :, lane_tile(tile)]
            incoming = incoming + jnp.where(gap >= 0, term, 0.0)
        starts = []
        for n in range(states):
            row = rate[n : n + 1]
            run = ends_ref[n, :, lane_tile(tile)]
            for d in (1, 2, 4):
                moved = jnp.exp(-(d * span) * row) * pltpu.roll(run, d, 0)
                run = run + jnp.where(index >= d, moved, 0.0)
            run = jnp.where(index >= 1, pltpu.roll(run, 1, 0), 0.0)
            starts.append(run + jnp.exp(-before * row) * incoming[n : n + 1])
        decays = [spread(decay[n : n + 1]) for n in range(states)]
        scales = [spread(scale[n : n + 1]) for n in range(states)]

        def step(i, held):
            u = u_tiles[tile, pl.ds(i, SUBS, stride=span), :]
            held = tuple(d * h + u for d, h in zip(decays, held))
            parts = [s * h for s, h in zip(scales, held)]
            while len(parts) > 1:
                parts = [a + b for a, b in zip(parts[::2], parts[1::2])]
            y_tiles[tile, pl.ds(i, SUBS, stride=span), :] = parts[0]
            return held

        lax.fori_loop(0, span, step, tuple(starts), unroll=2)
        context_ref[:, lane_tile(tile)] = y_tiles[tile].astype(bf16)


def whole_rows(block):
    return block.reshape(block.shape[0] * block.shape[1], block.shape[2])


def head(index):
    return slice(index * HD, (index + 1) * HD)


def split_pieces(refs, col_parts, row_parts):
    return [refs[k * row_parts : (k + 1) * row_parts] for k in range(col_parts)]


def head_copies(pieces, buffer, place, sems, inward):
    copies = []
    for k, group in enumerate(pieces):
        for r, piece in enumerate(group):
            for i in range(4):
                outside = piece.at[:, pl.ds(i * HD, HD)]
                inside = buffer.at[i, place[2] ^ r, :, pl.ds(k * HD, HD)]
                ends = (outside, inside) if inward else (inside, outside)
                copies.append(pltpu.make_async_copy(*ends, sems.at[k, r, i]))
    return copies


def attend_kernel(team, col_parts, row_parts, place, normed_ref, *refs):
    contexts, refs = refs[:team], refs[team:]
    count = col_parts * row_parts
    pieces, refs = split_pieces(refs[:count], col_parts, row_parts), refs[count:]
    context_ref, part_ref, kept_ref, probs_ref, weights, sems = refs
    copies = head_copies(pieces, weights, place, sems, True)
    for copy in copies:
        copy.start()
    width = contexts[0].shape[1]
    for k in range(team):
        lanes = pl.ds(pl.multiple_of((place[0] ^ k) * width, LANES), width)
        context_ref[:, lanes] = contexts[k][...]
    for copy in copies:
        copy.wait()
    kept_ref[0] = dot(normed_ref[...], whole_rows(weights[0])).astype(bf16)
    kept_ref[1] = dot(context_ref[...], whole_rows(weights[1])).astype(bf16)
    kept_ref[2] = dot(context_ref[...], whole_rows(weights[2])).astype(bf16)
    length = normed_ref.shape[0]
    rows = lax.broadcasted_iota(jnp.int32, (length, length), 0)
    cols = lax.broadcasted_iota(jnp.int32, (length, length), 1)
    for h in range(col_parts):
        scores = dot_t(kept_ref[0, :, head(h)], kept_ref[1, :, head(h)]) * score_scale
        scores = jnp.where(rows >= cols, scores, -1e30)
        shifted = jnp.exp(scores - jnp.max(scores, axis=-1, keepdims=True))
        inverse = 1.0 / jnp.sum(shifted, axis=-1, keepdims=True)
        probs = (shifted * inverse).astype(bf16)
        probs_ref[h] = probs
        kept_ref[3, :, head(h)] = dot(probs, kept_ref[2, :, head(h)]).astype(bf16)
    part_ref[...] = dot_t(kept_ref[3], whole_rows(weights[3])).astype(bf16)


def feed_kernel(team, col_parts, row_parts, place, x_ref, cot_ref, gain_ref, *refs):
    parts, refs = refs[:team], refs[team:]
    groups = [refs[:row_parts], refs[row_parts : 2 * row_parts]]
    refs = refs[2 * row_parts :]
    middle_ref, out_ref, two_ref = refs[:3]
    refs = refs[3:]
    groups += [refs[:row_parts], refs[row_parts : 2 * row_parts]]
    refs = refs[2 * row_parts :]
    up_all, down_all, grad_up, grad_down, normed, normed_t, cot_t, out_total, two_total, sems = refs
    buffers = (up_all, down_all, grad_up, grad_down)
    z = pl.program_id(0)

    def copies(which, k):
        found = []
        for r, pieces in enumerate(groups[which]):
            inside = buffers[which].at[k, place[2] ^ r]
            ends = (pieces.at[k], inside) if which < 2 else (inside, pieces.at[k])
            found.append(pltpu.make_async_copy(*ends, sems.at[which, k, r]))
        return found

    @pl.when(z == 0)
    def start():
        for k in range(col_parts):
            for copy in copies(0, k) + copies(1, k):
                copy.start()
        attn = parts[0][...].astype(f32)
        for part in parts[1:]:
            attn = attn + part[...].astype(f32)
        middle = x_ref[...].astype(f32) + attn
        middle_ref[...] = middle
        unit, unused = normalise(middle)
        low = (unit * gain_ref[...]).astype(bf16)
        normed[...] = low
        normed_t[...] = low.T
        cot_t[...] = cot_ref[...].T
        out_total[...] = jnp.zeros_like(out_total)
        two_total[...] = jnp.zeros_like(two_total)

    for k in range(col_parts):

        @pl.when(z == k)
        def arrive():
            for copy in copies(0, k) + copies(1, k):
                copy.wait()

    up = whole_rows(up_all[z])
    down = whole_rows(down_all[z])
    hidden = dot(normed[...], up)
    grad_act = dot(cot_ref[...], down)
    cdf = 0.5 * (1.0 + lax.erf(hidden * math.sqrt(0.5)))
    activated = (hidden * cdf).astype(bf16)
    slope = cdf + hidden * jnp.exp(-0.5 * hidden * hidden) * (1.0 / math.sqrt(2.0 * math.pi))
    grad_pre = (grad_act * slope).astype(bf16)
    out_total[...] += dot_t(activated, down)
    two_total[...] += dot_t(grad_pre, up)
    shape = grad_up.shape[1:]
    grad_up[z] = dot(normed_t[...], grad_pre).astype(bf16).reshape(shape)
    grad_down[z] = dot(cot_t[...], activated).astype(bf16).reshape(shape)

    for k in range(col_parts):

        @pl.when(z == k)
        def leave():
            for copy in copies(2, k) + copies(3, k):
                copy.start()

    @pl.when(z == col_parts - 1)
    def finish():
        out_ref[...] = out_total[...].astype(bf16)
        two_ref[...] = two_total[...].astype(bf16)
        for k in range(col_parts):
            for copy in copies(2, k) + copies(3, k):
                copy.wait()


def attend_back_kernel(team, col_parts, row_parts, place, middle_ref, gain_ref, cot_ref, *refs):
    parts, refs = refs[:team], refs[team:]
    normed_ref, context_ref, kept_ref, probs_ref = refs[:4]
    refs = refs[4:]
    count = col_parts * row_parts
    pieces, refs = split_pieces(refs[:count], col_parts, row_parts), refs[count:]
    middle_grad_ref, gain_grad_ref, one_ref = refs[:3]
    refs = refs[3:]
    context_grads, refs = refs[:team], refs[team:]
    near, far, refs = refs[:row_parts], refs[row_parts : 2 * row_parts], refs[2 * row_parts :]
    half = col_parts // 2
    grad_pieces = [[piece.at[k] for piece in near] for k in range(half)]
    grad_pieces += [[piece.at[k] for piece in far] for k in range(half)]
    weights, grads, low, grad_out, grad_q, grad_k, grad_v, sems, out_sems = refs
    copies = head_copies(pieces, weights, place, sems, True)
    for copy in copies:
        copy.start()
    own_rows = middle_ref.shape[0] // team
    grad_two = parts[0][...].astype(f32)
    for part in parts[1:]:
        grad_two = grad_two + part[...].astype(f32)
    unit, inverse = normalise(middle_ref[...])
    grad_gain = grad_two * unit
    rows = lax.broadcasted_iota(jnp.int32, grad_gain.shape, 0)
    first = place[0] * own_rows
    mine = (rows >= first) & (rows < first + own_rows)
    gain_grad_ref[...] = jnp.sum(jnp.where(mine, grad_gain, 0.0), axis=0, keepdims=True)
    grad = cot_ref[...].astype(f32) + normalise_back(unit, inverse, grad_two * gain_ref[...])
    middle_grad_ref[...] = grad
    low[...] = grad.astype(bf16)
    for copy in copies:
        copy.wait()
    grad_out[...] = dot(low[...], whole_rows(weights[3])).astype(bf16)
    for h in range(col_parts):
        q, k, v = (kept_ref[i, :, head(h)] for i in range(3))
        probs = probs_ref[h]
        grad_heads = grad_out[:, head(h)]
        grad_v[:, head(h)] = dot(probs.T, grad_heads).astype(bf16)
        probs = probs.astype(f32)
        grad_probs = dot_t(grad_heads, v)
        inner = jnp.sum(grad_probs * probs, axis=-1, keepdims=True)
        grad_scores = (probs * (grad_probs - inner)).astype(bf16)
        grad_q[:, head(h)] = (dot(grad_scores, k) * score_scale).astype(bf16)
        grad_k[:, head(h)] = (dot(grad_scores.T, q) * score_scale).astype(bf16)
    shape = grads.shape[1:]
    normed_t = normed_ref[...].T
    context_t = context_ref[...].T
    grads[3] = dot(low[...].T, kept_ref[3]).astype(bf16).reshape(shape)
    grads[0] = dot(normed_t, grad_q[...]).astype(bf16).reshape(shape)
    grads[1] = dot(context_t, grad_k[...]).astype(bf16).reshape(shape)
    grads[2] = dot(context_t, grad_v[...]).astype(bf16).reshape(shape)
    copies = head_copies(grad_pieces, grads, place, out_sems, False)
    for copy in copies:
        copy.start()
    total = dot_t(grad_k[...], whole_rows(weights[1])) + dot_t(grad_v[...], whole_rows(weights[2]))
    middle_total = total.astype(bf16)
    low[...] = middle_total
    width = context_grads[0].shape[1]
    for k in range(team):
        lanes = pl.ds(pl.multiple_of((place[0] ^ k) * width, LANES), width)
        context_grads[k][...] = low[:, lanes]
    one_ref[...] = dot_t(grad_q[...], whole_rows(weights[0]))
    for copy in copies:
        copy.wait()


def adjoint_kernel(team, logr_ref, *refs):
    parts = refs[:team]
    grad_ref, ends_ref, total_ref, g_tiles = refs[team:]
    grad = parts[0][...].astype(f32)
    for part in parts[1:]:
        grad = grad + part[...].astype(f32)
    grad_ref[...] = grad.astype(bf16)
    tiles, length, unused = g_tiles.shape
    states = logr_ref.shape[0]
    span = length // SUBS
    fill_tiles(g_tiles, grad_ref, 0)
    before = (sub_index() * span).astype(f32)
    for tile in range(tiles):
        rate = jnp.exp(logr_ref[:, lane_tile(tile)])
        decay = jnp.exp(-rate)
        decays = [spread(decay[n : n + 1]) for n in range(states)]

        def step(i, held):
            g = g_tiles[tile, pl.ds(span - 1 - i, SUBS, stride=span), :]
            later = []
            for d, (b, w) in zip(decays, held):
                shrunk = d * b
                later.append((g + shrunk, d * w + shrunk))
            return tuple(later)

        zero = no_state(g_tiles)
        held = lax.fori_loop(0, span, step, ((zero, zero),) * states, unroll=2)
        for n in range(states):
            b, w = held[n]
            ends_ref[0, n, :, lane_tile(tile)] = b
            ends_ref[1, n, :, lane_tile(tile)] = w
            shrink = jnp.exp(-before * rate[n : n + 1])
            total_ref[0, n : n + 1, lane_tile(tile)] = jnp.sum(shrink * b, axis=0, keepdims=True)
            total_ref[1, n : n + 1, lane_tile(tile)] = jnp.sum(
                shrink * (w + before * b), axis=0, keepdims=True
            )


def context_back_kernel(
    team, place, grad_ref, normed_ref, ends_ref, all_ref, logr_ref, coef_ref, one_ref, *refs
):
    pieces = refs[:team]
    grad_ssm_ref, u_tiles, g_tiles, y_tiles, full = refs[team:]
    tiles, length, unused = u_tiles.shape
    states = logr_ref.shape[0]
    span = length // SUBS
    width = tiles * LANES
    fill_tiles(u_tiles, normed_ref, place[0] * width)
    fill_tiles(g_tiles, grad_ref, 0)
    index = sub_index()
    after = ((SUBS - 1 - index) * span).astype(f32)
    full[...] = one_ref[...]
    group = 8
    for tile in range(tiles):
        lanes = lane_tile(tile)
        rate = jnp.exp(logr_ref[:, lanes])
        decay = jnp.exp(-rate)
        root = jnp.sqrt(2.0 * rate)
        scale = coef_ref[:, lanes] * root
        in_b = jnp.zeros((states, LANES), f32)
        in_w = jnp.zeros((states, LANES), f32)
        for j in range(all_ref.shape[0]):
            gap = j - place[1] - 1
            distance = (jnp.maximum(gap, 0) * length).astype(f32)
            shrink = jnp.exp(-distance * rate)
            b, w = all_ref[j, 0, :, lanes], all_ref[j, 1, :, lanes]
            in_b = in_b + jnp.where(gap >= 0, shrink * b, 0.0)
            in_w = in_w + jnp.where(gap >= 0, shrink * (w + distance * b), 0.0)
        for first in range(0, states, group):
            chosen = range(first, first + group)
            starts = []
            for n in chosen:
                row = rate[n : n + 1]
                b, w = ends_ref[0, n, :, lanes], ends_ref[1, n, :, lanes]
                for d in (1, 2, 4):
                    shrink = jnp.exp(-(d * span) * row)
                    next_b = pltpu.roll(b, SUBS - d, 0)
                    next_w = pltpu.roll(w, SUBS - d, 0)
                    inside = index < SUBS - d
                    b, w = (
                        b + jnp.where(inside, shrink * next_b, 0.0),
                        w + jnp.where(inside, shrink * (next_w + (d * span) * next_b), 0.0),
                    )
                inside = index < SUBS - 1
                b = jnp.where(inside, pltpu.roll(b, SUBS - 1, 0), 0.0)
                w = jnp.where(inside, pltpu.roll(w, SUBS - 1, 0), 0.0)
                shrink = jnp.exp(-after * row)
                b_row, w_row = in_b[n : n + 1], in_w[n : n + 1]
                b = b + shrink * b_row
                w = w + shrink * (w_row + after * b_row)
                zero = no_state(u_tiles)
                starts.append((b, w, zero, zero))
            decays = [spread(decay[n : n + 1]) for n in chosen]
            scales = [spread(scale[n : n + 1]) for n in chosen]

            def step(i, held):
                at = pl.ds(span - 1 - i, SUBS, stride=span)
                g = g_tiles[tile, at, :]
                u = u_tiles[tile, at, :]
                later, parts = [], []
                for d, s, (b, w, sum_b, sum_w) in zip(decays, scales, held):
                    shrunk = d * b
                    w = d * w + shrunk
                    b = g + shrunk
                    later.append((b, w, sum_b + u * b, sum_w + u * w))
                    parts.append(s * b)
                while len(parts) > 1:
                    parts = [p + q for p, q in zip(parts[::2], parts[1::2])]
                if first > 0:
                    parts[0] = parts[0] + y_tiles[tile, at, :]
                y_tiles[tile, at, :] = parts[0]
                return tuple(later)

            held = lax.fori_loop(0, span, step, tuple(starts), unroll=2)
            for n, (unused_b, unused_w, sum_b, sum_w) in zip(chosen, held):
                sum_b = jnp.sum(sum_b, axis=0, keepdims=True)
                sum_w = jnp.sum(sum_w, axis=0, keepdims=True)
                row = slice(n, n + 1)
                grad_ssm_ref[0, row, lanes] = root[row] * sum_b
                grad_ssm_ref[1, row, lanes] = scale[row] * (0.5 * sum_b - rate[row] * sum_w)
        at_lanes = pl.ds(pl.multiple_of(place[0] * width + tile * LANES, LANES), LANES)
        full[:, at_lanes] += y_tiles[tile].astype(bf16).astype(f32)
    rows = pieces[0].shape[0]
    for k in range(team):
        at_rows = pl.ds(pl.multiple_of((place[0] ^ k) * rows, rows), rows)
        pieces[k][...] = full[at_rows, :].astype(bf16)


def input_grad_kernel(team, place, x_ref, gain_ref, middle_grad_ref, *refs):
    parts, (out_ref, gain_grad_ref) = refs[:team], refs[team:]
    rows = out_ref.shape[0]
    at_rows = pl.ds(pl.multiple_of(place[0] * rows, rows), rows)
    grad_one = parts[0][...].astype(f32)
    for part in parts[1:]:
        grad_one = grad_one + part[...].astype(f32)
    unit, inverse = normalise(x_ref[at_rows, :].astype(f32))
    gain_grad_ref[...] = jnp.sum(grad_one * unit, axis=0, keepdims=True)
    back = normalise_back(unit, inverse, grad_one * gain_ref[...])
    out_ref[...] = (middle_grad_ref[at_rows, :] + back).astype(bf16)


def assemble_kernel(halves, low_count, place, own_ref, *refs):
    others, out_ref = refs[:-1], refs[-1]
    count, rows, unused = own_ref.shape
    half = place[4]

    def put(value, sequence, which, member):
        at_rows = pl.ds(pl.multiple_of((which * low_count + member) * rows, rows), rows)
        out_ref[sequence, at_rows, :] = value.astype(out_ref.dtype)

    for sequence in range(count // (halves * low_count)):
        if halves == 1:
            for member in range(low_count):
                put(own_ref[sequence * low_count + member], sequence, 0, member)
        else:
            put(own_ref[sequence * halves + half], sequence, half, 0)
            put(others[0][sequence], sequence, 1 - half, 0)


def pack_kernel(halves, place, qkv_ref, out_ref, up_ref, down_ref, *refs):
    rows = up_ref.shape[0]
    heads, hidden = out_ref.shape[0] // halves, up_ref.shape[1] // halves
    for which in range(halves):
        side = place[4] if which == 0 else 1 - place[4]
        at_heads = pl.ds(pl.multiple_of(side * heads, LANES), heads)
        at_hidden = pl.ds(pl.multiple_of(side * hidden, LANES), hidden)
        if which == 0:
            head_ref, wide_ref, deep_ref = refs[:3]
        else:
            packed = refs[3]
            head_ref = packed.at[:, : 4 * heads]
            wide_ref = packed.at[:, 4 * heads : 4 * heads + hidden]
            deep_ref = packed.at[:, 4 * heads + hidden :]
        for i in range(3):
            head_ref[:, i * heads : (i + 1) * heads] = qkv_ref[i, :, at_heads].astype(bf16)
        head_ref[:, 3 * heads :] = out_ref[at_heads, :].T.astype(bf16)
        wide_ref[...] = up_ref[:, at_hidden].astype(bf16)
        deep_ref[...] = down_ref[at_hidden, :].T.astype(bf16)


def lamb_moments(weight, grad_item, first_old, second_old):
    first_new = beta_first * first_old + (1.0 - beta_first) * grad_item
    second_new = beta_second * second_old + (1.0 - beta_second) * grad_item * grad_item
    direction = (
        first_new
        / (1.0 - beta_first**STEP)
        / (jnp.sqrt(second_new / (1.0 - beta_second**STEP)) + lamb_eps)
        + weight_decay * weight
    )
    return (first_new, second_new, direction)


def place_sums(sums_ref, sums):
    rows = lax.broadcasted_iota(jnp.int32, sums_ref.shape, 0)
    lanes = lax.broadcasted_iota(jnp.int32, sums_ref.shape, 1)
    found = jnp.zeros(sums_ref.shape, f32)
    for index, pair in sums.items():
        for row, value in enumerate(pair):
            found = jnp.where((rows == row) & (lanes == index), value, found)
    sums_ref[...] = found


def moments_kernel(halves, matrices, place, *refs):
    count = 1 + max(item[1] for item in matrices)
    grads, refs = [refs[halves * i : halves * (i + 1)] for i in range(count)], refs[halves * count :]
    arrays = len({(item[1], item[4] is None) for item in matrices})
    ins = [refs[3 * i : 3 * i + 3] for i in range(arrays)]
    outs = [refs[3 * (arrays + i) : 3 * (arrays + i) + 3] for i in range(arrays)]
    sums_ref = refs[6 * arrays]
    keys = []
    sums = {}
    for number, source, column, turned, stacked in matrices:
        key = (source, stacked is None)
        if key not in keys:
            keys.append(key)
        pick = (lambda ref: ref) if stacked is None else (lambda ref, i=stacked: ref.at[i])
        weight, first, second = (pick(ref) for ref in ins[keys.index(key)])
        news = [pick(ref) for ref in outs[keys.index(key)]]
        width = weight.shape[0 if turned else 1] // halves
        rows = weight.shape[1 if turned else 0]
        cols = slice(column * width, (column + 1) * width)
        total_weight = total_update = 0.0
        for which, grad_ref in enumerate(grads[source]):
            side = place[4] if which == 0 else 1 - place[4]
            at = pl.ds(pl.multiple_of(side * width, width), width)
            if which == 0:
                grad = grad_ref[pl.ds(pl.multiple_of(side * rows, rows), rows), cols].astype(f32)
            else:
                grad = grad_ref[:, cols].astype(f32)
            at = (at, slice(None)) if turned else (slice(None), at)
            grad = grad.T if turned else grad
            old = weight[at]
            found = lamb_moments(old, grad, first[at], second[at])
            for ref, value in zip(news, found):
                ref[at] = value
            total_weight = total_weight + jnp.sum(old * old)
            total_update = total_update + jnp.sum(found[2] * found[2])
        sums[number] = (total_weight, total_update)
    place_sums(sums_ref, sums)


def small_moments_kernel(numbers, grads_ref, *refs):
    ins, outs, sums_ref = (refs[:3], refs[3:6]), (refs[6:9], refs[9:12]), refs[12]
    states = (grads_ref.shape[0] - 2) // 2
    sums = {}
    for (weight, first, second), news, start, rows, first_number in (
        (ins[0], outs[0], 2 * states, 1, numbers[0]),
        (ins[1], outs[1], 0, states, numbers[1]),
    ):
        for i in range(2):
            grad = grads_ref[start + i * rows : start + (i + 1) * rows, :]
            at = slice(i * rows, (i + 1) * rows)
            found = lamb_moments(weight[at, :], grad, first[at, :], second[at, :])
            for ref, value in zip(news, found):
                ref[at, :] = value
            sums[first_number + i] = (
                jnp.sum(weight[at, :] * weight[at, :]),
                jnp.sum(found[2] * found[2]),
            )
    place_sums(sums_ref, sums)


def update_kernel(stacks, sums_ref, *refs):
    count = len(stacks)
    weights, directions, news = refs[:count], refs[count : 2 * count], refs[2 * count : 3 * count]
    norms = jnp.sqrt(jnp.sum(sums_ref[...], axis=0))
    refs[3 * count][...] = norms
    ratios = norms[0:1] / norms[1:2]
    lanes = lax.broadcasted_iota(jnp.int32, ratios.shape, 1)
    for numbers, weight, direction, new in zip(stacks, weights, directions, news):
        step = weight.shape[0] // len(numbers)
        for i, number in enumerate(numbers):
            ratio = jnp.sum(jnp.where(lanes == number, ratios, 0.0), axis=1, keepdims=True)
            at = slice(i * step, (i + 1) * step)
            scale = learn_rate * ratio.reshape((1,) * weight.ndim)
            new[at] = weight[at] - scale * direction[at]


def call(body, ins, outs, scratch=(), grid=None, in_specs=None, out_specs=None, flops=0):
    moved = sum(a.size * a.dtype.itemsize for a in list(ins) + list(outs))
    params = pltpu.CompilerParams(vmem_limit_bytes=VMEM_BYTES)
    cost = pl.CostEstimate(flops=flops, bytes_accessed=moved, transcendentals=0)
    whole = pl.BlockSpec(memory_space=pltpu.VMEM)
    extra = {}
    if grid is not None:
        extra["grid"] = grid
    return pl.pallas_call(
        body,
        out_shape=tuple(outs),
        in_specs=in_specs or [whole for unused in ins],
        out_specs=tuple(out_specs or [whole for unused in outs]),
        scratch_shapes=list(scratch),
        compiler_params=params,
        cost_estimate=cost,
        **extra,
    )(*ins)


def shaped(shape, kind):
    return jax.ShapeDtypeStruct(tuple(shape), kind)


def on_device(
    tokens,
    cotangent,
    w_qkv,
    w_out,
    w_up,
    w_down,
    norm_gains,
    ssm_param,
    first_qkv,
    second_qkv,
    first_out,
    second_out,
    first_up,
    second_up,
    first_down,
    second_down,
    first_gain,
    second_gain,
    first_ssm,
    second_ssm,
):
    halves = lax.axis_size("sl")
    low_count = lax.axis_size("ml")
    row_parts = lax.axis_size("sh")
    col_parts = lax.axis_size("mb") * lax.axis_size("mq")
    team = halves * low_count
    sl, ml, mb, mq = (lax.axis_index(name) for name in ("sl", "ml", "mb", "mq"))
    rank = sl * low_count + ml
    block_index = lax.axis_index("sh") * halves + mq
    seq_total, length, width = tokens.shape
    assert length == BLK and seq_total == lax.axis_size("mb")
    states = ssm_param.shape[1]
    channels = width // team
    tiles = channels // LANES
    row_count = width // row_parts
    own_rows = length // team
    place = [rank, block_index, lax.axis_index("sh"), lax.axis_index(MODEL), sl, sl ^ mq]
    place = jnp.stack(place).astype(jnp.int32)
    smem = pl.BlockSpec(memory_space=pltpu.SMEM)
    vmem = pl.BlockSpec(memory_space=pltpu.VMEM)

    def permute(value, axes, moves):
        return lax.ppermute(value, axes, moves)

    def swap(value):
        return permute(value, "sl", [(0, 1), (1, 0)])

    def in_order(own, other, axis):
        return jnp.where(
            sl == 0, jnp.concatenate([own, other], axis), jnp.concatenate([other, own], axis)
        )

    def team_send(pieces):
        moved = [pieces[0]]
        for k in range(1, team):
            moved.append(permute(pieces[k], TEAM, [(i, i ^ k) for i in range(team)]))
        return moved

    def pick_block(array):
        own = lax.dynamic_index_in_dim(array, mb, 0, keepdims=False)
        if halves == 1:
            return own
        return jnp.where(sl == mq, own, swap(own))

    def across(value, bit):
        return permute(value, "sh", [(i, i ^ bit) for i in range(row_parts)])

    def along(value, axes, step):
        count = lax.axis_size(axes)
        return permute(value, axes, [(i, (i + step) % count) for i in range(count)])

    bits = [1 << i for i in range(row_parts.bit_length() - 1)]

    def bit_order(k):
        return bits if k % 2 == 0 else bits[::-1]

    def double_rows(value, order):
        found = {0: value}
        for bit in order:
            for r in list(found):
                found[r | bit] = across(found[r], bit)
        return [found[r] for r in range(row_parts)]

    def add(*items):
        return sum(item.astype(f32) for item in items).astype(bf16)

    def halve_rows(pieces, order):
        sums = {r: [piece] for r, piece in enumerate(pieces)}
        for bit in reversed(order):
            for r in [r for r in sums if r & bit]:
                sums[r ^ bit].append(across(add(*sums.pop(r)), bit))
        return add(*sums[0])

    def ring_gather(shard):
        pieces, held = [], shard
        for k in range(col_parts):
            if k > 0:
                held = along(held, COLS, 1)
            pieces.append(double_rows(held, bits if k % 2 == 0 else bits[::-1]))
        return pieces

    def ring_sum(near, far):
        held = None
        for stack in (far, near):
            for k in reversed(range(stack.shape[0])):
                held = stack[k] if held is None else add(stack[k], along(held, COLS, -1))
        return held

    def everywhere(value, axes):
        count = lax.axis_size(axes)
        copies = jnp.broadcast_to(value[None], (count, *value.shape))
        return lax.all_to_all(copies, axes, 0, 0, tiled=True)

    small = jnp.concatenate([ssm_param.reshape(2 * states, -1), norm_gains], 0)
    small = jnp.transpose(everywhere(small, ALL), (1, 0, 2)).reshape(2 * states + 2, width)
    own_ssm = lax.dynamic_slice_in_dim(
        small[: 2 * states].reshape(2, states, width), rank * channels, channels, 2
    )
    coef, logr = own_ssm[0], own_ssm[1]
    gain_one = small[2 * states : 2 * states + 1]
    gain_two = small[2 * states + 1 : 2 * states + 2]

    rows_dev = w_up.shape[0]
    hidden_cols = w_up.shape[1] // halves
    head_cols = 4 * w_out.shape[0] // halves
    sides = [shaped((rows_dev, cols), bf16) for cols in (head_cols, hidden_cols, hidden_cols)]
    packed_cols = head_cols + 2 * hidden_cols
    shards = call(
        functools.partial(pack_kernel, halves),
        (place, w_qkv, w_out, w_up, w_down),
        sides + [shaped((rows_dev, packed_cols), bf16)] * (halves - 1),
        in_specs=[smem] + [vmem] * 4,
    )
    if halves == 2:
        other = swap(shards[3])
        cuts = (0, head_cols, head_cols + hidden_cols, packed_cols)
        shards = [
            in_order(own, other[:, first:last], 0)
            for own, first, last in zip(shards, cuts, cuts[1:])
        ]
    head_shard, up_shard, down_shard = shards[:3]
    attn_w = ring_gather(head_shard)
    up_w = double_rows(lax.all_gather(up_shard, COLS, axis=0, tiled=False), bits)
    down_w = double_rows(lax.all_gather(down_shard, COLS, axis=0, tiled=False), bits[::-1])

    x = pick_block(tokens)
    cot = pick_block(cotangent)

    def flat(pieces):
        return [piece for group in pieces for piece in group]

    piece_count = row_parts * col_parts
    anywhere = [pl.BlockSpec(memory_space=pl.ANY)]

    def fixed(*shape):
        return pl.BlockSpec(shape, lambda z: (0,) * len(shape))

    wide = fixed(length, width)
    row = fixed(1, width)

    normed_one, ends, total = call(
        norm_kernel,
        (place, x, gain_one, logr),
        (
            shaped((length, width), bf16),
            shaped((states, SUBS, channels), f32),
            shaped((states, channels), f32),
        ),
        scratch=[pltpu.VMEM((tiles, length, LANES), f32)],
        in_specs=[smem, vmem, vmem, vmem],
        flops=length * channels * states * 64,
    )
    totals = everywhere(total, ("sh", "mq"))
    (context_own,) = call(
        context_kernel,
        (place, normed_one, ends, totals, logr, coef),
        (shaped((length, channels), bf16),),
        scratch=[pltpu.VMEM((tiles, length, LANES), f32)] * 2,
        in_specs=[smem] + [vmem] * 5,
        flops=length * channels * states * 128,
    )
    contexts = team_send([context_own] * team)

    head_piece = shaped((col_parts // 2, row_count, head_cols), bf16)
    hidden_piece = shaped((col_parts, row_count, hidden_cols), bf16)
    sizes = (team, col_parts, row_parts)
    head_buffer = pltpu.VMEM((4, row_parts, row_count, col_parts * HD), bf16)
    head_sems = pltpu.SemaphoreType.DMA((col_parts, row_parts, 4))
    kept_shape = shaped((4, length, col_parts * HD), bf16)
    context, attn_part, kept, probs = call(
        functools.partial(attend_kernel, *sizes),
        (place, normed_one, *contexts, *flat(attn_w)),
        (
            shaped((length, width), bf16),
            shaped((length, width), bf16),
            kept_shape,
            shaped((col_parts, length, length), bf16),
        ),
        scratch=[head_buffer, head_sems],
        in_specs=[smem] + [vmem] * (1 + team) + anywhere * piece_count,
        flops=2 * length * width * head_cols * col_parts,
    )
    attn_parts = team_send([attn_part] * team)

    hidden_buffer = pltpu.VMEM((col_parts, row_parts, row_count, hidden_cols), bf16)
    middle, out_part, two_part, *hidden_grads = call(
        functools.partial(feed_kernel, *sizes),
        (place, x, cot, gain_two, *attn_parts, *up_w, *down_w),
        (
            shaped((length, width), f32),
            shaped((length, width), bf16),
            shaped((length, width), bf16),
            *[hidden_piece] * (2 * row_parts),
        ),
        scratch=[
            *[hidden_buffer] * 4,
            pltpu.VMEM((length, width), bf16),
            pltpu.VMEM((width, length), bf16),
            pltpu.VMEM((width, length), bf16),
            pltpu.VMEM((length, width), f32),
            pltpu.VMEM((length, width), f32),
            pltpu.SemaphoreType.DMA((4, col_parts, row_parts)),
        ],
        grid=(col_parts,),
        in_specs=[smem, wide, wide, row] + [wide] * team + anywhere * (2 * row_parts),
        out_specs=[wide, wide, wide] + anywhere * (2 * row_parts),
        flops=12 * length * width * hidden_cols * col_parts,
    )
    two_parts = team_send([two_part] * team)

    def rows_of(array, member):
        return lax.dynamic_slice_in_dim(array, member * own_rows, own_rows, 0)

    def share_rows(own_piece, kind):
        pieces = lax.all_gather(own_piece, MODEL, axis=0, tiled=False)
        others = []
        if halves == 2:
            pairs = pieces.reshape(seq_total, halves, own_rows, width)
            others = [swap(lax.dynamic_index_in_dim(pairs, 1 - sl, 1, keepdims=False))]
        (blocks,) = call(
            functools.partial(assemble_kernel, halves, low_count),
            (place, pieces, *others),
            (shaped((seq_total, length, width), kind),),
            in_specs=[smem, vmem] + [vmem] * len(others),
        )
        return blocks

    out_pieces = team_send([rows_of(out_part, rank ^ k) for k in range(team)])
    result = rows_of(middle, rank) + sum(item.astype(f32) for item in out_pieces)
    layer_out = share_rows(result.astype(bf16), bf16)

    def both_halves(own):
        if halves == 1:
            return [own]
        return [own, swap(lax.dynamic_slice_in_dim(own, (1 - sl) * rows_dev, rows_dev, 0))]

    def sum_over_z(stack):
        return lax.psum_scatter(stack, COLS, scatter_dimension=0, tiled=False)

    grad_up = sum_over_z(halve_rows(hidden_grads[:row_parts], bits))
    grad_down = sum_over_z(halve_rows(hidden_grads[row_parts:], bits[::-1]))

    middle_grad, gain_two_grad, one_part, *rest = call(
        functools.partial(attend_back_kernel, *sizes),
        (place, middle, gain_two, cot, *two_parts, normed_one, context, kept, probs, *flat(attn_w)),
        (
            shaped((length, width), f32),
            shaped((1, width), f32),
            shaped((length, width), f32),
            *[shaped((length, channels), bf16)] * team,
            *[head_piece] * (2 * row_parts),
        ),
        scratch=[
            head_buffer,
            head_buffer,
            pltpu.VMEM((length, width), bf16),
            *[pltpu.VMEM((length, col_parts * HD), bf16)] * 4,
            head_sems,
            head_sems,
        ],
        in_specs=[smem] + [vmem] * (3 + team + 4) + anywhere * piece_count,
        out_specs=[vmem] * (3 + team) + anywhere * (2 * row_parts),
        flops=4 * length * width * head_cols * col_parts,
    )
    context_grads = team_send(rest[:team])
    far = halve_rows(rest[team + row_parts :], bits[::-1])
    near = halve_rows(rest[team : team + row_parts], bits)
    grad_heads = ring_sum(near, far)

    context_grad, adjoint_ends, adjoint_total = call(
        functools.partial(adjoint_kernel, team),
        (logr, *context_grads),
        (
            shaped((length, channels), bf16),
            shaped((2, states, SUBS, channels), f32),
            shaped((2, states, channels), f32),
        ),
        scratch=[pltpu.VMEM((tiles, length, LANES), f32)],
        flops=length * channels * states * 128,
    )
    adjoint_totals = everywhere(adjoint_total, ("sh", "mq"))
    *one_pieces, grad_ssm = call(
        functools.partial(context_back_kernel, team),
        (place, context_grad, normed_one, adjoint_ends, adjoint_totals, logr, coef, one_part),
        (
            *[shaped((own_rows, width), bf16)] * team,
            shaped((2, states, channels), f32),
        ),
        scratch=[pltpu.VMEM((tiles, length, LANES), f32)] * 3 + [pltpu.VMEM((length, width), f32)],
        in_specs=[smem] + [vmem] * 7,
        flops=length * channels * states * 256,
    )
    one_pieces = team_send(one_pieces)
    grad_rows, gain_one_grad = call(
        functools.partial(input_grad_kernel, team),
        (place, x, gain_one, middle_grad, *one_pieces),
        (shaped((own_rows, width), bf16), shaped((1, width), f32)),
        in_specs=[smem] + [vmem] * (3 + team),
    )
    input_grad = share_rows(grad_rows, f32)

    placed_ssm = lax.dynamic_update_slice_in_dim(
        jnp.zeros((2 * states, width), f32),
        grad_ssm.reshape(2 * states, channels),
        rank * channels,
        1,
    )
    small_grads = jnp.concatenate([placed_ssm, gain_one_grad, gain_two_grad], 0)
    small_grads = small_grads.reshape(2 * states + 2, lax.axis_size(ALL), -1)
    small_grads = lax.all_to_all(jnp.transpose(small_grads, (1, 0, 2)), ALL, 0, 0, tiled=True)
    small_grads = jnp.sum(small_grads, axis=0)

    def moments(matrices, grads, arrays):
        changed = [shaped(old.shape, f32) for group in arrays for old in group]
        grad_parts = [part for grad in grads for part in both_halves(grad)]
        ins = [item for group in arrays for item in group]
        *found, sums = call(
            functools.partial(moments_kernel, halves, matrices),
            (place, *grad_parts, *ins),
            (*changed, shaped((2, LANES), f32)),
            in_specs=[smem] + [vmem] * (len(grad_parts) + len(ins)),
        )
        return [found[3 * i : 3 * i + 3] for i in range(len(arrays))], sums

    hidden_new, hidden_sums = moments(
        ((4, 0, 0, False, None), (5, 1, 0, True, None)),
        (grad_up, grad_down),
        ((w_up, first_up, second_up), (w_down, first_down, second_down)),
    )
    heads_new, head_sums = moments(
        tuple((i, 0, i, False, i) for i in range(3)) + ((3, 0, 3, True, None),),
        (grad_heads,),
        ((w_qkv, first_qkv, second_qkv), (w_out, first_out, second_out)),
    )
    own_channels = norm_gains.shape[1]
    ssm_items = [item.reshape(2 * states, own_channels) for item in (ssm_param, first_ssm, second_ssm)]
    small_items = [norm_gains, first_gain, second_gain, *ssm_items]
    *small_new, small_sums = call(
        functools.partial(small_moments_kernel, (6, 8)),
        (small_grads.reshape(2 * states + 2, own_channels), *small_items),
        (*[shaped(item.shape, f32) for item in small_items], shaped((2, LANES), f32)),
    )
    all_sums = everywhere(hidden_sums + head_sums + small_sums, ALL)
    masters = (w_qkv, w_out, w_up, w_down, norm_gains, ssm_items[0])
    news = (*heads_new, *hidden_new, small_new[:3], small_new[3:])
    *weights, norms = call(
        functools.partial(update_kernel, ((0, 1, 2), (3,), (4,), (5,), (6, 7), (8, 9))),
        (all_sums, *masters, *[group[2] for group in news]),
        (*[shaped(item.shape, f32) for item in masters], shaped((2, LANES), f32)),
    )
    outputs = [layer_out, input_grad]
    for index, (weight, (first_new, second_new, unused)) in enumerate(zip(weights, news)):
        if index == 4:
            outputs += [weight, first_new, second_new[0], second_new[1]]
        else:
            kept_shape = ssm_param.shape if index == 5 else weight.shape
            outputs += [item.reshape(kept_shape) for item in (weight, first_new, second_new)]
    outputs.append(norms[:, :10])
    return tuple(outputs)


def solution(mesh):
    seq_count, model_count = mesh.shape["seq"], mesh.shape["mp"]
    halves = 2 if HEADS // model_count >= 2 else 1
    sizes = (seq_count // halves, halves, SEQS, halves, model_count // (SEQS * halves))
    fine = Mesh(mesh.devices.reshape(sizes), ALL)
    seq, model = ("sh", "sl"), ("mb", "mq", "ml")
    rows_cols, cols_rows = P(seq, model), P(model, seq)
    token = P(None, seq, None)
    stack = P(None, seq, model)
    gains = P(None, ALL)
    ssm = P(None, None, ALL)
    return jax.shard_map(
        on_device,
        mesh=fine,
        in_specs=(token, token, stack, cols_rows, rows_cols, cols_rows, gains, ssm)
        + (stack,) * 2
        + (cols_rows,) * 2
        + (rows_cols,) * 2
        + (cols_rows,) * 2
        + (gains,) * 2
        + (ssm,) * 2,
        out_specs=(token, token)
        + (stack,) * 3
        + (cols_rows,) * 3
        + (rows_cols,) * 3
        + (cols_rows,) * 3
        + (gains, gains, P(ALL), P(ALL))
        + (ssm,) * 3
        + (P(),),
        check_vma=False,
    )
```

```python
import functools
import math

import jax
import jax.numpy as jnp
from jax import lax
from jax.experimental import pallas as pl
from jax.experimental.pallas import tpu as pltpu
from jax.sharding import Mesh
from jax.sharding import PartitionSpec as P

HD = 128
HEADS = 8
BLK = 512
STEP = 10
SEQS = 2
LANES = 128
SUBS = 8

norm_eps = 1e-05
beta_first = 0.9
beta_second = 0.999
lamb_eps = 1e-06
weight_decay = 0.01
learn_rate = 0.5
score_scale = HD ** (-0.5)

f32 = jnp.float32
bf16 = jnp.bfloat16
VMEM_BYTES = 56 * 1024 * 1024

ALL = ("sh", "sl", "mb", "mq", "ml")
MODEL = ("mb", "mq", "ml")
COLS = ("mb", "mq")
TEAM = ("sl", "ml")


def dot(left, right):
    return lax.dot_general(left, right, (((1,), (0,)), ((), ())), preferred_element_type=f32)


def dot_t(left, right):
    return lax.dot_general(left, right, (((1,), (1,)), ((), ())), preferred_element_type=f32)


def normalise(values):
    centred = values - jnp.mean(values, axis=-1, keepdims=True)
    inverse = lax.rsqrt(jnp.mean(centred * centred, axis=-1, keepdims=True) + norm_eps)
    return centred * inverse, inverse


def normalise_back(unit, inverse, grad_unit):
    mean_one = jnp.mean(grad_unit, axis=-1, keepdims=True)
    mean_two = jnp.mean(grad_unit * unit, axis=-1, keepdims=True)
    return inverse * (grad_unit - mean_one - unit * mean_two)


def sub_index():
    return lax.broadcasted_iota(jnp.int32, (SUBS, LANES), 0)


def spread(row):
    return jnp.broadcast_to(row, (SUBS, LANES))


def lane_tile(index):
    return slice(index * LANES, (index + 1) * LANES)


def no_state(tiles):
    rows = tiles[0, :SUBS, :]
    return rows - rows


def fill_tiles(scratch, ref, start):
    for tile in range(scratch.shape[0]):
        lanes = pl.ds(pl.multiple_of(start + tile * LANES, LANES), LANES)
        scratch[tile] = ref[:, lanes].astype(f32)


def norm_kernel(place, x_ref, gain_ref, logr_ref, normed_ref, ends_ref, total_ref, u_tiles):
    unit, unused = normalise(x_ref[...].astype(f32))
    normed_ref[...] = (unit * gain_ref[...]).astype(bf16)
    tiles, length, unused = u_tiles.shape
    states = logr_ref.shape[0]
    span = length // SUBS
    fill_tiles(u_tiles, normed_ref, place[0] * (tiles * LANES))
    left = ((SUBS - 1 - sub_index()) * span).astype(f32)
    for tile in range(tiles):
        rate = jnp.exp(logr_ref[:, lane_tile(tile)])
        decay = jnp.exp(-rate)
        decays = [spread(decay[n : n + 1]) for n in range(states)]

        def step(i, held):
            u = u_tiles[tile, pl.ds(i, SUBS, stride=span), :]
            return tuple(d * h + u for d, h in zip(decays, held))

        zero = no_state(u_tiles)
        held = lax.fori_loop(0, span, step, (zero,) * states, unroll=4)
        for n in range(states):
            ends_ref[n, :, lane_tile(tile)] = held[n]
            total_ref[n : n + 1, lane_tile(tile)] = jnp.sum(
                held[n] * jnp.exp(-left * rate[n : n + 1]), axis=0, keepdims=True
            )


def context_kernel(
    place, normed_ref, ends_ref, all_ref, logr_ref, coef_ref, context_ref, u_tiles, y_tiles
):
    tiles, length, unused = u_tiles.shape
    states = logr_ref.shape[0]
    span = length // SUBS
    fill_tiles(u_tiles, normed_ref, place[0] * (tiles * LANES))
    index = sub_index()
    before = (index * span).astype(f32)
    for tile in range(tiles):
        rate = jnp.exp(logr_ref[:, lane_tile(tile)])
        decay = jnp.exp(-rate)
        scale = coef_ref[:, lane_tile(tile)] * jnp.sqrt(2.0 * rate)
        incoming = jnp.zeros((states, LANES), f32)
        for j in range(all_ref.shape[0]):
            gap = place[1] - 1 - j
            distance = (jnp.maximum(gap, 0) * length).astype(f32)
            term = jnp.exp(-distance * rate) * all_ref[j, :, lane_tile(tile)]
            incoming = incoming + jnp.where(gap >= 0, term, 0.0)
        starts = []
        for n in range(states):
            row = rate[n : n + 1]
            run = ends_ref[n, :, lane_tile(tile)]
            for d in (1, 2, 4):
                moved = jnp.exp(-(d * span) * row) * pltpu.roll(run, d, 0)
                run = run + jnp.where(index >= d, moved, 0.0)
            run = jnp.where(index >= 1, pltpu.roll(run, 1, 0), 0.0)
            starts.append(run + jnp.exp(-before * row) * incoming[n : n + 1])
        decays = [spread(decay[n : n + 1]) for n in range(states)]
        scales = [spread(scale[n : n + 1]) for n in range(states)]

        def step(i, held):
            u = u_tiles[tile, pl.ds(i, SUBS, stride=span), :]
            held = tuple(d * h + u for d, h in zip(decays, held))
            parts = [s * h for s, h in zip(scales, held)]
            while len(parts) > 1:
                parts = [a + b for a, b in zip(parts[::2], parts[1::2])]
            y_tiles[tile, pl.ds(i, SUBS, stride=span), :] = parts[0]
            return held

        lax.fori_loop(0, span, step, tuple(starts), unroll=2)
        context_ref[:, lane_tile(tile)] = y_tiles[tile].astype(bf16)


def whole_rows(block):
    return block.reshape(block.shape[0] * block.shape[1], block.shape[2])


def head(index):
    return slice(index * HD, (index + 1) * HD)


def split_pieces(refs, col_parts, row_parts):
    return [refs[k * row_parts : (k + 1) * row_parts] for k in range(col_parts)]


def head_copies(pieces, buffer, place, sems, inward):
    copies = []
    for k, group in enumerate(pieces):
        for r, piece in enumerate(group):
            for i in range(4):
                outside = piece.at[:, pl.ds(i * HD, HD)]
                inside = buffer.at[i, place[2] ^ r, :, pl.ds(k * HD, HD)]
                ends = (outside, inside) if inward else (inside, outside)
                copies.append(pltpu.make_async_copy(*ends, sems.at[k, r, i]))
    return copies


def attend_kernel(team, col_parts, row_parts, place, normed_ref, *refs):
    contexts, refs = refs[:team], refs[team:]
    count = col_parts * row_parts
    pieces, refs = split_pieces(refs[:count], col_parts, row_parts), refs[count:]
    context_ref, part_ref, kept_ref, probs_ref, weights, sems = refs
    copies = head_copies(pieces, weights, place, sems, True)
    for copy in copies:
        copy.start()
    width = contexts[0].shape[1]
    for k in range(team):
        lanes = pl.ds(pl.multiple_of((place[0] ^ k) * width, LANES), width)
        context_ref[:, lanes] = contexts[k][...]
    for copy in copies:
        copy.wait()
    kept_ref[0] = dot(normed_ref[...], whole_rows(weights[0])).astype(bf16)
    kept_ref[1] = dot(context_ref[...], whole_rows(weights[1])).astype(bf16)
    kept_ref[2] = dot(context_ref[...], whole_rows(weights[2])).astype(bf16)
    length = normed_ref.shape[0]
    rows = lax.broadcasted_iota(jnp.int32, (length, length), 0)
    cols = lax.broadcasted_iota(jnp.int32, (length, length), 1)
    for h in range(col_parts):
        scores = dot_t(kept_ref[0, :, head(h)], kept_ref[1, :, head(h)]) * score_scale
        scores = jnp.where(rows >= cols, scores, -1e30)
        shifted = jnp.exp(scores - jnp.max(scores, axis=-1, keepdims=True))
        inverse = 1.0 / jnp.sum(shifted, axis=-1, keepdims=True)
        probs = (shifted * inverse).astype(bf16)
        probs_ref[h] = probs
        kept_ref[3, :, head(h)] = dot(probs, kept_ref[2, :, head(h)]).astype(bf16)
    part_ref[...] = dot_t(kept_ref[3], whole_rows(weights[3])).astype(bf16)


def feed_kernel(team, col_parts, row_parts, place, x_ref, cot_ref, gain_ref, *refs):
    parts, refs = refs[:team], refs[team:]
    groups = [refs[:row_parts], refs[row_parts : 2 * row_parts]]
    refs = refs[2 * row_parts :]
    middle_ref, out_ref, two_ref = refs[:3]
    refs = refs[3:]
    groups += [refs[:row_parts], refs[row_parts : 2 * row_parts]]
    refs = refs[2 * row_parts :]
    up_all, down_all, grad_up, grad_down, normed, normed_t, cot_t, out_total, two_total, sems = refs
    buffers = (up_all, down_all, grad_up, grad_down)
    z = pl.program_id(0)

    def copies(which, k):
        found = []
        for r, pieces in enumerate(groups[which]):
            inside = buffers[which].at[k, place[2] ^ r]
            ends = (pieces.at[k], inside) if which < 2 else (inside, pieces.at[k])
            found.append(pltpu.make_async_copy(*ends, sems.at[which, k, r]))
        return found

    @pl.when(z == 0)
    def start():
        for k in range(col_parts):
            for copy in copies(0, k) + copies(1, k):
                copy.start()
        attn = parts[0][...].astype(f32)
        for part in parts[1:]:
            attn = attn + part[...].astype(f32)
        middle = x_ref[...].astype(f32) + attn
        middle_ref[...] = middle
        unit, unused = normalise(middle)
        low = (unit * gain_ref[...]).astype(bf16)
        normed[...] = low
        normed_t[...] = low.T
        cot_t[...] = cot_ref[...].T
        out_total[...] = jnp.zeros_like(out_total)
        two_total[...] = jnp.zeros_like(two_total)

    for k in range(col_parts):

        @pl.when(z == k)
        def arrive():
            for copy in copies(0, k) + copies(1, k):
                copy.wait()

    up = whole_rows(up_all[z])
    down = whole_rows(down_all[z])
    hidden = dot(normed[...], up)
    grad_act = dot(cot_ref[...], down)
    cdf = 0.5 * (1.0 + lax.erf(hidden * math.sqrt(0.5)))
    activated = (hidden * cdf).astype(bf16)
    slope = cdf + hidden * jnp.exp(-0.5 * hidden * hidden) * (1.0 / math.sqrt(2.0 * math.pi))
    grad_pre = (grad_act * slope).astype(bf16)
    out_total[...] += dot_t(activated, down)
    two_total[...] += dot_t(grad_pre, up)
    shape = grad_up.shape[1:]
    grad_up[z] = dot(normed_t[...], grad_pre).astype(bf16).reshape(shape)
    grad_down[z] = dot(cot_t[...], activated).astype(bf16).reshape(shape)

    for k in range(col_parts):

        @pl.when(z == k)
        def leave():
            for copy in copies(2, k) + copies(3, k):
                copy.start()

    @pl.when(z == col_parts - 1)
    def finish():
        out_ref[...] = out_total[...].astype(bf16)
        two_ref[...] = two_total[...].astype(bf16)
        for k in range(col_parts):
            for copy in copies(2, k) + copies(3, k):
                copy.wait()


def attend_back_kernel(team, col_parts, row_parts, place, middle_ref, gain_ref, cot_ref, *refs):
    parts, refs = refs[:team], refs[team:]
    normed_ref, context_ref, kept_ref, probs_ref = refs[:4]
    refs = refs[4:]
    count = col_parts * row_parts
    pieces, refs = split_pieces(refs[:count], col_parts, row_parts), refs[count:]
    middle_grad_ref, gain_grad_ref, one_ref = refs[:3]
    refs = refs[3:]
    context_grads, refs = refs[:team], refs[team:]
    near, far, refs = refs[:row_parts], refs[row_parts : 2 * row_parts], refs[2 * row_parts :]
    half = col_parts // 2
    grad_pieces = [[piece.at[k] for piece in near] for k in range(half)]
    grad_pieces += [[piece.at[k] for piece in far] for k in range(half)]
    weights, grads, low, grad_out, grad_q, grad_k, grad_v, sems, out_sems = refs
    copies = head_copies(pieces, weights, place, sems, True)
    for copy in copies:
        copy.start()
    own_rows = middle_ref.shape[0] // team
    grad_two = parts[0][...].astype(f32)
    for part in parts[1:]:
        grad_two = grad_two + part[...].astype(f32)
    unit, inverse = normalise(middle_ref[...])
    grad_gain = grad_two * unit
    rows = lax.broadcasted_iota(jnp.int32, grad_gain.shape, 0)
    first = place[0] * own_rows
    mine = (rows >= first) & (rows < first + own_rows)
    gain_grad_ref[...] = jnp.sum(jnp.where(mine, grad_gain, 0.0), axis=0, keepdims=True)
    grad = cot_ref[...].astype(f32) + normalise_back(unit, inverse, grad_two * gain_ref[...])
    middle_grad_ref[...] = grad
    low[...] = grad.astype(bf16)
    for copy in copies:
        copy.wait()
    grad_out[...] = dot(low[...], whole_rows(weights[3])).astype(bf16)
    for h in range(col_parts):
        q, k, v = (kept_ref[i, :, head(h)] for i in range(3))
        probs = probs_ref[h]
        grad_heads = grad_out[:, head(h)]
        grad_v[:, head(h)] = dot(probs.T, grad_heads).astype(bf16)
        probs = probs.astype(f32)
        grad_probs = dot_t(grad_heads, v)
        inner = jnp.sum(grad_probs * probs, axis=-1, keepdims=True)
        grad_scores = (probs * (grad_probs - inner)).astype(bf16)
        grad_q[:, head(h)] = (dot(grad_scores, k) * score_scale).astype(bf16)
        grad_k[:, head(h)] = (dot(grad_scores.T, q) * score_scale).astype(bf16)
    shape = grads.shape[1:]
    normed_t = normed_ref[...].T
    context_t = context_ref[...].T
    grads[3] = dot(low[...].T, kept_ref[3]).astype(bf16).reshape(shape)
    grads[0] = dot(normed_t, grad_q[...]).astype(bf16).reshape(shape)
    grads[1] = dot(context_t, grad_k[...]).astype(bf16).reshape(shape)
    grads[2] = dot(context_t, grad_v[...]).astype(bf16).reshape(shape)
    copies = head_copies(grad_pieces, grads, place, out_sems, False)
    for copy in copies:
        copy.start()
    total = dot_t(grad_k[...], whole_rows(weights[1])) + dot_t(grad_v[...], whole_rows(weights[2]))
    middle_total = total.astype(bf16)
    low[...] = middle_total
    width = context_grads[0].shape[1]
    for k in range(team):
        lanes = pl.ds(pl.multiple_of((place[0] ^ k) * width, LANES), width)
        context_grads[k][...] = low[:, lanes]
    one_ref[...] = dot_t(grad_q[...], whole_rows(weights[0]))
    for copy in copies:
        copy.wait()


def adjoint_kernel(team, logr_ref, *refs):
    parts = refs[:team]
    grad_ref, ends_ref, total_ref, g_tiles = refs[team:]
    grad = parts[0][...].astype(f32)
    for part in parts[1:]:
        grad = grad + part[...].astype(f32)
    grad_ref[...] = grad.astype(bf16)
    tiles, length, unused = g_tiles.shape
    states = logr_ref.shape[0]
    span = length // SUBS
    fill_tiles(g_tiles, grad_ref, 0)
    before = (sub_index() * span).astype(f32)
    for tile in range(tiles):
        rate = jnp.exp(logr_ref[:, lane_tile(tile)])
        decay = jnp.exp(-rate)
        decays = [spread(decay[n : n + 1]) for n in range(states)]

        def step(i, held):
            g = g_tiles[tile, pl.ds(span - 1 - i, SUBS, stride=span), :]
            later = []
            for d, (b, w) in zip(decays, held):
                shrunk = d * b
                later.append((g + shrunk, d * w + shrunk))
            return tuple(later)

        zero = no_state(g_tiles)
        held = lax.fori_loop(0, span, step, ((zero, zero),) * states, unroll=2)
        for n in range(states):
            b, w = held[n]
            ends_ref[0, n, :, lane_tile(tile)] = b
            ends_ref[1, n, :, lane_tile(tile)] = w
            shrink = jnp.exp(-before * rate[n : n + 1])
            total_ref[0, n : n + 1, lane_tile(tile)] = jnp.sum(shrink * b, axis=0, keepdims=True)
            total_ref[1, n : n + 1, lane_tile(tile)] = jnp.sum(
                shrink * (w + before * b), axis=0, keepdims=True
            )


def context_back_kernel(
    team, place, grad_ref, normed_ref, ends_ref, all_ref, logr_ref, coef_ref, one_ref, *refs
):
    pieces = refs[:team]
    grad_ssm_ref, u_tiles, g_tiles, y_tiles, full = refs[team:]
    tiles, length, unused = u_tiles.shape
    states = logr_ref.shape[0]
    span = length // SUBS
    width = tiles * LANES
    fill_tiles(u_tiles, normed_ref, place[0] * width)
    fill_tiles(g_tiles, grad_ref, 0)
    index = sub_index()
    after = ((SUBS - 1 - index) * span).astype(f32)
    full[...] = one_ref[...]
    group = 8
    for tile in range(tiles):
        lanes = lane_tile(tile)
        rate = jnp.exp(logr_ref[:, lanes])
        decay = jnp.exp(-rate)
        root = jnp.sqrt(2.0 * rate)
        scale = coef_ref[:, lanes] * root
        in_b = jnp.zeros((states, LANES), f32)
        in_w = jnp.zeros((states, LANES), f32)
        for j in range(all_ref.shape[0]):
            gap = j - place[1] - 1
            distance = (jnp.maximum(gap, 0) * length).astype(f32)
            shrink = jnp.exp(-distance * rate)
            b, w = all_ref[j, 0, :, lanes], all_ref[j, 1, :, lanes]
            in_b = in_b + jnp.where(gap >= 0, shrink * b, 0.0)
            in_w = in_w + jnp.where(gap >= 0, shrink * (w + distance * b), 0.0)
        for first in range(0, states, group):
            chosen = range(first, first + group)
            starts = []
            for n in chosen:
                row = rate[n : n + 1]
                b, w = ends_ref[0, n, :, lanes], ends_ref[1, n, :, lanes]
                for d in (1, 2, 4):
                    shrink = jnp.exp(-(d * span) * row)
                    next_b = pltpu.roll(b, SUBS - d, 0)
                    next_w = pltpu.roll(w, SUBS - d, 0)
                    inside = index < SUBS - d
                    b, w = (
                        b + jnp.where(inside, shrink * next_b, 0.0),
                        w + jnp.where(inside, shrink * (next_w + (d * span) * next_b), 0.0),
                    )
                inside = index < SUBS - 1
                b = jnp.where(inside, pltpu.roll(b, SUBS - 1, 0), 0.0)
                w = jnp.where(inside, pltpu.roll(w, SUBS - 1, 0), 0.0)
                shrink = jnp.exp(-after * row)
                b_row, w_row = in_b[n : n + 1], in_w[n : n + 1]
                b = b + shrink * b_row
                w = w + shrink * (w_row + after * b_row)
                zero = no_state(u_tiles)
                starts.append((b, w, zero, zero))
            decays = [spread(decay[n : n + 1]) for n in chosen]
            scales = [spread(scale[n : n + 1]) for n in chosen]

            def step(i, held):
                at = pl.ds(span - 1 - i, SUBS, stride=span)
                g = g_tiles[tile, at, :]
                u = u_tiles[tile, at, :]
                later, parts = [], []
                for d, s, (b, w, sum_b, sum_w) in zip(decays, scales, held):
                    shrunk = d * b
                    w = d * w + shrunk
                    b = g + shrunk
                    later.append((b, w, sum_b + u * b, sum_w + u * w))
                    parts.append(s * b)
                while len(parts) > 1:
                    parts = [p + q for p, q in zip(parts[::2], parts[1::2])]
                if first > 0:
                    parts[0] = parts[0] + y_tiles[tile, at, :]
                y_tiles[tile, at, :] = parts[0]
                return tuple(later)

            held = lax.fori_loop(0, span, step, tuple(starts), unroll=2)
            for n, (unused_b, unused_w, sum_b, sum_w) in zip(chosen, held):
                sum_b = jnp.sum(sum_b, axis=0, keepdims=True)
                sum_w = jnp.sum(sum_w, axis=0, keepdims=True)
                row = slice(n, n + 1)
                grad_ssm_ref[0, row, lanes] = root[row] * sum_b
                grad_ssm_ref[1, row, lanes] = scale[row] * (0.5 * sum_b - rate[row] * sum_w)
        at_lanes = pl.ds(pl.multiple_of(place[0] * width + tile * LANES, LANES), LANES)
        full[:, at_lanes] += y_tiles[tile].astype(bf16).astype(f32)
    rows = pieces[0].shape[0]
    for k in range(team):
        at_rows = pl.ds(pl.multiple_of((place[0] ^ k) * rows, rows), rows)
        pieces[k][...] = full[at_rows, :].astype(bf16)


def input_grad_kernel(team, place, x_ref, gain_ref, middle_grad_ref, *refs):
    parts, (out_ref, gain_grad_ref) = refs[:team], refs[team:]
    rows = out_ref.shape[0]
    at_rows = pl.ds(pl.multiple_of(place[0] * rows, rows), rows)
    grad_one = parts[0][...].astype(f32)
    for part in parts[1:]:
        grad_one = grad_one + part[...].astype(f32)
    unit, inverse = normalise(x_ref[at_rows, :].astype(f32))
    gain_grad_ref[...] = jnp.sum(grad_one * unit, axis=0, keepdims=True)
    back = normalise_back(unit, inverse, grad_one * gain_ref[...])
    out_ref[...] = (middle_grad_ref[at_rows, :] + back).astype(bf16)


def assemble_kernel(halves, low_count, place, own_ref, *refs):
    others, out_ref = refs[:-1], refs[-1]
    count, rows, unused = own_ref.shape
    half = place[4]

    def put(value, sequence, which, member):
        at_rows = pl.ds(pl.multiple_of((which * low_count + member) * rows, rows), rows)
        out_ref[sequence, at_rows, :] = value.astype(out_ref.dtype)

    for sequence in range(count // (halves * low_count)):
        if halves == 1:
            for member in range(low_count):
                put(own_ref[sequence * low_count + member], sequence, 0, member)
        else:
            put(own_ref[sequence * halves + half], sequence, half, 0)
            put(others[0][sequence], sequence, 1 - half, 0)


def pack_kernel(halves, place, qkv_ref, out_ref, up_ref, down_ref, *refs):
    rows = up_ref.shape[0]
    heads, hidden = out_ref.shape[0] // halves, up_ref.shape[1] // halves
    for which in range(halves):
        side = place[4] if which == 0 else 1 - place[4]
        at_heads = pl.ds(pl.multiple_of(side * heads, LANES), heads)
        at_hidden = pl.ds(pl.multiple_of(side * hidden, LANES), hidden)
        if which == 0:
            head_ref, wide_ref, deep_ref = refs[:3]
        else:
            packed = refs[3]
            head_ref = packed.at[:, : 4 * heads]
            wide_ref = packed.at[:, 4 * heads : 4 * heads + hidden]
            deep_ref = packed.at[:, 4 * heads + hidden :]
        for i in range(3):
            head_ref[:, i * heads : (i + 1) * heads] = qkv_ref[i, :, at_heads].astype(bf16)
        head_ref[:, 3 * heads :] = out_ref[at_heads, :].T.astype(bf16)
        wide_ref[...] = up_ref[:, at_hidden].astype(bf16)
        deep_ref[...] = down_ref[at_hidden, :].T.astype(bf16)


def lamb_moments(weight, grad_item, first_old, second_old):
    first_new = beta_first * first_old + (1.0 - beta_first) * grad_item
    second_new = beta_second * second_old + (1.0 - beta_second) * grad_item * grad_item
    direction = (
        first_new
        / (1.0 - beta_first**STEP)
        / (jnp.sqrt(second_new / (1.0 - beta_second**STEP)) + lamb_eps)
        + weight_decay * weight
    )
    return (first_new, second_new, direction)


def place_sums(sums_ref, sums):
    rows = lax.broadcasted_iota(jnp.int32, sums_ref.shape, 0)
    lanes = lax.broadcasted_iota(jnp.int32, sums_ref.shape, 1)
    found = jnp.zeros(sums_ref.shape, f32)
    for index, pair in sums.items():
        for row, value in enumerate(pair):
            found = jnp.where((rows == row) & (lanes == index), value, found)
    sums_ref[...] = found


def moments_kernel(halves, matrices, place, *refs):
    count = 1 + max(item[1] for item in matrices)
    grads, refs = [refs[halves * i : halves * (i + 1)] for i in range(count)], refs[halves * count :]
    arrays = len({(item[1], item[4] is None) for item in matrices})
    ins = [refs[3 * i : 3 * i + 3] for i in range(arrays)]
    outs = [refs[3 * (arrays + i) : 3 * (arrays + i) + 3] for i in range(arrays)]
    sums_ref = refs[6 * arrays]
    keys = []
    sums = {}
    for number, source, column, turned, stacked in matrices:
        key = (source, stacked is None)
        if key not in keys:
            keys.append(key)
        pick = (lambda ref: ref) if stacked is None else (lambda ref, i=stacked: ref.at[i])
        weight, first, second = (pick(ref) for ref in ins[keys.index(key)])
        news = [pick(ref) for ref in outs[keys.index(key)]]
        width = weight.shape[0 if turned else 1] // halves
        rows = weight.shape[1 if turned else 0]
        cols = slice(column * width, (column + 1) * width)
        total_weight = total_update = 0.0
        for which, grad_ref in enumerate(grads[source]):
            side = place[4] if which == 0 else 1 - place[4]
            at = pl.ds(pl.multiple_of(side * width, width), width)
            if which == 0:
                grad = grad_ref[pl.ds(pl.multiple_of(side * rows, rows), rows), cols].astype(f32)
            else:
                grad = grad_ref[:, cols].astype(f32)
            at = (at, slice(None)) if turned else (slice(None), at)
            grad = grad.T if turned else grad
            old = weight[at]
            found = lamb_moments(old, grad, first[at], second[at])
            for ref, value in zip(news, found):
                ref[at] = value
            total_weight = total_weight + jnp.sum(old * old)
            total_update = total_update + jnp.sum(found[2] * found[2])
        sums[number] = (total_weight, total_update)
    place_sums(sums_ref, sums)


def small_moments_kernel(numbers, grads_ref, *refs):
    ins, outs, sums_ref = (refs[:3], refs[3:6]), (refs[6:9], refs[9:12]), refs[12]
    states = (grads_ref.shape[0] - 2) // 2
    sums = {}
    for (weight, first, second), news, start, rows, first_number in (
        (ins[0], outs[0], 2 * states, 1, numbers[0]),
        (ins[1], outs[1], 0, states, numbers[1]),
    ):
        for i in range(2):
            grad = grads_ref[start + i * rows : start + (i + 1) * rows, :]
            at = slice(i * rows, (i + 1) * rows)
            found = lamb_moments(weight[at, :], grad, first[at, :], second[at, :])
            for ref, value in zip(news, found):
                ref[at, :] = value
            sums[first_number + i] = (
                jnp.sum(weight[at, :] * weight[at, :]),
                jnp.sum(found[2] * found[2]),
            )
    place_sums(sums_ref, sums)


def update_kernel(stacks, sums_ref, *refs):
    count = len(stacks)
    weights, directions, news = refs[:count], refs[count : 2 * count], refs[2 * count : 3 * count]
    norms = jnp.sqrt(jnp.sum(sums_ref[...], axis=0))
    refs[3 * count][...] = norms
    ratios = norms[0:1] / norms[1:2]
    lanes = lax.broadcasted_iota(jnp.int32, ratios.shape, 1)
    for numbers, weight, direction, new in zip(stacks, weights, directions, news):
        step = weight.shape[0] // len(numbers)
        for i, number in enumerate(numbers):
            ratio = jnp.sum(jnp.where(lanes == number, ratios, 0.0), axis=1, keepdims=True)
            at = slice(i * step, (i + 1) * step)
            scale = learn_rate * ratio.reshape((1,) * weight.ndim)
            new[at] = weight[at] - scale * direction[at]


def call(body, ins, outs, scratch=(), grid=None, in_specs=None, out_specs=None, time=1.0):
    moved = sum(a.size * a.dtype.itemsize for a in list(ins) + list(outs))
    params = pltpu.CompilerParams(vmem_limit_bytes=VMEM_BYTES)
    cost = pl.CostEstimate(flops=int(time * 1.15e+09), bytes_accessed=moved, transcendentals=0)
    whole = pl.BlockSpec(memory_space=pltpu.VMEM)
    extra = {}
    if grid is not None:
        extra["grid"] = grid
    return pl.pallas_call(
        body,
        out_shape=tuple(outs),
        in_specs=in_specs or [whole for unused in ins],
        out_specs=tuple(out_specs or [whole for unused in outs]),
        scratch_shapes=list(scratch),
        compiler_params=params,
        cost_estimate=cost,
        **extra,
    )(*ins)


def shaped(shape, kind):
    return jax.ShapeDtypeStruct(tuple(shape), kind)


def on_device(
    tokens,
    cotangent,
    w_qkv,
    w_out,
    w_up,
    w_down,
    norm_gains,
    ssm_param,
    first_qkv,
    second_qkv,
    first_out,
    second_out,
    first_up,
    second_up,
    first_down,
    second_down,
    first_gain,
    second_gain,
    first_ssm,
    second_ssm,
):
    halves = lax.axis_size("sl")
    low_count = lax.axis_size("ml")
    row_parts = lax.axis_size("sh")
    col_parts = lax.axis_size("mb") * lax.axis_size("mq")
    team = halves * low_count
    sl, ml, mb, mq = (lax.axis_index(name) for name in ("sl", "ml", "mb", "mq"))
    rank = sl * low_count + ml
    block_index = lax.axis_index("sh") * halves + mq
    seq_total, length, width = tokens.shape
    assert length == BLK and seq_total == lax.axis_size("mb")
    states = ssm_param.shape[1]
    channels = width // team
    tiles = channels // LANES
    row_count = width // row_parts
    own_rows = length // team
    place = [rank, block_index, lax.axis_index("sh"), lax.axis_index(MODEL), sl, sl ^ mq]
    place = jnp.stack(place).astype(jnp.int32)
    smem = pl.BlockSpec(memory_space=pltpu.SMEM)
    vmem = pl.BlockSpec(memory_space=pltpu.VMEM)

    def permute(value, axes, moves):
        return lax.ppermute(value, axes, moves)

    def swap(value):
        return permute(value, "sl", [(0, 1), (1, 0)])

    def in_order(own, other, axis):
        return jnp.where(
            sl == 0, jnp.concatenate([own, other], axis), jnp.concatenate([other, own], axis)
        )

    def team_send(pieces):
        moved = [pieces[0]]
        for k in range(1, team):
            moved.append(permute(pieces[k], TEAM, [(i, i ^ k) for i in range(team)]))
        return moved

    def pick_block(array):
        own = lax.dynamic_index_in_dim(array, mb, 0, keepdims=False)
        if halves == 1:
            return own
        return jnp.where(sl == mq, own, swap(own))

    def across(value, bit):
        return permute(value, "sh", [(i, i ^ bit) for i in range(row_parts)])

    def along(value, axes, step):
        count = lax.axis_size(axes)
        return permute(value, axes, [(i, (i + step) % count) for i in range(count)])

    bits = [1 << i for i in range(row_parts.bit_length() - 1)]

    def bit_order(k):
        return bits if k % 2 == 0 else bits[::-1]

    def double_rows(value, order):
        found = {0: value}
        for bit in order:
            for r in list(found):
                found[r | bit] = across(found[r], bit)
        return [found[r] for r in range(row_parts)]

    def add(*items):
        return sum(item.astype(f32) for item in items).astype(bf16)

    def halve_rows(pieces, order):
        sums = {r: [piece] for r, piece in enumerate(pieces)}
        for bit in reversed(order):
            for r in [r for r in sums if r & bit]:
                sums[r ^ bit].append(across(add(*sums.pop(r)), bit))
        return add(*sums[0])

    def ring_gather(shard):
        pieces, held = [], shard
        for k in range(col_parts):
            if k > 0:
                held = along(held, COLS, 1)
            pieces.append(double_rows(held, bits if k % 2 == 0 else bits[::-1]))
        return pieces

    def ring_sum(near, far):
        held = None
        for stack in (far, near):
            for k in reversed(range(stack.shape[0])):
                held = stack[k] if held is None else add(stack[k], along(held, COLS, -1))
        return held

    def everywhere(value, axes):
        count = lax.axis_size(axes)
        copies = jnp.broadcast_to(value[None], (count, *value.shape))
        return lax.all_to_all(copies, axes, 0, 0, tiled=True)

    small = jnp.concatenate([ssm_param.reshape(2 * states, -1), norm_gains], 0)
    small = jnp.transpose(everywhere(small, ALL), (1, 0, 2)).reshape(2 * states + 2, width)
    own_ssm = lax.dynamic_slice_in_dim(
        small[: 2 * states].reshape(2, states, width), rank * channels, channels, 2
    )
    coef, logr = own_ssm[0], own_ssm[1]
    gain_one = small[2 * states : 2 * states + 1]
    gain_two = small[2 * states + 1 : 2 * states + 2]

    rows_dev = w_up.shape[0]
    hidden_cols = w_up.shape[1] // halves
    head_cols = 4 * w_out.shape[0] // halves
    sides = [shaped((rows_dev, cols), bf16) for cols in (head_cols, hidden_cols, hidden_cols)]
    packed_cols = head_cols + 2 * hidden_cols
    shards = call(
        functools.partial(pack_kernel, halves),
        (place, w_qkv, w_out, w_up, w_down),
        sides + [shaped((rows_dev, packed_cols), bf16)] * (halves - 1),
        in_specs=[smem] + [vmem] * 4,
        time=2.4,
    )
    if halves == 2:
        other = swap(shards[3])
        cuts = (0, head_cols, head_cols + hidden_cols, packed_cols)
        shards = [
            in_order(own, other[:, first:last], 0)
            for own, first, last in zip(shards, cuts, cuts[1:])
        ]
    head_shard, up_shard, down_shard = shards[:3]
    attn_w = ring_gather(head_shard)
    up_w = double_rows(lax.all_gather(up_shard, COLS, axis=0, tiled=False), bits)
    down_w = double_rows(lax.all_gather(down_shard, COLS, axis=0, tiled=False), bits[::-1])

    x = pick_block(tokens)
    cot = pick_block(cotangent)

    def flat(pieces):
        return [piece for group in pieces for piece in group]

    piece_count = row_parts * col_parts
    anywhere = [pl.BlockSpec(memory_space=pl.ANY)]

    def fixed(*shape):
        return pl.BlockSpec(shape, lambda z: (0,) * len(shape))

    wide = fixed(length, width)
    row = fixed(1, width)

    normed_one, ends, total = call(
        norm_kernel,
        (place, x, gain_one, logr),
        (
            shaped((length, width), bf16),
            shaped((states, SUBS, channels), f32),
            shaped((states, channels), f32),
        ),
        scratch=[pltpu.VMEM((tiles, length, LANES), f32)],
        in_specs=[smem, vmem, vmem, vmem],
        time=5,
    )
    totals = everywhere(total, ("sh", "mq"))
    (context_own,) = call(
        context_kernel,
        (place, normed_one, ends, totals, logr, coef),
        (shaped((length, channels), bf16),),
        scratch=[pltpu.VMEM((tiles, length, LANES), f32)] * 2,
        in_specs=[smem] + [vmem] * 5,
        time=7,
    )
    contexts = team_send([context_own] * team)

    head_piece = shaped((col_parts // 2, row_count, head_cols), bf16)
    hidden_piece = shaped((col_parts, row_count, hidden_cols), bf16)
    sizes = (team, col_parts, row_parts)
    head_buffer = pltpu.VMEM((4, row_parts, row_count, col_parts * HD), bf16)
    head_sems = pltpu.SemaphoreType.DMA((col_parts, row_parts, 4))
    kept_shape = shaped((4, length, col_parts * HD), bf16)
    context, attn_part, kept, probs = call(
        functools.partial(attend_kernel, *sizes),
        (place, normed_one, *contexts, *flat(attn_w)),
        (
            shaped((length, width), bf16),
            shaped((length, width), bf16),
            kept_shape,
            shaped((col_parts, length, length), bf16),
        ),
        scratch=[head_buffer, head_sems],
        in_specs=[smem] + [vmem] * (1 + team) + anywhere * piece_count,
        time=10.3,
    )
    attn_parts = team_send([attn_part] * team)

    hidden_buffer = pltpu.VMEM((col_parts, row_parts, row_count, hidden_cols), bf16)
    middle, out_part, two_part, *hidden_grads = call(
        functools.partial(feed_kernel, *sizes),
        (place, x, cot, gain_two, *attn_parts, *up_w, *down_w),
        (
            shaped((length, width), f32),
            shaped((length, width), bf16),
            shaped((length, width), bf16),
            *[hidden_piece] * (2 * row_parts),
        ),
        scratch=[
            *[hidden_buffer] * 4,
            pltpu.VMEM((length, width), bf16),
            pltpu.VMEM((width, length), bf16),
            pltpu.VMEM((width, length), bf16),
            pltpu.VMEM((length, width), f32),
            pltpu.VMEM((length, width), f32),
            pltpu.SemaphoreType.DMA((4, col_parts, row_parts)),
        ],
        grid=(col_parts,),
        in_specs=[smem, wide, wide, row] + [wide] * team + anywhere * (2 * row_parts),
        out_specs=[wide, wide, wide] + anywhere * (2 * row_parts),
        time=22,
    )
    two_parts = team_send([two_part] * team)

    def rows_of(array, member):
        return lax.dynamic_slice_in_dim(array, member * own_rows, own_rows, 0)

    def share_rows(own_piece, kind):
        pieces = lax.all_gather(own_piece, MODEL, axis=0, tiled=False)
        others = []
        if halves == 2:
            pairs = pieces.reshape(seq_total, halves, own_rows, width)
            others = [swap(lax.dynamic_index_in_dim(pairs, 1 - sl, 1, keepdims=False))]
        (blocks,) = call(
            functools.partial(assemble_kernel, halves, low_count),
            (place, pieces, *others),
            (shaped((seq_total, length, width), kind),),
            in_specs=[smem, vmem] + [vmem] * len(others),
            time=3.5,
        )
        return blocks

    out_pieces = team_send([rows_of(out_part, rank ^ k) for k in range(team)])
    result = rows_of(middle, rank) + sum(item.astype(f32) for item in out_pieces)
    layer_out = share_rows(result.astype(bf16), bf16)

    def both_halves(own):
        if halves == 1:
            return [own]
        return [own, swap(lax.dynamic_slice_in_dim(own, (1 - sl) * rows_dev, rows_dev, 0))]

    def sum_over_z(stack):
        return lax.psum_scatter(stack, COLS, scatter_dimension=0, tiled=False)

    grad_up = sum_over_z(halve_rows(hidden_grads[:row_parts], bits))
    grad_down = sum_over_z(halve_rows(hidden_grads[row_parts:], bits[::-1]))

    middle_grad, gain_two_grad, one_part, *rest = call(
        functools.partial(attend_back_kernel, *sizes),
        (place, middle, gain_two, cot, *two_parts, normed_one, context, kept, probs, *flat(attn_w)),
        (
            shaped((length, width), f32),
            shaped((1, width), f32),
            shaped((length, width), f32),
            *[shaped((length, channels), bf16)] * team,
            *[head_piece] * (2 * row_parts),
        ),
        scratch=[
            head_buffer,
            head_buffer,
            pltpu.VMEM((length, width), bf16),
            *[pltpu.VMEM((length, col_parts * HD), bf16)] * 4,
            head_sems,
            head_sems,
        ],
        in_specs=[smem] + [vmem] * (3 + team + 4) + anywhere * piece_count,
        out_specs=[vmem] * (3 + team) + anywhere * (2 * row_parts),
        time=20.5,
    )
    context_grads = team_send(rest[:team])
    far = halve_rows(rest[team + row_parts :], bits[::-1])
    near = halve_rows(rest[team : team + row_parts], bits)
    grad_heads = ring_sum(near, far)

    context_grad, adjoint_ends, adjoint_total = call(
        functools.partial(adjoint_kernel, team),
        (logr, *context_grads),
        (
            shaped((length, channels), bf16),
            shaped((2, states, SUBS, channels), f32),
            shaped((2, states, channels), f32),
        ),
        scratch=[pltpu.VMEM((tiles, length, LANES), f32)],
        time=6.7,
    )
    adjoint_totals = everywhere(adjoint_total, ("sh", "mq"))
    *one_pieces, grad_ssm = call(
        functools.partial(context_back_kernel, team),
        (place, context_grad, normed_one, adjoint_ends, adjoint_totals, logr, coef, one_part),
        (
            *[shaped((own_rows, width), bf16)] * team,
            shaped((2, states, channels), f32),
        ),
        scratch=[pltpu.VMEM((tiles, length, LANES), f32)] * 3 + [pltpu.VMEM((length, width), f32)],
        in_specs=[smem] + [vmem] * 7,
        time=16,
    )
    one_pieces = team_send(one_pieces)
    grad_rows, gain_one_grad = call(
        functools.partial(input_grad_kernel, team),
        (place, x, gain_one, middle_grad, *one_pieces),
        (shaped((own_rows, width), bf16), shaped((1, width), f32)),
        in_specs=[smem] + [vmem] * (3 + team),
        time=4,
    )
    input_grad = share_rows(grad_rows, f32)

    placed_ssm = lax.dynamic_update_slice_in_dim(
        jnp.zeros((2 * states, width), f32),
        grad_ssm.reshape(2 * states, channels),
        rank * channels,
        1,
    )
    small_grads = jnp.concatenate([placed_ssm, gain_one_grad, gain_two_grad], 0)
    small_grads = small_grads.reshape(2 * states + 2, lax.axis_size(ALL), -1)
    small_grads = lax.all_to_all(jnp.transpose(small_grads, (1, 0, 2)), ALL, 0, 0, tiled=True)
    small_grads = jnp.sum(small_grads, axis=0)

    def moments(matrices, grads, arrays):
        changed = [shaped(old.shape, f32) for group in arrays for old in group]
        grad_parts = [part for grad in grads for part in both_halves(grad)]
        ins = [item for group in arrays for item in group]
        *found, sums = call(
            functools.partial(moments_kernel, halves, matrices),
            (place, *grad_parts, *ins),
            (*changed, shaped((2, LANES), f32)),
            in_specs=[smem] + [vmem] * (len(grad_parts) + len(ins)),
            time=4,
        )
        return [found[3 * i : 3 * i + 3] for i in range(len(arrays))], sums

    hidden_new, hidden_sums = moments(
        ((4, 0, 0, False, None), (5, 1, 0, True, None)),
        (grad_up, grad_down),
        ((w_up, first_up, second_up), (w_down, first_down, second_down)),
    )
    heads_new, head_sums = moments(
        tuple((i, 0, i, False, i) for i in range(3)) + ((3, 0, 3, True, None),),
        (grad_heads,),
        ((w_qkv, first_qkv, second_qkv), (w_out, first_out, second_out)),
    )
    own_channels = norm_gains.shape[1]
    ssm_items = [item.reshape(2 * states, own_channels) for item in (ssm_param, first_ssm, second_ssm)]
    small_items = [norm_gains, first_gain, second_gain, *ssm_items]
    *small_new, small_sums = call(
        functools.partial(small_moments_kernel, (6, 8)),
        (small_grads.reshape(2 * states + 2, own_channels), *small_items),
        (*[shaped(item.shape, f32) for item in small_items], shaped((2, LANES), f32)),
    )
    all_sums = everywhere(hidden_sums + head_sums + small_sums, ALL)
    masters = (w_qkv, w_out, w_up, w_down, norm_gains, ssm_items[0])
    news = (*heads_new, *hidden_new, small_new[:3], small_new[3:])
    *weights, norms = call(
        functools.partial(update_kernel, ((0, 1, 2), (3,), (4,), (5,), (6, 7), (8, 9))),
        (all_sums, *masters, *[group[2] for group in news]),
        (*[shaped(item.shape, f32) for item in masters], shaped((2, LANES), f32)),
        time=3.2,
    )
    outputs = [layer_out, input_grad]
    for index, (weight, (first_new, second_new, unused)) in enumerate(zip(weights, news)):
        if index == 4:
            outputs += [weight, first_new, second_new[0], second_new[1]]
        else:
            kept_shape = ssm_param.shape if index == 5 else weight.shape
            outputs += [item.reshape(kept_shape) for item in (weight, first_new, second_new)]
    outputs.append(norms[:, :10])
    return tuple(outputs)


def solution(mesh):
    seq_count, model_count = mesh.shape["seq"], mesh.shape["mp"]
    halves = 2 if HEADS // model_count >= 2 else 1
    sizes = (seq_count // halves, halves, SEQS, halves, model_count // (SEQS * halves))
    fine = Mesh(mesh.devices.reshape(sizes), ALL)
    seq, model = ("sh", "sl"), ("mb", "mq", "ml")
    rows_cols, cols_rows = P(seq, model), P(model, seq)
    token = P(None, seq, None)
    stack = P(None, seq, model)
    gains = P(None, ALL)
    ssm = P(None, None, ALL)
    return jax.shard_map(
        on_device,
        mesh=fine,
        in_specs=(token, token, stack, cols_rows, rows_cols, cols_rows, gains, ssm)
        + (stack,) * 2
        + (cols_rows,) * 2
        + (rows_cols,) * 2
        + (cols_rows,) * 2
        + (gains,) * 2
        + (ssm,) * 2,
        out_specs=(token, token)
        + (stack,) * 3
        + (cols_rows,) * 3
        + (rows_cols,) * 3
        + (cols_rows,) * 3
        + (gains, gains, P(ALL), P(ALL))
        + (ssm,) * 3
        + (P(),),
        check_vma=False,
    )
```

```python
import functools
import math

import jax
import jax.numpy as jnp
from jax import lax
from jax.experimental import pallas as pl
from jax.experimental.pallas import tpu as pltpu
from jax.sharding import Mesh
from jax.sharding import PartitionSpec as P

HD = 128
HEADS = 8
BLK = 512
STEP = 10
SEQS = 2
LANES = 128
SUBS = 8
GROUP = 8

norm_eps = 1e-05
beta_first = 0.9
beta_second = 0.999
lamb_eps = 1e-06
weight_decay = 0.01
learn_rate = 0.5
score_scale = HD ** (-0.5)

f32 = jnp.float32
bf16 = jnp.bfloat16
VMEM_BYTES = 56 * 1024 * 1024

ALL = ("sh", "sl", "mb", "mq", "ml")
MODEL = ("mb", "mq", "ml")
COLS = ("mb", "mq")
TEAM = ("sl", "ml")


def dot(left, right):
    return lax.dot_general(left, right, (((1,), (0,)), ((), ())), preferred_element_type=f32)


def dot_t(left, right):
    return lax.dot_general(left, right, (((1,), (1,)), ((), ())), preferred_element_type=f32)


def normalise(values):
    centred = values - jnp.mean(values, axis=-1, keepdims=True)
    inverse = lax.rsqrt(jnp.mean(centred * centred, axis=-1, keepdims=True) + norm_eps)
    return centred * inverse, inverse


def normalise_back(unit, inverse, grad_unit):
    mean_one = jnp.mean(grad_unit, axis=-1, keepdims=True)
    mean_two = jnp.mean(grad_unit * unit, axis=-1, keepdims=True)
    return inverse * (grad_unit - mean_one - unit * mean_two)


def sub_index():
    return lax.broadcasted_iota(jnp.int32, (SUBS, LANES), 0)


def spread(row):
    return jnp.broadcast_to(row, (SUBS, LANES))


def lane_tile(index):
    return slice(index * LANES, (index + 1) * LANES)


def no_state(tiles):
    rows = tiles[0, :SUBS, :]
    return rows - rows


def fill_tiles(scratch, ref, start):
    for tile in range(scratch.shape[0]):
        lanes = pl.ds(pl.multiple_of(start + tile * LANES, LANES), LANES)
        scratch[tile] = ref[:, lanes].astype(f32)


def norm_kernel(
    place, x_ref, gain_ref, logr_ref, normed_ref, turned_ref, ends_ref, total_ref, u_tiles
):
    unit, unused = normalise(x_ref[...].astype(f32))
    normed_ref[...] = (unit * gain_ref[...]).astype(bf16)
    turned_ref[...] = normed_ref[...].T
    tiles, length, unused = u_tiles.shape
    states = logr_ref.shape[0]
    span = length // SUBS
    fill_tiles(u_tiles, normed_ref, place[0] * (tiles * LANES))
    left = ((SUBS - 1 - sub_index()) * span).astype(f32)
    for tile in range(tiles):
        rate = jnp.exp(logr_ref[:, lane_tile(tile)])
        decay = jnp.exp(-rate)
        decays = [spread(decay[n : n + 1]) for n in range(states)]

        def step(i, held):
            u = u_tiles[tile, pl.ds(i, SUBS, stride=span), :]
            return tuple(d * h + u for d, h in zip(decays, held))

        zero = no_state(u_tiles)
        held = lax.fori_loop(0, span, step, (zero,) * states, unroll=4)
        for n in range(states):
            ends_ref[n, :, lane_tile(tile)] = held[n]
            total_ref[n : n + 1, lane_tile(tile)] = jnp.sum(
                held[n] * jnp.exp(-left * rate[n : n + 1]), axis=0, keepdims=True
            )


def context_kernel(
    place, normed_ref, ends_ref, all_ref, logr_ref, coef_ref, context_ref, u_tiles, y_tiles
):
    tiles, length, unused = u_tiles.shape
    states = logr_ref.shape[0]
    span = length // SUBS
    fill_tiles(u_tiles, normed_ref, place[0] * (tiles * LANES))
    index = sub_index()
    before = (index * span).astype(f32)
    for tile in range(tiles):
        rate = jnp.exp(logr_ref[:, lane_tile(tile)])
        decay = jnp.exp(-rate)
        scale = coef_ref[:, lane_tile(tile)] * jnp.sqrt(2.0 * rate)
        incoming = jnp.zeros((states, LANES), f32)
        for j in range(all_ref.shape[0]):
            gap = place[1] - 1 - j
            distance = (jnp.maximum(gap, 0) * length).astype(f32)
            term = jnp.exp(-distance * rate) * all_ref[j, :, lane_tile(tile)]
            incoming = incoming + jnp.where(gap >= 0, term, 0.0)
        for first in range(0, states, GROUP):
            chosen = range(first, first + GROUP)
            starts = []
            for n in chosen:
                row = rate[n : n + 1]
                run = ends_ref[n, :, lane_tile(tile)]
                for d in (1, 2, 4):
                    moved = jnp.exp(-(d * span) * row) * pltpu.roll(run, d, 0)
                    run = run + jnp.where(index >= d, moved, 0.0)
                run = jnp.where(index >= 1, pltpu.roll(run, 1, 0), 0.0)
                starts.append(run + jnp.exp(-before * row) * incoming[n : n + 1])
            decays = [spread(decay[n : n + 1]) for n in chosen]
            scales = [spread(scale[n : n + 1]) for n in chosen]

            def step(i, held):
                at = pl.ds(i, SUBS, stride=span)
                u = u_tiles[tile, at, :]
                held = tuple(d * h + u for d, h in zip(decays, held))
                parts = [s * h for s, h in zip(scales, held)]
                if first > 0:
                    parts[0] = parts[0] + y_tiles[tile, at, :]
                while len(parts) > 1:
                    parts = [a + b for a, b in zip(parts[::2], parts[1::2])]
                y_tiles[tile, at, :] = parts[0]
                return held

            lax.fori_loop(0, span, step, tuple(starts), unroll=4)
        context_ref[:, lane_tile(tile)] = y_tiles[tile].astype(bf16)


def whole_rows(block):
    return block.reshape(block.shape[0] * block.shape[1], block.shape[2])


def head(index):
    return slice(index * HD, (index + 1) * HD)


def head_copies(arrays, buffer, place, sems, inward, index_of):
    copies = []
    for k in range(sems.shape[0]):
        for j, group in enumerate(arrays):
            for r, array in enumerate(group):
                for i in range(2):
                    outside = index_of(array, j, k).at[:, pl.ds(i * HD, HD)]
                    inside = buffer.at[2 * j + i, place[2] ^ r, :, pl.ds(k * HD, HD)]
                    ends = (outside, inside) if inward else (inside, outside)
                    copies.append(pltpu.make_async_copy(*ends, sems.at[k, r, 2 * j + i]))
    return copies


def weight_copies(arrays, buffer, place, sems):
    count = sems.shape[0]

    def index_of(array, j, k):
        return array.at[lax.rem(place[6] + count - k, count)]

    return head_copies(arrays, buffer, place, sems, True, index_of)


def attend_kernel(team, col_parts, row_parts, place, normed_ref, cot_ref, *refs):
    contexts, refs = refs[:team], refs[team:]
    arrays, refs = (refs[:row_parts], refs[row_parts : 2 * row_parts]), refs[2 * row_parts :]
    context_t_ref, cot_t_ref, part_ref, kept_ref, probs_ref, probs_t_ref = refs[:6]
    context_ref, weights, sems = refs[6:]
    copies = weight_copies(arrays, weights, place, sems)
    for copy in copies:
        copy.start()
    width = contexts[0].shape[1]
    for k in range(team):
        lanes = pl.ds(pl.multiple_of((place[0] ^ k) * width, LANES), width)
        context_ref[:, lanes] = contexts[k][...]
    context_t_ref[...] = context_ref[...].T
    cot_t_ref[...] = cot_ref[...].T
    for copy in copies:
        copy.wait()
    kept_ref[0] = dot(normed_ref[...], whole_rows(weights[0])).astype(bf16)
    kept_ref[1] = dot(context_ref[...], whole_rows(weights[1])).astype(bf16)
    kept_ref[2] = dot(context_ref[...], whole_rows(weights[2])).astype(bf16)
    length = normed_ref.shape[0]
    rows = lax.broadcasted_iota(jnp.int32, (length, length), 0)
    cols = lax.broadcasted_iota(jnp.int32, (length, length), 1)
    for h in range(col_parts):
        scores = dot_t(kept_ref[0, :, head(h)], kept_ref[1, :, head(h)]) * score_scale
        scores = jnp.where(rows >= cols, scores, -1e30)
        shifted = jnp.exp(scores - jnp.max(scores, axis=-1, keepdims=True))
        inverse = 1.0 / jnp.sum(shifted, axis=-1, keepdims=True)
        probs = (shifted * inverse).astype(bf16)
        probs_ref[h] = probs
        probs_t_ref[h] = probs.T
        kept_ref[3, :, head(h)] = dot(probs, kept_ref[2, :, head(h)]).astype(bf16)
    part_ref[...] = dot_t(kept_ref[3], whole_rows(weights[3])).astype(bf16)


def gelu_parts(hidden, grad_act):
    cdf = 0.5 * (1.0 + lax.erf(hidden * math.sqrt(0.5)))
    slope = cdf + hidden * jnp.exp(-0.5 * hidden * hidden) * (1.0 / math.sqrt(2.0 * math.pi))
    return (hidden * cdf).astype(bf16), (grad_act * slope).astype(bf16)


def feed_kernel(team, col_parts, row_parts, place, x_ref, cot_ref, cot_t_ref, gain_ref, *refs):
    parts, refs = refs[:team], refs[team:]
    count = col_parts * row_parts
    pieces, refs = refs[:count], refs[count:]
    middle_ref, out_ref, two_ref = refs[:3]
    refs = refs[3:]
    up_grads, refs = (refs[:row_parts], refs[row_parts : 2 * row_parts]), refs[2 * row_parts :]
    down_grads, refs = (refs[:row_parts], refs[row_parts : 2 * row_parts]), refs[2 * row_parts :]
    up_all, down_all, grad_up, grad_down, normed, normed_t, out_total, two_total, sems = refs
    z = pl.program_id(0)
    half = col_parts // 2
    hidden_cols = up_all.shape[3]

    def copies(k):
        found = []
        for r in range(row_parts):
            piece = pieces[k * row_parts + r]
            for which, buffer in enumerate((up_all, down_all)):
                outside = piece.at[:, pl.ds(which * hidden_cols, hidden_cols)]
                inside = buffer.at[k, place[2] ^ r]
                found.append(pltpu.make_async_copy(outside, inside, sems.at[which, k, r]))
        return found

    def leaving(which, k, far, slot):
        stacks = (up_grads, down_grads)[which][far]
        buffer = (grad_up, grad_down)[which]
        return [
            pltpu.make_async_copy(
                buffer.at[k, place[2] ^ r], stacks[r].at[slot], sems.at[2 + which, k, r]
            )
            for r in range(row_parts)
        ]

    def each_leaving(k, act):
        for copy in leaving(0, k, k // half, k % half):
            act(copy)
        owner = lax.rem(place[6] + col_parts - k, col_parts)
        for far in range(2):

            @pl.when(owner // half == far)
            def down_leaves():
                for copy in leaving(1, k, far, lax.rem(owner, half)):
                    act(copy)

    @pl.when(z == 0)
    def start():
        for k in range(col_parts):
            for copy in copies(k):
                copy.start()
        attn = parts[0][...].astype(f32)
        for part in parts[1:]:
            attn = attn + part[...].astype(f32)
        middle = x_ref[...].astype(f32) + attn
        middle_ref[...] = middle
        unit, unused = normalise(middle)
        low = (unit * gain_ref[...]).astype(bf16)
        normed[...] = low
        normed_t[...] = low.T
        out_total[...] = jnp.zeros_like(out_total)
        two_total[...] = jnp.zeros_like(two_total)

    for k in range(col_parts):

        @pl.when(z == k)
        def arrive():
            for copy in copies(k):
                copy.wait()

    up = whole_rows(up_all[z])
    down = whole_rows(down_all[z])
    first = hidden_cols // 2
    cuts = (slice(0, first), slice(first, hidden_cols))
    befores = [(dot(normed[...], up[:, at]), dot(cot_ref[...], down[:, at])) for at in cuts]
    shape = (row_parts, up_all.shape[2], first)
    for at, (hidden, grad_act) in zip(cuts, befores):
        activated, grad_pre = gelu_parts(hidden, grad_act)
        out_total[...] += dot_t(activated, down[:, at])
        two_total[...] += dot_t(grad_pre, up[:, at])
        grad_up[z, :, :, at] = dot(normed_t[...], grad_pre).astype(bf16).reshape(shape)
        grad_down[z, :, :, at] = dot(cot_t_ref[...], activated).astype(bf16).reshape(shape)

    for k in range(col_parts):

        @pl.when(z == k)
        def leave():
            each_leaving(k, lambda copy: copy.start())

    @pl.when(z == col_parts - 1)
    def finish():
        out_ref[...] = out_total[...].astype(bf16)
        two_ref[...] = two_total[...].astype(bf16)
        for k in range(col_parts):
            each_leaving(k, lambda copy: copy.wait())


def attend_back_kernel(team, col_parts, row_parts, place, middle_ref, gain_ref, cot_ref, *refs):
    parts, refs = refs[:team], refs[team:]
    normed_t_ref, context_t_ref, kept_ref, probs_ref, probs_t_ref = refs[:5]
    refs = refs[5:]
    arrays, refs = (refs[:row_parts], refs[row_parts : 2 * row_parts]), refs[2 * row_parts :]
    middle_grad_ref, gain_grad_ref, one_ref = refs[:3]
    refs = refs[3:]
    context_grads, refs = refs[:team], refs[team:]
    near, far, refs = refs[:row_parts], refs[row_parts : 2 * row_parts], refs[2 * row_parts :]
    weights, grads, low, grad_out, grad_q, grad_k, grad_v, sems, out_sems = refs
    half = col_parts // 2

    def index_of(pair, j, k):
        return pair[k // half].at[k % half, :, pl.ds(2 * j * HD, 2 * HD)]

    copies = weight_copies(arrays, weights, place, sems)
    for copy in copies:
        copy.start()
    own_rows = middle_ref.shape[0] // team
    grad_two = parts[0][...].astype(f32)
    for part in parts[1:]:
        grad_two = grad_two + part[...].astype(f32)
    unit, inverse = normalise(middle_ref[...])
    grad_gain = grad_two * unit
    rows = lax.broadcasted_iota(jnp.int32, grad_gain.shape, 0)
    first = place[0] * own_rows
    mine = (rows >= first) & (rows < first + own_rows)
    gain_grad_ref[...] = jnp.sum(jnp.where(mine, grad_gain, 0.0), axis=0, keepdims=True)
    grad = cot_ref[...].astype(f32) + normalise_back(unit, inverse, grad_two * gain_ref[...])
    middle_grad_ref[...] = grad
    low[...] = grad.astype(bf16)
    for copy in copies:
        copy.wait()
    grad_out[...] = dot(low[...], whole_rows(weights[3])).astype(bf16)
    for h in range(col_parts):
        q, k, v = (kept_ref[i, :, head(h)] for i in range(3))
        grad_heads = grad_out[:, head(h)]
        grad_v[:, head(h)] = dot(probs_t_ref[h], grad_heads).astype(bf16)
        probs = probs_ref[h].astype(f32)
        grad_probs = dot_t(grad_heads, v)
        inner = jnp.sum(grad_probs * probs, axis=-1, keepdims=True)
        grad_scores = (probs * (grad_probs - inner)).astype(bf16)
        grad_q[:, head(h)] = (dot(grad_scores, k) * score_scale).astype(bf16)
        turned = dot_t(v, grad_heads) - inner.T
        turned = (probs_t_ref[h].astype(f32) * turned).astype(bf16)
        grad_k[:, head(h)] = (dot(turned, q) * score_scale).astype(bf16)
    shape = grads.shape[1:]
    grads[3] = dot(low[...].T, kept_ref[3]).astype(bf16).reshape(shape)
    grads[0] = dot(normed_t_ref[...], grad_q[...]).astype(bf16).reshape(shape)
    grads[1] = dot(context_t_ref[...], grad_k[...]).astype(bf16).reshape(shape)
    grads[2] = dot(context_t_ref[...], grad_v[...]).astype(bf16).reshape(shape)
    pairs = list(zip(near, far))
    copies = head_copies((pairs, pairs), grads, place, out_sems, False, index_of)
    for copy in copies:
        copy.start()
    total = dot_t(grad_k[...], whole_rows(weights[1])) + dot_t(grad_v[...], whole_rows(weights[2]))
    middle_total = total.astype(bf16)
    low[...] = middle_total
    width = context_grads[0].shape[1]
    for k in range(team):
        lanes = pl.ds(pl.multiple_of((place[0] ^ k) * width, LANES), width)
        context_grads[k][...] = low[:, lanes]
    one_ref[...] = dot_t(grad_q[...], whole_rows(weights[0]))
    for copy in copies:
        copy.wait()


def adjoint_kernel(team, logr_ref, *refs):
    parts = refs[:team]
    grad_ref, ends_ref, total_ref, g_tiles = refs[team:]
    grad = parts[0][...].astype(f32)
    for part in parts[1:]:
        grad = grad + part[...].astype(f32)
    grad_ref[...] = grad.astype(bf16)
    tiles, length, unused = g_tiles.shape
    states = logr_ref.shape[0]
    span = length // SUBS
    fill_tiles(g_tiles, grad_ref, 0)
    before = (sub_index() * span).astype(f32)
    for tile in range(tiles):
        rate = jnp.exp(logr_ref[:, lane_tile(tile)])
        decay = jnp.exp(-rate)
        for first in range(0, states, GROUP):
            chosen = range(first, first + GROUP)
            decays = [spread(decay[n : n + 1]) for n in chosen]

            def step(i, held):
                g = g_tiles[tile, pl.ds(span - 1 - i, SUBS, stride=span), :]
                later = []
                for d, (b, w) in zip(decays, held):
                    shrunk = d * b
                    later.append((g + shrunk, d * w + shrunk))
                return tuple(later)

            zero = no_state(g_tiles)
            held = lax.fori_loop(0, span, step, ((zero, zero),) * GROUP, unroll=4)
            for n, (b, w) in zip(chosen, held):
                ends_ref[0, n, :, lane_tile(tile)] = b
                ends_ref[1, n, :, lane_tile(tile)] = w
                shrink = jnp.exp(-before * rate[n : n + 1])
                total_ref[0, n : n + 1, lane_tile(tile)] = jnp.sum(
                    shrink * b, axis=0, keepdims=True
                )
                total_ref[1, n : n + 1, lane_tile(tile)] = jnp.sum(
                    shrink * (w + before * b), axis=0, keepdims=True
                )


def context_back_kernel(
    team, place, grad_ref, normed_ref, ends_ref, all_ref, logr_ref, coef_ref, one_ref, *refs
):
    pieces = refs[:team]
    grad_ssm_ref, u_tiles, g_tiles, y_tiles, full = refs[team:]
    tiles, length, unused = u_tiles.shape
    states = logr_ref.shape[0]
    span = length // SUBS
    width = tiles * LANES
    fill_tiles(u_tiles, normed_ref, place[0] * width)
    fill_tiles(g_tiles, grad_ref, 0)
    index = sub_index()
    after = ((SUBS - 1 - index) * span).astype(f32)
    full[...] = one_ref[...]
    group = GROUP // 2
    for tile in range(tiles):
        lanes = lane_tile(tile)
        rate = jnp.exp(logr_ref[:, lanes])
        decay = jnp.exp(-rate)
        root = jnp.sqrt(2.0 * rate)
        scale = coef_ref[:, lanes] * root
        in_b = jnp.zeros((states, LANES), f32)
        in_w = jnp.zeros((states, LANES), f32)
        for j in range(all_ref.shape[0]):
            gap = j - place[1] - 1
            distance = (jnp.maximum(gap, 0) * length).astype(f32)
            shrink = jnp.exp(-distance * rate)
            b, w = all_ref[j, 0, :, lanes], all_ref[j, 1, :, lanes]
            in_b = in_b + jnp.where(gap >= 0, shrink * b, 0.0)
            in_w = in_w + jnp.where(gap >= 0, shrink * (w + distance * b), 0.0)
        for first in range(0, states, group):
            chosen = range(first, first + group)
            starts = []
            for n in chosen:
                row = rate[n : n + 1]
                b, w = ends_ref[0, n, :, lanes], ends_ref[1, n, :, lanes]
                for d in (1, 2, 4):
                    shrink = jnp.exp(-(d * span) * row)
                    next_b = pltpu.roll(b, SUBS - d, 0)
                    next_w = pltpu.roll(w, SUBS - d, 0)
                    inside = index < SUBS - d
                    b, w = (
                        b + jnp.where(inside, shrink * next_b, 0.0),
                        w + jnp.where(inside, shrink * (next_w + (d * span) * next_b), 0.0),
                    )
                inside = index < SUBS - 1
                b = jnp.where(inside, pltpu.roll(b, SUBS - 1, 0), 0.0)
                w = jnp.where(inside, pltpu.roll(w, SUBS - 1, 0), 0.0)
                shrink = jnp.exp(-after * row)
                b_row, w_row = in_b[n : n + 1], in_w[n : n + 1]
                b = b + shrink * b_row
                w = w + shrink * (w_row + after * b_row)
                zero = no_state(u_tiles)
                starts.append((b, w, zero, zero))
            decays = [spread(decay[n : n + 1]) for n in chosen]
            scales = [spread(scale[n : n + 1]) for n in chosen]

            def step(i, held):
                at = pl.ds(span - 1 - i, SUBS, stride=span)
                g = g_tiles[tile, at, :]
                u = u_tiles[tile, at, :]
                later, parts = [], []
                for d, s, (b, w, sum_b, sum_w) in zip(decays, scales, held):
                    shrunk = d * b
                    w = d * w + shrunk
                    b = g + shrunk
                    later.append((b, w, sum_b + u * b, sum_w + u * w))
                    parts.append(s * b)
                while len(parts) > 1:
                    parts = [p + q for p, q in zip(parts[::2], parts[1::2])]
                if first > 0:
                    parts[0] = parts[0] + y_tiles[tile, at, :]
                y_tiles[tile, at, :] = parts[0]
                return tuple(later)

            held = lax.fori_loop(0, span, step, tuple(starts), unroll=4)
            for n, (unused_b, unused_w, sum_b, sum_w) in zip(chosen, held):
                sum_b = jnp.sum(sum_b, axis=0, keepdims=True)
                sum_w = jnp.sum(sum_w, axis=0, keepdims=True)
                row = slice(n, n + 1)
                grad_ssm_ref[0, row, lanes] = root[row] * sum_b
                grad_ssm_ref[1, row, lanes] = scale[row] * (0.5 * sum_b - rate[row] * sum_w)
        at_lanes = pl.ds(pl.multiple_of(place[0] * width + tile * LANES, LANES), LANES)
        full[:, at_lanes] += y_tiles[tile].astype(bf16).astype(f32)
    rows = pieces[0].shape[0]
    for k in range(team):
        at_rows = pl.ds(pl.multiple_of((place[0] ^ k) * rows, rows), rows)
        pieces[k][...] = full[at_rows, :].astype(bf16)


def input_grad_kernel(team, place, x_ref, gain_ref, middle_grad_ref, *refs):
    parts, (out_ref, gain_grad_ref) = refs[:team], refs[team:]
    rows = out_ref.shape[0]
    at_rows = pl.ds(pl.multiple_of(place[0] * rows, rows), rows)
    grad_one = parts[0][...].astype(f32)
    for part in parts[1:]:
        grad_one = grad_one + part[...].astype(f32)
    unit, inverse = normalise(x_ref[at_rows, :].astype(f32))
    gain_grad_ref[...] = jnp.sum(grad_one * unit, axis=0, keepdims=True)
    back = normalise_back(unit, inverse, grad_one * gain_ref[...])
    out_ref[...] = (middle_grad_ref[at_rows, :] + back).astype(bf16)


def assemble_kernel(halves, low_count, place, own_ref, *refs):
    others, out_ref = refs[:-1], refs[-1]
    count, rows, unused = own_ref.shape
    half = place[4]

    def put(value, sequence, which, member):
        at_rows = pl.ds(pl.multiple_of((which * low_count + member) * rows, rows), rows)
        out_ref[sequence, at_rows, :] = value.astype(out_ref.dtype)

    for sequence in range(count // (halves * low_count)):
        if halves == 1:
            for member in range(low_count):
                put(own_ref[sequence * low_count + member], sequence, 0, member)
        else:
            put(own_ref[sequence * halves + half], sequence, half, 0)
            put(others[0][sequence], sequence, 1 - half, 0)


def assemble_ring_kernel(halves, low_count, count, place, *refs):
    own, others, out_ref = refs[:count], refs[count:-1], refs[-1]
    rows = own[0].shape[0]
    index, half, swapped = place[3], place[4], place[5]

    def put(piece, steps, which):
        source = lax.rem(index + count - steps, count)
        member = lax.rem(source, low_count)
        sequence = source // (halves * low_count)
        at_rows = pl.ds(pl.multiple_of((which * low_count + member) * rows, rows), rows)
        out_ref[sequence, at_rows, :] = piece[...].astype(out_ref.dtype)

    if halves == 1:
        for k in range(count):
            put(own[k], k, 0)
        return
    for j in range(count // 2):
        put(others[j], 2 * j + swapped, 1 - half)
        for odd in range(2):

            @pl.when(swapped == odd)
            def keep():
                put(own[2 * j + odd], 2 * j + odd, half)


def pack_kernel(halves, place, qkv_ref, out_ref, up_ref, down_ref, *refs):
    rows = up_ref.shape[0]
    heads, hidden = out_ref.shape[0] // halves, up_ref.shape[1] // halves
    for which in range(halves):
        side = place[4] if which == 0 else 1 - place[4]
        at_heads = pl.ds(pl.multiple_of(side * heads, LANES), heads)
        at_hidden = pl.ds(pl.multiple_of(side * hidden, LANES), hidden)
        if which == 0:
            head_ref = refs[0]
            wide_ref, deep_ref = refs[1].at[:, :hidden], refs[1].at[:, hidden:]
        else:
            packed = refs[2]
            head_ref = packed.at[:, : 4 * heads]
            wide_ref = packed.at[:, 4 * heads : 4 * heads + hidden]
            deep_ref = packed.at[:, 4 * heads + hidden :]
        for i in range(3):
            head_ref[:, i * heads : (i + 1) * heads] = qkv_ref[i, :, at_heads].astype(bf16)
        head_ref[:, 3 * heads :] = out_ref[at_heads, :].T.astype(bf16)
        wide_ref[...] = up_ref[:, at_hidden].astype(bf16)
        deep_ref[...] = down_ref[at_hidden, :].T.astype(bf16)


def lamb_moments(weight, grad_item, first_old, second_old):
    first_new = beta_first * first_old + (1.0 - beta_first) * grad_item
    second_new = beta_second * second_old + (1.0 - beta_second) * grad_item * grad_item
    direction = (
        first_new
        / (1.0 - beta_first**STEP)
        / (jnp.sqrt(second_new / (1.0 - beta_second**STEP)) + lamb_eps)
        + weight_decay * weight
    )
    return (first_new, second_new, direction)


def place_sums(sums_ref, sums):
    rows = lax.broadcasted_iota(jnp.int32, sums_ref.shape, 0)
    lanes = lax.broadcasted_iota(jnp.int32, sums_ref.shape, 1)
    found = jnp.zeros(sums_ref.shape, f32)
    for index, pair in sums.items():
        for row, value in enumerate(pair):
            found = jnp.where((rows == row) & (lanes == index), value, found)
    sums_ref[...] = found


def moments_kernel(halves, matrices, place, *refs):
    count = 1 + max(item[1] for item in matrices)
    grads, refs = [refs[halves * i : halves * (i + 1)] for i in range(count)], refs[halves * count :]
    arrays = len({(item[1], item[4] is None) for item in matrices})
    ins = [refs[3 * i : 3 * i + 3] for i in range(arrays)]
    outs = [refs[3 * (arrays + i) : 3 * (arrays + i) + 3] for i in range(arrays)]
    sums_ref = refs[6 * arrays]
    keys = []
    sums = {}
    for number, source, column, turned, stacked in matrices:
        key = (source, stacked is None)
        if key not in keys:
            keys.append(key)
        pick = (lambda ref: ref) if stacked is None else (lambda ref, i=stacked: ref.at[i])
        weight, first, second = (pick(ref) for ref in ins[keys.index(key)])
        news = [pick(ref) for ref in outs[keys.index(key)]]
        width = weight.shape[0 if turned else 1] // halves
        rows = weight.shape[1 if turned else 0]
        cols = slice(column * width, (column + 1) * width)
        total_weight = total_update = 0.0
        for which, grad_ref in enumerate(grads[source]):
            side = place[4] if which == 0 else 1 - place[4]
            at = pl.ds(pl.multiple_of(side * width, width), width)
            if which == 0:
                grad = grad_ref[pl.ds(pl.multiple_of(side * rows, rows), rows), cols].astype(f32)
            else:
                grad = grad_ref[:, cols].astype(f32)
            at = (at, slice(None)) if turned else (slice(None), at)
            grad = grad.T if turned else grad
            old = weight[at]
            found = lamb_moments(old, grad, first[at], second[at])
            for ref, value in zip(news, found):
                ref[at] = value
            total_weight = total_weight + jnp.sum(old * old)
            total_update = total_update + jnp.sum(found[2] * found[2])
        sums[number] = (total_weight, total_update)
    place_sums(sums_ref, sums)


def small_moments_kernel(numbers, grads_ref, *refs):
    ins, outs, sums_ref = (refs[:3], refs[3:6]), (refs[6:9], refs[9:12]), refs[12]
    states = (grads_ref.shape[0] - 2) // 2
    sums = {}
    for (weight, first, second), news, start, rows, first_number in (
        (ins[0], outs[0], 2 * states, 1, numbers[0]),
        (ins[1], outs[1], 0, states, numbers[1]),
    ):
        for i in range(2):
            grad = grads_ref[start + i * rows : start + (i + 1) * rows, :]
            at = slice(i * rows, (i + 1) * rows)
            found = lamb_moments(weight[at, :], grad, first[at, :], second[at, :])
            for ref, value in zip(news, found):
                ref[at, :] = value
            sums[first_number + i] = (
                jnp.sum(weight[at, :] * weight[at, :]),
                jnp.sum(found[2] * found[2]),
            )
    place_sums(sums_ref, sums)


def update_kernel(stacks, sums_ref, *refs):
    count = len(stacks)
    weights, directions, news = refs[:count], refs[count : 2 * count], refs[2 * count : 3 * count]
    norms = jnp.sqrt(jnp.sum(sums_ref[...], axis=0))
    refs[3 * count][...] = norms
    ratios = norms[0:1] / norms[1:2]
    lanes = lax.broadcasted_iota(jnp.int32, ratios.shape, 1)
    for numbers, weight, direction, new in zip(stacks, weights, directions, news):
        step = weight.shape[0] // len(numbers)
        for i, number in enumerate(numbers):
            ratio = jnp.sum(jnp.where(lanes == number, ratios, 0.0), axis=1, keepdims=True)
            at = slice(i * step, (i + 1) * step)
            scale = learn_rate * ratio.reshape((1,) * weight.ndim)
            new[at] = weight[at] - scale * direction[at]


def call(
    body, ins, outs, scratch=(), grid=None, in_specs=None, out_specs=None, time=1.0, after=(), token=False
):
    moved = sum(a.size * a.dtype.itemsize for a in list(ins) + list(outs))
    params = pltpu.CompilerParams(vmem_limit_bytes=VMEM_BYTES)
    cost = pl.CostEstimate(flops=int(time * 1.15e9), bytes_accessed=moved, transcendentals=0)
    whole = pl.BlockSpec(memory_space=pltpu.VMEM)
    anywhere = pl.BlockSpec(memory_space=pl.ANY)
    in_specs = list(in_specs or [whole] * len(ins)) + [anywhere] * len(after)
    out_specs = list(out_specs or [whole] * len(outs))
    outs = list(outs)
    first_out = len(ins) + len(after)
    last_out = first_out + len(outs)
    if token:
        outs.append(jax.ShapeDtypeStruct((SUBS, LANES), f32))
        out_specs.append(whole)

    def run(*refs):
        refs = list(refs)
        if token:
            refs[last_out][...] = jnp.zeros((SUBS, LANES), f32)
            del refs[last_out]
        body(*refs[: len(ins)], *refs[first_out:])

    return pl.pallas_call(
        run,
        out_shape=tuple(outs),
        in_specs=in_specs,
        out_specs=tuple(out_specs),
        scratch_shapes=list(scratch),
        compiler_params=params,
        cost_estimate=cost,
        **({} if grid is None else {"grid": grid}),
    )(*ins, *after)


def shaped(shape, kind):
    return jax.ShapeDtypeStruct(tuple(shape), kind)


def on_device(
    tokens,
    cotangent,
    w_qkv,
    w_out,
    w_up,
    w_down,
    norm_gains,
    ssm_param,
    first_qkv,
    second_qkv,
    first_out,
    second_out,
    first_up,
    second_up,
    first_down,
    second_down,
    first_gain,
    second_gain,
    first_ssm,
    second_ssm,
):
    halves = lax.axis_size("sl")
    low_count = lax.axis_size("ml")
    row_parts = lax.axis_size("sh")
    col_parts = lax.axis_size("mb") * lax.axis_size("mq")
    team = halves * low_count
    sl, ml, mb, mq = (lax.axis_index(name) for name in ("sl", "ml", "mb", "mq"))
    rank = sl * low_count + ml
    block_index = lax.axis_index("sh") * halves + mq
    seq_total, length, width = tokens.shape
    assert length == BLK and seq_total == lax.axis_size("mb")
    states = ssm_param.shape[1]
    channels = width // team
    tiles = channels // LANES
    row_count = width // row_parts
    own_rows = length // team
    place = [rank, block_index, lax.axis_index("sh"), lax.axis_index(MODEL), sl, sl ^ mq]
    place.append(lax.axis_index(COLS))
    place = jnp.stack(place).astype(jnp.int32)
    smem = pl.BlockSpec(memory_space=pltpu.SMEM)
    vmem = pl.BlockSpec(memory_space=pltpu.VMEM)

    def permute(value, axes, moves):
        return lax.ppermute(value, axes, moves)

    def swap(value):
        return permute(value, "sl", [(0, 1), (1, 0)])

    def in_order(own, other, axis):
        return jnp.where(
            sl == 0, jnp.concatenate([own, other], axis), jnp.concatenate([other, own], axis)
        )

    def team_send(pieces):
        moved = [pieces[0]]
        for k in range(1, team):
            moved.append(permute(pieces[k], TEAM, [(i, i ^ k) for i in range(team)]))
        return moved

    def pick_block(array):
        own = lax.dynamic_index_in_dim(array, mb, 0, keepdims=False)
        if halves == 1:
            return own
        return jnp.where(sl == mq, own, swap(own))

    def across(value, bit):
        return permute(value, "sh", [(i, i ^ bit) for i in range(row_parts)])

    def along(value, axes, step):
        count = lax.axis_size(axes)
        return permute(value, axes, [(i, (i + step) % count) for i in range(count)])

    bits = [1 << i for i in range(row_parts.bit_length() - 1)]

    def bit_order(k):
        return bits if k % 2 == 0 else bits[::-1]

    def double_rows(value, order):
        found = {0: value}
        for bit in order:
            for r in list(found):
                found[r | bit] = across(found[r], bit)
        return [found[r] for r in range(row_parts)]

    def add(*items, zero=None):
        total = sum(item.astype(f32) for item in items)
        return (total if zero is None else total + zero[0, 0]).astype(bf16)

    def halve_rows(pieces, order, zero=None):
        sums = {r: [piece] for r, piece in enumerate(pieces)}
        rounds = []
        for index, bit in enumerate(reversed(order)):
            arrived = []
            for r in sorted((r for r in sums if r & bit), reverse=True):
                items = sums.pop(r)
                sent = add(*items, zero=zero) if index > 0 else items[0]
                arrived.append(across(sent, bit))
                sums[r ^ bit].append(arrived[-1])
            rounds.append(arrived)
        return add(*sums[0]), rounds

    def halve_both(near, far, zero=None):
        near, near_rounds = halve_rows(near, bits, zero)
        far, far_rounds = halve_rows(far, bits[::-1], zero)
        return near, far, [a + b for a, b in zip(near_rounds, far_rounds)]

    def ring_gather(shard):
        pieces, held = [], shard
        for k in range(col_parts):
            if k > 0:
                held = along(held, COLS, 1)
            pieces.append(double_rows(held, bits if k % 2 == 0 else bits[::-1]))
        return pieces

    def ring_sum(near, far):
        held = None
        for stack in (far, near):
            for k in reversed(range(stack.shape[0])):
                held = stack[k] if held is None else add(stack[k], along(held, COLS, -1))
        return held

    def everywhere(value, axes):
        count = lax.axis_size(axes)
        copies = jnp.broadcast_to(value[None], (count, *value.shape))
        return lax.all_to_all(copies, axes, 0, 0, tiled=True)

    small = jnp.concatenate([ssm_param.reshape(2 * states, -1), norm_gains], 0)
    small = jnp.transpose(everywhere(small, ALL), (1, 0, 2)).reshape(2 * states + 2, width)
    own_ssm = lax.dynamic_slice_in_dim(
        small[: 2 * states].reshape(2, states, width), rank * channels, channels, 2
    )
    coef, logr = own_ssm[0], own_ssm[1]
    gain_one = small[2 * states : 2 * states + 1]
    gain_two = small[2 * states + 1 : 2 * states + 2]

    rows_dev = w_up.shape[0]
    hidden_cols = w_up.shape[1] // halves
    head_cols = 4 * w_out.shape[0] // halves
    packed_cols = head_cols + 2 * hidden_cols
    sides = [shaped((rows_dev, cols), bf16) for cols in (head_cols, 2 * hidden_cols)]
    shards = call(
        functools.partial(pack_kernel, halves),
        (place, w_qkv, w_out, w_up, w_down),
        sides + [shaped((rows_dev, packed_cols), bf16)] * (halves - 1),
        time=2.4,
        in_specs=[smem] + [vmem] * 4,
    )
    if halves == 2:
        other = swap(shards[2])
        cuts = (0, head_cols, packed_cols)
        shards = [
            in_order(own, other[:, first:last], 0)
            for own, first, last in zip(shards, cuts, cuts[1:])
        ]
    head_shard, hidden_shard = shards[:2]
    pair = head_cols // 2
    attn_w = [
        *double_rows(lax.all_gather(head_shard[:, :pair], COLS, axis=0, tiled=False), bits),
        *double_rows(lax.all_gather(head_shard[:, pair:], COLS, axis=0, tiled=False), bits[::-1]),
    ]
    hidden_w = ring_gather(hidden_shard)

    x = pick_block(tokens)
    cot = pick_block(cotangent)

    anywhere = [pl.BlockSpec(memory_space=pl.ANY)]

    def fixed(*shape):
        return pl.BlockSpec(shape, lambda z: (0,) * len(shape))

    wide = fixed(length, width)
    row = fixed(1, width)

    normed_one, normed_t, ends, total = call(
        norm_kernel,
        (place, x, gain_one, logr),
        (
            shaped((length, width), bf16),
            shaped((width, length), bf16),
            shaped((states, SUBS, channels), f32),
            shaped((states, channels), f32),
        ),
        scratch=[pltpu.VMEM((tiles, length, LANES), f32)],
        in_specs=[smem, vmem, vmem, vmem],
        after=(*hidden_w[0][1:-1], hidden_w[1][0]),
        time=5,
    )
    totals = everywhere(total, ("sh", "mq"))
    (context_own,) = call(
        context_kernel,
        (place, normed_one, ends, totals, logr, coef),
        (shaped((length, channels), bf16),),
        after=(hidden_w[0][-1], *hidden_w[1][1:-1], *[group[0] for group in hidden_w[2:3]]),
        scratch=[pltpu.VMEM((tiles, length, LANES), f32)] * 2,
        in_specs=[smem] + [vmem] * 5,
        time=7,
    )
    contexts = team_send([context_own] * team)

    head_piece = shaped((col_parts // 2, row_count, head_cols), bf16)
    hidden_piece = shaped((col_parts // 2, row_count, hidden_cols), bf16)
    sizes = (team, col_parts, row_parts)
    head_buffer = pltpu.VMEM((4, row_parts, row_count, col_parts * HD), bf16)
    head_sems = pltpu.SemaphoreType.DMA((col_parts, row_parts, 4))
    kept_shape = shaped((4, length, col_parts * HD), bf16)
    context_t, cot_t, attn_part, kept, probs, probs_t = call(
        functools.partial(attend_kernel, *sizes),
        (place, normed_one, cot, *contexts, *attn_w),
        (
            shaped((width, length), bf16),
            shaped((width, length), bf16),
            shaped((length, width), bf16),
            kept_shape,
            *[shaped((col_parts, length, length), bf16)] * 2,
        ),
        scratch=[pltpu.VMEM((length, width), bf16), head_buffer, head_sems],
        time=13,
        in_specs=[smem] + [vmem] * (2 + team) + anywhere * (2 * row_parts),
        after=(hidden_w[1][-1], *[group[0] for group in hidden_w[3:4]]),
    )
    attn_parts = team_send([attn_part] * team)

    hidden_buffer = pltpu.VMEM((col_parts, row_parts, row_count, hidden_cols), bf16)
    middle, out_part, two_part, *hidden_grads = call(
        functools.partial(feed_kernel, *sizes),
        (place, x, cot, cot_t, gain_two, *attn_parts, *[p for group in hidden_w for p in group]),
        (
            shaped((length, width), f32),
            shaped((length, width), bf16),
            shaped((length, width), bf16),
            *[hidden_piece] * (4 * row_parts),
        ),
        scratch=[
            *[hidden_buffer] * 4,
            pltpu.VMEM((length, width), bf16),
            pltpu.VMEM((width, length), bf16),
            pltpu.VMEM((length, width), f32),
            pltpu.VMEM((length, width), f32),
            pltpu.SemaphoreType.DMA((4, col_parts, row_parts)),
        ],
        time=20,
        grid=(col_parts,),
        in_specs=[smem, wide, wide, fixed(width, length), row]
        + [wide] * team
        + anywhere * (col_parts * row_parts),
        out_specs=[wide, wide, wide] + anywhere * (4 * row_parts),
    )
    two_parts = team_send([two_part] * team)

    def rows_of(array, member):
        return lax.dynamic_slice_in_dim(array, member * own_rows, own_rows, 0)

    def share_rows(own_piece, kind):
        pieces = lax.all_gather(own_piece, MODEL, axis=0, tiled=False)
        others = []
        if halves == 2:
            pairs = pieces.reshape(seq_total, halves, own_rows, width)
            others = [swap(lax.dynamic_index_in_dim(pairs, 1 - sl, 1, keepdims=False))]
        (blocks,) = call(
            functools.partial(assemble_kernel, halves, low_count),
            (place, pieces, *others),
            (shaped((seq_total, length, width), kind),),
            time=3.5,
            in_specs=[smem, vmem] + [vmem] * len(others),
        )
        return blocks

    def share_ring(own_piece, kind):
        pieces = [own_piece]
        count = lax.axis_size(MODEL)
        for unused in range(count - 1):
            pieces.append(along(pieces[-1], MODEL, 1))
        others = []
        if halves == 2:
            for even, odd in zip(pieces[::2], pieces[1::2]):
                others.append(swap(jnp.where(sl == mq, odd, even)))
        (blocks,) = call(
            functools.partial(assemble_ring_kernel, halves, low_count, count),
            (place, *pieces, *others),
            (shaped((seq_total, length, width), kind),),
            time=3.5,
            in_specs=[smem] + [vmem] * (len(pieces) + len(others)),
        )
        return blocks

    out_pieces = team_send([rows_of(out_part, rank ^ k) for k in range(team)])
    result = rows_of(middle, rank) + sum(item.astype(f32) for item in out_pieces)
    layer_out = share_rows(result.astype(bf16), bf16)

    def both_halves(own):
        if halves == 1:
            return [own]
        return [own, swap(lax.dynamic_slice_in_dim(own, (1 - sl) * rows_dev, rows_dev, 0))]

    middle_grad, gain_two_grad, one_part, *rest, back_done = call(
        functools.partial(attend_back_kernel, *sizes),
        (place, middle, gain_two, cot, *two_parts, normed_t, context_t, kept, probs, probs_t, *attn_w),
        (
            shaped((length, width), f32),
            shaped((1, width), f32),
            shaped((length, width), f32),
            *[shaped((length, channels), bf16)] * team,
            *[head_piece] * (2 * row_parts),
        ),
        scratch=[
            head_buffer,
            head_buffer,
            pltpu.VMEM((length, width), bf16),
            *[pltpu.VMEM((length, col_parts * HD), bf16)] * 4,
            head_sems,
            head_sems,
        ],
        in_specs=[smem] + [vmem] * (3 + team + 5) + anywhere * (2 * row_parts),
        out_specs=[vmem] * (3 + team) + anywhere * (2 * row_parts),
        token=True,
        time=20.5,
    )
    context_grads = team_send(rest[:team])
    groups = [hidden_grads[i * row_parts : (i + 1) * row_parts] for i in range(4)]
    down_near, down_far, down_rounds = halve_both(groups[2], groups[3], back_done)
    grad_down = lax.psum_scatter(
        jnp.concatenate([down_near, down_far], 0), COLS, scatter_dimension=0, tiled=False
    )

    context_grad, adjoint_ends, adjoint_total = call(
        functools.partial(adjoint_kernel, team),
        (logr, *context_grads),
        (
            shaped((length, channels), bf16),
            shaped((2, states, SUBS, channels), f32),
            shaped((2, states, channels), f32),
        ),
        scratch=[pltpu.VMEM((tiles, length, LANES), f32)],
        time=6.7,
        after=down_rounds[0],
    )
    adjoint_totals = everywhere(adjoint_total, ("sh", "mq"))
    *one_pieces, grad_ssm, adjoint_done = call(
        functools.partial(context_back_kernel, team),
        (place, context_grad, normed_one, adjoint_ends, adjoint_totals, logr, coef, one_part),
        (
            *[shaped((own_rows, width), bf16)] * team,
            shaped((2, states, channels), f32),
        ),
        scratch=[pltpu.VMEM((tiles, length, LANES), f32)] * 3 + [pltpu.VMEM((length, width), f32)],
        in_specs=[smem] + [vmem] * 7,
        time=12,
        after=down_rounds[-1],
        token=True,
    )
    one_pieces = team_send(one_pieces)
    up_near, up_far, up_rounds = halve_both(groups[0], groups[1], adjoint_done)
    grad_up = ring_sum(up_near, up_far)
    grad_rows, gain_one_grad = call(
        functools.partial(input_grad_kernel, team),
        (place, x, gain_one, middle_grad, *one_pieces),
        (shaped((own_rows, width), bf16), shaped((1, width), f32)),
        in_specs=[smem] + [vmem] * (3 + team),
        time=4,
    )
    input_grad = share_ring(grad_rows, f32)
    near, far, unused = halve_both(rest[team : team + row_parts], rest[team + row_parts :])
    grad_heads = ring_sum(near, far)

    placed_ssm = lax.dynamic_update_slice_in_dim(
        jnp.zeros((2 * states, width), f32),
        grad_ssm.reshape(2 * states, channels),
        rank * channels,
        1,
    )
    small_grads = jnp.concatenate([placed_ssm, gain_one_grad, gain_two_grad], 0)
    small_grads = small_grads.reshape(2 * states + 2, lax.axis_size(ALL), -1)
    small_grads = lax.all_to_all(jnp.transpose(small_grads, (1, 0, 2)), ALL, 0, 0, tiled=True)
    small_grads = jnp.sum(small_grads, axis=0)

    def moments(matrices, grads, arrays):
        changed = [shaped(old.shape, f32) for group in arrays for old in group]
        grad_parts = [part for grad in grads for part in both_halves(grad)]
        ins = [item for group in arrays for item in group]
        *found, sums = call(
            functools.partial(moments_kernel, halves, matrices),
            (place, *grad_parts, *ins),
            (*changed, shaped((2, LANES), f32)),
            in_specs=[smem] + [vmem] * (len(grad_parts) + len(ins)),
            time=4,
        )
        return [found[3 * i : 3 * i + 3] for i in range(len(arrays))], sums

    hidden_new, hidden_sums = moments(
        ((4, 0, 0, False, None), (5, 1, 0, True, None)),
        (grad_up, grad_down),
        ((w_up, first_up, second_up), (w_down, first_down, second_down)),
    )
    heads_new, head_sums = moments(
        tuple((i, 0, i, False, i) for i in range(3)) + ((3, 0, 3, True, None),),
        (grad_heads,),
        ((w_qkv, first_qkv, second_qkv), (w_out, first_out, second_out)),
    )
    own_channels = norm_gains.shape[1]
    ssm_items = [item.reshape(2 * states, own_channels) for item in (ssm_param, first_ssm, second_ssm)]
    small_items = [norm_gains, first_gain, second_gain, *ssm_items]
    *small_new, small_sums = call(
        functools.partial(small_moments_kernel, (6, 8)),
        (small_grads.reshape(2 * states + 2, own_channels), *small_items),
        (*[shaped(item.shape, f32) for item in small_items], shaped((2, LANES), f32)),
    )
    all_sums = everywhere(hidden_sums + head_sums + small_sums, ALL)
    masters = (w_qkv, w_out, w_up, w_down, norm_gains, ssm_items[0])
    news = (*heads_new, *hidden_new, small_new[:3], small_new[3:])
    *weights, norms = call(
        functools.partial(update_kernel, ((0, 1, 2), (3,), (4,), (5,), (6, 7), (8, 9))),
        (all_sums, *masters, *[group[2] for group in news]),
        (*[shaped(item.shape, f32) for item in masters], shaped((2, LANES), f32)),
        time=3.2,
    )
    outputs = [layer_out, input_grad]
    for index, (weight, (first_new, second_new, unused)) in enumerate(zip(weights, news)):
        if index == 4:
            outputs += [weight, first_new, second_new[0], second_new[1]]
        else:
            kept_shape = ssm_param.shape if index == 5 else weight.shape
            outputs += [item.reshape(kept_shape) for item in (weight, first_new, second_new)]
    outputs.append(norms[:, :10])
    return tuple(outputs)


def solution(mesh):
    seq_count, model_count = mesh.shape["seq"], mesh.shape["mp"]
    halves = 2 if HEADS // model_count >= 2 else 1
    sizes = (seq_count // halves, halves, SEQS, halves, model_count // (SEQS * halves))
    fine = Mesh(mesh.devices.reshape(sizes), ALL)
    seq, model = ("sh", "sl"), ("mb", "mq", "ml")
    rows_cols, cols_rows = P(seq, model), P(model, seq)
    token = P(None, seq, None)
    stack = P(None, seq, model)
    gains = P(None, ALL)
    ssm = P(None, None, ALL)
    return jax.shard_map(
        on_device,
        mesh=fine,
        in_specs=(token, token, stack, cols_rows, rows_cols, cols_rows, gains, ssm)
        + (stack,) * 2
        + (cols_rows,) * 2
        + (rows_cols,) * 2
        + (cols_rows,) * 2
        + (gains,) * 2
        + (ssm,) * 2,
        out_specs=(token, token)
        + (stack,) * 3
        + (cols_rows,) * 3
        + (rows_cols,) * 3
        + (cols_rows,) * 3
        + (gains, gains, P(ALL), P(ALL))
        + (ssm,) * 3
        + (P(),),
        check_vma=False,
    )
```

```python
import functools
import math

import jax
import jax.numpy as jnp
from jax import lax
from jax.experimental import pallas as pl
from jax.experimental.pallas import tpu as pltpu
from jax.sharding import Mesh
from jax.sharding import PartitionSpec as P

HD = 128
HEADS = 8
BLK = 512
STEP = 10
SEQS = 2
LANES = 128
SUBS = 8
GROUP = 8

norm_eps = 1e-05
beta_first = 0.9
beta_second = 0.999
lamb_eps = 1e-06
weight_decay = 0.01
learn_rate = 0.5
score_scale = HD ** (-0.5)

f32 = jnp.float32
bf16 = jnp.bfloat16
VMEM_BYTES = 56 * 1024 * 1024

ALL = ("sh", "sl", "mb", "mq", "ml")
MODEL = ("mb", "mq", "ml")
COLS = ("mb", "mq")
TEAM = ("sl", "ml")


def dot(left, right):
    return lax.dot_general(left, right, (((1,), (0,)), ((), ())), preferred_element_type=f32)


def dot_t(left, right):
    return lax.dot_general(left, right, (((1,), (1,)), ((), ())), preferred_element_type=f32)


def normalise(values):
    centred = values - jnp.mean(values, axis=-1, keepdims=True)
    inverse = lax.rsqrt(jnp.mean(centred * centred, axis=-1, keepdims=True) + norm_eps)
    return centred * inverse, inverse


def normalise_back(unit, inverse, grad_unit):
    mean_one = jnp.mean(grad_unit, axis=-1, keepdims=True)
    mean_two = jnp.mean(grad_unit * unit, axis=-1, keepdims=True)
    return inverse * (grad_unit - mean_one - unit * mean_two)


def sub_index():
    return lax.broadcasted_iota(jnp.int32, (SUBS, LANES), 0)


def spread(row):
    return jnp.broadcast_to(row, (SUBS, LANES))


def lane_tile(index):
    return slice(index * LANES, (index + 1) * LANES)


def no_state(tiles):
    rows = tiles[0, :SUBS, :]
    return rows - rows


def in_steps(steps, tile, rows):
    span = rows.shape[0] // SUBS

    def move(i, unused):
        steps[tile, pl.ds(pl.multiple_of(i * SUBS, SUBS), SUBS), :] = rows[
            pl.ds(i, SUBS, stride=span), :
        ]
        return unused

    lax.fori_loop(0, span, move, 0, unroll=8)


def from_steps(rows, steps, tile):
    span = rows.shape[0] // SUBS

    def move(i, unused):
        rows[pl.ds(i, SUBS, stride=span), :] = steps[
            tile, pl.ds(pl.multiple_of(i * SUBS, SUBS), SUBS), :
        ]
        return unused

    lax.fori_loop(0, span, move, 0, unroll=8)


def step_rows(i):
    return pl.ds(pl.multiple_of(i * SUBS, SUBS), SUBS)


def norm_kernel(
    place, x_ref, gain_ref, logr_ref, normed_ref, turned_ref, u_tiles, ends_ref, total_ref, rows
):
    unit, unused = normalise(x_ref[...].astype(f32))
    normed_ref[...] = (unit * gain_ref[...]).astype(bf16)
    turned_ref[...] = normed_ref[...].T
    tiles, length, unused = u_tiles.shape
    states = logr_ref.shape[0]
    span = length // SUBS
    for tile in range(tiles):
        start = place[0] * (tiles * LANES) + tile * LANES
        rows[...] = normed_ref[:, pl.ds(pl.multiple_of(start, LANES), LANES)].astype(f32)
        in_steps(u_tiles, tile, rows)
    left = ((SUBS - 1 - sub_index()) * span).astype(f32)
    for tile in range(tiles):
        rate = jnp.exp(logr_ref[:, lane_tile(tile)])
        decay = jnp.exp(-rate)
        decays = [spread(decay[n : n + 1]) for n in range(states)]

        def step(i, held):
            u = u_tiles[tile, step_rows(i), :]
            return tuple(d * h + u for d, h in zip(decays, held))

        zero = no_state(u_tiles)
        held = lax.fori_loop(0, span, step, (zero,) * states, unroll=4)
        for n in range(states):
            ends_ref[n, :, lane_tile(tile)] = held[n]
            total_ref[n : n + 1, lane_tile(tile)] = jnp.sum(
                held[n] * jnp.exp(-left * rate[n : n + 1]), axis=0, keepdims=True
            )


def context_kernel(
    place, u_tiles, ends_ref, all_ref, logr_ref, coef_ref, context_ref, y_tiles, rows
):
    tiles, length, unused = u_tiles.shape
    states = logr_ref.shape[0]
    span = length // SUBS
    index = sub_index()
    before = (index * span).astype(f32)
    for tile in range(tiles):
        rate = jnp.exp(logr_ref[:, lane_tile(tile)])
        decay = jnp.exp(-rate)
        scale = coef_ref[:, lane_tile(tile)] * jnp.sqrt(2.0 * rate)
        incoming = jnp.zeros((states, LANES), f32)
        for j in range(all_ref.shape[0]):
            gap = place[1] - 1 - j
            distance = (jnp.maximum(gap, 0) * length).astype(f32)
            term = jnp.exp(-distance * rate) * all_ref[j, :, lane_tile(tile)]
            incoming = incoming + jnp.where(gap >= 0, term, 0.0)
        for first in range(0, states, GROUP):
            chosen = range(first, first + GROUP)
            starts = []
            for n in chosen:
                row = rate[n : n + 1]
                run = ends_ref[n, :, lane_tile(tile)]
                for d in (1, 2, 4):
                    moved = jnp.exp(-(d * span) * row) * pltpu.roll(run, d, 0)
                    run = run + jnp.where(index >= d, moved, 0.0)
                run = jnp.where(index >= 1, pltpu.roll(run, 1, 0), 0.0)
                starts.append(run + jnp.exp(-before * row) * incoming[n : n + 1])
            decays = [spread(decay[n : n + 1]) for n in chosen]
            scales = [spread(scale[n : n + 1]) for n in chosen]

            def step(i, held):
                at = step_rows(i)
                u = u_tiles[tile, at, :]
                held = tuple(d * h + u for d, h in zip(decays, held))
                parts = [s * h for s, h in zip(scales, held)]
                if first > 0:
                    parts[0] = parts[0] + y_tiles[tile, at, :]
                while len(parts) > 1:
                    parts = [a + b for a, b in zip(parts[::2], parts[1::2])]
                y_tiles[tile, at, :] = parts[0]
                return held

            lax.fori_loop(0, span, step, tuple(starts), unroll=4)
        from_steps(rows, y_tiles, tile)
        context_ref[:, lane_tile(tile)] = rows[...].astype(bf16)


def whole_rows(block):
    return block.reshape(block.shape[0] * block.shape[1], block.shape[2])


def head(index):
    return slice(index * HD, (index + 1) * HD)


def head_copies(outsides, buffer, place, sems, inward):
    copies = []
    for k, group in enumerate(outsides):
        for r, outside in enumerate(group):
            for i in range(4):
                outer = outside.at[:, pl.ds(i * HD, HD)]
                inner = buffer.at[i, place[2] ^ r, :, pl.ds(k * HD, HD)]
                ends = (outer, inner) if inward else (inner, outer)
                copies.append(pltpu.make_async_copy(*ends, sems.at[k, r, i]))
    return copies


def weight_copies(near, far, buffer, place, sems, act):
    count = sems.shape[0]
    half = count // 2
    for k in range(count):
        owner = lax.rem(place[6] + count - k, count)
        inner = buffer.at[:, :, :, pl.ds(k * HD, HD)]
        for stacks, low in ((near, 0), (far, half)):

            @pl.when((owner >= low) & (owner < low + half))
            def move():
                group = [stack.at[owner - low] for stack in stacks]
                for copy in head_copies([group], inner, place, sems.at[pl.ds(k, 1)], True):
                    act(copy)


def gradient_slot(row_parts, order, r):
    position = 0
    for bit in reversed(order):
        position = 2 * position + (1 if r & bit else 0)
    return position // (row_parts // 2), position % (row_parts // 2)


def round_orders(row_parts):
    bits = [1 << i for i in range(row_parts.bit_length() - 1)]
    return bits, bits[::-1]


def gradient_pieces(stacks, row_parts, far, slot):
    found = []
    for r in range(row_parts):
        sent, at = gradient_slot(row_parts, round_orders(row_parts)[far], r)
        found.append(stacks[2 * far + sent].at[at, slot])
    return found


def attend_kernel(team, col_parts, row_parts, place, normed_ref, cot_ref, *refs):
    contexts, refs = refs[:team], refs[team:]
    near, far, refs = refs[:row_parts], refs[row_parts : 2 * row_parts], refs[2 * row_parts :]
    context_t_ref, cot_t_ref, part_ref, kept_ref, probs_ref, probs_t_ref = refs[:6]
    context_ref, weights, sems = refs[6:]
    weight_copies(near, far, weights, place, sems, lambda copy: copy.start())
    width = contexts[0].shape[1]
    for k in range(team):
        lanes = pl.ds(pl.multiple_of((place[0] ^ k) * width, LANES), width)
        context_ref[:, lanes] = contexts[k][...]
    context_t_ref[...] = context_ref[...].T
    cot_t_ref[...] = cot_ref[...].T
    weight_copies(near, far, weights, place, sems, lambda copy: copy.wait())
    kept_ref[0] = dot(normed_ref[...], whole_rows(weights[0])).astype(bf16)
    kept_ref[1] = dot(context_ref[...], whole_rows(weights[1])).astype(bf16)
    kept_ref[2] = dot(context_ref[...], whole_rows(weights[2])).astype(bf16)
    length = normed_ref.shape[0]
    rows = lax.broadcasted_iota(jnp.int32, (length, length), 0)
    cols = lax.broadcasted_iota(jnp.int32, (length, length), 1)
    for h in range(col_parts):
        scores = dot_t(kept_ref[0, :, head(h)], kept_ref[1, :, head(h)]) * score_scale
        scores = jnp.where(rows >= cols, scores, -1e30)
        shifted = jnp.exp(scores - jnp.max(scores, axis=-1, keepdims=True))
        inverse = 1.0 / jnp.sum(shifted, axis=-1, keepdims=True)
        probs = (shifted * inverse).astype(bf16)
        probs_ref[h] = probs
        probs_t_ref[h] = probs.T
        kept_ref[3, :, head(h)] = dot(probs, kept_ref[2, :, head(h)]).astype(bf16)
    part_ref[...] = dot_t(kept_ref[3], whole_rows(weights[3])).astype(bf16)


def gelu_parts(hidden, grad_act):
    cdf = 0.5 * (1.0 + lax.erf(hidden * math.sqrt(0.5)))
    slope = cdf + hidden * jnp.exp(-0.5 * hidden * hidden) * (1.0 / math.sqrt(2.0 * math.pi))
    return (hidden * cdf).astype(bf16), (grad_act * slope).astype(bf16)


def middle_kernel(team, x_ref, gain_ref, *refs):
    parts, (middle_ref, normed_ref, normed_t_ref) = refs[:team], refs[team:]
    attn = parts[0][...].astype(f32)
    for part in parts[1:]:
        attn = attn + part[...].astype(f32)
    middle = x_ref[...].astype(f32) + attn
    middle_ref[...] = middle
    unit, unused = normalise(middle)
    normed_ref[...] = (unit * gain_ref[...]).astype(bf16)
    normed_t_ref[...] = normed_ref[...].T


def feed_kernel(col_parts, row_parts, place, normed_ref, normed_t_ref, cot_ref, cot_t_ref, *refs):
    count = col_parts * row_parts
    pieces, refs = refs[:count], refs[count:]
    out_ref, two_ref = refs[:2]
    stacks, refs = (refs[2:6], refs[6:10]), refs[10:]
    up_all, down_all, grad_up, grad_down, activated_all, grad_all, sems = refs
    z = pl.program_id(0)
    half = col_parts // 2
    hidden_cols = grad_up.shape[3]

    def copies(k):
        found = []
        for r in range(row_parts):
            piece = pieces[k * row_parts + r]
            for which, buffer in enumerate((up_all, down_all)):
                outside = piece.at[:, pl.ds(which * hidden_cols, hidden_cols)]
                inside = buffer.at[place[2] ^ r, :, pl.ds(k * hidden_cols, hidden_cols)]
                found.append(pltpu.make_async_copy(outside, inside, sems.at[which, k, r]))
        return found

    def leaving(which, k, far, slot, act):
        buffer = (grad_up, grad_down)[which]
        for r, piece in enumerate(gradient_pieces(stacks[which], row_parts, far, slot)):
            act(pltpu.make_async_copy(buffer.at[k, place[2] ^ r], piece, sems.at[2 + which, k, r]))

    def each_leaving(k, act):
        leaving(0, k, k // half, k % half, act)
        owner = lax.rem(place[6] + col_parts - k, col_parts)
        for far in range(2):

            @pl.when(owner // half == far)
            def down_leaves():
                leaving(1, k, far, lax.rem(owner, half), act)

    @pl.when(z == 0)
    def start():
        for k in range(col_parts):
            for copy in copies(k):
                copy.start()

    for k in range(col_parts):

        @pl.when(z == k)
        def arrive():
            for copy in copies(k):
                copy.wait()

    at = pl.ds(pl.multiple_of(z * hidden_cols, hidden_cols), hidden_cols)
    hidden = dot(normed_ref[...], whole_rows(up_all[:, :, at]))
    grad_act = dot(cot_ref[...], whole_rows(down_all[:, :, at]))
    activated, grad_pre = gelu_parts(hidden, grad_act)
    activated_all[:, at] = activated
    grad_all[:, at] = grad_pre
    shape = grad_up.shape[1:]
    grad_up[z] = dot(normed_t_ref[...], grad_pre).astype(bf16).reshape(shape)
    grad_down[z] = dot(cot_t_ref[...], activated).astype(bf16).reshape(shape)

    for k in range(col_parts):

        @pl.when(z == k)
        def leave():
            each_leaving(k, lambda copy: copy.start())

    @pl.when(z == col_parts - 1)
    def finish():
        two_ref[...] = dot_t(grad_all[...], whole_rows(up_all[...])).astype(bf16)
        out_ref[...] = dot_t(activated_all[...], whole_rows(down_all[...])).astype(bf16)
        for k in range(col_parts):
            each_leaving(k, lambda copy: copy.wait())


def attend_back_kernel(team, col_parts, row_parts, place, middle_ref, gain_ref, cot_ref, *refs):
    parts, refs = refs[:team], refs[team:]
    late, refs = refs[:5], refs[5:]
    near, far, refs = refs[:row_parts], refs[row_parts : 2 * row_parts], refs[2 * row_parts :]
    middle_grad_ref, gain_grad_ref, one_ref = refs[:3]
    refs = refs[3:]
    context_grads, refs = refs[:team], refs[team:]
    stacks, refs = refs[:4], refs[4:]
    weights, grads, low, grad_out, grad_q, grad_k, grad_v = refs[:7]
    held, (sems, out_sems, late_sems) = refs[7:12], refs[12:]
    normed_t_ref, context_t_ref, kept_ref, probs_ref, probs_t_ref = held
    half = col_parts // 2
    weight_copies(near, far, weights, place, sems, lambda copy: copy.start())
    late_copies = [
        pltpu.make_async_copy(outside, inside, late_sems.at[i])
        for i, (outside, inside) in enumerate(zip(late, held))
    ]
    for copy in late_copies:
        copy.start()
    own_rows = middle_ref.shape[0] // team
    grad_two = parts[0][...].astype(f32)
    for part in parts[1:]:
        grad_two = grad_two + part[...].astype(f32)
    unit, inverse = normalise(middle_ref[...])
    grad_gain = grad_two * unit
    rows = lax.broadcasted_iota(jnp.int32, grad_gain.shape, 0)
    first = place[0] * own_rows
    mine = (rows >= first) & (rows < first + own_rows)
    gain_grad_ref[...] = jnp.sum(jnp.where(mine, grad_gain, 0.0), axis=0, keepdims=True)
    grad = cot_ref[...].astype(f32) + normalise_back(unit, inverse, grad_two * gain_ref[...])
    low[...] = grad.astype(bf16)
    for k in range(team):

        @pl.when(place[0] == k)
        def own():
            middle_grad_ref[...] = grad[k * own_rows : (k + 1) * own_rows, :]

    weight_copies(near, far, weights, place, sems, lambda copy: copy.wait())
    for copy in late_copies:
        copy.wait()
    grad_out[...] = dot(low[...], whole_rows(weights[3])).astype(bf16)
    for h in range(col_parts):
        q, k, v = (kept_ref[i, :, head(h)] for i in range(3))
        grad_heads = grad_out[:, head(h)]
        grad_v[:, head(h)] = dot(probs_t_ref[h], grad_heads).astype(bf16)
        probs = probs_ref[h].astype(f32)
        grad_probs = dot_t(grad_heads, v)
        inner = jnp.sum(grad_probs * probs, axis=-1, keepdims=True)
        grad_scores = (probs * (grad_probs - inner)).astype(bf16)
        grad_q[:, head(h)] = (dot(grad_scores, k) * score_scale).astype(bf16)
        turned = dot_t(v, grad_heads) - inner.T
        turned = (probs_t_ref[h].astype(f32) * turned).astype(bf16)
        grad_k[:, head(h)] = (dot(turned, q) * score_scale).astype(bf16)
    shape = grads.shape[1:]
    grads[3] = dot(low[...].T, kept_ref[3]).astype(bf16).reshape(shape)
    grads[0] = dot(normed_t_ref[...], grad_q[...]).astype(bf16).reshape(shape)
    grads[1] = dot(context_t_ref[...], grad_k[...]).astype(bf16).reshape(shape)
    grads[2] = dot(context_t_ref[...], grad_v[...]).astype(bf16).reshape(shape)
    outsides = [gradient_pieces(stacks, row_parts, k // half, k % half) for k in range(col_parts)]
    copies = []
    for slot in range(col_parts):
        sem = out_sems.at[pl.ds(slot, 1)]
        copies += head_copies([outsides[slot]], grads.at[:, :, :, pl.ds(slot * HD, HD)], place, sem, False)
    for copy in copies:
        copy.start()
    total = dot_t(grad_k[...], whole_rows(weights[1])) + dot_t(grad_v[...], whole_rows(weights[2]))
    middle_total = total.astype(bf16)
    low[...] = middle_total
    width = context_grads[0].shape[1]
    for k in range(team):
        lanes = pl.ds(pl.multiple_of((place[0] ^ k) * width, LANES), width)
        context_grads[k][...] = low[:, lanes]
    one_ref[...] = dot_t(grad_q[...], whole_rows(weights[0])).astype(bf16)
    for copy in copies:
        copy.wait()


def adjoint_kernel(team, logr_ref, *refs):
    parts = refs[:team]
    g_tiles, ends_ref, total_ref, rows = refs[team:]
    grad = parts[0][...].astype(f32)
    for part in parts[1:]:
        grad = grad + part[...].astype(f32)
    grad = grad.astype(bf16).astype(f32)
    tiles, length, unused = g_tiles.shape
    states = logr_ref.shape[0]
    span = length // SUBS
    for tile in range(tiles):
        rows[...] = grad[:, lane_tile(tile)]
        in_steps(g_tiles, tile, rows)
    before = (sub_index() * span).astype(f32)
    for tile in range(tiles):
        rate = jnp.exp(logr_ref[:, lane_tile(tile)])
        decay = jnp.exp(-rate)
        for first in range(0, states, GROUP):
            chosen = range(first, first + GROUP)
            decays = [spread(decay[n : n + 1]) for n in chosen]

            def step(i, held):
                g = g_tiles[tile, step_rows(span - 1 - i), :]
                later = []
                for d, (b, w) in zip(decays, held):
                    shrunk = d * b
                    later.append((g + shrunk, d * w + shrunk))
                return tuple(later)

            zero = no_state(g_tiles)
            held = lax.fori_loop(0, span, step, ((zero, zero),) * GROUP, unroll=4)
            for n, (b, w) in zip(chosen, held):
                ends_ref[0, n, :, lane_tile(tile)] = b
                ends_ref[1, n, :, lane_tile(tile)] = w
                shrink = jnp.exp(-before * rate[n : n + 1])
                total_ref[0, n : n + 1, lane_tile(tile)] = jnp.sum(
                    shrink * b, axis=0, keepdims=True
                )
                total_ref[1, n : n + 1, lane_tile(tile)] = jnp.sum(
                    shrink * (w + before * b), axis=0, keepdims=True
                )


def context_back_kernel(
    team, place, g_tiles, u_tiles, ends_ref, all_ref, logr_ref, coef_ref, one_ref, *refs
):
    pieces = refs[:team]
    grad_ssm_ref, y_tiles, full, rows = refs[team:]
    tiles, length, unused = u_tiles.shape
    states = logr_ref.shape[0]
    span = length // SUBS
    width = tiles * LANES
    index = sub_index()
    after = ((SUBS - 1 - index) * span).astype(f32)
    full[...] = one_ref[...].astype(f32)
    group = GROUP
    for tile in range(tiles):
        lanes = lane_tile(tile)
        rate = jnp.exp(logr_ref[:, lanes])
        decay = jnp.exp(-rate)
        root = jnp.sqrt(2.0 * rate)
        scale = coef_ref[:, lanes] * root
        in_b = jnp.zeros((states, LANES), f32)
        in_w = jnp.zeros((states, LANES), f32)
        for j in range(all_ref.shape[0]):
            gap = j - place[1] - 1
            distance = (jnp.maximum(gap, 0) * length).astype(f32)
            shrink = jnp.exp(-distance * rate)
            b, w = all_ref[j, 0, :, lanes], all_ref[j, 1, :, lanes]
            in_b = in_b + jnp.where(gap >= 0, shrink * b, 0.0)
            in_w = in_w + jnp.where(gap >= 0, shrink * (w + distance * b), 0.0)
        for first in range(0, states, group):
            chosen = range(first, first + group)
            starts = []
            for n in chosen:
                row = rate[n : n + 1]
                b, w = ends_ref[0, n, :, lanes], ends_ref[1, n, :, lanes]
                for d in (1, 2, 4):
                    shrink = jnp.exp(-(d * span) * row)
                    next_b = pltpu.roll(b, SUBS - d, 0)
                    next_w = pltpu.roll(w, SUBS - d, 0)
                    inside = index < SUBS - d
                    b, w = (
                        b + jnp.where(inside, shrink * next_b, 0.0),
                        w + jnp.where(inside, shrink * (next_w + (d * span) * next_b), 0.0),
                    )
                inside = index < SUBS - 1
                b = jnp.where(inside, pltpu.roll(b, SUBS - 1, 0), 0.0)
                w = jnp.where(inside, pltpu.roll(w, SUBS - 1, 0), 0.0)
                shrink = jnp.exp(-after * row)
                b_row, w_row = in_b[n : n + 1], in_w[n : n + 1]
                b = b + shrink * b_row
                w = w + shrink * (w_row + after * b_row)
                zero = no_state(u_tiles)
                starts.append((b, w, zero, zero))
            decays = [spread(decay[n : n + 1]) for n in chosen]
            scales = [spread(scale[n : n + 1]) for n in chosen]

            def step(i, held):
                at = step_rows(span - 1 - i)
                g = g_tiles[tile, at, :]
                u = u_tiles[tile, at, :]
                later, parts = [], []
                for d, s, (b, w, sum_b, sum_w) in zip(decays, scales, held):
                    shrunk = d * b
                    w = d * w + shrunk
                    b = g + shrunk
                    later.append((b, w, sum_b + u * b, sum_w + u * w))
                    parts.append(s * b)
                while len(parts) > 1:
                    parts = [p + q for p, q in zip(parts[::2], parts[1::2])]
                if first > 0:
                    parts[0] = parts[0] + y_tiles[tile, at, :]
                y_tiles[tile, at, :] = parts[0]
                return tuple(later)

            held = lax.fori_loop(0, span, step, tuple(starts), unroll=2)
            for n, (unused_b, unused_w, sum_b, sum_w) in zip(chosen, held):
                sum_b = jnp.sum(sum_b, axis=0, keepdims=True)
                sum_w = jnp.sum(sum_w, axis=0, keepdims=True)
                row = slice(n, n + 1)
                grad_ssm_ref[0, row, lanes] = root[row] * sum_b
                grad_ssm_ref[1, row, lanes] = scale[row] * (0.5 * sum_b - rate[row] * sum_w)
        at_lanes = pl.ds(pl.multiple_of(place[0] * width + tile * LANES, LANES), LANES)
        from_steps(rows, y_tiles, tile)
        full[:, at_lanes] += rows[...].astype(bf16).astype(f32)
    count = pieces[0].shape[0]
    for k in range(team):
        at_rows = pl.ds(pl.multiple_of((place[0] ^ k) * count, count), count)
        pieces[k][...] = full[at_rows, :].astype(bf16)


def input_grad_kernel(team, place, x_ref, gain_ref, middle_grad_ref, *refs):
    parts, (out_ref, gain_grad_ref) = refs[:team], refs[team:]
    rows = out_ref.shape[0]
    at_rows = pl.ds(pl.multiple_of(place[0] * rows, rows), rows)
    grad_one = parts[0][...].astype(f32)
    for part in parts[1:]:
        grad_one = grad_one + part[...].astype(f32)
    unit, inverse = normalise(x_ref[at_rows, :].astype(f32))
    gain_grad_ref[...] = jnp.sum(grad_one * unit, axis=0, keepdims=True)
    back = normalise_back(unit, inverse, grad_one * gain_ref[...])
    out_ref[...] = (middle_grad_ref[...] + back).astype(bf16)


def assemble_kernel(halves, low_count, place, own_ref, *refs):
    others, out_ref = refs[:-1], refs[-1]
    count, rows, unused = own_ref.shape
    half = place[4]

    def put(value, sequence, which, member):
        at_rows = pl.ds(pl.multiple_of((which * low_count + member) * rows, rows), rows)
        out_ref[sequence, at_rows, :] = value.astype(out_ref.dtype)

    for sequence in range(count // (halves * low_count)):
        if halves == 1:
            for member in range(low_count):
                put(own_ref[sequence * low_count + member], sequence, 0, member)
        else:
            put(own_ref[sequence * halves + half], sequence, half, 0)
            put(others[0][sequence], sequence, 1 - half, 0)


def assemble_ring_kernel(halves, low_count, count, place, *refs):
    own, others, out_ref = refs[:count], refs[count:-1], refs[-1]
    rows = own[0].shape[0]
    index, half, swapped = place[3], place[4], place[5]

    def put(piece, steps, which):
        source = lax.rem(index + count - steps, count)
        member = lax.rem(source, low_count)
        sequence = source // (halves * low_count)
        at_rows = pl.ds(pl.multiple_of((which * low_count + member) * rows, rows), rows)
        out_ref[sequence, at_rows, :] = piece[...].astype(out_ref.dtype)

    if halves == 1:
        for k in range(count):
            put(own[k], k, 0)
        return
    for j in range(count // 2):
        put(others[j], 2 * j + swapped, 1 - half)
        for odd in range(2):

            @pl.when(swapped == odd)
            def keep():
                put(own[2 * j + odd], 2 * j + odd, half)


def pack_kernel(halves, place, qkv_ref, out_ref, up_ref, down_ref, *refs):
    rows = up_ref.shape[0]
    heads, hidden = out_ref.shape[0] // halves, up_ref.shape[1] // halves
    for which in range(halves):
        side = place[4] if which == 0 else 1 - place[4]
        at_heads = pl.ds(pl.multiple_of(side * heads, LANES), heads)
        at_hidden = pl.ds(pl.multiple_of(side * hidden, LANES), hidden)
        if which == 0:
            head_ref = refs[0]
            wide_ref, deep_ref = refs[1].at[:, :hidden], refs[1].at[:, hidden:]
        else:
            packed = refs[2]
            head_ref = packed.at[:, : 4 * heads]
            wide_ref = packed.at[:, 4 * heads : 4 * heads + hidden]
            deep_ref = packed.at[:, 4 * heads + hidden :]
        for i in range(3):
            head_ref[:, i * heads : (i + 1) * heads] = qkv_ref[i, :, at_heads].astype(bf16)
        head_ref[:, 3 * heads :] = out_ref[at_heads, :].T.astype(bf16)
        wide_ref[...] = up_ref[:, at_hidden].astype(bf16)
        deep_ref[...] = down_ref[at_hidden, :].T.astype(bf16)


def lamb_moments(weight, grad_item, first_old, second_old):
    first_new = beta_first * first_old + (1.0 - beta_first) * grad_item
    second_new = beta_second * second_old + (1.0 - beta_second) * grad_item * grad_item
    direction = (
        first_new
        / (1.0 - beta_first**STEP)
        / (jnp.sqrt(second_new / (1.0 - beta_second**STEP)) + lamb_eps)
        + weight_decay * weight
    )
    return (first_new, second_new, direction)


def place_sums(sums_ref, sums):
    rows = lax.broadcasted_iota(jnp.int32, sums_ref.shape, 0)
    lanes = lax.broadcasted_iota(jnp.int32, sums_ref.shape, 1)
    found = jnp.zeros(sums_ref.shape, f32)
    for index, pair in sums.items():
        for row, value in enumerate(pair):
            found = jnp.where((rows == row) & (lanes == index), value, found)
    sums_ref[...] = found


def moments_kernel(halves, matrices, place, *refs):
    count = 1 + max(item[1] for item in matrices)
    grads, refs = [refs[halves * i : halves * (i + 1)] for i in range(count)], refs[halves * count :]
    arrays = len({(item[1], item[4] is None) for item in matrices})
    ins = [refs[3 * i : 3 * i + 3] for i in range(arrays)]
    outs = [refs[3 * (arrays + i) : 3 * (arrays + i) + 3] for i in range(arrays)]
    sums_ref = refs[6 * arrays]
    keys = []
    sums = {}
    for number, source, column, turned, stacked in matrices:
        key = (source, stacked is None)
        if key not in keys:
            keys.append(key)
        pick = (lambda ref: ref) if stacked is None else (lambda ref, i=stacked: ref.at[i])
        weight, first, second = (pick(ref) for ref in ins[keys.index(key)])
        news = [pick(ref) for ref in outs[keys.index(key)]]
        width = weight.shape[0 if turned else 1] // halves
        rows = weight.shape[1 if turned else 0]
        cols = slice(column * width, (column + 1) * width)
        total_weight = total_update = 0.0
        for which, grad_ref in enumerate(grads[source]):
            side = place[4] if which == 0 else 1 - place[4]
            at = pl.ds(pl.multiple_of(side * width, width), width)
            if which == 0:
                grad = grad_ref[pl.ds(pl.multiple_of(side * rows, rows), rows), cols].astype(f32)
            else:
                grad = grad_ref[:, cols].astype(f32)
            at = (at, slice(None)) if turned else (slice(None), at)
            grad = grad.T if turned else grad
            old = weight[at]
            found = lamb_moments(old, grad, first[at], second[at])
            for ref, value in zip(news, found):
                ref[at] = value
            total_weight = total_weight + jnp.sum(old * old)
            total_update = total_update + jnp.sum(found[2] * found[2])
        sums[number] = (total_weight, total_update)
    place_sums(sums_ref, sums)


def small_moments_kernel(numbers, grads_ref, *refs):
    ins, outs, sums_ref = (refs[:3], refs[3:6]), (refs[6:9], refs[9:12]), refs[12]
    states = (grads_ref.shape[0] - 2) // 2
    sums = {}
    for (weight, first, second), news, start, rows, first_number in (
        (ins[0], outs[0], 2 * states, 1, numbers[0]),
        (ins[1], outs[1], 0, states, numbers[1]),
    ):
        for i in range(2):
            grad = grads_ref[start + i * rows : start + (i + 1) * rows, :]
            at = slice(i * rows, (i + 1) * rows)
            found = lamb_moments(weight[at, :], grad, first[at, :], second[at, :])
            for ref, value in zip(news, found):
                ref[at, :] = value
            sums[first_number + i] = (
                jnp.sum(weight[at, :] * weight[at, :]),
                jnp.sum(found[2] * found[2]),
            )
    place_sums(sums_ref, sums)


def update_kernel(stacks, sums_ref, *refs):
    count = len(stacks)
    weights, directions, news = refs[:count], refs[count : 2 * count], refs[2 * count : 3 * count]
    norms = jnp.sqrt(jnp.sum(sums_ref[...], axis=0))
    refs[3 * count][...] = norms
    ratios = norms[0:1] / norms[1:2]
    lanes = lax.broadcasted_iota(jnp.int32, ratios.shape, 1)
    for numbers, weight, direction, new in zip(stacks, weights, directions, news):
        step = weight.shape[0] // len(numbers)
        for i, number in enumerate(numbers):
            ratio = jnp.sum(jnp.where(lanes == number, ratios, 0.0), axis=1, keepdims=True)
            at = slice(i * step, (i + 1) * step)
            scale = learn_rate * ratio.reshape((1,) * weight.ndim)
            new[at] = weight[at] - scale * direction[at]


def call(
    body, ins, outs, scratch=(), grid=None, in_specs=None, out_specs=None, time=1.0, after=(), token=False
):
    moved = sum(a.size * a.dtype.itemsize for a in list(ins) + list(outs))
    params = pltpu.CompilerParams(vmem_limit_bytes=VMEM_BYTES)
    cost = pl.CostEstimate(flops=int(time * 1.15e9), bytes_accessed=moved, transcendentals=0)
    whole = pl.BlockSpec(memory_space=pltpu.VMEM)
    anywhere = pl.BlockSpec(memory_space=pl.ANY)
    in_specs = list(in_specs or [whole] * len(ins)) + [anywhere] * len(after)
    out_specs = list(out_specs or [whole] * len(outs))
    outs = list(outs)
    first_out = len(ins) + len(after)
    last_out = first_out + len(outs)
    if token:
        outs.append(jax.ShapeDtypeStruct((SUBS, LANES), f32))
        out_specs.append(whole)

    def run(*refs):
        refs = list(refs)
        if token:
            refs[last_out][...] = jnp.zeros((SUBS, LANES), f32)
            del refs[last_out]
        body(*refs[: len(ins)], *refs[first_out:])

    return pl.pallas_call(
        run,
        out_shape=tuple(outs),
        in_specs=in_specs,
        out_specs=tuple(out_specs),
        scratch_shapes=list(scratch),
        compiler_params=params,
        cost_estimate=cost,
        **({} if grid is None else {"grid": grid}),
    )(*ins, *after)


def shaped(shape, kind):
    return jax.ShapeDtypeStruct(tuple(shape), kind)


def on_device(
    tokens,
    cotangent,
    w_qkv,
    w_out,
    w_up,
    w_down,
    norm_gains,
    ssm_param,
    first_qkv,
    second_qkv,
    first_out,
    second_out,
    first_up,
    second_up,
    first_down,
    second_down,
    first_gain,
    second_gain,
    first_ssm,
    second_ssm,
):
    halves = lax.axis_size("sl")
    low_count = lax.axis_size("ml")
    row_parts = lax.axis_size("sh")
    col_parts = lax.axis_size("mb") * lax.axis_size("mq")
    team = halves * low_count
    sl, ml, mb, mq = (lax.axis_index(name) for name in ("sl", "ml", "mb", "mq"))
    rank = sl * low_count + ml
    block_index = lax.axis_index("sh") * halves + mq
    seq_total, length, width = tokens.shape
    assert length == BLK and seq_total == lax.axis_size("mb")
    states = ssm_param.shape[1]
    channels = width // team
    tiles = channels // LANES
    row_count = width // row_parts
    own_rows = length // team
    place = [rank, block_index, lax.axis_index("sh"), lax.axis_index(MODEL), sl, sl ^ mq]
    place.append(lax.axis_index(COLS))
    place = jnp.stack(place).astype(jnp.int32)
    smem = pl.BlockSpec(memory_space=pltpu.SMEM)
    vmem = pl.BlockSpec(memory_space=pltpu.VMEM)

    def permute(value, axes, moves):
        return lax.ppermute(value, axes, moves)

    def swap(value):
        return permute(value, "sl", [(0, 1), (1, 0)])

    def in_order(own, other, axis):
        return jnp.where(
            sl == 0, jnp.concatenate([own, other], axis), jnp.concatenate([other, own], axis)
        )

    def team_send(pieces):
        moved = [pieces[0]]
        for k in range(1, team):
            moved.append(permute(pieces[k], TEAM, [(i, i ^ k) for i in range(team)]))
        return moved

    def pick_block(array):
        own = lax.dynamic_index_in_dim(array, mb, 0, keepdims=False)
        if halves == 1:
            return own, ()
        other = swap(own)
        return jnp.where(sl == mq, own, other), (other,)

    def across(value, bit):
        return permute(value, "sh", [(i, i ^ bit) for i in range(row_parts)])

    def along(value, axes, step):
        count = lax.axis_size(axes)
        return permute(value, axes, [(i, (i + step) % count) for i in range(count)])

    bits = [1 << i for i in range(row_parts.bit_length() - 1)]

    def bit_order(k):
        return bits if k % 2 == 0 else bits[::-1]

    def double_rows(value, order):
        found = {0: value}
        for bit in order:
            for r in list(found):
                found[r | bit] = across(found[r], bit)
        return [found[r] for r in range(row_parts)]

    def add(*items, zero=None):
        total = sum(item.astype(f32) for item in items)
        return (total if zero is None else total + zero[0, 0]).astype(bf16)

    def halve_rows(keep, send, order, zero=None):
        items, first = [keep], None
        for bit in reversed(order):
            arrived = across(send, bit)
            first = arrived if first is None else first
            items.append(arrived)
            count = arrived.shape[0] // 2
            if count > 0:
                send = add(*[item[count:] for item in items], zero=zero)
                items = [item[:count] for item in items]
        return add(*[item[0] for item in items]), first

    def halve_both(stacks, zero=None):
        near, near_first = halve_rows(stacks[0], stacks[1], bits, zero)
        far, far_first = halve_rows(stacks[2], stacks[3], bits[::-1], zero)
        return near, far, (near_first, far_first)

    def ring_gather(shard):
        pieces, held = [], shard
        for k in range(col_parts):
            if k > 0:
                held = along(held, COLS, 1)
            pieces.append(double_rows(held, bits if k % 2 == 0 else bits[::-1]))
        return pieces

    def sum_over_z(near, far):
        pieces = [stack[k] for stack in (near, far) for k in range(col_parts // 2)]
        moved = [along(piece, COLS, -k) for k, piece in enumerate(pieces) if k > 0]
        return add(pieces[0], *moved)

    def everywhere(value, axes):
        count = lax.axis_size(axes)
        copies = jnp.broadcast_to(value[None], (count, *value.shape))
        return lax.all_to_all(copies, axes, 0, 0, tiled=True)

    rows_dev = w_up.shape[0]
    hidden_cols = w_up.shape[1] // halves
    head_cols = 4 * w_out.shape[0] // halves
    packed_cols = head_cols + 2 * hidden_cols
    sides = [shaped((rows_dev, cols), bf16) for cols in (head_cols, 2 * hidden_cols)]
    *shards, packed_done = call(
        functools.partial(pack_kernel, halves),
        (place, w_qkv, w_out, w_up, w_down),
        sides + [shaped((rows_dev, packed_cols), bf16)] * (halves - 1),
        time=2.4,
        in_specs=[smem] + [vmem] * 4,
        token=True,
    )
    if halves == 2:
        other = swap(shards[2])
        cuts = (0, head_cols, packed_cols)
        shards = [
            in_order(own, other[:, first:last], 0)
            for own, first, last in zip(shards, cuts, cuts[1:])
        ]
    head_shard, hidden_shard = shards[:2]
    attn_full = lax.all_gather(head_shard, COLS, axis=0, tiled=False)
    attn_w = [
        *double_rows(attn_full[: col_parts // 2], bits),
        *double_rows(attn_full[col_parts // 2 :], bits[::-1]),
    ]
    hidden_w = ring_gather(hidden_shard)

    small = jnp.concatenate([ssm_param.reshape(2 * states, -1), norm_gains], 0) + packed_done[0, 0]
    small = jnp.transpose(everywhere(small, ALL), (1, 0, 2)).reshape(2 * states + 2, width)
    own_ssm = lax.dynamic_slice_in_dim(
        small[: 2 * states].reshape(2, states, width), rank * channels, channels, 2
    )
    coef, logr = own_ssm[0], own_ssm[1]
    gain_one = small[2 * states : 2 * states + 1]
    gain_two = small[2 * states + 1 : 2 * states + 2]

    x, unused = pick_block(tokens)
    cot, cot_other = pick_block(cotangent)

    anywhere = [pl.BlockSpec(memory_space=pl.ANY)]

    def fixed(*shape):
        return pl.BlockSpec(shape, lambda z: (0,) * len(shape))

    wide = fixed(length, width)
    row = fixed(1, width)

    normed_one, normed_t, u_steps, ends, total = call(
        norm_kernel,
        (place, x, gain_one, logr),
        (
            shaped((length, width), bf16),
            shaped((width, length), bf16),
            shaped((tiles, length, LANES), f32),
            shaped((states, SUBS, channels), f32),
            shaped((states, channels), f32),
        ),
        scratch=[pltpu.VMEM((length, LANES), f32)],
        in_specs=[smem, vmem, vmem, vmem],
        after=(*hidden_w[0][1:-1], hidden_w[1][0], *cot_other),
        time=5,
    )
    totals = everywhere(total, ("sh", "mq"))
    (context_own,) = call(
        context_kernel,
        (place, u_steps, ends, totals, logr, coef),
        (shaped((length, channels), bf16),),
        after=(hidden_w[0][-1], *hidden_w[1][1:-1], *[group[0] for group in hidden_w[2:3]]),
        scratch=[pltpu.VMEM((tiles, length, LANES), f32), pltpu.VMEM((length, LANES), f32)],
        in_specs=[smem] + [vmem] * 5,
        time=7,
    )
    contexts = team_send([context_own] * team)

    stack_shape = (row_parts // 2, col_parts // 2, row_count)
    head_stacks = [shaped((*stack_shape, head_cols), bf16)] * 4
    hidden_stacks = [shaped((*stack_shape, hidden_cols), bf16)] * 8
    sizes = (team, col_parts, row_parts)
    head_buffer = pltpu.VMEM((4, row_parts, row_count, col_parts * HD), bf16)
    head_sems = pltpu.SemaphoreType.DMA((col_parts, row_parts, 4))
    kept_shape = shaped((4, length, col_parts * HD), bf16)
    context_t, cot_t, attn_part, kept, probs, probs_t = call(
        functools.partial(attend_kernel, *sizes),
        (place, normed_one, cot, *contexts, *attn_w),
        (
            shaped((width, length), bf16),
            shaped((width, length), bf16),
            shaped((length, width), bf16),
            kept_shape,
            *[shaped((col_parts, length, length), bf16)] * 2,
        ),
        scratch=[pltpu.VMEM((length, width), bf16), head_buffer, head_sems],
        time=13,
        in_specs=[smem] + [vmem] * (2 + team) + anywhere * (2 * row_parts),
        after=(hidden_w[1][-1], *[group[0] for group in hidden_w[3:4]]),
    )
    attn_parts = team_send([attn_part] * team)

    middle, normed_two, normed_two_t = call(
        functools.partial(middle_kernel, team),
        (x, gain_two, *attn_parts),
        (shaped((length, width), f32), shaped((length, width), bf16), shaped((width, length), bf16)),
        time=4,
    )
    weight_buffer = pltpu.VMEM((row_parts, row_count, col_parts * hidden_cols), bf16)
    grad_buffer = pltpu.VMEM((col_parts, row_parts, row_count, hidden_cols), bf16)
    out_part, two_part, *hidden_grads = call(
        functools.partial(feed_kernel, col_parts, row_parts),
        (place, normed_two, normed_two_t, cot, cot_t, *[p for group in hidden_w for p in group]),
        (shaped((length, width), bf16), shaped((length, width), bf16), *hidden_stacks),
        scratch=[
            *[weight_buffer] * 2,
            *[grad_buffer] * 2,
            *[pltpu.VMEM((length, col_parts * hidden_cols), bf16)] * 2,
            pltpu.SemaphoreType.DMA((4, col_parts, row_parts)),
        ],
        time=18,
        grid=(col_parts,),
        in_specs=[smem, wide, fixed(width, length), wide, fixed(width, length)]
        + anywhere * (col_parts * row_parts),
        out_specs=[wide, wide] + anywhere * 8,
    )
    two_parts = team_send([two_part] * team)

    def rows_of(array, member):
        return lax.dynamic_slice_in_dim(array, member * own_rows, own_rows, 0)

    def share_rows(own_piece, kind):
        pieces = lax.all_gather(own_piece, MODEL, axis=0, tiled=False)
        others = []
        if halves == 2:
            pairs = pieces.reshape(seq_total, halves, own_rows, width)
            others = [swap(lax.dynamic_index_in_dim(pairs, 1 - sl, 1, keepdims=False))]
        (blocks,) = call(
            functools.partial(assemble_kernel, halves, low_count),
            (place, pieces, *others),
            (shaped((seq_total, length, width), kind),),
            time=3.5,
            in_specs=[smem, vmem] + [vmem] * len(others),
        )
        return blocks

    def share_ring(own_piece, kind):
        count = lax.axis_size(MODEL)
        pieces = [own_piece] + [along(own_piece, MODEL, k) for k in range(1, count)]
        others = []
        if halves == 2:
            for even, odd in zip(pieces[::2], pieces[1::2]):
                others.append(swap(jnp.where(sl == mq, odd, even)))
        (blocks,) = call(
            functools.partial(assemble_ring_kernel, halves, low_count, count),
            (place, *pieces, *others),
            (shaped((seq_total, length, width), kind),),
            time=3.5,
            in_specs=[smem] + [vmem] * (len(pieces) + len(others)),
        )
        return blocks

    out_pieces = team_send([rows_of(out_part, rank ^ k) for k in range(team)])
    result = rows_of(middle, rank) + sum(item.astype(f32) for item in out_pieces)
    result = result.astype(bf16)
    layer_out = share_rows(result, bf16)

    def both_halves(own):
        if halves == 1:
            return [own]
        return [own, swap(lax.dynamic_slice_in_dim(own, (1 - sl) * rows_dev, rows_dev, 0))]

    middle_grad, gain_two_grad, one_part, *rest = call(
        functools.partial(attend_back_kernel, *sizes),
        (place, middle, gain_two, cot, *two_parts, normed_t, context_t, kept, probs, probs_t, *attn_w),
        (
            shaped((own_rows, width), f32),
            shaped((1, width), f32),
            shaped((length, width), bf16),
            *[shaped((length, channels), bf16)] * team,
            *head_stacks,
        ),
        scratch=[
            head_buffer,
            head_buffer,
            pltpu.VMEM((length, width), bf16),
            *[pltpu.VMEM((length, col_parts * HD), bf16)] * 4,
            *[pltpu.VMEM((width, length), bf16)] * 2,
            pltpu.VMEM(kept_shape.shape, bf16),
            *[pltpu.VMEM((col_parts, length, length), bf16)] * 2,
            head_sems,
            head_sems,
            pltpu.SemaphoreType.DMA((5,)),
        ],
        in_specs=[smem] + [vmem] * (3 + team) + anywhere * (5 + 2 * row_parts),
        out_specs=[vmem] * (3 + team) + anywhere * 4,
        time=1,
        after=(result,),
    )
    context_grads = team_send(rest[:team])
    g_steps, adjoint_ends, adjoint_total, adjoint_done = call(
        functools.partial(adjoint_kernel, team),
        (logr, *context_grads),
        (
            shaped((tiles, length, LANES), f32),
            shaped((2, states, SUBS, channels), f32),
            shaped((2, states, channels), f32),
        ),
        scratch=[pltpu.VMEM((length, LANES), f32)],
        time=1,
        token=True,
    )
    down_near, down_far, down_first = halve_both(hidden_grads[4:], adjoint_done)
    grad_down = lax.psum_scatter(
        jnp.concatenate([down_near, down_far], 0), COLS, scatter_dimension=0, tiled=False
    )
    adjoint_totals = everywhere(adjoint_total, ("sh", "mq"))
    *one_pieces, grad_ssm, context_done = call(
        functools.partial(context_back_kernel, team),
        (place, g_steps, u_steps, adjoint_ends, adjoint_totals, logr, coef, one_part),
        (
            *[shaped((own_rows, width), bf16)] * team,
            shaped((2, states, channels), f32),
        ),
        scratch=[
            pltpu.VMEM((tiles, length, LANES), f32),
            pltpu.VMEM((length, width), f32),
            pltpu.VMEM((length, LANES), f32),
        ],
        in_specs=[smem] + [vmem] * 7,
        time=10,
        after=(down_near, down_far),
        token=True,
    )
    one_pieces = team_send(one_pieces)
    up_near, up_far, up_first = halve_both(hidden_grads[:4], context_done)
    grad_up = sum_over_z(up_near, up_far)
    grad_rows, gain_one_grad, rows_done = call(
        functools.partial(input_grad_kernel, team),
        (place, x, gain_one, middle_grad, *one_pieces),
        (shaped((own_rows, width), bf16), shaped((1, width), f32)),
        in_specs=[smem] + [vmem] * (3 + team),
        time=4,
        after=up_first,
        token=True,
    )
    input_grad = share_ring(grad_rows, f32)
    near, far, unused = halve_both(rest[team:], rows_done)
    grad_heads = sum_over_z(near, far)

    placed_ssm = lax.dynamic_update_slice_in_dim(
        jnp.zeros((2 * states, width), f32),
        grad_ssm.reshape(2 * states, channels),
        rank * channels,
        1,
    )
    small_grads = jnp.concatenate([placed_ssm, gain_one_grad, gain_two_grad], 0)
    small_grads = small_grads.reshape(2 * states + 2, lax.axis_size(ALL), -1)
    small_grads = lax.all_to_all(jnp.transpose(small_grads, (1, 0, 2)), ALL, 0, 0, tiled=True)
    small_grads = jnp.sum(small_grads, axis=0)

    def moments(matrices, grads, arrays):
        changed = [shaped(old.shape, f32) for group in arrays for old in group]
        grad_parts = [part for grad in grads for part in both_halves(grad)]
        ins = [item for group in arrays for item in group]
        *found, sums = call(
            functools.partial(moments_kernel, halves, matrices),
            (place, *grad_parts, *ins),
            (*changed, shaped((2, LANES), f32)),
            in_specs=[smem] + [vmem] * (len(grad_parts) + len(ins)),
            time=4,
        )
        return [found[3 * i : 3 * i + 3] for i in range(len(arrays))], sums

    hidden_new, hidden_sums = moments(
        ((4, 0, 0, False, None), (5, 1, 0, True, None)),
        (grad_up, grad_down),
        ((w_up, first_up, second_up), (w_down, first_down, second_down)),
    )
    heads_new, head_sums = moments(
        tuple((i, 0, i, False, i) for i in range(3)) + ((3, 0, 3, True, None),),
        (grad_heads,),
        ((w_qkv, first_qkv, second_qkv), (w_out, first_out, second_out)),
    )
    own_channels = norm_gains.shape[1]
    ssm_items = [item.reshape(2 * states, own_channels) for item in (ssm_param, first_ssm, second_ssm)]
    small_items = [norm_gains, first_gain, second_gain, *ssm_items]
    *small_new, small_sums = call(
        functools.partial(small_moments_kernel, (6, 8)),
        (small_grads.reshape(2 * states + 2, own_channels), *small_items),
        (*[shaped(item.shape, f32) for item in small_items], shaped((2, LANES), f32)),
    )
    all_sums = everywhere(hidden_sums + head_sums + small_sums, ALL)
    masters = (w_qkv, w_out, w_up, w_down, norm_gains, ssm_items[0])
    news = (*heads_new, *hidden_new, small_new[:3], small_new[3:])
    *weights, norms = call(
        functools.partial(update_kernel, ((0, 1, 2), (3,), (4,), (5,), (6, 7), (8, 9))),
        (all_sums, *masters, *[group[2] for group in news]),
        (*[shaped(item.shape, f32) for item in masters], shaped((2, LANES), f32)),
        time=3.2,
    )
    outputs = [layer_out, input_grad]
    for index, (weight, (first_new, second_new, unused)) in enumerate(zip(weights, news)):
        if index == 4:
            outputs += [weight, first_new, second_new[0], second_new[1]]
        else:
            kept_shape = ssm_param.shape if index == 5 else weight.shape
            outputs += [item.reshape(kept_shape) for item in (weight, first_new, second_new)]
    outputs.append(norms[:, :10])
    return tuple(outputs)


def solution(mesh):
    seq_count, model_count = mesh.shape["seq"], mesh.shape["mp"]
    halves = 2 if HEADS // model_count >= 2 else 1
    sizes = (seq_count // halves, halves, SEQS, halves, model_count // (SEQS * halves))
    fine = Mesh(mesh.devices.reshape(sizes), ALL)
    seq, model = ("sh", "sl"), ("mb", "mq", "ml")
    rows_cols, cols_rows = P(seq, model), P(model, seq)
    token = P(None, seq, None)
    stack = P(None, seq, model)
    gains = P(None, ALL)
    ssm = P(None, None, ALL)
    return jax.shard_map(
        on_device,
        mesh=fine,
        in_specs=(token, token, stack, cols_rows, rows_cols, cols_rows, gains, ssm)
        + (stack,) * 2
        + (cols_rows,) * 2
        + (rows_cols,) * 2
        + (cols_rows,) * 2
        + (gains,) * 2
        + (ssm,) * 2,
        out_specs=(token, token)
        + (stack,) * 3
        + (cols_rows,) * 3
        + (rows_cols,) * 3
        + (cols_rows,) * 3
        + (gains, gains, P(ALL), P(ALL))
        + (ssm,) * 3
        + (P(),),
        check_vma=False,
    )
```

```python
import functools
import math

import jax
import jax.numpy as jnp
from jax import lax
from jax.experimental import pallas as pl
from jax.experimental.pallas import tpu as pltpu
from jax.sharding import Mesh
from jax.sharding import PartitionSpec as P

HD = 128
HEADS = 8
BLK = 512
STEP = 10
SEQS = 2
LANES = 128
SUBS = 8
GROUP = 8

norm_eps = 1e-05
beta_first = 0.9
beta_second = 0.999
lamb_eps = 1e-06
weight_decay = 0.01
learn_rate = 0.5
score_scale = HD ** (-0.5)

f32 = jnp.float32
bf16 = jnp.bfloat16
VMEM_BYTES = 56 * 1024 * 1024

ALL = ("sh", "sl", "mb", "mq", "ml")
MODEL = ("mb", "mq", "ml")
COLS = ("mb", "mq")
TEAM = ("sl", "ml")


def dot(left, right):
    return lax.dot_general(left, right, (((1,), (0,)), ((), ())), preferred_element_type=f32)


def dot_t(left, right):
    return lax.dot_general(left, right, (((1,), (1,)), ((), ())), preferred_element_type=f32)


def normalise(values):
    centred = values - jnp.mean(values, axis=-1, keepdims=True)
    inverse = lax.rsqrt(jnp.mean(centred * centred, axis=-1, keepdims=True) + norm_eps)
    return centred * inverse, inverse


def normalise_back(unit, inverse, grad_unit):
    mean_one = jnp.mean(grad_unit, axis=-1, keepdims=True)
    mean_two = jnp.mean(grad_unit * unit, axis=-1, keepdims=True)
    return inverse * (grad_unit - mean_one - unit * mean_two)


def sub_index():
    return lax.broadcasted_iota(jnp.int32, (SUBS, LANES), 0)


def spread(row):
    return jnp.broadcast_to(row, (SUBS, LANES))


def lane_tile(index):
    return slice(index * LANES, (index + 1) * LANES)


def no_state(tiles):
    rows = tiles[0, :SUBS, :]
    return rows - rows


def in_steps(steps, tile, rows):
    span = rows.shape[0] // SUBS

    def move(i, unused):
        steps[tile, pl.ds(pl.multiple_of(i * SUBS, SUBS), SUBS), :] = rows[
            pl.ds(i, SUBS, stride=span), :
        ]
        return unused

    lax.fori_loop(0, span, move, 0, unroll=8)


def from_steps(rows, steps, tile):
    span = rows.shape[0] // SUBS

    def move(i, unused):
        rows[pl.ds(i, SUBS, stride=span), :] = steps[
            tile, pl.ds(pl.multiple_of(i * SUBS, SUBS), SUBS), :
        ]
        return unused

    lax.fori_loop(0, span, move, 0, unroll=8)


def step_rows(i):
    return pl.ds(pl.multiple_of(i * SUBS, SUBS), SUBS)


def norm_kernel(
    place, x_ref, gain_ref, logr_ref, normed_ref, turned_ref, u_tiles, ends_ref, total_ref, rows
):
    unit, unused = normalise(x_ref[...].astype(f32))
    normed_ref[...] = (unit * gain_ref[...]).astype(bf16)
    turned_ref[...] = normed_ref[...].T
    tiles, length, unused = u_tiles.shape
    states = logr_ref.shape[0]
    span = length // SUBS
    for tile in range(tiles):
        start = place[0] * (tiles * LANES) + tile * LANES
        rows[...] = normed_ref[:, pl.ds(pl.multiple_of(start, LANES), LANES)].astype(f32)
        in_steps(u_tiles, tile, rows)
    left = ((SUBS - 1 - sub_index()) * span).astype(f32)
    for tile in range(tiles):
        rate = jnp.exp(logr_ref[:, lane_tile(tile)])
        decay = jnp.exp(-rate)
        decays = [spread(decay[n : n + 1]) for n in range(states)]

        def step(i, held):
            u = u_tiles[tile, step_rows(i), :]
            return tuple(d * h + u for d, h in zip(decays, held))

        zero = no_state(u_tiles)
        held = lax.fori_loop(0, span, step, (zero,) * states, unroll=4)
        for n in range(states):
            ends_ref[n, :, lane_tile(tile)] = held[n]
            total_ref[n : n + 1, lane_tile(tile)] = jnp.sum(
                held[n] * jnp.exp(-left * rate[n : n + 1]), axis=0, keepdims=True
            )


def context_kernel(
    place, u_tiles, ends_ref, all_ref, logr_ref, coef_ref, context_ref, y_tiles, rows
):
    tiles, length, unused = u_tiles.shape
    states = logr_ref.shape[0]
    span = length // SUBS
    index = sub_index()
    before = (index * span).astype(f32)
    for tile in range(tiles):
        rate = jnp.exp(logr_ref[:, lane_tile(tile)])
        decay = jnp.exp(-rate)
        scale = coef_ref[:, lane_tile(tile)] * jnp.sqrt(2.0 * rate)
        incoming = jnp.zeros((states, LANES), f32)
        for j in range(all_ref.shape[0]):
            gap = place[1] - 1 - j
            distance = (jnp.maximum(gap, 0) * length).astype(f32)
            term = jnp.exp(-distance * rate) * all_ref[j, :, lane_tile(tile)].astype(f32)
            incoming = incoming + jnp.where(gap >= 0, term, 0.0)
        for first in range(0, states, GROUP):
            chosen = range(first, first + GROUP)
            starts = []
            for n in chosen:
                row = rate[n : n + 1]
                run = ends_ref[n, :, lane_tile(tile)]
                for d in (1, 2, 4):
                    moved = jnp.exp(-(d * span) * row) * pltpu.roll(run, d, 0)
                    run = run + jnp.where(index >= d, moved, 0.0)
                run = jnp.where(index >= 1, pltpu.roll(run, 1, 0), 0.0)
                starts.append(run + jnp.exp(-before * row) * incoming[n : n + 1])
            decays = [spread(decay[n : n + 1]) for n in chosen]
            scales = [spread(scale[n : n + 1]) for n in chosen]

            def step(i, held):
                at = step_rows(i)
                u = u_tiles[tile, at, :]
                held = tuple(d * h + u for d, h in zip(decays, held))
                parts = [s * h for s, h in zip(scales, held)]
                if first > 0:
                    parts[0] = parts[0] + y_tiles[tile, at, :]
                while len(parts) > 1:
                    parts = [a + b for a, b in zip(parts[::2], parts[1::2])]
                y_tiles[tile, at, :] = parts[0]
                return held

            lax.fori_loop(0, span, step, tuple(starts), unroll=4)
        from_steps(rows, y_tiles, tile)
        context_ref[:, lane_tile(tile)] = rows[...].astype(bf16)


def whole_rows(block):
    return block.reshape(block.shape[0] * block.shape[1], block.shape[2])


def head(index):
    return slice(index * HD, (index + 1) * HD)


def weight_copies(near, far, buffer, place, sems, act):
    count = sems.shape[0]
    half = count // 2
    for k in range(count):
        owner = lax.rem(place[6] + count - k, count)
        for stacks, low in ((near, 0), (far, half)):

            @pl.when((owner >= low) & (owner < low + half))
            def move():
                for r, stack in enumerate(stacks):
                    inner = buffer.at[k, place[2] ^ r]
                    act(pltpu.make_async_copy(stack.at[owner - low], inner, sems.at[k, r]))


def of_heads(buffer, i):
    return jnp.concatenate([whole_rows(buffer[k, :, :, head(i)]) for k in range(buffer.shape[0])], axis=1)


def gradient_slot(row_parts, order, r):
    position = 0
    for bit in reversed(order):
        position = 2 * position + (1 if r & bit else 0)
    return position // (row_parts // 2), position % (row_parts // 2)


def round_orders(row_parts):
    bits = [1 << i for i in range(row_parts.bit_length() - 1)]
    return bits, bits[::-1]


def gradient_pieces(stacks, row_parts, far, slot):
    found = []
    for r in range(row_parts):
        sent, at = gradient_slot(row_parts, round_orders(row_parts)[far], r)
        found.append(stacks[2 * far + sent].at[at, slot])
    return found


def project_kernel(team, col_parts, row_parts, place, normed_ref, cot_ref, *refs):
    contexts, refs = refs[:team], refs[team:]
    near, far, refs = refs[:row_parts], refs[row_parts : 2 * row_parts], refs[2 * row_parts :]
    context_t_ref, cot_t_ref, kept_ref = refs[:3]
    context_ref, weights, sems = refs[3:]
    weight_copies(near, far, weights, place, sems, lambda copy: copy.start())
    width = contexts[0].shape[1]
    for k in range(team):
        lanes = pl.ds(pl.multiple_of((place[0] ^ k) * width, LANES), width)
        context_ref[:, lanes] = contexts[k][...]
    context_t_ref[...] = context_ref[...].T
    cot_t_ref[...] = cot_ref[...].T
    weight_copies(near, far, weights, place, sems, lambda copy: copy.wait())
    kept_ref[0] = dot(normed_ref[...], of_heads(weights, 0)).astype(bf16)
    kept_ref[1] = dot(context_ref[...], of_heads(weights, 1)).astype(bf16)
    kept_ref[2] = dot(context_ref[...], of_heads(weights, 2)).astype(bf16)


def attend_kernel(team, col_parts, row_parts, place, kept_ref, *refs):
    near, far, refs = refs[:row_parts], refs[row_parts : 2 * row_parts], refs[2 * row_parts :]
    part_ref, attended_ref, probs_ref, probs_t_ref, weights, sems = refs
    weight_copies(near, far, weights, place, sems, lambda copy: copy.start())
    length = kept_ref.shape[1]
    rows = lax.broadcasted_iota(jnp.int32, (length, length), 0)
    cols = lax.broadcasted_iota(jnp.int32, (length, length), 1)
    for h in range(col_parts):
        scores = dot_t(kept_ref[0, :, head(h)], kept_ref[1, :, head(h)]) * score_scale
        scores = jnp.where(rows >= cols, scores, -1e30)
        shifted = jnp.exp(scores - jnp.max(scores, axis=-1, keepdims=True))
        inverse = 1.0 / jnp.sum(shifted, axis=-1, keepdims=True)
        probs = (shifted * inverse).astype(bf16)
        probs_ref[h] = probs
        probs_t_ref[h] = probs.T
        attended_ref[:, head(h)] = dot(probs, kept_ref[2, :, head(h)]).astype(bf16)
    weight_copies(near, far, weights, place, sems, lambda copy: copy.wait())
    part_ref[...] = dot_t(attended_ref[...], of_heads(weights, 3)).astype(bf16)


def gelu_parts(hidden, grad_act):
    density = jnp.exp(-0.5 * hidden * hidden)
    t = 1.0 / (1.0 + (0.3275911 * math.sqrt(0.5)) * jnp.abs(hidden))
    series = 0.5 * 1.061405429
    for factor in (-1.453152027, 1.421413741, -0.284496736, 0.254829592):
        series = series * t + 0.5 * factor
    tail = series * t * density
    cdf = jnp.where(hidden >= 0.0, 1.0 - tail, tail)
    slope = cdf + hidden * density * (1.0 / math.sqrt(2.0 * math.pi))
    return (hidden * cdf).astype(bf16), (grad_act * slope).astype(bf16)


def middle_kernel(team, x_ref, gain_ref, *refs):
    parts, (middle_ref, normed_ref, normed_t_ref) = refs[:team], refs[team:]
    attn = parts[0][...].astype(f32)
    for part in parts[1:]:
        attn = attn + part[...].astype(f32)
    middle = x_ref[...].astype(f32) + attn
    middle_ref[...] = middle
    unit, unused = normalise(middle)
    normed_ref[...] = (unit * gain_ref[...]).astype(bf16)
    normed_t_ref[...] = normed_ref[...].T


def feed_kernel(col_parts, row_parts, place, normed_ref, normed_t_ref, cot_ref, cot_t_ref, *refs):
    count = col_parts * row_parts
    pieces, refs = refs[:count], refs[count:]
    out_ref, two_ref = refs[:2]
    stacks, refs = (refs[2:6], refs[6:10]), refs[10:]
    up_all, down_all, grad_up, grad_down, activated_all, grad_all, sems = refs
    z = pl.program_id(0)
    half = col_parts // 2
    hidden_cols = grad_up.shape[3]

    def copies(k):
        found = []
        for r in range(row_parts):
            piece = pieces[k * row_parts + r]
            for which, buffer in enumerate((up_all, down_all)):
                outside = piece.at[:, pl.ds(which * hidden_cols, hidden_cols)]
                inside = buffer.at[place[2] ^ r, :, pl.ds(k * hidden_cols, hidden_cols)]
                found.append(pltpu.make_async_copy(outside, inside, sems.at[which, k, r]))
        return found

    def leaving(which, k, far, slot, act):
        buffer = (grad_up, grad_down)[which]
        for r, piece in enumerate(gradient_pieces(stacks[which], row_parts, far, slot)):
            act(pltpu.make_async_copy(buffer.at[k, place[2] ^ r], piece, sems.at[2 + which, k, r]))

    def each_leaving(k, act):
        owner = lax.rem(place[6] + col_parts - k, col_parts)
        for far in range(2):

            @pl.when(owner // half == far)
            def leaves():
                for which in range(2):
                    leaving(which, k, far, lax.rem(owner, half), act)

    @pl.when(z == 0)
    def start():
        for k in range(col_parts):
            for copy in copies(k):
                copy.start()

    for k in range(col_parts):

        @pl.when(z == k)
        def arrive():
            for copy in copies(k):
                copy.wait()

    at = pl.ds(pl.multiple_of(z * hidden_cols, hidden_cols), hidden_cols)
    hidden = dot(normed_ref[...], whole_rows(up_all[:, :, at]))
    grad_act = dot(cot_ref[...], whole_rows(down_all[:, :, at]))
    activated, grad_pre = gelu_parts(hidden, grad_act)
    activated_all[:, at] = activated
    grad_all[:, at] = grad_pre
    shape = grad_up.shape[1:]
    grad_up[z] = dot(normed_t_ref[...], grad_pre).astype(bf16).reshape(shape)
    grad_down[z] = dot(cot_t_ref[...], activated).astype(bf16).reshape(shape)

    for k in range(col_parts):

        @pl.when(z == k)
        def leave():
            each_leaving(k, lambda copy: copy.start())

    @pl.when(z == col_parts - 1)
    def finish():
        two_ref[...] = dot_t(grad_all[...], whole_rows(up_all[...])).astype(bf16)
        out_ref[...] = dot_t(activated_all[...], whole_rows(down_all[...])).astype(bf16)
        for k in range(col_parts):
            each_leaving(k, lambda copy: copy.wait())


def attend_back_kernel(team, col_parts, row_parts, place, middle_ref, gain_ref, cot_ref, *refs):
    parts, refs = refs[:team], refs[team:]
    late, refs = refs[:6], refs[6:]
    near, far, refs = refs[:row_parts], refs[row_parts : 2 * row_parts], refs[2 * row_parts :]
    middle_grad_ref, gain_grad_ref, one_ref = refs[:3]
    refs = refs[3:]
    context_grads, refs = refs[:team], refs[team:]
    stacks, refs = refs[:4], refs[4:]
    weights, grads, low, grad_out, grad_q, grad_k, grad_v = refs[:7]
    held, (sems, out_sems, late_sems) = refs[7:13], refs[13:]
    normed_t_ref, context_t_ref, kept_ref, attended_ref, probs_ref, probs_t_ref = held
    half = col_parts // 2
    weight_copies(near, far, weights, place, sems, lambda copy: copy.start())
    late_copies = [
        pltpu.make_async_copy(outside, inside, late_sems.at[i])
        for i, (outside, inside) in enumerate(zip(late, held))
    ]
    for copy in late_copies:
        copy.start()
    own_rows = middle_ref.shape[0] // team
    grad_two = parts[0][...].astype(f32)
    for part in parts[1:]:
        grad_two = grad_two + part[...].astype(f32)
    unit, inverse = normalise(middle_ref[...])
    grad_gain = grad_two * unit
    rows = lax.broadcasted_iota(jnp.int32, grad_gain.shape, 0)
    first = place[0] * own_rows
    mine = (rows >= first) & (rows < first + own_rows)
    gain_grad_ref[...] = jnp.sum(jnp.where(mine, grad_gain, 0.0), axis=0, keepdims=True)
    grad = cot_ref[...].astype(f32) + normalise_back(unit, inverse, grad_two * gain_ref[...])
    low[...] = grad.astype(bf16)
    for k in range(team):

        @pl.when(place[0] == k)
        def own():
            middle_grad_ref[...] = grad[k * own_rows : (k + 1) * own_rows, :]

    weight_copies(near, far, weights, place, sems, lambda copy: copy.wait())
    for copy in late_copies:
        copy.wait()
    grad_out[...] = dot(low[...], of_heads(weights, 3)).astype(bf16)
    for h in range(col_parts):
        q, k, v = (kept_ref[i, :, head(h)] for i in range(3))
        grad_heads = grad_out[:, head(h)]
        grad_v[:, head(h)] = dot(probs_t_ref[h], grad_heads).astype(bf16)
        probs = probs_ref[h].astype(f32)
        grad_probs = dot_t(grad_heads, v)
        inner = jnp.sum(grad_probs * probs, axis=-1, keepdims=True)
        grad_scores = (probs * (grad_probs - inner)).astype(bf16)
        grad_q[:, head(h)] = (dot(grad_scores, k) * score_scale).astype(bf16)
        turned = dot_t(v, grad_heads) - inner.T
        turned = (probs_t_ref[h].astype(f32) * turned).astype(bf16)
        grad_k[:, head(h)] = (dot(turned, q) * score_scale).astype(bf16)
    shape = (*grads.shape[1:3], HD)

    def put(i, grad):
        for h in range(col_parts):
            grads[h, :, :, head(i)] = grad[:, head(h)].astype(bf16).reshape(shape)

    put(3, dot(low[...].T, attended_ref[...]))
    put(0, dot(normed_t_ref[...], grad_q[...]))
    put(1, dot(context_t_ref[...], grad_k[...]))
    put(2, dot(context_t_ref[...], grad_v[...]))
    copies = []
    for k in range(col_parts):
        for r, piece in enumerate(gradient_pieces(stacks, row_parts, k // half, k % half)):
            copies.append(pltpu.make_async_copy(grads.at[k, place[2] ^ r], piece, out_sems.at[k, r]))
    for copy in copies:
        copy.start()
    total = dot_t(grad_k[...], of_heads(weights, 1)) + dot_t(grad_v[...], of_heads(weights, 2))
    middle_total = total.astype(bf16)
    low[...] = middle_total
    width = context_grads[0].shape[1]
    for k in range(team):
        lanes = pl.ds(pl.multiple_of((place[0] ^ k) * width, LANES), width)
        context_grads[k][...] = low[:, lanes]
    one_ref[...] = dot_t(grad_q[...], of_heads(weights, 0)).astype(bf16)
    for copy in copies:
        copy.wait()


def adjoint_kernel(team, logr_ref, *refs):
    parts = refs[:team]
    g_tiles, ends_ref, total_ref, rows = refs[team:]
    grad = parts[0][...].astype(f32)
    for part in parts[1:]:
        grad = grad + part[...].astype(f32)
    grad = grad.astype(bf16).astype(f32)
    tiles, length, unused = g_tiles.shape
    states = logr_ref.shape[0]
    span = length // SUBS
    for tile in range(tiles):
        rows[...] = grad[:, lane_tile(tile)]
        in_steps(g_tiles, tile, rows)
    before = (sub_index() * span).astype(f32)
    for tile in range(tiles):
        rate = jnp.exp(logr_ref[:, lane_tile(tile)])
        decay = jnp.exp(-rate)
        for first in range(0, states, GROUP):
            chosen = range(first, first + GROUP)
            decays = [spread(decay[n : n + 1]) for n in chosen]

            def step(i, held):
                g = g_tiles[tile, step_rows(span - 1 - i), :]
                later = []
                for d, (b, w) in zip(decays, held):
                    shrunk = d * b
                    later.append((g + shrunk, d * w + shrunk))
                return tuple(later)

            zero = no_state(g_tiles)
            held = lax.fori_loop(0, span, step, ((zero, zero),) * GROUP, unroll=4)
            for n, (b, w) in zip(chosen, held):
                ends_ref[0, n, :, lane_tile(tile)] = b
                ends_ref[1, n, :, lane_tile(tile)] = w
                shrink = jnp.exp(-before * rate[n : n + 1])
                total_ref[0, n : n + 1, lane_tile(tile)] = jnp.sum(
                    shrink * b, axis=0, keepdims=True
                )
                total_ref[1, n : n + 1, lane_tile(tile)] = jnp.sum(
                    shrink * (w + before * b), axis=0, keepdims=True
                )


def context_back_kernel(
    team, place, g_tiles, u_tiles, ends_ref, all_ref, logr_ref, coef_ref, one_ref, *refs
):
    pieces = refs[:team]
    grad_ssm_ref, y_tiles, full, rows = refs[team:]
    tiles, length, unused = u_tiles.shape
    states = logr_ref.shape[0]
    span = length // SUBS
    width = tiles * LANES
    index = sub_index()
    after = ((SUBS - 1 - index) * span).astype(f32)
    full[...] = one_ref[...].astype(f32)
    group = GROUP
    for tile in range(tiles):
        lanes = lane_tile(tile)
        rate = jnp.exp(logr_ref[:, lanes])
        decay = jnp.exp(-rate)
        root = jnp.sqrt(2.0 * rate)
        scale = coef_ref[:, lanes] * root
        in_b = jnp.zeros((states, LANES), f32)
        in_w = jnp.zeros((states, LANES), f32)
        for j in range(all_ref.shape[0]):
            gap = j - place[1] - 1
            distance = (jnp.maximum(gap, 0) * length).astype(f32)
            shrink = jnp.exp(-distance * rate)
            b, w = all_ref[j, 0, :, lanes].astype(f32), all_ref[j, 1, :, lanes].astype(f32)
            in_b = in_b + jnp.where(gap >= 0, shrink * b, 0.0)
            in_w = in_w + jnp.where(gap >= 0, shrink * (w + distance * b), 0.0)
        for first in range(0, states, group):
            chosen = range(first, first + group)
            starts = []
            for n in chosen:
                row = rate[n : n + 1]
                b, w = ends_ref[0, n, :, lanes], ends_ref[1, n, :, lanes]
                for d in (1, 2, 4):
                    shrink = jnp.exp(-(d * span) * row)
                    next_b = pltpu.roll(b, SUBS - d, 0)
                    next_w = pltpu.roll(w, SUBS - d, 0)
                    inside = index < SUBS - d
                    b, w = (
                        b + jnp.where(inside, shrink * next_b, 0.0),
                        w + jnp.where(inside, shrink * (next_w + (d * span) * next_b), 0.0),
                    )
                inside = index < SUBS - 1
                b = jnp.where(inside, pltpu.roll(b, SUBS - 1, 0), 0.0)
                w = jnp.where(inside, pltpu.roll(w, SUBS - 1, 0), 0.0)
                shrink = jnp.exp(-after * row)
                b_row, w_row = in_b[n : n + 1], in_w[n : n + 1]
                b = b + shrink * b_row
                w = w + shrink * (w_row + after * b_row)
                zero = no_state(u_tiles)
                starts.append((b, w, zero, zero))
            decays = [spread(decay[n : n + 1]) for n in chosen]
            scales = [spread(scale[n : n + 1]) for n in chosen]

            def step(i, held):
                at = step_rows(span - 1 - i)
                g = g_tiles[tile, at, :]
                u = u_tiles[tile, at, :]
                later, parts = [], []
                for d, s, (b, w, sum_b, sum_w) in zip(decays, scales, held):
                    shrunk = d * b
                    w = d * w + shrunk
                    b = g + shrunk
                    later.append((b, w, sum_b + u * b, sum_w + u * w))
                    parts.append(s * b)
                while len(parts) > 1:
                    parts = [p + q for p, q in zip(parts[::2], parts[1::2])]
                if first > 0:
                    parts[0] = parts[0] + y_tiles[tile, at, :]
                y_tiles[tile, at, :] = parts[0]
                return tuple(later)

            held = lax.fori_loop(0, span, step, tuple(starts), unroll=2)
            for n, (unused_b, unused_w, sum_b, sum_w) in zip(chosen, held):
                sum_b = jnp.sum(sum_b, axis=0, keepdims=True)
                sum_w = jnp.sum(sum_w, axis=0, keepdims=True)
                row = slice(n, n + 1)
                grad_ssm_ref[0, row, lanes] = root[row] * sum_b
                grad_ssm_ref[1, row, lanes] = scale[row] * (0.5 * sum_b - rate[row] * sum_w)
        at_lanes = pl.ds(pl.multiple_of(place[0] * width + tile * LANES, LANES), LANES)
        from_steps(rows, y_tiles, tile)
        full[:, at_lanes] += rows[...].astype(bf16).astype(f32)
    count = pieces[0].shape[0]
    for k in range(team):
        at_rows = pl.ds(pl.multiple_of((place[0] ^ k) * count, count), count)
        pieces[k][...] = full[at_rows, :].astype(bf16)


def input_grad_kernel(team, place, x_ref, gain_ref, middle_grad_ref, *refs):
    parts, (out_ref, gain_grad_ref) = refs[:team], refs[team:]
    rows = out_ref.shape[0]
    at_rows = pl.ds(pl.multiple_of(place[0] * rows, rows), rows)
    grad_one = parts[0][...].astype(f32)
    for part in parts[1:]:
        grad_one = grad_one + part[...].astype(f32)
    unit, inverse = normalise(x_ref[at_rows, :].astype(f32))
    gain_grad_ref[...] = jnp.sum(grad_one * unit, axis=0, keepdims=True)
    back = normalise_back(unit, inverse, grad_one * gain_ref[...])
    out_ref[...] = (middle_grad_ref[...] + back).astype(bf16)


def assemble_kernel(halves, low_count, place, own_ref, *refs):
    others, out_ref = refs[:-1], refs[-1]
    count, rows, unused = own_ref.shape
    half = place[4]

    def put(value, sequence, which, member):
        at_rows = pl.ds(pl.multiple_of((which * low_count + member) * rows, rows), rows)
        out_ref[sequence, at_rows, :] = value.astype(out_ref.dtype)

    for sequence in range(count // (halves * low_count)):
        if halves == 1:
            for member in range(low_count):
                put(own_ref[sequence * low_count + member], sequence, 0, member)
        else:
            put(own_ref[sequence * halves + half], sequence, half, 0)
            put(others[0][sequence], sequence, 1 - half, 0)


def assemble_ring_kernel(halves, low_count, count, place, *refs):
    own, others, out_ref = refs[:count], refs[count:-1], refs[-1]
    rows = own[0].shape[0]
    index, half, swapped = place[3], place[4], place[5]

    def put(piece, steps, which):
        source = lax.rem(index + count - steps, count)
        member = lax.rem(source, low_count)
        sequence = source // (halves * low_count)
        at_rows = pl.ds(pl.multiple_of((which * low_count + member) * rows, rows), rows)
        out_ref[sequence, at_rows, :] = piece[...].astype(out_ref.dtype)

    if halves == 1:
        for k in range(count):
            put(own[k], k, 0)
        return
    for j in range(count // 2):
        put(others[j], 2 * j + swapped, 1 - half)
        for odd in range(2):

            @pl.when(swapped == odd)
            def keep():
                put(own[2 * j + odd], 2 * j + odd, half)


def pack_kernel(halves, place, qkv_ref, out_ref, up_ref, down_ref, *refs):
    rows = up_ref.shape[0]
    heads, hidden = out_ref.shape[0] // halves, up_ref.shape[1] // halves
    for which in range(halves):
        side = place[4] if which == 0 else 1 - place[4]
        at_heads = pl.ds(pl.multiple_of(side * heads, LANES), heads)
        at_hidden = pl.ds(pl.multiple_of(side * hidden, LANES), hidden)
        if which == 0:
            head_ref = refs[0]
            wide_ref, deep_ref = refs[1].at[:, :hidden], refs[1].at[:, hidden:]
        else:
            packed = refs[2]
            head_ref = packed.at[:, : 4 * heads]
            wide_ref = packed.at[:, 4 * heads : 4 * heads + hidden]
            deep_ref = packed.at[:, 4 * heads + hidden :]
        for i in range(3):
            head_ref[:, i * heads : (i + 1) * heads] = qkv_ref[i, :, at_heads].astype(bf16)
        head_ref[:, 3 * heads :] = out_ref[at_heads, :].T.astype(bf16)
        wide_ref[...] = up_ref[:, at_hidden].astype(bf16)
        deep_ref[...] = down_ref[at_hidden, :].T.astype(bf16)


def small_kernel(ssm_ref, gains_ref, out_ref):
    count = ssm_ref.shape[0]
    out_ref[:count, :] = ssm_ref[...]
    out_ref[count:, :] = gains_ref[...]


def lamb_moments(weight, grad_item, first_old, second_old):
    first_new = beta_first * first_old + (1.0 - beta_first) * grad_item
    second_new = beta_second * second_old + (1.0 - beta_second) * grad_item * grad_item
    direction = (
        first_new
        / (1.0 - beta_first**STEP)
        / (jnp.sqrt(second_new / (1.0 - beta_second**STEP)) + lamb_eps)
        + weight_decay * weight
    )
    return (first_new, second_new, direction)


def place_sums(sums_ref, sums):
    rows = lax.broadcasted_iota(jnp.int32, sums_ref.shape, 0)
    lanes = lax.broadcasted_iota(jnp.int32, sums_ref.shape, 1)
    found = jnp.zeros(sums_ref.shape, f32)
    for index, pair in sums.items():
        for row, value in enumerate(pair):
            found = jnp.where((rows == row) & (lanes == index), value, found)
    sums_ref[...] = found


def moments_kernel(halves, matrices, place, *refs):
    count = 1 + max(item[1] for item in matrices)
    grads, refs = [refs[halves * i : halves * (i + 1)] for i in range(count)], refs[halves * count :]
    arrays = len({(item[1], item[4] is None) for item in matrices})
    ins = [refs[3 * i : 3 * i + 3] for i in range(arrays)]
    outs = [refs[3 * (arrays + i) : 3 * (arrays + i) + 3] for i in range(arrays)]
    sums_ref = refs[6 * arrays]
    keys = []
    sums = {}
    for number, source, column, turned, stacked in matrices:
        key = (source, stacked is None)
        if key not in keys:
            keys.append(key)
        pick = (lambda ref: ref) if stacked is None else (lambda ref, i=stacked: ref.at[i])
        weight, first, second = (pick(ref) for ref in ins[keys.index(key)])
        news = [pick(ref) for ref in outs[keys.index(key)]]
        width = weight.shape[0 if turned else 1] // halves
        rows = weight.shape[1 if turned else 0]
        cols = slice(column * width, (column + 1) * width)
        total_weight = total_update = 0.0
        for which, grad_ref in enumerate(grads[source]):
            side = place[4] if which == 0 else 1 - place[4]
            at = pl.ds(pl.multiple_of(side * width, width), width)
            if which == 0:
                grad = grad_ref[pl.ds(pl.multiple_of(side * rows, rows), rows), cols].astype(f32)
            else:
                grad = grad_ref[:, cols].astype(f32)
            at = (at, slice(None)) if turned else (slice(None), at)
            grad = grad.T if turned else grad
            old = weight[at]
            found = lamb_moments(old, grad, first[at], second[at])
            for ref, value in zip(news, found):
                ref[at] = value
            total_weight = total_weight + jnp.sum(old * old)
            total_update = total_update + jnp.sum(found[2] * found[2])
        sums[number] = (total_weight, total_update)
    place_sums(sums_ref, sums)


def small_moments_kernel(numbers, grads_ref, *refs):
    ins, outs, sums_ref = (refs[:3], refs[3:6]), (refs[6:9], refs[9:12]), refs[12]
    states = (grads_ref.shape[0] - 2) // 2
    sums = {}
    for (weight, first, second), news, start, rows, first_number in (
        (ins[0], outs[0], 2 * states, 1, numbers[0]),
        (ins[1], outs[1], 0, states, numbers[1]),
    ):
        for i in range(2):
            grad = grads_ref[start + i * rows : start + (i + 1) * rows, :]
            at = slice(i * rows, (i + 1) * rows)
            found = lamb_moments(weight[at, :], grad, first[at, :], second[at, :])
            for ref, value in zip(news, found):
                ref[at, :] = value
            sums[first_number + i] = (
                jnp.sum(weight[at, :] * weight[at, :]),
                jnp.sum(found[2] * found[2]),
            )
    place_sums(sums_ref, sums)


def update_kernel(stacks, sums_ref, *refs):
    count = len(stacks)
    weights, directions, news = refs[:count], refs[count : 2 * count], refs[2 * count : 3 * count]
    norms = jnp.sqrt(jnp.sum(sums_ref[...], axis=0))
    refs[3 * count][...] = norms
    ratios = norms[0:1] / norms[1:2]
    lanes = lax.broadcasted_iota(jnp.int32, ratios.shape, 1)
    for numbers, weight, direction, new in zip(stacks, weights, directions, news):
        step = weight.shape[0] // len(numbers)
        for i, number in enumerate(numbers):
            ratio = jnp.sum(jnp.where(lanes == number, ratios, 0.0), axis=1, keepdims=True)
            at = slice(i * step, (i + 1) * step)
            scale = learn_rate * ratio.reshape((1,) * weight.ndim)
            new[at] = weight[at] - scale * direction[at]


def call(
    body, ins, outs, scratch=(), grid=None, in_specs=None, out_specs=None, time=1.0, after=(), token=False
):
    moved = sum(a.size * a.dtype.itemsize for a in list(ins) + list(outs))
    params = pltpu.CompilerParams(vmem_limit_bytes=VMEM_BYTES)
    cost = pl.CostEstimate(flops=int(time * 1.15e9), bytes_accessed=moved, transcendentals=0)
    whole = pl.BlockSpec(memory_space=pltpu.VMEM)
    anywhere = pl.BlockSpec(memory_space=pl.ANY)
    in_specs = list(in_specs or [whole] * len(ins)) + [anywhere] * len(after)
    out_specs = list(out_specs or [whole] * len(outs))
    outs = list(outs)
    first_out = len(ins) + len(after)
    last_out = first_out + len(outs)
    if token:
        outs.append(jax.ShapeDtypeStruct((SUBS, LANES), f32))
        out_specs.append(whole)

    def run(*refs):
        refs = list(refs)
        if token:
            refs[last_out][...] = jnp.zeros((SUBS, LANES), f32)
            del refs[last_out]
        body(*refs[: len(ins)], *refs[first_out:])

    return pl.pallas_call(
        run,
        out_shape=tuple(outs),
        in_specs=in_specs,
        out_specs=tuple(out_specs),
        scratch_shapes=list(scratch),
        compiler_params=params,
        cost_estimate=cost,
        **({} if grid is None else {"grid": grid}),
    )(*ins, *after)


def shaped(shape, kind):
    return jax.ShapeDtypeStruct(tuple(shape), kind)


def on_device(
    tokens,
    cotangent,
    w_qkv,
    w_out,
    w_up,
    w_down,
    norm_gains,
    ssm_param,
    first_qkv,
    second_qkv,
    first_out,
    second_out,
    first_up,
    second_up,
    first_down,
    second_down,
    first_gain,
    second_gain,
    first_ssm,
    second_ssm,
):
    halves = lax.axis_size("sl")
    low_count = lax.axis_size("ml")
    row_parts = lax.axis_size("sh")
    col_parts = lax.axis_size("mb") * lax.axis_size("mq")
    team = halves * low_count
    sl, ml, mb, mq = (lax.axis_index(name) for name in ("sl", "ml", "mb", "mq"))
    rank = sl * low_count + ml
    block_index = lax.axis_index("sh") * halves + mq
    seq_total, length, width = tokens.shape
    assert length == BLK and seq_total == lax.axis_size("mb")
    states = ssm_param.shape[1]
    channels = width // team
    tiles = channels // LANES
    row_count = width // row_parts
    own_rows = length // team
    place = [rank, block_index, lax.axis_index("sh"), lax.axis_index(MODEL), sl, sl ^ mq]
    place.append(lax.axis_index(COLS))
    place = jnp.stack(place).astype(jnp.int32)
    smem = pl.BlockSpec(memory_space=pltpu.SMEM)
    vmem = pl.BlockSpec(memory_space=pltpu.VMEM)

    def permute(value, axes, moves):
        return lax.ppermute(value, axes, moves)

    def swap(value):
        return permute(value, "sl", [(0, 1), (1, 0)])

    def in_order(own, other, axis):
        return jnp.where(
            sl == 0, jnp.concatenate([own, other], axis), jnp.concatenate([other, own], axis)
        )

    def team_send(pieces):
        moved = [pieces[0]]
        for k in range(1, team):
            moved.append(permute(pieces[k], TEAM, [(i, i ^ k) for i in range(team)]))
        return moved

    def pick_block(array):
        own = lax.dynamic_index_in_dim(array, mb, 0, keepdims=False)
        if halves == 1:
            return own, ()
        other = swap(own)
        return jnp.where(sl == mq, own, other), (other,)

    def across(value, bit):
        return permute(value, "sh", [(i, i ^ bit) for i in range(row_parts)])

    def along(value, axes, step):
        count = lax.axis_size(axes)
        return permute(value, axes, [(i, (i + step) % count) for i in range(count)])

    bits = [1 << i for i in range(row_parts.bit_length() - 1)]

    def bit_order(k):
        return bits if k % 2 == 0 else bits[::-1]

    def double_rows(value, order):
        found = {0: value}
        for bit in order:
            for r in list(found):
                found[r | bit] = across(found[r], bit)
        return [found[r] for r in range(row_parts)]

    def add(*items, zero=None):
        total = sum(item.astype(f32) for item in items)
        return (total if zero is None else total + zero[0, 0]).astype(bf16)

    def first_messages(stacks):
        return across(stacks[1], bits[-1]), across(stacks[3], bits[0])

    def halve_rows(keep, arrived, order, zero=None):
        items = [keep, arrived]
        for bit in order[-2::-1]:
            count = arrived.shape[0] // 2
            arrived = across(add(*[item[count:] for item in items], zero=zero), bit)
            items = [item[:count] for item in items] + [arrived]
        return add(*[item[0] for item in items])

    def halve_both(stacks, first, zero=None):
        near = halve_rows(stacks[0], first[0], bits, zero)
        return near, halve_rows(stacks[2], first[1], bits[::-1], zero)

    def ring_gather(shard):
        pieces, held = [], shard
        for k in range(col_parts):
            if k > 0:
                held = along(held, COLS, 1)
            pieces.append(double_rows(held, bits if k % 2 == 0 else bits[::-1]))
        return pieces

    def scatter_over_z(near, far):
        stack = jnp.concatenate([near, far], 0)
        return lax.psum_scatter(stack, COLS, scatter_dimension=0, tiled=False)

    def sum_over_z(near, far):
        pieces = [stack[k] for stack in (near, far) for k in range(col_parts // 2)]
        moved = [along(piece, COLS, -k) for k, piece in enumerate(pieces) if k > 0]
        return add(pieces[0], *moved)

    def everywhere(value, axes):
        count = lax.axis_size(axes)
        copies = jnp.broadcast_to(value[None], (count, *value.shape))
        return lax.all_to_all(copies, axes, 0, 0, tiled=True)

    rows_dev = w_up.shape[0]
    hidden_cols = w_up.shape[1] // halves
    head_cols = 4 * w_out.shape[0] // halves
    packed_cols = head_cols + 2 * hidden_cols
    sides = [shaped((rows_dev, cols), bf16) for cols in (head_cols, 2 * hidden_cols)]
    shards = call(
        functools.partial(pack_kernel, halves),
        (place, w_qkv, w_out, w_up, w_down),
        sides + [shaped((rows_dev, packed_cols), bf16)] * (halves - 1),
        time=2.4,
        in_specs=[smem] + [vmem] * 4,
    )
    if halves == 2:
        other = swap(shards[2])
        cuts = (0, head_cols, packed_cols)
        shards = [
            in_order(own, other[:, first:last], 0)
            for own, first, last in zip(shards, cuts, cuts[1:])
        ]
    head_shard, hidden_shard = shards[:2]
    attn_full = lax.all_gather(head_shard, COLS, axis=0, tiled=False)
    attn_w = [
        *double_rows(attn_full[: col_parts // 2], bits),
        *double_rows(attn_full[col_parts // 2 :], bits[::-1]),
    ]
    hidden_w = ring_gather(hidden_shard)

    small, = call(
        small_kernel,
        (ssm_param.reshape(2 * states, -1), norm_gains),
        (shaped((2 * states + 2, norm_gains.shape[1]), f32),),
        after=(hidden_w[1][0],),
    )
    small = jnp.transpose(everywhere(small, ALL), (1, 0, 2)).reshape(2 * states + 2, width)
    own_ssm = lax.dynamic_slice_in_dim(
        small[: 2 * states].reshape(2, states, width), rank * channels, channels, 2
    )
    coef, logr = own_ssm[0], own_ssm[1]
    gain_one = small[2 * states : 2 * states + 1]
    gain_two = small[2 * states + 1 : 2 * states + 2]

    x, unused = pick_block(tokens)
    cot, cot_other = pick_block(cotangent)

    anywhere = [pl.BlockSpec(memory_space=pl.ANY)]

    def fixed(*shape):
        return pl.BlockSpec(shape, lambda z: (0,) * len(shape))

    wide = fixed(length, width)
    row = fixed(1, width)

    normed_one, normed_t, u_steps, ends, total = call(
        norm_kernel,
        (place, x, gain_one, logr),
        (
            shaped((length, width), bf16),
            shaped((width, length), bf16),
            shaped((tiles, length, LANES), f32),
            shaped((states, SUBS, channels), f32),
            shaped((states, channels), f32),
        ),
        scratch=[pltpu.VMEM((length, LANES), f32)],
        in_specs=[smem, vmem, vmem, vmem],
        after=(*hidden_w[0][1:-1], hidden_w[1][0], *cot_other),
        time=5,
    )
    totals = everywhere(total.astype(bf16), ("sh", "mq"))
    (context_own,) = call(
        context_kernel,
        (place, u_steps, ends, totals, logr, coef),
        (shaped((length, channels), bf16),),
        after=(hidden_w[0][-1], *hidden_w[1][1:-1], *[group[0] for group in hidden_w[2:3]]),
        scratch=[pltpu.VMEM((tiles, length, LANES), f32), pltpu.VMEM((length, LANES), f32)],
        in_specs=[smem] + [vmem] * 5,
        time=7,
    )
    contexts = team_send([context_own] * team)

    stack_shape = (row_parts // 2, col_parts // 2, row_count)
    head_stacks = [shaped((*stack_shape, head_cols), bf16)] * 4
    hidden_stacks = [shaped((*stack_shape, hidden_cols), bf16)] * 8
    sizes = (team, col_parts, row_parts)
    head_buffer = pltpu.VMEM((col_parts, row_parts, row_count, 4 * HD), bf16)
    head_sems = pltpu.SemaphoreType.DMA((col_parts, row_parts))
    kept_shape = shaped((3, length, col_parts * HD), bf16)
    flat_shape = shaped((length, col_parts * HD), bf16)
    context_t, cot_t, kept = call(
        functools.partial(project_kernel, *sizes),
        (place, normed_one, cot, *contexts, *attn_w),
        (shaped((width, length), bf16), shaped((width, length), bf16), kept_shape),
        scratch=[pltpu.VMEM((length, width), bf16), head_buffer, head_sems],
        time=1,
        in_specs=[smem] + [vmem] * (2 + team) + anywhere * (2 * row_parts),
        after=(hidden_w[1][-1], *[piece for group in hidden_w[2:3] for piece in group[1:-1]]),
    )
    attn_part, attended, probs, probs_t = call(
        functools.partial(attend_kernel, *sizes),
        (place, kept, *attn_w),
        (
            shaped((length, width), bf16),
            flat_shape,
            *[shaped((col_parts, length, length), bf16)] * 2,
        ),
        scratch=[head_buffer, head_sems],
        time=1,
        in_specs=[smem, vmem] + anywhere * (2 * row_parts),
        after=[piece for group in hidden_w[3:] for piece in group[1:-1]],
    )
    attn_parts = team_send([attn_part] * team)

    middle, normed_two, normed_two_t = call(
        functools.partial(middle_kernel, team),
        (x, gain_two, *attn_parts),
        (shaped((length, width), f32), shaped((length, width), bf16), shaped((width, length), bf16)),
        time=1,
    )
    weight_buffer = pltpu.VMEM((row_parts, row_count, col_parts * hidden_cols), bf16)
    grad_buffer = pltpu.VMEM((col_parts, row_parts, row_count, hidden_cols), bf16)
    out_part, two_part, *hidden_grads = call(
        functools.partial(feed_kernel, col_parts, row_parts),
        (place, normed_two, normed_two_t, cot, cot_t, *[p for group in hidden_w for p in group]),
        (shaped((length, width), bf16), shaped((length, width), bf16), *hidden_stacks),
        scratch=[
            *[weight_buffer] * 2,
            *[grad_buffer] * 2,
            *[pltpu.VMEM((length, col_parts * hidden_cols), bf16)] * 2,
            pltpu.SemaphoreType.DMA((4, col_parts, row_parts)),
        ],
        time=18,
        grid=(col_parts,),
        in_specs=[smem, wide, fixed(width, length), wide, fixed(width, length)]
        + anywhere * (col_parts * row_parts),
        out_specs=[wide, wide] + anywhere * 8,
    )
    two_parts = team_send([two_part] * team)

    def rows_of(array, member):
        return lax.dynamic_slice_in_dim(array, member * own_rows, own_rows, 0)

    def share_rows(own_piece, kind):
        pieces = lax.all_gather(own_piece, MODEL, axis=0, tiled=False)
        others = []
        if halves == 2:
            pairs = pieces.reshape(seq_total, halves, own_rows, width)
            others = [swap(lax.dynamic_index_in_dim(pairs, 1 - sl, 1, keepdims=False))]
        (blocks,) = call(
            functools.partial(assemble_kernel, halves, low_count),
            (place, pieces, *others),
            (shaped((seq_total, length, width), kind),),
            time=3.5,
            in_specs=[smem, vmem] + [vmem] * len(others),
        )
        return blocks

    def share_ring(own_piece, kind):
        count = lax.axis_size(MODEL)
        pieces = [own_piece] + [along(own_piece, MODEL, k) for k in range(1, count)]
        others = []
        if halves == 2:
            for even, odd in zip(pieces[::2], pieces[1::2]):
                others.append(swap(jnp.where(sl == mq, odd, even)))
        (blocks,) = call(
            functools.partial(assemble_ring_kernel, halves, low_count, count),
            (place, *pieces, *others),
            (shaped((seq_total, length, width), kind),),
            time=3.5,
            in_specs=[smem] + [vmem] * (len(pieces) + len(others)),
        )
        return blocks

    out_pieces = team_send([rows_of(out_part, rank ^ k) for k in range(team)])
    result = rows_of(middle, rank) + sum(item.astype(f32) for item in out_pieces)
    result = result.astype(bf16)
    layer_out = share_rows(result, bf16)

    def both_halves(own):
        if halves == 1:
            return [own]
        return [own, swap(lax.dynamic_slice_in_dim(own, (1 - sl) * rows_dev, rows_dev, 0))]

    middle_grad, gain_two_grad, one_part, *rest = call(
        functools.partial(attend_back_kernel, *sizes),
        (place, middle, gain_two, cot, *two_parts, normed_t, context_t, kept, attended, probs, probs_t, *attn_w),
        (
            shaped((own_rows, width), f32),
            shaped((1, width), f32),
            shaped((length, width), bf16),
            *[shaped((length, channels), bf16)] * team,
            *head_stacks,
        ),
        scratch=[
            head_buffer,
            head_buffer,
            pltpu.VMEM((length, width), bf16),
            *[pltpu.VMEM((length, col_parts * HD), bf16)] * 4,
            *[pltpu.VMEM((width, length), bf16)] * 2,
            pltpu.VMEM(kept_shape.shape, bf16),
            pltpu.VMEM(flat_shape.shape, bf16),
            *[pltpu.VMEM((col_parts, length, length), bf16)] * 2,
            head_sems,
            head_sems,
            pltpu.SemaphoreType.DMA((6,)),
        ],
        in_specs=[smem] + [vmem] * (3 + team) + anywhere * (6 + 2 * row_parts),
        out_specs=[vmem] * (3 + team) + anywhere * 4,
        time=1,
        after=(result,),
    )
    context_grads = team_send(rest[:team])
    down_first = first_messages(hidden_grads[4:])
    up_first = first_messages(hidden_grads[:4])
    g_steps, adjoint_ends, adjoint_total, adjoint_done = call(
        functools.partial(adjoint_kernel, team),
        (logr, *context_grads),
        (
            shaped((tiles, length, LANES), f32),
            shaped((2, states, SUBS, channels), f32),
            shaped((2, states, channels), f32),
        ),
        scratch=[pltpu.VMEM((length, LANES), f32)],
        time=1,
        after=down_first,
        token=True,
    )
    down_near, down_far = halve_both(hidden_grads[4:], down_first, adjoint_done)
    grad_down = scatter_over_z(down_near, down_far)
    up_near, up_far = halve_both(hidden_grads[:4], up_first, adjoint_done)
    grad_up = scatter_over_z(up_near, up_far)
    adjoint_totals = everywhere(adjoint_total.astype(bf16), ("sh", "mq"))
    *one_pieces, grad_ssm = call(
        functools.partial(context_back_kernel, team),
        (place, g_steps, u_steps, adjoint_ends, adjoint_totals, logr, coef, one_part),
        (
            *[shaped((own_rows, width), bf16)] * team,
            shaped((2, states, channels), f32),
        ),
        scratch=[
            pltpu.VMEM((tiles, length, LANES), f32),
            pltpu.VMEM((length, width), f32),
            pltpu.VMEM((length, LANES), f32),
        ],
        in_specs=[smem] + [vmem] * 7,
        time=10,
        after=(down_near, down_far, *up_first),
    )
    one_pieces = team_send(one_pieces)
    grad_rows, gain_one_grad, rows_done = call(
        functools.partial(input_grad_kernel, team),
        (place, x, gain_one, middle_grad, *one_pieces),
        (shaped((own_rows, width), bf16), shaped((1, width), f32)),
        in_specs=[smem] + [vmem] * (3 + team),
        time=4,
        after=(up_near, up_far),
        token=True,
    )
    input_grad = share_ring(grad_rows, f32)
    near, far = halve_both(rest[team:], first_messages(rest[team:]), rows_done)
    grad_heads = sum_over_z(near, far)

    placed_ssm = lax.dynamic_update_slice_in_dim(
        jnp.zeros((2 * states, width), f32),
        grad_ssm.reshape(2 * states, channels),
        rank * channels,
        1,
    )
    small_grads = jnp.concatenate([placed_ssm, gain_one_grad, gain_two_grad], 0)
    small_grads = small_grads.reshape(2 * states + 2, lax.axis_size(ALL), -1)
    small_grads = lax.all_to_all(jnp.transpose(small_grads, (1, 0, 2)), ALL, 0, 0, tiled=True)
    small_grads = jnp.sum(small_grads, axis=0)

    def moments(matrices, grads, arrays):
        changed = [shaped(old.shape, f32) for group in arrays for old in group]
        grad_parts = [part for grad in grads for part in both_halves(grad)]
        ins = [item for group in arrays for item in group]
        *found, sums = call(
            functools.partial(moments_kernel, halves, matrices),
            (place, *grad_parts, *ins),
            (*changed, shaped((2, LANES), f32)),
            in_specs=[smem] + [vmem] * (len(grad_parts) + len(ins)),
            time=4,
        )
        return [found[3 * i : 3 * i + 3] for i in range(len(arrays))], sums

    hidden_new, hidden_sums = moments(
        ((4, 0, 0, False, None), (5, 1, 0, True, None)),
        (grad_up, grad_down),
        ((w_up, first_up, second_up), (w_down, first_down, second_down)),
    )
    heads_new, head_sums = moments(
        tuple((i, 0, i, False, i) for i in range(3)) + ((3, 0, 3, True, None),),
        (grad_heads,),
        ((w_qkv, first_qkv, second_qkv), (w_out, first_out, second_out)),
    )
    own_channels = norm_gains.shape[1]
    ssm_items = [item.reshape(2 * states, own_channels) for item in (ssm_param, first_ssm, second_ssm)]
    small_items = [norm_gains, first_gain, second_gain, *ssm_items]
    *small_new, small_sums = call(
        functools.partial(small_moments_kernel, (6, 8)),
        (small_grads.reshape(2 * states + 2, own_channels), *small_items),
        (*[shaped(item.shape, f32) for item in small_items], shaped((2, LANES), f32)),
    )
    all_sums = everywhere(hidden_sums + head_sums + small_sums, ALL)
    masters = (w_qkv, w_out, w_up, w_down, norm_gains, ssm_items[0])
    news = (*heads_new, *hidden_new, small_new[:3], small_new[3:])
    *weights, norms = call(
        functools.partial(update_kernel, ((0, 1, 2), (3,), (4,), (5,), (6, 7), (8, 9))),
        (all_sums, *masters, *[group[2] for group in news]),
        (*[shaped(item.shape, f32) for item in masters], shaped((2, LANES), f32)),
        time=3.2,
    )
    outputs = [layer_out, input_grad]
    for index, (weight, (first_new, second_new, unused)) in enumerate(zip(weights, news)):
        if index == 4:
            outputs += [weight, first_new, second_new[0], second_new[1]]
        else:
            kept_shape = ssm_param.shape if index == 5 else weight.shape
            outputs += [item.reshape(kept_shape) for item in (weight, first_new, second_new)]
    outputs.append(norms[:, :10])
    return tuple(outputs)


def solution(mesh):
    seq_count, model_count = mesh.shape["seq"], mesh.shape["mp"]
    halves = 2 if HEADS // model_count >= 2 else 1
    sizes = (seq_count // halves, halves, SEQS, halves, model_count // (SEQS * halves))
    fine = Mesh(mesh.devices.reshape(sizes), ALL)
    seq, model = ("sh", "sl"), ("mb", "mq", "ml")
    rows_cols, cols_rows = P(seq, model), P(model, seq)
    token = P(None, seq, None)
    stack = P(None, seq, model)
    gains = P(None, ALL)
    ssm = P(None, None, ALL)
    return jax.shard_map(
        on_device,
        mesh=fine,
        in_specs=(token, token, stack, cols_rows, rows_cols, cols_rows, gains, ssm)
        + (stack,) * 2
        + (cols_rows,) * 2
        + (rows_cols,) * 2
        + (cols_rows,) * 2
        + (gains,) * 2
        + (ssm,) * 2,
        out_specs=(token, token)
        + (stack,) * 3
        + (cols_rows,) * 3
        + (rows_cols,) * 3
        + (cols_rows,) * 3
        + (gains, gains, P(ALL), P(ALL))
        + (ssm,) * 3
        + (P(),),
        check_vma=False,
    )
```

```python
import functools
import math

import jax
import jax.numpy as jnp
from jax import lax
from jax.experimental import pallas as pl
from jax.experimental.pallas import tpu as pltpu
from jax.sharding import Mesh
from jax.sharding import PartitionSpec as P

HD = 128
HEADS = 8
BLK = 512
STEP = 10
SEQS = 2
LANES = 128
SUBS = 8
GROUP = 8

norm_eps = 1e-05
beta_first = 0.9
beta_second = 0.999
lamb_eps = 1e-06
weight_decay = 0.01
learn_rate = 0.5
score_scale = HD ** (-0.5)

f32 = jnp.float32
bf16 = jnp.bfloat16
VMEM_BYTES = 56 * 1024 * 1024

ALL = ("sh", "sl", "mb", "mq", "ml")
MODEL = ("mb", "mq", "ml")
COLS = ("mb", "mq")
TEAM = ("sl", "ml")


def dot(left, right):
    return lax.dot_general(left, right, (((1,), (0,)), ((), ())), preferred_element_type=f32)


def dot_t(left, right):
    return lax.dot_general(left, right, (((1,), (1,)), ((), ())), preferred_element_type=f32)


def normalise(values):
    centred = values - jnp.mean(values, axis=-1, keepdims=True)
    inverse = lax.rsqrt(jnp.mean(centred * centred, axis=-1, keepdims=True) + norm_eps)
    return centred * inverse, inverse


def normalise_back(unit, inverse, grad_unit):
    mean_one = jnp.mean(grad_unit, axis=-1, keepdims=True)
    mean_two = jnp.mean(grad_unit * unit, axis=-1, keepdims=True)
    return inverse * (grad_unit - mean_one - unit * mean_two)


def sub_index():
    return lax.broadcasted_iota(jnp.int32, (SUBS, LANES), 0)


def spread(row):
    return jnp.broadcast_to(row, (SUBS, LANES))


def lane_tile(index):
    return slice(index * LANES, (index + 1) * LANES)


def no_state(tiles):
    rows = tiles[0, :SUBS, :]
    return rows - rows


def in_steps(steps, tile, rows):
    span = rows.shape[0] // SUBS

    def move(i, unused):
        steps[tile, pl.ds(pl.multiple_of(i * SUBS, SUBS), SUBS), :] = rows[
            pl.ds(i, SUBS, stride=span), :
        ]
        return unused

    lax.fori_loop(0, span, move, 0, unroll=8)


def from_steps(rows, steps, tile):
    span = rows.shape[0] // SUBS

    def move(i, unused):
        rows[pl.ds(i, SUBS, stride=span), :] = steps[
            tile, pl.ds(pl.multiple_of(i * SUBS, SUBS), SUBS), :
        ]
        return unused

    lax.fori_loop(0, span, move, 0, unroll=8)


def step_rows(i):
    return pl.ds(pl.multiple_of(i * SUBS, SUBS), SUBS)


def norm_kernel(
    place, x_ref, gain_ref, logr_ref, normed_ref, turned_ref, u_tiles, ends_ref, total_ref, rows
):
    unit, unused = normalise(x_ref[...].astype(f32))
    normed_ref[...] = (unit * gain_ref[...]).astype(bf16)
    turned_ref[...] = normed_ref[...].T
    tiles, length, unused = u_tiles.shape
    states = logr_ref.shape[0]
    span = length // SUBS
    for tile in range(tiles):
        start = place[0] * (tiles * LANES) + tile * LANES
        rows[...] = normed_ref[:, pl.ds(pl.multiple_of(start, LANES), LANES)].astype(f32)
        in_steps(u_tiles, tile, rows)
    left = ((SUBS - 1 - sub_index()) * span).astype(f32)
    for tile in range(tiles):
        rate = jnp.exp(logr_ref[:, lane_tile(tile)])
        decay = jnp.exp(-rate)
        decays = [spread(decay[n : n + 1]) for n in range(states)]

        def step(i, held):
            u = u_tiles[tile, step_rows(i), :]
            return tuple(d * h + u for d, h in zip(decays, held))

        zero = no_state(u_tiles)
        held = lax.fori_loop(0, span, step, (zero,) * states, unroll=4)
        for n in range(states):
            ends_ref[n, :, lane_tile(tile)] = held[n]
            total_ref[n : n + 1, lane_tile(tile)] = jnp.sum(
                held[n] * jnp.exp(-left * rate[n : n + 1]), axis=0, keepdims=True
            )


def context_kernel(
    place, u_tiles, ends_ref, all_ref, logr_ref, coef_ref, context_ref, y_tiles, rows
):
    tiles, length, unused = u_tiles.shape
    states = logr_ref.shape[0]
    span = length // SUBS
    index = sub_index()
    before = (index * span).astype(f32)
    for tile in range(tiles):
        rate = jnp.exp(logr_ref[:, lane_tile(tile)])
        decay = jnp.exp(-rate)
        scale = coef_ref[:, lane_tile(tile)] * jnp.sqrt(2.0 * rate)
        incoming = jnp.zeros((states, LANES), f32)
        for j in range(all_ref.shape[0]):
            gap = place[1] - 1 - j
            distance = (jnp.maximum(gap, 0) * length).astype(f32)
            term = jnp.exp(-distance * rate) * all_ref[j, :, lane_tile(tile)].astype(f32)
            incoming = incoming + jnp.where(gap >= 0, term, 0.0)
        for first in range(0, states, GROUP):
            chosen = range(first, first + GROUP)
            starts = []
            for n in chosen:
                row = rate[n : n + 1]
                run = ends_ref[n, :, lane_tile(tile)]
                for d in (1, 2, 4):
                    moved = jnp.exp(-(d * span) * row) * pltpu.roll(run, d, 0)
                    run = run + jnp.where(index >= d, moved, 0.0)
                run = jnp.where(index >= 1, pltpu.roll(run, 1, 0), 0.0)
                starts.append(run + jnp.exp(-before * row) * incoming[n : n + 1])
            decays = [spread(decay[n : n + 1]) for n in chosen]
            scales = [spread(scale[n : n + 1]) for n in chosen]

            def step(i, held):
                at = step_rows(i)
                u = u_tiles[tile, at, :]
                held = tuple(d * h + u for d, h in zip(decays, held))
                parts = [s * h for s, h in zip(scales, held)]
                if first > 0:
                    parts[0] = parts[0] + y_tiles[tile, at, :]
                while len(parts) > 1:
                    parts = [a + b for a, b in zip(parts[::2], parts[1::2])]
                y_tiles[tile, at, :] = parts[0]
                return held

            lax.fori_loop(0, span, step, tuple(starts), unroll=4)
        from_steps(rows, y_tiles, tile)
        context_ref[:, lane_tile(tile)] = rows[...].astype(bf16)


def whole_rows(block):
    return block.reshape(block.shape[0] * block.shape[1], block.shape[2])


def head(index):
    return slice(index * HD, (index + 1) * HD)


def weight_copies(pieces, buffer, place, sems, act):
    col_parts, row_parts = sems.shape
    for k in range(col_parts):
        for r in range(row_parts):
            inner = buffer.at[k, place[2] ^ r]
            act(pltpu.make_async_copy(pieces[k * row_parts + r], inner, sems.at[k, r]))


def of_heads(buffer, i):
    return jnp.concatenate([whole_rows(buffer[k, :, :, head(i)]) for k in range(buffer.shape[0])], axis=1)


def gradient_slot(row_parts, order, r):
    position = 0
    for bit in reversed(order):
        position = 2 * position + (1 if r & bit else 0)
    return position // (row_parts // 2), position % (row_parts // 2)


def round_orders(row_parts):
    bits = [1 << i for i in range(row_parts.bit_length() - 1)]
    return bits, bits[::-1]


def gradient_pieces(stacks, row_parts, far, slot):
    found = []
    for r in range(row_parts):
        sent, at = gradient_slot(row_parts, round_orders(row_parts)[far], r)
        found.append(stacks[2 * far + sent].at[at, slot])
    return found


def project_kernel(team, col_parts, row_parts, place, normed_ref, cot_ref, *refs):
    contexts, refs = refs[:team], refs[team:]
    count = col_parts * row_parts
    pieces, refs = refs[:count], refs[count:]
    context_t_ref, cot_t_ref, kept_ref = refs[:3]
    context_ref, weights, sems = refs[3:]
    weight_copies(pieces, weights, place, sems, lambda copy: copy.start())
    width = contexts[0].shape[1]
    for k in range(team):
        lanes = pl.ds(pl.multiple_of((place[0] ^ k) * width, LANES), width)
        context_ref[:, lanes] = contexts[k][...]
    context_t_ref[...] = context_ref[...].T
    cot_t_ref[...] = cot_ref[...].T
    weight_copies(pieces, weights, place, sems, lambda copy: copy.wait())
    kept_ref[0] = dot(normed_ref[...], of_heads(weights, 0)).astype(bf16)
    kept_ref[1] = dot(context_ref[...], of_heads(weights, 1)).astype(bf16)
    kept_ref[2] = dot(context_ref[...], of_heads(weights, 2)).astype(bf16)


def attend_kernel(team, col_parts, row_parts, place, kept_ref, *refs):
    count = col_parts * row_parts
    pieces, refs = refs[:count], refs[count:]
    part_ref, attended_ref, probs_ref, probs_t_ref, weights, sems = refs
    weight_copies(pieces, weights, place, sems, lambda copy: copy.start())
    length = kept_ref.shape[1]
    rows = lax.broadcasted_iota(jnp.int32, (length, length), 0)
    cols = lax.broadcasted_iota(jnp.int32, (length, length), 1)
    for h in range(col_parts):
        scores = dot_t(kept_ref[0, :, head(h)], kept_ref[1, :, head(h)]) * score_scale
        scores = jnp.where(rows >= cols, scores, -1e30)
        shifted = jnp.exp(scores - jnp.max(scores, axis=-1, keepdims=True))
        inverse = 1.0 / jnp.sum(shifted, axis=-1, keepdims=True)
        probs = (shifted * inverse).astype(bf16)
        probs_ref[h] = probs
        probs_t_ref[h] = probs.T
        attended_ref[:, head(h)] = dot(probs, kept_ref[2, :, head(h)]).astype(bf16)
    weight_copies(pieces, weights, place, sems, lambda copy: copy.wait())
    part_ref[...] = dot_t(attended_ref[...], of_heads(weights, 3)).astype(bf16)


def gelu_parts(hidden, grad_act):
    density = jnp.exp(-0.5 * hidden * hidden)
    t = 1.0 / (1.0 + (0.3275911 * math.sqrt(0.5)) * jnp.abs(hidden))
    series = 0.5 * 1.061405429
    for factor in (-1.453152027, 1.421413741, -0.284496736, 0.254829592):
        series = series * t + 0.5 * factor
    tail = series * t * density
    cdf = jnp.where(hidden >= 0.0, 1.0 - tail, tail)
    slope = cdf + hidden * density * (1.0 / math.sqrt(2.0 * math.pi))
    return (hidden * cdf).astype(bf16), (grad_act * slope).astype(bf16)


def middle_kernel(team, x_ref, gain_ref, *refs):
    parts, (middle_ref, normed_ref, normed_t_ref) = refs[:team], refs[team:]
    attn = parts[0][...].astype(f32)
    for part in parts[1:]:
        attn = attn + part[...].astype(f32)
    middle = x_ref[...].astype(f32) + attn
    middle_ref[...] = middle
    unit, unused = normalise(middle)
    normed_ref[...] = (unit * gain_ref[...]).astype(bf16)
    normed_t_ref[...] = normed_ref[...].T


def feed_kernel(col_parts, row_parts, place, normed_ref, normed_t_ref, cot_ref, cot_t_ref, *refs):
    arrays, refs = (refs[:row_parts], refs[row_parts : 2 * row_parts]), refs[2 * row_parts :]
    out_ref, two_ref = refs[:2]
    stacks, refs = (refs[2:6], refs[6:10]), refs[10:]
    up_all, down_all, grad_up, grad_down, activated_all, grad_all, sems = refs
    z = pl.program_id(0)
    half = col_parts // 2
    hidden_cols = grad_up.shape[3]

    def copies(k):
        found = []
        for r in range(row_parts):
            for which, buffer in enumerate((up_all, down_all)):
                outside = arrays[which][r].at[k]
                inside = buffer.at[place[2] ^ r, :, pl.ds(k * hidden_cols, hidden_cols)]
                found.append(pltpu.make_async_copy(outside, inside, sems.at[which, k, r]))
        return found

    def each_leaving(k, act):
        for which, buffer in enumerate((grad_up, grad_down)):
            steps = lax.rem(place[6] + col_parts - k, col_parts)
            for far in range(2):

                @pl.when(steps // half == far)
                def leaves():
                    slot = lax.rem(steps, half)
                    for r, piece in enumerate(gradient_pieces(stacks[which], row_parts, far, slot)):
                        inner = buffer.at[k, place[2] ^ r]
                        act(pltpu.make_async_copy(inner, piece, sems.at[2 + which, k, r]))

    @pl.when(z == 0)
    def start():
        for k in range(col_parts):
            for copy in copies(k):
                copy.start()

    for k in range(col_parts):

        @pl.when(z == k)
        def arrive():
            for copy in copies(k):
                copy.wait()

    at = pl.ds(pl.multiple_of(z * hidden_cols, hidden_cols), hidden_cols)
    hidden = dot(normed_ref[...], whole_rows(up_all[:, :, at]))
    grad_act = dot(cot_ref[...], whole_rows(down_all[:, :, at]))
    activated, grad_pre = gelu_parts(hidden, grad_act)
    activated_all[:, at] = activated
    grad_all[:, at] = grad_pre
    shape = grad_up.shape[1:]
    grad_up[z] = dot(normed_t_ref[...], grad_pre).astype(bf16).reshape(shape)
    grad_down[z] = dot(cot_t_ref[...], activated).astype(bf16).reshape(shape)

    for k in range(col_parts):

        @pl.when(z == k)
        def leave():
            each_leaving(k, lambda copy: copy.start())

    @pl.when(z == col_parts - 1)
    def finish():
        two_ref[...] = dot_t(grad_all[...], whole_rows(up_all[...])).astype(bf16)
        out_ref[...] = dot_t(activated_all[...], whole_rows(down_all[...])).astype(bf16)
        for k in range(col_parts):
            each_leaving(k, lambda copy: copy.wait())


def attend_back_kernel(team, col_parts, row_parts, place, middle_ref, gain_ref, cot_ref, *refs):
    parts, refs = refs[:team], refs[team:]
    late, refs = refs[:6], refs[6:]
    count = col_parts * row_parts
    pieces, refs = refs[:count], refs[count:]
    middle_grad_ref, gain_grad_ref, one_ref = refs[:3]
    refs = refs[3:]
    context_grads, refs = refs[:team], refs[team:]
    stacks, refs = refs[:4], refs[4:]
    weights, grads, low, grad_out, grad_q, grad_k, grad_v = refs[:7]
    held, (sems, out_sems, late_sems) = refs[7:13], refs[13:]
    normed_t_ref, context_t_ref, kept_ref, attended_ref, probs_ref, probs_t_ref = held
    half = col_parts // 2
    weight_copies(pieces, weights, place, sems, lambda copy: copy.start())
    late_copies = [
        pltpu.make_async_copy(outside, inside, late_sems.at[i])
        for i, (outside, inside) in enumerate(zip(late, held))
    ]
    for copy in late_copies:
        copy.start()
    own_rows = middle_ref.shape[0] // team
    grad_two = parts[0][...].astype(f32)
    for part in parts[1:]:
        grad_two = grad_two + part[...].astype(f32)
    unit, inverse = normalise(middle_ref[...])
    grad_gain = grad_two * unit
    rows = lax.broadcasted_iota(jnp.int32, grad_gain.shape, 0)
    first = place[0] * own_rows
    mine = (rows >= first) & (rows < first + own_rows)
    gain_grad_ref[...] = jnp.sum(jnp.where(mine, grad_gain, 0.0), axis=0, keepdims=True)
    grad = cot_ref[...].astype(f32) + normalise_back(unit, inverse, grad_two * gain_ref[...])
    low[...] = grad.astype(bf16)
    for k in range(team):

        @pl.when(place[0] == k)
        def own():
            middle_grad_ref[...] = grad[k * own_rows : (k + 1) * own_rows, :]

    weight_copies(pieces, weights, place, sems, lambda copy: copy.wait())
    for copy in late_copies:
        copy.wait()
    grad_out[...] = dot(low[...], of_heads(weights, 3)).astype(bf16)
    for h in range(col_parts):
        q, k, v = (kept_ref[i, :, head(h)] for i in range(3))
        grad_heads = grad_out[:, head(h)]
        grad_v[:, head(h)] = dot(probs_t_ref[h], grad_heads).astype(bf16)
        probs = probs_ref[h].astype(f32)
        grad_probs = dot_t(grad_heads, v)
        inner = jnp.sum(grad_probs * probs, axis=-1, keepdims=True)
        grad_scores = (probs * (grad_probs - inner)).astype(bf16)
        grad_q[:, head(h)] = (dot(grad_scores, k) * score_scale).astype(bf16)
        turned = dot_t(v, grad_heads) - inner.T
        turned = (probs_t_ref[h].astype(f32) * turned).astype(bf16)
        grad_k[:, head(h)] = (dot(turned, q) * score_scale).astype(bf16)
    shape = (*grads.shape[1:3], HD)

    def put(i, grad):
        for h in range(col_parts):
            grads[h, :, :, head(i)] = grad[:, head(h)].astype(bf16).reshape(shape)

    put(3, dot(low[...].T, attended_ref[...]))
    put(0, dot(normed_t_ref[...], grad_q[...]))
    put(1, dot(context_t_ref[...], grad_k[...]))
    put(2, dot(context_t_ref[...], grad_v[...]))
    copies = []
    for k in range(col_parts):
        for r, piece in enumerate(gradient_pieces(stacks, row_parts, k // half, k % half)):
            copies.append(pltpu.make_async_copy(grads.at[k, place[2] ^ r], piece, out_sems.at[k, r]))
    for copy in copies:
        copy.start()
    total = dot_t(grad_k[...], of_heads(weights, 1)) + dot_t(grad_v[...], of_heads(weights, 2))
    middle_total = total.astype(bf16)
    low[...] = middle_total
    width = context_grads[0].shape[1]
    for k in range(team):
        lanes = pl.ds(pl.multiple_of((place[0] ^ k) * width, LANES), width)
        context_grads[k][...] = low[:, lanes]
    one_ref[...] = dot_t(grad_q[...], of_heads(weights, 0)).astype(bf16)
    for copy in copies:
        copy.wait()


def adjoint_kernel(team, logr_ref, *refs):
    parts = refs[:team]
    g_tiles, ends_ref, total_ref, rows = refs[team:]
    grad = parts[0][...].astype(f32)
    for part in parts[1:]:
        grad = grad + part[...].astype(f32)
    grad = grad.astype(bf16).astype(f32)
    tiles, length, unused = g_tiles.shape
    states = logr_ref.shape[0]
    span = length // SUBS
    for tile in range(tiles):
        rows[...] = grad[:, lane_tile(tile)]
        in_steps(g_tiles, tile, rows)
    before = (sub_index() * span).astype(f32)
    for tile in range(tiles):
        rate = jnp.exp(logr_ref[:, lane_tile(tile)])
        decay = jnp.exp(-rate)
        for first in range(0, states, GROUP):
            chosen = range(first, first + GROUP)
            decays = [spread(decay[n : n + 1]) for n in chosen]

            def step(i, held):
                g = g_tiles[tile, step_rows(span - 1 - i), :]
                later = []
                for d, (b, w) in zip(decays, held):
                    shrunk = d * b
                    later.append((g + shrunk, d * w + shrunk))
                return tuple(later)

            zero = no_state(g_tiles)
            held = lax.fori_loop(0, span, step, ((zero, zero),) * GROUP, unroll=4)
            for n, (b, w) in zip(chosen, held):
                ends_ref[0, n, :, lane_tile(tile)] = b
                ends_ref[1, n, :, lane_tile(tile)] = w
                shrink = jnp.exp(-before * rate[n : n + 1])
                total_ref[0, n : n + 1, lane_tile(tile)] = jnp.sum(
                    shrink * b, axis=0, keepdims=True
                )
                total_ref[1, n : n + 1, lane_tile(tile)] = jnp.sum(
                    shrink * (w + before * b), axis=0, keepdims=True
                )


def context_back_kernel(
    team, place, g_tiles, u_tiles, ends_ref, all_ref, logr_ref, coef_ref, one_ref, *refs
):
    pieces = refs[:team]
    grad_ssm_ref, y_tiles, full, rows = refs[team:]
    tiles, length, unused = u_tiles.shape
    states = logr_ref.shape[0]
    span = length // SUBS
    width = tiles * LANES
    index = sub_index()
    after = ((SUBS - 1 - index) * span).astype(f32)
    full[...] = one_ref[...].astype(f32)
    group = GROUP
    for tile in range(tiles):
        lanes = lane_tile(tile)
        rate = jnp.exp(logr_ref[:, lanes])
        decay = jnp.exp(-rate)
        root = jnp.sqrt(2.0 * rate)
        scale = coef_ref[:, lanes] * root
        in_b = jnp.zeros((states, LANES), f32)
        in_w = jnp.zeros((states, LANES), f32)
        for j in range(all_ref.shape[0]):
            gap = j - place[1] - 1
            distance = (jnp.maximum(gap, 0) * length).astype(f32)
            shrink = jnp.exp(-distance * rate)
            b, w = all_ref[j, 0, :, lanes].astype(f32), all_ref[j, 1, :, lanes].astype(f32)
            in_b = in_b + jnp.where(gap >= 0, shrink * b, 0.0)
            in_w = in_w + jnp.where(gap >= 0, shrink * (w + distance * b), 0.0)
        for first in range(0, states, group):
            chosen = range(first, first + group)
            starts = []
            for n in chosen:
                row = rate[n : n + 1]
                b, w = ends_ref[0, n, :, lanes], ends_ref[1, n, :, lanes]
                for d in (1, 2, 4):
                    shrink = jnp.exp(-(d * span) * row)
                    next_b = pltpu.roll(b, SUBS - d, 0)
                    next_w = pltpu.roll(w, SUBS - d, 0)
                    inside = index < SUBS - d
                    b, w = (
                        b + jnp.where(inside, shrink * next_b, 0.0),
                        w + jnp.where(inside, shrink * (next_w + (d * span) * next_b), 0.0),
                    )
                inside = index < SUBS - 1
                b = jnp.where(inside, pltpu.roll(b, SUBS - 1, 0), 0.0)
                w = jnp.where(inside, pltpu.roll(w, SUBS - 1, 0), 0.0)
                shrink = jnp.exp(-after * row)
                b_row, w_row = in_b[n : n + 1], in_w[n : n + 1]
                b = b + shrink * b_row
                w = w + shrink * (w_row + after * b_row)
                zero = no_state(u_tiles)
                starts.append((b, w, zero, zero))
            decays = [spread(decay[n : n + 1]) for n in chosen]
            scales = [spread(scale[n : n + 1]) for n in chosen]

            def step(i, held):
                at = step_rows(span - 1 - i)
                g = g_tiles[tile, at, :]
                u = u_tiles[tile, at, :]
                later, parts = [], []
                for d, s, (b, w, sum_b, sum_w) in zip(decays, scales, held):
                    shrunk = d * b
                    w = d * w + shrunk
                    b = g + shrunk
                    later.append((b, w, sum_b + u * b, sum_w + u * w))
                    parts.append(s * b)
                while len(parts) > 1:
                    parts = [p + q for p, q in zip(parts[::2], parts[1::2])]
                if first > 0:
                    parts[0] = parts[0] + y_tiles[tile, at, :]
                y_tiles[tile, at, :] = parts[0]
                return tuple(later)

            held = lax.fori_loop(0, span, step, tuple(starts), unroll=2)
            for n, (unused_b, unused_w, sum_b, sum_w) in zip(chosen, held):
                sum_b = jnp.sum(sum_b, axis=0, keepdims=True)
                sum_w = jnp.sum(sum_w, axis=0, keepdims=True)
                row = slice(n, n + 1)
                grad_ssm_ref[0, row, lanes] = root[row] * sum_b
                grad_ssm_ref[1, row, lanes] = scale[row] * (0.5 * sum_b - rate[row] * sum_w)
        at_lanes = pl.ds(pl.multiple_of(place[0] * width + tile * LANES, LANES), LANES)
        from_steps(rows, y_tiles, tile)
        full[:, at_lanes] += rows[...].astype(bf16).astype(f32)
    count = pieces[0].shape[0]
    for k in range(team):
        at_rows = pl.ds(pl.multiple_of((place[0] ^ k) * count, count), count)
        pieces[k][...] = full[at_rows, :].astype(bf16)


def input_grad_kernel(team, place, x_ref, gain_ref, middle_grad_ref, *refs):
    parts, (out_ref, gain_grad_ref) = refs[:team], refs[team:]
    rows = out_ref.shape[0]
    at_rows = pl.ds(pl.multiple_of(place[0] * rows, rows), rows)
    grad_one = parts[0][...].astype(f32)
    for part in parts[1:]:
        grad_one = grad_one + part[...].astype(f32)
    unit, inverse = normalise(x_ref[at_rows, :].astype(f32))
    gain_grad_ref[...] = jnp.sum(grad_one * unit, axis=0, keepdims=True)
    back = normalise_back(unit, inverse, grad_one * gain_ref[...])
    out_ref[...] = (middle_grad_ref[...] + back).astype(bf16)


def assemble_kernel(halves, low_count, place, own_ref, *refs):
    others, out_ref = refs[:-1], refs[-1]
    count, rows, unused = own_ref.shape
    half = place[4]

    def put(value, sequence, which, member):
        at_rows = pl.ds(pl.multiple_of((which * low_count + member) * rows, rows), rows)
        out_ref[sequence, at_rows, :] = value.astype(out_ref.dtype)

    for sequence in range(count // (halves * low_count)):
        if halves == 1:
            for member in range(low_count):
                put(own_ref[sequence * low_count + member], sequence, 0, member)
        else:
            put(own_ref[sequence * halves + half], sequence, half, 0)
            put(others[0][sequence], sequence, 1 - half, 0)


def pack_kernel(halves, place, qkv_ref, out_ref, up_ref, down_ref, *refs):
    rows = up_ref.shape[0]
    heads, hidden = out_ref.shape[0] // halves, up_ref.shape[1] // halves
    for which in range(halves):
        side = place[4] if which == 0 else 1 - place[4]
        at_heads = pl.ds(pl.multiple_of(side * heads, LANES), heads)
        at_hidden = pl.ds(pl.multiple_of(side * hidden, LANES), hidden)
        if which == 0:
            head_ref, wide_ref, deep_ref = refs[:3]
        else:
            packed = refs[3]
            head_ref = packed.at[:, : 4 * heads]
            wide_ref = packed.at[:, 4 * heads : 4 * heads + hidden]
            deep_ref = packed.at[:, 4 * heads + hidden :]
        for i in range(3):
            head_ref[:, i * heads : (i + 1) * heads] = qkv_ref[i, :, at_heads].astype(bf16)
        head_ref[:, 3 * heads :] = out_ref[at_heads, :].T.astype(bf16)
        wide_ref[...] = up_ref[:, at_hidden].astype(bf16)
        deep_ref[...] = down_ref[at_hidden, :].T.astype(bf16)


def small_kernel(ssm_ref, gains_ref, out_ref):
    count = ssm_ref.shape[0]
    out_ref[:count, :] = ssm_ref[...]
    out_ref[count:, :] = gains_ref[...]


def lamb_moments(weight, grad_item, first_old, second_old):
    first_new = beta_first * first_old + (1.0 - beta_first) * grad_item
    second_new = beta_second * second_old + (1.0 - beta_second) * grad_item * grad_item
    direction = (
        first_new
        / (1.0 - beta_first**STEP)
        / (jnp.sqrt(second_new / (1.0 - beta_second**STEP)) + lamb_eps)
        + weight_decay * weight
    )
    return (first_new, second_new, direction)


def place_sums(sums_ref, sums):
    rows = lax.broadcasted_iota(jnp.int32, sums_ref.shape, 0)
    lanes = lax.broadcasted_iota(jnp.int32, sums_ref.shape, 1)
    found = jnp.zeros(sums_ref.shape, f32)
    for index, pair in sums.items():
        for row, value in enumerate(pair):
            found = jnp.where((rows == row) & (lanes == index), value, found)
    sums_ref[...] = found


def moments_kernel(halves, matrices, place, *refs):
    count = 1 + max(item[1] for item in matrices)
    grads, refs = [refs[halves * i : halves * (i + 1)] for i in range(count)], refs[halves * count :]
    arrays = len({(item[1], item[4] is None) for item in matrices})
    ins = [refs[3 * i : 3 * i + 3] for i in range(arrays)]
    outs = [refs[3 * (arrays + i) : 3 * (arrays + i) + 3] for i in range(arrays)]
    sums_ref = refs[6 * arrays]
    keys = []
    sums = {}
    for number, source, column, turned, stacked in matrices:
        key = (source, stacked is None)
        if key not in keys:
            keys.append(key)
        pick = (lambda ref: ref) if stacked is None else (lambda ref, i=stacked: ref.at[i])
        weight, first, second = (pick(ref) for ref in ins[keys.index(key)])
        news = [pick(ref) for ref in outs[keys.index(key)]]
        width = weight.shape[0 if turned else 1] // halves
        rows = weight.shape[1 if turned else 0]
        cols = slice(column * width, (column + 1) * width)
        total_weight = total_update = 0.0
        for which, grad_ref in enumerate(grads[source]):
            side = place[4] if which == 0 else 1 - place[4]
            at = pl.ds(pl.multiple_of(side * width, width), width)
            if which == 0:
                grad = grad_ref[pl.ds(pl.multiple_of(side * rows, rows), rows), cols].astype(f32)
            else:
                grad = grad_ref[:, cols].astype(f32)
            at = (at, slice(None)) if turned else (slice(None), at)
            grad = grad.T if turned else grad
            old = weight[at]
            found = lamb_moments(old, grad, first[at], second[at])
            for ref, value in zip(news, found):
                ref[at] = value
            total_weight = total_weight + jnp.sum(old * old)
            total_update = total_update + jnp.sum(found[2] * found[2])
        sums[number] = (total_weight, total_update)
    place_sums(sums_ref, sums)


def small_moments_kernel(numbers, grads_ref, *refs):
    ins, outs, sums_ref = (refs[:3], refs[3:6]), (refs[6:9], refs[9:12]), refs[12]
    states = (grads_ref.shape[0] - 2) // 2
    sums = {}
    for (weight, first, second), news, start, rows, first_number in (
        (ins[0], outs[0], 2 * states, 1, numbers[0]),
        (ins[1], outs[1], 0, states, numbers[1]),
    ):
        for i in range(2):
            grad = grads_ref[start + i * rows : start + (i + 1) * rows, :]
            at = slice(i * rows, (i + 1) * rows)
            found = lamb_moments(weight[at, :], grad, first[at, :], second[at, :])
            for ref, value in zip(news, found):
                ref[at, :] = value
            sums[first_number + i] = (
                jnp.sum(weight[at, :] * weight[at, :]),
                jnp.sum(found[2] * found[2]),
            )
    place_sums(sums_ref, sums)


def update_kernel(stacks, sums_ref, *refs):
    count = len(stacks)
    weights, directions, news = refs[:count], refs[count : 2 * count], refs[2 * count : 3 * count]
    norms = jnp.sqrt(jnp.sum(sums_ref[...], axis=0))
    refs[3 * count][...] = norms
    ratios = norms[0:1] / norms[1:2]
    lanes = lax.broadcasted_iota(jnp.int32, ratios.shape, 1)
    for numbers, weight, direction, new in zip(stacks, weights, directions, news):
        step = weight.shape[0] // len(numbers)
        for i, number in enumerate(numbers):
            ratio = jnp.sum(jnp.where(lanes == number, ratios, 0.0), axis=1, keepdims=True)
            at = slice(i * step, (i + 1) * step)
            scale = learn_rate * ratio.reshape((1,) * weight.ndim)
            new[at] = weight[at] - scale * direction[at]


def call(
    body, ins, outs, scratch=(), grid=None, in_specs=None, out_specs=None, time=1.0, after=(), token=False
):
    moved = sum(a.size * a.dtype.itemsize for a in list(ins) + list(outs))
    params = pltpu.CompilerParams(vmem_limit_bytes=VMEM_BYTES)
    cost = pl.CostEstimate(flops=int(time * 1.15e9), bytes_accessed=moved, transcendentals=0)
    whole = pl.BlockSpec(memory_space=pltpu.VMEM)
    anywhere = pl.BlockSpec(memory_space=pl.ANY)
    in_specs = list(in_specs or [whole] * len(ins)) + [anywhere] * len(after)
    out_specs = list(out_specs or [whole] * len(outs))
    outs = list(outs)
    first_out = len(ins) + len(after)
    last_out = first_out + len(outs)
    if token:
        outs.append(jax.ShapeDtypeStruct((SUBS, LANES), f32))
        out_specs.append(whole)

    def run(*refs):
        refs = list(refs)
        if token:
            refs[last_out][...] = jnp.zeros((SUBS, LANES), f32)
            del refs[last_out]
        body(*refs[: len(ins)], *refs[first_out:])

    return pl.pallas_call(
        run,
        out_shape=tuple(outs),
        in_specs=in_specs,
        out_specs=tuple(out_specs),
        scratch_shapes=list(scratch),
        compiler_params=params,
        cost_estimate=cost,
        **({} if grid is None else {"grid": grid}),
    )(*ins, *after)


def shaped(shape, kind):
    return jax.ShapeDtypeStruct(tuple(shape), kind)


def on_device(
    tokens,
    cotangent,
    w_qkv,
    w_out,
    w_up,
    w_down,
    norm_gains,
    ssm_param,
    first_qkv,
    second_qkv,
    first_out,
    second_out,
    first_up,
    second_up,
    first_down,
    second_down,
    first_gain,
    second_gain,
    first_ssm,
    second_ssm,
):
    halves = lax.axis_size("sl")
    low_count = lax.axis_size("ml")
    row_parts = lax.axis_size("sh")
    col_parts = lax.axis_size("mb") * lax.axis_size("mq")
    team = halves * low_count
    sl, ml, mb, mq = (lax.axis_index(name) for name in ("sl", "ml", "mb", "mq"))
    rank = sl * low_count + ml
    block_index = lax.axis_index("sh") * halves + mq
    seq_total, length, width = tokens.shape
    assert length == BLK and seq_total == lax.axis_size("mb")
    states = ssm_param.shape[1]
    channels = width // team
    tiles = channels // LANES
    row_count = width // row_parts
    own_rows = length // team
    place = [rank, block_index, lax.axis_index("sh"), lax.axis_index(MODEL), sl, sl ^ mq]
    place.append(lax.axis_index(COLS))
    place = jnp.stack(place).astype(jnp.int32)
    smem = pl.BlockSpec(memory_space=pltpu.SMEM)
    vmem = pl.BlockSpec(memory_space=pltpu.VMEM)

    def permute(value, axes, moves):
        return lax.ppermute(value, axes, moves)

    def swap(value):
        return permute(value, "sl", [(0, 1), (1, 0)])

    def in_order(own, other, axis):
        return jnp.where(
            sl == 0, jnp.concatenate([own, other], axis), jnp.concatenate([other, own], axis)
        )

    def team_send(pieces):
        moved = [pieces[0]]
        for k in range(1, team):
            moved.append(permute(pieces[k], TEAM, [(i, i ^ k) for i in range(team)]))
        return moved

    def pick_block(array):
        own = lax.dynamic_index_in_dim(array, mb, 0, keepdims=False)
        if halves == 1:
            return own, ()
        other = swap(own)
        return jnp.where(sl == mq, own, other), (other,)

    def across(value, bit):
        return permute(value, "sh", [(i, i ^ bit) for i in range(row_parts)])

    def along(value, axes, step):
        count = lax.axis_size(axes)
        return permute(value, axes, [(i, (i + step) % count) for i in range(count)])

    bits = [1 << i for i in range(row_parts.bit_length() - 1)]

    def bit_order(k):
        return bits if k % 2 == 0 else bits[::-1]

    def double_rows(value, order):
        found = {0: value}
        for bit in order:
            for r in list(found):
                found[r | bit] = across(found[r], bit)
        return [found[r] for r in range(row_parts)]

    def add(*items, zero=None):
        total = sum(item.astype(f32) for item in items)
        return (total if zero is None else total + zero[0, 0]).astype(bf16)

    def first_messages(stacks):
        return across(stacks[1], bits[-1]), across(stacks[3], bits[0])

    def halve_rows(keep, arrived, order, zero=None, last=None):
        items = [keep, arrived]
        for bit in order[-2::-1]:
            count = arrived.shape[0] // 2
            arrived = across(add(*[item[count:] for item in items], zero=zero), bit)
            items = [item[:count] for item in items] + [arrived]
        return add(*[item[0] for item in items], zero=last)

    def halve_both(stacks, first, zero=None, last=None):
        near = halve_rows(stacks[0], first[0], bits, zero, last)
        return near, halve_rows(stacks[2], first[1], bits[::-1], zero, last)

    def token_after(*arrays):
        return call(lambda: None, (), (), after=arrays, token=True)[0]

    def ring_gather(shard):
        pieces, held = [], shard
        for k in range(col_parts):
            if k > 0:
                held = along(held, COLS, 1)
            pieces.append(double_rows(held, bits if k % 2 == 0 else bits[::-1]))
        return pieces

    def sum_over_z(near, far):
        pieces = [stack[k] for stack in (near, far) for k in range(col_parts // 2)]
        moved = [along(piece, COLS, -k) for k, piece in enumerate(pieces) if k > 0]
        return add(pieces[0], *moved)

    def everywhere(value, axes):
        count = lax.axis_size(axes)
        copies = jnp.broadcast_to(value[None], (count, *value.shape))
        return lax.all_to_all(copies, axes, 0, 0, tiled=True)

    rows_dev = w_up.shape[0]
    hidden_cols = w_up.shape[1] // halves
    head_cols = 4 * w_out.shape[0] // halves
    packed_cols = head_cols + 2 * hidden_cols
    sides = [shaped((rows_dev, cols), bf16) for cols in (head_cols, hidden_cols, hidden_cols)]
    shards = call(
        functools.partial(pack_kernel, halves),
        (place, w_qkv, w_out, w_up, w_down),
        sides + [shaped((rows_dev, packed_cols), bf16)] * (halves - 1),
        time=2.4,
        in_specs=[smem] + [vmem] * 4,
    )
    if halves == 2:
        other = swap(shards[3])
        cuts = (0, head_cols, head_cols + hidden_cols, packed_cols)
        shards = [
            in_order(own, other[:, first:last], 0)
            for own, first, last in zip(shards, cuts, cuts[1:])
        ]
    head_shard, up_shard, down_shard = shards[:3]
    attn_w = ring_gather(head_shard)
    up_full = lax.all_gather(up_shard, COLS, axis=0, tiled=False)
    down_full = lax.all_gather(down_shard, COLS, axis=0, tiled=False)
    up_w = double_rows(up_full, bits)
    down_w = double_rows(down_full, bits[::-1])
    attn_flat = [piece for group in attn_w for piece in group]

    small, = call(
        small_kernel,
        (ssm_param.reshape(2 * states, -1), norm_gains),
        (shaped((2 * states + 2, norm_gains.shape[1]), f32),),
        after=(attn_w[1][0],),
    )
    small = jnp.transpose(everywhere(small, ALL), (1, 0, 2)).reshape(2 * states + 2, width)
    own_ssm = lax.dynamic_slice_in_dim(
        small[: 2 * states].reshape(2, states, width), rank * channels, channels, 2
    )
    coef, logr = own_ssm[0], own_ssm[1]
    gain_one = small[2 * states : 2 * states + 1]
    gain_two = small[2 * states + 1 : 2 * states + 2]

    x, unused = pick_block(tokens)
    cot, cot_other = pick_block(cotangent)

    anywhere = [pl.BlockSpec(memory_space=pl.ANY)]

    def fixed(*shape):
        return pl.BlockSpec(shape, lambda z: (0,) * len(shape))

    wide = fixed(length, width)
    row = fixed(1, width)

    normed_one, normed_t, u_steps, ends, total = call(
        norm_kernel,
        (place, x, gain_one, logr),
        (
            shaped((length, width), bf16),
            shaped((width, length), bf16),
            shaped((tiles, length, LANES), f32),
            shaped((states, SUBS, channels), f32),
            shaped((states, channels), f32),
        ),
        scratch=[pltpu.VMEM((length, LANES), f32)],
        in_specs=[smem, vmem, vmem, vmem],
        after=(*attn_w[0][1:-1], *cot_other),
        time=5,
    )
    totals = everywhere(total.astype(bf16), ("sh", "mq"))
    (context_own,) = call(
        context_kernel,
        (place, u_steps, ends, totals, logr, coef),
        (shaped((length, channels), bf16),),
        after=(attn_w[0][-1], *attn_w[1][1:-1], attn_w[-1][0], up_full),
        scratch=[pltpu.VMEM((tiles, length, LANES), f32), pltpu.VMEM((length, LANES), f32)],
        in_specs=[smem] + [vmem] * 5,
        time=7,
    )
    contexts = team_send([context_own] * team)

    stack_shape = (row_parts // 2, col_parts // 2, row_count)
    head_stacks = [shaped((*stack_shape, head_cols), bf16)] * 4
    hidden_stacks = [shaped((*stack_shape, hidden_cols), bf16)] * 8
    sizes = (team, col_parts, row_parts)
    head_buffer = pltpu.VMEM((col_parts, row_parts, row_count, 4 * HD), bf16)
    head_sems = pltpu.SemaphoreType.DMA((col_parts, row_parts))
    kept_shape = shaped((3, length, col_parts * HD), bf16)
    flat_shape = shaped((length, col_parts * HD), bf16)
    context_t, cot_t, kept = call(
        functools.partial(project_kernel, *sizes),
        (place, normed_one, cot, *contexts, *attn_flat),
        (shaped((width, length), bf16), shaped((width, length), bf16), kept_shape),
        scratch=[pltpu.VMEM((length, width), bf16), head_buffer, head_sems],
        time=1,
        in_specs=[smem] + [vmem] * (2 + team) + anywhere * len(attn_flat),
        after=(*up_w[1:-1], down_full),
    )
    attn_part, attended, probs, probs_t = call(
        functools.partial(attend_kernel, *sizes),
        (place, kept, *attn_flat),
        (
            shaped((length, width), bf16),
            flat_shape,
            *[shaped((col_parts, length, length), bf16)] * 2,
        ),
        scratch=[head_buffer, head_sems],
        time=1,
        in_specs=[smem, vmem] + anywhere * len(attn_flat),
        after=down_w[1:-1],
    )
    attn_parts = team_send([attn_part] * team)

    middle, normed_two, normed_two_t = call(
        functools.partial(middle_kernel, team),
        (x, gain_two, *attn_parts),
        (shaped((length, width), f32), shaped((length, width), bf16), shaped((width, length), bf16)),
        time=1,
    )
    weight_buffer = pltpu.VMEM((row_parts, row_count, col_parts * hidden_cols), bf16)
    grad_buffer = pltpu.VMEM((col_parts, row_parts, row_count, hidden_cols), bf16)
    out_part, two_part, *hidden_grads = call(
        functools.partial(feed_kernel, col_parts, row_parts),
        (place, normed_two, normed_two_t, cot, cot_t, *up_w, *down_w),
        (shaped((length, width), bf16), shaped((length, width), bf16), *hidden_stacks),
        scratch=[
            *[weight_buffer] * 2,
            *[grad_buffer] * 2,
            *[pltpu.VMEM((length, col_parts * hidden_cols), bf16)] * 2,
            pltpu.SemaphoreType.DMA((4, col_parts, row_parts)),
        ],
        time=18,
        grid=(col_parts,),
        in_specs=[smem, wide, fixed(width, length), wide, fixed(width, length)]
        + anywhere * (2 * row_parts),
        out_specs=[wide, wide] + anywhere * 8,
    )
    two_parts = team_send([two_part] * team)

    def rows_of(array, member):
        return lax.dynamic_slice_in_dim(array, member * own_rows, own_rows, 0)

    def share_rows(pieces, kind):
        others = []
        if halves == 2:
            pairs = pieces.reshape(seq_total, halves, own_rows, width)
            others = [swap(lax.dynamic_index_in_dim(pairs, 1 - sl, 1, keepdims=False))]
        (blocks,) = call(
            functools.partial(assemble_kernel, halves, low_count),
            (place, pieces, *others),
            (shaped((seq_total, length, width), kind),),
            time=3.5,
            in_specs=[smem, vmem] + [vmem] * len(others),
        )
        return blocks

    out_pieces = team_send([rows_of(out_part, rank ^ k) for k in range(team)])
    result = rows_of(middle, rank) + sum(item.astype(f32) for item in out_pieces)
    result = result.astype(bf16)
    layer_pieces = lax.all_gather(result, MODEL, axis=0, tiled=False)
    layer_out = share_rows(layer_pieces, bf16)

    def both_halves(own):
        if halves == 1:
            return [own]
        return [own, swap(lax.dynamic_slice_in_dim(own, (1 - sl) * rows_dev, rows_dev, 0))]

    middle_grad, gain_two_grad, one_part, *rest = call(
        functools.partial(attend_back_kernel, *sizes),
        (place, middle, gain_two, cot, *two_parts, normed_t, context_t, kept, attended, probs, probs_t, *attn_flat),
        (
            shaped((own_rows, width), f32),
            shaped((1, width), f32),
            shaped((length, width), bf16),
            *[shaped((length, channels), bf16)] * team,
            *head_stacks,
        ),
        scratch=[
            head_buffer,
            head_buffer,
            pltpu.VMEM((length, width), bf16),
            *[pltpu.VMEM((length, col_parts * HD), bf16)] * 4,
            *[pltpu.VMEM((width, length), bf16)] * 2,
            pltpu.VMEM(kept_shape.shape, bf16),
            pltpu.VMEM(flat_shape.shape, bf16),
            *[pltpu.VMEM((col_parts, length, length), bf16)] * 2,
            head_sems,
            head_sems,
            pltpu.SemaphoreType.DMA((6,)),
        ],
        in_specs=[smem] + [vmem] * (3 + team) + anywhere * (6 + len(attn_flat)),
        out_specs=[vmem] * (3 + team) + anywhere * 4,
        time=1,
        after=(result,),
    )
    context_grads = team_send(rest[:team])
    down_first = first_messages(hidden_grads[4:])
    up_first = first_messages(hidden_grads[:4])
    g_steps, adjoint_ends, adjoint_total = call(
        functools.partial(adjoint_kernel, team),
        (logr, *context_grads),
        (
            shaped((tiles, length, LANES), f32),
            shaped((2, states, SUBS, channels), f32),
            shaped((2, states, channels), f32),
        ),
        scratch=[pltpu.VMEM((length, LANES), f32)],
        time=1,
        after=down_first,
    )
    adjoint_totals = everywhere(adjoint_total.astype(bf16), ("sh", "mq"))
    head_first = first_messages(rest[team:])
    totals_there = token_after(adjoint_totals)
    *one_pieces, grad_ssm, context_done = call(
        functools.partial(context_back_kernel, team),
        (place, g_steps, u_steps, adjoint_ends, adjoint_totals, logr, coef, one_part),
        (
            *[shaped((own_rows, width), bf16)] * team,
            shaped((2, states, channels), f32),
        ),
        scratch=[
            pltpu.VMEM((tiles, length, LANES), f32),
            pltpu.VMEM((length, width), f32),
            pltpu.VMEM((length, LANES), f32),
        ],
        in_specs=[smem] + [vmem] * 7,
        time=1,
        after=(totals_there,),
        token=True,
    )
    one_pieces = team_send(one_pieces)
    down_sums = halve_both(hidden_grads[4:], down_first, totals_there, context_done)
    grad_rows, gain_one_grad, rows_done = call(
        functools.partial(input_grad_kernel, team),
        (place, x, gain_one, middle_grad, *one_pieces),
        (shaped((own_rows, width), bf16), shaped((1, width), f32)),
        in_specs=[smem] + [vmem] * (3 + team),
        time=1,
        after=(layer_pieces, *down_sums),
        token=True,
    )
    grad_down = sum_over_z(*down_sums)
    head_sums = halve_both(rest[team:], head_first, rows_done)
    heads_there = token_after(*head_sums)
    grad_up = sum_over_z(*halve_both(hidden_grads[:4], up_first, context_done, heads_there))
    grad_heads = sum_over_z(*head_sums)
    input_grad = share_rows(lax.all_gather(grad_rows, MODEL, axis=0, tiled=False), f32)

    placed_ssm = lax.dynamic_update_slice_in_dim(
        jnp.zeros((2 * states, width), f32),
        grad_ssm.reshape(2 * states, channels),
        rank * channels,
        1,
    )
    small_grads = jnp.concatenate([placed_ssm, gain_one_grad, gain_two_grad], 0)
    small_grads = small_grads.reshape(2 * states + 2, lax.axis_size(ALL), -1)
    small_grads = lax.all_to_all(jnp.transpose(small_grads, (1, 0, 2)), ALL, 0, 0, tiled=True)
    small_grads = jnp.sum(small_grads, axis=0)

    def moments(matrices, grads, arrays):
        changed = [shaped(old.shape, f32) for group in arrays for old in group]
        grad_parts = [part for grad in grads for part in both_halves(grad)]
        ins = [item for group in arrays for item in group]
        *found, sums = call(
            functools.partial(moments_kernel, halves, matrices),
            (place, *grad_parts, *ins),
            (*changed, shaped((2, LANES), f32)),
            in_specs=[smem] + [vmem] * (len(grad_parts) + len(ins)),
            time=4,
        )
        return [found[3 * i : 3 * i + 3] for i in range(len(arrays))], sums

    hidden_new, hidden_sums = moments(
        ((4, 0, 0, False, None), (5, 1, 0, True, None)),
        (grad_up, grad_down),
        ((w_up, first_up, second_up), (w_down, first_down, second_down)),
    )
    heads_new, head_sums = moments(
        tuple((i, 0, i, False, i) for i in range(3)) + ((3, 0, 3, True, None),),
        (grad_heads,),
        ((w_qkv, first_qkv, second_qkv), (w_out, first_out, second_out)),
    )
    own_channels = norm_gains.shape[1]
    ssm_items = [item.reshape(2 * states, own_channels) for item in (ssm_param, first_ssm, second_ssm)]
    small_items = [norm_gains, first_gain, second_gain, *ssm_items]
    *small_new, small_sums = call(
        functools.partial(small_moments_kernel, (6, 8)),
        (small_grads.reshape(2 * states + 2, own_channels), *small_items),
        (*[shaped(item.shape, f32) for item in small_items], shaped((2, LANES), f32)),
    )
    all_sums = everywhere(hidden_sums + head_sums + small_sums, ALL)
    masters = (w_qkv, w_out, w_up, w_down, norm_gains, ssm_items[0])
    news = (*heads_new, *hidden_new, small_new[:3], small_new[3:])
    *weights, norms = call(
        functools.partial(update_kernel, ((0, 1, 2), (3,), (4,), (5,), (6, 7), (8, 9))),
        (all_sums, *masters, *[group[2] for group in news]),
        (*[shaped(item.shape, f32) for item in masters], shaped((2, LANES), f32)),
        time=3.2,
    )
    outputs = [layer_out, input_grad]
    for index, (weight, (first_new, second_new, unused)) in enumerate(zip(weights, news)):
        if index == 4:
            outputs += [weight, first_new, second_new[0], second_new[1]]
        else:
            kept_shape = ssm_param.shape if index == 5 else weight.shape
            outputs += [item.reshape(kept_shape) for item in (weight, first_new, second_new)]
    outputs.append(norms[:, :10])
    return tuple(outputs)


def solution(mesh):
    seq_count, model_count = mesh.shape["seq"], mesh.shape["mp"]
    halves = 2 if HEADS // model_count >= 2 else 1
    sizes = (seq_count // halves, halves, SEQS, halves, model_count // (SEQS * halves))
    fine = Mesh(mesh.devices.reshape(sizes), ALL)
    seq, model = ("sh", "sl"), ("mb", "mq", "ml")
    rows_cols, cols_rows = P(seq, model), P(model, seq)
    token = P(None, seq, None)
    stack = P(None, seq, model)
    gains = P(None, ALL)
    ssm = P(None, None, ALL)
    return jax.shard_map(
        on_device,
        mesh=fine,
        in_specs=(token, token, stack, cols_rows, rows_cols, cols_rows, gains, ssm)
        + (stack,) * 2
        + (cols_rows,) * 2
        + (rows_cols,) * 2
        + (cols_rows,) * 2
        + (gains,) * 2
        + (ssm,) * 2,
        out_specs=(token, token)
        + (stack,) * 3
        + (cols_rows,) * 3
        + (rows_cols,) * 3
        + (cols_rows,) * 3
        + (gains, gains, P(ALL), P(ALL))
        + (ssm,) * 3
        + (P(),),
        check_vma=False,
    )
```

```python
import functools
import math

import jax
import jax.numpy as jnp
from jax import lax
from jax.experimental import pallas as pl
from jax.experimental.pallas import tpu as pltpu
from jax.sharding import Mesh
from jax.sharding import PartitionSpec as P

HD = 128
HEADS = 8
BLK = 512
STEP = 10
SEQS = 2
LANES = 128
SUBS = 8
GROUP = 8

norm_eps = 1e-05
beta_first = 0.9
beta_second = 0.999
lamb_eps = 1e-06
weight_decay = 0.01
learn_rate = 0.5
score_scale = HD ** (-0.5)

f32 = jnp.float32
bf16 = jnp.bfloat16
VMEM_BYTES = 56 * 1024 * 1024

ALL = ("sh", "sl", "mb", "mq", "ml")
MODEL = ("mb", "mq", "ml")
COLS = ("mb", "mq")
TEAM = ("sl", "ml")


def dot(left, right):
    return lax.dot_general(left, right, (((1,), (0,)), ((), ())), preferred_element_type=f32)


def dot_t(left, right):
    return lax.dot_general(left, right, (((1,), (1,)), ((), ())), preferred_element_type=f32)


def normalise(values):
    centred = values - jnp.mean(values, axis=-1, keepdims=True)
    inverse = lax.rsqrt(jnp.mean(centred * centred, axis=-1, keepdims=True) + norm_eps)
    return centred * inverse, inverse


def normalise_back(unit, inverse, grad_unit):
    mean_one = jnp.mean(grad_unit, axis=-1, keepdims=True)
    mean_two = jnp.mean(grad_unit * unit, axis=-1, keepdims=True)
    return inverse * (grad_unit - mean_one - unit * mean_two)


def sub_index():
    return lax.broadcasted_iota(jnp.int32, (SUBS, LANES), 0)


def spread(row):
    return jnp.broadcast_to(row, (SUBS, LANES))


def lane_tile(index):
    return slice(index * LANES, (index + 1) * LANES)


def no_state(tiles):
    rows = tiles[0, :SUBS, :]
    return rows - rows


def in_steps(steps, tile, rows):
    span = rows.shape[0] // SUBS

    def move(i, unused):
        steps[tile, pl.ds(pl.multiple_of(i * SUBS, SUBS), SUBS), :] = rows[
            pl.ds(i, SUBS, stride=span), :
        ]
        return unused

    lax.fori_loop(0, span, move, 0, unroll=8)


def from_steps(rows, steps, tile):
    span = rows.shape[0] // SUBS

    def move(i, unused):
        rows[pl.ds(i, SUBS, stride=span), :] = steps[
            tile, pl.ds(pl.multiple_of(i * SUBS, SUBS), SUBS), :
        ]
        return unused

    lax.fori_loop(0, span, move, 0, unroll=8)


def step_rows(i):
    return pl.ds(pl.multiple_of(i * SUBS, SUBS), SUBS)


def norm_kernel(
    place, x_ref, gain_ref, logr_ref, normed_ref, turned_ref, u_tiles, ends_ref, total_ref, rows
):
    unit, unused = normalise(x_ref[...].astype(f32))
    normed_ref[...] = (unit * gain_ref[...]).astype(bf16)
    turned_ref[...] = normed_ref[...].T
    tiles, length, unused = u_tiles.shape
    states = logr_ref.shape[0]
    span = length // SUBS
    for tile in range(tiles):
        start = place[0] * (tiles * LANES) + tile * LANES
        rows[...] = normed_ref[:, pl.ds(pl.multiple_of(start, LANES), LANES)].astype(f32)
        in_steps(u_tiles, tile, rows)
    left = ((SUBS - 1 - sub_index()) * span).astype(f32)
    for tile in range(tiles):
        rate = jnp.exp(logr_ref[:, lane_tile(tile)])
        decay = jnp.exp(-rate)
        decays = [spread(decay[n : n + 1]) for n in range(states)]

        def step(i, held):
            u = u_tiles[tile, step_rows(i), :]
            return tuple(d * h + u for d, h in zip(decays, held))

        zero = no_state(u_tiles)
        held = lax.fori_loop(0, span, step, (zero,) * states, unroll=4)
        for n in range(states):
            ends_ref[n, :, lane_tile(tile)] = held[n]
            total_ref[n : n + 1, lane_tile(tile)] = jnp.sum(
                held[n] * jnp.exp(-left * rate[n : n + 1]), axis=0, keepdims=True
            )


def context_kernel(
    place, u_tiles, ends_ref, all_ref, logr_ref, coef_ref, context_ref, y_tiles, rows
):
    tiles, length, unused = u_tiles.shape
    states = logr_ref.shape[0]
    span = length // SUBS
    index = sub_index()
    before = (index * span).astype(f32)
    for tile in range(tiles):
        rate = jnp.exp(logr_ref[:, lane_tile(tile)])
        decay = jnp.exp(-rate)
        scale = coef_ref[:, lane_tile(tile)] * jnp.sqrt(2.0 * rate)
        incoming = jnp.zeros((states, LANES), f32)
        for j in range(all_ref.shape[0]):
            gap = place[1] - 1 - j
            distance = (jnp.maximum(gap, 0) * length).astype(f32)
            term = jnp.exp(-distance * rate) * all_ref[j, :, lane_tile(tile)].astype(f32)
            incoming = incoming + jnp.where(gap >= 0, term, 0.0)
        for first in range(0, states, GROUP):
            chosen = range(first, first + GROUP)
            starts = []
            for n in chosen:
                row = rate[n : n + 1]
                run = ends_ref[n, :, lane_tile(tile)]
                for d in (1, 2, 4):
                    moved = jnp.exp(-(d * span) * row) * pltpu.roll(run, d, 0)
                    run = run + jnp.where(index >= d, moved, 0.0)
                run = jnp.where(index >= 1, pltpu.roll(run, 1, 0), 0.0)
                starts.append(run + jnp.exp(-before * row) * incoming[n : n + 1])
            decays = [spread(decay[n : n + 1]) for n in chosen]
            scales = [spread(scale[n : n + 1]) for n in chosen]

            def step(i, held):
                at = step_rows(i)
                u = u_tiles[tile, at, :]
                held = tuple(d * h + u for d, h in zip(decays, held))
                parts = [s * h for s, h in zip(scales, held)]
                if first > 0:
                    parts[0] = parts[0] + y_tiles[tile, at, :]
                while len(parts) > 1:
                    parts = [a + b for a, b in zip(parts[::2], parts[1::2])]
                y_tiles[tile, at, :] = parts[0]
                return held

            lax.fori_loop(0, span, step, tuple(starts), unroll=4)
        from_steps(rows, y_tiles, tile)
        context_ref[:, lane_tile(tile)] = rows[...].astype(bf16)


def whole_rows(block):
    return block.reshape(block.shape[0] * block.shape[1], block.shape[2])


def head(index):
    return slice(index * HD, (index + 1) * HD)


def weight_copies(pieces, buffer, place, sems, act):
    col_parts, row_parts = sems.shape
    for k in range(col_parts):
        for r in range(row_parts):
            inner = buffer.at[k, place[2] ^ r]
            act(pltpu.make_async_copy(pieces[k * row_parts + r], inner, sems.at[k, r]))


def of_heads(buffer, i):
    return jnp.concatenate([whole_rows(buffer[k, :, :, head(i)]) for k in range(buffer.shape[0])], axis=1)


def gradient_slot(row_parts, order, r):
    position = 0
    for bit in reversed(order):
        position = 2 * position + (1 if r & bit else 0)
    return position // (row_parts // 2), position % (row_parts // 2)


def round_orders(row_parts):
    bits = [1 << i for i in range(row_parts.bit_length() - 1)]
    return bits, bits[::-1]


def gradient_pieces(stacks, row_parts, far, slot):
    found = []
    for r in range(row_parts):
        sent, at = gradient_slot(row_parts, round_orders(row_parts)[far], r)
        found.append(stacks[2 * far + sent].at[at, slot])
    return found


def project_kernel(team, col_parts, row_parts, place, normed_ref, cot_ref, *refs):
    contexts, refs = refs[:team], refs[team:]
    count = col_parts * row_parts
    pieces, refs = refs[:count], refs[count:]
    context_t_ref, cot_t_ref, kept_ref = refs[:3]
    context_ref, weights, sems = refs[3:]
    weight_copies(pieces, weights, place, sems, lambda copy: copy.start())
    width = contexts[0].shape[1]
    for k in range(team):
        lanes = pl.ds(pl.multiple_of((place[0] ^ k) * width, LANES), width)
        context_ref[:, lanes] = contexts[k][...]
    context_t_ref[...] = context_ref[...].T
    cot_t_ref[...] = cot_ref[...].T
    weight_copies(pieces, weights, place, sems, lambda copy: copy.wait())
    kept_ref[0] = dot(normed_ref[...], of_heads(weights, 0)).astype(bf16)
    kept_ref[1] = dot(context_ref[...], of_heads(weights, 1)).astype(bf16)
    kept_ref[2] = dot(context_ref[...], of_heads(weights, 2)).astype(bf16)


def attend_kernel(team, col_parts, row_parts, place, kept_ref, *refs):
    count = col_parts * row_parts
    pieces, refs = refs[:count], refs[count:]
    part_ref, attended_ref, probs_ref, probs_t_ref, weights, sems = refs
    weight_copies(pieces, weights, place, sems, lambda copy: copy.start())
    length = kept_ref.shape[1]
    rows = lax.broadcasted_iota(jnp.int32, (length, length), 0)
    cols = lax.broadcasted_iota(jnp.int32, (length, length), 1)
    for h in range(col_parts):
        scores = dot_t(kept_ref[0, :, head(h)], kept_ref[1, :, head(h)]) * score_scale
        scores = jnp.where(rows >= cols, scores, -1e30)
        shifted = jnp.exp(scores - jnp.max(scores, axis=-1, keepdims=True))
        inverse = 1.0 / jnp.sum(shifted, axis=-1, keepdims=True)
        probs = (shifted * inverse).astype(bf16)
        probs_ref[h] = probs
        probs_t_ref[h] = probs.T
        attended_ref[:, head(h)] = dot(probs, kept_ref[2, :, head(h)]).astype(bf16)
    weight_copies(pieces, weights, place, sems, lambda copy: copy.wait())
    part_ref[...] = dot_t(attended_ref[...], of_heads(weights, 3)).astype(bf16)


def gelu_parts(hidden, grad_act):
    density = jnp.exp(-0.5 * hidden * hidden)
    t = 1.0 / (1.0 + (0.3275911 * math.sqrt(0.5)) * jnp.abs(hidden))
    series = 0.5 * 1.061405429
    for factor in (-1.453152027, 1.421413741, -0.284496736, 0.254829592):
        series = series * t + 0.5 * factor
    tail = series * t * density
    cdf = jnp.where(hidden >= 0.0, 1.0 - tail, tail)
    slope = cdf + hidden * density * (1.0 / math.sqrt(2.0 * math.pi))
    return (hidden * cdf).astype(bf16), (grad_act * slope).astype(bf16)


def middle_kernel(team, x_ref, gain_ref, *refs):
    parts, (middle_ref, normed_ref, normed_t_ref) = refs[:team], refs[team:]
    attn = parts[0][...].astype(f32)
    for part in parts[1:]:
        attn = attn + part[...].astype(f32)
    middle = x_ref[...].astype(f32) + attn
    middle_ref[...] = middle
    unit, unused = normalise(middle)
    normed_ref[...] = (unit * gain_ref[...]).astype(bf16)
    normed_t_ref[...] = normed_ref[...].T


def feed_kernel(col_parts, row_parts, place, normed_ref, normed_t_ref, cot_ref, cot_t_ref, *refs):
    arrays, refs = (refs[:row_parts], refs[row_parts : 2 * row_parts]), refs[2 * row_parts :]
    out_ref, two_ref = refs[:2]
    stacks, refs = (refs[2:6], refs[6:10]), refs[10:]
    up_all, down_all, grad_up, grad_down, activated_all, grad_all, sems = refs
    z = pl.program_id(0)
    half = col_parts // 2
    hidden_cols = grad_up.shape[3]

    def copies(k):
        found = []
        for r in range(row_parts):
            for which, buffer in enumerate((up_all, down_all)):
                outside = arrays[which][r].at[k]
                inside = buffer.at[place[2] ^ r, :, pl.ds(k * hidden_cols, hidden_cols)]
                found.append(pltpu.make_async_copy(outside, inside, sems.at[which, k, r]))
        return found

    def each_leaving(k, act):
        for which, buffer in enumerate((grad_up, grad_down)):
            steps = lax.rem(place[6] + col_parts - k, col_parts)
            for far in range(2):

                @pl.when(steps // half == far)
                def leaves():
                    slot = lax.rem(steps, half)
                    for r, piece in enumerate(gradient_pieces(stacks[which], row_parts, far, slot)):
                        inner = buffer.at[k, place[2] ^ r]
                        act(pltpu.make_async_copy(inner, piece, sems.at[2 + which, k, r]))

    @pl.when(z == 0)
    def start():
        for k in range(col_parts):
            for copy in copies(k):
                copy.start()

    for k in range(col_parts):

        @pl.when(z == k)
        def arrive():
            for copy in copies(k):
                copy.wait()

    at = pl.ds(pl.multiple_of(z * hidden_cols, hidden_cols), hidden_cols)
    hidden = dot(normed_ref[...], whole_rows(up_all[:, :, at]))
    grad_act = dot(cot_ref[...], whole_rows(down_all[:, :, at]))
    activated, grad_pre = gelu_parts(hidden, grad_act)
    activated_all[:, at] = activated
    grad_all[:, at] = grad_pre
    shape = grad_up.shape[1:]
    grad_up[z] = dot(normed_t_ref[...], grad_pre).astype(bf16).reshape(shape)
    grad_down[z] = dot(cot_t_ref[...], activated).astype(bf16).reshape(shape)

    for k in range(col_parts):

        @pl.when(z == k)
        def leave():
            each_leaving(k, lambda copy: copy.start())

    @pl.when(z == col_parts - 1)
    def finish():
        two_ref[...] = dot_t(grad_all[...], whole_rows(up_all[...])).astype(bf16)
        out_ref[...] = dot_t(activated_all[...], whole_rows(down_all[...])).astype(bf16)
        for k in range(col_parts):
            each_leaving(k, lambda copy: copy.wait())


def attend_back_kernel(team, col_parts, row_parts, place, middle_ref, gain_ref, cot_ref, *refs):
    parts, refs = refs[:team], refs[team:]
    late, refs = refs[:6], refs[6:]
    count = col_parts * row_parts
    pieces, refs = refs[:count], refs[count:]
    middle_grad_ref, gain_grad_ref, one_ref = refs[:3]
    refs = refs[3:]
    context_grads, refs = refs[:team], refs[team:]
    stacks, refs = refs[:4], refs[4:]
    weights, grads, low, grad_out, grad_q, grad_k, grad_v = refs[:7]
    held, (sems, out_sems, late_sems) = refs[7:13], refs[13:]
    normed_t_ref, context_t_ref, kept_ref, attended_ref, probs_ref, probs_t_ref = held
    half = col_parts // 2
    weight_copies(pieces, weights, place, sems, lambda copy: copy.start())
    late_copies = [
        pltpu.make_async_copy(outside, inside, late_sems.at[i])
        for i, (outside, inside) in enumerate(zip(late, held))
    ]
    for copy in late_copies:
        copy.start()
    own_rows = middle_ref.shape[0] // team
    grad_two = parts[0][...].astype(f32)
    for part in parts[1:]:
        grad_two = grad_two + part[...].astype(f32)
    unit, inverse = normalise(middle_ref[...])
    grad_gain = grad_two * unit
    rows = lax.broadcasted_iota(jnp.int32, grad_gain.shape, 0)
    first = place[0] * own_rows
    mine = (rows >= first) & (rows < first + own_rows)
    gain_grad_ref[...] = jnp.sum(jnp.where(mine, grad_gain, 0.0), axis=0, keepdims=True)
    grad = cot_ref[...].astype(f32) + normalise_back(unit, inverse, grad_two * gain_ref[...])
    low[...] = grad.astype(bf16)
    for k in range(team):

        @pl.when(place[0] == k)
        def own():
            middle_grad_ref[...] = grad[k * own_rows : (k + 1) * own_rows, :]

    weight_copies(pieces, weights, place, sems, lambda copy: copy.wait())
    for copy in late_copies:
        copy.wait()
    grad_out[...] = dot(low[...], of_heads(weights, 3)).astype(bf16)
    for h in range(col_parts):
        q, k, v = (kept_ref[i, :, head(h)] for i in range(3))
        grad_heads = grad_out[:, head(h)]
        grad_v[:, head(h)] = dot(probs_t_ref[h], grad_heads).astype(bf16)
        probs = probs_ref[h].astype(f32)
        grad_probs = dot_t(grad_heads, v)
        inner = jnp.sum(grad_probs * probs, axis=-1, keepdims=True)
        grad_scores = (probs * (grad_probs - inner)).astype(bf16)
        grad_q[:, head(h)] = (dot(grad_scores, k) * score_scale).astype(bf16)
        turned = dot_t(v, grad_heads) - inner.T
        turned = (probs_t_ref[h].astype(f32) * turned).astype(bf16)
        grad_k[:, head(h)] = (dot(turned, q) * score_scale).astype(bf16)
    shape = (*grads.shape[1:3], HD)

    def put(i, grad):
        for h in range(col_parts):
            grads[h, :, :, head(i)] = grad[:, head(h)].astype(bf16).reshape(shape)

    put(3, dot(low[...].T, attended_ref[...]))
    put(0, dot(normed_t_ref[...], grad_q[...]))
    put(1, dot(context_t_ref[...], grad_k[...]))
    put(2, dot(context_t_ref[...], grad_v[...]))
    copies = []
    for k in range(col_parts):
        for r, piece in enumerate(gradient_pieces(stacks, row_parts, k // half, k % half)):
            copies.append(pltpu.make_async_copy(grads.at[k, place[2] ^ r], piece, out_sems.at[k, r]))
    for copy in copies:
        copy.start()
    total = dot_t(grad_k[...], of_heads(weights, 1)) + dot_t(grad_v[...], of_heads(weights, 2))
    middle_total = total.astype(bf16)
    low[...] = middle_total
    width = context_grads[0].shape[1]
    for k in range(team):
        lanes = pl.ds(pl.multiple_of((place[0] ^ k) * width, LANES), width)
        context_grads[k][...] = low[:, lanes]
    one_ref[...] = dot_t(grad_q[...], of_heads(weights, 0)).astype(bf16)
    for copy in copies:
        copy.wait()


def adjoint_kernel(team, logr_ref, *refs):
    parts = refs[:team]
    g_tiles, ends_ref, total_ref, rows = refs[team:]
    grad = parts[0][...].astype(f32)
    for part in parts[1:]:
        grad = grad + part[...].astype(f32)
    grad = grad.astype(bf16).astype(f32)
    tiles, length, unused = g_tiles.shape
    states = logr_ref.shape[0]
    span = length // SUBS
    for tile in range(tiles):
        rows[...] = grad[:, lane_tile(tile)]
        in_steps(g_tiles, tile, rows)
    before = (sub_index() * span).astype(f32)
    for tile in range(tiles):
        rate = jnp.exp(logr_ref[:, lane_tile(tile)])
        decay = jnp.exp(-rate)
        for first in range(0, states, GROUP):
            chosen = range(first, first + GROUP)
            decays = [spread(decay[n : n + 1]) for n in chosen]

            def step(i, held):
                g = g_tiles[tile, step_rows(span - 1 - i), :]
                later = []
                for d, (b, w) in zip(decays, held):
                    shrunk = d * b
                    later.append((g + shrunk, d * w + shrunk))
                return tuple(later)

            zero = no_state(g_tiles)
            held = lax.fori_loop(0, span, step, ((zero, zero),) * GROUP, unroll=4)
            for n, (b, w) in zip(chosen, held):
                ends_ref[0, n, :, lane_tile(tile)] = b
                ends_ref[1, n, :, lane_tile(tile)] = w
                shrink = jnp.exp(-before * rate[n : n + 1])
                total_ref[0, n : n + 1, lane_tile(tile)] = jnp.sum(
                    shrink * b, axis=0, keepdims=True
                )
                total_ref[1, n : n + 1, lane_tile(tile)] = jnp.sum(
                    shrink * (w + before * b), axis=0, keepdims=True
                )


def context_back_kernel(
    team, place, g_tiles, u_tiles, ends_ref, all_ref, logr_ref, coef_ref, one_ref, *refs
):
    pieces = refs[:team]
    grad_ssm_ref, y_tiles, full, rows = refs[team:]
    tiles, length, unused = u_tiles.shape
    states = logr_ref.shape[0]
    span = length // SUBS
    width = tiles * LANES
    index = sub_index()
    after = ((SUBS - 1 - index) * span).astype(f32)
    full[...] = one_ref[...].astype(f32)
    group = GROUP
    for tile in range(tiles):
        lanes = lane_tile(tile)
        rate = jnp.exp(logr_ref[:, lanes])
        decay = jnp.exp(-rate)
        root = jnp.sqrt(2.0 * rate)
        scale = coef_ref[:, lanes] * root
        in_b = jnp.zeros((states, LANES), f32)
        in_w = jnp.zeros((states, LANES), f32)
        for j in range(all_ref.shape[0]):
            gap = j - place[1] - 1
            distance = (jnp.maximum(gap, 0) * length).astype(f32)
            shrink = jnp.exp(-distance * rate)
            b, w = all_ref[j, 0, :, lanes].astype(f32), all_ref[j, 1, :, lanes].astype(f32)
            in_b = in_b + jnp.where(gap >= 0, shrink * b, 0.0)
            in_w = in_w + jnp.where(gap >= 0, shrink * (w + distance * b), 0.0)
        for first in range(0, states, group):
            chosen = range(first, first + group)
            starts = []
            for n in chosen:
                row = rate[n : n + 1]
                b, w = ends_ref[0, n, :, lanes], ends_ref[1, n, :, lanes]
                for d in (1, 2, 4):
                    shrink = jnp.exp(-(d * span) * row)
                    next_b = pltpu.roll(b, SUBS - d, 0)
                    next_w = pltpu.roll(w, SUBS - d, 0)
                    inside = index < SUBS - d
                    b, w = (
                        b + jnp.where(inside, shrink * next_b, 0.0),
                        w + jnp.where(inside, shrink * (next_w + (d * span) * next_b), 0.0),
                    )
                inside = index < SUBS - 1
                b = jnp.where(inside, pltpu.roll(b, SUBS - 1, 0), 0.0)
                w = jnp.where(inside, pltpu.roll(w, SUBS - 1, 0), 0.0)
                shrink = jnp.exp(-after * row)
                b_row, w_row = in_b[n : n + 1], in_w[n : n + 1]
                b = b + shrink * b_row
                w = w + shrink * (w_row + after * b_row)
                zero = no_state(u_tiles)
                starts.append((b, w, zero, zero))
            decays = [spread(decay[n : n + 1]) for n in chosen]
            scales = [spread(scale[n : n + 1]) for n in chosen]

            def step(i, held):
                at = step_rows(span - 1 - i)
                g = g_tiles[tile, at, :]
                u = u_tiles[tile, at, :]
                later, parts = [], []
                for d, s, (b, w, sum_b, sum_w) in zip(decays, scales, held):
                    shrunk = d * b
                    w = d * w + shrunk
                    b = g + shrunk
                    later.append((b, w, sum_b + u * b, sum_w + u * w))
                    parts.append(s * b)
                while len(parts) > 1:
                    parts = [p + q for p, q in zip(parts[::2], parts[1::2])]
                if first > 0:
                    parts[0] = parts[0] + y_tiles[tile, at, :]
                y_tiles[tile, at, :] = parts[0]
                return tuple(later)

            held = lax.fori_loop(0, span, step, tuple(starts), unroll=2)
            for n, (unused_b, unused_w, sum_b, sum_w) in zip(chosen, held):
                sum_b = jnp.sum(sum_b, axis=0, keepdims=True)
                sum_w = jnp.sum(sum_w, axis=0, keepdims=True)
                row = slice(n, n + 1)
                grad_ssm_ref[0, row, lanes] = root[row] * sum_b
                grad_ssm_ref[1, row, lanes] = scale[row] * (0.5 * sum_b - rate[row] * sum_w)
        at_lanes = pl.ds(pl.multiple_of(place[0] * width + tile * LANES, LANES), LANES)
        from_steps(rows, y_tiles, tile)
        full[:, at_lanes] += rows[...].astype(bf16).astype(f32)
    count = pieces[0].shape[0]
    for k in range(team):
        at_rows = pl.ds(pl.multiple_of((place[0] ^ k) * count, count), count)
        pieces[k][...] = full[at_rows, :].astype(bf16)


def input_grad_kernel(team, place, x_ref, gain_ref, middle_grad_ref, *refs):
    parts, (out_ref, gain_grad_ref) = refs[:team], refs[team:]
    rows = out_ref.shape[0]
    at_rows = pl.ds(pl.multiple_of(place[0] * rows, rows), rows)
    grad_one = parts[0][...].astype(f32)
    for part in parts[1:]:
        grad_one = grad_one + part[...].astype(f32)
    unit, inverse = normalise(x_ref[at_rows, :].astype(f32))
    gain_grad_ref[...] = jnp.sum(grad_one * unit, axis=0, keepdims=True)
    back = normalise_back(unit, inverse, grad_one * gain_ref[...])
    out_ref[...] = (middle_grad_ref[...] + back).astype(bf16)


def assemble_kernel(halves, low_count, place, own_ref, *refs):
    others, out_ref = refs[:-1], refs[-1]
    count, rows, unused = own_ref.shape
    half = place[4]

    def put(value, sequence, which, member):
        at_rows = pl.ds(pl.multiple_of((which * low_count + member) * rows, rows), rows)
        out_ref[sequence, at_rows, :] = value.astype(out_ref.dtype)

    for sequence in range(count // (halves * low_count)):
        if halves == 1:
            for member in range(low_count):
                put(own_ref[sequence * low_count + member], sequence, 0, member)
        else:
            put(own_ref[sequence * halves + half], sequence, half, 0)
            put(others[0][sequence], sequence, 1 - half, 0)


def pack_kernel(halves, place, qkv_ref, out_ref, up_ref, down_ref, *refs):
    rows = up_ref.shape[0]
    heads, hidden = out_ref.shape[0] // halves, up_ref.shape[1] // halves
    for which in range(halves):
        side = place[4] if which == 0 else 1 - place[4]
        at_heads = pl.ds(pl.multiple_of(side * heads, LANES), heads)
        at_hidden = pl.ds(pl.multiple_of(side * hidden, LANES), hidden)
        if which == 0:
            head_ref, wide_ref, deep_ref = refs[:3]
        else:
            packed = refs[3]
            head_ref = packed.at[:, : 4 * heads]
            wide_ref = packed.at[:, 4 * heads : 4 * heads + hidden]
            deep_ref = packed.at[:, 4 * heads + hidden :]
        for i in range(3):
            head_ref[:, i * heads : (i + 1) * heads] = qkv_ref[i, :, at_heads].astype(bf16)
        head_ref[:, 3 * heads :] = out_ref[at_heads, :].T.astype(bf16)
        wide_ref[...] = up_ref[:, at_hidden].astype(bf16)
        deep_ref[...] = down_ref[at_hidden, :].T.astype(bf16)


def small_kernel(ssm_ref, gains_ref, out_ref):
    count = ssm_ref.shape[0]
    out_ref[:count, :] = ssm_ref[...]
    out_ref[count:, :] = gains_ref[...]


def lamb_moments(weight, grad_item, first_old, second_old):
    first_new = beta_first * first_old + (1.0 - beta_first) * grad_item
    second_new = beta_second * second_old + (1.0 - beta_second) * grad_item * grad_item
    direction = (
        first_new
        / (1.0 - beta_first**STEP)
        / (jnp.sqrt(second_new / (1.0 - beta_second**STEP)) + lamb_eps)
        + weight_decay * weight
    )
    return (first_new, second_new, direction)


def place_sums(sums_ref, sums):
    rows = lax.broadcasted_iota(jnp.int32, sums_ref.shape, 0)
    lanes = lax.broadcasted_iota(jnp.int32, sums_ref.shape, 1)
    found = jnp.zeros(sums_ref.shape, f32)
    for index, pair in sums.items():
        for row, value in enumerate(pair):
            found = jnp.where((rows == row) & (lanes == index), value, found)
    sums_ref[...] = found


def moments_kernel(halves, matrices, place, *refs):
    count = 1 + max(item[1] for item in matrices)
    grads, refs = [refs[halves * i : halves * (i + 1)] for i in range(count)], refs[halves * count :]
    arrays = len({(item[1], item[4] is None) for item in matrices})
    ins = [refs[3 * i : 3 * i + 3] for i in range(arrays)]
    outs = [refs[3 * (arrays + i) : 3 * (arrays + i) + 3] for i in range(arrays)]
    sums_ref = refs[6 * arrays]
    keys = []
    sums = {}
    for number, source, column, turned, stacked in matrices:
        key = (source, stacked is None)
        if key not in keys:
            keys.append(key)
        pick = (lambda ref: ref) if stacked is None else (lambda ref, i=stacked: ref.at[i])
        weight, first, second = (pick(ref) for ref in ins[keys.index(key)])
        news = [pick(ref) for ref in outs[keys.index(key)]]
        width = weight.shape[0 if turned else 1] // halves
        rows = weight.shape[1 if turned else 0]
        cols = slice(column * width, (column + 1) * width)
        total_weight = total_update = 0.0
        for which, grad_ref in enumerate(grads[source]):
            side = place[4] if which == 0 else 1 - place[4]
            at = pl.ds(pl.multiple_of(side * width, width), width)
            if which == 0:
                grad = grad_ref[pl.ds(pl.multiple_of(side * rows, rows), rows), cols].astype(f32)
            else:
                grad = grad_ref[:, cols].astype(f32)
            at = (at, slice(None)) if turned else (slice(None), at)
            grad = grad.T if turned else grad
            old = weight[at]
            found = lamb_moments(old, grad, first[at], second[at])
            for ref, value in zip(news, found):
                ref[at] = value
            total_weight = total_weight + jnp.sum(old * old)
            total_update = total_update + jnp.sum(found[2] * found[2])
        sums[number] = (total_weight, total_update)
    place_sums(sums_ref, sums)


def small_moments_kernel(numbers, grads_ref, *refs):
    ins, outs, sums_ref = (refs[:3], refs[3:6]), (refs[6:9], refs[9:12]), refs[12]
    states = (grads_ref.shape[0] - 2) // 2
    sums = {}
    for (weight, first, second), news, start, rows, first_number in (
        (ins[0], outs[0], 2 * states, 1, numbers[0]),
        (ins[1], outs[1], 0, states, numbers[1]),
    ):
        for i in range(2):
            grad = grads_ref[start + i * rows : start + (i + 1) * rows, :]
            at = slice(i * rows, (i + 1) * rows)
            found = lamb_moments(weight[at, :], grad, first[at, :], second[at, :])
            for ref, value in zip(news, found):
                ref[at, :] = value
            sums[first_number + i] = (
                jnp.sum(weight[at, :] * weight[at, :]),
                jnp.sum(found[2] * found[2]),
            )
    place_sums(sums_ref, sums)


def update_kernel(stacks, sums_ref, *refs):
    count = len(stacks)
    weights, directions, news = refs[:count], refs[count : 2 * count], refs[2 * count : 3 * count]
    norms = jnp.sqrt(jnp.sum(sums_ref[...], axis=0))
    refs[3 * count][...] = norms
    ratios = norms[0:1] / norms[1:2]
    lanes = lax.broadcasted_iota(jnp.int32, ratios.shape, 1)
    for numbers, weight, direction, new in zip(stacks, weights, directions, news):
        step = weight.shape[0] // len(numbers)
        for i, number in enumerate(numbers):
            ratio = jnp.sum(jnp.where(lanes == number, ratios, 0.0), axis=1, keepdims=True)
            at = slice(i * step, (i + 1) * step)
            scale = learn_rate * ratio.reshape((1,) * weight.ndim)
            new[at] = weight[at] - scale * direction[at]


def call(
    body, ins, outs, scratch=(), grid=None, in_specs=None, out_specs=None, time=1.0, after=(), token=False
):
    moved = sum(a.size * a.dtype.itemsize for a in list(ins) + list(outs))
    params = pltpu.CompilerParams(vmem_limit_bytes=VMEM_BYTES)
    cost = pl.CostEstimate(flops=int(time * 1.15e9), bytes_accessed=moved, transcendentals=0)
    whole = pl.BlockSpec(memory_space=pltpu.VMEM)
    anywhere = pl.BlockSpec(memory_space=pl.ANY)
    in_specs = list(in_specs or [whole] * len(ins)) + [anywhere] * len(after)
    out_specs = list(out_specs or [whole] * len(outs))
    outs = list(outs)
    first_out = len(ins) + len(after)
    last_out = first_out + len(outs)
    if token:
        outs.append(jax.ShapeDtypeStruct((SUBS, LANES), f32))
        out_specs.append(whole)

    def run(*refs):
        refs = list(refs)
        if token:
            refs[last_out][...] = jnp.zeros((SUBS, LANES), f32)
            del refs[last_out]
        body(*refs[: len(ins)], *refs[first_out:])

    return pl.pallas_call(
        run,
        out_shape=tuple(outs),
        in_specs=in_specs,
        out_specs=tuple(out_specs),
        scratch_shapes=list(scratch),
        compiler_params=params,
        cost_estimate=cost,
        **({} if grid is None else {"grid": grid}),
    )(*ins, *after)


def shaped(shape, kind):
    return jax.ShapeDtypeStruct(tuple(shape), kind)


def on_device(
    tokens,
    cotangent,
    w_qkv,
    w_out,
    w_up,
    w_down,
    norm_gains,
    ssm_param,
    first_qkv,
    second_qkv,
    first_out,
    second_out,
    first_up,
    second_up,
    first_down,
    second_down,
    first_gain,
    second_gain,
    first_ssm,
    second_ssm,
):
    halves = lax.axis_size("sl")
    low_count = lax.axis_size("ml")
    row_parts = lax.axis_size("sh")
    col_parts = lax.axis_size("mb") * lax.axis_size("mq")
    team = halves * low_count
    sl, ml, mb, mq = (lax.axis_index(name) for name in ("sl", "ml", "mb", "mq"))
    rank = sl * low_count + ml
    block_index = lax.axis_index("sh") * halves + mq
    seq_total, length, width = tokens.shape
    assert length == BLK and seq_total == lax.axis_size("mb")
    states = ssm_param.shape[1]
    channels = width // team
    tiles = channels // LANES
    row_count = width // row_parts
    own_rows = length // team
    place = [rank, block_index, lax.axis_index("sh"), lax.axis_index(MODEL), sl, sl ^ mq]
    place.append(lax.axis_index(COLS))
    place = jnp.stack(place).astype(jnp.int32)
    smem = pl.BlockSpec(memory_space=pltpu.SMEM)
    vmem = pl.BlockSpec(memory_space=pltpu.VMEM)

    def permute(value, axes, moves):
        return lax.ppermute(value, axes, moves)

    def swap(value):
        return permute(value, "sl", [(0, 1), (1, 0)])

    def in_order(own, other, axis):
        return jnp.where(
            sl == 0, jnp.concatenate([own, other], axis), jnp.concatenate([other, own], axis)
        )

    def team_send(pieces):
        moved = [pieces[0]]
        for k in range(1, team):
            moved.append(permute(pieces[k], TEAM, [(i, i ^ k) for i in range(team)]))
        return moved

    def pick_block(array):
        own = lax.dynamic_index_in_dim(array, mb, 0, keepdims=False)
        if halves == 1:
            return own, ()
        other = swap(own)
        return jnp.where(sl == mq, own, other), (other,)

    def across(value, bit):
        return permute(value, "sh", [(i, i ^ bit) for i in range(row_parts)])

    def along(value, axes, step):
        count = lax.axis_size(axes)
        return permute(value, axes, [(i, (i + step) % count) for i in range(count)])

    bits = [1 << i for i in range(row_parts.bit_length() - 1)]

    def bit_order(k):
        return bits if k % 2 == 0 else bits[::-1]

    def double_rows(value, order):
        found = {0: value}
        for bit in order:
            for r in list(found):
                found[r | bit] = across(found[r], bit)
        return [found[r] for r in range(row_parts)]

    def add(*items, zero=None):
        total = sum(item.astype(f32) for item in items)
        return (total if zero is None else total + zero[0, 0]).astype(bf16)

    def first_messages(stacks):
        return across(stacks[1], bits[-1]), across(stacks[3], bits[0])

    def halve_rows(keep, arrived, order, zero=None, last=None):
        items = [keep, arrived]
        for bit in order[-2::-1]:
            count = arrived.shape[0] // 2
            arrived = across(add(*[item[count:] for item in items], zero=zero), bit)
            items = [item[:count] for item in items] + [arrived]
        return add(*[item[0] for item in items], zero=last)

    def halve_both(stacks, first, zero=None, last=None):
        near = halve_rows(stacks[0], first[0], bits, zero, last)
        return near, halve_rows(stacks[2], first[1], bits[::-1], zero, last)

    def token_after(*arrays):
        return call(lambda: None, (), (), after=arrays, token=True)[0]

    def ring_gather(shard):
        pieces, held = [], shard
        for k in range(col_parts):
            if k > 0:
                held = along(held, COLS, 1)
            pieces.append(double_rows(held, bits if k % 2 == 0 else bits[::-1]))
        return pieces

    def sum_over_z(near, far):
        held = None
        for stack in (far, near):
            for k in reversed(range(stack.shape[0])):
                held = stack[k] if held is None else add(stack[k], along(held, COLS, -1))
        return held

    def everywhere(value, axes):
        count = lax.axis_size(axes)
        copies = jnp.broadcast_to(value[None], (count, *value.shape))
        return lax.all_to_all(copies, axes, 0, 0, tiled=True)

    rows_dev = w_up.shape[0]
    hidden_cols = w_up.shape[1] // halves
    head_cols = 4 * w_out.shape[0] // halves
    packed_cols = head_cols + 2 * hidden_cols
    sides = [shaped((rows_dev, cols), bf16) for cols in (head_cols, hidden_cols, hidden_cols)]
    shards = call(
        functools.partial(pack_kernel, halves),
        (place, w_qkv, w_out, w_up, w_down),
        sides + [shaped((rows_dev, packed_cols), bf16)] * (halves - 1),
        time=2.4,
        in_specs=[smem] + [vmem] * 4,
    )
    if halves == 2:
        other = swap(shards[3])
        cuts = (0, head_cols, head_cols + hidden_cols, packed_cols)
        shards = [
            in_order(own, other[:, first:last], 0)
            for own, first, last in zip(shards, cuts, cuts[1:])
        ]
    head_shard, up_shard, down_shard = shards[:3]
    attn_w = ring_gather(head_shard)
    up_full = lax.all_gather(up_shard, COLS, axis=0, tiled=False)
    down_full = lax.all_gather(down_shard, COLS, axis=0, tiled=False)
    up_w = double_rows(up_full, bits)
    down_w = double_rows(down_full, bits[::-1])
    attn_flat = [piece for group in attn_w for piece in group]

    small, = call(
        small_kernel,
        (ssm_param.reshape(2 * states, -1), norm_gains),
        (shaped((2 * states + 2, norm_gains.shape[1]), f32),),
        after=(*attn_w[0][1:-1], attn_w[1][0]),
    )
    small = jnp.transpose(everywhere(small, ALL), (1, 0, 2)).reshape(2 * states + 2, width)
    own_ssm = lax.dynamic_slice_in_dim(
        small[: 2 * states].reshape(2, states, width), rank * channels, channels, 2
    )
    coef, logr = own_ssm[0], own_ssm[1]
    gain_one = small[2 * states : 2 * states + 1]
    gain_two = small[2 * states + 1 : 2 * states + 2]

    x, unused = pick_block(tokens)
    cot, cot_other = pick_block(cotangent)

    anywhere = [pl.BlockSpec(memory_space=pl.ANY)]

    def fixed(*shape):
        return pl.BlockSpec(shape, lambda z: (0,) * len(shape))

    wide = fixed(length, width)
    row = fixed(1, width)

    normed_one, normed_t, u_steps, ends, total = call(
        norm_kernel,
        (place, x, gain_one, logr),
        (
            shaped((length, width), bf16),
            shaped((width, length), bf16),
            shaped((tiles, length, LANES), f32),
            shaped((states, SUBS, channels), f32),
            shaped((states, channels), f32),
        ),
        scratch=[pltpu.VMEM((length, LANES), f32)],
        in_specs=[smem, vmem, vmem, vmem],
        after=(attn_w[0][-1], *attn_w[1][1:-1], attn_w[-1][0], up_full, *cot_other),
        time=5,
    )
    totals = everywhere(total.astype(bf16), ("sh", "mq"))
    (context_own,) = call(
        context_kernel,
        (place, u_steps, ends, totals, logr, coef),
        (shaped((length, channels), bf16),),
        after=(*attn_w[-1][1:], *up_w[1:-1]),
        scratch=[pltpu.VMEM((tiles, length, LANES), f32), pltpu.VMEM((length, LANES), f32)],
        in_specs=[smem] + [vmem] * 5,
        time=7,
    )
    contexts = team_send([context_own] * team)

    stack_shape = (row_parts // 2, col_parts // 2, row_count)
    head_stacks = [shaped((*stack_shape, head_cols), bf16)] * 4
    hidden_stacks = [shaped((*stack_shape, hidden_cols), bf16)] * 8
    sizes = (team, col_parts, row_parts)
    head_buffer = pltpu.VMEM((col_parts, row_parts, row_count, 4 * HD), bf16)
    head_sems = pltpu.SemaphoreType.DMA((col_parts, row_parts))
    kept_shape = shaped((3, length, col_parts * HD), bf16)
    flat_shape = shaped((length, col_parts * HD), bf16)
    context_t, cot_t, kept = call(
        functools.partial(project_kernel, *sizes),
        (place, normed_one, cot, *contexts, *attn_flat),
        (shaped((width, length), bf16), shaped((width, length), bf16), kept_shape),
        scratch=[pltpu.VMEM((length, width), bf16), head_buffer, head_sems],
        time=1,
        in_specs=[smem] + [vmem] * (2 + team) + anywhere * len(attn_flat),
        after=down_w[1:-1],
    )
    attn_part, attended, probs, probs_t = call(
        functools.partial(attend_kernel, *sizes),
        (place, kept, *attn_flat),
        (
            shaped((length, width), bf16),
            flat_shape,
            *[shaped((col_parts, length, length), bf16)] * 2,
        ),
        scratch=[head_buffer, head_sems],
        time=1,
        in_specs=[smem, vmem] + anywhere * len(attn_flat),
        after=up_w[-1:],
    )
    attn_parts = team_send([attn_part] * team)

    middle, normed_two, normed_two_t = call(
        functools.partial(middle_kernel, team),
        (x, gain_two, *attn_parts),
        (shaped((length, width), f32), shaped((length, width), bf16), shaped((width, length), bf16)),
        time=1,
    )
    weight_buffer = pltpu.VMEM((row_parts, row_count, col_parts * hidden_cols), bf16)
    grad_buffer = pltpu.VMEM((col_parts, row_parts, row_count, hidden_cols), bf16)
    out_part, two_part, *hidden_grads = call(
        functools.partial(feed_kernel, col_parts, row_parts),
        (place, normed_two, normed_two_t, cot, cot_t, *up_w, *down_w),
        (shaped((length, width), bf16), shaped((length, width), bf16), *hidden_stacks),
        scratch=[
            *[weight_buffer] * 2,
            *[grad_buffer] * 2,
            *[pltpu.VMEM((length, col_parts * hidden_cols), bf16)] * 2,
            pltpu.SemaphoreType.DMA((4, col_parts, row_parts)),
        ],
        time=18,
        grid=(col_parts,),
        in_specs=[smem, wide, fixed(width, length), wide, fixed(width, length)]
        + anywhere * (2 * row_parts),
        out_specs=[wide, wide] + anywhere * 8,
    )
    two_parts = team_send([two_part] * team)

    def rows_of(array, member):
        return lax.dynamic_slice_in_dim(array, member * own_rows, own_rows, 0)

    def share_rows(pieces, kind):
        others = []
        if halves == 2:
            pairs = pieces.reshape(seq_total, halves, own_rows, width)
            others = [swap(lax.dynamic_index_in_dim(pairs, 1 - sl, 1, keepdims=False))]
        (blocks,) = call(
            functools.partial(assemble_kernel, halves, low_count),
            (place, pieces, *others),
            (shaped((seq_total, length, width), kind),),
            time=3.5,
            in_specs=[smem, vmem] + [vmem] * len(others),
        )
        return blocks

    out_pieces = team_send([rows_of(out_part, rank ^ k) for k in range(team)])
    result = rows_of(middle, rank) + sum(item.astype(f32) for item in out_pieces)
    result = result.astype(bf16)
    layer_pieces = lax.all_gather(result, MODEL, axis=0, tiled=False)
    layer_out = share_rows(layer_pieces, bf16)

    def both_halves(own):
        if halves == 1:
            return [own]
        return [own, swap(lax.dynamic_slice_in_dim(own, (1 - sl) * rows_dev, rows_dev, 0))]

    middle_grad, gain_two_grad, one_part, *rest = call(
        functools.partial(attend_back_kernel, *sizes),
        (place, middle, gain_two, cot, *two_parts, normed_t, context_t, kept, attended, probs, probs_t, *attn_flat),
        (
            shaped((own_rows, width), f32),
            shaped((1, width), f32),
            shaped((length, width), bf16),
            *[shaped((length, channels), bf16)] * team,
            *head_stacks,
        ),
        scratch=[
            head_buffer,
            head_buffer,
            pltpu.VMEM((length, width), bf16),
            *[pltpu.VMEM((length, col_parts * HD), bf16)] * 4,
            *[pltpu.VMEM((width, length), bf16)] * 2,
            pltpu.VMEM(kept_shape.shape, bf16),
            pltpu.VMEM(flat_shape.shape, bf16),
            *[pltpu.VMEM((col_parts, length, length), bf16)] * 2,
            head_sems,
            head_sems,
            pltpu.SemaphoreType.DMA((6,)),
        ],
        in_specs=[smem] + [vmem] * (3 + team) + anywhere * (6 + len(attn_flat)),
        out_specs=[vmem] * (3 + team) + anywhere * 4,
        time=1,
        after=(result,),
    )
    context_grads = team_send(rest[:team])
    down_first = first_messages(hidden_grads[4:])
    up_first = first_messages(hidden_grads[:4])
    g_steps, adjoint_ends, adjoint_total = call(
        functools.partial(adjoint_kernel, team),
        (logr, *context_grads),
        (
            shaped((tiles, length, LANES), f32),
            shaped((2, states, SUBS, channels), f32),
            shaped((2, states, channels), f32),
        ),
        scratch=[pltpu.VMEM((length, LANES), f32)],
        time=1,
        after=down_first,
    )
    adjoint_totals = everywhere(adjoint_total.astype(bf16), ("sh", "mq"))
    head_first = first_messages(rest[team:])
    *one_pieces, grad_ssm = call(
        functools.partial(context_back_kernel, team),
        (place, g_steps, u_steps, adjoint_ends, adjoint_totals, logr, coef, one_part),
        (
            *[shaped((own_rows, width), bf16)] * team,
            shaped((2, states, channels), f32),
        ),
        scratch=[
            pltpu.VMEM((tiles, length, LANES), f32),
            pltpu.VMEM((length, width), f32),
            pltpu.VMEM((length, LANES), f32),
        ],
        in_specs=[smem] + [vmem] * 7,
        time=1,
        after=up_first,
    )
    one_pieces = team_send(one_pieces)
    grad_rows, gain_one_grad, rows_done = call(
        functools.partial(input_grad_kernel, team),
        (place, x, gain_one, middle_grad, *one_pieces),
        (shaped((own_rows, width), bf16), shaped((1, width), f32)),
        in_specs=[smem] + [vmem] * (3 + team),
        time=1,
        after=(layer_pieces, *head_first),
        token=True,
    )
    grad_down = sum_over_z(*halve_both(hidden_grads[4:], down_first, rows_done))
    head_sums = halve_both(rest[team:], head_first, rows_done)
    grad_up = sum_over_z(*halve_both(hidden_grads[:4], up_first, rows_done))
    grad_heads = sum_over_z(*head_sums)
    input_grad = share_rows(lax.all_gather(grad_rows, MODEL, axis=0, tiled=False), f32)

    placed_ssm = lax.dynamic_update_slice_in_dim(
        jnp.zeros((2 * states, width), f32),
        grad_ssm.reshape(2 * states, channels),
        rank * channels,
        1,
    )
    small_grads = jnp.concatenate([placed_ssm, gain_one_grad, gain_two_grad], 0)
    small_grads = small_grads.reshape(2 * states + 2, lax.axis_size(ALL), -1)
    small_grads = lax.all_to_all(jnp.transpose(small_grads, (1, 0, 2)), ALL, 0, 0, tiled=True)
    small_grads = jnp.sum(small_grads, axis=0)

    def moments(matrices, grads, arrays):
        changed = [shaped(old.shape, f32) for group in arrays for old in group]
        grad_parts = [part for grad in grads for part in both_halves(grad)]
        ins = [item for group in arrays for item in group]
        *found, sums = call(
            functools.partial(moments_kernel, halves, matrices),
            (place, *grad_parts, *ins),
            (*changed, shaped((2, LANES), f32)),
            in_specs=[smem] + [vmem] * (len(grad_parts) + len(ins)),
            time=4,
        )
        return [found[3 * i : 3 * i + 3] for i in range(len(arrays))], sums

    hidden_new, hidden_sums = moments(
        ((4, 0, 0, False, None), (5, 1, 0, True, None)),
        (grad_up, grad_down),
        ((w_up, first_up, second_up), (w_down, first_down, second_down)),
    )
    heads_new, head_sums = moments(
        tuple((i, 0, i, False, i) for i in range(3)) + ((3, 0, 3, True, None),),
        (grad_heads,),
        ((w_qkv, first_qkv, second_qkv), (w_out, first_out, second_out)),
    )
    own_channels = norm_gains.shape[1]
    ssm_items = [item.reshape(2 * states, own_channels) for item in (ssm_param, first_ssm, second_ssm)]
    small_items = [norm_gains, first_gain, second_gain, *ssm_items]
    *small_new, small_sums = call(
        functools.partial(small_moments_kernel, (6, 8)),
        (small_grads.reshape(2 * states + 2, own_channels), *small_items),
        (*[shaped(item.shape, f32) for item in small_items], shaped((2, LANES), f32)),
    )
    all_sums = everywhere(hidden_sums + head_sums + small_sums, ALL)
    masters = (w_qkv, w_out, w_up, w_down, norm_gains, ssm_items[0])
    news = (*heads_new, *hidden_new, small_new[:3], small_new[3:])
    *weights, norms = call(
        functools.partial(update_kernel, ((0, 1, 2), (3,), (4,), (5,), (6, 7), (8, 9))),
        (all_sums, *masters, *[group[2] for group in news]),
        (*[shaped(item.shape, f32) for item in masters], shaped((2, LANES), f32)),
        time=3.2,
    )
    outputs = [layer_out, input_grad]
    for index, (weight, (first_new, second_new, unused)) in enumerate(zip(weights, news)):
        if index == 4:
            outputs += [weight, first_new, second_new[0], second_new[1]]
        else:
            kept_shape = ssm_param.shape if index == 5 else weight.shape
            outputs += [item.reshape(kept_shape) for item in (weight, first_new, second_new)]
    outputs.append(norms[:, :10])
    return tuple(outputs)


def solution(mesh):
    seq_count, model_count = mesh.shape["seq"], mesh.shape["mp"]
    halves = 2 if HEADS // model_count >= 2 else 1
    sizes = (seq_count // halves, halves, SEQS, halves, model_count // (SEQS * halves))
    fine = Mesh(mesh.devices.reshape(sizes), ALL)
    seq, model = ("sh", "sl"), ("mb", "mq", "ml")
    rows_cols, cols_rows = P(seq, model), P(model, seq)
    token = P(None, seq, None)
    stack = P(None, seq, model)
    gains = P(None, ALL)
    ssm = P(None, None, ALL)
    return jax.shard_map(
        on_device,
        mesh=fine,
        in_specs=(token, token, stack, cols_rows, rows_cols, cols_rows, gains, ssm)
        + (stack,) * 2
        + (cols_rows,) * 2
        + (rows_cols,) * 2
        + (cols_rows,) * 2
        + (gains,) * 2
        + (ssm,) * 2,
        out_specs=(token, token)
        + (stack,) * 3
        + (cols_rows,) * 3
        + (rows_cols,) * 3
        + (cols_rows,) * 3
        + (gains, gains, P(ALL), P(ALL))
        + (ssm,) * 3
        + (P(),),
        check_vma=False,
    )
```

```python
import functools
import math

import jax
import jax.numpy as jnp
from jax import lax
from jax.experimental import pallas as pl
from jax.experimental.pallas import tpu as pltpu
from jax.sharding import Mesh
from jax.sharding import PartitionSpec as P

HD = 128
HEADS = 8
BLK = 512
STEP = 10
SEQS = 2
LANES = 128
SUBS = 8
GROUP = 8

norm_eps = 1e-05
beta_first = 0.9
beta_second = 0.999
lamb_eps = 1e-06
weight_decay = 0.01
learn_rate = 0.5
score_scale = HD ** (-0.5)

f32 = jnp.float32
bf16 = jnp.bfloat16
VMEM_BYTES = 56 * 1024 * 1024

ALL = ("sh", "sl", "mb", "mq", "ml")
MODEL = ("mb", "mq", "ml")
COLS = ("mb", "mq")
TEAM = ("sl", "ml")


def dot(left, right):
    return lax.dot_general(left, right, (((1,), (0,)), ((), ())), preferred_element_type=f32)


def dot_t(left, right):
    return lax.dot_general(left, right, (((1,), (1,)), ((), ())), preferred_element_type=f32)


def normalise(values):
    centred = values - jnp.mean(values, axis=-1, keepdims=True)
    inverse = lax.rsqrt(jnp.mean(centred * centred, axis=-1, keepdims=True) + norm_eps)
    return centred * inverse, inverse


def normalise_back(unit, inverse, grad_unit):
    mean_one = jnp.mean(grad_unit, axis=-1, keepdims=True)
    mean_two = jnp.mean(grad_unit * unit, axis=-1, keepdims=True)
    return inverse * (grad_unit - mean_one - unit * mean_two)


def sub_index():
    return lax.broadcasted_iota(jnp.int32, (SUBS, LANES), 0)


def spread(row):
    return jnp.broadcast_to(row, (SUBS, LANES))


def lane_tile(index):
    return slice(index * LANES, (index + 1) * LANES)


def no_state(tiles):
    rows = tiles[0, :SUBS, :]
    return rows - rows


def in_steps(steps, tile, rows):
    span = rows.shape[0] // SUBS

    def move(i, unused):
        steps[tile, pl.ds(pl.multiple_of(i * SUBS, SUBS), SUBS), :] = rows[
            pl.ds(i, SUBS, stride=span), :
        ]
        return unused

    lax.fori_loop(0, span, move, 0, unroll=8)


def from_steps(rows, steps, tile):
    span = rows.shape[0] // SUBS

    def move(i, unused):
        rows[pl.ds(i, SUBS, stride=span), :] = steps[
            tile, pl.ds(pl.multiple_of(i * SUBS, SUBS), SUBS), :
        ]
        return unused

    lax.fori_loop(0, span, move, 0, unroll=8)


def step_rows(i):
    return pl.ds(pl.multiple_of(i * SUBS, SUBS), SUBS)


def norm_kernel(
    place, x_ref, gain_ref, logr_ref, normed_ref, turned_ref, u_tiles, ends_ref, total_ref, rows
):
    unit, unused = normalise(x_ref[...].astype(f32))
    normed_ref[...] = (unit * gain_ref[...]).astype(bf16)
    turned_ref[...] = normed_ref[...].T
    tiles, length, unused = u_tiles.shape
    states = logr_ref.shape[0]
    span = length // SUBS
    for tile in range(tiles):
        start = place[0] * (tiles * LANES) + tile * LANES
        rows[...] = normed_ref[:, pl.ds(pl.multiple_of(start, LANES), LANES)].astype(f32)
        in_steps(u_tiles, tile, rows)
    left = ((SUBS - 1 - sub_index()) * span).astype(f32)
    for tile in range(tiles):
        rate = jnp.exp(logr_ref[:, lane_tile(tile)])
        decay = jnp.exp(-rate)
        decays = [spread(decay[n : n + 1]) for n in range(states)]

        def step(i, held):
            u = u_tiles[tile, step_rows(i), :]
            return tuple(d * h + u for d, h in zip(decays, held))

        zero = no_state(u_tiles)
        held = lax.fori_loop(0, span, step, (zero,) * states, unroll=4)
        for n in range(states):
            ends_ref[n, :, lane_tile(tile)] = held[n]
            total_ref[n : n + 1, lane_tile(tile)] = jnp.sum(
                held[n] * jnp.exp(-left * rate[n : n + 1]), axis=0, keepdims=True
            )


def context_kernel(
    place, u_tiles, ends_ref, all_ref, logr_ref, coef_ref, context_ref, y_tiles, rows
):
    tiles, length, unused = u_tiles.shape
    states = logr_ref.shape[0]
    span = length // SUBS
    index = sub_index()
    before = (index * span).astype(f32)
    for tile in range(tiles):
        rate = jnp.exp(logr_ref[:, lane_tile(tile)])
        decay = jnp.exp(-rate)
        scale = coef_ref[:, lane_tile(tile)] * jnp.sqrt(2.0 * rate)
        incoming = jnp.zeros((states, LANES), f32)
        for j in range(all_ref.shape[0]):
            gap = place[1] - 1 - j
            distance = (jnp.maximum(gap, 0) * length).astype(f32)
            term = jnp.exp(-distance * rate) * all_ref[j, :, lane_tile(tile)].astype(f32)
            incoming = incoming + jnp.where(gap >= 0, term, 0.0)
        for first in range(0, states, GROUP):
            chosen = range(first, first + GROUP)
            starts = []
            for n in chosen:
                row = rate[n : n + 1]
                run = ends_ref[n, :, lane_tile(tile)]
                for d in (1, 2, 4):
                    moved = jnp.exp(-(d * span) * row) * pltpu.roll(run, d, 0)
                    run = run + jnp.where(index >= d, moved, 0.0)
                run = jnp.where(index >= 1, pltpu.roll(run, 1, 0), 0.0)
                starts.append(run + jnp.exp(-before * row) * incoming[n : n + 1])
            decays = [spread(decay[n : n + 1]) for n in chosen]
            scales = [spread(scale[n : n + 1]) for n in chosen]

            def step(i, held):
                at = step_rows(i)
                u = u_tiles[tile, at, :]
                held = tuple(d * h + u for d, h in zip(decays, held))
                parts = [s * h for s, h in zip(scales, held)]
                if first > 0:
                    parts[0] = parts[0] + y_tiles[tile, at, :]
                while len(parts) > 1:
                    parts = [a + b for a, b in zip(parts[::2], parts[1::2])]
                y_tiles[tile, at, :] = parts[0]
                return held

            lax.fori_loop(0, span, step, tuple(starts), unroll=4)
        from_steps(rows, y_tiles, tile)
        context_ref[:, lane_tile(tile)] = rows[...].astype(bf16)


def whole_rows(block):
    return block.reshape(block.shape[0] * block.shape[1], block.shape[2])


def head(index):
    return slice(index * HD, (index + 1) * HD)


def weight_copies(pieces, buffer, place, sems, act):
    col_parts, row_parts = sems.shape
    for k in range(col_parts):
        for r in range(row_parts):
            inner = buffer.at[k, place[2] ^ r]
            act(pltpu.make_async_copy(pieces[k * row_parts + r], inner, sems.at[k, r]))


def of_heads(buffer, i):
    return jnp.concatenate([whole_rows(buffer[k, :, :, head(i)]) for k in range(buffer.shape[0])], axis=1)


def gradient_slot(row_parts, order, r):
    position = 0
    for bit in reversed(order):
        position = 2 * position + (1 if r & bit else 0)
    return position // (row_parts // 2), position % (row_parts // 2)


def round_orders(row_parts):
    bits = [1 << i for i in range(row_parts.bit_length() - 1)]
    return bits, bits[::-1]


def gradient_pieces(stacks, row_parts, far, slot):
    found = []
    for r in range(row_parts):
        sent, at = gradient_slot(row_parts, round_orders(row_parts)[far], r)
        found.append(stacks[2 * far + sent].at[at, slot])
    return found


def project_kernel(team, col_parts, row_parts, place, normed_ref, cot_ref, *refs):
    contexts, refs = refs[:team], refs[team:]
    count = col_parts * row_parts
    pieces, refs = refs[:count], refs[count:]
    context_t_ref, cot_t_ref, kept_ref = refs[:3]
    context_ref, weights, sems = refs[3:]
    weight_copies(pieces, weights, place, sems, lambda copy: copy.start())
    width = contexts[0].shape[1]
    for k in range(team):
        lanes = pl.ds(pl.multiple_of((place[0] ^ k) * width, LANES), width)
        context_ref[:, lanes] = contexts[k][...]
    context_t_ref[...] = context_ref[...].T
    cot_t_ref[...] = cot_ref[...].T
    weight_copies(pieces, weights, place, sems, lambda copy: copy.wait())
    kept_ref[0] = dot(normed_ref[...], of_heads(weights, 0)).astype(bf16)
    kept_ref[1] = dot(context_ref[...], of_heads(weights, 1)).astype(bf16)
    kept_ref[2] = dot(context_ref[...], of_heads(weights, 2)).astype(bf16)


def attend_kernel(team, col_parts, row_parts, place, kept_ref, *refs):
    count = col_parts * row_parts
    pieces, refs = refs[:count], refs[count:]
    part_ref, attended_ref, probs_ref, probs_t_ref, weights, sems = refs
    weight_copies(pieces, weights, place, sems, lambda copy: copy.start())
    length = kept_ref.shape[1]
    rows = lax.broadcasted_iota(jnp.int32, (length, length), 0)
    cols = lax.broadcasted_iota(jnp.int32, (length, length), 1)
    for h in range(col_parts):
        scores = dot_t(kept_ref[0, :, head(h)], kept_ref[1, :, head(h)]) * score_scale
        scores = jnp.where(rows >= cols, scores, -1e30)
        shifted = jnp.exp(scores - jnp.max(scores, axis=-1, keepdims=True))
        inverse = 1.0 / jnp.sum(shifted, axis=-1, keepdims=True)
        probs = (shifted * inverse).astype(bf16)
        probs_ref[h] = probs
        probs_t_ref[h] = probs.T
        attended_ref[:, head(h)] = dot(probs, kept_ref[2, :, head(h)]).astype(bf16)
    weight_copies(pieces, weights, place, sems, lambda copy: copy.wait())
    part_ref[...] = dot_t(attended_ref[...], of_heads(weights, 3)).astype(bf16)


def gelu_parts(hidden, grad_act):
    density = jnp.exp(-0.5 * hidden * hidden)
    t = 1.0 / (1.0 + (0.3275911 * math.sqrt(0.5)) * jnp.abs(hidden))
    series = 0.5 * 1.061405429
    for factor in (-1.453152027, 1.421413741, -0.284496736, 0.254829592):
        series = series * t + 0.5 * factor
    tail = series * t * density
    cdf = jnp.where(hidden >= 0.0, 1.0 - tail, tail)
    slope = cdf + hidden * density * (1.0 / math.sqrt(2.0 * math.pi))
    return (hidden * cdf).astype(bf16), (grad_act * slope).astype(bf16)


def middle_kernel(team, x_ref, gain_ref, *refs):
    parts, (middle_ref, normed_ref, normed_t_ref) = refs[:team], refs[team:]
    attn = parts[0][...].astype(f32)
    for part in parts[1:]:
        attn = attn + part[...].astype(f32)
    middle = x_ref[...].astype(f32) + attn
    middle_ref[...] = middle
    unit, unused = normalise(middle)
    normed_ref[...] = (unit * gain_ref[...]).astype(bf16)
    normed_t_ref[...] = normed_ref[...].T


def feed_kernel(team, col_parts, row_parts, place, normed_ref, normed_t_ref, cot_ref, cot_t_ref, *refs):
    arrays, refs = (refs[:row_parts], refs[row_parts : 2 * row_parts]), refs[2 * row_parts :]
    outs, two_ref, refs = refs[:team], refs[team], refs[team + 1 :]
    stacks, refs = (refs[:4], refs[4:8]), refs[8:]
    up_all, down_all, grad_up, grad_down, activated_all, grad_all, sems = refs
    z = pl.program_id(0)
    half = col_parts // 2
    hidden_cols = grad_up.shape[3]

    def copies(k):
        found = []
        for r in range(row_parts):
            for which, buffer in enumerate((up_all, down_all)):
                outside = arrays[which][r].at[k]
                inside = buffer.at[place[2] ^ r, :, pl.ds(k * hidden_cols, hidden_cols)]
                found.append(pltpu.make_async_copy(outside, inside, sems.at[which, k, r]))
        return found

    def each_leaving(k, act):
        for which, buffer in enumerate((grad_up, grad_down)):
            steps = lax.rem(place[6] + col_parts - k, col_parts)
            for far in range(2):

                @pl.when(steps // half == far)
                def leaves():
                    slot = lax.rem(steps, half)
                    for r, piece in enumerate(gradient_pieces(stacks[which], row_parts, far, slot)):
                        inner = buffer.at[k, place[2] ^ r]
                        act(pltpu.make_async_copy(inner, piece, sems.at[2 + which, k, r]))

    @pl.when(z == 0)
    def start():
        for k in range(col_parts):
            for copy in copies(k):
                copy.start()

    for k in range(col_parts):

        @pl.when(z == k)
        def arrive():
            for copy in copies(k):
                copy.wait()

    at = pl.ds(pl.multiple_of(z * hidden_cols, hidden_cols), hidden_cols)
    hidden = dot(normed_ref[...], whole_rows(up_all[:, :, at]))
    grad_act = dot(cot_ref[...], whole_rows(down_all[:, :, at]))
    activated, grad_pre = gelu_parts(hidden, grad_act)
    activated_all[:, at] = activated
    grad_all[:, at] = grad_pre
    shape = grad_up.shape[1:]
    grad_up[z] = dot(normed_t_ref[...], grad_pre).astype(bf16).reshape(shape)
    grad_down[z] = dot(cot_t_ref[...], activated).astype(bf16).reshape(shape)

    for k in range(col_parts):

        @pl.when(z == k)
        def leave():
            each_leaving(k, lambda copy: copy.start())

    @pl.when(z == col_parts - 1)
    def finish():
        two_ref[...] = dot_t(grad_all[...], whole_rows(up_all[...])).astype(bf16)
        rows = outs[0].shape[0]
        for k in range(team):
            at_rows = pl.ds(pl.multiple_of((place[0] ^ k) * rows, rows), rows)
            outs[k][...] = dot_t(activated_all[at_rows, :], whole_rows(down_all[...])).astype(bf16)
        for k in range(col_parts):
            each_leaving(k, lambda copy: copy.wait())


def attend_back_kernel(team, col_parts, row_parts, place, middle_ref, gain_ref, cot_ref, *refs):
    parts, refs = refs[:team], refs[team:]
    late, refs = refs[:3], refs[3:]
    count = col_parts * row_parts
    pieces, refs = refs[:count], refs[count:]
    middle_grad_ref, gain_grad_ref, one_ref, low = refs[:4]
    grad_q, grad_k, grad_v = refs[4:7]
    context_grads, refs = refs[7 : 7 + team], refs[7 + team :]
    weights, grad_out, total_low = refs[:3]
    held, (sems, late_sems) = refs[3:6], refs[6:]
    kept_ref, probs_ref, probs_t_ref = held
    weight_copies(pieces, weights, place, sems, lambda copy: copy.start())
    late_copies = [
        pltpu.make_async_copy(outside, inside, late_sems.at[i])
        for i, (outside, inside) in enumerate(zip(late, held))
    ]
    for copy in late_copies:
        copy.start()
    own_rows = middle_ref.shape[0] // team
    grad_two = parts[0][...].astype(f32)
    for part in parts[1:]:
        grad_two = grad_two + part[...].astype(f32)
    unit, inverse = normalise(middle_ref[...])
    grad_gain = grad_two * unit
    rows = lax.broadcasted_iota(jnp.int32, grad_gain.shape, 0)
    first = place[0] * own_rows
    mine = (rows >= first) & (rows < first + own_rows)
    gain_grad_ref[...] = jnp.sum(jnp.where(mine, grad_gain, 0.0), axis=0, keepdims=True)
    grad = cot_ref[...].astype(f32) + normalise_back(unit, inverse, grad_two * gain_ref[...])
    low[...] = grad.astype(bf16)
    for k in range(team):

        @pl.when(place[0] == k)
        def own():
            middle_grad_ref[...] = grad[k * own_rows : (k + 1) * own_rows, :]

    weight_copies(pieces, weights, place, sems, lambda copy: copy.wait())
    for copy in late_copies:
        copy.wait()
    grad_out[...] = dot(low[...], of_heads(weights, 3)).astype(bf16)
    for h in range(col_parts):
        q, k, v = (kept_ref[i, :, head(h)] for i in range(3))
        grad_heads = grad_out[:, head(h)]
        grad_v[:, head(h)] = dot(probs_t_ref[h], grad_heads).astype(bf16)
        probs = probs_ref[h].astype(f32)
        grad_probs = dot_t(grad_heads, v)
        inner = jnp.sum(grad_probs * probs, axis=-1, keepdims=True)
        grad_scores = (probs * (grad_probs - inner)).astype(bf16)
        grad_q[:, head(h)] = (dot(grad_scores, k) * score_scale).astype(bf16)
        turned = dot_t(v, grad_heads) - inner.T
        turned = (probs_t_ref[h].astype(f32) * turned).astype(bf16)
        grad_k[:, head(h)] = (dot(turned, q) * score_scale).astype(bf16)
    total = dot_t(grad_k[...], of_heads(weights, 1)) + dot_t(grad_v[...], of_heads(weights, 2))
    total_low[...] = total.astype(bf16)
    width = context_grads[0].shape[1]
    for k in range(team):
        lanes = pl.ds(pl.multiple_of((place[0] ^ k) * width, LANES), width)
        context_grads[k][...] = total_low[:, lanes]
    one_ref[...] = dot_t(grad_q[...], of_heads(weights, 0)).astype(bf16)


def head_grads_kernel(col_parts, row_parts, place, low, attended_ref, *refs):
    normed_t_ref, context_t_ref, grad_q, grad_k, grad_v = refs[:5]
    stacks, (grads, out_sems) = refs[5:9], refs[9:]
    half = col_parts // 2
    shape = (*grads.shape[1:3], HD)

    def put(i, grad):
        for h in range(col_parts):
            grads[h, :, :, head(i)] = grad[:, head(h)].astype(bf16).reshape(shape)

    put(0, dot(normed_t_ref[...], grad_q[...]))
    put(1, dot(context_t_ref[...], grad_k[...]))
    put(2, dot(context_t_ref[...], grad_v[...]))
    put(3, dot(low[...].T, attended_ref[...]))
    copies = []
    for k in range(col_parts):
        for r, piece in enumerate(gradient_pieces(stacks, row_parts, k // half, k % half)):
            copies.append(pltpu.make_async_copy(grads.at[k, place[2] ^ r], piece, out_sems.at[k, r]))
    for copy in copies:
        copy.start()
    for copy in copies:
        copy.wait()


def adjoint_kernel(team, logr_ref, *refs):
    parts = refs[:team]
    g_tiles, ends_ref, total_ref, rows = refs[team:]
    grad = parts[0][...].astype(f32)
    for part in parts[1:]:
        grad = grad + part[...].astype(f32)
    grad = grad.astype(bf16).astype(f32)
    tiles, length, unused = g_tiles.shape
    states = logr_ref.shape[0]
    span = length // SUBS
    for tile in range(tiles):
        rows[...] = grad[:, lane_tile(tile)]
        in_steps(g_tiles, tile, rows)
    before = (sub_index() * span).astype(f32)
    for tile in range(tiles):
        rate = jnp.exp(logr_ref[:, lane_tile(tile)])
        decay = jnp.exp(-rate)
        for first in range(0, states, GROUP):
            chosen = range(first, first + GROUP)
            decays = [spread(decay[n : n + 1]) for n in chosen]

            def step(i, held):
                g = g_tiles[tile, step_rows(span - 1 - i), :]
                later = []
                for d, (b, w) in zip(decays, held):
                    shrunk = d * b
                    later.append((g + shrunk, d * w + shrunk))
                return tuple(later)

            zero = no_state(g_tiles)
            held = lax.fori_loop(0, span, step, ((zero, zero),) * GROUP, unroll=4)
            for n, (b, w) in zip(chosen, held):
                ends_ref[0, n, :, lane_tile(tile)] = b
                ends_ref[1, n, :, lane_tile(tile)] = w
                shrink = jnp.exp(-before * rate[n : n + 1])
                total_ref[0, n : n + 1, lane_tile(tile)] = jnp.sum(
                    shrink * b, axis=0, keepdims=True
                )
                total_ref[1, n : n + 1, lane_tile(tile)] = jnp.sum(
                    shrink * (w + before * b), axis=0, keepdims=True
                )


def context_back_kernel(
    team, place, g_tiles, u_tiles, ends_ref, all_ref, logr_ref, coef_ref, one_ref, *refs
):
    pieces = refs[:team]
    grad_ssm_ref, y_tiles, full, rows = refs[team:]
    tiles, length, unused = u_tiles.shape
    states = logr_ref.shape[0]
    span = length // SUBS
    width = tiles * LANES
    index = sub_index()
    after = ((SUBS - 1 - index) * span).astype(f32)
    full[...] = one_ref[...].astype(f32)
    group = GROUP
    for tile in range(tiles):
        lanes = lane_tile(tile)
        rate = jnp.exp(logr_ref[:, lanes])
        decay = jnp.exp(-rate)
        root = jnp.sqrt(2.0 * rate)
        scale = coef_ref[:, lanes] * root
        in_b = jnp.zeros((states, LANES), f32)
        in_w = jnp.zeros((states, LANES), f32)
        for j in range(all_ref.shape[0]):
            gap = j - place[1] - 1
            distance = (jnp.maximum(gap, 0) * length).astype(f32)
            shrink = jnp.exp(-distance * rate)
            b, w = all_ref[j, 0, :, lanes].astype(f32), all_ref[j, 1, :, lanes].astype(f32)
            in_b = in_b + jnp.where(gap >= 0, shrink * b, 0.0)
            in_w = in_w + jnp.where(gap >= 0, shrink * (w + distance * b), 0.0)
        for first in range(0, states, group):
            chosen = range(first, first + group)
            starts = []
            for n in chosen:
                row = rate[n : n + 1]
                b, w = ends_ref[0, n, :, lanes], ends_ref[1, n, :, lanes]
                for d in (1, 2, 4):
                    shrink = jnp.exp(-(d * span) * row)
                    next_b = pltpu.roll(b, SUBS - d, 0)
                    next_w = pltpu.roll(w, SUBS - d, 0)
                    inside = index < SUBS - d
                    b, w = (
                        b + jnp.where(inside, shrink * next_b, 0.0),
                        w + jnp.where(inside, shrink * (next_w + (d * span) * next_b), 0.0),
                    )
                inside = index < SUBS - 1
                b = jnp.where(inside, pltpu.roll(b, SUBS - 1, 0), 0.0)
                w = jnp.where(inside, pltpu.roll(w, SUBS - 1, 0), 0.0)
                shrink = jnp.exp(-after * row)
                b_row, w_row = in_b[n : n + 1], in_w[n : n + 1]
                b = b + shrink * b_row
                w = w + shrink * (w_row + after * b_row)
                zero = no_state(u_tiles)
                starts.append((b, w, zero, zero))
            decays = [spread(decay[n : n + 1]) for n in chosen]
            scales = [spread(scale[n : n + 1]) for n in chosen]

            def step(i, held):
                at = step_rows(span - 1 - i)
                g = g_tiles[tile, at, :]
                u = u_tiles[tile, at, :]
                later, parts = [], []
                for d, s, (b, w, sum_b, sum_w) in zip(decays, scales, held):
                    shrunk = d * b
                    w = d * w + shrunk
                    b = g + shrunk
                    later.append((b, w, sum_b + u * b, sum_w + u * w))
                    parts.append(s * b)
                while len(parts) > 1:
                    parts = [p + q for p, q in zip(parts[::2], parts[1::2])]
                if first > 0:
                    parts[0] = parts[0] + y_tiles[tile, at, :]
                y_tiles[tile, at, :] = parts[0]
                return tuple(later)

            held = lax.fori_loop(0, span, step, tuple(starts), unroll=2)
            for n, (unused_b, unused_w, sum_b, sum_w) in zip(chosen, held):
                sum_b = jnp.sum(sum_b, axis=0, keepdims=True)
                sum_w = jnp.sum(sum_w, axis=0, keepdims=True)
                row = slice(n, n + 1)
                grad_ssm_ref[0, row, lanes] = root[row] * sum_b
                grad_ssm_ref[1, row, lanes] = scale[row] * (0.5 * sum_b - rate[row] * sum_w)
        at_lanes = pl.ds(pl.multiple_of(place[0] * width + tile * LANES, LANES), LANES)
        from_steps(rows, y_tiles, tile)
        full[:, at_lanes] += rows[...].astype(bf16).astype(f32)
    count = pieces[0].shape[0]
    for k in range(team):
        at_rows = pl.ds(pl.multiple_of((place[0] ^ k) * count, count), count)
        pieces[k][...] = full[at_rows, :].astype(bf16)


def input_grad_kernel(team, place, x_ref, gain_ref, middle_grad_ref, *refs):
    parts, (out_ref, gain_grad_ref) = refs[:team], refs[team:]
    rows = out_ref.shape[0]
    at_rows = pl.ds(pl.multiple_of(place[0] * rows, rows), rows)
    grad_one = parts[0][...].astype(f32)
    for part in parts[1:]:
        grad_one = grad_one + part[...].astype(f32)
    unit, inverse = normalise(x_ref[at_rows, :].astype(f32))
    gain_grad_ref[...] = jnp.sum(grad_one * unit, axis=0, keepdims=True)
    back = normalise_back(unit, inverse, grad_one * gain_ref[...])
    out_ref[...] = (middle_grad_ref[...] + back).astype(bf16)


def assemble_kernel(halves, low_count, place, own_ref, *refs):
    others, out_ref = refs[:-1], refs[-1]
    count, rows, unused = own_ref.shape
    half = place[4]

    def put(value, sequence, which, member):
        at_rows = pl.ds(pl.multiple_of((which * low_count + member) * rows, rows), rows)
        out_ref[sequence, at_rows, :] = value.astype(out_ref.dtype)

    for sequence in range(count // (halves * low_count)):
        if halves == 1:
            for member in range(low_count):
                put(own_ref[sequence * low_count + member], sequence, 0, member)
        else:
            put(own_ref[sequence * halves + half], sequence, half, 0)
            put(others[0][sequence], sequence, 1 - half, 0)


def pack_kernel(halves, place, qkv_ref, out_ref, up_ref, down_ref, *refs):
    rows = up_ref.shape[0]
    heads, hidden = out_ref.shape[0] // halves, up_ref.shape[1] // halves
    for which in range(halves):
        side = place[4] if which == 0 else 1 - place[4]
        at_heads = pl.ds(pl.multiple_of(side * heads, LANES), heads)
        at_hidden = pl.ds(pl.multiple_of(side * hidden, LANES), hidden)
        if which == 0:
            head_ref, wide_ref, deep_ref = refs[:3]
        else:
            packed = refs[3]
            head_ref = packed.at[:, : 4 * heads]
            wide_ref = packed.at[:, 4 * heads : 4 * heads + hidden]
            deep_ref = packed.at[:, 4 * heads + hidden :]
        for i in range(3):
            head_ref[:, i * heads : (i + 1) * heads] = qkv_ref[i, :, at_heads].astype(bf16)
        head_ref[:, 3 * heads :] = out_ref[at_heads, :].T.astype(bf16)
        wide_ref[...] = up_ref[:, at_hidden].astype(bf16)
        deep_ref[...] = down_ref[at_hidden, :].T.astype(bf16)


def small_kernel(ssm_ref, gains_ref, out_ref):
    count = ssm_ref.shape[0]
    out_ref[:count, :] = ssm_ref[...]
    out_ref[count:, :] = gains_ref[...]


def lamb_moments(weight, grad_item, first_old, second_old):
    first_new = beta_first * first_old + (1.0 - beta_first) * grad_item
    second_new = beta_second * second_old + (1.0 - beta_second) * grad_item * grad_item
    direction = (
        first_new
        / (1.0 - beta_first**STEP)
        / (jnp.sqrt(second_new / (1.0 - beta_second**STEP)) + lamb_eps)
        + weight_decay * weight
    )
    return (first_new, second_new, direction)


def place_sums(sums_ref, sums):
    rows = lax.broadcasted_iota(jnp.int32, sums_ref.shape, 0)
    lanes = lax.broadcasted_iota(jnp.int32, sums_ref.shape, 1)
    found = jnp.zeros(sums_ref.shape, f32)
    for index, pair in sums.items():
        for row, value in enumerate(pair):
            found = jnp.where((rows == row) & (lanes == index), value, found)
    sums_ref[...] = found


def moments_kernel(halves, matrices, place, *refs):
    count = 1 + max(item[1] for item in matrices)
    grads, refs = [refs[halves * i : halves * (i + 1)] for i in range(count)], refs[halves * count :]
    arrays = len({(item[1], item[4] is None) for item in matrices})
    ins = [refs[3 * i : 3 * i + 3] for i in range(arrays)]
    outs = [refs[3 * (arrays + i) : 3 * (arrays + i) + 3] for i in range(arrays)]
    sums_ref = refs[6 * arrays]
    keys = []
    sums = {}
    for number, source, column, turned, stacked in matrices:
        key = (source, stacked is None)
        if key not in keys:
            keys.append(key)
        pick = (lambda ref: ref) if stacked is None else (lambda ref, i=stacked: ref.at[i])
        weight, first, second = (pick(ref) for ref in ins[keys.index(key)])
        news = [pick(ref) for ref in outs[keys.index(key)]]
        width = weight.shape[0 if turned else 1] // halves
        rows = weight.shape[1 if turned else 0]
        cols = slice(column * width, (column + 1) * width)
        total_weight = total_update = 0.0
        for which, grad_ref in enumerate(grads[source]):
            side = place[4] if which == 0 else 1 - place[4]
            at = pl.ds(pl.multiple_of(side * width, width), width)
            if which == 0:
                grad = grad_ref[pl.ds(pl.multiple_of(side * rows, rows), rows), cols].astype(f32)
            else:
                grad = grad_ref[:, cols].astype(f32)
            at = (at, slice(None)) if turned else (slice(None), at)
            grad = grad.T if turned else grad
            old = weight[at]
            found = lamb_moments(old, grad, first[at], second[at])
            for ref, value in zip(news, found):
                ref[at] = value
            total_weight = total_weight + jnp.sum(old * old)
            total_update = total_update + jnp.sum(found[2] * found[2])
        sums[number] = (total_weight, total_update)
    place_sums(sums_ref, sums)


def small_moments_kernel(numbers, grads_ref, *refs):
    ins, outs, sums_ref = (refs[:3], refs[3:6]), (refs[6:9], refs[9:12]), refs[12]
    states = (grads_ref.shape[0] - 2) // 2
    sums = {}
    for (weight, first, second), news, start, rows, first_number in (
        (ins[0], outs[0], 2 * states, 1, numbers[0]),
        (ins[1], outs[1], 0, states, numbers[1]),
    ):
        for i in range(2):
            grad = grads_ref[start + i * rows : start + (i + 1) * rows, :]
            at = slice(i * rows, (i + 1) * rows)
            found = lamb_moments(weight[at, :], grad, first[at, :], second[at, :])
            for ref, value in zip(news, found):
                ref[at, :] = value
            sums[first_number + i] = (
                jnp.sum(weight[at, :] * weight[at, :]),
                jnp.sum(found[2] * found[2]),
            )
    place_sums(sums_ref, sums)


def update_kernel(stacks, sums_ref, *refs):
    count = len(stacks)
    weights, directions, news = refs[:count], refs[count : 2 * count], refs[2 * count : 3 * count]
    norms = jnp.sqrt(jnp.sum(sums_ref[...], axis=0))
    refs[3 * count][...] = norms
    ratios = norms[0:1] / norms[1:2]
    lanes = lax.broadcasted_iota(jnp.int32, ratios.shape, 1)
    for numbers, weight, direction, new in zip(stacks, weights, directions, news):
        step = weight.shape[0] // len(numbers)
        for i, number in enumerate(numbers):
            ratio = jnp.sum(jnp.where(lanes == number, ratios, 0.0), axis=1, keepdims=True)
            at = slice(i * step, (i + 1) * step)
            scale = learn_rate * ratio.reshape((1,) * weight.ndim)
            new[at] = weight[at] - scale * direction[at]


def call(
    body, ins, outs, scratch=(), grid=None, in_specs=None, out_specs=None, time=1.0, after=(), token=False
):
    moved = sum(a.size * a.dtype.itemsize for a in list(ins) + list(outs))
    params = pltpu.CompilerParams(vmem_limit_bytes=VMEM_BYTES)
    cost = pl.CostEstimate(flops=int(time * 1.15e9), bytes_accessed=moved, transcendentals=0)
    whole = pl.BlockSpec(memory_space=pltpu.VMEM)
    anywhere = pl.BlockSpec(memory_space=pl.ANY)
    in_specs = list(in_specs or [whole] * len(ins)) + [anywhere] * len(after)
    out_specs = list(out_specs or [whole] * len(outs))
    outs = list(outs)
    first_out = len(ins) + len(after)
    last_out = first_out + len(outs)
    if token:
        outs.append(jax.ShapeDtypeStruct((SUBS, LANES), f32))
        out_specs.append(whole)

    def run(*refs):
        refs = list(refs)
        if token:
            refs[last_out][...] = jnp.zeros((SUBS, LANES), f32)
            del refs[last_out]
        body(*refs[: len(ins)], *refs[first_out:])

    return pl.pallas_call(
        run,
        out_shape=tuple(outs),
        in_specs=in_specs,
        out_specs=tuple(out_specs),
        scratch_shapes=list(scratch),
        compiler_params=params,
        cost_estimate=cost,
        **({} if grid is None else {"grid": grid}),
    )(*ins, *after)


def shaped(shape, kind):
    return jax.ShapeDtypeStruct(tuple(shape), kind)


def on_device(
    tokens,
    cotangent,
    w_qkv,
    w_out,
    w_up,
    w_down,
    norm_gains,
    ssm_param,
    first_qkv,
    second_qkv,
    first_out,
    second_out,
    first_up,
    second_up,
    first_down,
    second_down,
    first_gain,
    second_gain,
    first_ssm,
    second_ssm,
):
    halves = lax.axis_size("sl")
    low_count = lax.axis_size("ml")
    row_parts = lax.axis_size("sh")
    col_parts = lax.axis_size("mb") * lax.axis_size("mq")
    team = halves * low_count
    sl, ml, mb, mq = (lax.axis_index(name) for name in ("sl", "ml", "mb", "mq"))
    rank = sl * low_count + ml
    block_index = lax.axis_index("sh") * halves + mq
    seq_total, length, width = tokens.shape
    assert length == BLK and seq_total == lax.axis_size("mb")
    states = ssm_param.shape[1]
    channels = width // team
    tiles = channels // LANES
    row_count = width // row_parts
    own_rows = length // team
    place = [rank, block_index, lax.axis_index("sh"), lax.axis_index(MODEL), sl, sl ^ mq]
    place.append(lax.axis_index(COLS))
    place = jnp.stack(place).astype(jnp.int32)
    smem = pl.BlockSpec(memory_space=pltpu.SMEM)
    vmem = pl.BlockSpec(memory_space=pltpu.VMEM)

    def permute(value, axes, moves):
        return lax.ppermute(value, axes, moves)

    def swap(value):
        return permute(value, "sl", [(0, 1), (1, 0)])

    def in_order(own, other, axis):
        return jnp.where(
            sl == 0, jnp.concatenate([own, other], axis), jnp.concatenate([other, own], axis)
        )

    def team_send(pieces):
        moved = [pieces[0]]
        for k in range(1, team):
            moved.append(permute(pieces[k], TEAM, [(i, i ^ k) for i in range(team)]))
        return moved

    def pick_block(array):
        own = lax.dynamic_index_in_dim(array, mb, 0, keepdims=False)
        if halves == 1:
            return own, ()
        other = swap(own)
        return jnp.where(sl == mq, own, other), (other,)

    def across(value, bit):
        return permute(value, "sh", [(i, i ^ bit) for i in range(row_parts)])

    def along(value, axes, step):
        count = lax.axis_size(axes)
        return permute(value, axes, [(i, (i + step) % count) for i in range(count)])

    bits = [1 << i for i in range(row_parts.bit_length() - 1)]

    def bit_order(k):
        return bits if k % 2 == 0 else bits[::-1]

    def double_rows(value, order):
        found = {0: value}
        for bit in order:
            for r in list(found):
                found[r | bit] = across(found[r], bit)
        return [found[r] for r in range(row_parts)]

    def add(*items, zero=None):
        total = sum(item.astype(f32) for item in items)
        return (total if zero is None else total + zero[0, 0]).astype(bf16)

    def first_messages(stacks):
        return across(stacks[1], bits[-1]), across(stacks[3], bits[0])

    def halve_rows(keep, arrived, order, zero, sent):
        items = [keep, arrived]
        for bit in order[-2::-1]:
            count = arrived.shape[0] // 2
            sent.append(add(*[item[count:] for item in items], zero=zero))
            arrived = across(sent[-1], bit)
            items = [item[:count] for item in items] + [arrived]
        return add(*[item[0] for item in items])

    def halve_both(stacks, first, zero):
        sent = []
        near = halve_rows(stacks[0], first[0], bits, zero, sent)
        return (near, halve_rows(stacks[2], first[1], bits[::-1], zero, sent)), sent

    def hold(arrays, after):
        anywhere = pl.BlockSpec(memory_space=pl.ANY)
        return pl.pallas_call(
            lambda *refs: None,
            out_shape=tuple(shaped(item.shape, item.dtype) for item in arrays),
            in_specs=[anywhere] * (len(arrays) + len(after)),
            out_specs=(anywhere,) * len(arrays),
            input_output_aliases={i: i for i in range(len(arrays))},
        )(*arrays, *after)

    def ring_gather(shard):
        pieces, held = [], shard
        for k in range(col_parts):
            if k > 0:
                held = along(held, COLS, 1)
            pieces.append(double_rows(held, bits if k % 2 == 0 else bits[::-1]))
        return pieces

    def sum_over_z(near, far, ring=True):
        if not ring:
            pieces = [stack[k] for stack in (near, far) for k in range(col_parts // 2)]
            moved = [along(piece, COLS, -k) for k, piece in enumerate(pieces) if k > 0]
            return add(pieces[0], *moved)
        held = None
        for stack in (far, near):
            for k in reversed(range(stack.shape[0])):
                held = stack[k] if held is None else add(stack[k], along(held, COLS, -1))
        return held

    def everywhere(value, axes):
        count = lax.axis_size(axes)
        copies = jnp.broadcast_to(value[None], (count, *value.shape))
        return lax.all_to_all(copies, axes, 0, 0, tiled=True)

    rows_dev = w_up.shape[0]
    hidden_cols = w_up.shape[1] // halves
    head_cols = 4 * w_out.shape[0] // halves
    packed_cols = head_cols + 2 * hidden_cols
    sides = [shaped((rows_dev, cols), bf16) for cols in (head_cols, hidden_cols, hidden_cols)]
    shards = call(
        functools.partial(pack_kernel, halves),
        (place, w_qkv, w_out, w_up, w_down),
        sides + [shaped((rows_dev, packed_cols), bf16)] * (halves - 1),
        time=2.4,
        in_specs=[smem] + [vmem] * 4,
    )
    if halves == 2:
        other = swap(shards[3])
        cuts = (0, head_cols, head_cols + hidden_cols, packed_cols)
        shards = [
            in_order(own, other[:, first:last], 0)
            for own, first, last in zip(shards, cuts, cuts[1:])
        ]
    head_shard, up_shard, down_shard = shards[:3]
    attn_w = ring_gather(head_shard)
    up_full = lax.all_gather(up_shard, COLS, axis=0, tiled=False)
    down_full = lax.all_gather(down_shard, COLS, axis=0, tiled=False)
    up_w = double_rows(up_full, bits)
    down_w = double_rows(down_full, bits[::-1])
    attn_flat = [piece for group in attn_w for piece in group]

    small, = call(
        small_kernel,
        (ssm_param.reshape(2 * states, -1), norm_gains),
        (shaped((2 * states + 2, norm_gains.shape[1]), f32),),
        after=(head_shard,),
    )
    small = jnp.transpose(everywhere(small, ALL), (1, 0, 2)).reshape(2 * states + 2, width)
    own_ssm = lax.dynamic_slice_in_dim(
        small[: 2 * states].reshape(2, states, width), rank * channels, channels, 2
    )
    coef, logr = own_ssm[0], own_ssm[1]
    gain_one = small[2 * states : 2 * states + 1]
    gain_two = small[2 * states + 1 : 2 * states + 2]

    x, unused = pick_block(tokens)
    cot, cot_other = pick_block(cotangent)

    anywhere = [pl.BlockSpec(memory_space=pl.ANY)]

    def fixed(*shape):
        return pl.BlockSpec(shape, lambda z: (0,) * len(shape))

    wide = fixed(length, width)
    row = fixed(1, width)

    normed_one, normed_t, u_steps, ends, total = call(
        norm_kernel,
        (place, x, gain_one, logr),
        (
            shaped((length, width), bf16),
            shaped((width, length), bf16),
            shaped((tiles, length, LANES), f32),
            shaped((states, SUBS, channels), f32),
            shaped((states, channels), f32),
        ),
        scratch=[pltpu.VMEM((length, LANES), f32)],
        in_specs=[smem, vmem, vmem, vmem],
        after=(*attn_w[0][1:-1], attn_w[1][0], *cot_other),
        time=5,
    )
    totals = everywhere(total.astype(bf16), ("sh", "mq"))
    (context_own,) = call(
        context_kernel,
        (place, u_steps, ends, totals, logr, coef),
        (shaped((length, channels), bf16),),
        after=(attn_w[0][-1], *attn_w[1][1:-1], attn_w[-1][0]),
        scratch=[pltpu.VMEM((tiles, length, LANES), f32), pltpu.VMEM((length, LANES), f32)],
        in_specs=[smem] + [vmem] * 5,
        time=7,
    )
    contexts = team_send([context_own] * team)

    stack_shape = (row_parts // 2, col_parts // 2, row_count)
    head_stacks = [shaped((*stack_shape, head_cols), bf16)] * 4
    hidden_stacks = [shaped((*stack_shape, hidden_cols), bf16)] * 8
    sizes = (team, col_parts, row_parts)
    head_buffer = pltpu.VMEM((col_parts, row_parts, row_count, 4 * HD), bf16)
    head_sems = pltpu.SemaphoreType.DMA((col_parts, row_parts))
    kept_shape = shaped((3, length, col_parts * HD), bf16)
    flat_shape = shaped((length, col_parts * HD), bf16)
    context_t, cot_t, kept = call(
        functools.partial(project_kernel, *sizes),
        (place, normed_one, cot, *contexts, *attn_flat),
        (shaped((width, length), bf16), shaped((width, length), bf16), kept_shape),
        scratch=[pltpu.VMEM((length, width), bf16), head_buffer, head_sems],
        time=1,
        in_specs=[smem] + [vmem] * (2 + team) + anywhere * len(attn_flat),
        after=(up_full,),
    )
    attn_part, attended, probs, probs_t = call(
        functools.partial(attend_kernel, *sizes),
        (place, kept, *attn_flat),
        (
            shaped((length, width), bf16),
            flat_shape,
            *[shaped((col_parts, length, length), bf16)] * 2,
        ),
        scratch=[head_buffer, head_sems],
        time=1,
        in_specs=[smem, vmem] + anywhere * len(attn_flat),
        after=up_w[1:-1],
    )
    attn_parts = team_send([attn_part] * team)

    middle, normed_two, normed_two_t = call(
        functools.partial(middle_kernel, team),
        (x, gain_two, *attn_parts),
        (shaped((length, width), f32), shaped((length, width), bf16), shaped((width, length), bf16)),
        time=1,
        after=(up_w[-1], *down_w[1:-1]),
    )
    weight_buffer = pltpu.VMEM((row_parts, row_count, col_parts * hidden_cols), bf16)
    grad_buffer = pltpu.VMEM((col_parts, row_parts, row_count, hidden_cols), bf16)
    fed = call(
        functools.partial(feed_kernel, team, col_parts, row_parts),
        (place, normed_two, normed_two_t, cot, cot_t, *up_w, *down_w),
        (
            *[shaped((own_rows, width), bf16)] * team,
            shaped((length, width), bf16),
            *hidden_stacks,
        ),
        scratch=[
            *[weight_buffer] * 2,
            *[grad_buffer] * 2,
            *[pltpu.VMEM((length, col_parts * hidden_cols), bf16)] * 2,
            pltpu.SemaphoreType.DMA((4, col_parts, row_parts)),
        ],
        time=18,
        grid=(col_parts,),
        in_specs=[smem, wide, fixed(width, length), wide, fixed(width, length)]
        + anywhere * (2 * row_parts),
        out_specs=[fixed(own_rows, width)] * team + [wide] + anywhere * 8,
    )
    out_pieces, two_part, hidden_grads = fed[:team], fed[team], fed[team + 1 :]
    two_parts = team_send([two_part] * team)

    def rows_of(array, member):
        return lax.dynamic_slice_in_dim(array, member * own_rows, own_rows, 0)

    def share_rows(pieces, kind):
        others = []
        if halves == 2:
            pairs = pieces.reshape(seq_total, halves, own_rows, width)
            others = [swap(lax.dynamic_index_in_dim(pairs, 1 - sl, 1, keepdims=False))]
        (blocks,) = call(
            functools.partial(assemble_kernel, halves, low_count),
            (place, pieces, *others),
            (shaped((seq_total, length, width), kind),),
            time=3.5,
            in_specs=[smem, vmem] + [vmem] * len(others),
        )
        return blocks

    out_pieces = team_send(list(out_pieces))
    result = rows_of(middle, rank) + sum(item.astype(f32) for item in out_pieces)
    result = result.astype(bf16)
    layer_pieces = lax.all_gather(result, MODEL, axis=0, tiled=False)
    layer_out = share_rows(layer_pieces, bf16)

    def both_halves(own):
        if halves == 1:
            return [own]
        return [own, swap(lax.dynamic_slice_in_dim(own, (1 - sl) * rows_dev, rows_dev, 0))]

    middle_grad, gain_two_grad, one_part, low_grad, *rest = call(
        functools.partial(attend_back_kernel, *sizes),
        (place, middle, gain_two, cot, *two_parts, kept, probs, probs_t, *attn_flat),
        (
            shaped((own_rows, width), f32),
            shaped((1, width), f32),
            shaped((length, width), bf16),
            shaped((length, width), bf16),
            *[flat_shape] * 3,
            *[shaped((length, channels), bf16)] * team,
        ),
        scratch=[
            head_buffer,
            pltpu.VMEM(flat_shape.shape, bf16),
            pltpu.VMEM((length, width), bf16),
            pltpu.VMEM(kept_shape.shape, bf16),
            *[pltpu.VMEM((col_parts, length, length), bf16)] * 2,
            head_sems,
            pltpu.SemaphoreType.DMA((3,)),
        ],
        time=1,
        in_specs=[smem] + [vmem] * (3 + team) + anywhere * (3 + len(attn_flat)),
        after=(result,),
    )
    head_grads, context_grads = rest[:3], rest[3:]
    context_grads = team_send(context_grads)
    down_first = first_messages(hidden_grads[4:])
    g_steps, adjoint_ends, adjoint_total, adjoint_done = call(
        functools.partial(adjoint_kernel, team),
        (logr, *context_grads),
        (
            shaped((tiles, length, LANES), f32),
            shaped((2, states, SUBS, channels), f32),
            shaped((2, states, channels), f32),
        ),
        scratch=[pltpu.VMEM((length, LANES), f32)],
        time=1,
        after=down_first,
        token=True,
    )
    adjoint_totals = everywhere(adjoint_total.astype(bf16), ("sh", "mq"))
    down_sums, down_sent = halve_both(hidden_grads[4:], down_first, adjoint_done)
    *head_stacks, heads_done = call(
        functools.partial(head_grads_kernel, col_parts, row_parts),
        (place, low_grad, attended, normed_t, context_t, *head_grads),
        head_stacks,
        scratch=[head_buffer, head_sems],
        time=8,
        in_specs=[smem] + [vmem] * 7,
        out_specs=anywhere * 4,
        after=(adjoint_total,),
        token=True,
    )
    up_stacks = list(hidden_grads[:4])
    up_stacks[1::2] = hold(up_stacks[1::2], (adjoint_totals, *down_sent))
    up_first = first_messages(up_stacks)
    *one_pieces, grad_ssm = call(
        functools.partial(context_back_kernel, team),
        (place, g_steps, u_steps, adjoint_ends, adjoint_totals, logr, coef, one_part),
        (
            *[shaped((own_rows, width), bf16)] * team,
            shaped((2, states, channels), f32),
        ),
        scratch=[
            pltpu.VMEM((tiles, length, LANES), f32),
            pltpu.VMEM((length, width), f32),
            pltpu.VMEM((length, LANES), f32),
        ],
        in_specs=[smem] + [vmem] * 7,
        time=1,
        after=(heads_done,),
    )
    one_pieces = team_send(one_pieces)
    grad_rows, gain_one_grad, rows_done = call(
        functools.partial(input_grad_kernel, team),
        (place, x, gain_one, middle_grad, *one_pieces),
        (shaped((own_rows, width), bf16), shaped((1, width), f32)),
        in_specs=[smem] + [vmem] * (3 + team),
        time=1,
        after=(layer_pieces, *up_first, *down_sums),
        token=True,
    )
    grad_down = sum_over_z(*down_sums, False)
    head_stacks[1::2] = hold(head_stacks[1::2], (grad_rows,))
    head_sums, unused = halve_both(head_stacks, first_messages(head_stacks), rows_done)
    up_sums, unused = halve_both(up_stacks, up_first, rows_done)
    grad_up = sum_over_z(*up_sums)
    grad_heads = sum_over_z(*head_sums)
    input_grad = share_rows(lax.all_gather(grad_rows, MODEL, axis=0, tiled=False), f32)

    placed_ssm = lax.dynamic_update_slice_in_dim(
        jnp.zeros((2 * states, width), f32),
        grad_ssm.reshape(2 * states, channels),
        rank * channels,
        1,
    )
    small_grads = jnp.concatenate([placed_ssm, gain_one_grad, gain_two_grad], 0)
    small_grads = small_grads.reshape(2 * states + 2, lax.axis_size(ALL), -1)
    small_grads = lax.all_to_all(jnp.transpose(small_grads, (1, 0, 2)), ALL, 0, 0, tiled=True)
    small_grads = jnp.sum(small_grads, axis=0)

    def moments(matrices, grads, arrays):
        changed = [shaped(old.shape, f32) for group in arrays for old in group]
        grad_parts = [part for grad in grads for part in both_halves(grad)]
        ins = [item for group in arrays for item in group]
        *found, sums = call(
            functools.partial(moments_kernel, halves, matrices),
            (place, *grad_parts, *ins),
            (*changed, shaped((2, LANES), f32)),
            in_specs=[smem] + [vmem] * (len(grad_parts) + len(ins)),
            time=4,
        )
        return [found[3 * i : 3 * i + 3] for i in range(len(arrays))], sums

    hidden_new, hidden_sums = moments(
        ((4, 0, 0, False, None), (5, 1, 0, True, None)),
        (grad_up, grad_down),
        ((w_up, first_up, second_up), (w_down, first_down, second_down)),
    )
    heads_new, head_sums = moments(
        tuple((i, 0, i, False, i) for i in range(3)) + ((3, 0, 3, True, None),),
        (grad_heads,),
        ((w_qkv, first_qkv, second_qkv), (w_out, first_out, second_out)),
    )
    own_channels = norm_gains.shape[1]
    ssm_items = [item.reshape(2 * states, own_channels) for item in (ssm_param, first_ssm, second_ssm)]
    small_items = [norm_gains, first_gain, second_gain, *ssm_items]
    *small_new, small_sums = call(
        functools.partial(small_moments_kernel, (6, 8)),
        (small_grads.reshape(2 * states + 2, own_channels), *small_items),
        (*[shaped(item.shape, f32) for item in small_items], shaped((2, LANES), f32)),
    )
    all_sums = everywhere(hidden_sums + head_sums + small_sums, ALL)
    masters = (w_qkv, w_out, w_up, w_down, norm_gains, ssm_items[0])
    news = (*heads_new, *hidden_new, small_new[:3], small_new[3:])
    *weights, norms = call(
        functools.partial(update_kernel, ((0, 1, 2), (3,), (4,), (5,), (6, 7), (8, 9))),
        (all_sums, *masters, *[group[2] for group in news]),
        (*[shaped(item.shape, f32) for item in masters], shaped((2, LANES), f32)),
        time=3.2,
    )
    outputs = [layer_out, input_grad]
    for index, (weight, (first_new, second_new, unused)) in enumerate(zip(weights, news)):
        if index == 4:
            outputs += [weight, first_new, second_new[0], second_new[1]]
        else:
            kept_shape = ssm_param.shape if index == 5 else weight.shape
            outputs += [item.reshape(kept_shape) for item in (weight, first_new, second_new)]
    outputs.append(norms[:, :10])
    return tuple(outputs)


def solution(mesh):
    seq_count, model_count = mesh.shape["seq"], mesh.shape["mp"]
    halves = 2 if HEADS // model_count >= 2 else 1
    sizes = (seq_count // halves, halves, SEQS, halves, model_count // (SEQS * halves))
    fine = Mesh(mesh.devices.reshape(sizes), ALL)
    seq, model = ("sh", "sl"), ("mb", "mq", "ml")
    rows_cols, cols_rows = P(seq, model), P(model, seq)
    token = P(None, seq, None)
    stack = P(None, seq, model)
    gains = P(None, ALL)
    ssm = P(None, None, ALL)
    return jax.shard_map(
        on_device,
        mesh=fine,
        in_specs=(token, token, stack, cols_rows, rows_cols, cols_rows, gains, ssm)
        + (stack,) * 2
        + (cols_rows,) * 2
        + (rows_cols,) * 2
        + (cols_rows,) * 2
        + (gains,) * 2
        + (ssm,) * 2,
        out_specs=(token, token)
        + (stack,) * 3
        + (cols_rows,) * 3
        + (rows_cols,) * 3
        + (cols_rows,) * 3
        + (gains, gains, P(ALL), P(ALL))
        + (ssm,) * 3
        + (P(),),
        check_vma=False,
    )
```

```python
import functools
import math

import jax
import jax.numpy as jnp
from jax import lax
from jax.experimental import pallas as pl
from jax.experimental.pallas import tpu as pltpu
from jax.sharding import Mesh
from jax.sharding import PartitionSpec as P

HD = 128
HEADS = 8
BLK = 512
STEP = 10
SEQS = 2
LANES = 128
SUBS = 8
GROUP = 8

norm_eps = 1e-05
beta_first = 0.9
beta_second = 0.999
lamb_eps = 1e-06
weight_decay = 0.01
learn_rate = 0.5
score_scale = HD ** (-0.5)

f32 = jnp.float32
bf16 = jnp.bfloat16
VMEM_BYTES = 56 * 1024 * 1024

ALL = ("sh", "sl", "mb", "mq", "ml")
MODEL = ("mb", "mq", "ml")
COLS = ("mb", "mq")
TEAM = ("sl", "ml")


def dot(left, right):
    return lax.dot_general(left, right, (((1,), (0,)), ((), ())), preferred_element_type=f32)


def dot_t(left, right):
    return lax.dot_general(left, right, (((1,), (1,)), ((), ())), preferred_element_type=f32)


def normalise(values):
    centred = values - jnp.mean(values, axis=-1, keepdims=True)
    inverse = lax.rsqrt(jnp.mean(centred * centred, axis=-1, keepdims=True) + norm_eps)
    return centred * inverse, inverse


def normalise_back(unit, inverse, grad_unit):
    mean_one = jnp.mean(grad_unit, axis=-1, keepdims=True)
    mean_two = jnp.mean(grad_unit * unit, axis=-1, keepdims=True)
    return inverse * (grad_unit - mean_one - unit * mean_two)


def sub_index():
    return lax.broadcasted_iota(jnp.int32, (SUBS, LANES), 0)


def spread(row):
    return jnp.broadcast_to(row, (SUBS, LANES))


def lane_tile(index):
    return slice(index * LANES, (index + 1) * LANES)


def no_state(tiles):
    rows = tiles[0, :SUBS, :]
    return rows - rows


def in_steps(steps, tile, rows):
    span = rows.shape[0] // SUBS

    def move(i, unused):
        steps[tile, pl.ds(pl.multiple_of(i * SUBS, SUBS), SUBS), :] = rows[
            pl.ds(i, SUBS, stride=span), :
        ]
        return unused

    lax.fori_loop(0, span, move, 0, unroll=8)


def from_steps(rows, steps, tile):
    span = rows.shape[0] // SUBS

    def move(i, unused):
        rows[pl.ds(i, SUBS, stride=span), :] = steps[
            tile, pl.ds(pl.multiple_of(i * SUBS, SUBS), SUBS), :
        ]
        return unused

    lax.fori_loop(0, span, move, 0, unroll=8)


def step_rows(i):
    return pl.ds(pl.multiple_of(i * SUBS, SUBS), SUBS)


def norm_kernel(
    place, x_ref, gain_ref, logr_ref, normed_ref, turned_ref, u_tiles, ends_ref, total_ref, rows
):
    unit, unused = normalise(x_ref[...].astype(f32))
    normed_ref[...] = (unit * gain_ref[...]).astype(bf16)
    turned_ref[...] = normed_ref[...].T
    tiles, length, unused = u_tiles.shape
    states = logr_ref.shape[0]
    span = length // SUBS
    for tile in range(tiles):
        start = place[0] * (tiles * LANES) + tile * LANES
        rows[...] = normed_ref[:, pl.ds(pl.multiple_of(start, LANES), LANES)].astype(f32)
        in_steps(u_tiles, tile, rows)
    left = ((SUBS - 1 - sub_index()) * span).astype(f32)
    for tile in range(tiles):
        rate = jnp.exp(logr_ref[:, lane_tile(tile)])
        decay = jnp.exp(-rate)
        decays = [spread(decay[n : n + 1]) for n in range(states)]

        def step(i, held):
            u = u_tiles[tile, step_rows(i), :]
            return tuple(d * h + u for d, h in zip(decays, held))

        zero = no_state(u_tiles)
        held = lax.fori_loop(0, span, step, (zero,) * states, unroll=4)
        for n in range(states):
            ends_ref[n, :, lane_tile(tile)] = held[n]
            total_ref[n : n + 1, lane_tile(tile)] = jnp.sum(
                held[n] * jnp.exp(-left * rate[n : n + 1]), axis=0, keepdims=True
            )


def context_kernel(
    place, u_tiles, ends_ref, all_ref, logr_ref, coef_ref, context_ref, y_tiles, rows
):
    tiles, length, unused = u_tiles.shape
    states = logr_ref.shape[0]
    span = length // SUBS
    index = sub_index()
    before = (index * span).astype(f32)
    for tile in range(tiles):
        rate = jnp.exp(logr_ref[:, lane_tile(tile)])
        decay = jnp.exp(-rate)
        scale = coef_ref[:, lane_tile(tile)] * jnp.sqrt(2.0 * rate)
        incoming = jnp.zeros((states, LANES), f32)
        for j in range(all_ref.shape[0]):
            gap = place[1] - 1 - j
            distance = (jnp.maximum(gap, 0) * length).astype(f32)
            term = jnp.exp(-distance * rate) * all_ref[j, :, lane_tile(tile)].astype(f32)
            incoming = incoming + jnp.where(gap >= 0, term, 0.0)
        for first in range(0, states, GROUP):
            chosen = range(first, first + GROUP)
            starts = []
            for n in chosen:
                row = rate[n : n + 1]
                run = ends_ref[n, :, lane_tile(tile)]
                for d in (1, 2, 4):
                    moved = jnp.exp(-(d * span) * row) * pltpu.roll(run, d, 0)
                    run = run + jnp.where(index >= d, moved, 0.0)
                run = jnp.where(index >= 1, pltpu.roll(run, 1, 0), 0.0)
                starts.append(run + jnp.exp(-before * row) * incoming[n : n + 1])
            decays = [spread(decay[n : n + 1]) for n in chosen]
            scales = [spread(scale[n : n + 1]) for n in chosen]

            def step(i, held):
                at = step_rows(i)
                u = u_tiles[tile, at, :]
                held = tuple(d * h + u for d, h in zip(decays, held))
                parts = [s * h for s, h in zip(scales, held)]
                if first > 0:
                    parts[0] = parts[0] + y_tiles[tile, at, :]
                while len(parts) > 1:
                    parts = [a + b for a, b in zip(parts[::2], parts[1::2])]
                y_tiles[tile, at, :] = parts[0]
                return held

            lax.fori_loop(0, span, step, tuple(starts), unroll=4)
        from_steps(rows, y_tiles, tile)
        context_ref[:, lane_tile(tile)] = rows[...].astype(bf16)


def whole_rows(block):
    return block.reshape(block.shape[0] * block.shape[1], block.shape[2])


def head(index):
    return slice(index * HD, (index + 1) * HD)


def weight_copies(pieces, buffer, place, sems, act):
    col_parts, row_parts = sems.shape
    for k in range(col_parts):
        for r in range(row_parts):
            inner = buffer.at[k, place[2] ^ r]
            act(pltpu.make_async_copy(pieces[k * row_parts + r], inner, sems.at[k, r]))


def of_heads(buffer, i):
    return jnp.concatenate([whole_rows(buffer[k, :, :, head(i)]) for k in range(buffer.shape[0])], axis=1)


def gradient_slot(row_parts, order, r):
    position = 0
    for bit in reversed(order):
        position = 2 * position + (1 if r & bit else 0)
    return position // (row_parts // 2), position % (row_parts // 2)


def round_orders(row_parts):
    bits = [1 << i for i in range(row_parts.bit_length() - 1)]
    return bits, bits[::-1]


def gradient_pieces(stacks, row_parts, far, slot):
    found = []
    for r in range(row_parts):
        sent, at = gradient_slot(row_parts, round_orders(row_parts)[far], r)
        found.append(stacks[2 * far + sent].at[at, slot])
    return found


def project_kernel(team, col_parts, row_parts, place, normed_ref, cot_ref, *refs):
    contexts, refs = refs[:team], refs[team:]
    count = col_parts * row_parts
    pieces, refs = refs[:count], refs[count:]
    context_t_ref, cot_t_ref, kept_ref = refs[:3]
    context_ref, weights, sems = refs[3:]
    weight_copies(pieces, weights, place, sems, lambda copy: copy.start())
    width = contexts[0].shape[1]
    for k in range(team):
        lanes = pl.ds(pl.multiple_of((place[0] ^ k) * width, LANES), width)
        context_ref[:, lanes] = contexts[k][...]
    context_t_ref[...] = context_ref[...].T
    cot_t_ref[...] = cot_ref[...].T
    weight_copies(pieces, weights, place, sems, lambda copy: copy.wait())
    kept_ref[0] = dot(normed_ref[...], of_heads(weights, 0)).astype(bf16)
    kept_ref[1] = dot(context_ref[...], of_heads(weights, 1)).astype(bf16)
    kept_ref[2] = dot(context_ref[...], of_heads(weights, 2)).astype(bf16)


def attend_kernel(team, col_parts, row_parts, place, kept_ref, *refs):
    count = col_parts * row_parts
    pieces, refs = refs[:count], refs[count:]
    part_ref, attended_ref, probs_ref, probs_t_ref, weights, sems = refs
    weight_copies(pieces, weights, place, sems, lambda copy: copy.start())
    length = kept_ref.shape[1]
    rows = lax.broadcasted_iota(jnp.int32, (length, length), 0)
    cols = lax.broadcasted_iota(jnp.int32, (length, length), 1)
    for h in range(col_parts):
        scores = dot_t(kept_ref[0, :, head(h)], kept_ref[1, :, head(h)]) * score_scale
        scores = jnp.where(rows >= cols, scores, -1e30)
        shifted = jnp.exp(scores - jnp.max(scores, axis=-1, keepdims=True))
        inverse = 1.0 / jnp.sum(shifted, axis=-1, keepdims=True)
        probs = (shifted * inverse).astype(bf16)
        probs_ref[h] = probs
        probs_t_ref[h] = probs.T
        attended_ref[:, head(h)] = dot(probs, kept_ref[2, :, head(h)]).astype(bf16)
    weight_copies(pieces, weights, place, sems, lambda copy: copy.wait())
    part_ref[...] = dot_t(attended_ref[...], of_heads(weights, 3)).astype(bf16)


def gelu_parts(hidden, grad_act):
    density = jnp.exp(-0.5 * hidden * hidden)
    t = 1.0 / (1.0 + (0.3275911 * math.sqrt(0.5)) * jnp.abs(hidden))
    series = 0.5 * 1.061405429
    for factor in (-1.453152027, 1.421413741, -0.284496736, 0.254829592):
        series = series * t + 0.5 * factor
    tail = series * t * density
    cdf = jnp.where(hidden >= 0.0, 1.0 - tail, tail)
    slope = cdf + hidden * density * (1.0 / math.sqrt(2.0 * math.pi))
    return (hidden * cdf).astype(bf16), (grad_act * slope).astype(bf16)


def middle_kernel(team, x_ref, gain_ref, *refs):
    parts, (middle_ref, normed_ref, normed_t_ref) = refs[:team], refs[team:]
    attn = parts[0][...].astype(f32)
    for part in parts[1:]:
        attn = attn + part[...].astype(f32)
    middle = x_ref[...].astype(f32) + attn
    middle_ref[...] = middle
    unit, unused = normalise(middle)
    normed_ref[...] = (unit * gain_ref[...]).astype(bf16)
    normed_t_ref[...] = normed_ref[...].T


def feed_kernel(team, col_parts, row_parts, place, normed_ref, normed_t_ref, cot_ref, cot_t_ref, *refs):
    arrays, refs = (refs[:row_parts], refs[row_parts : 2 * row_parts]), refs[2 * row_parts :]
    outs, two_ref, refs = refs[:team], refs[team], refs[team + 1 :]
    stacks, refs = (refs[:4], refs[4:8]), refs[8:]
    up_all, down_all, grad_up, grad_down, activated_all, grad_all, sems = refs
    z = pl.program_id(0)
    half = col_parts // 2
    hidden_cols = grad_up.shape[3]

    def copies(k):
        found = []
        for r in range(row_parts):
            for which, buffer in enumerate((up_all, down_all)):
                outside = arrays[which][r].at[k]
                inside = buffer.at[place[2] ^ r, :, pl.ds(k * hidden_cols, hidden_cols)]
                found.append(pltpu.make_async_copy(outside, inside, sems.at[which, k, r]))
        return found

    def each_leaving(k, act):
        for which, buffer in enumerate((grad_up, grad_down)):
            steps = lax.rem(place[6] + col_parts - k, col_parts)
            for far in range(2):

                @pl.when(steps // half == far)
                def leaves():
                    slot = lax.rem(steps, half)
                    for r, piece in enumerate(gradient_pieces(stacks[which], row_parts, far, slot)):
                        inner = buffer.at[k, place[2] ^ r]
                        act(pltpu.make_async_copy(inner, piece, sems.at[2 + which, k, r]))

    @pl.when(z == 0)
    def start():
        for k in range(col_parts):
            for copy in copies(k):
                copy.start()

    for k in range(col_parts):

        @pl.when(z == k)
        def arrive():
            for copy in copies(k):
                copy.wait()

    at = pl.ds(pl.multiple_of(z * hidden_cols, hidden_cols), hidden_cols)
    hidden = dot(normed_ref[...], whole_rows(up_all[:, :, at]))
    grad_act = dot(cot_ref[...], whole_rows(down_all[:, :, at]))
    activated, grad_pre = gelu_parts(hidden, grad_act)
    activated_all[:, at] = activated
    grad_all[:, at] = grad_pre
    shape = grad_up.shape[1:]
    grad_up[z] = dot(normed_t_ref[...], grad_pre).astype(bf16).reshape(shape)
    grad_down[z] = dot(cot_t_ref[...], activated).astype(bf16).reshape(shape)

    for k in range(col_parts):

        @pl.when(z == k)
        def leave():
            each_leaving(k, lambda copy: copy.start())

    @pl.when(z == col_parts - 1)
    def finish():
        two_ref[...] = dot_t(grad_all[...], whole_rows(up_all[...])).astype(bf16)
        rows = outs[0].shape[0]
        for k in range(team):
            at_rows = pl.ds(pl.multiple_of((place[0] ^ k) * rows, rows), rows)
            outs[k][...] = dot_t(activated_all[at_rows, :], whole_rows(down_all[...])).astype(bf16)
        for k in range(col_parts):
            each_leaving(k, lambda copy: copy.wait())


def attend_back_kernel(team, col_parts, row_parts, place, middle_ref, gain_ref, cot_ref, *refs):
    parts, refs = refs[:team], refs[team:]
    late, refs = refs[:3], refs[3:]
    count = col_parts * row_parts
    pieces, refs = refs[:count], refs[count:]
    middle_grad_ref, gain_grad_ref, one_ref, low = refs[:4]
    grad_q, grad_k, grad_v = refs[4:7]
    context_grads, refs = refs[7 : 7 + team], refs[7 + team :]
    weights, grad_out, total_low = refs[:3]
    held, (sems, late_sems) = refs[3:6], refs[6:]
    kept_ref, probs_ref, probs_t_ref = held
    weight_copies(pieces, weights, place, sems, lambda copy: copy.start())
    late_copies = [
        pltpu.make_async_copy(outside, inside, late_sems.at[i])
        for i, (outside, inside) in enumerate(zip(late, held))
    ]
    for copy in late_copies:
        copy.start()
    own_rows = middle_ref.shape[0] // team
    grad_two = parts[0][...].astype(f32)
    for part in parts[1:]:
        grad_two = grad_two + part[...].astype(f32)
    unit, inverse = normalise(middle_ref[...])
    grad_gain = grad_two * unit
    rows = lax.broadcasted_iota(jnp.int32, grad_gain.shape, 0)
    first = place[0] * own_rows
    mine = (rows >= first) & (rows < first + own_rows)
    gain_grad_ref[...] = jnp.sum(jnp.where(mine, grad_gain, 0.0), axis=0, keepdims=True)
    grad = cot_ref[...].astype(f32) + normalise_back(unit, inverse, grad_two * gain_ref[...])
    low[...] = grad.astype(bf16)
    for k in range(team):

        @pl.when(place[0] == k)
        def own():
            middle_grad_ref[...] = grad[k * own_rows : (k + 1) * own_rows, :]

    weight_copies(pieces, weights, place, sems, lambda copy: copy.wait())
    for copy in late_copies:
        copy.wait()
    grad_out[...] = dot(low[...], of_heads(weights, 3)).astype(bf16)
    for h in range(col_parts):
        q, k, v = (kept_ref[i, :, head(h)] for i in range(3))
        grad_heads = grad_out[:, head(h)]
        grad_v[:, head(h)] = dot(probs_t_ref[h], grad_heads).astype(bf16)
        probs = probs_ref[h].astype(f32)
        grad_probs = dot_t(grad_heads, v)
        inner = jnp.sum(grad_probs * probs, axis=-1, keepdims=True)
        grad_scores = (probs * (grad_probs - inner)).astype(bf16)
        grad_q[:, head(h)] = (dot(grad_scores, k) * score_scale).astype(bf16)
        turned = dot_t(v, grad_heads) - inner.T
        turned = (probs_t_ref[h].astype(f32) * turned).astype(bf16)
        grad_k[:, head(h)] = (dot(turned, q) * score_scale).astype(bf16)
    total = dot_t(grad_k[...], of_heads(weights, 1)) + dot_t(grad_v[...], of_heads(weights, 2))
    total_low[...] = total.astype(bf16)
    width = context_grads[0].shape[1]
    for k in range(team):
        lanes = pl.ds(pl.multiple_of((place[0] ^ k) * width, LANES), width)
        context_grads[k][...] = total_low[:, lanes]
    one_ref[...] = dot_t(grad_q[...], of_heads(weights, 0)).astype(bf16)


def head_grads_kernel(col_parts, row_parts, place, low, attended_ref, *refs):
    normed_t_ref, context_t_ref, grad_q, grad_k, grad_v = refs[:5]
    stacks, (grads, out_sems) = refs[5:9], refs[9:]
    half = col_parts // 2
    shape = (*grads.shape[1:3], HD)

    def put(i, grad):
        for h in range(col_parts):
            grads[h, :, :, head(i)] = grad[:, head(h)].astype(bf16).reshape(shape)

    put(0, dot(normed_t_ref[...], grad_q[...]))
    put(1, dot(context_t_ref[...], grad_k[...]))
    put(2, dot(context_t_ref[...], grad_v[...]))
    put(3, dot(low[...].T, attended_ref[...]))
    copies = []
    for k in range(col_parts):
        for r, piece in enumerate(gradient_pieces(stacks, row_parts, k // half, k % half)):
            copies.append(pltpu.make_async_copy(grads.at[k, place[2] ^ r], piece, out_sems.at[k, r]))
    for copy in copies:
        copy.start()
    for copy in copies:
        copy.wait()


def adjoint_kernel(team, logr_ref, *refs):
    parts = refs[:team]
    g_tiles, ends_ref, total_ref, rows = refs[team:]
    grad = parts[0][...].astype(f32)
    for part in parts[1:]:
        grad = grad + part[...].astype(f32)
    grad = grad.astype(bf16).astype(f32)
    tiles, length, unused = g_tiles.shape
    states = logr_ref.shape[0]
    span = length // SUBS
    for tile in range(tiles):
        rows[...] = grad[:, lane_tile(tile)]
        in_steps(g_tiles, tile, rows)
    before = (sub_index() * span).astype(f32)
    for tile in range(tiles):
        rate = jnp.exp(logr_ref[:, lane_tile(tile)])
        decay = jnp.exp(-rate)
        for first in range(0, states, GROUP):
            chosen = range(first, first + GROUP)
            decays = [spread(decay[n : n + 1]) for n in chosen]

            def step(i, held):
                g = g_tiles[tile, step_rows(span - 1 - i), :]
                later = []
                for d, (b, w) in zip(decays, held):
                    shrunk = d * b
                    later.append((g + shrunk, d * w + shrunk))
                return tuple(later)

            zero = no_state(g_tiles)
            held = lax.fori_loop(0, span, step, ((zero, zero),) * GROUP, unroll=4)
            for n, (b, w) in zip(chosen, held):
                ends_ref[0, n, :, lane_tile(tile)] = b
                ends_ref[1, n, :, lane_tile(tile)] = w
                shrink = jnp.exp(-before * rate[n : n + 1])
                total_ref[0, n : n + 1, lane_tile(tile)] = jnp.sum(
                    shrink * b, axis=0, keepdims=True
                )
                total_ref[1, n : n + 1, lane_tile(tile)] = jnp.sum(
                    shrink * (w + before * b), axis=0, keepdims=True
                )


def context_back_kernel(
    team, place, g_tiles, u_tiles, ends_ref, all_ref, logr_ref, coef_ref, one_ref, *refs
):
    pieces = refs[:team]
    grad_ssm_ref, y_tiles, full, rows = refs[team:]
    tiles, length, unused = u_tiles.shape
    states = logr_ref.shape[0]
    span = length // SUBS
    width = tiles * LANES
    index = sub_index()
    after = ((SUBS - 1 - index) * span).astype(f32)
    full[...] = one_ref[...].astype(f32)
    group = GROUP
    for tile in range(tiles):
        lanes = lane_tile(tile)
        rate = jnp.exp(logr_ref[:, lanes])
        decay = jnp.exp(-rate)
        root = jnp.sqrt(2.0 * rate)
        scale = coef_ref[:, lanes] * root
        in_b = jnp.zeros((states, LANES), f32)
        in_w = jnp.zeros((states, LANES), f32)
        for j in range(all_ref.shape[0]):
            gap = j - place[1] - 1
            distance = (jnp.maximum(gap, 0) * length).astype(f32)
            shrink = jnp.exp(-distance * rate)
            b, w = all_ref[j, 0, :, lanes].astype(f32), all_ref[j, 1, :, lanes].astype(f32)
            in_b = in_b + jnp.where(gap >= 0, shrink * b, 0.0)
            in_w = in_w + jnp.where(gap >= 0, shrink * (w + distance * b), 0.0)
        for first in range(0, states, group):
            chosen = range(first, first + group)
            starts = []
            for n in chosen:
                row = rate[n : n + 1]
                b, w = ends_ref[0, n, :, lanes], ends_ref[1, n, :, lanes]
                for d in (1, 2, 4):
                    shrink = jnp.exp(-(d * span) * row)
                    next_b = pltpu.roll(b, SUBS - d, 0)
                    next_w = pltpu.roll(w, SUBS - d, 0)
                    inside = index < SUBS - d
                    b, w = (
                        b + jnp.where(inside, shrink * next_b, 0.0),
                        w + jnp.where(inside, shrink * (next_w + (d * span) * next_b), 0.0),
                    )
                inside = index < SUBS - 1
                b = jnp.where(inside, pltpu.roll(b, SUBS - 1, 0), 0.0)
                w = jnp.where(inside, pltpu.roll(w, SUBS - 1, 0), 0.0)
                shrink = jnp.exp(-after * row)
                b_row, w_row = in_b[n : n + 1], in_w[n : n + 1]
                b = b + shrink * b_row
                w = w + shrink * (w_row + after * b_row)
                zero = no_state(u_tiles)
                starts.append((b, w, zero, zero))
            decays = [spread(decay[n : n + 1]) for n in chosen]
            scales = [spread(scale[n : n + 1]) for n in chosen]

            def step(i, held):
                at = step_rows(span - 1 - i)
                g = g_tiles[tile, at, :]
                u = u_tiles[tile, at, :]
                later, parts = [], []
                for d, s, (b, w, sum_b, sum_w) in zip(decays, scales, held):
                    shrunk = d * b
                    w = d * w + shrunk
                    b = g + shrunk
                    later.append((b, w, sum_b + u * b, sum_w + u * w))
                    parts.append(s * b)
                while len(parts) > 1:
                    parts = [p + q for p, q in zip(parts[::2], parts[1::2])]
                if first > 0:
                    parts[0] = parts[0] + y_tiles[tile, at, :]
                y_tiles[tile, at, :] = parts[0]
                return tuple(later)

            held = lax.fori_loop(0, span, step, tuple(starts), unroll=2)
            for n, (unused_b, unused_w, sum_b, sum_w) in zip(chosen, held):
                sum_b = jnp.sum(sum_b, axis=0, keepdims=True)
                sum_w = jnp.sum(sum_w, axis=0, keepdims=True)
                row = slice(n, n + 1)
                grad_ssm_ref[0, row, lanes] = root[row] * sum_b
                grad_ssm_ref[1, row, lanes] = scale[row] * (0.5 * sum_b - rate[row] * sum_w)
        at_lanes = pl.ds(pl.multiple_of(place[0] * width + tile * LANES, LANES), LANES)
        from_steps(rows, y_tiles, tile)
        full[:, at_lanes] += rows[...].astype(bf16).astype(f32)
    count = pieces[0].shape[0]
    for k in range(team):
        at_rows = pl.ds(pl.multiple_of((place[0] ^ k) * count, count), count)
        pieces[k][...] = full[at_rows, :].astype(bf16)


def input_grad_kernel(team, place, x_ref, gain_ref, middle_grad_ref, *refs):
    parts, (out_ref, gain_grad_ref) = refs[:team], refs[team:]
    rows = out_ref.shape[0]
    at_rows = pl.ds(pl.multiple_of(place[0] * rows, rows), rows)
    grad_one = parts[0][...].astype(f32)
    for part in parts[1:]:
        grad_one = grad_one + part[...].astype(f32)
    unit, inverse = normalise(x_ref[at_rows, :].astype(f32))
    gain_grad_ref[...] = jnp.sum(grad_one * unit, axis=0, keepdims=True)
    back = normalise_back(unit, inverse, grad_one * gain_ref[...])
    out_ref[...] = (middle_grad_ref[...] + back).astype(bf16)


def assemble_kernel(halves, low_count, place, own_ref, *refs):
    others, out_ref = refs[:-1], refs[-1]
    count, rows, unused = own_ref.shape
    half = place[4]

    def put(value, sequence, which, member):
        at_rows = pl.ds(pl.multiple_of((which * low_count + member) * rows, rows), rows)
        out_ref[sequence, at_rows, :] = value.astype(out_ref.dtype)

    for sequence in range(count // (halves * low_count)):
        if halves == 1:
            for member in range(low_count):
                put(own_ref[sequence * low_count + member], sequence, 0, member)
        else:
            put(own_ref[sequence * halves + half], sequence, half, 0)
            put(others[0][sequence], sequence, 1 - half, 0)


def pack_kernel(halves, place, qkv_ref, out_ref, up_ref, down_ref, *refs):
    rows = up_ref.shape[0]
    heads, hidden = out_ref.shape[0] // halves, up_ref.shape[1] // halves
    for which in range(halves):
        side = place[4] if which == 0 else 1 - place[4]
        at_heads = pl.ds(pl.multiple_of(side * heads, LANES), heads)
        at_hidden = pl.ds(pl.multiple_of(side * hidden, LANES), hidden)
        if which == 0:
            head_ref, wide_ref, deep_ref = refs[:3]
        else:
            packed = refs[3]
            head_ref = packed.at[:, : 4 * heads]
            wide_ref = packed.at[:, 4 * heads : 4 * heads + hidden]
            deep_ref = packed.at[:, 4 * heads + hidden :]
        for i in range(3):
            head_ref[:, i * heads : (i + 1) * heads] = qkv_ref[i, :, at_heads].astype(bf16)
        head_ref[:, 3 * heads :] = out_ref[at_heads, :].T.astype(bf16)
        wide_ref[...] = up_ref[:, at_hidden].astype(bf16)
        deep_ref[...] = down_ref[at_hidden, :].T.astype(bf16)


def small_kernel(ssm_ref, gains_ref, out_ref):
    count = ssm_ref.shape[0]
    out_ref[:count, :] = ssm_ref[...]
    out_ref[count:, :] = gains_ref[...]


def lamb_moments(weight, grad_item, first_old, second_old):
    first_new = beta_first * first_old + (1.0 - beta_first) * grad_item
    second_new = beta_second * second_old + (1.0 - beta_second) * grad_item * grad_item
    direction = (
        first_new
        / (1.0 - beta_first**STEP)
        / (jnp.sqrt(second_new / (1.0 - beta_second**STEP)) + lamb_eps)
        + weight_decay * weight
    )
    return (first_new, second_new, direction)


def place_sums(sums_ref, sums):
    rows = lax.broadcasted_iota(jnp.int32, sums_ref.shape, 0)
    lanes = lax.broadcasted_iota(jnp.int32, sums_ref.shape, 1)
    found = jnp.zeros(sums_ref.shape, f32)
    for index, pair in sums.items():
        for row, value in enumerate(pair):
            found = jnp.where((rows == row) & (lanes == index), value, found)
    sums_ref[...] = found


def moments_kernel(halves, matrices, place, *refs):
    count = 1 + max(item[1] for item in matrices)
    grads, refs = [refs[halves * i : halves * (i + 1)] for i in range(count)], refs[halves * count :]
    arrays = len({(item[1], item[4] is None) for item in matrices})
    ins = [refs[3 * i : 3 * i + 3] for i in range(arrays)]
    outs = [refs[3 * (arrays + i) : 3 * (arrays + i) + 3] for i in range(arrays)]
    sums_ref = refs[6 * arrays]
    keys = []
    sums = {}
    for number, source, column, turned, stacked in matrices:
        key = (source, stacked is None)
        if key not in keys:
            keys.append(key)
        pick = (lambda ref: ref) if stacked is None else (lambda ref, i=stacked: ref.at[i])
        weight, first, second = (pick(ref) for ref in ins[keys.index(key)])
        news = [pick(ref) for ref in outs[keys.index(key)]]
        width = weight.shape[0 if turned else 1] // halves
        rows = weight.shape[1 if turned else 0]
        cols = slice(column * width, (column + 1) * width)
        total_weight = total_update = 0.0
        for which, grad_ref in enumerate(grads[source]):
            side = place[4] if which == 0 else 1 - place[4]
            at = pl.ds(pl.multiple_of(side * width, width), width)
            if which == 0:
                grad = grad_ref[pl.ds(pl.multiple_of(side * rows, rows), rows), cols].astype(f32)
            else:
                grad = grad_ref[:, cols].astype(f32)
            at = (at, slice(None)) if turned else (slice(None), at)
            grad = grad.T if turned else grad
            old = weight[at]
            found = lamb_moments(old, grad, first[at], second[at])
            for ref, value in zip(news, found):
                ref[at] = value
            total_weight = total_weight + jnp.sum(old * old)
            total_update = total_update + jnp.sum(found[2] * found[2])
        sums[number] = (total_weight, total_update)
    place_sums(sums_ref, sums)


def small_moments_kernel(numbers, grads_ref, *refs):
    ins, outs, sums_ref = (refs[:3], refs[3:6]), (refs[6:9], refs[9:12]), refs[12]
    states = (grads_ref.shape[0] - 2) // 2
    sums = {}
    for (weight, first, second), news, start, rows, first_number in (
        (ins[0], outs[0], 2 * states, 1, numbers[0]),
        (ins[1], outs[1], 0, states, numbers[1]),
    ):
        for i in range(2):
            grad = grads_ref[start + i * rows : start + (i + 1) * rows, :]
            at = slice(i * rows, (i + 1) * rows)
            found = lamb_moments(weight[at, :], grad, first[at, :], second[at, :])
            for ref, value in zip(news, found):
                ref[at, :] = value
            sums[first_number + i] = (
                jnp.sum(weight[at, :] * weight[at, :]),
                jnp.sum(found[2] * found[2]),
            )
    place_sums(sums_ref, sums)


def update_kernel(stacks, sums_ref, *refs):
    count = len(stacks)
    weights, directions, news = refs[:count], refs[count : 2 * count], refs[2 * count : 3 * count]
    norms = jnp.sqrt(jnp.sum(sums_ref[...], axis=0))
    refs[3 * count][...] = norms
    ratios = norms[0:1] / norms[1:2]
    lanes = lax.broadcasted_iota(jnp.int32, ratios.shape, 1)
    for numbers, weight, direction, new in zip(stacks, weights, directions, news):
        step = weight.shape[0] // len(numbers)
        for i, number in enumerate(numbers):
            ratio = jnp.sum(jnp.where(lanes == number, ratios, 0.0), axis=1, keepdims=True)
            at = slice(i * step, (i + 1) * step)
            scale = learn_rate * ratio.reshape((1,) * weight.ndim)
            new[at] = weight[at] - scale * direction[at]


def call(
    body, ins, outs, scratch=(), grid=None, in_specs=None, out_specs=None, time=1.0, after=(), token=False
):
    moved = sum(a.size * a.dtype.itemsize for a in list(ins) + list(outs))
    params = pltpu.CompilerParams(vmem_limit_bytes=VMEM_BYTES)
    cost = pl.CostEstimate(flops=int(time * 1.15e9), bytes_accessed=moved, transcendentals=0)
    whole = pl.BlockSpec(memory_space=pltpu.VMEM)
    anywhere = pl.BlockSpec(memory_space=pl.ANY)
    in_specs = list(in_specs or [whole] * len(ins)) + [anywhere] * len(after)
    out_specs = list(out_specs or [whole] * len(outs))
    outs = list(outs)
    first_out = len(ins) + len(after)
    last_out = first_out + len(outs)
    if token:
        outs.append(jax.ShapeDtypeStruct((SUBS, LANES), f32))
        out_specs.append(whole)

    def run(*refs):
        refs = list(refs)
        if token:
            refs[last_out][...] = jnp.zeros((SUBS, LANES), f32)
            del refs[last_out]
        body(*refs[: len(ins)], *refs[first_out:])

    return pl.pallas_call(
        run,
        out_shape=tuple(outs),
        in_specs=in_specs,
        out_specs=tuple(out_specs),
        scratch_shapes=list(scratch),
        compiler_params=params,
        cost_estimate=cost,
        **({} if grid is None else {"grid": grid}),
    )(*ins, *after)


def shaped(shape, kind):
    return jax.ShapeDtypeStruct(tuple(shape), kind)


def on_device(
    tokens,
    cotangent,
    w_qkv,
    w_out,
    w_up,
    w_down,
    norm_gains,
    ssm_param,
    first_qkv,
    second_qkv,
    first_out,
    second_out,
    first_up,
    second_up,
    first_down,
    second_down,
    first_gain,
    second_gain,
    first_ssm,
    second_ssm,
):
    halves = lax.axis_size("sl")
    low_count = lax.axis_size("ml")
    row_parts = lax.axis_size("sh")
    col_parts = lax.axis_size("mb") * lax.axis_size("mq")
    team = halves * low_count
    sl, ml, mb, mq = (lax.axis_index(name) for name in ("sl", "ml", "mb", "mq"))
    rank = sl * low_count + ml
    block_index = lax.axis_index("sh") * halves + mq
    seq_total, length, width = tokens.shape
    assert length == BLK and seq_total == lax.axis_size("mb")
    states = ssm_param.shape[1]
    channels = width // team
    tiles = channels // LANES
    row_count = width // row_parts
    own_rows = length // team
    place = [rank, block_index, lax.axis_index("sh"), lax.axis_index(MODEL), sl, sl ^ mq]
    place.append(lax.axis_index(COLS))
    place = jnp.stack(place).astype(jnp.int32)
    smem = pl.BlockSpec(memory_space=pltpu.SMEM)
    vmem = pl.BlockSpec(memory_space=pltpu.VMEM)

    def permute(value, axes, moves):
        return lax.ppermute(value, axes, moves)

    def swap(value):
        return permute(value, "sl", [(0, 1), (1, 0)])

    def in_order(own, other, axis):
        return jnp.where(
            sl == 0, jnp.concatenate([own, other], axis), jnp.concatenate([other, own], axis)
        )

    def team_send(pieces):
        moved = [pieces[0]]
        for k in range(1, team):
            moved.append(permute(pieces[k], TEAM, [(i, i ^ k) for i in range(team)]))
        return moved

    def pick_block(array):
        own = lax.dynamic_index_in_dim(array, mb, 0, keepdims=False)
        if halves == 1:
            return own, ()
        other = swap(own)
        return jnp.where(sl == mq, own, other), (other,)

    def across(value, bit):
        return permute(value, "sh", [(i, i ^ bit) for i in range(row_parts)])

    def along(value, axes, step):
        count = lax.axis_size(axes)
        return permute(value, axes, [(i, (i + step) % count) for i in range(count)])

    bits = [1 << i for i in range(row_parts.bit_length() - 1)]

    def bit_order(k):
        return bits if k % 2 == 0 else bits[::-1]

    def double_rows(value, order):
        found = {0: value}
        for bit in order:
            for r in list(found):
                found[r | bit] = across(found[r], bit)
        return [found[r] for r in range(row_parts)]

    def add(*items, zero=None):
        total = sum(item.astype(f32) for item in items)
        return (total if zero is None else total + zero[0, 0]).astype(bf16)

    def first_messages(stacks):
        return across(stacks[1], bits[-1]), across(stacks[3], bits[0])

    def halve_rows(keep, arrived, order, zero, after):
        items = [keep, arrived]
        for bit in order[-2::-1]:
            count = arrived.shape[0] // 2
            sent = add(*[item[count:] for item in items], zero=zero)
            arrived = across(hold((sent,), after)[0] if after else sent, bit)
            items = [item[:count] for item in items] + [arrived]
        return add(*[item[0] for item in items])

    def halve_both(stacks, first, zero, after=()):
        near = halve_rows(stacks[0], first[0], bits, zero, after)
        return near, halve_rows(stacks[2], first[1], bits[::-1], zero, after)

    def hold(arrays, after):
        anywhere = pl.BlockSpec(memory_space=pl.ANY)
        return pl.pallas_call(
            lambda *refs: None,
            out_shape=tuple(shaped(item.shape, item.dtype) for item in arrays),
            in_specs=[anywhere] * (len(arrays) + len(after)),
            out_specs=(anywhere,) * len(arrays),
            input_output_aliases={i: i for i in range(len(arrays))},
        )(*arrays, *after)

    def ring_gather(shard):
        pieces, held = [], shard
        for k in range(col_parts):
            if k > 0:
                held = along(held, COLS, 1)
            pieces.append(double_rows(held, bits if k % 2 == 0 else bits[::-1]))
        return pieces

    def sum_over_z(near, far, ring=True):
        if not ring:
            pieces = [stack[k] for stack in (near, far) for k in range(col_parts // 2)]
            moved = [along(piece, COLS, -k) for k, piece in enumerate(pieces) if k > 0]
            return add(pieces[0], *moved)
        held = None
        for stack in (far, near):
            for k in reversed(range(stack.shape[0])):
                held = stack[k] if held is None else add(stack[k], along(held, COLS, -1))
        return held

    def everywhere(value, axes):
        count = lax.axis_size(axes)
        copies = jnp.broadcast_to(value[None], (count, *value.shape))
        return lax.all_to_all(copies, axes, 0, 0, tiled=True)

    rows_dev = w_up.shape[0]
    hidden_cols = w_up.shape[1] // halves
    head_cols = 4 * w_out.shape[0] // halves
    packed_cols = head_cols + 2 * hidden_cols
    sides = [shaped((rows_dev, cols), bf16) for cols in (head_cols, hidden_cols, hidden_cols)]
    shards = call(
        functools.partial(pack_kernel, halves),
        (place, w_qkv, w_out, w_up, w_down),
        sides + [shaped((rows_dev, packed_cols), bf16)] * (halves - 1),
        time=2.4,
        in_specs=[smem] + [vmem] * 4,
    )
    if halves == 2:
        other = swap(shards[3])
        cuts = (0, head_cols, head_cols + hidden_cols, packed_cols)
        shards = [
            in_order(own, other[:, first:last], 0)
            for own, first, last in zip(shards, cuts, cuts[1:])
        ]
    head_shard, up_shard, down_shard = shards[:3]
    small, = call(
        small_kernel,
        (ssm_param.reshape(2 * states, -1), norm_gains),
        (shaped((2 * states + 2, norm_gains.shape[1]), f32),),
        after=(head_shard,),
    )
    small = jnp.transpose(everywhere(small, ALL), (1, 0, 2)).reshape(2 * states + 2, width)
    own_ssm = lax.dynamic_slice_in_dim(
        small[: 2 * states].reshape(2, states, width), rank * channels, channels, 2
    )
    coef, logr = own_ssm[0], own_ssm[1]
    gain_one = small[2 * states : 2 * states + 1]
    gain_two = small[2 * states + 1 : 2 * states + 2]

    attn_w = ring_gather(head_shard)
    up_shard, down_shard = hold((up_shard, down_shard), (attn_w[-1][0], small, *attn_w[0][1:-1]))
    up_full = lax.all_gather(up_shard, COLS, axis=0, tiled=False)
    down_full = lax.all_gather(down_shard, COLS, axis=0, tiled=False)
    up_w = double_rows(up_full, bits)
    down_w = double_rows(down_full, bits[::-1])
    attn_flat = [piece for group in attn_w for piece in group]

    x, unused = pick_block(tokens)
    cot, cot_other = pick_block(cotangent)

    anywhere = [pl.BlockSpec(memory_space=pl.ANY)]

    def fixed(*shape):
        return pl.BlockSpec(shape, lambda z: (0,) * len(shape))

    wide = fixed(length, width)
    row = fixed(1, width)

    normed_one, normed_t, u_steps, ends, total = call(
        norm_kernel,
        (place, x, gain_one, logr),
        (
            shaped((length, width), bf16),
            shaped((width, length), bf16),
            shaped((tiles, length, LANES), f32),
            shaped((states, SUBS, channels), f32),
            shaped((states, channels), f32),
        ),
        scratch=[pltpu.VMEM((length, LANES), f32)],
        in_specs=[smem, vmem, vmem, vmem],
        after=(*attn_w[0][1:-1], attn_w[1][0], *cot_other),
        time=5,
    )
    totals = everywhere(total.astype(bf16), ("sh", "mq"))
    (context_own,) = call(
        context_kernel,
        (place, u_steps, ends, totals, logr, coef),
        (shaped((length, channels), bf16),),
        after=(attn_w[0][-1], *attn_w[1][1:-1], attn_w[-1][0]),
        scratch=[pltpu.VMEM((tiles, length, LANES), f32), pltpu.VMEM((length, LANES), f32)],
        in_specs=[smem] + [vmem] * 5,
        time=7,
    )
    contexts = team_send([context_own] * team)

    stack_shape = (row_parts // 2, col_parts // 2, row_count)
    head_stacks = [shaped((*stack_shape, head_cols), bf16)] * 4
    hidden_stacks = [shaped((*stack_shape, hidden_cols), bf16)] * 8
    sizes = (team, col_parts, row_parts)
    head_buffer = pltpu.VMEM((col_parts, row_parts, row_count, 4 * HD), bf16)
    head_sems = pltpu.SemaphoreType.DMA((col_parts, row_parts))
    kept_shape = shaped((3, length, col_parts * HD), bf16)
    flat_shape = shaped((length, col_parts * HD), bf16)
    context_t, cot_t, kept = call(
        functools.partial(project_kernel, *sizes),
        (place, normed_one, cot, *contexts, *attn_flat),
        (shaped((width, length), bf16), shaped((width, length), bf16), kept_shape),
        scratch=[pltpu.VMEM((length, width), bf16), head_buffer, head_sems],
        time=1,
        in_specs=[smem] + [vmem] * (2 + team) + anywhere * len(attn_flat),
        after=(up_full,),
    )
    attn_part, attended, probs, probs_t = call(
        functools.partial(attend_kernel, *sizes),
        (place, kept, *attn_flat),
        (
            shaped((length, width), bf16),
            flat_shape,
            *[shaped((col_parts, length, length), bf16)] * 2,
        ),
        scratch=[head_buffer, head_sems],
        time=1,
        in_specs=[smem, vmem] + anywhere * len(attn_flat),
        after=up_w[1:-1],
    )
    attn_parts = team_send([attn_part] * team)

    middle, normed_two, normed_two_t = call(
        functools.partial(middle_kernel, team),
        (x, gain_two, *attn_parts),
        (shaped((length, width), f32), shaped((length, width), bf16), shaped((width, length), bf16)),
        time=1,
        after=(up_w[-1], *down_w[1:-1]),
    )
    weight_buffer = pltpu.VMEM((row_parts, row_count, col_parts * hidden_cols), bf16)
    grad_buffer = pltpu.VMEM((col_parts, row_parts, row_count, hidden_cols), bf16)
    fed = call(
        functools.partial(feed_kernel, team, col_parts, row_parts),
        (place, normed_two, normed_two_t, cot, cot_t, *up_w, *down_w),
        (
            *[shaped((own_rows, width), bf16)] * team,
            shaped((length, width), bf16),
            *hidden_stacks,
        ),
        scratch=[
            *[weight_buffer] * 2,
            *[grad_buffer] * 2,
            *[pltpu.VMEM((length, col_parts * hidden_cols), bf16)] * 2,
            pltpu.SemaphoreType.DMA((4, col_parts, row_parts)),
        ],
        time=18,
        grid=(col_parts,),
        in_specs=[smem, wide, fixed(width, length), wide, fixed(width, length)]
        + anywhere * (2 * row_parts),
        out_specs=[fixed(own_rows, width)] * team + [wide] + anywhere * 8,
    )
    out_pieces, two_part, hidden_grads = fed[:team], fed[team], fed[team + 1 :]
    two_parts = team_send([two_part] * team)

    def rows_of(array, member):
        return lax.dynamic_slice_in_dim(array, member * own_rows, own_rows, 0)

    def share_rows(pieces, kind):
        others = []
        if halves == 2:
            pairs = pieces.reshape(seq_total, halves, own_rows, width)
            others = [swap(lax.dynamic_index_in_dim(pairs, 1 - sl, 1, keepdims=False))]
        (blocks,) = call(
            functools.partial(assemble_kernel, halves, low_count),
            (place, pieces, *others),
            (shaped((seq_total, length, width), kind),),
            time=3.5,
            in_specs=[smem, vmem] + [vmem] * len(others),
        )
        return blocks

    out_pieces = team_send(list(out_pieces))
    result = rows_of(middle, rank) + sum(item.astype(f32) for item in out_pieces)
    result = result.astype(bf16)
    layer_pieces = lax.all_gather(result, MODEL, axis=0, tiled=False)
    layer_out = share_rows(layer_pieces, bf16)

    def both_halves(own):
        if halves == 1:
            return [own]
        return [own, swap(lax.dynamic_slice_in_dim(own, (1 - sl) * rows_dev, rows_dev, 0))]

    middle_grad, gain_two_grad, one_part, low_grad, *rest = call(
        functools.partial(attend_back_kernel, *sizes),
        (place, middle, gain_two, cot, *two_parts, kept, probs, probs_t, *attn_flat),
        (
            shaped((own_rows, width), f32),
            shaped((1, width), f32),
            shaped((length, width), bf16),
            shaped((length, width), bf16),
            *[flat_shape] * 3,
            *[shaped((length, channels), bf16)] * team,
        ),
        scratch=[
            head_buffer,
            pltpu.VMEM(flat_shape.shape, bf16),
            pltpu.VMEM((length, width), bf16),
            pltpu.VMEM(kept_shape.shape, bf16),
            *[pltpu.VMEM((col_parts, length, length), bf16)] * 2,
            head_sems,
            pltpu.SemaphoreType.DMA((3,)),
        ],
        time=1,
        in_specs=[smem] + [vmem] * (3 + team) + anywhere * (3 + len(attn_flat)),
        after=(result,),
    )
    head_grads, context_grads = rest[:3], rest[3:]
    context_grads = team_send(context_grads)
    *head_stacks, heads_done = call(
        functools.partial(head_grads_kernel, col_parts, row_parts),
        (place, low_grad, attended, normed_t, context_t, *head_grads),
        head_stacks,
        scratch=[head_buffer, head_sems],
        time=8,
        in_specs=[smem] + [vmem] * 7,
        out_specs=anywhere * 4,
        token=True,
    )
    down_first = first_messages(hidden_grads[4:])
    g_steps, adjoint_ends, adjoint_total, adjoint_done = call(
        functools.partial(adjoint_kernel, team),
        (logr, *context_grads),
        (
            shaped((tiles, length, LANES), f32),
            shaped((2, states, SUBS, channels), f32),
            shaped((2, states, channels), f32),
        ),
        scratch=[pltpu.VMEM((length, LANES), f32)],
        time=1,
        after=(*down_first, heads_done),
        token=True,
    )
    adjoint_totals = everywhere(adjoint_total.astype(bf16), ("sh", "mq"))
    up_stacks = list(hidden_grads[:4])
    down_sums = halve_both(hidden_grads[4:], down_first, adjoint_done, (adjoint_totals,))
    up_stacks[1::2] = hold(up_stacks[1::2], (adjoint_totals,))
    up_first = first_messages(up_stacks)
    *one_pieces, grad_ssm = call(
        functools.partial(context_back_kernel, team),
        (place, g_steps, u_steps, adjoint_ends, adjoint_totals, logr, coef, one_part),
        (
            *[shaped((own_rows, width), bf16)] * team,
            shaped((2, states, channels), f32),
        ),
        scratch=[
            pltpu.VMEM((tiles, length, LANES), f32),
            pltpu.VMEM((length, width), f32),
            pltpu.VMEM((length, LANES), f32),
        ],
        in_specs=[smem] + [vmem] * 7,
        time=1,
    )
    one_pieces = team_send(one_pieces)
    grad_rows, gain_one_grad, rows_done = call(
        functools.partial(input_grad_kernel, team),
        (place, x, gain_one, middle_grad, *one_pieces),
        (shaped((own_rows, width), bf16), shaped((1, width), f32)),
        in_specs=[smem] + [vmem] * (3 + team),
        time=1,
        after=(layer_pieces, *up_first, *down_sums),
        token=True,
    )
    grad_down = sum_over_z(*down_sums, False)
    head_stacks[1::2] = hold(head_stacks[1::2], (grad_rows,))
    head_sums = halve_both(head_stacks, first_messages(head_stacks), rows_done)
    up_sums = halve_both(up_stacks, up_first, rows_done)
    grad_up = sum_over_z(*up_sums)
    grad_heads = sum_over_z(*head_sums)
    input_grad = share_rows(lax.all_gather(grad_rows, MODEL, axis=0, tiled=False), f32)

    placed_ssm = lax.dynamic_update_slice_in_dim(
        jnp.zeros((2 * states, width), f32),
        grad_ssm.reshape(2 * states, channels),
        rank * channels,
        1,
    )
    small_grads = jnp.concatenate([placed_ssm, gain_one_grad, gain_two_grad], 0)
    (small_grads,) = hold((small_grads,), head_sums)
    small_grads = small_grads.reshape(2 * states + 2, lax.axis_size(ALL), -1)
    small_grads = lax.all_to_all(jnp.transpose(small_grads, (1, 0, 2)), ALL, 0, 0, tiled=True)
    small_grads = jnp.sum(small_grads, axis=0)

    def moments(matrices, grads, arrays, after=()):
        changed = [shaped(old.shape, f32) for group in arrays for old in group]
        grad_parts = [part for grad in grads for part in both_halves(grad)]
        ins = [item for group in arrays for item in group]
        *found, sums = call(
            functools.partial(moments_kernel, halves, matrices),
            (place, *grad_parts, *ins),
            (*changed, shaped((2, LANES), f32)),
            in_specs=[smem] + [vmem] * (len(grad_parts) + len(ins)),
            after=after,
            time=4,
        )
        return [found[3 * i : 3 * i + 3] for i in range(len(arrays))], sums

    hidden_new, hidden_sums = moments(
        ((4, 0, 0, False, None), (5, 1, 0, True, None)),
        (grad_up, grad_down),
        ((w_up, first_up, second_up), (w_down, first_down, second_down)),
    )
    heads_new, head_sums = moments(
        tuple((i, 0, i, False, i) for i in range(3)) + ((3, 0, 3, True, None),),
        (grad_heads,),
        ((w_qkv, first_qkv, second_qkv), (w_out, first_out, second_out)),
        (layer_out, input_grad),
    )
    own_channels = norm_gains.shape[1]
    ssm_items = [item.reshape(2 * states, own_channels) for item in (ssm_param, first_ssm, second_ssm)]
    small_items = [norm_gains, first_gain, second_gain, *ssm_items]
    *small_new, small_sums = call(
        functools.partial(small_moments_kernel, (6, 8)),
        (small_grads.reshape(2 * states + 2, own_channels), *small_items),
        (*[shaped(item.shape, f32) for item in small_items], shaped((2, LANES), f32)),
    )
    all_sums = everywhere(hidden_sums + head_sums + small_sums, ALL)
    masters = (w_qkv, w_out, w_up, w_down, norm_gains, ssm_items[0])
    news = (*heads_new, *hidden_new, small_new[:3], small_new[3:])
    *weights, norms = call(
        functools.partial(update_kernel, ((0, 1, 2), (3,), (4,), (5,), (6, 7), (8, 9))),
        (all_sums, *masters, *[group[2] for group in news]),
        (*[shaped(item.shape, f32) for item in masters], shaped((2, LANES), f32)),
        time=3.2,
    )
    outputs = [layer_out, input_grad]
    for index, (weight, (first_new, second_new, unused)) in enumerate(zip(weights, news)):
        if index == 4:
            outputs += [weight, first_new, second_new[0], second_new[1]]
        else:
            kept_shape = ssm_param.shape if index == 5 else weight.shape
            outputs += [item.reshape(kept_shape) for item in (weight, first_new, second_new)]
    outputs.append(norms[:, :10])
    return tuple(outputs)


def solution(mesh):
    seq_count, model_count = mesh.shape["seq"], mesh.shape["mp"]
    halves = 2 if HEADS // model_count >= 2 else 1
    sizes = (seq_count // halves, halves, SEQS, halves, model_count // (SEQS * halves))
    fine = Mesh(mesh.devices.reshape(sizes), ALL)
    seq, model = ("sh", "sl"), ("mb", "mq", "ml")
    rows_cols, cols_rows = P(seq, model), P(model, seq)
    token = P(None, seq, None)
    stack = P(None, seq, model)
    gains = P(None, ALL)
    ssm = P(None, None, ALL)
    return jax.shard_map(
        on_device,
        mesh=fine,
        in_specs=(token, token, stack, cols_rows, rows_cols, cols_rows, gains, ssm)
        + (stack,) * 2
        + (cols_rows,) * 2
        + (rows_cols,) * 2
        + (cols_rows,) * 2
        + (gains,) * 2
        + (ssm,) * 2,
        out_specs=(token, token)
        + (stack,) * 3
        + (cols_rows,) * 3
        + (rows_cols,) * 3
        + (cols_rows,) * 3
        + (gains, gains, P(ALL), P(ALL))
        + (ssm,) * 3
        + (P(),),
        check_vma=False,
    )
```

```python
import functools
import math

import jax
import jax.numpy as jnp
from jax import lax
from jax.experimental import pallas as pl
from jax.experimental.pallas import tpu as pltpu
from jax.sharding import Mesh
from jax.sharding import PartitionSpec as P

HD = 128
HEADS = 8
BLK = 512
STEP = 10
SEQS = 2
LANES = 128
SUBS = 8
GROUP = 8

norm_eps = 1e-05
beta_first = 0.9
beta_second = 0.999
lamb_eps = 1e-06
weight_decay = 0.01
learn_rate = 0.5
score_scale = HD ** (-0.5)

f32 = jnp.float32
bf16 = jnp.bfloat16
VMEM_BYTES = 56 * 1024 * 1024

ALL = ("sh", "sl", "mb", "mq", "ml")
MODEL = ("mb", "mq", "ml")
COLS = ("mb", "mq")
TEAM = ("sl", "ml")


def dot(left, right):
    return lax.dot_general(left, right, (((1,), (0,)), ((), ())), preferred_element_type=f32)


def dot_t(left, right):
    return lax.dot_general(left, right, (((1,), (1,)), ((), ())), preferred_element_type=f32)


def normalise(values):
    centred = values - jnp.mean(values, axis=-1, keepdims=True)
    inverse = lax.rsqrt(jnp.mean(centred * centred, axis=-1, keepdims=True) + norm_eps)
    return centred * inverse, inverse


def normalise_back(unit, inverse, grad_unit):
    mean_one = jnp.mean(grad_unit, axis=-1, keepdims=True)
    mean_two = jnp.mean(grad_unit * unit, axis=-1, keepdims=True)
    return inverse * (grad_unit - mean_one - unit * mean_two)


def sub_index():
    return lax.broadcasted_iota(jnp.int32, (SUBS, LANES), 0)


def spread(row):
    return jnp.broadcast_to(row, (SUBS, LANES))


def lane_tile(index):
    return slice(index * LANES, (index + 1) * LANES)


def no_state(tiles):
    rows = tiles[0, :SUBS, :]
    return rows - rows


def in_steps(steps, tile, rows):
    span = rows.shape[0] // SUBS

    def move(i, unused):
        steps[tile, pl.ds(pl.multiple_of(i * SUBS, SUBS), SUBS), :] = rows[
            pl.ds(i, SUBS, stride=span), :
        ]
        return unused

    lax.fori_loop(0, span, move, 0, unroll=8)


def from_steps(rows, steps, tile):
    span = rows.shape[0] // SUBS

    def move(i, unused):
        rows[pl.ds(i, SUBS, stride=span), :] = steps[
            tile, pl.ds(pl.multiple_of(i * SUBS, SUBS), SUBS), :
        ]
        return unused

    lax.fori_loop(0, span, move, 0, unroll=8)


def step_rows(i):
    return pl.ds(pl.multiple_of(i * SUBS, SUBS), SUBS)


def norm_kernel(
    place, x_ref, gain_ref, logr_ref, normed_ref, turned_ref, u_tiles, ends_ref, total_ref, rows
):
    unit, unused = normalise(x_ref[...].astype(f32))
    normed_ref[...] = (unit * gain_ref[...]).astype(bf16)
    turned_ref[...] = normed_ref[...].T
    tiles, length, unused = u_tiles.shape
    states = logr_ref.shape[0]
    span = length // SUBS
    for tile in range(tiles):
        start = place[0] * (tiles * LANES) + tile * LANES
        rows[...] = normed_ref[:, pl.ds(pl.multiple_of(start, LANES), LANES)].astype(f32)
        in_steps(u_tiles, tile, rows)
    left = ((SUBS - 1 - sub_index()) * span).astype(f32)
    for tile in range(tiles):
        rate = jnp.exp(logr_ref[:, lane_tile(tile)])
        decay = jnp.exp(-rate)
        decays = [spread(decay[n : n + 1]) for n in range(states)]

        def step(i, held):
            u = u_tiles[tile, step_rows(i), :]
            return tuple(d * h + u for d, h in zip(decays, held))

        zero = no_state(u_tiles)
        held = lax.fori_loop(0, span, step, (zero,) * states, unroll=4)
        for n in range(states):
            ends_ref[n, :, lane_tile(tile)] = held[n]
            total_ref[n : n + 1, lane_tile(tile)] = jnp.sum(
                held[n] * jnp.exp(-left * rate[n : n + 1]), axis=0, keepdims=True
            )


def context_kernel(
    place, u_tiles, ends_ref, all_ref, logr_ref, coef_ref, context_ref, y_tiles, rows
):
    tiles, length, unused = u_tiles.shape
    states = logr_ref.shape[0]
    span = length // SUBS
    index = sub_index()
    before = (index * span).astype(f32)
    for tile in range(tiles):
        rate = jnp.exp(logr_ref[:, lane_tile(tile)])
        decay = jnp.exp(-rate)
        scale = coef_ref[:, lane_tile(tile)] * jnp.sqrt(2.0 * rate)
        incoming = jnp.zeros((states, LANES), f32)
        for j in range(all_ref.shape[0]):
            gap = place[1] - 1 - j
            distance = (jnp.maximum(gap, 0) * length).astype(f32)
            term = jnp.exp(-distance * rate) * all_ref[j, :, lane_tile(tile)].astype(f32)
            incoming = incoming + jnp.where(gap >= 0, term, 0.0)
        for first in range(0, states, GROUP):
            chosen = range(first, first + GROUP)
            starts = []
            for n in chosen:
                row = rate[n : n + 1]
                run = ends_ref[n, :, lane_tile(tile)]
                for d in (1, 2, 4):
                    moved = jnp.exp(-(d * span) * row) * pltpu.roll(run, d, 0)
                    run = run + jnp.where(index >= d, moved, 0.0)
                run = jnp.where(index >= 1, pltpu.roll(run, 1, 0), 0.0)
                starts.append(run + jnp.exp(-before * row) * incoming[n : n + 1])
            decays = [spread(decay[n : n + 1]) for n in chosen]
            scales = [spread(scale[n : n + 1]) for n in chosen]

            def step(i, held):
                at = step_rows(i)
                u = u_tiles[tile, at, :]
                held = tuple(d * h + u for d, h in zip(decays, held))
                parts = [s * h for s, h in zip(scales, held)]
                if first > 0:
                    parts[0] = parts[0] + y_tiles[tile, at, :]
                while len(parts) > 1:
                    parts = [a + b for a, b in zip(parts[::2], parts[1::2])]
                y_tiles[tile, at, :] = parts[0]
                return held

            lax.fori_loop(0, span, step, tuple(starts), unroll=4)
        from_steps(rows, y_tiles, tile)
        context_ref[:, lane_tile(tile)] = rows[...].astype(bf16)


def whole_rows(block):
    return block.reshape(block.shape[0] * block.shape[1], block.shape[2])


def head(index):
    return slice(index * HD, (index + 1) * HD)


def weight_copies(pieces, buffer, place, sems, act):
    col_parts, row_parts = sems.shape
    for k in range(col_parts):
        for r in range(row_parts):
            inner = buffer.at[k, place[2] ^ r]
            act(pltpu.make_async_copy(pieces[k * row_parts + r], inner, sems.at[k, r]))


def of_heads(buffer, i):
    return jnp.concatenate([whole_rows(buffer[k, :, :, head(i)]) for k in range(buffer.shape[0])], axis=1)


def gradient_slot(row_parts, order, r):
    position = 0
    for bit in reversed(order):
        position = 2 * position + (1 if r & bit else 0)
    return position // (row_parts // 2), position % (row_parts // 2)


def round_orders(row_parts):
    bits = [1 << i for i in range(row_parts.bit_length() - 1)]
    return bits, bits[::-1]


def gradient_pieces(stacks, row_parts, far, slot):
    found = []
    for r in range(row_parts):
        sent, at = gradient_slot(row_parts, round_orders(row_parts)[far], r)
        found.append(stacks[2 * far + sent].at[at, slot])
    return found


def project_kernel(team, col_parts, row_parts, place, normed_ref, cot_ref, *refs):
    contexts, refs = refs[:team], refs[team:]
    count = col_parts * row_parts
    pieces, refs = refs[:count], refs[count:]
    context_t_ref, cot_t_ref, kept_ref = refs[:3]
    context_ref, weights, sems = refs[3:]
    weight_copies(pieces, weights, place, sems, lambda copy: copy.start())
    width = contexts[0].shape[1]
    for k in range(team):
        lanes = pl.ds(pl.multiple_of((place[0] ^ k) * width, LANES), width)
        context_ref[:, lanes] = contexts[k][...]
    context_t_ref[...] = context_ref[...].T
    cot_t_ref[...] = cot_ref[...].T
    weight_copies(pieces, weights, place, sems, lambda copy: copy.wait())
    kept_ref[0] = dot(normed_ref[...], of_heads(weights, 0)).astype(bf16)
    kept_ref[1] = dot(context_ref[...], of_heads(weights, 1)).astype(bf16)
    kept_ref[2] = dot(context_ref[...], of_heads(weights, 2)).astype(bf16)


def attend_kernel(team, col_parts, row_parts, place, kept_ref, *refs):
    count = col_parts * row_parts
    pieces, refs = refs[:count], refs[count:]
    part_ref, attended_ref, probs_ref, probs_t_ref, weights, sems = refs
    weight_copies(pieces, weights, place, sems, lambda copy: copy.start())
    length = kept_ref.shape[1]
    rows = lax.broadcasted_iota(jnp.int32, (length, length), 0)
    cols = lax.broadcasted_iota(jnp.int32, (length, length), 1)
    for h in range(col_parts):
        scores = dot_t(kept_ref[0, :, head(h)], kept_ref[1, :, head(h)]) * score_scale
        scores = jnp.where(rows >= cols, scores, -1e30)
        shifted = jnp.exp(scores - jnp.max(scores, axis=-1, keepdims=True))
        inverse = 1.0 / jnp.sum(shifted, axis=-1, keepdims=True)
        probs = (shifted * inverse).astype(bf16)
        probs_ref[h] = probs
        probs_t_ref[h] = probs.T
        attended_ref[:, head(h)] = dot(probs, kept_ref[2, :, head(h)]).astype(bf16)
    weight_copies(pieces, weights, place, sems, lambda copy: copy.wait())
    part_ref[...] = dot_t(attended_ref[...], of_heads(weights, 3)).astype(bf16)


def gelu_parts(hidden, grad_act):
    density = jnp.exp(-0.5 * hidden * hidden)
    t = 1.0 / (1.0 + (0.3275911 * math.sqrt(0.5)) * jnp.abs(hidden))
    series = 0.5 * 1.061405429
    for factor in (-1.453152027, 1.421413741, -0.284496736, 0.254829592):
        series = series * t + 0.5 * factor
    tail = series * t * density
    cdf = jnp.where(hidden >= 0.0, 1.0 - tail, tail)
    slope = cdf + hidden * density * (1.0 / math.sqrt(2.0 * math.pi))
    return (hidden * cdf).astype(bf16), (grad_act * slope).astype(bf16)


def middle_kernel(team, x_ref, gain_ref, *refs):
    parts, (middle_ref, normed_ref, normed_t_ref) = refs[:team], refs[team:]
    attn = parts[0][...].astype(f32)
    for part in parts[1:]:
        attn = attn + part[...].astype(f32)
    middle = x_ref[...].astype(f32) + attn
    middle_ref[...] = middle
    unit, unused = normalise(middle)
    normed_ref[...] = (unit * gain_ref[...]).astype(bf16)
    normed_t_ref[...] = normed_ref[...].T


def feed_kernel(team, col_parts, row_parts, place, normed_ref, normed_t_ref, cot_ref, cot_t_ref, *refs):
    arrays, refs = (refs[:row_parts], refs[row_parts : 2 * row_parts]), refs[2 * row_parts :]
    outs, two_ref, refs = refs[:team], refs[team], refs[team + 1 :]
    stacks, refs = (refs[:4], refs[4:8]), refs[8:]
    up_all, down_all, grad_up, grad_down, activated_all, grad_all, sems = refs
    z = pl.program_id(0)
    half = col_parts // 2
    hidden_cols = grad_up.shape[3]

    def copies(k):
        found = []
        for r in range(row_parts):
            for which, buffer in enumerate((up_all, down_all)):
                outside = arrays[which][r].at[k]
                inside = buffer.at[place[2] ^ r, :, pl.ds(k * hidden_cols, hidden_cols)]
                found.append(pltpu.make_async_copy(outside, inside, sems.at[which, k, r]))
        return found

    def each_leaving(k, act):
        for which, buffer in enumerate((grad_up, grad_down)):
            steps = lax.rem(place[6] + col_parts - k, col_parts) if which == 0 else k
            for far in range(2):

                @pl.when(steps // half == far)
                def leaves():
                    slot = lax.rem(steps, half)
                    for r, piece in enumerate(gradient_pieces(stacks[which], row_parts, far, slot)):
                        inner = buffer.at[k, place[2] ^ r]
                        act(pltpu.make_async_copy(inner, piece, sems.at[2 + which, k, r]))

    @pl.when(z == 0)
    def start():
        for k in range(col_parts):
            for copy in copies(k):
                copy.start()

    for k in range(col_parts):

        @pl.when(z == k)
        def arrive():
            for copy in copies(k):
                copy.wait()

    at = pl.ds(pl.multiple_of(z * hidden_cols, hidden_cols), hidden_cols)
    hidden = dot(normed_ref[...], whole_rows(up_all[:, :, at]))
    grad_act = dot(cot_ref[...], whole_rows(down_all[:, :, at]))
    activated, grad_pre = gelu_parts(hidden, grad_act)
    activated_all[:, at] = activated
    grad_all[:, at] = grad_pre
    shape = grad_up.shape[1:]
    grad_up[z] = dot(normed_t_ref[...], grad_pre).astype(bf16).reshape(shape)
    grad_down[z] = dot(cot_t_ref[...], activated).astype(bf16).reshape(shape)

    for k in range(col_parts):

        @pl.when(z == k)
        def leave():
            each_leaving(k, lambda copy: copy.start())

    @pl.when(z == col_parts - 1)
    def finish():
        two_ref[...] = dot_t(grad_all[...], whole_rows(up_all[...])).astype(bf16)
        rows = outs[0].shape[0]
        for k in range(team):
            at_rows = pl.ds(pl.multiple_of((place[0] ^ k) * rows, rows), rows)
            outs[k][...] = dot_t(activated_all[at_rows, :], whole_rows(down_all[...])).astype(bf16)
        for k in range(col_parts):
            each_leaving(k, lambda copy: copy.wait())


def attend_back_kernel(team, col_parts, row_parts, place, middle_ref, gain_ref, cot_ref, *refs):
    parts, refs = refs[:team], refs[team:]
    late, refs = refs[:3], refs[3:]
    count = col_parts * row_parts
    pieces, refs = refs[:count], refs[count:]
    middle_grad_ref, gain_grad_ref, one_ref, low = refs[:4]
    grad_q, grad_k, grad_v = refs[4:7]
    context_grads, refs = refs[7 : 7 + team], refs[7 + team :]
    weights, grad_out, total_low = refs[:3]
    held, (sems, late_sems) = refs[3:6], refs[6:]
    kept_ref, probs_ref, probs_t_ref = held
    weight_copies(pieces, weights, place, sems, lambda copy: copy.start())
    late_copies = [
        pltpu.make_async_copy(outside, inside, late_sems.at[i])
        for i, (outside, inside) in enumerate(zip(late, held))
    ]
    for copy in late_copies:
        copy.start()
    own_rows = middle_ref.shape[0] // team
    grad_two = parts[0][...].astype(f32)
    for part in parts[1:]:
        grad_two = grad_two + part[...].astype(f32)
    unit, inverse = normalise(middle_ref[...])
    grad_gain = grad_two * unit
    rows = lax.broadcasted_iota(jnp.int32, grad_gain.shape, 0)
    first = place[0] * own_rows
    mine = (rows >= first) & (rows < first + own_rows)
    gain_grad_ref[...] = jnp.sum(jnp.where(mine, grad_gain, 0.0), axis=0, keepdims=True)
    grad = cot_ref[...].astype(f32) + normalise_back(unit, inverse, grad_two * gain_ref[...])
    low[...] = grad.astype(bf16)
    for k in range(team):

        @pl.when(place[0] == k)
        def own():
            middle_grad_ref[...] = grad[k * own_rows : (k + 1) * own_rows, :]

    weight_copies(pieces, weights, place, sems, lambda copy: copy.wait())
    for copy in late_copies:
        copy.wait()
    grad_out[...] = dot(low[...], of_heads(weights, 3)).astype(bf16)
    for h in range(col_parts):
        q, k, v = (kept_ref[i, :, head(h)] for i in range(3))
        grad_heads = grad_out[:, head(h)]
        grad_v[:, head(h)] = dot(probs_t_ref[h], grad_heads).astype(bf16)
        probs = probs_ref[h].astype(f32)
        grad_probs = dot_t(grad_heads, v)
        inner = jnp.sum(grad_probs * probs, axis=-1, keepdims=True)
        grad_scores = (probs * (grad_probs - inner)).astype(bf16)
        grad_q[:, head(h)] = (dot(grad_scores, k) * score_scale).astype(bf16)
        turned = dot_t(v, grad_heads) - inner.T
        turned = (probs_t_ref[h].astype(f32) * turned).astype(bf16)
        grad_k[:, head(h)] = (dot(turned, q) * score_scale).astype(bf16)
    total = dot_t(grad_k[...], of_heads(weights, 1)) + dot_t(grad_v[...], of_heads(weights, 2))
    total_low[...] = total.astype(bf16)
    width = context_grads[0].shape[1]
    for k in range(team):
        lanes = pl.ds(pl.multiple_of((place[0] ^ k) * width, LANES), width)
        context_grads[k][...] = total_low[:, lanes]
    one_ref[...] = dot_t(grad_q[...], of_heads(weights, 0)).astype(bf16)


def head_grads_kernel(col_parts, row_parts, place, low, attended_ref, *refs):
    normed_t_ref, context_t_ref, grad_q, grad_k, grad_v = refs[:5]
    stacks, (grads, out_sems) = refs[5:9], refs[9:]
    half = col_parts // 2
    shape = (*grads.shape[1:3], HD)

    def put(i, grad):
        for h in range(col_parts):
            grads[h, :, :, head(i)] = grad[:, head(h)].astype(bf16).reshape(shape)

    put(0, dot(normed_t_ref[...], grad_q[...]))
    put(1, dot(context_t_ref[...], grad_k[...]))
    put(2, dot(context_t_ref[...], grad_v[...]))
    put(3, dot(low[...].T, attended_ref[...]))
    copies = []
    for k in range(col_parts):
        for r, piece in enumerate(gradient_pieces(stacks, row_parts, k // half, k % half)):
            copies.append(pltpu.make_async_copy(grads.at[k, place[2] ^ r], piece, out_sems.at[k, r]))
    for copy in copies:
        copy.start()
    for copy in copies:
        copy.wait()


def adjoint_kernel(team, logr_ref, *refs):
    parts = refs[:team]
    g_tiles, ends_ref, total_ref, rows = refs[team:]
    grad = parts[0][...].astype(f32)
    for part in parts[1:]:
        grad = grad + part[...].astype(f32)
    grad = grad.astype(bf16).astype(f32)
    tiles, length, unused = g_tiles.shape
    states = logr_ref.shape[0]
    span = length // SUBS
    for tile in range(tiles):
        rows[...] = grad[:, lane_tile(tile)]
        in_steps(g_tiles, tile, rows)
    before = (sub_index() * span).astype(f32)
    for tile in range(tiles):
        rate = jnp.exp(logr_ref[:, lane_tile(tile)])
        decay = jnp.exp(-rate)
        for first in range(0, states, GROUP):
            chosen = range(first, first + GROUP)
            decays = [spread(decay[n : n + 1]) for n in chosen]

            def step(i, held):
                g = g_tiles[tile, step_rows(span - 1 - i), :]
                later = []
                for d, (b, w) in zip(decays, held):
                    shrunk = d * b
                    later.append((g + shrunk, d * w + shrunk))
                return tuple(later)

            zero = no_state(g_tiles)
            held = lax.fori_loop(0, span, step, ((zero, zero),) * GROUP, unroll=4)
            for n, (b, w) in zip(chosen, held):
                ends_ref[0, n, :, lane_tile(tile)] = b
                ends_ref[1, n, :, lane_tile(tile)] = w
                shrink = jnp.exp(-before * rate[n : n + 1])
                total_ref[0, n : n + 1, lane_tile(tile)] = jnp.sum(
                    shrink * b, axis=0, keepdims=True
                )
                total_ref[1, n : n + 1, lane_tile(tile)] = jnp.sum(
                    shrink * (w + before * b), axis=0, keepdims=True
                )


def context_back_kernel(
    team, place, g_tiles, u_tiles, ends_ref, all_ref, logr_ref, coef_ref, one_ref, *refs
):
    pieces = refs[:team]
    grad_ssm_ref, y_tiles, full, rows = refs[team:]
    tiles, length, unused = u_tiles.shape
    states = logr_ref.shape[0]
    span = length // SUBS
    width = tiles * LANES
    index = sub_index()
    after = ((SUBS - 1 - index) * span).astype(f32)
    full[...] = one_ref[...].astype(f32)
    group = GROUP
    for tile in range(tiles):
        lanes = lane_tile(tile)
        rate = jnp.exp(logr_ref[:, lanes])
        decay = jnp.exp(-rate)
        root = jnp.sqrt(2.0 * rate)
        scale = coef_ref[:, lanes] * root
        in_b = jnp.zeros((states, LANES), f32)
        in_w = jnp.zeros((states, LANES), f32)
        for j in range(all_ref.shape[0]):
            gap = j - place[1] - 1
            distance = (jnp.maximum(gap, 0) * length).astype(f32)
            shrink = jnp.exp(-distance * rate)
            b, w = all_ref[j, 0, :, lanes].astype(f32), all_ref[j, 1, :, lanes].astype(f32)
            in_b = in_b + jnp.where(gap >= 0, shrink * b, 0.0)
            in_w = in_w + jnp.where(gap >= 0, shrink * (w + distance * b), 0.0)
        for first in range(0, states, group):
            chosen = range(first, first + group)
            starts = []
            for n in chosen:
                row = rate[n : n + 1]
                b, w = ends_ref[0, n, :, lanes], ends_ref[1, n, :, lanes]
                for d in (1, 2, 4):
                    shrink = jnp.exp(-(d * span) * row)
                    next_b = pltpu.roll(b, SUBS - d, 0)
                    next_w = pltpu.roll(w, SUBS - d, 0)
                    inside = index < SUBS - d
                    b, w = (
                        b + jnp.where(inside, shrink * next_b, 0.0),
                        w + jnp.where(inside, shrink * (next_w + (d * span) * next_b), 0.0),
                    )
                inside = index < SUBS - 1
                b = jnp.where(inside, pltpu.roll(b, SUBS - 1, 0), 0.0)
                w = jnp.where(inside, pltpu.roll(w, SUBS - 1, 0), 0.0)
                shrink = jnp.exp(-after * row)
                b_row, w_row = in_b[n : n + 1], in_w[n : n + 1]
                b = b + shrink * b_row
                w = w + shrink * (w_row + after * b_row)
                zero = no_state(u_tiles)
                starts.append((b, w, zero, zero))
            decays = [spread(decay[n : n + 1]) for n in chosen]
            scales = [spread(scale[n : n + 1]) for n in chosen]

            def step(i, held):
                at = step_rows(span - 1 - i)
                g = g_tiles[tile, at, :]
                u = u_tiles[tile, at, :]
                later, parts = [], []
                for d, s, (b, w, sum_b, sum_w) in zip(decays, scales, held):
                    shrunk = d * b
                    w = d * w + shrunk
                    b = g + shrunk
                    later.append((b, w, sum_b + u * b, sum_w + u * w))
                    parts.append(s * b)
                while len(parts) > 1:
                    parts = [p + q for p, q in zip(parts[::2], parts[1::2])]
                if first > 0:
                    parts[0] = parts[0] + y_tiles[tile, at, :]
                y_tiles[tile, at, :] = parts[0]
                return tuple(later)

            held = lax.fori_loop(0, span, step, tuple(starts), unroll=2)
            for n, (unused_b, unused_w, sum_b, sum_w) in zip(chosen, held):
                sum_b = jnp.sum(sum_b, axis=0, keepdims=True)
                sum_w = jnp.sum(sum_w, axis=0, keepdims=True)
                row = slice(n, n + 1)
                grad_ssm_ref[0, row, lanes] = root[row] * sum_b
                grad_ssm_ref[1, row, lanes] = scale[row] * (0.5 * sum_b - rate[row] * sum_w)
        at_lanes = pl.ds(pl.multiple_of(place[0] * width + tile * LANES, LANES), LANES)
        from_steps(rows, y_tiles, tile)
        full[:, at_lanes] += rows[...].astype(bf16).astype(f32)
    count = pieces[0].shape[0]
    for k in range(team):
        at_rows = pl.ds(pl.multiple_of((place[0] ^ k) * count, count), count)
        pieces[k][...] = full[at_rows, :].astype(bf16)


def input_grad_kernel(team, place, x_ref, gain_ref, middle_grad_ref, *refs):
    parts, (out_ref, gain_grad_ref) = refs[:team], refs[team:]
    rows = out_ref.shape[0]
    at_rows = pl.ds(pl.multiple_of(place[0] * rows, rows), rows)
    grad_one = parts[0][...].astype(f32)
    for part in parts[1:]:
        grad_one = grad_one + part[...].astype(f32)
    unit, inverse = normalise(x_ref[at_rows, :].astype(f32))
    gain_grad_ref[...] = jnp.sum(grad_one * unit, axis=0, keepdims=True)
    back = normalise_back(unit, inverse, grad_one * gain_ref[...])
    out_ref[...] = (middle_grad_ref[...] + back).astype(bf16)


def assemble_kernel(halves, low_count, place, own_ref, *refs):
    others, out_ref = refs[:-1], refs[-1]
    count, rows, unused = own_ref.shape
    half = place[4]

    def put(value, sequence, which, member):
        at_rows = pl.ds(pl.multiple_of((which * low_count + member) * rows, rows), rows)
        out_ref[sequence, at_rows, :] = value.astype(out_ref.dtype)

    for sequence in range(count // (halves * low_count)):
        if halves == 1:
            for member in range(low_count):
                put(own_ref[sequence * low_count + member], sequence, 0, member)
        else:
            put(own_ref[sequence * halves + half], sequence, half, 0)
            put(others[0][sequence], sequence, 1 - half, 0)


def pack_kernel(halves, place, qkv_ref, out_ref, up_ref, down_ref, *refs):
    rows = up_ref.shape[0]
    heads, hidden = out_ref.shape[0] // halves, up_ref.shape[1] // halves
    for which in range(halves):
        side = place[4] if which == 0 else 1 - place[4]
        at_heads = pl.ds(pl.multiple_of(side * heads, LANES), heads)
        at_hidden = pl.ds(pl.multiple_of(side * hidden, LANES), hidden)
        if which == 0:
            head_ref, wide_ref, deep_ref = refs[:3]
        else:
            packed = refs[3]
            head_ref = packed.at[:, : 4 * heads]
            wide_ref = packed.at[:, 4 * heads : 4 * heads + hidden]
            deep_ref = packed.at[:, 4 * heads + hidden :]
        for i in range(3):
            head_ref[:, i * heads : (i + 1) * heads] = qkv_ref[i, :, at_heads].astype(bf16)
        head_ref[:, 3 * heads :] = out_ref[at_heads, :].T.astype(bf16)
        wide_ref[...] = up_ref[:, at_hidden].astype(bf16)
        deep_ref[...] = down_ref[at_hidden, :].T.astype(bf16)


def small_kernel(ssm_ref, gains_ref, out_ref):
    count = ssm_ref.shape[0]
    out_ref[:count, :] = ssm_ref[...]
    out_ref[count:, :] = gains_ref[...]


def lamb_moments(weight, grad_item, first_old, second_old):
    first_new = beta_first * first_old + (1.0 - beta_first) * grad_item
    second_new = beta_second * second_old + (1.0 - beta_second) * grad_item * grad_item
    direction = (
        first_new
        / (1.0 - beta_first**STEP)
        / (jnp.sqrt(second_new / (1.0 - beta_second**STEP)) + lamb_eps)
        + weight_decay * weight
    )
    return (first_new, second_new, direction)


def place_sums(sums_ref, sums):
    rows = lax.broadcasted_iota(jnp.int32, sums_ref.shape, 0)
    lanes = lax.broadcasted_iota(jnp.int32, sums_ref.shape, 1)
    found = jnp.zeros(sums_ref.shape, f32)
    for index, pair in sums.items():
        for row, value in enumerate(pair):
            found = jnp.where((rows == row) & (lanes == index), value, found)
    sums_ref[...] = found


def moments_kernel(halves, matrices, place, *refs):
    count = 1 + max(item[1] for item in matrices)
    grads, refs = [refs[halves * i : halves * (i + 1)] for i in range(count)], refs[halves * count :]
    arrays = len({(item[1], item[4] is None) for item in matrices})
    ins = [refs[3 * i : 3 * i + 3] for i in range(arrays)]
    outs = [refs[3 * (arrays + i) : 3 * (arrays + i) + 3] for i in range(arrays)]
    sums_ref = refs[6 * arrays]
    keys = []
    sums = {}
    for number, source, column, turned, stacked in matrices:
        key = (source, stacked is None)
        if key not in keys:
            keys.append(key)
        pick = (lambda ref: ref) if stacked is None else (lambda ref, i=stacked: ref.at[i])
        weight, first, second = (pick(ref) for ref in ins[keys.index(key)])
        news = [pick(ref) for ref in outs[keys.index(key)]]
        width = weight.shape[0 if turned else 1] // halves
        rows = weight.shape[1 if turned else 0]
        cols = slice(column * width, (column + 1) * width)
        total_weight = total_update = 0.0
        for which, grad_ref in enumerate(grads[source]):
            side = place[4] if which == 0 else 1 - place[4]
            at = pl.ds(pl.multiple_of(side * width, width), width)
            if which == 0:
                grad = grad_ref[pl.ds(pl.multiple_of(side * rows, rows), rows), cols].astype(f32)
            else:
                grad = grad_ref[:, cols].astype(f32)
            at = (at, slice(None)) if turned else (slice(None), at)
            grad = grad.T if turned else grad
            old = weight[at]
            found = lamb_moments(old, grad, first[at], second[at])
            for ref, value in zip(news, found):
                ref[at] = value
            total_weight = total_weight + jnp.sum(old * old)
            total_update = total_update + jnp.sum(found[2] * found[2])
        sums[number] = (total_weight, total_update)
    place_sums(sums_ref, sums)


def small_moments_kernel(numbers, grads_ref, *refs):
    ins, outs, sums_ref = (refs[:3], refs[3:6]), (refs[6:9], refs[9:12]), refs[12]
    states = (grads_ref.shape[0] - 2) // 2
    sums = {}
    for (weight, first, second), news, start, rows, first_number in (
        (ins[0], outs[0], 2 * states, 1, numbers[0]),
        (ins[1], outs[1], 0, states, numbers[1]),
    ):
        for i in range(2):
            grad = grads_ref[start + i * rows : start + (i + 1) * rows, :]
            at = slice(i * rows, (i + 1) * rows)
            found = lamb_moments(weight[at, :], grad, first[at, :], second[at, :])
            for ref, value in zip(news, found):
                ref[at, :] = value
            sums[first_number + i] = (
                jnp.sum(weight[at, :] * weight[at, :]),
                jnp.sum(found[2] * found[2]),
            )
    place_sums(sums_ref, sums)


def update_kernel(stacks, sums_ref, *refs):
    count = len(stacks)
    weights, directions, news = refs[:count], refs[count : 2 * count], refs[2 * count : 3 * count]
    norms = jnp.sqrt(jnp.sum(sums_ref[...], axis=0))
    refs[3 * count][...] = norms
    ratios = norms[0:1] / norms[1:2]
    lanes = lax.broadcasted_iota(jnp.int32, ratios.shape, 1)
    for numbers, weight, direction, new in zip(stacks, weights, directions, news):
        step = weight.shape[0] // len(numbers)
        for i, number in enumerate(numbers):
            ratio = jnp.sum(jnp.where(lanes == number, ratios, 0.0), axis=1, keepdims=True)
            at = slice(i * step, (i + 1) * step)
            scale = learn_rate * ratio.reshape((1,) * weight.ndim)
            new[at] = weight[at] - scale * direction[at]


def call(
    body, ins, outs, scratch=(), grid=None, in_specs=None, out_specs=None, time=1.0, after=(), token=False
):
    moved = sum(a.size * a.dtype.itemsize for a in list(ins) + list(outs))
    params = pltpu.CompilerParams(vmem_limit_bytes=VMEM_BYTES)
    cost = pl.CostEstimate(flops=int(time * 1.15e9), bytes_accessed=moved, transcendentals=0)
    whole = pl.BlockSpec(memory_space=pltpu.VMEM)
    anywhere = pl.BlockSpec(memory_space=pl.ANY)
    in_specs = list(in_specs or [whole] * len(ins)) + [anywhere] * len(after)
    out_specs = list(out_specs or [whole] * len(outs))
    outs = list(outs)
    first_out = len(ins) + len(after)
    last_out = first_out + len(outs)
    if token:
        outs.append(jax.ShapeDtypeStruct((SUBS, LANES), f32))
        out_specs.append(whole)

    def run(*refs):
        refs = list(refs)
        if token:
            refs[last_out][...] = jnp.zeros((SUBS, LANES), f32)
            del refs[last_out]
        body(*refs[: len(ins)], *refs[first_out:])

    return pl.pallas_call(
        run,
        out_shape=tuple(outs),
        in_specs=in_specs,
        out_specs=tuple(out_specs),
        scratch_shapes=list(scratch),
        compiler_params=params,
        cost_estimate=cost,
        **({} if grid is None else {"grid": grid}),
    )(*ins, *after)


def shaped(shape, kind):
    return jax.ShapeDtypeStruct(tuple(shape), kind)


def on_device(
    tokens,
    cotangent,
    w_qkv,
    w_out,
    w_up,
    w_down,
    norm_gains,
    ssm_param,
    first_qkv,
    second_qkv,
    first_out,
    second_out,
    first_up,
    second_up,
    first_down,
    second_down,
    first_gain,
    second_gain,
    first_ssm,
    second_ssm,
):
    halves = lax.axis_size("sl")
    low_count = lax.axis_size("ml")
    row_parts = lax.axis_size("sh")
    col_parts = lax.axis_size("mb") * lax.axis_size("mq")
    team = halves * low_count
    sl, ml, mb, mq = (lax.axis_index(name) for name in ("sl", "ml", "mb", "mq"))
    rank = sl * low_count + ml
    block_index = lax.axis_index("sh") * halves + mq
    seq_total, length, width = tokens.shape
    assert length == BLK and seq_total == lax.axis_size("mb")
    states = ssm_param.shape[1]
    channels = width // team
    tiles = channels // LANES
    row_count = width // row_parts
    own_rows = length // team
    place = [rank, block_index, lax.axis_index("sh"), lax.axis_index(MODEL), sl, sl ^ mq]
    place.append(lax.axis_index(COLS))
    place = jnp.stack(place).astype(jnp.int32)
    smem = pl.BlockSpec(memory_space=pltpu.SMEM)
    vmem = pl.BlockSpec(memory_space=pltpu.VMEM)

    def permute(value, axes, moves):
        return lax.ppermute(value, axes, moves)

    def swap(value):
        return permute(value, "sl", [(0, 1), (1, 0)])

    def in_order(own, other, axis):
        return jnp.where(
            sl == 0, jnp.concatenate([own, other], axis), jnp.concatenate([other, own], axis)
        )

    def team_send(pieces):
        moved = [pieces[0]]
        for k in range(1, team):
            moved.append(permute(pieces[k], TEAM, [(i, i ^ k) for i in range(team)]))
        return moved

    def pick_block(array):
        own = lax.dynamic_index_in_dim(array, mb, 0, keepdims=False)
        if halves == 1:
            return own, ()
        other = swap(own)
        return jnp.where(sl == mq, own, other), (other,)

    def across(value, bit):
        return permute(value, "sh", [(i, i ^ bit) for i in range(row_parts)])

    def along(value, axes, step):
        count = lax.axis_size(axes)
        return permute(value, axes, [(i, (i + step) % count) for i in range(count)])

    bits = [1 << i for i in range(row_parts.bit_length() - 1)]

    def bit_order(k):
        return bits if k % 2 == 0 else bits[::-1]

    def double_rows(value, order):
        found = {0: value}
        for bit in order:
            for r in list(found):
                found[r | bit] = across(found[r], bit)
        return [found[r] for r in range(row_parts)]

    def add(*items, zero=None):
        total = sum(item.astype(f32) for item in items)
        return (total if zero is None else total + zero[0, 0]).astype(bf16)

    def first_messages(stacks):
        return across(stacks[1], bits[-1]), across(stacks[3], bits[0])

    def halve_rows(keep, arrived, order, zero, after):
        items = [keep, arrived]
        for bit in order[-2::-1]:
            count = arrived.shape[0] // 2
            sent = add(*[item[count:] for item in items], zero=zero)
            arrived = across(hold((sent,), after)[0] if after else sent, bit)
            items = [item[:count] for item in items] + [arrived]
        return add(*[item[0] for item in items])

    def halve_both(stacks, first, zero, after=()):
        near = halve_rows(stacks[0], first[0], bits, zero, after)
        return near, halve_rows(stacks[2], first[1], bits[::-1], zero, after)

    def hold(arrays, after):
        anywhere = pl.BlockSpec(memory_space=pl.ANY)
        return pl.pallas_call(
            lambda *refs: None,
            out_shape=tuple(shaped(item.shape, item.dtype) for item in arrays),
            in_specs=[anywhere] * (len(arrays) + len(after)),
            out_specs=(anywhere,) * len(arrays),
            input_output_aliases={i: i for i in range(len(arrays))},
        )(*arrays, *after)

    def ring_gather(shard):
        pieces = []
        for k in range(col_parts):
            held = along(shard, COLS, k) if k > 0 else shard
            pieces.append(double_rows(held, bits if k % 2 == 0 else bits[::-1]))
        return pieces

    def sum_over_z(near, far, ring=True):
        if not ring:
            pieces = [stack[k] for stack in (near, far) for k in range(col_parts // 2)]
            moved = [along(piece, COLS, -k) for k, piece in enumerate(pieces) if k > 0]
            return add(pieces[0], *moved)
        held = None
        for stack in (far, near):
            for k in reversed(range(stack.shape[0])):
                held = stack[k] if held is None else add(stack[k], along(held, COLS, -1))
        return held

    def everywhere(value, axes):
        count = lax.axis_size(axes)
        copies = jnp.broadcast_to(value[None], (count, *value.shape))
        return lax.all_to_all(copies, axes, 0, 0, tiled=True)

    rows_dev = w_up.shape[0]
    hidden_cols = w_up.shape[1] // halves
    head_cols = 4 * w_out.shape[0] // halves
    packed_cols = head_cols + 2 * hidden_cols
    sides = [shaped((rows_dev, cols), bf16) for cols in (head_cols, hidden_cols, hidden_cols)]
    shards = call(
        functools.partial(pack_kernel, halves),
        (place, w_qkv, w_out, w_up, w_down),
        sides + [shaped((rows_dev, packed_cols), bf16)] * (halves - 1),
        time=2.4,
        in_specs=[smem] + [vmem] * 4,
    )
    if halves == 2:
        other = swap(shards[3])
        cuts = (0, head_cols, head_cols + hidden_cols, packed_cols)
        shards = [
            in_order(own, other[:, first:last], 0)
            for own, first, last in zip(shards, cuts, cuts[1:])
        ]
    head_shard, up_shard, down_shard = shards[:3]
    small, = call(
        small_kernel,
        (ssm_param.reshape(2 * states, -1), norm_gains),
        (shaped((2 * states + 2, norm_gains.shape[1]), f32),),
        after=(head_shard,),
    )
    small = jnp.transpose(everywhere(small, ALL), (1, 0, 2)).reshape(2 * states + 2, width)
    own_ssm = lax.dynamic_slice_in_dim(
        small[: 2 * states].reshape(2, states, width), rank * channels, channels, 2
    )
    coef, logr = own_ssm[0], own_ssm[1]
    gain_one = small[2 * states : 2 * states + 1]
    gain_two = small[2 * states + 1 : 2 * states + 2]

    attn_w = ring_gather(head_shard)
    up_shard, down_shard = hold(
        (up_shard, down_shard), (*[group[0] for group in attn_w[1:]], small, *attn_w[0][1:-1])
    )
    up_full = lax.all_gather(up_shard, COLS, axis=0, tiled=False)
    down_full = lax.all_gather(down_shard, COLS, axis=0, tiled=False)
    attn_flat = [piece for group in attn_w for piece in group]

    x, unused = pick_block(tokens)
    cot, cot_other = pick_block(cotangent)

    anywhere = [pl.BlockSpec(memory_space=pl.ANY)]

    def fixed(*shape):
        return pl.BlockSpec(shape, lambda z: (0,) * len(shape))

    wide = fixed(length, width)
    row = fixed(1, width)

    normed_one, normed_t, u_steps, ends, total = call(
        norm_kernel,
        (place, x, gain_one, logr),
        (
            shaped((length, width), bf16),
            shaped((width, length), bf16),
            shaped((tiles, length, LANES), f32),
            shaped((states, SUBS, channels), f32),
            shaped((states, channels), f32),
        ),
        scratch=[pltpu.VMEM((length, LANES), f32)],
        in_specs=[smem, vmem, vmem, vmem],
        after=(*attn_w[0][1:-1], attn_w[1][0], *cot_other),
        time=5,
    )
    (up_full,) = hold((up_full,), (total,))
    up_w = double_rows(up_full, bits)
    totals = everywhere(total.astype(bf16), ("sh", "mq"))
    (context_own,) = call(
        context_kernel,
        (place, u_steps, ends, totals, logr, coef),
        (shaped((length, channels), bf16),),
        after=(attn_w[0][-1], *attn_w[1][1:-1], attn_w[-1][0]),
        scratch=[pltpu.VMEM((tiles, length, LANES), f32), pltpu.VMEM((length, LANES), f32)],
        in_specs=[smem] + [vmem] * 5,
        time=7,
    )
    (down_full,) = hold((down_full,), (context_own,))
    down_w = double_rows(down_full, bits[::-1])
    contexts = team_send([context_own] * team)

    stack_shape = (row_parts // 2, col_parts // 2, row_count)
    head_stacks = [shaped((*stack_shape, head_cols), bf16)] * 4
    hidden_stacks = [shaped((*stack_shape, hidden_cols), bf16)] * 8
    sizes = (team, col_parts, row_parts)
    head_buffer = pltpu.VMEM((col_parts, row_parts, row_count, 4 * HD), bf16)
    head_sems = pltpu.SemaphoreType.DMA((col_parts, row_parts))
    kept_shape = shaped((3, length, col_parts * HD), bf16)
    flat_shape = shaped((length, col_parts * HD), bf16)
    context_t, cot_t, kept = call(
        functools.partial(project_kernel, *sizes),
        (place, normed_one, cot, *contexts, *attn_flat),
        (shaped((width, length), bf16), shaped((width, length), bf16), kept_shape),
        scratch=[pltpu.VMEM((length, width), bf16), head_buffer, head_sems],
        time=1,
        in_specs=[smem] + [vmem] * (2 + team) + anywhere * len(attn_flat),
        after=(up_full,),
    )
    attn_part, attended, probs, probs_t = call(
        functools.partial(attend_kernel, *sizes),
        (place, kept, *attn_flat),
        (
            shaped((length, width), bf16),
            flat_shape,
            *[shaped((col_parts, length, length), bf16)] * 2,
        ),
        scratch=[head_buffer, head_sems],
        time=1,
        in_specs=[smem, vmem] + anywhere * len(attn_flat),
        after=up_w[1:-1],
    )
    attn_parts = team_send([attn_part] * team)

    middle, normed_two, normed_two_t = call(
        functools.partial(middle_kernel, team),
        (x, gain_two, *attn_parts),
        (shaped((length, width), f32), shaped((length, width), bf16), shaped((width, length), bf16)),
        time=1,
        after=(up_w[-1], *down_w[1:-1]),
    )
    weight_buffer = pltpu.VMEM((row_parts, row_count, col_parts * hidden_cols), bf16)
    grad_buffer = pltpu.VMEM((col_parts, row_parts, row_count, hidden_cols), bf16)
    fed = call(
        functools.partial(feed_kernel, team, col_parts, row_parts),
        (place, normed_two, normed_two_t, cot, cot_t, *up_w, *down_w),
        (
            *[shaped((own_rows, width), bf16)] * team,
            shaped((length, width), bf16),
            *hidden_stacks,
        ),
        scratch=[
            *[weight_buffer] * 2,
            *[grad_buffer] * 2,
            *[pltpu.VMEM((length, col_parts * hidden_cols), bf16)] * 2,
            pltpu.SemaphoreType.DMA((4, col_parts, row_parts)),
        ],
        time=18,
        grid=(col_parts,),
        in_specs=[smem, wide, fixed(width, length), wide, fixed(width, length)]
        + anywhere * (2 * row_parts),
        out_specs=[fixed(own_rows, width)] * team + [wide] + anywhere * 8,
    )
    out_pieces, two_part, hidden_grads = fed[:team], fed[team], fed[team + 1 :]
    two_parts = team_send([two_part] * team)

    def rows_of(array, member):
        return lax.dynamic_slice_in_dim(array, member * own_rows, own_rows, 0)

    def share_rows(pieces, kind):
        others = []
        if halves == 2:
            pairs = pieces.reshape(seq_total, halves, own_rows, width)
            others = [swap(lax.dynamic_index_in_dim(pairs, 1 - sl, 1, keepdims=False))]
        (blocks,) = call(
            functools.partial(assemble_kernel, halves, low_count),
            (place, pieces, *others),
            (shaped((seq_total, length, width), kind),),
            time=3.5,
            in_specs=[smem, vmem] + [vmem] * len(others),
        )
        return blocks

    out_pieces = team_send(list(out_pieces))
    result = rows_of(middle, rank) + sum(item.astype(f32) for item in out_pieces)
    result = result.astype(bf16)
    layer_pieces = lax.all_gather(result, MODEL, axis=0, tiled=False)
    layer_out = share_rows(layer_pieces, bf16)

    def both_halves(own):
        if halves == 1:
            return [own]
        return [own, swap(lax.dynamic_slice_in_dim(own, (1 - sl) * rows_dev, rows_dev, 0))]

    middle_grad, gain_two_grad, one_part, low_grad, *rest = call(
        functools.partial(attend_back_kernel, *sizes),
        (place, middle, gain_two, cot, *two_parts, kept, probs, probs_t, *attn_flat),
        (
            shaped((own_rows, width), f32),
            shaped((1, width), f32),
            shaped((length, width), bf16),
            shaped((length, width), bf16),
            *[flat_shape] * 3,
            *[shaped((length, channels), bf16)] * team,
        ),
        scratch=[
            head_buffer,
            pltpu.VMEM(flat_shape.shape, bf16),
            pltpu.VMEM((length, width), bf16),
            pltpu.VMEM(kept_shape.shape, bf16),
            *[pltpu.VMEM((col_parts, length, length), bf16)] * 2,
            head_sems,
            pltpu.SemaphoreType.DMA((3,)),
        ],
        time=1,
        in_specs=[smem] + [vmem] * (3 + team) + anywhere * (3 + len(attn_flat)),
        after=(result,),
    )
    head_grads, context_grads = rest[:3], rest[3:]
    context_grads = team_send(context_grads)
    *head_stacks, heads_done = call(
        functools.partial(head_grads_kernel, col_parts, row_parts),
        (place, low_grad, attended, normed_t, context_t, *head_grads),
        head_stacks,
        scratch=[head_buffer, head_sems],
        time=8,
        in_specs=[smem] + [vmem] * 7,
        out_specs=anywhere * 4,
        token=True,
    )
    down_first = first_messages(hidden_grads[4:])
    g_steps, adjoint_ends, adjoint_total, adjoint_done = call(
        functools.partial(adjoint_kernel, team),
        (logr, *context_grads),
        (
            shaped((tiles, length, LANES), f32),
            shaped((2, states, SUBS, channels), f32),
            shaped((2, states, channels), f32),
        ),
        scratch=[pltpu.VMEM((length, LANES), f32)],
        time=1,
        after=(*down_first, heads_done),
        token=True,
    )
    adjoint_totals = everywhere(adjoint_total.astype(bf16), ("sh", "mq"))
    up_stacks = list(hidden_grads[:4])
    down_sums = halve_both(hidden_grads[4:], down_first, adjoint_done, (adjoint_totals,))
    up_stacks[1::2] = hold(up_stacks[1::2], (adjoint_totals,))
    up_first = first_messages(up_stacks)
    *one_pieces, grad_ssm = call(
        functools.partial(context_back_kernel, team),
        (place, g_steps, u_steps, adjoint_ends, adjoint_totals, logr, coef, one_part),
        (
            *[shaped((own_rows, width), bf16)] * team,
            shaped((2, states, channels), f32),
        ),
        scratch=[
            pltpu.VMEM((tiles, length, LANES), f32),
            pltpu.VMEM((length, width), f32),
            pltpu.VMEM((length, LANES), f32),
        ],
        in_specs=[smem] + [vmem] * 7,
        time=1,
    )
    one_part_done = one_pieces[0]
    one_pieces = team_send(one_pieces)
    grad_rows, gain_one_grad, rows_done = call(
        functools.partial(input_grad_kernel, team),
        (place, x, gain_one, middle_grad, *one_pieces),
        (shaped((own_rows, width), bf16), shaped((1, width), f32)),
        in_specs=[smem] + [vmem] * (3 + team),
        time=1,
        after=(layer_pieces, *up_first),
        token=True,
    )
    grad_down = lax.psum_scatter(
        jnp.concatenate(down_sums, 0), COLS, scatter_dimension=0, tiled=False
    )
    head_stacks[1::2] = hold(head_stacks[1::2], (one_part_done,))
    head_sums = halve_both(head_stacks, first_messages(head_stacks), rows_done)
    up_sums = halve_both(up_stacks, up_first, rows_done)
    grad_up = sum_over_z(*up_sums)
    grad_heads = sum_over_z(*head_sums)
    input_grad = share_rows(lax.all_gather(grad_rows, MODEL, axis=0, tiled=False), f32)

    placed_ssm = lax.dynamic_update_slice_in_dim(
        jnp.zeros((2 * states, width), f32),
        grad_ssm.reshape(2 * states, channels),
        rank * channels,
        1,
    )
    small_grads = jnp.concatenate([placed_ssm, gain_one_grad, gain_two_grad], 0)
    (small_grads,) = hold((small_grads,), head_sums)
    small_grads = small_grads.reshape(2 * states + 2, lax.axis_size(ALL), -1)
    small_grads = lax.all_to_all(jnp.transpose(small_grads, (1, 0, 2)), ALL, 0, 0, tiled=True)
    small_grads = jnp.sum(small_grads, axis=0)

    def moments(matrices, grads, arrays, after=()):
        changed = [shaped(old.shape, f32) for group in arrays for old in group]
        grad_parts = [part for grad in grads for part in both_halves(grad)]
        ins = [item for group in arrays for item in group]
        *found, sums = call(
            functools.partial(moments_kernel, halves, matrices),
            (place, *grad_parts, *ins),
            (*changed, shaped((2, LANES), f32)),
            in_specs=[smem] + [vmem] * (len(grad_parts) + len(ins)),
            after=after,
            time=4,
        )
        return [found[3 * i : 3 * i + 3] for i in range(len(arrays))], sums

    hidden_new, hidden_sums = moments(
        ((4, 0, 0, False, None), (5, 1, 0, True, None)),
        (grad_up, grad_down),
        ((w_up, first_up, second_up), (w_down, first_down, second_down)),
    )
    heads_new, head_sums = moments(
        tuple((i, 0, i, False, i) for i in range(3)) + ((3, 0, 3, True, None),),
        (grad_heads,),
        ((w_qkv, first_qkv, second_qkv), (w_out, first_out, second_out)),
        (layer_out, input_grad),
    )
    own_channels = norm_gains.shape[1]
    ssm_items = [item.reshape(2 * states, own_channels) for item in (ssm_param, first_ssm, second_ssm)]
    small_items = [norm_gains, first_gain, second_gain, *ssm_items]
    *small_new, small_sums = call(
        functools.partial(small_moments_kernel, (6, 8)),
        (small_grads.reshape(2 * states + 2, own_channels), *small_items),
        (*[shaped(item.shape, f32) for item in small_items], shaped((2, LANES), f32)),
    )
    all_sums = everywhere(hidden_sums + head_sums + small_sums, ALL)
    masters = (w_qkv, w_out, w_up, w_down, norm_gains, ssm_items[0])
    news = (*heads_new, *hidden_new, small_new[:3], small_new[3:])
    *weights, norms = call(
        functools.partial(update_kernel, ((0, 1, 2), (3,), (4,), (5,), (6, 7), (8, 9))),
        (all_sums, *masters, *[group[2] for group in news]),
        (*[shaped(item.shape, f32) for item in masters], shaped((2, LANES), f32)),
        time=3.2,
    )
    outputs = [layer_out, input_grad]
    for index, (weight, (first_new, second_new, unused)) in enumerate(zip(weights, news)):
        if index == 4:
            outputs += [weight, first_new, second_new[0], second_new[1]]
        else:
            kept_shape = ssm_param.shape if index == 5 else weight.shape
            outputs += [item.reshape(kept_shape) for item in (weight, first_new, second_new)]
    outputs.append(norms[:, :10])
    return tuple(outputs)


def solution(mesh):
    seq_count, model_count = mesh.shape["seq"], mesh.shape["mp"]
    halves = 2 if HEADS // model_count >= 2 else 1
    sizes = (seq_count // halves, halves, SEQS, halves, model_count // (SEQS * halves))
    fine = Mesh(mesh.devices.reshape(sizes), ALL)
    seq, model = ("sh", "sl"), ("mb", "mq", "ml")
    rows_cols, cols_rows = P(seq, model), P(model, seq)
    token = P(None, seq, None)
    stack = P(None, seq, model)
    gains = P(None, ALL)
    ssm = P(None, None, ALL)
    return jax.shard_map(
        on_device,
        mesh=fine,
        in_specs=(token, token, stack, cols_rows, rows_cols, cols_rows, gains, ssm)
        + (stack,) * 2
        + (cols_rows,) * 2
        + (rows_cols,) * 2
        + (cols_rows,) * 2
        + (gains,) * 2
        + (ssm,) * 2,
        out_specs=(token, token)
        + (stack,) * 3
        + (cols_rows,) * 3
        + (rows_cols,) * 3
        + (cols_rows,) * 3
        + (gains, gains, P(ALL), P(ALL))
        + (ssm,) * 3
        + (P(),),
        check_vma=False,
    )
```

```python
import functools
import math

import jax
import jax.numpy as jnp
from jax import lax
from jax.experimental import pallas as pl
from jax.experimental.pallas import tpu as pltpu
from jax.sharding import Mesh
from jax.sharding import PartitionSpec as P

HD = 128
HEADS = 8
BLK = 512
STEP = 10
SEQS = 2
LANES = 128
SUBS = 8
GROUP = 8

norm_eps = 1e-05
beta_first = 0.9
beta_second = 0.999
lamb_eps = 1e-06
weight_decay = 0.01
learn_rate = 0.5
score_scale = HD ** (-0.5)

f32 = jnp.float32
bf16 = jnp.bfloat16
VMEM_BYTES = 56 * 1024 * 1024

ALL = ("sh", "sl", "mb", "mq", "ml")
MODEL = ("mb", "mq", "ml")
COLS = ("mb", "mq")
COPIES = ("sh", "mb", "mq")
TEAM = ("sl", "ml")


def dot(left, right):
    return lax.dot_general(left, right, (((1,), (0,)), ((), ())), preferred_element_type=f32)


def dot_t(left, right):
    return lax.dot_general(left, right, (((1,), (1,)), ((), ())), preferred_element_type=f32)


def normalise(values):
    centred = values - jnp.mean(values, axis=-1, keepdims=True)
    inverse = lax.rsqrt(jnp.mean(centred * centred, axis=-1, keepdims=True) + norm_eps)
    return centred * inverse, inverse


def normalise_back(unit, inverse, grad_unit):
    mean_one = jnp.mean(grad_unit, axis=-1, keepdims=True)
    mean_two = jnp.mean(grad_unit * unit, axis=-1, keepdims=True)
    return inverse * (grad_unit - mean_one - unit * mean_two)


def sub_index():
    return lax.broadcasted_iota(jnp.int32, (SUBS, LANES), 0)


def spread(row):
    return jnp.broadcast_to(row, (SUBS, LANES))


def lane_tile(index):
    return slice(index * LANES, (index + 1) * LANES)


def no_state(tiles):
    rows = tiles[0, :SUBS, :]
    return rows - rows


def in_steps(steps, tile, rows):
    span = rows.shape[0] // SUBS

    def move(i, unused):
        steps[tile, pl.ds(pl.multiple_of(i * SUBS, SUBS), SUBS), :] = rows[
            pl.ds(i, SUBS, stride=span), :
        ]
        return unused

    lax.fori_loop(0, span, move, 0, unroll=8)


def from_steps(rows, steps, tile):
    span = rows.shape[0] // SUBS

    def move(i, unused):
        rows[pl.ds(i, SUBS, stride=span), :] = steps[
            tile, pl.ds(pl.multiple_of(i * SUBS, SUBS), SUBS), :
        ]
        return unused

    lax.fori_loop(0, span, move, 0, unroll=8)


def step_rows(i):
    return pl.ds(pl.multiple_of(i * SUBS, SUBS), SUBS)


def norm_kernel(
    place, x_ref, gain_ref, logr_ref, normed_ref, turned_ref, u_tiles, ends_ref, total_ref, rows
):
    unit, unused = normalise(x_ref[...].astype(f32))
    normed_ref[...] = (unit * gain_ref[...]).astype(bf16)
    turned_ref[...] = normed_ref[...].T
    tiles, length, unused = u_tiles.shape
    states = logr_ref.shape[0]
    span = length // SUBS
    for tile in range(tiles):
        start = place[0] * (tiles * LANES) + tile * LANES
        rows[...] = normed_ref[:, pl.ds(pl.multiple_of(start, LANES), LANES)].astype(f32)
        in_steps(u_tiles, tile, rows)
    left = ((SUBS - 1 - sub_index()) * span).astype(f32)
    for tile in range(tiles):
        rate = jnp.exp(logr_ref[:, lane_tile(tile)])
        decay = jnp.exp(-rate)
        decays = [spread(decay[n : n + 1]) for n in range(states)]

        def step(i, held):
            u = u_tiles[tile, step_rows(i), :]
            return tuple(d * h + u for d, h in zip(decays, held))

        zero = no_state(u_tiles)
        held = lax.fori_loop(0, span, step, (zero,) * states, unroll=4)
        for n in range(states):
            ends_ref[n, :, lane_tile(tile)] = held[n]
            total_ref[n : n + 1, lane_tile(tile)] = jnp.sum(
                held[n] * jnp.exp(-left * rate[n : n + 1]), axis=0, keepdims=True
            )


def context_kernel(
    place, u_tiles, ends_ref, all_ref, logr_ref, coef_ref, context_ref, y_tiles, rows
):
    tiles, length, unused = u_tiles.shape
    states = logr_ref.shape[0]
    span = length // SUBS
    index = sub_index()
    before = (index * span).astype(f32)
    for tile in range(tiles):
        rate = jnp.exp(logr_ref[:, lane_tile(tile)])
        decay = jnp.exp(-rate)
        scale = coef_ref[:, lane_tile(tile)] * jnp.sqrt(2.0 * rate)
        incoming = jnp.zeros((states, LANES), f32)
        for j in range(all_ref.shape[0]):
            gap = place[1] - 1 - j
            distance = (jnp.maximum(gap, 0) * length).astype(f32)
            term = jnp.exp(-distance * rate) * all_ref[j, :, lane_tile(tile)].astype(f32)
            incoming = incoming + jnp.where(gap >= 0, term, 0.0)
        for first in range(0, states, GROUP):
            chosen = range(first, first + GROUP)
            starts = []
            for n in chosen:
                row = rate[n : n + 1]
                run = ends_ref[n, :, lane_tile(tile)]
                for d in (1, 2, 4):
                    moved = jnp.exp(-(d * span) * row) * pltpu.roll(run, d, 0)
                    run = run + jnp.where(index >= d, moved, 0.0)
                run = jnp.where(index >= 1, pltpu.roll(run, 1, 0), 0.0)
                starts.append(run + jnp.exp(-before * row) * incoming[n : n + 1])
            decays = [spread(decay[n : n + 1]) for n in chosen]
            scales = [spread(scale[n : n + 1]) for n in chosen]

            def step(i, held):
                at = step_rows(i)
                u = u_tiles[tile, at, :]
                held = tuple(d * h + u for d, h in zip(decays, held))
                parts = [s * h for s, h in zip(scales, held)]
                if first > 0:
                    parts[0] = parts[0] + y_tiles[tile, at, :]
                while len(parts) > 1:
                    parts = [a + b for a, b in zip(parts[::2], parts[1::2])]
                y_tiles[tile, at, :] = parts[0]
                return held

            lax.fori_loop(0, span, step, tuple(starts), unroll=4)
        from_steps(rows, y_tiles, tile)
        context_ref[:, lane_tile(tile)] = rows[...].astype(bf16)


def whole_rows(block):
    return block.reshape(block.shape[0] * block.shape[1], block.shape[2])


def head(index):
    return slice(index * HD, (index + 1) * HD)


def weight_copies(full, buffer, place, sems, act):
    col_parts, row_parts = sems.shape
    for k in range(col_parts):
        owner = lax.rem(place[6] + col_parts - k, col_parts)
        for r in range(row_parts):
            act(pltpu.make_async_copy(full.at[r * col_parts + owner], buffer.at[k, r], sems.at[k, r]))


def of_heads(buffer, i):
    return jnp.concatenate([whole_rows(buffer[k, :, :, head(i)]) for k in range(buffer.shape[0])], axis=1)


def gradient_slot(row_parts, order, r):
    position = 0
    for bit in reversed(order):
        position = 2 * position + (1 if r & bit else 0)
    return position // (row_parts // 2), position % (row_parts // 2)


def round_orders(row_parts):
    bits = [1 << i for i in range(row_parts.bit_length() - 1)]
    return bits, bits[::-1]


def gradient_pieces(stacks, row_parts, far, slot):
    found = []
    for r in range(row_parts):
        sent, at = gradient_slot(row_parts, round_orders(row_parts)[far], r)
        found.append(stacks[2 * far + sent].at[at, slot])
    return found


def project_kernel(team, col_parts, row_parts, place, normed_ref, cot_ref, *refs):
    contexts, refs = refs[:team], refs[team:]
    full, refs = refs[0], refs[1:]
    context_t_ref, cot_t_ref, kept_ref = refs[:3]
    context_ref, weights, sems = refs[3:]
    weight_copies(full, weights, place, sems, lambda copy: copy.start())
    width = contexts[0].shape[1]
    for k in range(team):
        lanes = pl.ds(pl.multiple_of((place[0] ^ k) * width, LANES), width)
        context_ref[:, lanes] = contexts[k][...]
    context_t_ref[...] = context_ref[...].T
    cot_t_ref[...] = cot_ref[...].T
    weight_copies(full, weights, place, sems, lambda copy: copy.wait())
    kept_ref[0] = dot(normed_ref[...], of_heads(weights, 0)).astype(bf16)
    kept_ref[1] = dot(context_ref[...], of_heads(weights, 1)).astype(bf16)
    kept_ref[2] = dot(context_ref[...], of_heads(weights, 2)).astype(bf16)


def attend_kernel(team, col_parts, row_parts, place, kept_ref, *refs):
    full, refs = refs[0], refs[1:]
    part_ref, attended_ref, probs_ref, probs_t_ref, weights, sems = refs
    weight_copies(full, weights, place, sems, lambda copy: copy.start())
    length = kept_ref.shape[1]
    rows = lax.broadcasted_iota(jnp.int32, (length, length), 0)
    cols = lax.broadcasted_iota(jnp.int32, (length, length), 1)
    for h in range(col_parts):
        scores = dot_t(kept_ref[0, :, head(h)], kept_ref[1, :, head(h)]) * score_scale
        scores = jnp.where(rows >= cols, scores, -1e30)
        shifted = jnp.exp(scores - jnp.max(scores, axis=-1, keepdims=True))
        inverse = 1.0 / jnp.sum(shifted, axis=-1, keepdims=True)
        probs = (shifted * inverse).astype(bf16)
        probs_ref[h] = probs
        probs_t_ref[h] = probs.T
        attended_ref[:, head(h)] = dot(probs, kept_ref[2, :, head(h)]).astype(bf16)
    weight_copies(full, weights, place, sems, lambda copy: copy.wait())
    part_ref[...] = dot_t(attended_ref[...], of_heads(weights, 3)).astype(bf16)


def gelu_parts(hidden, grad_act):
    density = jnp.exp(-0.5 * hidden * hidden)
    t = 1.0 / (1.0 + (0.3275911 * math.sqrt(0.5)) * jnp.abs(hidden))
    series = 0.5 * 1.061405429
    for factor in (-1.453152027, 1.421413741, -0.284496736, 0.254829592):
        series = series * t + 0.5 * factor
    tail = series * t * density
    cdf = jnp.where(hidden >= 0.0, 1.0 - tail, tail)
    slope = cdf + hidden * density * (1.0 / math.sqrt(2.0 * math.pi))
    return (hidden * cdf).astype(bf16), (grad_act * slope).astype(bf16)


def middle_kernel(team, x_ref, gain_ref, *refs):
    parts, (middle_ref, normed_ref, normed_t_ref) = refs[:team], refs[team:]
    attn = parts[0][...].astype(f32)
    for part in parts[1:]:
        attn = attn + part[...].astype(f32)
    middle = x_ref[...].astype(f32) + attn
    middle_ref[...] = middle
    unit, unused = normalise(middle)
    normed_ref[...] = (unit * gain_ref[...]).astype(bf16)
    normed_t_ref[...] = normed_ref[...].T


def feed_kernel(team, col_parts, row_parts, place, normed_ref, normed_t_ref, cot_ref, cot_t_ref, *refs):
    count = col_parts * row_parts
    pieces, refs = refs[:count], refs[count:]
    outs, two_ref, refs = refs[:team], refs[team], refs[team + 1 :]
    stacks, refs = (refs[:4], refs[4:8]), refs[8:]
    up_all, down_all, grad_up, grad_down, activated_all, grad_all, sems = refs
    z = pl.program_id(0)
    half = col_parts // 2
    hidden_cols = grad_up.shape[3]

    def copies(k):
        found = []
        for r in range(row_parts):
            for which, buffer in enumerate((up_all, down_all)):
                outside = pieces[k * row_parts + r].at[:, pl.ds(which * hidden_cols, hidden_cols)]
                inside = buffer.at[place[2] ^ r, :, pl.ds(k * hidden_cols, hidden_cols)]
                found.append(pltpu.make_async_copy(outside, inside, sems.at[which, k, r]))
        return found

    def each_leaving(k, act):
        for which, buffer in enumerate((grad_up, grad_down)):
            steps = k if which == 0 else lax.rem(place[6] + col_parts - k, col_parts)
            for far in range(2):

                @pl.when(steps // half == far)
                def leaves():
                    slot = lax.rem(steps, half)
                    for r, piece in enumerate(gradient_pieces(stacks[which], row_parts, far, slot)):
                        inner = buffer.at[k, place[2] ^ r]
                        act(pltpu.make_async_copy(inner, piece, sems.at[2 + which, k, r]))

    @pl.when(z == 0)
    def start():
        for k in range(col_parts):
            for copy in copies(k):
                copy.start()

    for k in range(col_parts):

        @pl.when(z == k)
        def arrive():
            for copy in copies(k):
                copy.wait()

    at = pl.ds(pl.multiple_of(z * hidden_cols, hidden_cols), hidden_cols)
    hidden = dot(normed_ref[...], whole_rows(up_all[:, :, at]))
    grad_act = dot(cot_ref[...], whole_rows(down_all[:, :, at]))
    activated, grad_pre = gelu_parts(hidden, grad_act)
    activated_all[:, at] = activated
    grad_all[:, at] = grad_pre
    shape = grad_up.shape[1:]
    grad_up[z] = dot(normed_t_ref[...], grad_pre).astype(bf16).reshape(shape)
    grad_down[z] = dot(cot_t_ref[...], activated).astype(bf16).reshape(shape)

    for k in range(col_parts):

        @pl.when(z == k)
        def leave():
            each_leaving(k, lambda copy: copy.start())

    @pl.when(z == col_parts - 1)
    def finish():
        two_ref[...] = dot_t(grad_all[...], whole_rows(up_all[...])).astype(bf16)
        rows = outs[0].shape[0]
        for k in range(team):
            at_rows = pl.ds(pl.multiple_of((place[0] ^ k) * rows, rows), rows)
            outs[k][...] = dot_t(activated_all[at_rows, :], whole_rows(down_all[...])).astype(bf16)
        for k in range(col_parts):
            each_leaving(k, lambda copy: copy.wait())


def attend_back_kernel(team, col_parts, row_parts, place, middle_ref, gain_ref, cot_ref, *refs):
    parts, refs = refs[:team], refs[team:]
    late, refs = refs[:3], refs[3:]
    full, refs = refs[0], refs[1:]
    middle_grad_ref, gain_grad_ref, one_ref, low = refs[:4]
    grad_q, grad_k, grad_v = refs[4:7]
    context_grads, refs = refs[7 : 7 + team], refs[7 + team :]
    weights, grad_out, total_low = refs[:3]
    held, (sems, late_sems) = refs[3:6], refs[6:]
    kept_ref, probs_ref, probs_t_ref = held
    weight_copies(full, weights, place, sems, lambda copy: copy.start())
    late_copies = [
        pltpu.make_async_copy(outside, inside, late_sems.at[i])
        for i, (outside, inside) in enumerate(zip(late, held))
    ]
    for copy in late_copies:
        copy.start()
    own_rows = middle_ref.shape[0] // team
    grad_two = parts[0][...].astype(f32)
    for part in parts[1:]:
        grad_two = grad_two + part[...].astype(f32)
    unit, inverse = normalise(middle_ref[...])
    grad_gain = grad_two * unit
    rows = lax.broadcasted_iota(jnp.int32, grad_gain.shape, 0)
    first = place[0] * own_rows
    mine = (rows >= first) & (rows < first + own_rows)
    gain_grad_ref[...] = jnp.sum(jnp.where(mine, grad_gain, 0.0), axis=0, keepdims=True)
    grad = cot_ref[...].astype(f32) + normalise_back(unit, inverse, grad_two * gain_ref[...])
    low[...] = grad.astype(bf16)
    for k in range(team):

        @pl.when(place[0] == k)
        def own():
            middle_grad_ref[...] = grad[k * own_rows : (k + 1) * own_rows, :]

    weight_copies(full, weights, place, sems, lambda copy: copy.wait())
    for copy in late_copies:
        copy.wait()
    grad_out[...] = dot(low[...], of_heads(weights, 3)).astype(bf16)
    for h in range(col_parts):
        q, k, v = (kept_ref[i, :, head(h)] for i in range(3))
        grad_heads = grad_out[:, head(h)]
        grad_v[:, head(h)] = dot(probs_t_ref[h], grad_heads).astype(bf16)
        probs = probs_ref[h].astype(f32)
        grad_probs = dot_t(grad_heads, v)
        inner = jnp.sum(grad_probs * probs, axis=-1, keepdims=True)
        grad_scores = (probs * (grad_probs - inner)).astype(bf16)
        grad_q[:, head(h)] = (dot(grad_scores, k) * score_scale).astype(bf16)
        turned = dot_t(v, grad_heads) - inner.T
        turned = (probs_t_ref[h].astype(f32) * turned).astype(bf16)
        grad_k[:, head(h)] = (dot(turned, q) * score_scale).astype(bf16)
    total = dot_t(grad_k[...], of_heads(weights, 1)) + dot_t(grad_v[...], of_heads(weights, 2))
    total_low[...] = total.astype(bf16)
    width = context_grads[0].shape[1]
    for k in range(team):
        lanes = pl.ds(pl.multiple_of((place[0] ^ k) * width, LANES), width)
        context_grads[k][...] = total_low[:, lanes]
    one_ref[...] = dot_t(grad_q[...], of_heads(weights, 0)).astype(bf16)


def head_grads_kernel(col_parts, row_parts, place, low, attended_ref, *refs):
    normed_t_ref, context_t_ref, grad_q, grad_k, grad_v = refs[:5]
    stacks, (grads, out_sems) = refs[5:9], refs[9:]
    half = col_parts // 2
    shape = (*grads.shape[1:3], HD)

    def put(i, grad):
        for h in range(col_parts):
            grads[h, :, :, head(i)] = grad[:, head(h)].astype(bf16).reshape(shape)

    put(0, dot(normed_t_ref[...], grad_q[...]))
    put(1, dot(context_t_ref[...], grad_k[...]))
    put(2, dot(context_t_ref[...], grad_v[...]))
    put(3, dot(low[...].T, attended_ref[...]))
    copies = []
    for k in range(col_parts):
        for r, piece in enumerate(gradient_pieces(stacks, row_parts, k // half, k % half)):
            copies.append(pltpu.make_async_copy(grads.at[k, place[2] ^ r], piece, out_sems.at[k, r]))
    for copy in copies:
        copy.start()
    for copy in copies:
        copy.wait()


def adjoint_kernel(team, logr_ref, *refs):
    parts = refs[:team]
    g_tiles, ends_ref, total_ref, rows = refs[team:]
    grad = parts[0][...].astype(f32)
    for part in parts[1:]:
        grad = grad + part[...].astype(f32)
    grad = grad.astype(bf16).astype(f32)
    tiles, length, unused = g_tiles.shape
    states = logr_ref.shape[0]
    span = length // SUBS
    for tile in range(tiles):
        rows[...] = grad[:, lane_tile(tile)]
        in_steps(g_tiles, tile, rows)
    before = (sub_index() * span).astype(f32)
    for tile in range(tiles):
        rate = jnp.exp(logr_ref[:, lane_tile(tile)])
        decay = jnp.exp(-rate)
        for first in range(0, states, GROUP):
            chosen = range(first, first + GROUP)
            decays = [spread(decay[n : n + 1]) for n in chosen]

            def step(i, held):
                g = g_tiles[tile, step_rows(span - 1 - i), :]
                later = []
                for d, (b, w) in zip(decays, held):
                    shrunk = d * b
                    later.append((g + shrunk, d * w + shrunk))
                return tuple(later)

            zero = no_state(g_tiles)
            held = lax.fori_loop(0, span, step, ((zero, zero),) * GROUP, unroll=4)
            for n, (b, w) in zip(chosen, held):
                ends_ref[0, n, :, lane_tile(tile)] = b
                ends_ref[1, n, :, lane_tile(tile)] = w
                shrink = jnp.exp(-before * rate[n : n + 1])
                total_ref[0, n : n + 1, lane_tile(tile)] = jnp.sum(
                    shrink * b, axis=0, keepdims=True
                )
                total_ref[1, n : n + 1, lane_tile(tile)] = jnp.sum(
                    shrink * (w + before * b), axis=0, keepdims=True
                )


def context_back_kernel(
    team, place, g_tiles, u_tiles, ends_ref, all_ref, logr_ref, coef_ref, one_ref, *refs
):
    pieces = refs[:team]
    grad_ssm_ref, y_tiles, full, rows = refs[team:]
    tiles, length, unused = u_tiles.shape
    states = logr_ref.shape[0]
    span = length // SUBS
    width = tiles * LANES
    index = sub_index()
    after = ((SUBS - 1 - index) * span).astype(f32)
    full[...] = one_ref[...].astype(f32)
    group = GROUP
    for tile in range(tiles):
        lanes = lane_tile(tile)
        rate = jnp.exp(logr_ref[:, lanes])
        decay = jnp.exp(-rate)
        root = jnp.sqrt(2.0 * rate)
        scale = coef_ref[:, lanes] * root
        in_b = jnp.zeros((states, LANES), f32)
        in_w = jnp.zeros((states, LANES), f32)
        for j in range(all_ref.shape[0]):
            gap = j - place[1] - 1
            distance = (jnp.maximum(gap, 0) * length).astype(f32)
            shrink = jnp.exp(-distance * rate)
            b, w = all_ref[j, 0, :, lanes].astype(f32), all_ref[j, 1, :, lanes].astype(f32)
            in_b = in_b + jnp.where(gap >= 0, shrink * b, 0.0)
            in_w = in_w + jnp.where(gap >= 0, shrink * (w + distance * b), 0.0)
        for first in range(0, states, group):
            chosen = range(first, first + group)
            starts = []
            for n in chosen:
                row = rate[n : n + 1]
                b, w = ends_ref[0, n, :, lanes], ends_ref[1, n, :, lanes]
                for d in (1, 2, 4):
                    shrink = jnp.exp(-(d * span) * row)
                    next_b = pltpu.roll(b, SUBS - d, 0)
                    next_w = pltpu.roll(w, SUBS - d, 0)
                    inside = index < SUBS - d
                    b, w = (
                        b + jnp.where(inside, shrink * next_b, 0.0),
                        w + jnp.where(inside, shrink * (next_w + (d * span) * next_b), 0.0),
                    )
                inside = index < SUBS - 1
                b = jnp.where(inside, pltpu.roll(b, SUBS - 1, 0), 0.0)
                w = jnp.where(inside, pltpu.roll(w, SUBS - 1, 0), 0.0)
                shrink = jnp.exp(-after * row)
                b_row, w_row = in_b[n : n + 1], in_w[n : n + 1]
                b = b + shrink * b_row
                w = w + shrink * (w_row + after * b_row)
                zero = no_state(u_tiles)
                starts.append((b, w, zero, zero))
            decays = [spread(decay[n : n + 1]) for n in chosen]
            scales = [spread(scale[n : n + 1]) for n in chosen]

            def step(i, held):
                at = step_rows(span - 1 - i)
                g = g_tiles[tile, at, :]
                u = u_tiles[tile, at, :]
                later, parts = [], []
                for d, s, (b, w, sum_b, sum_w) in zip(decays, scales, held):
                    shrunk = d * b
                    w = d * w + shrunk
                    b = g + shrunk
                    later.append((b, w, sum_b + u * b, sum_w + u * w))
                    parts.append(s * b)
                while len(parts) > 1:
                    parts = [p + q for p, q in zip(parts[::2], parts[1::2])]
                if first > 0:
                    parts[0] = parts[0] + y_tiles[tile, at, :]
                y_tiles[tile, at, :] = parts[0]
                return tuple(later)

            held = lax.fori_loop(0, span, step, tuple(starts), unroll=2)
            for n, (unused_b, unused_w, sum_b, sum_w) in zip(chosen, held):
                sum_b = jnp.sum(sum_b, axis=0, keepdims=True)
                sum_w = jnp.sum(sum_w, axis=0, keepdims=True)
                row = slice(n, n + 1)
                grad_ssm_ref[0, row, lanes] = root[row] * sum_b
                grad_ssm_ref[1, row, lanes] = scale[row] * (0.5 * sum_b - rate[row] * sum_w)
        at_lanes = pl.ds(pl.multiple_of(place[0] * width + tile * LANES, LANES), LANES)
        from_steps(rows, y_tiles, tile)
        full[:, at_lanes] += rows[...].astype(bf16).astype(f32)
    count = pieces[0].shape[0]
    for k in range(team):
        at_rows = pl.ds(pl.multiple_of((place[0] ^ k) * count, count), count)
        pieces[k][...] = full[at_rows, :].astype(bf16)


def input_grad_kernel(team, place, x_ref, gain_ref, middle_grad_ref, *refs):
    parts, (out_ref, gain_grad_ref) = refs[:team], refs[team:]
    rows = out_ref.shape[0]
    at_rows = pl.ds(pl.multiple_of(place[0] * rows, rows), rows)
    grad_one = parts[0][...].astype(f32)
    for part in parts[1:]:
        grad_one = grad_one + part[...].astype(f32)
    unit, inverse = normalise(x_ref[at_rows, :].astype(f32))
    gain_grad_ref[...] = jnp.sum(grad_one * unit, axis=0, keepdims=True)
    back = normalise_back(unit, inverse, grad_one * gain_ref[...])
    out_ref[...] = (middle_grad_ref[...] + back).astype(bf16)


def assemble_kernel(halves, low_count, place, own_ref, *refs):
    others, out_ref = refs[:-1], refs[-1]
    count, rows, unused = own_ref.shape
    half = place[4]

    def put(value, sequence, which, member):
        at_rows = pl.ds(pl.multiple_of((which * low_count + member) * rows, rows), rows)
        out_ref[sequence, at_rows, :] = value.astype(out_ref.dtype)

    for sequence in range(count // (halves * low_count)):
        if halves == 1:
            for member in range(low_count):
                put(own_ref[sequence * low_count + member], sequence, 0, member)
        else:
            put(own_ref[sequence * halves + half], sequence, half, 0)
            put(others[0][sequence], sequence, 1 - half, 0)


def pack_kernel(halves, place, qkv_ref, out_ref, up_ref, down_ref, *refs):
    rows = up_ref.shape[0]
    heads, hidden = out_ref.shape[0] // halves, up_ref.shape[1] // halves
    for which in range(halves):
        side = place[4] if which == 0 else 1 - place[4]
        at_heads = pl.ds(pl.multiple_of(side * heads, LANES), heads)
        at_hidden = pl.ds(pl.multiple_of(side * hidden, LANES), hidden)
        if which == 0:
            head_ref = refs[0]
            wide_ref, deep_ref = refs[1].at[:, :hidden], refs[1].at[:, hidden:]
        else:
            packed = refs[2]
            head_ref = packed.at[:, : 4 * heads]
            wide_ref = packed.at[:, 4 * heads : 4 * heads + hidden]
            deep_ref = packed.at[:, 4 * heads + hidden :]
        for i in range(3):
            head_ref[:, i * heads : (i + 1) * heads] = qkv_ref[i, :, at_heads].astype(bf16)
        head_ref[:, 3 * heads :] = out_ref[at_heads, :].T.astype(bf16)
        wide_ref[...] = up_ref[:, at_hidden].astype(bf16)
        deep_ref[...] = down_ref[at_hidden, :].T.astype(bf16)


def small_kernel(ssm_ref, gains_ref, out_ref):
    count = ssm_ref.shape[0]
    out_ref[:count, :] = ssm_ref[...]
    out_ref[count:, :] = gains_ref[...]


def lamb_moments(weight, grad_item, first_old, second_old):
    first_new = beta_first * first_old + (1.0 - beta_first) * grad_item
    second_new = beta_second * second_old + (1.0 - beta_second) * grad_item * grad_item
    direction = (
        first_new
        / (1.0 - beta_first**STEP)
        / (jnp.sqrt(second_new / (1.0 - beta_second**STEP)) + lamb_eps)
        + weight_decay * weight
    )
    return (first_new, second_new, direction)


def place_sums(sums_ref, sums):
    rows = lax.broadcasted_iota(jnp.int32, sums_ref.shape, 0)
    lanes = lax.broadcasted_iota(jnp.int32, sums_ref.shape, 1)
    found = jnp.zeros(sums_ref.shape, f32)
    for index, pair in sums.items():
        for row, value in enumerate(pair):
            found = jnp.where((rows == row) & (lanes == index), value, found)
    sums_ref[...] = found


def moments_kernel(halves, matrices, place, *refs):
    count = 1 + max(item[1] for item in matrices)
    grads, refs = [refs[halves * i : halves * (i + 1)] for i in range(count)], refs[halves * count :]
    arrays = len({(item[1], item[4] is None) for item in matrices})
    ins = [refs[3 * i : 3 * i + 3] for i in range(arrays)]
    outs = [refs[3 * (arrays + i) : 3 * (arrays + i) + 3] for i in range(arrays)]
    sums_ref = refs[6 * arrays]
    keys = []
    sums = {}
    for number, source, column, turned, stacked in matrices:
        key = (source, stacked is None)
        if key not in keys:
            keys.append(key)
        pick = (lambda ref: ref) if stacked is None else (lambda ref, i=stacked: ref.at[i])
        weight, first, second = (pick(ref) for ref in ins[keys.index(key)])
        news = [pick(ref) for ref in outs[keys.index(key)]]
        width = weight.shape[0 if turned else 1] // halves
        rows = weight.shape[1 if turned else 0]
        cols = slice(column * width, (column + 1) * width)
        total_weight = total_update = 0.0
        for which, grad_ref in enumerate(grads[source]):
            side = place[4] if which == 0 else 1 - place[4]
            at = pl.ds(pl.multiple_of(side * width, width), width)
            if which == 0:
                grad = grad_ref[pl.ds(pl.multiple_of(side * rows, rows), rows), cols].astype(f32)
            else:
                grad = grad_ref[:, cols].astype(f32)
            at = (at, slice(None)) if turned else (slice(None), at)
            grad = grad.T if turned else grad
            old = weight[at]
            found = lamb_moments(old, grad, first[at], second[at])
            for ref, value in zip(news, found):
                ref[at] = value
            total_weight = total_weight + jnp.sum(old * old)
            total_update = total_update + jnp.sum(found[2] * found[2])
        sums[number] = (total_weight, total_update)
    place_sums(sums_ref, sums)


def small_moments_kernel(numbers, grads_ref, *refs):
    ins, outs, sums_ref = (refs[:3], refs[3:6]), (refs[6:9], refs[9:12]), refs[12]
    states = (grads_ref.shape[0] - 2) // 2
    sums = {}
    for (weight, first, second), news, start, rows, first_number in (
        (ins[0], outs[0], 2 * states, 1, numbers[0]),
        (ins[1], outs[1], 0, states, numbers[1]),
    ):
        for i in range(2):
            grad = grads_ref[start + i * rows : start + (i + 1) * rows, :]
            at = slice(i * rows, (i + 1) * rows)
            found = lamb_moments(weight[at, :], grad, first[at, :], second[at, :])
            for ref, value in zip(news, found):
                ref[at, :] = value
            sums[first_number + i] = (
                jnp.sum(weight[at, :] * weight[at, :]),
                jnp.sum(found[2] * found[2]),
            )
    place_sums(sums_ref, sums)


def update_kernel(stacks, sums_ref, *refs):
    count = len(stacks)
    weights, directions, news = refs[:count], refs[count : 2 * count], refs[2 * count : 3 * count]
    norms = jnp.sqrt(jnp.sum(sums_ref[...], axis=0))
    refs[3 * count][...] = norms
    ratios = norms[0:1] / norms[1:2]
    lanes = lax.broadcasted_iota(jnp.int32, ratios.shape, 1)
    for numbers, weight, direction, new in zip(stacks, weights, directions, news):
        step = weight.shape[0] // len(numbers)
        for i, number in enumerate(numbers):
            ratio = jnp.sum(jnp.where(lanes == number, ratios, 0.0), axis=1, keepdims=True)
            at = slice(i * step, (i + 1) * step)
            scale = learn_rate * ratio.reshape((1,) * weight.ndim)
            new[at] = weight[at] - scale * direction[at]


def call(
    body, ins, outs, scratch=(), grid=None, in_specs=None, out_specs=None, time=1.0, after=(), token=False
):
    moved = sum(a.size * a.dtype.itemsize for a in list(ins) + list(outs))
    params = pltpu.CompilerParams(vmem_limit_bytes=VMEM_BYTES)
    cost = pl.CostEstimate(flops=int(time * 1.15e9), bytes_accessed=moved, transcendentals=0)
    whole = pl.BlockSpec(memory_space=pltpu.VMEM)
    anywhere = pl.BlockSpec(memory_space=pl.ANY)
    in_specs = list(in_specs or [whole] * len(ins)) + [anywhere] * len(after)
    out_specs = list(out_specs or [whole] * len(outs))
    outs = list(outs)
    first_out = len(ins) + len(after)
    last_out = first_out + len(outs)
    if token:
        outs.append(jax.ShapeDtypeStruct((SUBS, LANES), f32))
        out_specs.append(whole)

    def run(*refs):
        refs = list(refs)
        if token:
            refs[last_out][...] = jnp.zeros((SUBS, LANES), f32)
            del refs[last_out]
        body(*refs[: len(ins)], *refs[first_out:])

    return pl.pallas_call(
        run,
        out_shape=tuple(outs),
        in_specs=in_specs,
        out_specs=tuple(out_specs),
        scratch_shapes=list(scratch),
        compiler_params=params,
        cost_estimate=cost,
        **({} if grid is None else {"grid": grid}),
    )(*ins, *after)


def shaped(shape, kind):
    return jax.ShapeDtypeStruct(tuple(shape), kind)


def on_device(
    tokens,
    cotangent,
    w_qkv,
    w_out,
    w_up,
    w_down,
    norm_gains,
    ssm_param,
    first_qkv,
    second_qkv,
    first_out,
    second_out,
    first_up,
    second_up,
    first_down,
    second_down,
    first_gain,
    second_gain,
    first_ssm,
    second_ssm,
):
    halves = lax.axis_size("sl")
    low_count = lax.axis_size("ml")
    row_parts = lax.axis_size("sh")
    col_parts = lax.axis_size("mb") * lax.axis_size("mq")
    team = halves * low_count
    sl, ml, mb, mq = (lax.axis_index(name) for name in ("sl", "ml", "mb", "mq"))
    rank = sl * low_count + ml
    block_index = lax.axis_index("sh") * halves + mq
    seq_total, length, width = tokens.shape
    assert length == BLK and seq_total == lax.axis_size("mb")
    states = ssm_param.shape[1]
    channels = width // team
    tiles = channels // LANES
    row_count = width // row_parts
    own_rows = length // team
    place = [rank, block_index, lax.axis_index("sh"), lax.axis_index(MODEL), sl, sl ^ mq]
    place.append(lax.axis_index(COLS))
    place = jnp.stack(place).astype(jnp.int32)
    smem = pl.BlockSpec(memory_space=pltpu.SMEM)
    vmem = pl.BlockSpec(memory_space=pltpu.VMEM)

    def permute(value, axes, moves):
        return lax.ppermute(value, axes, moves)

    def swap(value):
        return permute(value, "sl", [(0, 1), (1, 0)])

    def in_order(own, other, axis):
        return jnp.where(
            sl == 0, jnp.concatenate([own, other], axis), jnp.concatenate([other, own], axis)
        )

    def team_send(pieces):
        moved = [pieces[0]]
        for k in range(1, team):
            moved.append(permute(pieces[k], TEAM, [(i, i ^ k) for i in range(team)]))
        return moved

    def pick_block(array):
        own = lax.dynamic_index_in_dim(array, mb, 0, keepdims=False)
        if halves == 1:
            return own, ()
        other = swap(own)
        return jnp.where(sl == mq, own, other), (other,)

    def across(value, bit):
        return permute(value, "sh", [(i, i ^ bit) for i in range(row_parts)])

    def along(value, axes, step):
        count = lax.axis_size(axes)
        return permute(value, axes, [(i, (i + step) % count) for i in range(count)])

    bits = [1 << i for i in range(row_parts.bit_length() - 1)]

    def bit_order(k):
        return bits if k % 2 == 0 else bits[::-1]

    def double_rows(value, order):
        found = {0: value}
        for bit in order:
            for r in list(found):
                found[r | bit] = across(found[r], bit)
        return [found[r] for r in range(row_parts)]

    def add(*items, zero=None):
        total = sum(item.astype(f32) for item in items)
        return (total if zero is None else total + zero[0, 0]).astype(bf16)

    def first_messages(stacks):
        return across(stacks[1], bits[-1]), across(stacks[3], bits[0])

    def halve_rows(keep, arrived, order, zero, after, last):
        items = [keep, arrived]
        for bit in order[-2::-1]:
            count = arrived.shape[0] // 2
            sent = add(*[item[count:] for item in items], zero=zero)
            arrived = across(hold((sent,), after)[0] if after else sent, bit)
            items = [item[:count] for item in items] + [arrived]
        return add(*[item[0] for item in items], zero=last)

    def halve_both(stacks, first, zero, after=(), last=None):
        near = halve_rows(stacks[0], first[0], bits, zero, after, last)
        return near, halve_rows(stacks[2], first[1], bits[::-1], zero, after, last)

    def hold(arrays, after):
        anywhere = pl.BlockSpec(memory_space=pl.ANY)
        return pl.pallas_call(
            lambda *refs: None,
            out_shape=tuple(shaped(item.shape, item.dtype) for item in arrays),
            in_specs=[anywhere] * (len(arrays) + len(after)),
            out_specs=(anywhere,) * len(arrays),
            input_output_aliases={i: i for i in range(len(arrays))},
        )(*arrays, *after)

    def gather_pieces(shard):
        pieces = []
        for k in range(col_parts):
            held = along(shard, COLS, k) if k > 0 else shard
            pieces.append(double_rows(held, bits if k % 2 == 0 else bits[::-1]))
        return pieces

    def sum_over_z(near, far, ring=True):
        if not ring:
            pieces = [stack[k] for stack in (near, far) for k in range(col_parts // 2)]
            moved = [along(piece, COLS, -k) for k, piece in enumerate(pieces) if k > 0]
            return add(pieces[0], *moved)
        held = None
        for stack in (far, near):
            for k in reversed(range(stack.shape[0])):
                held = stack[k] if held is None else add(stack[k], along(held, COLS, -1))
        return held

    def everywhere(value, axes):
        count = lax.axis_size(axes)
        copies = jnp.broadcast_to(value[None], (count, *value.shape))
        return lax.all_to_all(copies, axes, 0, 0, tiled=True)

    rows_dev = w_up.shape[0]
    hidden_cols = w_up.shape[1] // halves
    head_cols = 4 * w_out.shape[0] // halves
    packed_cols = head_cols + 2 * hidden_cols
    sides = [shaped((rows_dev, cols), bf16) for cols in (head_cols, 2 * hidden_cols)]
    shards = call(
        functools.partial(pack_kernel, halves),
        (place, w_qkv, w_out, w_up, w_down),
        sides + [shaped((rows_dev, packed_cols), bf16)] * (halves - 1),
        time=2.4,
        in_specs=[smem] + [vmem] * 4,
    )
    if halves == 2:
        other = swap(shards[2])
        cuts = (0, head_cols, packed_cols)
        shards = [
            in_order(own, other[:, first:last], 0)
            for own, first, last in zip(shards, cuts, cuts[1:])
        ]
    head_shard, hidden_shard = shards[:2]
    small, = call(
        small_kernel,
        (ssm_param.reshape(2 * states, -1), norm_gains),
        (shaped((2 * states + 2, norm_gains.shape[1]), f32),),
        after=(head_shard,),
    )
    small = jnp.transpose(everywhere(small, ALL), (1, 0, 2)).reshape(2 * states + 2, width)
    own_ssm = lax.dynamic_slice_in_dim(
        small[: 2 * states].reshape(2, states, width), rank * channels, channels, 2
    )
    coef, logr = own_ssm[0], own_ssm[1]
    gain_one = small[2 * states : 2 * states + 1]
    gain_two = small[2 * states + 1 : 2 * states + 2]

    attn_w = lax.all_gather(head_shard, COPIES, axis=0, tiled=False)
    hidden_w = gather_pieces(hidden_shard)
    hidden_flat = [piece for group in hidden_w for piece in group]

    x, unused = pick_block(tokens)
    cot, cot_other = pick_block(cotangent)

    anywhere = [pl.BlockSpec(memory_space=pl.ANY)]

    def fixed(*shape):
        return pl.BlockSpec(shape, lambda z: (0,) * len(shape))

    wide = fixed(length, width)
    row = fixed(1, width)

    normed_one, normed_t, u_steps, ends, total = call(
        norm_kernel,
        (place, x, gain_one, logr),
        (
            shaped((length, width), bf16),
            shaped((width, length), bf16),
            shaped((tiles, length, LANES), f32),
            shaped((states, SUBS, channels), f32),
            shaped((states, channels), f32),
        ),
        scratch=[pltpu.VMEM((length, LANES), f32)],
        in_specs=[smem, vmem, vmem, vmem],
        after=(*hidden_w[0][1:-1], *cot_other),
        time=5,
    )
    totals = everywhere(total.astype(bf16), ("sh", "mq"))
    (context_own,) = call(
        context_kernel,
        (place, u_steps, ends, totals, logr, coef),
        (shaped((length, channels), bf16),),
        after=(hidden_w[0][-1], *hidden_w[1][1:-1], *[group[0] for group in hidden_w[1:]]),
        scratch=[pltpu.VMEM((tiles, length, LANES), f32), pltpu.VMEM((length, LANES), f32)],
        in_specs=[smem] + [vmem] * 5,
        time=7,
    )
    contexts = team_send([context_own] * team)

    stack_shape = (row_parts // 2, col_parts // 2, row_count)
    head_stacks = [shaped((*stack_shape, head_cols), bf16)] * 4
    hidden_stacks = [shaped((*stack_shape, hidden_cols), bf16)] * 8
    sizes = (team, col_parts, row_parts)
    head_buffer = pltpu.VMEM((col_parts, row_parts, row_count, 4 * HD), bf16)
    head_sems = pltpu.SemaphoreType.DMA((col_parts, row_parts))
    kept_shape = shaped((3, length, col_parts * HD), bf16)
    flat_shape = shaped((length, col_parts * HD), bf16)
    context_t, cot_t, kept = call(
        functools.partial(project_kernel, *sizes),
        (place, normed_one, cot, *contexts, attn_w),
        (shaped((width, length), bf16), shaped((width, length), bf16), kept_shape),
        scratch=[pltpu.VMEM((length, width), bf16), head_buffer, head_sems],
        time=1,
        in_specs=[smem] + [vmem] * (2 + team) + anywhere * 1,
        after=(hidden_w[1][-1], *[piece for group in hidden_w[2:3] for piece in group[1:]]),
    )
    attn_part, attended, probs, probs_t = call(
        functools.partial(attend_kernel, *sizes),
        (place, kept, attn_w),
        (
            shaped((length, width), bf16),
            flat_shape,
            *[shaped((col_parts, length, length), bf16)] * 2,
        ),
        scratch=[head_buffer, head_sems],
        time=1,
        in_specs=[smem, vmem] + anywhere * 1,
        after=[piece for group in hidden_w[3:] for piece in group[1:-1]],
    )
    attn_parts = team_send([attn_part] * team)

    middle, normed_two, normed_two_t = call(
        functools.partial(middle_kernel, team),
        (x, gain_two, *attn_parts),
        (shaped((length, width), f32), shaped((length, width), bf16), shaped((width, length), bf16)),
        time=1,
    )
    weight_buffer = pltpu.VMEM((row_parts, row_count, col_parts * hidden_cols), bf16)
    grad_buffer = pltpu.VMEM((col_parts, row_parts, row_count, hidden_cols), bf16)
    fed = call(
        functools.partial(feed_kernel, team, col_parts, row_parts),
        (place, normed_two, normed_two_t, cot, cot_t, *hidden_flat),
        (
            *[shaped((own_rows, width), bf16)] * team,
            shaped((length, width), bf16),
            *hidden_stacks,
        ),
        scratch=[
            *[weight_buffer] * 2,
            *[grad_buffer] * 2,
            *[pltpu.VMEM((length, col_parts * hidden_cols), bf16)] * 2,
            pltpu.SemaphoreType.DMA((4, col_parts, row_parts)),
        ],
        time=18,
        grid=(col_parts,),
        in_specs=[smem, wide, fixed(width, length), wide, fixed(width, length)]
        + anywhere * len(hidden_flat),
        out_specs=[fixed(own_rows, width)] * team + [wide] + anywhere * 8,
    )
    out_pieces, two_part, hidden_grads = fed[:team], fed[team], fed[team + 1 :]
    two_parts = team_send([two_part] * team)

    def rows_of(array, member):
        return lax.dynamic_slice_in_dim(array, member * own_rows, own_rows, 0)

    def share_rows(pieces, kind):
        others = []
        if halves == 2:
            pairs = pieces.reshape(seq_total, halves, own_rows, width)
            others = [swap(lax.dynamic_index_in_dim(pairs, 1 - sl, 1, keepdims=False))]
        (blocks,) = call(
            functools.partial(assemble_kernel, halves, low_count),
            (place, pieces, *others),
            (shaped((seq_total, length, width), kind),),
            time=3.5,
            in_specs=[smem, vmem] + [vmem] * len(others),
        )
        return blocks

    out_pieces = team_send(list(out_pieces))
    result = rows_of(middle, rank) + sum(item.astype(f32) for item in out_pieces)
    result = result.astype(bf16)
    layer_pieces = lax.all_gather(result, MODEL, axis=0, tiled=False)
    layer_out = share_rows(layer_pieces, bf16)

    def both_halves(own):
        if halves == 1:
            return [own]
        return [own, swap(lax.dynamic_slice_in_dim(own, (1 - sl) * rows_dev, rows_dev, 0))]

    middle_grad, gain_two_grad, one_part, low_grad, *rest = call(
        functools.partial(attend_back_kernel, *sizes),
        (place, middle, gain_two, cot, *two_parts, kept, probs, probs_t, attn_w),
        (
            shaped((own_rows, width), f32),
            shaped((1, width), f32),
            shaped((length, width), bf16),
            shaped((length, width), bf16),
            *[flat_shape] * 3,
            *[shaped((length, channels), bf16)] * team,
        ),
        scratch=[
            head_buffer,
            pltpu.VMEM(flat_shape.shape, bf16),
            pltpu.VMEM((length, width), bf16),
            pltpu.VMEM(kept_shape.shape, bf16),
            *[pltpu.VMEM((col_parts, length, length), bf16)] * 2,
            head_sems,
            pltpu.SemaphoreType.DMA((3,)),
        ],
        time=1,
        in_specs=[smem] + [vmem] * (3 + team) + anywhere * (3 + 1),
        after=(result,),
    )
    head_grads, context_grads = rest[:3], rest[3:]
    context_grads = team_send(context_grads)
    *head_stacks, heads_done = call(
        functools.partial(head_grads_kernel, col_parts, row_parts),
        (place, low_grad, attended, normed_t, context_t, *head_grads),
        head_stacks,
        scratch=[head_buffer, head_sems],
        time=8,
        in_specs=[smem] + [vmem] * 7,
        out_specs=anywhere * 4,
        token=True,
    )
    down_first = first_messages(hidden_grads[4:])
    g_steps, adjoint_ends, adjoint_total, adjoint_done = call(
        functools.partial(adjoint_kernel, team),
        (logr, *context_grads),
        (
            shaped((tiles, length, LANES), f32),
            shaped((2, states, SUBS, channels), f32),
            shaped((2, states, channels), f32),
        ),
        scratch=[pltpu.VMEM((length, LANES), f32)],
        time=1,
        after=(*down_first, heads_done),
        token=True,
    )
    adjoint_totals = everywhere(adjoint_total.astype(bf16), ("sh", "mq"))
    up_stacks = list(hidden_grads[:4])
    up_stacks[1::2] = hold(up_stacks[1::2], (adjoint_totals,))
    up_first = first_messages(up_stacks)
    *one_pieces, grad_ssm, context_done = call(
        functools.partial(context_back_kernel, team),
        (place, g_steps, u_steps, adjoint_ends, adjoint_totals, logr, coef, one_part),
        (
            *[shaped((own_rows, width), bf16)] * team,
            shaped((2, states, channels), f32),
        ),
        scratch=[
            pltpu.VMEM((tiles, length, LANES), f32),
            pltpu.VMEM((length, width), f32),
            pltpu.VMEM((length, LANES), f32),
        ],
        in_specs=[smem] + [vmem] * 7,
        time=1,
        after=up_stacks[1::2],
        token=True,
    )
    one_pieces = team_send(one_pieces)
    down_sums = halve_both(hidden_grads[4:], down_first, adjoint_done, (adjoint_totals,), context_done)
    grad_rows, gain_one_grad, rows_done = call(
        functools.partial(input_grad_kernel, team),
        (place, x, gain_one, middle_grad, *one_pieces),
        (shaped((own_rows, width), bf16), shaped((1, width), f32)),
        in_specs=[smem] + [vmem] * (3 + team),
        time=1,
        after=(layer_pieces, *up_first),
        token=True,
    )
    grad_down = lax.psum_scatter(
        jnp.concatenate(down_sums, 0), COLS, scatter_dimension=0, tiled=False
    )
    head_stacks[1::2] = hold(head_stacks[1::2], (grad_rows,))
    head_sums = halve_both(head_stacks, first_messages(head_stacks), rows_done)
    up_sums = halve_both(up_stacks, up_first, rows_done)
    grad_up = sum_over_z(*up_sums)
    grad_heads = sum_over_z(*head_sums)
    input_grad = share_rows(lax.all_gather(grad_rows, MODEL, axis=0, tiled=False), f32)

    placed_ssm = lax.dynamic_update_slice_in_dim(
        jnp.zeros((2 * states, width), f32),
        grad_ssm.reshape(2 * states, channels),
        rank * channels,
        1,
    )
    small_grads = jnp.concatenate([placed_ssm, gain_one_grad, gain_two_grad], 0)
    (small_grads,) = hold((small_grads,), head_sums)
    small_grads = small_grads.reshape(2 * states + 2, lax.axis_size(ALL), -1)
    small_grads = lax.all_to_all(jnp.transpose(small_grads, (1, 0, 2)), ALL, 0, 0, tiled=True)
    small_grads = jnp.sum(small_grads, axis=0)

    def moments(matrices, grads, arrays, after=()):
        changed = [shaped(old.shape, f32) for group in arrays for old in group]
        grad_parts = [part for grad in grads for part in both_halves(grad)]
        ins = [item for group in arrays for item in group]
        *found, sums = call(
            functools.partial(moments_kernel, halves, matrices),
            (place, *grad_parts, *ins),
            (*changed, shaped((2, LANES), f32)),
            in_specs=[smem] + [vmem] * (len(grad_parts) + len(ins)),
            after=after,
            time=4,
        )
        return [found[3 * i : 3 * i + 3] for i in range(len(arrays))], sums

    hidden_new, hidden_sums = moments(
        ((4, 0, 0, False, None), (5, 1, 0, True, None)),
        (grad_up, grad_down),
        ((w_up, first_up, second_up), (w_down, first_down, second_down)),
    )
    heads_new, head_sums = moments(
        tuple((i, 0, i, False, i) for i in range(3)) + ((3, 0, 3, True, None),),
        (grad_heads,),
        ((w_qkv, first_qkv, second_qkv), (w_out, first_out, second_out)),
        (layer_out, input_grad),
    )
    own_channels = norm_gains.shape[1]
    ssm_items = [item.reshape(2 * states, own_channels) for item in (ssm_param, first_ssm, second_ssm)]
    small_items = [norm_gains, first_gain, second_gain, *ssm_items]
    *small_new, small_sums = call(
        functools.partial(small_moments_kernel, (6, 8)),
        (small_grads.reshape(2 * states + 2, own_channels), *small_items),
        (*[shaped(item.shape, f32) for item in small_items], shaped((2, LANES), f32)),
    )
    all_sums = everywhere(hidden_sums + head_sums + small_sums, ALL)
    masters = (w_qkv, w_out, w_up, w_down, norm_gains, ssm_items[0])
    news = (*heads_new, *hidden_new, small_new[:3], small_new[3:])
    *weights, norms = call(
        functools.partial(update_kernel, ((0, 1, 2), (3,), (4,), (5,), (6, 7), (8, 9))),
        (all_sums, *masters, *[group[2] for group in news]),
        (*[shaped(item.shape, f32) for item in masters], shaped((2, LANES), f32)),
        time=3.2,
    )
    outputs = [layer_out, input_grad]
    for index, (weight, (first_new, second_new, unused)) in enumerate(zip(weights, news)):
        if index == 4:
            outputs += [weight, first_new, second_new[0], second_new[1]]
        else:
            kept_shape = ssm_param.shape if index == 5 else weight.shape
            outputs += [item.reshape(kept_shape) for item in (weight, first_new, second_new)]
    outputs.append(norms[:, :10])
    return tuple(outputs)


def solution(mesh):
    seq_count, model_count = mesh.shape["seq"], mesh.shape["mp"]
    halves = 2 if HEADS // model_count >= 2 else 1
    sizes = (seq_count // halves, halves, SEQS, halves, model_count // (SEQS * halves))
    fine = Mesh(mesh.devices.reshape(sizes), ALL)
    seq, model = ("sh", "sl"), ("mb", "mq", "ml")
    rows_cols, cols_rows = P(seq, model), P(model, seq)
    token = P(None, seq, None)
    stack = P(None, seq, model)
    gains = P(None, ALL)
    ssm = P(None, None, ALL)
    return jax.shard_map(
        on_device,
        mesh=fine,
        in_specs=(token, token, stack, cols_rows, rows_cols, cols_rows, gains, ssm)
        + (stack,) * 2
        + (cols_rows,) * 2
        + (rows_cols,) * 2
        + (cols_rows,) * 2
        + (gains,) * 2
        + (ssm,) * 2,
        out_specs=(token, token)
        + (stack,) * 3
        + (cols_rows,) * 3
        + (rows_cols,) * 3
        + (cols_rows,) * 3
        + (gains, gains, P(ALL), P(ALL))
        + (ssm,) * 3
        + (P(),),
        check_vma=False,
    )
```

```python
import functools
import math

import jax
import jax.numpy as jnp
from jax import lax
from jax.experimental import pallas as pl
from jax.experimental.pallas import tpu as pltpu
from jax.sharding import Mesh
from jax.sharding import PartitionSpec as P

HD = 128
HEADS = 8
BLK = 512
STEP = 10
SEQS = 2
LANES = 128
SUBS = 8
GROUP = 8

norm_eps = 1e-05
beta_first = 0.9
beta_second = 0.999
lamb_eps = 1e-06
weight_decay = 0.01
learn_rate = 0.5
score_scale = HD ** (-0.5)

f32 = jnp.float32
bf16 = jnp.bfloat16
VMEM_BYTES = 56 * 1024 * 1024

ALL = ("sh", "sl", "mb", "mq", "ml")
MODEL = ("mb", "mq", "ml")
COLS = ("mb", "mq")
TEAM = ("sl", "ml")


def dot(left, right):
    return lax.dot_general(left, right, (((1,), (0,)), ((), ())), preferred_element_type=f32)


def dot_t(left, right):
    return lax.dot_general(left, right, (((1,), (1,)), ((), ())), preferred_element_type=f32)


def normalise(values):
    centred = values - jnp.mean(values, axis=-1, keepdims=True)
    inverse = lax.rsqrt(jnp.mean(centred * centred, axis=-1, keepdims=True) + norm_eps)
    return centred * inverse, inverse


def normalise_back(unit, inverse, grad_unit):
    mean_one = jnp.mean(grad_unit, axis=-1, keepdims=True)
    mean_two = jnp.mean(grad_unit * unit, axis=-1, keepdims=True)
    return inverse * (grad_unit - mean_one - unit * mean_two)


def sub_index():
    return lax.broadcasted_iota(jnp.int32, (SUBS, LANES), 0)


def spread(row):
    return jnp.broadcast_to(row, (SUBS, LANES))


def lane_tile(index):
    return slice(index * LANES, (index + 1) * LANES)


def no_state(tiles):
    rows = tiles[0, :SUBS, :]
    return rows - rows


def in_steps(steps, tile, rows):
    span = rows.shape[0] // SUBS

    def move(i, unused):
        steps[tile, pl.ds(pl.multiple_of(i * SUBS, SUBS), SUBS), :] = rows[
            pl.ds(i, SUBS, stride=span), :
        ]
        return unused

    lax.fori_loop(0, span, move, 0, unroll=8)


def from_steps(rows, steps, tile):
    span = rows.shape[0] // SUBS

    def move(i, unused):
        rows[pl.ds(i, SUBS, stride=span), :] = steps[
            tile, pl.ds(pl.multiple_of(i * SUBS, SUBS), SUBS), :
        ]
        return unused

    lax.fori_loop(0, span, move, 0, unroll=8)


def step_rows(i):
    return pl.ds(pl.multiple_of(i * SUBS, SUBS), SUBS)


def norm_kernel(
    place, x_ref, gain_ref, logr_ref, normed_ref, turned_ref, u_tiles, ends_ref, total_ref, rows
):
    unit, unused = normalise(x_ref[...].astype(f32))
    normed_ref[...] = (unit * gain_ref[...]).astype(bf16)
    turned_ref[...] = normed_ref[...].T
    tiles, length, unused = u_tiles.shape
    states = logr_ref.shape[0]
    span = length // SUBS
    for tile in range(tiles):
        start = place[0] * (tiles * LANES) + tile * LANES
        rows[...] = normed_ref[:, pl.ds(pl.multiple_of(start, LANES), LANES)].astype(f32)
        in_steps(u_tiles, tile, rows)
    left = ((SUBS - 1 - sub_index()) * span).astype(f32)
    for tile in range(tiles):
        rate = jnp.exp(logr_ref[:, lane_tile(tile)])
        decay = jnp.exp(-rate)
        decays = [spread(decay[n : n + 1]) for n in range(states)]

        def step(i, held):
            u = u_tiles[tile, step_rows(i), :]
            return tuple(d * h + u for d, h in zip(decays, held))

        zero = no_state(u_tiles)
        held = lax.fori_loop(0, span, step, (zero,) * states, unroll=4)
        for n in range(states):
            ends_ref[n, :, lane_tile(tile)] = held[n]
            total_ref[n : n + 1, lane_tile(tile)] = jnp.sum(
                held[n] * jnp.exp(-left * rate[n : n + 1]), axis=0, keepdims=True
            )


def context_kernel(
    place, u_tiles, ends_ref, all_ref, logr_ref, coef_ref, context_ref, y_tiles, rows
):
    tiles, length, unused = u_tiles.shape
    states = logr_ref.shape[0]
    span = length // SUBS
    index = sub_index()
    before = (index * span).astype(f32)
    for tile in range(tiles):
        rate = jnp.exp(logr_ref[:, lane_tile(tile)])
        decay = jnp.exp(-rate)
        scale = coef_ref[:, lane_tile(tile)] * jnp.sqrt(2.0 * rate)
        incoming = jnp.zeros((states, LANES), f32)
        for j in range(all_ref.shape[0]):
            gap = place[1] - 1 - j
            distance = (jnp.maximum(gap, 0) * length).astype(f32)
            term = jnp.exp(-distance * rate) * all_ref[j, :, lane_tile(tile)].astype(f32)
            incoming = incoming + jnp.where(gap >= 0, term, 0.0)
        for first in range(0, states, GROUP):
            chosen = range(first, first + GROUP)
            starts = []
            for n in chosen:
                row = rate[n : n + 1]
                run = ends_ref[n, :, lane_tile(tile)]
                for d in (1, 2, 4):
                    moved = jnp.exp(-(d * span) * row) * pltpu.roll(run, d, 0)
                    run = run + jnp.where(index >= d, moved, 0.0)
                run = jnp.where(index >= 1, pltpu.roll(run, 1, 0), 0.0)
                starts.append(run + jnp.exp(-before * row) * incoming[n : n + 1])
            decays = [spread(decay[n : n + 1]) for n in chosen]
            scales = [spread(scale[n : n + 1]) for n in chosen]

            def step(i, held):
                at = step_rows(i)
                u = u_tiles[tile, at, :]
                held = tuple(d * h + u for d, h in zip(decays, held))
                parts = [s * h for s, h in zip(scales, held)]
                if first > 0:
                    parts[0] = parts[0] + y_tiles[tile, at, :]
                while len(parts) > 1:
                    parts = [a + b for a, b in zip(parts[::2], parts[1::2])]
                y_tiles[tile, at, :] = parts[0]
                return held

            lax.fori_loop(0, span, step, tuple(starts), unroll=4)
        from_steps(rows, y_tiles, tile)
        context_ref[:, lane_tile(tile)] = rows[...].astype(bf16)


def whole_rows(block):
    return block.reshape(block.shape[0] * block.shape[1], block.shape[2])


def head(index):
    return slice(index * HD, (index + 1) * HD)


def weight_copies(near, far, buffer, place, sems, act):
    count = sems.shape[0]
    half = count // 2
    for k in range(count):
        owner = lax.rem(place[6] + count - k, count)
        for stacks, low in ((near, 0), (far, half)):

            @pl.when((owner >= low) & (owner < low + half))
            def move():
                for r, stack in enumerate(stacks):
                    inner = buffer.at[k, place[2] ^ r]
                    act(pltpu.make_async_copy(stack.at[owner - low], inner, sems.at[k, r]))


def of_heads(buffer, i):
    return jnp.concatenate([whole_rows(buffer[k, :, :, head(i)]) for k in range(buffer.shape[0])], axis=1)


def gradient_slot(row_parts, order, r):
    position = 0
    for bit in reversed(order):
        position = 2 * position + (1 if r & bit else 0)
    return position // (row_parts // 2), position % (row_parts // 2)


def round_orders(row_parts):
    bits = [1 << i for i in range(row_parts.bit_length() - 1)]
    return bits, bits[::-1]


def gradient_pieces(stacks, row_parts, far, slot):
    found = []
    for r in range(row_parts):
        sent, at = gradient_slot(row_parts, round_orders(row_parts)[far], r)
        found.append(stacks[2 * far + sent].at[at, slot])
    return found


def project_kernel(team, col_parts, row_parts, place, normed_ref, cot_ref, *refs):
    contexts, refs = refs[:team], refs[team:]
    near, far, refs = refs[:row_parts], refs[row_parts : 2 * row_parts], refs[2 * row_parts :]
    context_t_ref, cot_t_ref, kept_ref = refs[:3]
    context_ref, weights, sems = refs[3:]
    weight_copies(near, far, weights, place, sems, lambda copy: copy.start())
    width = contexts[0].shape[1]
    for k in range(team):
        lanes = pl.ds(pl.multiple_of((place[0] ^ k) * width, LANES), width)
        context_ref[:, lanes] = contexts[k][...]
    context_t_ref[...] = context_ref[...].T
    cot_t_ref[...] = cot_ref[...].T
    weight_copies(near, far, weights, place, sems, lambda copy: copy.wait())
    kept_ref[0] = dot(normed_ref[...], of_heads(weights, 0)).astype(bf16)
    kept_ref[1] = dot(context_ref[...], of_heads(weights, 1)).astype(bf16)
    kept_ref[2] = dot(context_ref[...], of_heads(weights, 2)).astype(bf16)


def attend_kernel(team, col_parts, row_parts, place, kept_ref, *refs):
    near, far, refs = refs[:row_parts], refs[row_parts : 2 * row_parts], refs[2 * row_parts :]
    part_ref, attended_ref, probs_ref, probs_t_ref, weights, sems = refs
    weight_copies(near, far, weights, place, sems, lambda copy: copy.start())
    length = kept_ref.shape[1]
    rows = lax.broadcasted_iota(jnp.int32, (length, length), 0)
    cols = lax.broadcasted_iota(jnp.int32, (length, length), 1)
    for h in range(col_parts):
        scores = dot_t(kept_ref[0, :, head(h)], kept_ref[1, :, head(h)]) * score_scale
        scores = jnp.where(rows >= cols, scores, -1e30)
        shifted = jnp.exp(scores - jnp.max(scores, axis=-1, keepdims=True))
        inverse = 1.0 / jnp.sum(shifted, axis=-1, keepdims=True)
        probs = (shifted * inverse).astype(bf16)
        probs_ref[h] = probs
        probs_t_ref[h] = probs.T
        attended_ref[:, head(h)] = dot(probs, kept_ref[2, :, head(h)]).astype(bf16)
    weight_copies(near, far, weights, place, sems, lambda copy: copy.wait())
    part_ref[...] = dot_t(attended_ref[...], of_heads(weights, 3)).astype(bf16)


def gelu_parts(hidden, grad_act):
    density = jnp.exp(-0.5 * hidden * hidden)
    t = 1.0 / (1.0 + (0.3275911 * math.sqrt(0.5)) * jnp.abs(hidden))
    series = 0.5 * 1.061405429
    for factor in (-1.453152027, 1.421413741, -0.284496736, 0.254829592):
        series = series * t + 0.5 * factor
    tail = series * t * density
    cdf = jnp.where(hidden >= 0.0, 1.0 - tail, tail)
    slope = cdf + hidden * density * (1.0 / math.sqrt(2.0 * math.pi))
    return (hidden * cdf).astype(bf16), (grad_act * slope).astype(bf16)


def middle_kernel(team, x_ref, gain_ref, *refs):
    parts, (middle_ref, normed_ref, normed_t_ref) = refs[:team], refs[team:]
    attn = parts[0][...].astype(f32)
    for part in parts[1:]:
        attn = attn + part[...].astype(f32)
    middle = x_ref[...].astype(f32) + attn
    middle_ref[...] = middle
    unit, unused = normalise(middle)
    normed_ref[...] = (unit * gain_ref[...]).astype(bf16)
    normed_t_ref[...] = normed_ref[...].T


def feed_kernel(team, col_parts, row_parts, place, normed_ref, normed_t_ref, cot_ref, cot_t_ref, *refs):
    count = col_parts * row_parts
    pieces, refs = refs[:count], refs[count:]
    outs, two_ref, refs = refs[:team], refs[team], refs[team + 1 :]
    stacks, refs = (refs[:4], refs[4:8]), refs[8:]
    up_all, down_all, grad_up, grad_down, activated_all, grad_all, sems = refs
    z = pl.program_id(0)
    half = col_parts // 2
    hidden_cols = grad_up.shape[3]

    def copies(k):
        found = []
        for r in range(row_parts):
            for which, buffer in enumerate((up_all, down_all)):
                outside = pieces[k * row_parts + r].at[:, pl.ds(which * hidden_cols, hidden_cols)]
                inside = buffer.at[place[2] ^ r, :, pl.ds(k * hidden_cols, hidden_cols)]
                found.append(pltpu.make_async_copy(outside, inside, sems.at[which, k, r]))
        return found

    def each_leaving(k, act):
        for which, buffer in enumerate((grad_up, grad_down)):
            for r, piece in enumerate(gradient_pieces(stacks[which], row_parts, k // half, k % half)):
                inner = buffer.at[k, place[2] ^ r]
                act(pltpu.make_async_copy(inner, piece, sems.at[2 + which, k, r]))

    @pl.when(z == 0)
    def start():
        for k in range(col_parts):
            for copy in copies(k):
                copy.start()

    for k in range(col_parts):

        @pl.when(z == k)
        def arrive():
            for copy in copies(k):
                copy.wait()

    at = pl.ds(pl.multiple_of(z * hidden_cols, hidden_cols), hidden_cols)
    hidden = dot(normed_ref[...], whole_rows(up_all[:, :, at]))
    grad_act = dot(cot_ref[...], whole_rows(down_all[:, :, at]))
    activated, grad_pre = gelu_parts(hidden, grad_act)
    activated_all[:, at] = activated
    grad_all[:, at] = grad_pre
    shape = grad_up.shape[1:]
    grad_up[z] = dot(normed_t_ref[...], grad_pre).astype(bf16).reshape(shape)
    grad_down[z] = dot(cot_t_ref[...], activated).astype(bf16).reshape(shape)

    for k in range(col_parts):

        @pl.when(z == k)
        def leave():
            each_leaving(k, lambda copy: copy.start())

    @pl.when(z == col_parts - 1)
    def finish():
        two_ref[...] = dot_t(grad_all[...], whole_rows(up_all[...])).astype(bf16)
        rows = outs[0].shape[0]
        for k in range(team):
            at_rows = pl.ds(pl.multiple_of((place[0] ^ k) * rows, rows), rows)
            outs[k][...] = dot_t(activated_all[at_rows, :], whole_rows(down_all[...])).astype(bf16)
        for k in range(col_parts):
            each_leaving(k, lambda copy: copy.wait())


def attend_back_kernel(team, col_parts, row_parts, place, middle_ref, gain_ref, cot_ref, *refs):
    parts, refs = refs[:team], refs[team:]
    late, refs = refs[:3], refs[3:]
    near, far, refs = refs[:row_parts], refs[row_parts : 2 * row_parts], refs[2 * row_parts :]
    middle_grad_ref, gain_grad_ref, one_ref, low = refs[:4]
    grad_q, grad_k, grad_v = refs[4:7]
    context_grads, refs = refs[7 : 7 + team], refs[7 + team :]
    weights, grad_out, total_low = refs[:3]
    held, (sems, late_sems) = refs[3:6], refs[6:]
    kept_ref, probs_ref, probs_t_ref = held
    weight_copies(near, far, weights, place, sems, lambda copy: copy.start())
    late_copies = [
        pltpu.make_async_copy(outside, inside, late_sems.at[i])
        for i, (outside, inside) in enumerate(zip(late, held))
    ]
    for copy in late_copies:
        copy.start()
    own_rows = middle_ref.shape[0] // team
    grad_two = parts[0][...].astype(f32)
    for part in parts[1:]:
        grad_two = grad_two + part[...].astype(f32)
    unit, inverse = normalise(middle_ref[...])
    grad_gain = grad_two * unit
    rows = lax.broadcasted_iota(jnp.int32, grad_gain.shape, 0)
    first = place[0] * own_rows
    mine = (rows >= first) & (rows < first + own_rows)
    gain_grad_ref[...] = jnp.sum(jnp.where(mine, grad_gain, 0.0), axis=0, keepdims=True)
    grad = cot_ref[...].astype(f32) + normalise_back(unit, inverse, grad_two * gain_ref[...])
    low[...] = grad.astype(bf16)
    for k in range(team):

        @pl.when(place[0] == k)
        def own():
            middle_grad_ref[...] = grad[k * own_rows : (k + 1) * own_rows, :]

    weight_copies(near, far, weights, place, sems, lambda copy: copy.wait())
    for copy in late_copies:
        copy.wait()
    grad_out[...] = dot(low[...], of_heads(weights, 3)).astype(bf16)
    for h in range(col_parts):
        q, k, v = (kept_ref[i, :, head(h)] for i in range(3))
        grad_heads = grad_out[:, head(h)]
        grad_v[:, head(h)] = dot(probs_t_ref[h], grad_heads).astype(bf16)
        probs = probs_ref[h].astype(f32)
        grad_probs = dot_t(grad_heads, v)
        inner = jnp.sum(grad_probs * probs, axis=-1, keepdims=True)
        grad_scores = (probs * (grad_probs - inner)).astype(bf16)
        grad_q[:, head(h)] = (dot(grad_scores, k) * score_scale).astype(bf16)
        turned = dot_t(v, grad_heads) - inner.T
        turned = (probs_t_ref[h].astype(f32) * turned).astype(bf16)
        grad_k[:, head(h)] = (dot(turned, q) * score_scale).astype(bf16)
    total = dot_t(grad_k[...], of_heads(weights, 1)) + dot_t(grad_v[...], of_heads(weights, 2))
    total_low[...] = total.astype(bf16)
    width = context_grads[0].shape[1]
    for k in range(team):
        lanes = pl.ds(pl.multiple_of((place[0] ^ k) * width, LANES), width)
        context_grads[k][...] = total_low[:, lanes]
    one_ref[...] = dot_t(grad_q[...], of_heads(weights, 0)).astype(bf16)


def head_grads_kernel(col_parts, row_parts, place, low, attended_ref, *refs):
    normed_t_ref, context_t_ref, grad_q, grad_k, grad_v = refs[:5]
    stacks, (grads, out_sems) = refs[5:9], refs[9:]
    half = col_parts // 2
    shape = (*grads.shape[1:3], HD)

    def put(i, grad):
        for h in range(col_parts):
            grads[h, :, :, head(i)] = grad[:, head(h)].astype(bf16).reshape(shape)

    put(0, dot(normed_t_ref[...], grad_q[...]))
    put(1, dot(context_t_ref[...], grad_k[...]))
    put(2, dot(context_t_ref[...], grad_v[...]))
    put(3, dot(low[...].T, attended_ref[...]))
    copies = []
    for k in range(col_parts):
        for r, piece in enumerate(gradient_pieces(stacks, row_parts, k // half, k % half)):
            copies.append(pltpu.make_async_copy(grads.at[k, place[2] ^ r], piece, out_sems.at[k, r]))
    for copy in copies:
        copy.start()
    for copy in copies:
        copy.wait()


def adjoint_kernel(team, logr_ref, *refs):
    parts = refs[:team]
    g_tiles, ends_ref, total_ref, rows = refs[team:]
    grad = parts[0][...].astype(f32)
    for part in parts[1:]:
        grad = grad + part[...].astype(f32)
    grad = grad.astype(bf16).astype(f32)
    tiles, length, unused = g_tiles.shape
    states = logr_ref.shape[0]
    span = length // SUBS
    for tile in range(tiles):
        rows[...] = grad[:, lane_tile(tile)]
        in_steps(g_tiles, tile, rows)
    before = (sub_index() * span).astype(f32)
    for tile in range(tiles):
        rate = jnp.exp(logr_ref[:, lane_tile(tile)])
        decay = jnp.exp(-rate)
        for first in range(0, states, GROUP):
            chosen = range(first, first + GROUP)
            decays = [spread(decay[n : n + 1]) for n in chosen]

            def step(i, held):
                g = g_tiles[tile, step_rows(span - 1 - i), :]
                later = []
                for d, (b, w) in zip(decays, held):
                    shrunk = d * b
                    later.append((g + shrunk, d * w + shrunk))
                return tuple(later)

            zero = no_state(g_tiles)
            held = lax.fori_loop(0, span, step, ((zero, zero),) * GROUP, unroll=4)
            for n, (b, w) in zip(chosen, held):
                ends_ref[0, n, :, lane_tile(tile)] = b
                ends_ref[1, n, :, lane_tile(tile)] = w
                shrink = jnp.exp(-before * rate[n : n + 1])
                total_ref[0, n : n + 1, lane_tile(tile)] = jnp.sum(
                    shrink * b, axis=0, keepdims=True
                )
                total_ref[1, n : n + 1, lane_tile(tile)] = jnp.sum(
                    shrink * (w + before * b), axis=0, keepdims=True
                )


def context_back_kernel(
    team, place, g_tiles, u_tiles, ends_ref, all_ref, logr_ref, coef_ref, one_ref, *refs
):
    pieces = refs[:team]
    grad_ssm_ref, y_tiles, full, rows = refs[team:]
    tiles, length, unused = u_tiles.shape
    states = logr_ref.shape[0]
    span = length // SUBS
    width = tiles * LANES
    index = sub_index()
    after = ((SUBS - 1 - index) * span).astype(f32)
    full[...] = one_ref[...].astype(f32)
    group = GROUP
    for tile in range(tiles):
        lanes = lane_tile(tile)
        rate = jnp.exp(logr_ref[:, lanes])
        decay = jnp.exp(-rate)
        root = jnp.sqrt(2.0 * rate)
        scale = coef_ref[:, lanes] * root
        in_b = jnp.zeros((states, LANES), f32)
        in_w = jnp.zeros((states, LANES), f32)
        for j in range(all_ref.shape[0]):
            gap = j - place[1] - 1
            distance = (jnp.maximum(gap, 0) * length).astype(f32)
            shrink = jnp.exp(-distance * rate)
            b, w = all_ref[j, 0, :, lanes].astype(f32), all_ref[j, 1, :, lanes].astype(f32)
            in_b = in_b + jnp.where(gap >= 0, shrink * b, 0.0)
            in_w = in_w + jnp.where(gap >= 0, shrink * (w + distance * b), 0.0)
        for first in range(0, states, group):
            chosen = range(first, first + group)
            starts = []
            for n in chosen:
                row = rate[n : n + 1]
                b, w = ends_ref[0, n, :, lanes], ends_ref[1, n, :, lanes]
                for d in (1, 2, 4):
                    shrink = jnp.exp(-(d * span) * row)
                    next_b = pltpu.roll(b, SUBS - d, 0)
                    next_w = pltpu.roll(w, SUBS - d, 0)
                    inside = index < SUBS - d
                    b, w = (
                        b + jnp.where(inside, shrink * next_b, 0.0),
                        w + jnp.where(inside, shrink * (next_w + (d * span) * next_b), 0.0),
                    )
                inside = index < SUBS - 1
                b = jnp.where(inside, pltpu.roll(b, SUBS - 1, 0), 0.0)
                w = jnp.where(inside, pltpu.roll(w, SUBS - 1, 0), 0.0)
                shrink = jnp.exp(-after * row)
                b_row, w_row = in_b[n : n + 1], in_w[n : n + 1]
                b = b + shrink * b_row
                w = w + shrink * (w_row + after * b_row)
                zero = no_state(u_tiles)
                starts.append((b, w, zero, zero))
            decays = [spread(decay[n : n + 1]) for n in chosen]
            scales = [spread(scale[n : n + 1]) for n in chosen]

            def step(i, held):
                at = step_rows(span - 1 - i)
                g = g_tiles[tile, at, :]
                u = u_tiles[tile, at, :]
                later, parts = [], []
                for d, s, (b, w, sum_b, sum_w) in zip(decays, scales, held):
                    shrunk = d * b
                    w = d * w + shrunk
                    b = g + shrunk
                    later.append((b, w, sum_b + u * b, sum_w + u * w))
                    parts.append(s * b)
                while len(parts) > 1:
                    parts = [p + q for p, q in zip(parts[::2], parts[1::2])]
                if first > 0:
                    parts[0] = parts[0] + y_tiles[tile, at, :]
                y_tiles[tile, at, :] = parts[0]
                return tuple(later)

            held = lax.fori_loop(0, span, step, tuple(starts), unroll=2)
            for n, (unused_b, unused_w, sum_b, sum_w) in zip(chosen, held):
                sum_b = jnp.sum(sum_b, axis=0, keepdims=True)
                sum_w = jnp.sum(sum_w, axis=0, keepdims=True)
                row = slice(n, n + 1)
                grad_ssm_ref[0, row, lanes] = root[row] * sum_b
                grad_ssm_ref[1, row, lanes] = scale[row] * (0.5 * sum_b - rate[row] * sum_w)
        at_lanes = pl.ds(pl.multiple_of(place[0] * width + tile * LANES, LANES), LANES)
        from_steps(rows, y_tiles, tile)
        full[:, at_lanes] += rows[...].astype(bf16).astype(f32)
    count = pieces[0].shape[0]
    for k in range(team):
        at_rows = pl.ds(pl.multiple_of((place[0] ^ k) * count, count), count)
        pieces[k][...] = full[at_rows, :].astype(bf16)


def input_grad_kernel(team, place, x_ref, gain_ref, middle_grad_ref, *refs):
    parts, (out_ref, gain_grad_ref) = refs[:team], refs[team:]
    rows = out_ref.shape[0]
    at_rows = pl.ds(pl.multiple_of(place[0] * rows, rows), rows)
    grad_one = parts[0][...].astype(f32)
    for part in parts[1:]:
        grad_one = grad_one + part[...].astype(f32)
    unit, inverse = normalise(x_ref[at_rows, :].astype(f32))
    gain_grad_ref[...] = jnp.sum(grad_one * unit, axis=0, keepdims=True)
    back = normalise_back(unit, inverse, grad_one * gain_ref[...])
    out_ref[...] = (middle_grad_ref[...] + back).astype(bf16)


def assemble_kernel(halves, low_count, place, own_ref, *refs):
    others, out_ref = refs[:-1], refs[-1]
    count, rows, unused = own_ref.shape
    half = place[4]

    def put(value, sequence, which, member):
        at_rows = pl.ds(pl.multiple_of((which * low_count + member) * rows, rows), rows)
        out_ref[sequence, at_rows, :] = value.astype(out_ref.dtype)

    for sequence in range(count // (halves * low_count)):
        if halves == 1:
            for member in range(low_count):
                put(own_ref[sequence * low_count + member], sequence, 0, member)
        else:
            put(own_ref[sequence * halves + half], sequence, half, 0)
            put(others[0][sequence], sequence, 1 - half, 0)


def pack_kernel(halves, place, qkv_ref, out_ref, up_ref, down_ref, *refs):
    rows = up_ref.shape[0]
    heads, hidden = out_ref.shape[0] // halves, up_ref.shape[1] // halves
    for which in range(halves):
        side = place[4] if which == 0 else 1 - place[4]
        at_heads = pl.ds(pl.multiple_of(side * heads, LANES), heads)
        at_hidden = pl.ds(pl.multiple_of(side * hidden, LANES), hidden)
        if which == 0:
            head_ref = refs[0]
            wide_ref, deep_ref = refs[1].at[:, :hidden], refs[1].at[:, hidden:]
        else:
            packed = refs[2]
            head_ref = packed.at[:, : 4 * heads]
            wide_ref = packed.at[:, 4 * heads : 4 * heads + hidden]
            deep_ref = packed.at[:, 4 * heads + hidden :]
        for i in range(3):
            head_ref[:, i * heads : (i + 1) * heads] = qkv_ref[i, :, at_heads].astype(bf16)
        head_ref[:, 3 * heads :] = out_ref[at_heads, :].T.astype(bf16)
        wide_ref[...] = up_ref[:, at_hidden].astype(bf16)
        deep_ref[...] = down_ref[at_hidden, :].T.astype(bf16)


def small_kernel(ssm_ref, gains_ref, out_ref):
    count = ssm_ref.shape[0]
    out_ref[:count, :] = ssm_ref[...]
    out_ref[count:, :] = gains_ref[...]


def lamb_moments(weight, grad_item, first_old, second_old):
    first_new = beta_first * first_old + (1.0 - beta_first) * grad_item
    second_new = beta_second * second_old + (1.0 - beta_second) * grad_item * grad_item
    direction = (
        first_new
        / (1.0 - beta_first**STEP)
        / (jnp.sqrt(second_new / (1.0 - beta_second**STEP)) + lamb_eps)
        + weight_decay * weight
    )
    return (first_new, second_new, direction)


def place_sums(sums_ref, sums):
    rows = lax.broadcasted_iota(jnp.int32, sums_ref.shape, 0)
    lanes = lax.broadcasted_iota(jnp.int32, sums_ref.shape, 1)
    found = jnp.zeros(sums_ref.shape, f32)
    for index, pair in sums.items():
        for row, value in enumerate(pair):
            found = jnp.where((rows == row) & (lanes == index), value, found)
    sums_ref[...] = found


def moments_kernel(halves, matrices, place, *refs):
    count = 1 + max(item[1] for item in matrices)
    grads, refs = [refs[halves * i : halves * (i + 1)] for i in range(count)], refs[halves * count :]
    arrays = len({(item[1], item[4] is None) for item in matrices})
    ins = [refs[3 * i : 3 * i + 3] for i in range(arrays)]
    outs = [refs[3 * (arrays + i) : 3 * (arrays + i) + 3] for i in range(arrays)]
    sums_ref = refs[6 * arrays]
    keys = []
    sums = {}
    for number, source, column, turned, stacked in matrices:
        key = (source, stacked is None)
        if key not in keys:
            keys.append(key)
        pick = (lambda ref: ref) if stacked is None else (lambda ref, i=stacked: ref.at[i])
        weight, first, second = (pick(ref) for ref in ins[keys.index(key)])
        news = [pick(ref) for ref in outs[keys.index(key)]]
        width = weight.shape[0 if turned else 1] // halves
        rows = weight.shape[1 if turned else 0]
        cols = slice(column * width, (column + 1) * width)
        total_weight = total_update = 0.0
        for which, grad_ref in enumerate(grads[source]):
            side = place[4] if which == 0 else 1 - place[4]
            at = pl.ds(pl.multiple_of(side * width, width), width)
            if which == 0:
                grad = grad_ref[pl.ds(pl.multiple_of(side * rows, rows), rows), cols].astype(f32)
            else:
                grad = grad_ref[:, cols].astype(f32)
            at = (at, slice(None)) if turned else (slice(None), at)
            grad = grad.T if turned else grad
            old = weight[at]
            found = lamb_moments(old, grad, first[at], second[at])
            for ref, value in zip(news, found):
                ref[at] = value
            total_weight = total_weight + jnp.sum(old * old)
            total_update = total_update + jnp.sum(found[2] * found[2])
        sums[number] = (total_weight, total_update)
    place_sums(sums_ref, sums)


def small_moments_kernel(numbers, grads_ref, *refs):
    ins, outs, sums_ref = (refs[:3], refs[3:6]), (refs[6:9], refs[9:12]), refs[12]
    states = (grads_ref.shape[0] - 2) // 2
    sums = {}
    for (weight, first, second), news, start, rows, first_number in (
        (ins[0], outs[0], 2 * states, 1, numbers[0]),
        (ins[1], outs[1], 0, states, numbers[1]),
    ):
        for i in range(2):
            grad = grads_ref[start + i * rows : start + (i + 1) * rows, :]
            at = slice(i * rows, (i + 1) * rows)
            found = lamb_moments(weight[at, :], grad, first[at, :], second[at, :])
            for ref, value in zip(news, found):
                ref[at, :] = value
            sums[first_number + i] = (
                jnp.sum(weight[at, :] * weight[at, :]),
                jnp.sum(found[2] * found[2]),
            )
    place_sums(sums_ref, sums)


def update_kernel(stacks, sums_ref, *refs):
    count = len(stacks)
    weights, directions, news = refs[:count], refs[count : 2 * count], refs[2 * count : 3 * count]
    norms = jnp.sqrt(jnp.sum(sums_ref[...], axis=0))
    refs[3 * count][...] = norms
    ratios = norms[0:1] / norms[1:2]
    lanes = lax.broadcasted_iota(jnp.int32, ratios.shape, 1)
    for numbers, weight, direction, new in zip(stacks, weights, directions, news):
        step = weight.shape[0] // len(numbers)
        for i, number in enumerate(numbers):
            ratio = jnp.sum(jnp.where(lanes == number, ratios, 0.0), axis=1, keepdims=True)
            at = slice(i * step, (i + 1) * step)
            scale = learn_rate * ratio.reshape((1,) * weight.ndim)
            new[at] = weight[at] - scale * direction[at]


def call(
    body, ins, outs, scratch=(), grid=None, in_specs=None, out_specs=None, time=1.0, after=(), token=False
):
    moved = sum(a.size * a.dtype.itemsize for a in list(ins) + list(outs))
    params = pltpu.CompilerParams(vmem_limit_bytes=VMEM_BYTES)
    cost = pl.CostEstimate(flops=int(time * 1.15e9), bytes_accessed=moved, transcendentals=0)
    whole = pl.BlockSpec(memory_space=pltpu.VMEM)
    anywhere = pl.BlockSpec(memory_space=pl.ANY)
    in_specs = list(in_specs or [whole] * len(ins)) + [anywhere] * len(after)
    out_specs = list(out_specs or [whole] * len(outs))
    outs = list(outs)
    first_out = len(ins) + len(after)
    last_out = first_out + len(outs)
    if token:
        outs.append(jax.ShapeDtypeStruct((SUBS, LANES), f32))
        out_specs.append(whole)

    def run(*refs):
        refs = list(refs)
        if token:
            refs[last_out][...] = jnp.zeros((SUBS, LANES), f32)
            del refs[last_out]
        body(*refs[: len(ins)], *refs[first_out:])

    return pl.pallas_call(
        run,
        out_shape=tuple(outs),
        in_specs=in_specs,
        out_specs=tuple(out_specs),
        scratch_shapes=list(scratch),
        compiler_params=params,
        cost_estimate=cost,
        **({} if grid is None else {"grid": grid}),
    )(*ins, *after)


def shaped(shape, kind):
    return jax.ShapeDtypeStruct(tuple(shape), kind)


def on_device(
    tokens,
    cotangent,
    w_qkv,
    w_out,
    w_up,
    w_down,
    norm_gains,
    ssm_param,
    first_qkv,
    second_qkv,
    first_out,
    second_out,
    first_up,
    second_up,
    first_down,
    second_down,
    first_gain,
    second_gain,
    first_ssm,
    second_ssm,
):
    halves = lax.axis_size("sl")
    low_count = lax.axis_size("ml")
    row_parts = lax.axis_size("sh")
    col_parts = lax.axis_size("mb") * lax.axis_size("mq")
    team = halves * low_count
    sl, ml, mb, mq = (lax.axis_index(name) for name in ("sl", "ml", "mb", "mq"))
    rank = sl * low_count + ml
    block_index = lax.axis_index("sh") * halves + mq
    seq_total, length, width = tokens.shape
    assert length == BLK and seq_total == lax.axis_size("mb")
    states = ssm_param.shape[1]
    channels = width // team
    tiles = channels // LANES
    row_count = width // row_parts
    own_rows = length // team
    place = [rank, block_index, lax.axis_index("sh"), lax.axis_index(MODEL), sl, sl ^ mq]
    place.append(lax.axis_index(COLS))
    place = jnp.stack(place).astype(jnp.int32)
    smem = pl.BlockSpec(memory_space=pltpu.SMEM)
    vmem = pl.BlockSpec(memory_space=pltpu.VMEM)

    def permute(value, axes, moves):
        return lax.ppermute(value, axes, moves)

    def swap(value):
        return permute(value, "sl", [(0, 1), (1, 0)])

    def in_order(own, other, axis):
        return jnp.where(
            sl == 0, jnp.concatenate([own, other], axis), jnp.concatenate([other, own], axis)
        )

    def team_send(pieces):
        moved = [pieces[0]]
        for k in range(1, team):
            moved.append(permute(pieces[k], TEAM, [(i, i ^ k) for i in range(team)]))
        return moved

    def pick_block(array):
        own = lax.dynamic_index_in_dim(array, mb, 0, keepdims=False)
        if halves == 1:
            return own, ()
        other = swap(own)
        return jnp.where(sl == mq, own, other), (other,)

    def across(value, bit):
        return permute(value, "sh", [(i, i ^ bit) for i in range(row_parts)])

    def along(value, axes, step):
        count = lax.axis_size(axes)
        return permute(value, axes, [(i, (i + step) % count) for i in range(count)])

    bits = [1 << i for i in range(row_parts.bit_length() - 1)]

    def bit_order(k):
        return bits if k % 2 == 0 else bits[::-1]

    def double_rows(value, order):
        found = {0: value}
        for bit in order:
            for r in list(found):
                found[r | bit] = across(found[r], bit)
        return [found[r] for r in range(row_parts)]

    def add(*items, zero=None):
        total = sum(item.astype(f32) for item in items)
        return (total if zero is None else total + zero[0, 0]).astype(bf16)

    def first_messages(stacks):
        return across(stacks[1], bits[-1]), across(stacks[3], bits[0])

    def second_messages(stacks, first, zero):
        count = first[0].shape[0] // 2
        return [add(stacks[2 * i][count:], first[i][count:], zero=zero) for i in range(2)]

    def halve_rows(keep, arrived, order, send, last):
        items = [keep, arrived]
        for bit in order[-2::-1]:
            count = arrived.shape[0] // 2
            if send is None:
                send = add(*[item[count:] for item in items])
            arrived = across(send, bit)
            items = [item[:count] for item in items] + [arrived]
            send = None
        return add(*[item[0] for item in items], zero=last)

    def halve_both(stacks, first, send, last=None):
        near = halve_rows(stacks[0], first[0], bits, send[0], last)
        return near, halve_rows(stacks[2], first[1], bits[::-1], send[1], last)

    def hold(arrays, after):
        anywhere = pl.BlockSpec(memory_space=pl.ANY)
        return pl.pallas_call(
            lambda *refs: None,
            out_shape=tuple(shaped(item.shape, item.dtype) for item in arrays),
            in_specs=[anywhere] * (len(arrays) + len(after)),
            out_specs=(anywhere,) * len(arrays),
            input_output_aliases={i: i for i in range(len(arrays))},
        )(*arrays, *after)

    def gather_pieces(shard):
        pieces = []
        for k in range(col_parts):
            held = along(held, COLS, 1) if k > 0 else shard
            pieces.append(double_rows(held, bits if k % 2 == 0 else bits[::-1]))
        return pieces

    def sum_over_z(near, far, ring=True):
        if not ring:
            pieces = [stack[k] for stack in (near, far) for k in range(col_parts // 2)]
            moved = [along(piece, COLS, -k) for k, piece in enumerate(pieces) if k > 0]
            return add(pieces[0], *moved)
        held = None
        for stack in (far, near):
            for k in reversed(range(stack.shape[0])):
                held = stack[k] if held is None else add(stack[k], along(held, COLS, -1))
        return held

    def everywhere(value, axes):
        count = lax.axis_size(axes)
        copies = jnp.broadcast_to(value[None], (count, *value.shape))
        return lax.all_to_all(copies, axes, 0, 0, tiled=True)

    rows_dev = w_up.shape[0]
    hidden_cols = w_up.shape[1] // halves
    head_cols = 4 * w_out.shape[0] // halves
    packed_cols = head_cols + 2 * hidden_cols
    sides = [shaped((rows_dev, cols), bf16) for cols in (head_cols, 2 * hidden_cols)]
    shards = call(
        functools.partial(pack_kernel, halves),
        (place, w_qkv, w_out, w_up, w_down),
        sides + [shaped((rows_dev, packed_cols), bf16)] * (halves - 1),
        time=2.4,
        in_specs=[smem] + [vmem] * 4,
    )
    if halves == 2:
        other = swap(shards[2])
        cuts = (0, head_cols, packed_cols)
        shards = [
            in_order(own, other[:, first:last], 0)
            for own, first, last in zip(shards, cuts, cuts[1:])
        ]
    head_shard, hidden_shard = shards[:2]
    attn_full = lax.all_gather(head_shard, COLS, axis=0, tiled=False)
    hidden_w = gather_pieces(hidden_shard)
    hidden_flat = [piece for group in hidden_w for piece in group]

    small, = call(
        small_kernel,
        (ssm_param.reshape(2 * states, -1), norm_gains),
        (shaped((2 * states + 2, norm_gains.shape[1]), f32),),
        after=hidden_w[0][1:-1],
    )
    small = jnp.transpose(everywhere(small, ALL), (1, 0, 2)).reshape(2 * states + 2, width)
    own_ssm = lax.dynamic_slice_in_dim(
        small[: 2 * states].reshape(2, states, width), rank * channels, channels, 2
    )
    coef, logr = own_ssm[0], own_ssm[1]
    gain_one = small[2 * states : 2 * states + 1]
    gain_two = small[2 * states + 1 : 2 * states + 2]

    x, unused = pick_block(tokens)
    cot, cot_other = pick_block(cotangent)

    anywhere = [pl.BlockSpec(memory_space=pl.ANY)]

    def fixed(*shape):
        return pl.BlockSpec(shape, lambda z: (0,) * len(shape))

    wide = fixed(length, width)
    row = fixed(1, width)

    normed_one, normed_t, u_steps, ends, total = call(
        norm_kernel,
        (place, x, gain_one, logr),
        (
            shaped((length, width), bf16),
            shaped((width, length), bf16),
            shaped((tiles, length, LANES), f32),
            shaped((states, SUBS, channels), f32),
            shaped((states, channels), f32),
        ),
        scratch=[pltpu.VMEM((length, LANES), f32)],
        in_specs=[smem, vmem, vmem, vmem],
        after=(hidden_w[1][0], *cot_other),
        time=5,
    )
    (attn_full,) = hold((attn_full,), (total,))
    attn_w = [
        *double_rows(attn_full[: col_parts // 2], bits),
        *double_rows(attn_full[col_parts // 2 :], bits[::-1]),
    ]
    totals = everywhere(total.astype(bf16), ("sh", "mq"))
    (context_own,) = call(
        context_kernel,
        (place, u_steps, ends, totals, logr, coef),
        (shaped((length, channels), bf16),),
        after=(hidden_w[0][-1], *hidden_w[1][1:-1], hidden_w[-1][0], *attn_w[1 : row_parts - 1]),
        scratch=[pltpu.VMEM((tiles, length, LANES), f32), pltpu.VMEM((length, LANES), f32)],
        in_specs=[smem] + [vmem] * 5,
        time=7,
    )
    contexts = team_send([context_own] * team)

    stack_shape = (row_parts // 2, col_parts // 2, row_count)
    head_stacks = [shaped((*stack_shape, head_cols), bf16)] * 4
    hidden_stacks = [shaped((*stack_shape, hidden_cols), bf16)] * 8
    sizes = (team, col_parts, row_parts)
    head_buffer = pltpu.VMEM((col_parts, row_parts, row_count, 4 * HD), bf16)
    head_sems = pltpu.SemaphoreType.DMA((col_parts, row_parts))
    kept_shape = shaped((3, length, col_parts * HD), bf16)
    flat_shape = shaped((length, col_parts * HD), bf16)
    context_t, cot_t, kept = call(
        functools.partial(project_kernel, *sizes),
        (place, normed_one, cot, *contexts, *attn_w),
        (shaped((width, length), bf16), shaped((width, length), bf16), kept_shape),
        scratch=[pltpu.VMEM((length, width), bf16), head_buffer, head_sems],
        time=1,
        in_specs=[smem] + [vmem] * (2 + team) + anywhere * len(attn_w),
        after=(hidden_w[1][-1], *[piece for group in hidden_w[2:3] for piece in group[1:]]),
    )
    attn_part, attended, probs, probs_t = call(
        functools.partial(attend_kernel, *sizes),
        (place, kept, *attn_w),
        (
            shaped((length, width), bf16),
            flat_shape,
            *[shaped((col_parts, length, length), bf16)] * 2,
        ),
        scratch=[head_buffer, head_sems],
        time=1,
        in_specs=[smem, vmem] + anywhere * len(attn_w),
        after=[piece for group in hidden_w[3:] for piece in group[1:-1]],
    )
    attn_parts = team_send([attn_part] * team)

    middle, normed_two, normed_two_t = call(
        functools.partial(middle_kernel, team),
        (x, gain_two, *attn_parts),
        (shaped((length, width), f32), shaped((length, width), bf16), shaped((width, length), bf16)),
        time=1,
    )
    weight_buffer = pltpu.VMEM((row_parts, row_count, col_parts * hidden_cols), bf16)
    grad_buffer = pltpu.VMEM((col_parts, row_parts, row_count, hidden_cols), bf16)
    fed = call(
        functools.partial(feed_kernel, team, col_parts, row_parts),
        (place, normed_two, normed_two_t, cot, cot_t, *hidden_flat),
        (
            *[shaped((own_rows, width), bf16)] * team,
            shaped((length, width), bf16),
            *hidden_stacks,
        ),
        scratch=[
            *[weight_buffer] * 2,
            *[grad_buffer] * 2,
            *[pltpu.VMEM((length, col_parts * hidden_cols), bf16)] * 2,
            pltpu.SemaphoreType.DMA((4, col_parts, row_parts)),
        ],
        time=18,
        grid=(col_parts,),
        in_specs=[smem, wide, fixed(width, length), wide, fixed(width, length)]
        + anywhere * len(hidden_flat),
        out_specs=[fixed(own_rows, width)] * team + [wide] + anywhere * 8,
    )
    out_pieces, two_part, hidden_grads = fed[:team], fed[team], fed[team + 1 :]
    two_parts = team_send([two_part] * team)

    def rows_of(array, member):
        return lax.dynamic_slice_in_dim(array, member * own_rows, own_rows, 0)

    def share_rows(pieces, kind):
        others = []
        if halves == 2:
            pairs = pieces.reshape(seq_total, halves, own_rows, width)
            others = [swap(lax.dynamic_index_in_dim(pairs, 1 - sl, 1, keepdims=False))]
        (blocks,) = call(
            functools.partial(assemble_kernel, halves, low_count),
            (place, pieces, *others),
            (shaped((seq_total, length, width), kind),),
            time=3.5,
            in_specs=[smem, vmem] + [vmem] * len(others),
        )
        return blocks

    out_pieces = team_send(list(out_pieces))
    result = rows_of(middle, rank) + sum(item.astype(f32) for item in out_pieces)
    result = result.astype(bf16)
    layer_pieces = lax.all_gather(result, MODEL, axis=0, tiled=False)
    layer_out = share_rows(layer_pieces, bf16)

    def both_halves(own):
        if halves == 1:
            return [own]
        return [own, swap(lax.dynamic_slice_in_dim(own, (1 - sl) * rows_dev, rows_dev, 0))]

    middle_grad, gain_two_grad, one_part, low_grad, *rest = call(
        functools.partial(attend_back_kernel, *sizes),
        (place, middle, gain_two, cot, *two_parts, kept, probs, probs_t, *attn_w),
        (
            shaped((own_rows, width), f32),
            shaped((1, width), f32),
            shaped((length, width), bf16),
            shaped((length, width), bf16),
            *[flat_shape] * 3,
            *[shaped((length, channels), bf16)] * team,
        ),
        scratch=[
            head_buffer,
            pltpu.VMEM(flat_shape.shape, bf16),
            pltpu.VMEM((length, width), bf16),
            pltpu.VMEM(kept_shape.shape, bf16),
            *[pltpu.VMEM((col_parts, length, length), bf16)] * 2,
            head_sems,
            pltpu.SemaphoreType.DMA((3,)),
        ],
        time=1,
        in_specs=[smem] + [vmem] * (3 + team) + anywhere * (3 + len(attn_w)),
        after=(result,),
    )
    head_grads, context_grads = rest[:3], rest[3:]
    context_grads = team_send(context_grads)
    *head_stacks, heads_done = call(
        functools.partial(head_grads_kernel, col_parts, row_parts),
        (place, low_grad, attended, normed_t, context_t, *head_grads),
        head_stacks,
        scratch=[head_buffer, head_sems],
        time=8,
        in_specs=[smem] + [vmem] * 7,
        out_specs=anywhere * 4,
        token=True,
    )
    down_first = first_messages(hidden_grads[4:])
    g_steps, adjoint_ends, adjoint_total, adjoint_done = call(
        functools.partial(adjoint_kernel, team),
        (logr, *context_grads),
        (
            shaped((tiles, length, LANES), f32),
            shaped((2, states, SUBS, channels), f32),
            shaped((2, states, channels), f32),
        ),
        scratch=[pltpu.VMEM((length, LANES), f32)],
        time=1,
        after=(heads_done,),
        token=True,
    )
    up_first = first_messages(hidden_grads[:4])
    (own_total,) = hold((adjoint_total.astype(bf16),), (*down_first, *up_first))
    adjoint_totals = everywhere(own_total, ("sh", "mq"))
    second = second_messages(hidden_grads[4:], down_first, adjoint_done)
    second += second_messages(hidden_grads[:4], up_first, adjoint_done)
    second = hold(second, (adjoint_totals,))
    *one_pieces, grad_ssm, context_done = call(
        functools.partial(context_back_kernel, team),
        (place, g_steps, u_steps, adjoint_ends, adjoint_totals, logr, coef, one_part),
        (
            *[shaped((own_rows, width), bf16)] * team,
            shaped((2, states, channels), f32),
        ),
        scratch=[
            pltpu.VMEM((tiles, length, LANES), f32),
            pltpu.VMEM((length, width), f32),
            pltpu.VMEM((length, LANES), f32),
        ],
        in_specs=[smem] + [vmem] * 7,
        time=1,
        after=(*second, layer_pieces),
        token=True,
    )
    one_pieces = team_send(one_pieces)
    down_sums = halve_both(hidden_grads[4:], down_first, second[:2], context_done)
    up_sums = halve_both(hidden_grads[:4], up_first, second[2:], context_done)
    grad_rows, gain_one_grad, rows_done = call(
        functools.partial(input_grad_kernel, team),
        (place, x, gain_one, middle_grad, *one_pieces),
        (shaped((own_rows, width), bf16), shaped((1, width), f32)),
        in_specs=[smem] + [vmem] * (3 + team),
        time=1,
        after=(layer_pieces, *down_sums, *up_sums),
        token=True,
    )
    head_stacks[1::2] = hold(head_stacks[1::2], (grad_rows,))
    down_sums = hold(down_sums, head_stacks[1::2])
    up_sums = hold(up_sums, head_stacks[1::2])
    grad_down = sum_over_z(*down_sums)
    head_first = first_messages(head_stacks)
    head_second = second_messages(head_stacks, head_first, rows_done)
    head_sums = halve_both(head_stacks, head_first, head_second)
    grad_up = sum_over_z(*up_sums)
    grad_heads = sum_over_z(*head_sums)
    input_grad = share_rows(lax.all_gather(grad_rows, MODEL, axis=0, tiled=False), f32)

    placed_ssm = lax.dynamic_update_slice_in_dim(
        jnp.zeros((2 * states, width), f32),
        grad_ssm.reshape(2 * states, channels),
        rank * channels,
        1,
    )
    small_grads = jnp.concatenate([placed_ssm, gain_one_grad, gain_two_grad], 0)
    (small_grads,) = hold((small_grads,), head_sums)
    small_grads = small_grads.reshape(2 * states + 2, lax.axis_size(ALL), -1)
    small_grads = lax.all_to_all(jnp.transpose(small_grads, (1, 0, 2)), ALL, 0, 0, tiled=True)
    small_grads = jnp.sum(small_grads, axis=0)

    def moments(matrices, grads, arrays, after=()):
        changed = [shaped(old.shape, f32) for group in arrays for old in group]
        grad_parts = [part for grad in grads for part in both_halves(grad)]
        ins = [item for group in arrays for item in group]
        *found, sums = call(
            functools.partial(moments_kernel, halves, matrices),
            (place, *grad_parts, *ins),
            (*changed, shaped((2, LANES), f32)),
            in_specs=[smem] + [vmem] * (len(grad_parts) + len(ins)),
            after=after,
            time=4,
        )
        return [found[3 * i : 3 * i + 3] for i in range(len(arrays))], sums

    hidden_new, hidden_sums = moments(
        ((4, 0, 0, False, None), (5, 1, 0, True, None)),
        (grad_up, grad_down),
        ((w_up, first_up, second_up), (w_down, first_down, second_down)),
    )
    heads_new, head_sums = moments(
        tuple((i, 0, i, False, i) for i in range(3)) + ((3, 0, 3, True, None),),
        (grad_heads,),
        ((w_qkv, first_qkv, second_qkv), (w_out, first_out, second_out)),
        (layer_out, input_grad),
    )
    own_channels = norm_gains.shape[1]
    ssm_items = [item.reshape(2 * states, own_channels) for item in (ssm_param, first_ssm, second_ssm)]
    small_items = [norm_gains, first_gain, second_gain, *ssm_items]
    *small_new, small_sums = call(
        functools.partial(small_moments_kernel, (6, 8)),
        (small_grads.reshape(2 * states + 2, own_channels), *small_items),
        (*[shaped(item.shape, f32) for item in small_items], shaped((2, LANES), f32)),
    )
    all_sums = everywhere(hidden_sums + head_sums + small_sums, ALL)
    masters = (w_qkv, w_out, w_up, w_down, norm_gains, ssm_items[0])
    news = (*heads_new, *hidden_new, small_new[:3], small_new[3:])
    *weights, norms = call(
        functools.partial(update_kernel, ((0, 1, 2), (3,), (4,), (5,), (6, 7), (8, 9))),
        (all_sums, *masters, *[group[2] for group in news]),
        (*[shaped(item.shape, f32) for item in masters], shaped((2, LANES), f32)),
        time=3.2,
    )
    outputs = [layer_out, input_grad]
    for index, (weight, (first_new, second_new, unused)) in enumerate(zip(weights, news)):
        if index == 4:
            outputs += [weight, first_new, second_new[0], second_new[1]]
        else:
            kept_shape = ssm_param.shape if index == 5 else weight.shape
            outputs += [item.reshape(kept_shape) for item in (weight, first_new, second_new)]
    outputs.append(norms[:, :10])
    return tuple(outputs)


def solution(mesh):
    seq_count, model_count = mesh.shape["seq"], mesh.shape["mp"]
    halves = 2 if HEADS // model_count >= 2 else 1
    sizes = (seq_count // halves, halves, SEQS, halves, model_count // (SEQS * halves))
    fine = Mesh(mesh.devices.reshape(sizes), ALL)
    seq, model = ("sh", "sl"), ("mb", "mq", "ml")
    rows_cols, cols_rows = P(seq, model), P(model, seq)
    token = P(None, seq, None)
    stack = P(None, seq, model)
    gains = P(None, ALL)
    ssm = P(None, None, ALL)
    return jax.shard_map(
        on_device,
        mesh=fine,
        in_specs=(token, token, stack, cols_rows, rows_cols, cols_rows, gains, ssm)
        + (stack,) * 2
        + (cols_rows,) * 2
        + (rows_cols,) * 2
        + (cols_rows,) * 2
        + (gains,) * 2
        + (ssm,) * 2,
        out_specs=(token, token)
        + (stack,) * 3
        + (cols_rows,) * 3
        + (rows_cols,) * 3
        + (cols_rows,) * 3
        + (gains, gains, P(ALL), P(ALL))
        + (ssm,) * 3
        + (P(),),
        check_vma=False,
    )
```

```python
import functools
import math

import jax
import jax.numpy as jnp
from jax import lax
from jax.experimental import pallas as pl
from jax.experimental.pallas import tpu as pltpu
from jax.sharding import Mesh
from jax.sharding import PartitionSpec as P

HD = 128
HEADS = 8
BLK = 512
STEP = 10
SEQS = 2
LANES = 128
SUBS = 8
GROUP = 8

norm_eps = 1e-05
beta_first = 0.9
beta_second = 0.999
lamb_eps = 1e-06
weight_decay = 0.01
learn_rate = 0.5
score_scale = HD ** (-0.5)

f32 = jnp.float32
bf16 = jnp.bfloat16
VMEM_BYTES = 56 * 1024 * 1024

ALL = ("sh", "sl", "mb", "mq", "ml")
MODEL = ("mb", "mq", "ml")
COLS = ("mb", "mq")
TEAM = ("sl", "ml")


def dot(left, right):
    return lax.dot_general(left, right, (((1,), (0,)), ((), ())), preferred_element_type=f32)


def dot_t(left, right):
    return lax.dot_general(left, right, (((1,), (1,)), ((), ())), preferred_element_type=f32)


def normalise(values):
    centred = values - jnp.mean(values, axis=-1, keepdims=True)
    inverse = lax.rsqrt(jnp.mean(centred * centred, axis=-1, keepdims=True) + norm_eps)
    return centred * inverse, inverse


def normalise_back(unit, inverse, grad_unit):
    mean_one = jnp.mean(grad_unit, axis=-1, keepdims=True)
    mean_two = jnp.mean(grad_unit * unit, axis=-1, keepdims=True)
    return inverse * (grad_unit - mean_one - unit * mean_two)


def sub_index():
    return lax.broadcasted_iota(jnp.int32, (SUBS, LANES), 0)


def spread(row):
    return jnp.broadcast_to(row, (SUBS, LANES))


def lane_tile(index):
    return slice(index * LANES, (index + 1) * LANES)


def no_state(tiles):
    rows = tiles[0, :SUBS, :]
    return rows - rows


def in_steps(steps, tile, rows):
    span = rows.shape[0] // SUBS

    def move(i, unused):
        steps[tile, pl.ds(pl.multiple_of(i * SUBS, SUBS), SUBS), :] = rows[
            pl.ds(i, SUBS, stride=span), :
        ]
        return unused

    lax.fori_loop(0, span, move, 0, unroll=8)


def from_steps(rows, steps, tile):
    span = rows.shape[0] // SUBS

    def move(i, unused):
        rows[pl.ds(i, SUBS, stride=span), :] = steps[
            tile, pl.ds(pl.multiple_of(i * SUBS, SUBS), SUBS), :
        ]
        return unused

    lax.fori_loop(0, span, move, 0, unroll=8)


def step_rows(i):
    return pl.ds(pl.multiple_of(i * SUBS, SUBS), SUBS)


def norm_kernel(
    place, x_ref, gain_ref, logr_ref, normed_ref, turned_ref, u_tiles, ends_ref, total_ref, rows
):
    unit, unused = normalise(x_ref[...].astype(f32))
    normed_ref[...] = (unit * gain_ref[...]).astype(bf16)
    turned_ref[...] = normed_ref[...].T
    tiles, length, unused = u_tiles.shape
    states = logr_ref.shape[0]
    span = length // SUBS
    for tile in range(tiles):
        start = place[0] * (tiles * LANES) + tile * LANES
        rows[...] = normed_ref[:, pl.ds(pl.multiple_of(start, LANES), LANES)].astype(f32)
        in_steps(u_tiles, tile, rows)
    left = ((SUBS - 1 - sub_index()) * span).astype(f32)
    for tile in range(tiles):
        rate = jnp.exp(logr_ref[:, lane_tile(tile)])
        decay = jnp.exp(-rate)
        decays = [spread(decay[n : n + 1]) for n in range(states)]

        def step(i, held):
            u = u_tiles[tile, step_rows(i), :]
            return tuple(d * h + u for d, h in zip(decays, held))

        zero = no_state(u_tiles)
        held = lax.fori_loop(0, span, step, (zero,) * states, unroll=4)
        for n in range(states):
            ends_ref[n, :, lane_tile(tile)] = held[n]
            total_ref[n : n + 1, lane_tile(tile)] = jnp.sum(
                held[n] * jnp.exp(-left * rate[n : n + 1]), axis=0, keepdims=True
            )


def context_kernel(
    place, u_tiles, ends_ref, all_ref, logr_ref, coef_ref, context_ref, y_tiles, rows
):
    tiles, length, unused = u_tiles.shape
    states = logr_ref.shape[0]
    span = length // SUBS
    index = sub_index()
    before = (index * span).astype(f32)
    for tile in range(tiles):
        rate = jnp.exp(logr_ref[:, lane_tile(tile)])
        decay = jnp.exp(-rate)
        scale = coef_ref[:, lane_tile(tile)] * jnp.sqrt(2.0 * rate)
        incoming = jnp.zeros((states, LANES), f32)
        for j in range(all_ref.shape[0]):
            gap = place[1] - 1 - j
            distance = (jnp.maximum(gap, 0) * length).astype(f32)
            term = jnp.exp(-distance * rate) * all_ref[j, :, lane_tile(tile)].astype(f32)
            incoming = incoming + jnp.where(gap >= 0, term, 0.0)
        for first in range(0, states, GROUP):
            chosen = range(first, first + GROUP)
            starts = []
            for n in chosen:
                row = rate[n : n + 1]
                run = ends_ref[n, :, lane_tile(tile)]
                for d in (1, 2, 4):
                    moved = jnp.exp(-(d * span) * row) * pltpu.roll(run, d, 0)
                    run = run + jnp.where(index >= d, moved, 0.0)
                run = jnp.where(index >= 1, pltpu.roll(run, 1, 0), 0.0)
                starts.append(run + jnp.exp(-before * row) * incoming[n : n + 1])
            decays = [spread(decay[n : n + 1]) for n in chosen]
            scales = [spread(scale[n : n + 1]) for n in chosen]

            def step(i, held):
                at = step_rows(i)
                u = u_tiles[tile, at, :]
                held = tuple(d * h + u for d, h in zip(decays, held))
                parts = [s * h for s, h in zip(scales, held)]
                if first > 0:
                    parts[0] = parts[0] + y_tiles[tile, at, :]
                while len(parts) > 1:
                    parts = [a + b for a, b in zip(parts[::2], parts[1::2])]
                y_tiles[tile, at, :] = parts[0]
                return held

            lax.fori_loop(0, span, step, tuple(starts), unroll=4)
        from_steps(rows, y_tiles, tile)
        context_ref[:, lane_tile(tile)] = rows[...].astype(bf16)


def whole_rows(block):
    return block.reshape(block.shape[0] * block.shape[1], block.shape[2])


def head(index):
    return slice(index * HD, (index + 1) * HD)


def weight_copies(near, far, buffer, place, sems, act):
    count = sems.shape[0]
    half = count // 2
    for k in range(count):
        owner = lax.rem(place[6] + count - k, count)
        for stacks, low in ((near, 0), (far, half)):

            @pl.when((owner >= low) & (owner < low + half))
            def move():
                for r, stack in enumerate(stacks):
                    inner = buffer.at[k, place[2] ^ r]
                    act(pltpu.make_async_copy(stack.at[owner - low], inner, sems.at[k, r]))


def of_heads(buffer, i):
    return jnp.concatenate([whole_rows(buffer[k, :, :, head(i)]) for k in range(buffer.shape[0])], axis=1)


def gradient_slot(row_parts, order, r):
    position = 0
    for bit in reversed(order):
        position = 2 * position + (1 if r & bit else 0)
    return position // (row_parts // 2), position % (row_parts // 2)


def round_orders(row_parts):
    bits = [1 << i for i in range(row_parts.bit_length() - 1)]
    return bits, bits[::-1]


def gradient_pieces(stacks, row_parts, far, slot):
    found = []
    for r in range(row_parts):
        sent, at = gradient_slot(row_parts, round_orders(row_parts)[far], r)
        found.append(stacks[2 * far + sent].at[at, slot])
    return found


def project_kernel(team, col_parts, row_parts, place, normed_ref, cot_ref, *refs):
    contexts, refs = refs[:team], refs[team:]
    near, far, refs = refs[:row_parts], refs[row_parts : 2 * row_parts], refs[2 * row_parts :]
    context_t_ref, cot_t_ref, kept_ref = refs[:3]
    context_ref, weights, sems = refs[3:]
    weight_copies(near, far, weights, place, sems, lambda copy: copy.start())
    width = contexts[0].shape[1]
    for k in range(team):
        lanes = pl.ds(pl.multiple_of((place[0] ^ k) * width, LANES), width)
        context_ref[:, lanes] = contexts[k][...]
    context_t_ref[...] = context_ref[...].T
    cot_t_ref[...] = cot_ref[...].T
    weight_copies(near, far, weights, place, sems, lambda copy: copy.wait())
    kept_ref[0] = dot(normed_ref[...], of_heads(weights, 0)).astype(bf16)
    kept_ref[1] = dot(context_ref[...], of_heads(weights, 1)).astype(bf16)
    kept_ref[2] = dot(context_ref[...], of_heads(weights, 2)).astype(bf16)


def attend_kernel(team, col_parts, row_parts, place, kept_ref, *refs):
    near, far, refs = refs[:row_parts], refs[row_parts : 2 * row_parts], refs[2 * row_parts :]
    part_ref, attended_ref, probs_ref, probs_t_ref, weights, sems = refs
    weight_copies(near, far, weights, place, sems, lambda copy: copy.start())
    length = kept_ref.shape[1]
    rows = lax.broadcasted_iota(jnp.int32, (length, length), 0)
    cols = lax.broadcasted_iota(jnp.int32, (length, length), 1)
    for h in range(col_parts):
        scores = dot_t(kept_ref[0, :, head(h)], kept_ref[1, :, head(h)]) * score_scale
        scores = jnp.where(rows >= cols, scores, -1e30)
        shifted = jnp.exp(scores - jnp.max(scores, axis=-1, keepdims=True))
        inverse = 1.0 / jnp.sum(shifted, axis=-1, keepdims=True)
        probs = (shifted * inverse).astype(bf16)
        probs_ref[h] = probs
        probs_t_ref[h] = probs.T
        attended_ref[:, head(h)] = dot(probs, kept_ref[2, :, head(h)]).astype(bf16)
    weight_copies(near, far, weights, place, sems, lambda copy: copy.wait())
    part_ref[...] = dot_t(attended_ref[...], of_heads(weights, 3)).astype(bf16)


def gelu_parts(hidden, grad_act):
    density = jnp.exp(-0.5 * hidden * hidden)
    t = 1.0 / (1.0 + (0.3275911 * math.sqrt(0.5)) * jnp.abs(hidden))
    series = 0.5 * 1.061405429
    for factor in (-1.453152027, 1.421413741, -0.284496736, 0.254829592):
        series = series * t + 0.5 * factor
    tail = series * t * density
    cdf = jnp.where(hidden >= 0.0, 1.0 - tail, tail)
    slope = cdf + hidden * density * (1.0 / math.sqrt(2.0 * math.pi))
    return (hidden * cdf).astype(bf16), (grad_act * slope).astype(bf16)


def middle_kernel(team, x_ref, gain_ref, *refs):
    parts, (middle_ref, normed_ref, normed_t_ref) = refs[:team], refs[team:]
    attn = parts[0][...].astype(f32)
    for part in parts[1:]:
        attn = attn + part[...].astype(f32)
    middle = x_ref[...].astype(f32) + attn
    middle_ref[...] = middle
    unit, unused = normalise(middle)
    normed_ref[...] = (unit * gain_ref[...]).astype(bf16)
    normed_t_ref[...] = normed_ref[...].T


def feed_kernel(team, col_parts, row_parts, place, normed_ref, normed_t_ref, cot_ref, cot_t_ref, *refs):
    count = col_parts * row_parts
    pieces, refs = refs[:count], refs[count:]
    outs, two_ref, refs = refs[:team], refs[team], refs[team + 1 :]
    stacks, refs = (refs[:4], refs[4:8]), refs[8:]
    up_all, down_all, grad_up, grad_down, activated_all, grad_all, sems = refs
    z = pl.program_id(0)
    half = col_parts // 2
    hidden_cols = grad_up.shape[3]

    def copies(k):
        found = []
        for r in range(row_parts):
            for which, buffer in enumerate((up_all, down_all)):
                outside = pieces[k * row_parts + r].at[:, pl.ds(which * hidden_cols, hidden_cols)]
                inside = buffer.at[place[2] ^ r, :, pl.ds(k * hidden_cols, hidden_cols)]
                found.append(pltpu.make_async_copy(outside, inside, sems.at[which, k, r]))
        return found

    def each_leaving(k, act):
        for which, buffer in enumerate((grad_up, grad_down)):
            for r, piece in enumerate(gradient_pieces(stacks[which], row_parts, k // half, k % half)):
                inner = buffer.at[k, place[2] ^ r]
                act(pltpu.make_async_copy(inner, piece, sems.at[2 + which, k, r]))

    @pl.when(z == 0)
    def start():
        for k in range(col_parts):
            for copy in copies(k):
                copy.start()

    for k in range(col_parts):

        @pl.when(z == k)
        def arrive():
            for copy in copies(k):
                copy.wait()

    at = pl.ds(pl.multiple_of(z * hidden_cols, hidden_cols), hidden_cols)
    hidden = dot(normed_ref[...], whole_rows(up_all[:, :, at]))
    grad_act = dot(cot_ref[...], whole_rows(down_all[:, :, at]))
    activated, grad_pre = gelu_parts(hidden, grad_act)
    activated_all[:, at] = activated
    grad_all[:, at] = grad_pre
    shape = grad_up.shape[1:]
    grad_up[z] = dot(normed_t_ref[...], grad_pre).astype(bf16).reshape(shape)
    grad_down[z] = dot(cot_t_ref[...], activated).astype(bf16).reshape(shape)

    for k in range(col_parts):

        @pl.when(z == k)
        def leave():
            each_leaving(k, lambda copy: copy.start())

    @pl.when(z == col_parts - 1)
    def finish():
        two_ref[...] = dot_t(grad_all[...], whole_rows(up_all[...])).astype(bf16)
        rows = outs[0].shape[0]
        for k in range(team):
            at_rows = pl.ds(pl.multiple_of((place[0] ^ k) * rows, rows), rows)
            outs[k][...] = dot_t(activated_all[at_rows, :], whole_rows(down_all[...])).astype(bf16)
        for k in range(col_parts):
            each_leaving(k, lambda copy: copy.wait())


def attend_back_kernel(team, col_parts, row_parts, place, middle_ref, gain_ref, cot_ref, *refs):
    parts, refs = refs[:team], refs[team:]
    late, refs = refs[:3], refs[3:]
    near, far, refs = refs[:row_parts], refs[row_parts : 2 * row_parts], refs[2 * row_parts :]
    middle_grad_ref, gain_grad_ref, one_ref, low = refs[:4]
    grad_q, grad_k, grad_v = refs[4:7]
    context_grads, refs = refs[7 : 7 + team], refs[7 + team :]
    weights, grad_out, total_low = refs[:3]
    held, (sems, late_sems) = refs[3:6], refs[6:]
    kept_ref, probs_ref, probs_t_ref = held
    weight_copies(near, far, weights, place, sems, lambda copy: copy.start())
    late_copies = [
        pltpu.make_async_copy(outside, inside, late_sems.at[i])
        for i, (outside, inside) in enumerate(zip(late, held))
    ]
    for copy in late_copies:
        copy.start()
    own_rows = middle_ref.shape[0] // team
    grad_two = parts[0][...].astype(f32)
    for part in parts[1:]:
        grad_two = grad_two + part[...].astype(f32)
    unit, inverse = normalise(middle_ref[...])
    grad_gain = grad_two * unit
    rows = lax.broadcasted_iota(jnp.int32, grad_gain.shape, 0)
    first = place[0] * own_rows
    mine = (rows >= first) & (rows < first + own_rows)
    gain_grad_ref[...] = jnp.sum(jnp.where(mine, grad_gain, 0.0), axis=0, keepdims=True)
    grad = cot_ref[...].astype(f32) + normalise_back(unit, inverse, grad_two * gain_ref[...])
    low[...] = grad.astype(bf16)
    for k in range(team):

        @pl.when(place[0] == k)
        def own():
            middle_grad_ref[...] = grad[k * own_rows : (k + 1) * own_rows, :]

    weight_copies(near, far, weights, place, sems, lambda copy: copy.wait())
    for copy in late_copies:
        copy.wait()
    grad_out[...] = dot(low[...], of_heads(weights, 3)).astype(bf16)
    for h in range(col_parts):
        q, k, v = (kept_ref[i, :, head(h)] for i in range(3))
        grad_heads = grad_out[:, head(h)]
        grad_v[:, head(h)] = dot(probs_t_ref[h], grad_heads).astype(bf16)
        probs = probs_ref[h].astype(f32)
        grad_probs = dot_t(grad_heads, v)
        inner = jnp.sum(grad_probs * probs, axis=-1, keepdims=True)
        grad_scores = (probs * (grad_probs - inner)).astype(bf16)
        grad_q[:, head(h)] = (dot(grad_scores, k) * score_scale).astype(bf16)
        turned = dot_t(v, grad_heads) - inner.T
        turned = (probs_t_ref[h].astype(f32) * turned).astype(bf16)
        grad_k[:, head(h)] = (dot(turned, q) * score_scale).astype(bf16)
    total = dot_t(grad_k[...], of_heads(weights, 1)) + dot_t(grad_v[...], of_heads(weights, 2))
    total_low[...] = total.astype(bf16)
    width = context_grads[0].shape[1]
    for k in range(team):
        lanes = pl.ds(pl.multiple_of((place[0] ^ k) * width, LANES), width)
        context_grads[k][...] = total_low[:, lanes]
    one_ref[...] = dot_t(grad_q[...], of_heads(weights, 0)).astype(bf16)


def head_grads_kernel(col_parts, row_parts, place, low, attended_ref, *refs):
    normed_t_ref, context_t_ref, grad_q, grad_k, grad_v = refs[:5]
    stacks, (grads, out_sems) = refs[5:9], refs[9:]
    half = col_parts // 2
    shape = (*grads.shape[1:3], HD)

    def put(i, grad):
        for h in range(col_parts):
            grads[h, :, :, head(i)] = grad[:, head(h)].astype(bf16).reshape(shape)

    put(0, dot(normed_t_ref[...], grad_q[...]))
    put(1, dot(context_t_ref[...], grad_k[...]))
    put(2, dot(context_t_ref[...], grad_v[...]))
    put(3, dot(low[...].T, attended_ref[...]))
    copies = []
    for k in range(col_parts):
        for r, piece in enumerate(gradient_pieces(stacks, row_parts, k // half, k % half)):
            copies.append(pltpu.make_async_copy(grads.at[k, place[2] ^ r], piece, out_sems.at[k, r]))
    for copy in copies:
        copy.start()
    for copy in copies:
        copy.wait()


def adjoint_kernel(team, logr_ref, *refs):
    parts = refs[:team]
    g_tiles, ends_ref, total_ref, rows = refs[team:]
    grad = parts[0][...].astype(f32)
    for part in parts[1:]:
        grad = grad + part[...].astype(f32)
    grad = grad.astype(bf16).astype(f32)
    tiles, length, unused = g_tiles.shape
    states = logr_ref.shape[0]
    span = length // SUBS
    for tile in range(tiles):
        rows[...] = grad[:, lane_tile(tile)]
        in_steps(g_tiles, tile, rows)
    before = (sub_index() * span).astype(f32)
    for tile in range(tiles):
        rate = jnp.exp(logr_ref[:, lane_tile(tile)])
        decay = jnp.exp(-rate)
        for first in range(0, states, GROUP):
            chosen = range(first, first + GROUP)
            decays = [spread(decay[n : n + 1]) for n in chosen]

            def step(i, held):
                g = g_tiles[tile, step_rows(span - 1 - i), :]
                later = []
                for d, (b, w) in zip(decays, held):
                    shrunk = d * b
                    later.append((g + shrunk, d * w + shrunk))
                return tuple(later)

            zero = no_state(g_tiles)
            held = lax.fori_loop(0, span, step, ((zero, zero),) * GROUP, unroll=4)
            for n, (b, w) in zip(chosen, held):
                ends_ref[0, n, :, lane_tile(tile)] = b
                ends_ref[1, n, :, lane_tile(tile)] = w
                shrink = jnp.exp(-before * rate[n : n + 1])
                total_ref[0, n : n + 1, lane_tile(tile)] = jnp.sum(
                    shrink * b, axis=0, keepdims=True
                )
                total_ref[1, n : n + 1, lane_tile(tile)] = jnp.sum(
                    shrink * (w + before * b), axis=0, keepdims=True
                )


def context_back_kernel(
    team, place, g_tiles, u_tiles, ends_ref, all_ref, logr_ref, coef_ref, one_ref, *refs
):
    pieces = refs[:team]
    grad_ssm_ref, y_tiles, full, rows = refs[team:]
    tiles, length, unused = u_tiles.shape
    states = logr_ref.shape[0]
    span = length // SUBS
    width = tiles * LANES
    index = sub_index()
    after = ((SUBS - 1 - index) * span).astype(f32)
    full[...] = one_ref[...].astype(f32)
    group = GROUP
    for tile in range(tiles):
        lanes = lane_tile(tile)
        rate = jnp.exp(logr_ref[:, lanes])
        decay = jnp.exp(-rate)
        root = jnp.sqrt(2.0 * rate)
        scale = coef_ref[:, lanes] * root
        in_b = jnp.zeros((states, LANES), f32)
        in_w = jnp.zeros((states, LANES), f32)
        for j in range(all_ref.shape[0]):
            gap = j - place[1] - 1
            distance = (jnp.maximum(gap, 0) * length).astype(f32)
            shrink = jnp.exp(-distance * rate)
            b, w = all_ref[j, 0, :, lanes].astype(f32), all_ref[j, 1, :, lanes].astype(f32)
            in_b = in_b + jnp.where(gap >= 0, shrink * b, 0.0)
            in_w = in_w + jnp.where(gap >= 0, shrink * (w + distance * b), 0.0)
        for first in range(0, states, group):
            chosen = range(first, first + group)
            starts = []
            for n in chosen:
                row = rate[n : n + 1]
                b, w = ends_ref[0, n, :, lanes], ends_ref[1, n, :, lanes]
                for d in (1, 2, 4):
                    shrink = jnp.exp(-(d * span) * row)
                    next_b = pltpu.roll(b, SUBS - d, 0)
                    next_w = pltpu.roll(w, SUBS - d, 0)
                    inside = index < SUBS - d
                    b, w = (
                        b + jnp.where(inside, shrink * next_b, 0.0),
                        w + jnp.where(inside, shrink * (next_w + (d * span) * next_b), 0.0),
                    )
                inside = index < SUBS - 1
                b = jnp.where(inside, pltpu.roll(b, SUBS - 1, 0), 0.0)
                w = jnp.where(inside, pltpu.roll(w, SUBS - 1, 0), 0.0)
                shrink = jnp.exp(-after * row)
                b_row, w_row = in_b[n : n + 1], in_w[n : n + 1]
                b = b + shrink * b_row
                w = w + shrink * (w_row + after * b_row)
                zero = no_state(u_tiles)
                starts.append((b, w, zero, zero))
            decays = [spread(decay[n : n + 1]) for n in chosen]
            scales = [spread(scale[n : n + 1]) for n in chosen]

            def step(i, held):
                at = step_rows(span - 1 - i)
                g = g_tiles[tile, at, :]
                u = u_tiles[tile, at, :]
                later, parts = [], []
                for d, s, (b, w, sum_b, sum_w) in zip(decays, scales, held):
                    shrunk = d * b
                    w = d * w + shrunk
                    b = g + shrunk
                    later.append((b, w, sum_b + u * b, sum_w + u * w))
                    parts.append(s * b)
                while len(parts) > 1:
                    parts = [p + q for p, q in zip(parts[::2], parts[1::2])]
                if first > 0:
                    parts[0] = parts[0] + y_tiles[tile, at, :]
                y_tiles[tile, at, :] = parts[0]
                return tuple(later)

            held = lax.fori_loop(0, span, step, tuple(starts), unroll=2)
            for n, (unused_b, unused_w, sum_b, sum_w) in zip(chosen, held):
                sum_b = jnp.sum(sum_b, axis=0, keepdims=True)
                sum_w = jnp.sum(sum_w, axis=0, keepdims=True)
                row = slice(n, n + 1)
                grad_ssm_ref[0, row, lanes] = root[row] * sum_b
                grad_ssm_ref[1, row, lanes] = scale[row] * (0.5 * sum_b - rate[row] * sum_w)
        at_lanes = pl.ds(pl.multiple_of(place[0] * width + tile * LANES, LANES), LANES)
        from_steps(rows, y_tiles, tile)
        full[:, at_lanes] += rows[...].astype(bf16).astype(f32)
    count = pieces[0].shape[0]
    for k in range(team):
        at_rows = pl.ds(pl.multiple_of((place[0] ^ k) * count, count), count)
        pieces[k][...] = full[at_rows, :].astype(bf16)


def input_grad_kernel(team, place, x_ref, gain_ref, middle_grad_ref, *refs):
    parts, (out_ref, gain_grad_ref) = refs[:team], refs[team:]
    rows = out_ref.shape[0]
    at_rows = pl.ds(pl.multiple_of(place[0] * rows, rows), rows)
    grad_one = parts[0][...].astype(f32)
    for part in parts[1:]:
        grad_one = grad_one + part[...].astype(f32)
    unit, inverse = normalise(x_ref[at_rows, :].astype(f32))
    gain_grad_ref[...] = jnp.sum(grad_one * unit, axis=0, keepdims=True)
    back = normalise_back(unit, inverse, grad_one * gain_ref[...])
    out_ref[...] = (middle_grad_ref[...] + back).astype(bf16)


def assemble_kernel(halves, low_count, place, own_ref, *refs):
    others, out_ref = refs[:-1], refs[-1]
    count, rows, unused = own_ref.shape
    half = place[4]

    def put(value, sequence, which, member):
        at_rows = pl.ds(pl.multiple_of((which * low_count + member) * rows, rows), rows)
        out_ref[sequence, at_rows, :] = value.astype(out_ref.dtype)

    for sequence in range(count // (halves * low_count)):
        if halves == 1:
            for member in range(low_count):
                put(own_ref[sequence * low_count + member], sequence, 0, member)
        else:
            put(own_ref[sequence * halves + half], sequence, half, 0)
            put(others[0][sequence], sequence, 1 - half, 0)


def pack_kernel(halves, place, qkv_ref, out_ref, up_ref, down_ref, *refs):
    rows = up_ref.shape[0]
    heads, hidden = out_ref.shape[0] // halves, up_ref.shape[1] // halves
    for which in range(halves):
        side = place[4] if which == 0 else 1 - place[4]
        at_heads = pl.ds(pl.multiple_of(side * heads, LANES), heads)
        at_hidden = pl.ds(pl.multiple_of(side * hidden, LANES), hidden)
        if which == 0:
            head_ref = refs[0]
            wide_ref, deep_ref = refs[1].at[:, :hidden], refs[1].at[:, hidden:]
        else:
            packed = refs[2]
            head_ref = packed.at[:, : 4 * heads]
            wide_ref = packed.at[:, 4 * heads : 4 * heads + hidden]
            deep_ref = packed.at[:, 4 * heads + hidden :]
        for i in range(3):
            head_ref[:, i * heads : (i + 1) * heads] = qkv_ref[i, :, at_heads].astype(bf16)
        head_ref[:, 3 * heads :] = out_ref[at_heads, :].T.astype(bf16)
        wide_ref[...] = up_ref[:, at_hidden].astype(bf16)
        deep_ref[...] = down_ref[at_hidden, :].T.astype(bf16)


def small_kernel(ssm_ref, gains_ref, out_ref):
    count = ssm_ref.shape[0]
    out_ref[:count, :] = ssm_ref[...]
    out_ref[count:, :] = gains_ref[...]


def lamb_moments(weight, grad_item, first_old, second_old):
    first_new = beta_first * first_old + (1.0 - beta_first) * grad_item
    second_new = beta_second * second_old + (1.0 - beta_second) * grad_item * grad_item
    direction = (
        first_new
        / (1.0 - beta_first**STEP)
        / (jnp.sqrt(second_new / (1.0 - beta_second**STEP)) + lamb_eps)
        + weight_decay * weight
    )
    return (first_new, second_new, direction)


def place_sums(sums_ref, sums):
    rows = lax.broadcasted_iota(jnp.int32, sums_ref.shape, 0)
    lanes = lax.broadcasted_iota(jnp.int32, sums_ref.shape, 1)
    found = jnp.zeros(sums_ref.shape, f32)
    for index, pair in sums.items():
        for row, value in enumerate(pair):
            found = jnp.where((rows == row) & (lanes == index), value, found)
    sums_ref[...] = found


def moments_kernel(halves, matrices, place, *refs):
    count = 1 + max(item[1] for item in matrices)
    grads, refs = [refs[halves * i : halves * (i + 1)] for i in range(count)], refs[halves * count :]
    arrays = len({(item[1], item[4] is None) for item in matrices})
    ins = [refs[3 * i : 3 * i + 3] for i in range(arrays)]
    outs = [refs[3 * (arrays + i) : 3 * (arrays + i) + 3] for i in range(arrays)]
    sums_ref = refs[6 * arrays]
    keys = []
    sums = {}
    for number, source, column, turned, stacked in matrices:
        key = (source, stacked is None)
        if key not in keys:
            keys.append(key)
        pick = (lambda ref: ref) if stacked is None else (lambda ref, i=stacked: ref.at[i])
        weight, first, second = (pick(ref) for ref in ins[keys.index(key)])
        news = [pick(ref) for ref in outs[keys.index(key)]]
        width = weight.shape[0 if turned else 1] // halves
        rows = weight.shape[1 if turned else 0]
        cols = slice(column * width, (column + 1) * width)
        total_weight = total_update = 0.0
        for which, grad_ref in enumerate(grads[source]):
            side = place[4] if which == 0 else 1 - place[4]
            at = pl.ds(pl.multiple_of(side * width, width), width)
            if which == 0:
                grad = grad_ref[pl.ds(pl.multiple_of(side * rows, rows), rows), cols].astype(f32)
            else:
                grad = grad_ref[:, cols].astype(f32)
            at = (at, slice(None)) if turned else (slice(None), at)
            grad = grad.T if turned else grad
            old = weight[at]
            found = lamb_moments(old, grad, first[at], second[at])
            for ref, value in zip(news, found):
                ref[at] = value
            total_weight = total_weight + jnp.sum(old * old)
            total_update = total_update + jnp.sum(found[2] * found[2])
        sums[number] = (total_weight, total_update)
    place_sums(sums_ref, sums)


def small_moments_kernel(numbers, grads_ref, *refs):
    ins, outs, sums_ref = (refs[:3], refs[3:6]), (refs[6:9], refs[9:12]), refs[12]
    states = (grads_ref.shape[0] - 2) // 2
    sums = {}
    for (weight, first, second), news, start, rows, first_number in (
        (ins[0], outs[0], 2 * states, 1, numbers[0]),
        (ins[1], outs[1], 0, states, numbers[1]),
    ):
        for i in range(2):
            grad = grads_ref[start + i * rows : start + (i + 1) * rows, :]
            at = slice(i * rows, (i + 1) * rows)
            found = lamb_moments(weight[at, :], grad, first[at, :], second[at, :])
            for ref, value in zip(news, found):
                ref[at, :] = value
            sums[first_number + i] = (
                jnp.sum(weight[at, :] * weight[at, :]),
                jnp.sum(found[2] * found[2]),
            )
    place_sums(sums_ref, sums)


def update_kernel(stacks, sums_ref, *refs):
    count = len(stacks)
    weights, directions, news = refs[:count], refs[count : 2 * count], refs[2 * count : 3 * count]
    norms = jnp.sqrt(jnp.sum(sums_ref[...], axis=0))
    refs[3 * count][...] = norms
    ratios = norms[0:1] / norms[1:2]
    lanes = lax.broadcasted_iota(jnp.int32, ratios.shape, 1)
    for numbers, weight, direction, new in zip(stacks, weights, directions, news):
        step = weight.shape[0] // len(numbers)
        for i, number in enumerate(numbers):
            ratio = jnp.sum(jnp.where(lanes == number, ratios, 0.0), axis=1, keepdims=True)
            at = slice(i * step, (i + 1) * step)
            scale = learn_rate * ratio.reshape((1,) * weight.ndim)
            new[at] = weight[at] - scale * direction[at]


def call(
    body, ins, outs, scratch=(), grid=None, in_specs=None, out_specs=None, time=1.0, after=(), token=False
):
    moved = sum(a.size * a.dtype.itemsize for a in list(ins) + list(outs))
    params = pltpu.CompilerParams(vmem_limit_bytes=VMEM_BYTES)
    cost = pl.CostEstimate(flops=int(time * 1.15e9), bytes_accessed=moved, transcendentals=0)
    whole = pl.BlockSpec(memory_space=pltpu.VMEM)
    anywhere = pl.BlockSpec(memory_space=pl.ANY)
    in_specs = list(in_specs or [whole] * len(ins)) + [anywhere] * len(after)
    out_specs = list(out_specs or [whole] * len(outs))
    outs = list(outs)
    first_out = len(ins) + len(after)
    last_out = first_out + len(outs)
    if token:
        outs.append(jax.ShapeDtypeStruct((SUBS, LANES), f32))
        out_specs.append(whole)

    def run(*refs):
        refs = list(refs)
        if token:
            refs[last_out][...] = jnp.zeros((SUBS, LANES), f32)
            del refs[last_out]
        body(*refs[: len(ins)], *refs[first_out:])

    return pl.pallas_call(
        run,
        out_shape=tuple(outs),
        in_specs=in_specs,
        out_specs=tuple(out_specs),
        scratch_shapes=list(scratch),
        compiler_params=params,
        cost_estimate=cost,
        **({} if grid is None else {"grid": grid}),
    )(*ins, *after)


def shaped(shape, kind):
    return jax.ShapeDtypeStruct(tuple(shape), kind)


def on_device(
    tokens,
    cotangent,
    w_qkv,
    w_out,
    w_up,
    w_down,
    norm_gains,
    ssm_param,
    first_qkv,
    second_qkv,
    first_out,
    second_out,
    first_up,
    second_up,
    first_down,
    second_down,
    first_gain,
    second_gain,
    first_ssm,
    second_ssm,
):
    halves = lax.axis_size("sl")
    low_count = lax.axis_size("ml")
    row_parts = lax.axis_size("sh")
    col_parts = lax.axis_size("mb") * lax.axis_size("mq")
    team = halves * low_count
    sl, ml, mb, mq = (lax.axis_index(name) for name in ("sl", "ml", "mb", "mq"))
    rank = sl * low_count + ml
    block_index = lax.axis_index("sh") * halves + mq
    seq_total, length, width = tokens.shape
    assert length == BLK and seq_total == lax.axis_size("mb")
    states = ssm_param.shape[1]
    channels = width // team
    tiles = channels // LANES
    row_count = width // row_parts
    own_rows = length // team
    place = [rank, block_index, lax.axis_index("sh"), lax.axis_index(MODEL), sl, sl ^ mq]
    place.append(lax.axis_index(COLS))
    place = jnp.stack(place).astype(jnp.int32)
    smem = pl.BlockSpec(memory_space=pltpu.SMEM)
    vmem = pl.BlockSpec(memory_space=pltpu.VMEM)

    def permute(value, axes, moves):
        return lax.ppermute(value, axes, moves)

    def swap(value):
        return permute(value, "sl", [(0, 1), (1, 0)])

    def in_order(own, other, axis):
        return jnp.where(
            sl == 0, jnp.concatenate([own, other], axis), jnp.concatenate([other, own], axis)
        )

    def team_send(pieces):
        moved = [pieces[0]]
        for k in range(1, team):
            moved.append(permute(pieces[k], TEAM, [(i, i ^ k) for i in range(team)]))
        return moved

    def pick_block(array):
        own = lax.dynamic_index_in_dim(array, mb, 0, keepdims=False)
        if halves == 1:
            return own, ()
        other = swap(own)
        return jnp.where(sl == mq, own, other), (other,)

    def across(value, bit):
        return permute(value, "sh", [(i, i ^ bit) for i in range(row_parts)])

    def along(value, axes, step):
        count = lax.axis_size(axes)
        return permute(value, axes, [(i, (i + step) % count) for i in range(count)])

    bits = [1 << i for i in range(row_parts.bit_length() - 1)]

    def bit_order(k):
        return bits if k % 2 == 0 else bits[::-1]

    def double_rows(value, order):
        found = {0: value}
        for bit in order:
            for r in list(found):
                found[r | bit] = across(found[r], bit)
        return [found[r] for r in range(row_parts)]

    def add(*items, zero=None):
        total = sum(item.astype(f32) for item in items)
        return (total if zero is None else total + zero[0, 0]).astype(bf16)

    def first_messages(stacks):
        return across(stacks[1], bits[-1]), across(stacks[3], bits[0])

    def second_messages(stacks, first, zero):
        count = first[0].shape[0] // 2
        return [add(stacks[2 * i][count:], first[i][count:], zero=zero) for i in range(2)]

    def halve_rows(keep, arrived, order, send, last):
        items = [keep, arrived]
        for bit in order[-2::-1]:
            count = arrived.shape[0] // 2
            if send is None:
                send = add(*[item[count:] for item in items])
            arrived = across(send, bit)
            items = [item[:count] for item in items] + [arrived]
            send = None
        return add(*[item[0] for item in items], zero=last)

    def halve_both(stacks, first, send, last=None):
        near = halve_rows(stacks[0], first[0], bits, send[0], last)
        return near, halve_rows(stacks[2], first[1], bits[::-1], send[1], last)

    def hold(arrays, after):
        anywhere = pl.BlockSpec(memory_space=pl.ANY)
        return pl.pallas_call(
            lambda *refs: None,
            out_shape=tuple(shaped(item.shape, item.dtype) for item in arrays),
            in_specs=[anywhere] * (len(arrays) + len(after)),
            out_specs=(anywhere,) * len(arrays),
            input_output_aliases={i: i for i in range(len(arrays))},
        )(*arrays, *after)

    def gather_pieces(shard):
        pieces = []
        for k in range(col_parts):
            held = along(held, COLS, 1) if k > 0 else shard
            pieces.append(double_rows(held, bits if k % 2 == 0 else bits[::-1]))
        return pieces

    def sum_over_z(near, far, ring=True):
        if not ring:
            pieces = [stack[k] for stack in (near, far) for k in range(col_parts // 2)]
            moved = [along(piece, COLS, -k) for k, piece in enumerate(pieces) if k > 0]
            return add(pieces[0], *moved)
        held = None
        for stack in (far, near):
            for k in reversed(range(stack.shape[0])):
                held = stack[k] if held is None else add(stack[k], along(held, COLS, -1))
        return held

    def everywhere(value, axes):
        count = lax.axis_size(axes)
        copies = jnp.broadcast_to(value[None], (count, *value.shape))
        return lax.all_to_all(copies, axes, 0, 0, tiled=True)

    rows_dev = w_up.shape[0]
    hidden_cols = w_up.shape[1] // halves
    head_cols = 4 * w_out.shape[0] // halves
    packed_cols = head_cols + 2 * hidden_cols
    sides = [shaped((rows_dev, cols), bf16) for cols in (head_cols, 2 * hidden_cols)]
    shards = call(
        functools.partial(pack_kernel, halves),
        (place, w_qkv, w_out, w_up, w_down),
        sides + [shaped((rows_dev, packed_cols), bf16)] * (halves - 1),
        time=2.4,
        in_specs=[smem] + [vmem] * 4,
    )
    if halves == 2:
        other = swap(shards[2])
        cuts = (0, head_cols, packed_cols)
        shards = [
            in_order(own, other[:, first:last], 0)
            for own, first, last in zip(shards, cuts, cuts[1:])
        ]
    head_shard, hidden_shard = shards[:2]
    hidden_w = gather_pieces(hidden_shard)
    (head_shard,) = hold((head_shard,), (hidden_w[1][0],))
    attn_full = lax.all_gather(head_shard, COLS, axis=0, tiled=False)
    hidden_flat = [piece for group in hidden_w for piece in group]

    small, = call(
        small_kernel,
        (ssm_param.reshape(2 * states, -1), norm_gains),
        (shaped((2 * states + 2, norm_gains.shape[1]), f32),),
        after=hidden_w[0][1:-1],
    )
    small = jnp.transpose(everywhere(small, ALL), (1, 0, 2)).reshape(2 * states + 2, width)
    own_ssm = lax.dynamic_slice_in_dim(
        small[: 2 * states].reshape(2, states, width), rank * channels, channels, 2
    )
    coef, logr = own_ssm[0], own_ssm[1]
    gain_one = small[2 * states : 2 * states + 1]
    gain_two = small[2 * states + 1 : 2 * states + 2]

    x, unused = pick_block(tokens)
    cot, cot_other = pick_block(cotangent)

    anywhere = [pl.BlockSpec(memory_space=pl.ANY)]

    def fixed(*shape):
        return pl.BlockSpec(shape, lambda z: (0,) * len(shape))

    wide = fixed(length, width)
    row = fixed(1, width)

    normed_one, normed_t, u_steps, ends, total = call(
        norm_kernel,
        (place, x, gain_one, logr),
        (
            shaped((length, width), bf16),
            shaped((width, length), bf16),
            shaped((tiles, length, LANES), f32),
            shaped((states, SUBS, channels), f32),
            shaped((states, channels), f32),
        ),
        scratch=[pltpu.VMEM((length, LANES), f32)],
        in_specs=[smem, vmem, vmem, vmem],
        after=(hidden_w[1][0], *cot_other),
        time=5,
    )
    (attn_full,) = hold((attn_full,), (total,))
    attn_w = [
        *double_rows(attn_full[: col_parts // 2], bits),
        *double_rows(attn_full[col_parts // 2 :], bits[::-1]),
    ]
    totals = everywhere(total.astype(bf16), ("sh", "mq"))
    (context_own,) = call(
        context_kernel,
        (place, u_steps, ends, totals, logr, coef),
        (shaped((length, channels), bf16),),
        after=(hidden_w[0][-1], *hidden_w[1][1:-1], hidden_w[-1][0], *attn_w[1 : row_parts - 1]),
        scratch=[pltpu.VMEM((tiles, length, LANES), f32), pltpu.VMEM((length, LANES), f32)],
        in_specs=[smem] + [vmem] * 5,
        time=7,
    )
    contexts = team_send([context_own] * team)

    stack_shape = (row_parts // 2, col_parts // 2, row_count)
    head_stacks = [shaped((*stack_shape, head_cols), bf16)] * 4
    hidden_stacks = [shaped((*stack_shape, hidden_cols), bf16)] * 8
    sizes = (team, col_parts, row_parts)
    head_buffer = pltpu.VMEM((col_parts, row_parts, row_count, 4 * HD), bf16)
    head_sems = pltpu.SemaphoreType.DMA((col_parts, row_parts))
    kept_shape = shaped((3, length, col_parts * HD), bf16)
    flat_shape = shaped((length, col_parts * HD), bf16)
    context_t, cot_t, kept = call(
        functools.partial(project_kernel, *sizes),
        (place, normed_one, cot, *contexts, *attn_w),
        (shaped((width, length), bf16), shaped((width, length), bf16), kept_shape),
        scratch=[pltpu.VMEM((length, width), bf16), head_buffer, head_sems],
        time=1,
        in_specs=[smem] + [vmem] * (2 + team) + anywhere * len(attn_w),
        after=(hidden_w[1][-1], *[piece for group in hidden_w[2:3] for piece in group[1:]]),
    )
    attn_part, attended, probs, probs_t = call(
        functools.partial(attend_kernel, *sizes),
        (place, kept, *attn_w),
        (
            shaped((length, width), bf16),
            flat_shape,
            *[shaped((col_parts, length, length), bf16)] * 2,
        ),
        scratch=[head_buffer, head_sems],
        time=1,
        in_specs=[smem, vmem] + anywhere * len(attn_w),
        after=[piece for group in hidden_w[3:] for piece in group[1:-1]],
    )
    attn_parts = team_send([attn_part] * team)

    middle, normed_two, normed_two_t = call(
        functools.partial(middle_kernel, team),
        (x, gain_two, *attn_parts),
        (shaped((length, width), f32), shaped((length, width), bf16), shaped((width, length), bf16)),
        time=1,
    )
    weight_buffer = pltpu.VMEM((row_parts, row_count, col_parts * hidden_cols), bf16)
    grad_buffer = pltpu.VMEM((col_parts, row_parts, row_count, hidden_cols), bf16)
    fed = call(
        functools.partial(feed_kernel, team, col_parts, row_parts),
        (place, normed_two, normed_two_t, cot, cot_t, *hidden_flat),
        (
            *[shaped((own_rows, width), bf16)] * team,
            shaped((length, width), bf16),
            *hidden_stacks,
        ),
        scratch=[
            *[weight_buffer] * 2,
            *[grad_buffer] * 2,
            *[pltpu.VMEM((length, col_parts * hidden_cols), bf16)] * 2,
            pltpu.SemaphoreType.DMA((4, col_parts, row_parts)),
        ],
        time=18,
        grid=(col_parts,),
        in_specs=[smem, wide, fixed(width, length), wide, fixed(width, length)]
        + anywhere * len(hidden_flat),
        out_specs=[fixed(own_rows, width)] * team + [wide] + anywhere * 8,
    )
    out_pieces, two_part, hidden_grads = fed[:team], fed[team], fed[team + 1 :]
    two_parts = team_send([two_part] * team)

    def rows_of(array, member):
        return lax.dynamic_slice_in_dim(array, member * own_rows, own_rows, 0)

    def share_rows(pieces, kind):
        others = []
        if halves == 2:
            pairs = pieces.reshape(seq_total, halves, own_rows, width)
            others = [swap(lax.dynamic_index_in_dim(pairs, 1 - sl, 1, keepdims=False))]
        (blocks,) = call(
            functools.partial(assemble_kernel, halves, low_count),
            (place, pieces, *others),
            (shaped((seq_total, length, width), kind),),
            time=3.5,
            in_specs=[smem, vmem] + [vmem] * len(others),
        )
        return blocks

    out_pieces = team_send(list(out_pieces))
    result = rows_of(middle, rank) + sum(item.astype(f32) for item in out_pieces)
    result = result.astype(bf16)
    layer_pieces = lax.all_gather(result, MODEL, axis=0, tiled=False)
    layer_out = share_rows(layer_pieces, bf16)

    def both_halves(own):
        if halves == 1:
            return [own]
        return [own, swap(lax.dynamic_slice_in_dim(own, (1 - sl) * rows_dev, rows_dev, 0))]

    middle_grad, gain_two_grad, one_part, low_grad, *rest = call(
        functools.partial(attend_back_kernel, *sizes),
        (place, middle, gain_two, cot, *two_parts, kept, probs, probs_t, *attn_w),
        (
            shaped((own_rows, width), f32),
            shaped((1, width), f32),
            shaped((length, width), bf16),
            shaped((length, width), bf16),
            *[flat_shape] * 3,
            *[shaped((length, channels), bf16)] * team,
        ),
        scratch=[
            head_buffer,
            pltpu.VMEM(flat_shape.shape, bf16),
            pltpu.VMEM((length, width), bf16),
            pltpu.VMEM(kept_shape.shape, bf16),
            *[pltpu.VMEM((col_parts, length, length), bf16)] * 2,
            head_sems,
            pltpu.SemaphoreType.DMA((3,)),
        ],
        time=1,
        in_specs=[smem] + [vmem] * (3 + team) + anywhere * (3 + len(attn_w)),
        after=(result,),
    )
    head_grads, context_grads = rest[:3], rest[3:]
    context_grads = team_send(context_grads)
    *head_stacks, heads_done = call(
        functools.partial(head_grads_kernel, col_parts, row_parts),
        (place, low_grad, attended, normed_t, context_t, *head_grads),
        head_stacks,
        scratch=[head_buffer, head_sems],
        time=8,
        in_specs=[smem] + [vmem] * 7,
        out_specs=anywhere * 4,
        token=True,
    )
    down_first = first_messages(hidden_grads[4:])
    down_second = second_messages(hidden_grads[4:], down_first, heads_done)
    down_sums = halve_both(hidden_grads[4:], down_first, down_second)
    g_steps, adjoint_ends, adjoint_total, adjoint_done = call(
        functools.partial(adjoint_kernel, team),
        (logr, *context_grads),
        (
            shaped((tiles, length, LANES), f32),
            shaped((2, states, SUBS, channels), f32),
            shaped((2, states, channels), f32),
        ),
        scratch=[pltpu.VMEM((length, LANES), f32)],
        time=1,
        after=(heads_done, *down_second),
        token=True,
    )
    up_stacks = list(hidden_grads[:4])
    up_stacks[1::2] = hold(up_stacks[1::2], down_first)
    up_first = first_messages(up_stacks)
    (own_total,) = hold((adjoint_total.astype(bf16),), (*down_sums, *up_first))
    adjoint_totals = everywhere(own_total, ("sh", "mq"))
    grad_down = sum_over_z(*down_sums, False)
    up_second = second_messages(up_stacks, up_first, adjoint_done)
    up_second = hold(up_second, (adjoint_totals,))
    *one_pieces, grad_ssm, context_done = call(
        functools.partial(context_back_kernel, team),
        (place, g_steps, u_steps, adjoint_ends, adjoint_totals, logr, coef, one_part),
        (
            *[shaped((own_rows, width), bf16)] * team,
            shaped((2, states, channels), f32),
        ),
        scratch=[
            pltpu.VMEM((tiles, length, LANES), f32),
            pltpu.VMEM((length, width), f32),
            pltpu.VMEM((length, LANES), f32),
        ],
        in_specs=[smem] + [vmem] * 7,
        time=1,
        after=(*up_second, layer_pieces),
        token=True,
    )
    one_pieces = team_send(one_pieces)
    up_sums = halve_both(up_stacks, up_first, up_second, context_done)
    grad_rows, gain_one_grad, rows_done = call(
        functools.partial(input_grad_kernel, team),
        (place, x, gain_one, middle_grad, *one_pieces),
        (shaped((own_rows, width), bf16), shaped((1, width), f32)),
        in_specs=[smem] + [vmem] * (3 + team),
        time=1,
        after=(grad_down, *up_sums),
        token=True,
    )
    head_stacks[1::2] = hold(head_stacks[1::2], (grad_rows,))
    up_sums = hold(up_sums, head_stacks[1::2])
    head_first = first_messages(head_stacks)
    head_second = second_messages(head_stacks, head_first, rows_done)
    head_sums = halve_both(head_stacks, head_first, head_second)
    grad_up = sum_over_z(*up_sums)
    grad_heads = sum_over_z(*head_sums)
    input_grad = share_rows(lax.all_gather(grad_rows, MODEL, axis=0, tiled=False), f32)

    placed_ssm = lax.dynamic_update_slice_in_dim(
        jnp.zeros((2 * states, width), f32),
        grad_ssm.reshape(2 * states, channels),
        rank * channels,
        1,
    )
    small_grads = jnp.concatenate([placed_ssm, gain_one_grad, gain_two_grad], 0)
    (small_grads,) = hold((small_grads,), head_sums)
    small_grads = small_grads.reshape(2 * states + 2, lax.axis_size(ALL), -1)
    small_grads = lax.all_to_all(jnp.transpose(small_grads, (1, 0, 2)), ALL, 0, 0, tiled=True)
    small_grads = jnp.sum(small_grads, axis=0)

    def moments(matrices, grads, arrays, after=()):
        changed = [shaped(old.shape, f32) for group in arrays for old in group]
        grad_parts = [part for grad in grads for part in both_halves(grad)]
        ins = [item for group in arrays for item in group]
        *found, sums = call(
            functools.partial(moments_kernel, halves, matrices),
            (place, *grad_parts, *ins),
            (*changed, shaped((2, LANES), f32)),
            in_specs=[smem] + [vmem] * (len(grad_parts) + len(ins)),
            after=after,
            time=4,
        )
        return [found[3 * i : 3 * i + 3] for i in range(len(arrays))], sums

    hidden_new, hidden_sums = moments(
        ((4, 0, 0, False, None), (5, 1, 0, True, None)),
        (grad_up, grad_down),
        ((w_up, first_up, second_up), (w_down, first_down, second_down)),
    )
    heads_new, head_sums = moments(
        tuple((i, 0, i, False, i) for i in range(3)) + ((3, 0, 3, True, None),),
        (grad_heads,),
        ((w_qkv, first_qkv, second_qkv), (w_out, first_out, second_out)),
        (layer_out, input_grad),
    )
    own_channels = norm_gains.shape[1]
    ssm_items = [item.reshape(2 * states, own_channels) for item in (ssm_param, first_ssm, second_ssm)]
    small_items = [norm_gains, first_gain, second_gain, *ssm_items]
    *small_new, small_sums = call(
        functools.partial(small_moments_kernel, (6, 8)),
        (small_grads.reshape(2 * states + 2, own_channels), *small_items),
        (*[shaped(item.shape, f32) for item in small_items], shaped((2, LANES), f32)),
    )
    all_sums = everywhere(hidden_sums + head_sums + small_sums, ALL)
    masters = (w_qkv, w_out, w_up, w_down, norm_gains, ssm_items[0])
    news = (*heads_new, *hidden_new, small_new[:3], small_new[3:])
    *weights, norms = call(
        functools.partial(update_kernel, ((0, 1, 2), (3,), (4,), (5,), (6, 7), (8, 9))),
        (all_sums, *masters, *[group[2] for group in news]),
        (*[shaped(item.shape, f32) for item in masters], shaped((2, LANES), f32)),
        time=3.2,
    )
    outputs = [layer_out, input_grad]
    for index, (weight, (first_new, second_new, unused)) in enumerate(zip(weights, news)):
        if index == 4:
            outputs += [weight, first_new, second_new[0], second_new[1]]
        else:
            kept_shape = ssm_param.shape if index == 5 else weight.shape
            outputs += [item.reshape(kept_shape) for item in (weight, first_new, second_new)]
    outputs.append(norms[:, :10])
    return tuple(outputs)


def solution(mesh):
    seq_count, model_count = mesh.shape["seq"], mesh.shape["mp"]
    halves = 2 if HEADS // model_count >= 2 else 1
    sizes = (seq_count // halves, halves, SEQS, halves, model_count // (SEQS * halves))
    fine = Mesh(mesh.devices.reshape(sizes), ALL)
    seq, model = ("sh", "sl"), ("mb", "mq", "ml")
    rows_cols, cols_rows = P(seq, model), P(model, seq)
    token = P(None, seq, None)
    stack = P(None, seq, model)
    gains = P(None, ALL)
    ssm = P(None, None, ALL)
    return jax.shard_map(
        on_device,
        mesh=fine,
        in_specs=(token, token, stack, cols_rows, rows_cols, cols_rows, gains, ssm)
        + (stack,) * 2
        + (cols_rows,) * 2
        + (rows_cols,) * 2
        + (cols_rows,) * 2
        + (gains,) * 2
        + (ssm,) * 2,
        out_specs=(token, token)
        + (stack,) * 3
        + (cols_rows,) * 3
        + (rows_cols,) * 3
        + (cols_rows,) * 3
        + (gains, gains, P(ALL), P(ALL))
        + (ssm,) * 3
        + (P(),),
        check_vma=False,
    )
```

```python
import functools
import math

import jax
import jax.numpy as jnp
from jax import lax
from jax.experimental import pallas as pl
from jax.experimental.pallas import tpu as pltpu
from jax.sharding import Mesh
from jax.sharding import PartitionSpec as P

HD = 128
HEADS = 8
BLK = 512
STEP = 10
SEQS = 2
LANES = 128
SUBS = 8
GROUP = 8

norm_eps = 1e-05
beta_first = 0.9
beta_second = 0.999
lamb_eps = 1e-06
weight_decay = 0.01
learn_rate = 0.5
score_scale = HD ** (-0.5)

f32 = jnp.float32
bf16 = jnp.bfloat16
VMEM_BYTES = 56 * 1024 * 1024

ALL = ("sh", "sl", "mb", "mq", "ml")
MODEL = ("mb", "mq", "ml")
COLS = ("mb", "mq")
TEAM = ("sl", "ml")


def dot(left, right):
    return lax.dot_general(left, right, (((1,), (0,)), ((), ())), preferred_element_type=f32)


def dot_t(left, right):
    return lax.dot_general(left, right, (((1,), (1,)), ((), ())), preferred_element_type=f32)


def normalise(values):
    centred = values - jnp.mean(values, axis=-1, keepdims=True)
    inverse = lax.rsqrt(jnp.mean(centred * centred, axis=-1, keepdims=True) + norm_eps)
    return centred * inverse, inverse


def normalise_back(unit, inverse, grad_unit):
    mean_one = jnp.mean(grad_unit, axis=-1, keepdims=True)
    mean_two = jnp.mean(grad_unit * unit, axis=-1, keepdims=True)
    return inverse * (grad_unit - mean_one - unit * mean_two)


def sub_index():
    return lax.broadcasted_iota(jnp.int32, (SUBS, LANES), 0)


def spread(row):
    return jnp.broadcast_to(row, (SUBS, LANES))


def lane_tile(index):
    return slice(index * LANES, (index + 1) * LANES)


def no_state(tiles):
    rows = tiles[0, :SUBS, :]
    return rows - rows


def in_steps(steps, tile, rows):
    span = rows.shape[0] // SUBS

    def move(i, unused):
        steps[tile, pl.ds(pl.multiple_of(i * SUBS, SUBS), SUBS), :] = rows[
            pl.ds(i, SUBS, stride=span), :
        ]
        return unused

    lax.fori_loop(0, span, move, 0, unroll=8)


def from_steps(rows, steps, tile):
    span = rows.shape[0] // SUBS

    def move(i, unused):
        rows[pl.ds(i, SUBS, stride=span), :] = steps[
            tile, pl.ds(pl.multiple_of(i * SUBS, SUBS), SUBS), :
        ]
        return unused

    lax.fori_loop(0, span, move, 0, unroll=8)


def step_rows(i):
    return pl.ds(pl.multiple_of(i * SUBS, SUBS), SUBS)


def norm_kernel(
    place, x_ref, gain_ref, logr_ref, normed_ref, turned_ref, u_tiles, ends_ref, total_ref, rows
):
    unit, unused = normalise(x_ref[...].astype(f32))
    normed_ref[...] = (unit * gain_ref[...]).astype(bf16)
    turned_ref[...] = normed_ref[...].T
    tiles, length, unused = u_tiles.shape
    states = logr_ref.shape[0]
    span = length // SUBS
    for tile in range(tiles):
        start = place[0] * (tiles * LANES) + tile * LANES
        rows[...] = normed_ref[:, pl.ds(pl.multiple_of(start, LANES), LANES)].astype(f32)
        in_steps(u_tiles, tile, rows)
    left = ((SUBS - 1 - sub_index()) * span).astype(f32)
    for tile in range(tiles):
        rate = jnp.exp(logr_ref[:, lane_tile(tile)])
        decay = jnp.exp(-rate)
        decays = [spread(decay[n : n + 1]) for n in range(states)]

        def step(i, held):
            u = u_tiles[tile, step_rows(i), :]
            return tuple(d * h + u for d, h in zip(decays, held))

        zero = no_state(u_tiles)
        held = lax.fori_loop(0, span, step, (zero,) * states, unroll=4)
        for n in range(states):
            ends_ref[n, :, lane_tile(tile)] = held[n]
            total_ref[n : n + 1, lane_tile(tile)] = jnp.sum(
                held[n] * jnp.exp(-left * rate[n : n + 1]), axis=0, keepdims=True
            )


def context_kernel(
    place, u_tiles, ends_ref, all_ref, logr_ref, coef_ref, context_ref, y_tiles, rows
):
    tiles, length, unused = u_tiles.shape
    states = logr_ref.shape[0]
    span = length // SUBS
    index = sub_index()
    before = (index * span).astype(f32)
    for tile in range(tiles):
        rate = jnp.exp(logr_ref[:, lane_tile(tile)])
        decay = jnp.exp(-rate)
        scale = coef_ref[:, lane_tile(tile)] * jnp.sqrt(2.0 * rate)
        incoming = jnp.zeros((states, LANES), f32)
        for j in range(all_ref.shape[0]):
            gap = place[1] - 1 - j
            distance = (jnp.maximum(gap, 0) * length).astype(f32)
            term = jnp.exp(-distance * rate) * all_ref[j, :, lane_tile(tile)].astype(f32)
            incoming = incoming + jnp.where(gap >= 0, term, 0.0)
        for first in range(0, states, GROUP):
            chosen = range(first, first + GROUP)
            starts = []
            for n in chosen:
                row = rate[n : n + 1]
                run = ends_ref[n, :, lane_tile(tile)]
                for d in (1, 2, 4):
                    moved = jnp.exp(-(d * span) * row) * pltpu.roll(run, d, 0)
                    run = run + jnp.where(index >= d, moved, 0.0)
                run = jnp.where(index >= 1, pltpu.roll(run, 1, 0), 0.0)
                starts.append(run + jnp.exp(-before * row) * incoming[n : n + 1])
            decays = [spread(decay[n : n + 1]) for n in chosen]
            scales = [spread(scale[n : n + 1]) for n in chosen]

            def step(i, held):
                at = step_rows(i)
                u = u_tiles[tile, at, :]
                held = tuple(d * h + u for d, h in zip(decays, held))
                parts = [s * h for s, h in zip(scales, held)]
                if first > 0:
                    parts[0] = parts[0] + y_tiles[tile, at, :]
                while len(parts) > 1:
                    parts = [a + b for a, b in zip(parts[::2], parts[1::2])]
                y_tiles[tile, at, :] = parts[0]
                return held

            lax.fori_loop(0, span, step, tuple(starts), unroll=4)
        from_steps(rows, y_tiles, tile)
        context_ref[:, lane_tile(tile)] = rows[...].astype(bf16)


def whole_rows(block):
    return block.reshape(block.shape[0] * block.shape[1], block.shape[2])


def head(index):
    return slice(index * HD, (index + 1) * HD)


def weight_copies(near, far, buffer, place, sems, act):
    count = sems.shape[0]
    half = count // 2
    for k in range(count):
        owner = lax.rem(place[6] + count - k, count)
        for stacks, low in ((near, 0), (far, half)):

            @pl.when((owner >= low) & (owner < low + half))
            def move():
                for r, stack in enumerate(stacks):
                    inner = buffer.at[k, place[2] ^ r]
                    act(pltpu.make_async_copy(stack.at[owner - low], inner, sems.at[k, r]))


def of_heads(buffer, i):
    return jnp.concatenate([whole_rows(buffer[k, :, :, head(i)]) for k in range(buffer.shape[0])], axis=1)


def gradient_slot(row_parts, order, r):
    position = 0
    for bit in reversed(order):
        position = 2 * position + (1 if r & bit else 0)
    return position // (row_parts // 2), position % (row_parts // 2)


def round_orders(row_parts):
    bits = [1 << i for i in range(row_parts.bit_length() - 1)]
    return bits, bits[::-1]


def gradient_pieces(stacks, row_parts, far, slot):
    found = []
    for r in range(row_parts):
        sent, at = gradient_slot(row_parts, round_orders(row_parts)[far], r)
        found.append(stacks[2 * far + sent].at[at, slot])
    return found


def project_kernel(team, col_parts, row_parts, place, normed_ref, cot_ref, *refs):
    contexts, refs = refs[:team], refs[team:]
    near, far, refs = refs[:row_parts], refs[row_parts : 2 * row_parts], refs[2 * row_parts :]
    context_t_ref, cot_t_ref, kept_ref = refs[:3]
    context_ref, weights, sems = refs[3:]
    weight_copies(near, far, weights, place, sems, lambda copy: copy.start())
    width = contexts[0].shape[1]
    for k in range(team):
        lanes = pl.ds(pl.multiple_of((place[0] ^ k) * width, LANES), width)
        context_ref[:, lanes] = contexts[k][...]
    context_t_ref[...] = context_ref[...].T
    cot_t_ref[...] = cot_ref[...].T
    weight_copies(near, far, weights, place, sems, lambda copy: copy.wait())
    kept_ref[0] = dot(normed_ref[...], of_heads(weights, 0)).astype(bf16)
    kept_ref[1] = dot(context_ref[...], of_heads(weights, 1)).astype(bf16)
    kept_ref[2] = dot(context_ref[...], of_heads(weights, 2)).astype(bf16)


def attend_kernel(team, col_parts, row_parts, place, kept_ref, *refs):
    near, far, refs = refs[:row_parts], refs[row_parts : 2 * row_parts], refs[2 * row_parts :]
    part_ref, attended_ref, probs_ref, probs_t_ref, weights, sems = refs
    weight_copies(near, far, weights, place, sems, lambda copy: copy.start())
    length = kept_ref.shape[1]
    rows = lax.broadcasted_iota(jnp.int32, (length, length), 0)
    cols = lax.broadcasted_iota(jnp.int32, (length, length), 1)
    for h in range(col_parts):
        scores = dot_t(kept_ref[0, :, head(h)], kept_ref[1, :, head(h)]) * score_scale
        scores = jnp.where(rows >= cols, scores, -1e30)
        shifted = jnp.exp(scores - jnp.max(scores, axis=-1, keepdims=True))
        inverse = 1.0 / jnp.sum(shifted, axis=-1, keepdims=True)
        probs = (shifted * inverse).astype(bf16)
        probs_ref[h] = probs
        probs_t_ref[h] = probs.T
        attended_ref[:, head(h)] = dot(probs, kept_ref[2, :, head(h)]).astype(bf16)
    weight_copies(near, far, weights, place, sems, lambda copy: copy.wait())
    part_ref[...] = dot_t(attended_ref[...], of_heads(weights, 3)).astype(bf16)


def gelu_parts(hidden, grad_act):
    density = jnp.exp(-0.5 * hidden * hidden)
    t = 1.0 / (1.0 + (0.3275911 * math.sqrt(0.5)) * jnp.abs(hidden))
    series = 0.5 * 1.061405429
    for factor in (-1.453152027, 1.421413741, -0.284496736, 0.254829592):
        series = series * t + 0.5 * factor
    tail = series * t * density
    cdf = jnp.where(hidden >= 0.0, 1.0 - tail, tail)
    slope = cdf + hidden * density * (1.0 / math.sqrt(2.0 * math.pi))
    return (hidden * cdf).astype(bf16), (grad_act * slope).astype(bf16)


def middle_kernel(team, x_ref, gain_ref, *refs):
    parts, (middle_ref, normed_ref, normed_t_ref) = refs[:team], refs[team:]
    attn = parts[0][...].astype(f32)
    for part in parts[1:]:
        attn = attn + part[...].astype(f32)
    middle = x_ref[...].astype(f32) + attn
    middle_ref[...] = middle
    unit, unused = normalise(middle)
    normed_ref[...] = (unit * gain_ref[...]).astype(bf16)
    normed_t_ref[...] = normed_ref[...].T


def feed_kernel(team, col_parts, row_parts, place, normed_ref, normed_t_ref, cot_ref, cot_t_ref, *refs):
    count = col_parts * row_parts
    pieces, refs = refs[:count], refs[count:]
    outs, two_ref, refs = refs[:team], refs[team], refs[team + 1 :]
    stacks, refs = (refs[:4], refs[4:8]), refs[8:]
    up_all, down_all, grad_up, grad_down, activated_all, grad_all, sems = refs
    z = pl.program_id(0)
    half = col_parts // 2
    hidden_cols = grad_up.shape[3]

    def copies(k):
        found = []
        for r in range(row_parts):
            for which, buffer in enumerate((up_all, down_all)):
                outside = pieces[k * row_parts + r].at[:, pl.ds(which * hidden_cols, hidden_cols)]
                inside = buffer.at[place[2] ^ r, :, pl.ds(k * hidden_cols, hidden_cols)]
                found.append(pltpu.make_async_copy(outside, inside, sems.at[which, k, r]))
        return found

    def each_leaving(k, act):
        for which, buffer in enumerate((grad_up, grad_down)):
            for r, piece in enumerate(gradient_pieces(stacks[which], row_parts, k // half, k % half)):
                inner = buffer.at[k, place[2] ^ r]
                act(pltpu.make_async_copy(inner, piece, sems.at[2 + which, k, r]))

    @pl.when(z == 0)
    def start():
        for k in range(col_parts):
            for copy in copies(k):
                copy.start()

    for k in range(col_parts):

        @pl.when(z == k)
        def arrive():
            for copy in copies(k):
                copy.wait()

    at = pl.ds(pl.multiple_of(z * hidden_cols, hidden_cols), hidden_cols)
    hidden = dot(normed_ref[...], whole_rows(up_all[:, :, at]))
    grad_act = dot(cot_ref[...], whole_rows(down_all[:, :, at]))
    activated, grad_pre = gelu_parts(hidden, grad_act)
    activated_all[:, at] = activated
    grad_all[:, at] = grad_pre
    shape = grad_up.shape[1:]
    grad_up[z] = dot(normed_t_ref[...], grad_pre).astype(bf16).reshape(shape)
    grad_down[z] = dot(cot_t_ref[...], activated).astype(bf16).reshape(shape)

    for k in range(col_parts):

        @pl.when(z == k)
        def leave():
            each_leaving(k, lambda copy: copy.start())

    @pl.when(z == col_parts - 1)
    def finish():
        two_ref[...] = dot_t(grad_all[...], whole_rows(up_all[...])).astype(bf16)
        rows = outs[0].shape[0]
        for k in range(team):
            at_rows = pl.ds(pl.multiple_of((place[0] ^ k) * rows, rows), rows)
            outs[k][...] = dot_t(activated_all[at_rows, :], whole_rows(down_all[...])).astype(bf16)
        for k in range(col_parts):
            each_leaving(k, lambda copy: copy.wait())


def attend_back_kernel(team, col_parts, row_parts, place, middle_ref, gain_ref, cot_ref, *refs):
    parts, refs = refs[:team], refs[team:]
    late, refs = refs[:3], refs[3:]
    near, far, refs = refs[:row_parts], refs[row_parts : 2 * row_parts], refs[2 * row_parts :]
    middle_grad_ref, gain_grad_ref, one_ref, low = refs[:4]
    grad_q, grad_k, grad_v = refs[4:7]
    context_grads, refs = refs[7 : 7 + team], refs[7 + team :]
    weights, grad_out, total_low = refs[:3]
    held, (sems, late_sems) = refs[3:6], refs[6:]
    kept_ref, probs_ref, probs_t_ref = held
    weight_copies(near, far, weights, place, sems, lambda copy: copy.start())
    late_copies = [
        pltpu.make_async_copy(outside, inside, late_sems.at[i])
        for i, (outside, inside) in enumerate(zip(late, held))
    ]
    for copy in late_copies:
        copy.start()
    own_rows = middle_ref.shape[0] // team
    grad_two = parts[0][...].astype(f32)
    for part in parts[1:]:
        grad_two = grad_two + part[...].astype(f32)
    unit, inverse = normalise(middle_ref[...])
    grad_gain = grad_two * unit
    rows = lax.broadcasted_iota(jnp.int32, grad_gain.shape, 0)
    first = place[0] * own_rows
    mine = (rows >= first) & (rows < first + own_rows)
    gain_grad_ref[...] = jnp.sum(jnp.where(mine, grad_gain, 0.0), axis=0, keepdims=True)
    grad = cot_ref[...].astype(f32) + normalise_back(unit, inverse, grad_two * gain_ref[...])
    low[...] = grad.astype(bf16)
    for k in range(team):

        @pl.when(place[0] == k)
        def own():
            middle_grad_ref[...] = grad[k * own_rows : (k + 1) * own_rows, :]

    weight_copies(near, far, weights, place, sems, lambda copy: copy.wait())
    for copy in late_copies:
        copy.wait()
    grad_out[...] = dot(low[...], of_heads(weights, 3)).astype(bf16)
    for h in range(col_parts):
        q, k, v = (kept_ref[i, :, head(h)] for i in range(3))
        grad_heads = grad_out[:, head(h)]
        grad_v[:, head(h)] = dot(probs_t_ref[h], grad_heads).astype(bf16)
        probs = probs_ref[h].astype(f32)
        grad_probs = dot_t(grad_heads, v)
        inner = jnp.sum(grad_probs * probs, axis=-1, keepdims=True)
        grad_scores = (probs * (grad_probs - inner)).astype(bf16)
        grad_q[:, head(h)] = (dot(grad_scores, k) * score_scale).astype(bf16)
        turned = dot_t(v, grad_heads) - inner.T
        turned = (probs_t_ref[h].astype(f32) * turned).astype(bf16)
        grad_k[:, head(h)] = (dot(turned, q) * score_scale).astype(bf16)
    total = dot_t(grad_k[...], of_heads(weights, 1)) + dot_t(grad_v[...], of_heads(weights, 2))
    total_low[...] = total.astype(bf16)
    width = context_grads[0].shape[1]
    for k in range(team):
        lanes = pl.ds(pl.multiple_of((place[0] ^ k) * width, LANES), width)
        context_grads[k][...] = total_low[:, lanes]
    one_ref[...] = dot_t(grad_q[...], of_heads(weights, 0)).astype(bf16)


def head_grads_kernel(col_parts, row_parts, place, low, attended_ref, *refs):
    normed_t_ref, context_t_ref, grad_q, grad_k, grad_v = refs[:5]
    stacks, (grads, out_sems) = refs[5:9], refs[9:]
    half = col_parts // 2
    shape = (*grads.shape[1:3], HD)

    def put(i, grad):
        for h in range(col_parts):
            grads[h, :, :, head(i)] = grad[:, head(h)].astype(bf16).reshape(shape)

    put(0, dot(normed_t_ref[...], grad_q[...]))
    put(1, dot(context_t_ref[...], grad_k[...]))
    put(2, dot(context_t_ref[...], grad_v[...]))
    put(3, dot(low[...].T, attended_ref[...]))
    copies = []
    for k in range(col_parts):
        for r, piece in enumerate(gradient_pieces(stacks, row_parts, k // half, k % half)):
            copies.append(pltpu.make_async_copy(grads.at[k, place[2] ^ r], piece, out_sems.at[k, r]))
    for copy in copies:
        copy.start()
    for copy in copies:
        copy.wait()


def adjoint_kernel(team, logr_ref, *refs):
    parts = refs[:team]
    g_tiles, ends_ref, total_ref, rows = refs[team:]
    grad = parts[0][...].astype(f32)
    for part in parts[1:]:
        grad = grad + part[...].astype(f32)
    grad = grad.astype(bf16).astype(f32)
    tiles, length, unused = g_tiles.shape
    states = logr_ref.shape[0]
    span = length // SUBS
    for tile in range(tiles):
        rows[...] = grad[:, lane_tile(tile)]
        in_steps(g_tiles, tile, rows)
    before = (sub_index() * span).astype(f32)
    for tile in range(tiles):
        rate = jnp.exp(logr_ref[:, lane_tile(tile)])
        decay = jnp.exp(-rate)
        for first in range(0, states, GROUP):
            chosen = range(first, first + GROUP)
            decays = [spread(decay[n : n + 1]) for n in chosen]

            def step(i, held):
                g = g_tiles[tile, step_rows(span - 1 - i), :]
                later = []
                for d, (b, w) in zip(decays, held):
                    shrunk = d * b
                    later.append((g + shrunk, d * w + shrunk))
                return tuple(later)

            zero = no_state(g_tiles)
            held = lax.fori_loop(0, span, step, ((zero, zero),) * GROUP, unroll=4)
            for n, (b, w) in zip(chosen, held):
                ends_ref[0, n, :, lane_tile(tile)] = b
                ends_ref[1, n, :, lane_tile(tile)] = w
                shrink = jnp.exp(-before * rate[n : n + 1])
                total_ref[0, n : n + 1, lane_tile(tile)] = jnp.sum(
                    shrink * b, axis=0, keepdims=True
                )
                total_ref[1, n : n + 1, lane_tile(tile)] = jnp.sum(
                    shrink * (w + before * b), axis=0, keepdims=True
                )


def context_back_kernel(
    team, place, g_tiles, u_tiles, ends_ref, all_ref, logr_ref, coef_ref, one_ref, *refs
):
    pieces = refs[:team]
    grad_ssm_ref, y_tiles, full, rows = refs[team:]
    tiles, length, unused = u_tiles.shape
    states = logr_ref.shape[0]
    span = length // SUBS
    width = tiles * LANES
    index = sub_index()
    after = ((SUBS - 1 - index) * span).astype(f32)
    full[...] = one_ref[...].astype(f32)
    group = GROUP
    for tile in range(tiles):
        lanes = lane_tile(tile)
        rate = jnp.exp(logr_ref[:, lanes])
        decay = jnp.exp(-rate)
        root = jnp.sqrt(2.0 * rate)
        scale = coef_ref[:, lanes] * root
        in_b = jnp.zeros((states, LANES), f32)
        in_w = jnp.zeros((states, LANES), f32)
        for j in range(all_ref.shape[0]):
            gap = j - place[1] - 1
            distance = (jnp.maximum(gap, 0) * length).astype(f32)
            shrink = jnp.exp(-distance * rate)
            b, w = all_ref[j, 0, :, lanes].astype(f32), all_ref[j, 1, :, lanes].astype(f32)
            in_b = in_b + jnp.where(gap >= 0, shrink * b, 0.0)
            in_w = in_w + jnp.where(gap >= 0, shrink * (w + distance * b), 0.0)
        for first in range(0, states, group):
            chosen = range(first, first + group)
            starts = []
            for n in chosen:
                row = rate[n : n + 1]
                b, w = ends_ref[0, n, :, lanes], ends_ref[1, n, :, lanes]
                for d in (1, 2, 4):
                    shrink = jnp.exp(-(d * span) * row)
                    next_b = pltpu.roll(b, SUBS - d, 0)
                    next_w = pltpu.roll(w, SUBS - d, 0)
                    inside = index < SUBS - d
                    b, w = (
                        b + jnp.where(inside, shrink * next_b, 0.0),
                        w + jnp.where(inside, shrink * (next_w + (d * span) * next_b), 0.0),
                    )
                inside = index < SUBS - 1
                b = jnp.where(inside, pltpu.roll(b, SUBS - 1, 0), 0.0)
                w = jnp.where(inside, pltpu.roll(w, SUBS - 1, 0), 0.0)
                shrink = jnp.exp(-after * row)
                b_row, w_row = in_b[n : n + 1], in_w[n : n + 1]
                b = b + shrink * b_row
                w = w + shrink * (w_row + after * b_row)
                zero = no_state(u_tiles)
                starts.append((b, w, zero, zero))
            decays = [spread(decay[n : n + 1]) for n in chosen]
            scales = [spread(scale[n : n + 1]) for n in chosen]

            def step(i, held):
                at = step_rows(span - 1 - i)
                g = g_tiles[tile, at, :]
                u = u_tiles[tile, at, :]
                later, parts = [], []
                for d, s, (b, w, sum_b, sum_w) in zip(decays, scales, held):
                    shrunk = d * b
                    w = d * w + shrunk
                    b = g + shrunk
                    later.append((b, w, sum_b + u * b, sum_w + u * w))
                    parts.append(s * b)
                while len(parts) > 1:
                    parts = [p + q for p, q in zip(parts[::2], parts[1::2])]
                if first > 0:
                    parts[0] = parts[0] + y_tiles[tile, at, :]
                y_tiles[tile, at, :] = parts[0]
                return tuple(later)

            held = lax.fori_loop(0, span, step, tuple(starts), unroll=2)
            for n, (unused_b, unused_w, sum_b, sum_w) in zip(chosen, held):
                sum_b = jnp.sum(sum_b, axis=0, keepdims=True)
                sum_w = jnp.sum(sum_w, axis=0, keepdims=True)
                row = slice(n, n + 1)
                grad_ssm_ref[0, row, lanes] = root[row] * sum_b
                grad_ssm_ref[1, row, lanes] = scale[row] * (0.5 * sum_b - rate[row] * sum_w)
        at_lanes = pl.ds(pl.multiple_of(place[0] * width + tile * LANES, LANES), LANES)
        from_steps(rows, y_tiles, tile)
        full[:, at_lanes] += rows[...].astype(bf16).astype(f32)
    count = pieces[0].shape[0]
    for k in range(team):
        at_rows = pl.ds(pl.multiple_of((place[0] ^ k) * count, count), count)
        pieces[k][...] = full[at_rows, :].astype(bf16)


def input_grad_kernel(team, place, x_ref, gain_ref, middle_grad_ref, *refs):
    parts, (out_ref, gain_grad_ref) = refs[:team], refs[team:]
    rows = out_ref.shape[0]
    at_rows = pl.ds(pl.multiple_of(place[0] * rows, rows), rows)
    grad_one = parts[0][...].astype(f32)
    for part in parts[1:]:
        grad_one = grad_one + part[...].astype(f32)
    unit, inverse = normalise(x_ref[at_rows, :].astype(f32))
    gain_grad_ref[...] = jnp.sum(grad_one * unit, axis=0, keepdims=True)
    back = normalise_back(unit, inverse, grad_one * gain_ref[...])
    out_ref[...] = (middle_grad_ref[...] + back).astype(bf16)


def assemble_kernel(halves, low_count, place, own_ref, *refs):
    others, out_ref = refs[:-1], refs[-1]
    count, rows, unused = own_ref.shape
    half = place[4]

    def put(value, sequence, which, member):
        at_rows = pl.ds(pl.multiple_of((which * low_count + member) * rows, rows), rows)
        out_ref[sequence, at_rows, :] = value.astype(out_ref.dtype)

    for sequence in range(count // (halves * low_count)):
        if halves == 1:
            for member in range(low_count):
                put(own_ref[sequence * low_count + member], sequence, 0, member)
        else:
            put(own_ref[sequence * halves + half], sequence, half, 0)
            put(others[0][sequence], sequence, 1 - half, 0)


def pack_kernel(halves, place, qkv_ref, out_ref, up_ref, down_ref, *refs):
    rows = up_ref.shape[0]
    heads, hidden = out_ref.shape[0] // halves, up_ref.shape[1] // halves
    for which in range(halves):
        side = place[4] if which == 0 else 1 - place[4]
        at_heads = pl.ds(pl.multiple_of(side * heads, LANES), heads)
        at_hidden = pl.ds(pl.multiple_of(side * hidden, LANES), hidden)
        if which == 0:
            head_ref = refs[0]
            wide_ref, deep_ref = refs[1].at[:, :hidden], refs[1].at[:, hidden:]
        else:
            packed = refs[2]
            head_ref = packed.at[:, : 4 * heads]
            wide_ref = packed.at[:, 4 * heads : 4 * heads + hidden]
            deep_ref = packed.at[:, 4 * heads + hidden :]
        for i in range(3):
            head_ref[:, i * heads : (i + 1) * heads] = qkv_ref[i, :, at_heads].astype(bf16)
        head_ref[:, 3 * heads :] = out_ref[at_heads, :].T.astype(bf16)
        wide_ref[...] = up_ref[:, at_hidden].astype(bf16)
        deep_ref[...] = down_ref[at_hidden, :].T.astype(bf16)


def small_kernel(ssm_ref, gains_ref, out_ref):
    count = ssm_ref.shape[0]
    out_ref[:count, :] = ssm_ref[...]
    out_ref[count:, :] = gains_ref[...]


def lamb_moments(weight, grad_item, first_old, second_old):
    first_new = beta_first * first_old + (1.0 - beta_first) * grad_item
    second_new = beta_second * second_old + (1.0 - beta_second) * grad_item * grad_item
    direction = (
        first_new
        / (1.0 - beta_first**STEP)
        / (jnp.sqrt(second_new / (1.0 - beta_second**STEP)) + lamb_eps)
        + weight_decay * weight
    )
    return (first_new, second_new, direction)


def place_sums(sums_ref, sums):
    rows = lax.broadcasted_iota(jnp.int32, sums_ref.shape, 0)
    lanes = lax.broadcasted_iota(jnp.int32, sums_ref.shape, 1)
    found = jnp.zeros(sums_ref.shape, f32)
    for index, pair in sums.items():
        for row, value in enumerate(pair):
            found = jnp.where((rows == row) & (lanes == index), value, found)
    sums_ref[...] = found


def moments_kernel(halves, matrices, place, *refs):
    count = 1 + max(item[1] for item in matrices)
    grads, refs = [refs[halves * i : halves * (i + 1)] for i in range(count)], refs[halves * count :]
    arrays = len({(item[1], item[4] is None) for item in matrices})
    ins = [refs[3 * i : 3 * i + 3] for i in range(arrays)]
    outs = [refs[3 * (arrays + i) : 3 * (arrays + i) + 3] for i in range(arrays)]
    sums_ref = refs[6 * arrays]
    keys = []
    sums = {}
    for number, source, column, turned, stacked in matrices:
        key = (source, stacked is None)
        if key not in keys:
            keys.append(key)
        pick = (lambda ref: ref) if stacked is None else (lambda ref, i=stacked: ref.at[i])
        weight, first, second = (pick(ref) for ref in ins[keys.index(key)])
        news = [pick(ref) for ref in outs[keys.index(key)]]
        width = weight.shape[0 if turned else 1] // halves
        rows = weight.shape[1 if turned else 0]
        cols = slice(column * width, (column + 1) * width)
        total_weight = total_update = 0.0
        for which, grad_ref in enumerate(grads[source]):
            side = place[4] if which == 0 else 1 - place[4]
            at = pl.ds(pl.multiple_of(side * width, width), width)
            if which == 0:
                grad = grad_ref[pl.ds(pl.multiple_of(side * rows, rows), rows), cols].astype(f32)
            else:
                grad = grad_ref[:, cols].astype(f32)
            at = (at, slice(None)) if turned else (slice(None), at)
            grad = grad.T if turned else grad
            old = weight[at]
            found = lamb_moments(old, grad, first[at], second[at])
            for ref, value in zip(news, found):
                ref[at] = value
            total_weight = total_weight + jnp.sum(old * old)
            total_update = total_update + jnp.sum(found[2] * found[2])
        sums[number] = (total_weight, total_update)
    place_sums(sums_ref, sums)


def small_moments_kernel(numbers, grads_ref, *refs):
    ins, outs, sums_ref = (refs[:3], refs[3:6]), (refs[6:9], refs[9:12]), refs[12]
    states = (grads_ref.shape[0] - 2) // 2
    sums = {}
    for (weight, first, second), news, start, rows, first_number in (
        (ins[0], outs[0], 2 * states, 1, numbers[0]),
        (ins[1], outs[1], 0, states, numbers[1]),
    ):
        for i in range(2):
            grad = grads_ref[start + i * rows : start + (i + 1) * rows, :]
            at = slice(i * rows, (i + 1) * rows)
            found = lamb_moments(weight[at, :], grad, first[at, :], second[at, :])
            for ref, value in zip(news, found):
                ref[at, :] = value
            sums[first_number + i] = (
                jnp.sum(weight[at, :] * weight[at, :]),
                jnp.sum(found[2] * found[2]),
            )
    place_sums(sums_ref, sums)


def update_kernel(stacks, sums_ref, *refs):
    count = len(stacks)
    weights, directions, news = refs[:count], refs[count : 2 * count], refs[2 * count : 3 * count]
    norms = jnp.sqrt(jnp.sum(sums_ref[...], axis=0))
    refs[3 * count][...] = norms
    ratios = norms[0:1] / norms[1:2]
    lanes = lax.broadcasted_iota(jnp.int32, ratios.shape, 1)
    for numbers, weight, direction, new in zip(stacks, weights, directions, news):
        step = weight.shape[0] // len(numbers)
        for i, number in enumerate(numbers):
            ratio = jnp.sum(jnp.where(lanes == number, ratios, 0.0), axis=1, keepdims=True)
            at = slice(i * step, (i + 1) * step)
            scale = learn_rate * ratio.reshape((1,) * weight.ndim)
            new[at] = weight[at] - scale * direction[at]


def call(
    body, ins, outs, scratch=(), grid=None, in_specs=None, out_specs=None, time=1.0, after=(), token=False
):
    moved = sum(a.size * a.dtype.itemsize for a in list(ins) + list(outs))
    params = pltpu.CompilerParams(vmem_limit_bytes=VMEM_BYTES)
    cost = pl.CostEstimate(flops=int(time * 1.15e9), bytes_accessed=moved, transcendentals=0)
    whole = pl.BlockSpec(memory_space=pltpu.VMEM)
    anywhere = pl.BlockSpec(memory_space=pl.ANY)
    in_specs = list(in_specs or [whole] * len(ins)) + [anywhere] * len(after)
    out_specs = list(out_specs or [whole] * len(outs))
    outs = list(outs)
    first_out = len(ins) + len(after)
    last_out = first_out + len(outs)
    if token:
        outs.append(jax.ShapeDtypeStruct((SUBS, LANES), f32))
        out_specs.append(whole)

    def run(*refs):
        refs = list(refs)
        if token:
            refs[last_out][...] = jnp.zeros((SUBS, LANES), f32)
            del refs[last_out]
        body(*refs[: len(ins)], *refs[first_out:])

    return pl.pallas_call(
        run,
        out_shape=tuple(outs),
        in_specs=in_specs,
        out_specs=tuple(out_specs),
        scratch_shapes=list(scratch),
        compiler_params=params,
        cost_estimate=cost,
        **({} if grid is None else {"grid": grid}),
    )(*ins, *after)


def shaped(shape, kind):
    return jax.ShapeDtypeStruct(tuple(shape), kind)


def on_device(
    tokens,
    cotangent,
    w_qkv,
    w_out,
    w_up,
    w_down,
    norm_gains,
    ssm_param,
    first_qkv,
    second_qkv,
    first_out,
    second_out,
    first_up,
    second_up,
    first_down,
    second_down,
    first_gain,
    second_gain,
    first_ssm,
    second_ssm,
):
    halves = lax.axis_size("sl")
    low_count = lax.axis_size("ml")
    row_parts = lax.axis_size("sh")
    col_parts = lax.axis_size("mb") * lax.axis_size("mq")
    team = halves * low_count
    sl, ml, mb, mq = (lax.axis_index(name) for name in ("sl", "ml", "mb", "mq"))
    rank = sl * low_count + ml
    block_index = lax.axis_index("sh") * halves + mq
    seq_total, length, width = tokens.shape
    assert length == BLK and seq_total == lax.axis_size("mb")
    states = ssm_param.shape[1]
    channels = width // team
    tiles = channels // LANES
    row_count = width // row_parts
    own_rows = length // team
    place = [rank, block_index, lax.axis_index("sh"), lax.axis_index(MODEL), sl, sl ^ mq]
    place.append(lax.axis_index(COLS))
    place = jnp.stack(place).astype(jnp.int32)
    smem = pl.BlockSpec(memory_space=pltpu.SMEM)
    vmem = pl.BlockSpec(memory_space=pltpu.VMEM)

    def permute(value, axes, moves):
        return lax.ppermute(value, axes, moves)

    def swap(value):
        return permute(value, "sl", [(0, 1), (1, 0)])

    def in_order(own, other, axis):
        return jnp.where(
            sl == 0, jnp.concatenate([own, other], axis), jnp.concatenate([other, own], axis)
        )

    def team_send(pieces):
        moved = [pieces[0]]
        for k in range(1, team):
            moved.append(permute(pieces[k], TEAM, [(i, i ^ k) for i in range(team)]))
        return moved

    def pick_block(array):
        own = lax.dynamic_index_in_dim(array, mb, 0, keepdims=False)
        if halves == 1:
            return own, ()
        other = swap(own)
        return jnp.where(sl == mq, own, other), (other,)

    def across(value, bit):
        return permute(value, "sh", [(i, i ^ bit) for i in range(row_parts)])

    def along(value, axes, step):
        count = lax.axis_size(axes)
        return permute(value, axes, [(i, (i + step) % count) for i in range(count)])

    bits = [1 << i for i in range(row_parts.bit_length() - 1)]

    def bit_order(k):
        return bits if k % 2 == 0 else bits[::-1]

    def double_rows(value, order):
        found = {0: value}
        for bit in order:
            for r in list(found):
                found[r | bit] = across(found[r], bit)
        return [found[r] for r in range(row_parts)]

    def add(*items, zero=None):
        total = sum(item.astype(f32) for item in items)
        return (total if zero is None else total + zero[0, 0]).astype(bf16)

    def first_messages(stacks):
        return across(stacks[1], bits[-1]), across(stacks[3], bits[0])

    def second_messages(stacks, first, zero):
        count = first[0].shape[0] // 2
        return [add(stacks[2 * i][count:], first[i][count:], zero=zero) for i in range(2)]

    def halve_rows(keep, arrived, order, send, last, log):
        items = [keep, arrived]
        for bit in order[-2::-1]:
            count = arrived.shape[0] // 2
            if send is None:
                send = add(*[item[count:] for item in items])
            arrived = across(send, bit)
            log.append(arrived)
            items = [item[:count] for item in items] + [arrived]
            send = None
        return add(*[item[0] for item in items], zero=last)

    def halve_both(stacks, first, send, last=None, log=None):
        log = [] if log is None else log
        near = halve_rows(stacks[0], first[0], bits, send[0], last, log)
        return near, halve_rows(stacks[2], first[1], bits[::-1], send[1], last, log)

    def hold(arrays, after):
        anywhere = pl.BlockSpec(memory_space=pl.ANY)
        return pl.pallas_call(
            lambda *refs: None,
            out_shape=tuple(shaped(item.shape, item.dtype) for item in arrays),
            in_specs=[anywhere] * (len(arrays) + len(after)),
            out_specs=(anywhere,) * len(arrays),
            input_output_aliases={i: i for i in range(len(arrays))},
        )(*arrays, *after)

    def gather_pieces(shard):
        pieces = []
        for k in range(col_parts):
            held = along(held, COLS, 1) if k > 0 else shard
            pieces.append(double_rows(held, bits if k % 2 == 0 else bits[::-1]))
        return pieces

    def sum_over_z(near, far, ring=True):
        if not ring:
            pieces = [stack[k] for stack in (near, far) for k in range(col_parts // 2)]
            moved = [along(piece, COLS, -k) for k, piece in enumerate(pieces) if k > 0]
            return add(pieces[0], *moved)
        held = None
        for stack in (far, near):
            for k in reversed(range(stack.shape[0])):
                held = stack[k] if held is None else add(stack[k], along(held, COLS, -1))
        return held

    def everywhere(value, axes):
        count = lax.axis_size(axes)
        copies = jnp.broadcast_to(value[None], (count, *value.shape))
        return lax.all_to_all(copies, axes, 0, 0, tiled=True)

    rows_dev = w_up.shape[0]
    hidden_cols = w_up.shape[1] // halves
    head_cols = 4 * w_out.shape[0] // halves
    packed_cols = head_cols + 2 * hidden_cols
    sides = [shaped((rows_dev, cols), bf16) for cols in (head_cols, 2 * hidden_cols)]
    shards = call(
        functools.partial(pack_kernel, halves),
        (place, w_qkv, w_out, w_up, w_down),
        sides + [shaped((rows_dev, packed_cols), bf16)] * (halves - 1),
        time=2.4,
        in_specs=[smem] + [vmem] * 4,
    )
    if halves == 2:
        other = swap(shards[2])
        cuts = (0, head_cols, packed_cols)
        shards = [
            in_order(own, other[:, first:last], 0)
            for own, first, last in zip(shards, cuts, cuts[1:])
        ]
    head_shard, hidden_shard = shards[:2]
    attn_full = lax.all_gather(head_shard, COLS, axis=0, tiled=False)
    hidden_w = gather_pieces(hidden_shard)
    hidden_flat = [piece for group in hidden_w for piece in group]

    small, = call(
        small_kernel,
        (ssm_param.reshape(2 * states, -1), norm_gains),
        (shaped((2 * states + 2, norm_gains.shape[1]), f32),),
        after=hidden_w[0][1:-1],
    )
    small = jnp.transpose(everywhere(small, ALL), (1, 0, 2)).reshape(2 * states + 2, width)
    own_ssm = lax.dynamic_slice_in_dim(
        small[: 2 * states].reshape(2, states, width), rank * channels, channels, 2
    )
    coef, logr = own_ssm[0], own_ssm[1]
    gain_one = small[2 * states : 2 * states + 1]
    gain_two = small[2 * states + 1 : 2 * states + 2]

    x, unused = pick_block(tokens)
    cot, cot_other = pick_block(cotangent)

    anywhere = [pl.BlockSpec(memory_space=pl.ANY)]

    def fixed(*shape):
        return pl.BlockSpec(shape, lambda z: (0,) * len(shape))

    wide = fixed(length, width)
    row = fixed(1, width)

    normed_one, normed_t, u_steps, ends, total = call(
        norm_kernel,
        (place, x, gain_one, logr),
        (
            shaped((length, width), bf16),
            shaped((width, length), bf16),
            shaped((tiles, length, LANES), f32),
            shaped((states, SUBS, channels), f32),
            shaped((states, channels), f32),
        ),
        scratch=[pltpu.VMEM((length, LANES), f32)],
        in_specs=[smem, vmem, vmem, vmem],
        after=(hidden_w[1][0], *cot_other),
        time=5,
    )
    (attn_full,) = hold((attn_full,), (total,))
    attn_w = [
        *double_rows(attn_full[: col_parts // 2], bits),
        *double_rows(attn_full[col_parts // 2 :], bits[::-1]),
    ]
    totals = everywhere(total.astype(bf16), ("sh", "mq"))
    (context_own,) = call(
        context_kernel,
        (place, u_steps, ends, totals, logr, coef),
        (shaped((length, channels), bf16),),
        after=(hidden_w[0][-1], *hidden_w[1][1:-1], hidden_w[-1][0], *attn_w[1 : row_parts - 1]),
        scratch=[pltpu.VMEM((tiles, length, LANES), f32), pltpu.VMEM((length, LANES), f32)],
        in_specs=[smem] + [vmem] * 5,
        time=7,
    )
    contexts = team_send([context_own] * team)

    stack_shape = (row_parts // 2, col_parts // 2, row_count)
    head_stacks = [shaped((*stack_shape, head_cols), bf16)] * 4
    hidden_stacks = [shaped((*stack_shape, hidden_cols), bf16)] * 8
    sizes = (team, col_parts, row_parts)
    head_buffer = pltpu.VMEM((col_parts, row_parts, row_count, 4 * HD), bf16)
    head_sems = pltpu.SemaphoreType.DMA((col_parts, row_parts))
    kept_shape = shaped((3, length, col_parts * HD), bf16)
    flat_shape = shaped((length, col_parts * HD), bf16)
    context_t, cot_t, kept = call(
        functools.partial(project_kernel, *sizes),
        (place, normed_one, cot, *contexts, *attn_w),
        (shaped((width, length), bf16), shaped((width, length), bf16), kept_shape),
        scratch=[pltpu.VMEM((length, width), bf16), head_buffer, head_sems],
        time=1,
        in_specs=[smem] + [vmem] * (2 + team) + anywhere * len(attn_w),
        after=(hidden_w[1][-1], *[piece for group in hidden_w[2:3] for piece in group[1:]]),
    )
    attn_part, attended, probs, probs_t = call(
        functools.partial(attend_kernel, *sizes),
        (place, kept, *attn_w),
        (
            shaped((length, width), bf16),
            flat_shape,
            *[shaped((col_parts, length, length), bf16)] * 2,
        ),
        scratch=[head_buffer, head_sems],
        time=1,
        in_specs=[smem, vmem] + anywhere * len(attn_w),
        after=[piece for group in hidden_w[3:] for piece in group[1:-1]],
    )
    attn_parts = team_send([attn_part] * team)

    middle, normed_two, normed_two_t = call(
        functools.partial(middle_kernel, team),
        (x, gain_two, *attn_parts),
        (shaped((length, width), f32), shaped((length, width), bf16), shaped((width, length), bf16)),
        time=1,
    )
    weight_buffer = pltpu.VMEM((row_parts, row_count, col_parts * hidden_cols), bf16)
    grad_buffer = pltpu.VMEM((col_parts, row_parts, row_count, hidden_cols), bf16)
    fed = call(
        functools.partial(feed_kernel, team, col_parts, row_parts),
        (place, normed_two, normed_two_t, cot, cot_t, *hidden_flat),
        (
            *[shaped((own_rows, width), bf16)] * team,
            shaped((length, width), bf16),
            *hidden_stacks,
        ),
        scratch=[
            *[weight_buffer] * 2,
            *[grad_buffer] * 2,
            *[pltpu.VMEM((length, col_parts * hidden_cols), bf16)] * 2,
            pltpu.SemaphoreType.DMA((4, col_parts, row_parts)),
        ],
        time=18,
        grid=(col_parts,),
        in_specs=[smem, wide, fixed(width, length), wide, fixed(width, length)]
        + anywhere * len(hidden_flat),
        out_specs=[fixed(own_rows, width)] * team + [wide] + anywhere * 8,
    )
    out_pieces, two_part, hidden_grads = fed[:team], fed[team], fed[team + 1 :]
    two_parts = team_send([two_part] * team)

    def rows_of(array, member):
        return lax.dynamic_slice_in_dim(array, member * own_rows, own_rows, 0)

    def share_rows(pieces, kind):
        others = []
        if halves == 2:
            pairs = pieces.reshape(seq_total, halves, own_rows, width)
            others = [swap(lax.dynamic_index_in_dim(pairs, 1 - sl, 1, keepdims=False))]
        (blocks,) = call(
            functools.partial(assemble_kernel, halves, low_count),
            (place, pieces, *others),
            (shaped((seq_total, length, width), kind),),
            time=3.5,
            in_specs=[smem, vmem] + [vmem] * len(others),
        )
        return blocks

    out_pieces = team_send(list(out_pieces))
    result = rows_of(middle, rank) + sum(item.astype(f32) for item in out_pieces)
    result = result.astype(bf16)
    layer_pieces = lax.all_gather(result, MODEL, axis=0, tiled=False)
    layer_out = share_rows(layer_pieces, bf16)

    def both_halves(own):
        if halves == 1:
            return [own]
        return [own, swap(lax.dynamic_slice_in_dim(own, (1 - sl) * rows_dev, rows_dev, 0))]

    middle_grad, gain_two_grad, one_part, low_grad, *rest = call(
        functools.partial(attend_back_kernel, *sizes),
        (place, middle, gain_two, cot, *two_parts, kept, probs, probs_t, *attn_w),
        (
            shaped((own_rows, width), f32),
            shaped((1, width), f32),
            shaped((length, width), bf16),
            shaped((length, width), bf16),
            *[flat_shape] * 3,
            *[shaped((length, channels), bf16)] * team,
        ),
        scratch=[
            head_buffer,
            pltpu.VMEM(flat_shape.shape, bf16),
            pltpu.VMEM((length, width), bf16),
            pltpu.VMEM(kept_shape.shape, bf16),
            *[pltpu.VMEM((col_parts, length, length), bf16)] * 2,
            head_sems,
            pltpu.SemaphoreType.DMA((3,)),
        ],
        time=1,
        in_specs=[smem] + [vmem] * (3 + team) + anywhere * (3 + len(attn_w)),
        after=(result,),
    )
    head_grads, context_grads = rest[:3], rest[3:]
    context_grads = team_send(context_grads)
    down_first = first_messages(hidden_grads[4:])
    g_steps, adjoint_ends, adjoint_total, adjoint_done = call(
        functools.partial(adjoint_kernel, team),
        (logr, *context_grads),
        (
            shaped((tiles, length, LANES), f32),
            shaped((2, states, SUBS, channels), f32),
            shaped((2, states, channels), f32),
        ),
        scratch=[pltpu.VMEM((length, LANES), f32)],
        time=1,
        after=down_first,
        token=True,
    )
    adjoint_totals = everywhere(adjoint_total.astype(bf16), ("sh", "mq"))
    down_second = second_messages(hidden_grads[4:], down_first, adjoint_done)
    down_second = hold(down_second, (adjoint_totals,))
    up_stacks = list(hidden_grads[:4])
    up_stacks[1::2] = hold(up_stacks[1::2], (adjoint_totals,))
    up_first = first_messages(up_stacks)
    *one_pieces, grad_ssm, context_done = call(
        functools.partial(context_back_kernel, team),
        (place, g_steps, u_steps, adjoint_ends, adjoint_totals, logr, coef, one_part),
        (
            *[shaped((own_rows, width), bf16)] * team,
            shaped((2, states, channels), f32),
        ),
        scratch=[
            pltpu.VMEM((tiles, length, LANES), f32),
            pltpu.VMEM((length, width), f32),
            pltpu.VMEM((length, LANES), f32),
        ],
        in_specs=[smem] + [vmem] * 7,
        time=1,
        after=(*down_second, *up_stacks[1::2]),
        token=True,
    )
    one_pieces = team_send(one_pieces)
    down_arrived = []
    down_sums = halve_both(
        hidden_grads[4:], down_first, down_second, context_done, down_arrived
    )
    grad_rows, gain_one_grad, rows_done = call(
        functools.partial(input_grad_kernel, team),
        (place, x, gain_one, middle_grad, *one_pieces),
        (shaped((own_rows, width), bf16), shaped((1, width), f32)),
        in_specs=[smem] + [vmem] * (3 + team),
        time=1,
        after=(layer_pieces, *down_arrived),
        token=True,
    )
    grad_down = sum_over_z(*down_sums, False)
    head_stacks = call(
        functools.partial(head_grads_kernel, col_parts, row_parts),
        (place, low_grad, attended, normed_t, context_t, *head_grads),
        head_stacks,
        scratch=[head_buffer, head_sems],
        time=1,
        in_specs=[smem] + [vmem] * 7,
        out_specs=anywhere * 4,
        after=(grad_rows,),
    )
    up_second = second_messages(up_stacks, up_first, rows_done)
    up_sums = halve_both(up_stacks, up_first, up_second)
    head_first = first_messages(head_stacks)
    head_second = second_messages(head_stacks, head_first, rows_done)
    head_sums = halve_both(head_stacks, head_first, head_second)
    grad_up = sum_over_z(*up_sums)
    grad_heads = sum_over_z(*head_sums)
    input_grad = share_rows(lax.all_gather(grad_rows, MODEL, axis=0, tiled=False), f32)

    placed_ssm = lax.dynamic_update_slice_in_dim(
        jnp.zeros((2 * states, width), f32),
        grad_ssm.reshape(2 * states, channels),
        rank * channels,
        1,
    )
    small_grads = jnp.concatenate([placed_ssm, gain_one_grad, gain_two_grad], 0)
    (small_grads,) = hold((small_grads,), head_sums)
    small_grads = small_grads.reshape(2 * states + 2, lax.axis_size(ALL), -1)
    small_grads = lax.all_to_all(jnp.transpose(small_grads, (1, 0, 2)), ALL, 0, 0, tiled=True)
    small_grads = jnp.sum(small_grads, axis=0)

    def moments(matrices, grads, arrays, after=()):
        changed = [shaped(old.shape, f32) for group in arrays for old in group]
        grad_parts = [part for grad in grads for part in both_halves(grad)]
        ins = [item for group in arrays for item in group]
        *found, sums = call(
            functools.partial(moments_kernel, halves, matrices),
            (place, *grad_parts, *ins),
            (*changed, shaped((2, LANES), f32)),
            in_specs=[smem] + [vmem] * (len(grad_parts) + len(ins)),
            after=after,
            time=4,
        )
        return [found[3 * i : 3 * i + 3] for i in range(len(arrays))], sums

    hidden_new, hidden_sums = moments(
        ((4, 0, 0, False, None), (5, 1, 0, True, None)),
        (grad_up, grad_down),
        ((w_up, first_up, second_up), (w_down, first_down, second_down)),
    )
    heads_new, head_sums = moments(
        tuple((i, 0, i, False, i) for i in range(3)) + ((3, 0, 3, True, None),),
        (grad_heads,),
        ((w_qkv, first_qkv, second_qkv), (w_out, first_out, second_out)),
        (layer_out, input_grad),
    )
    own_channels = norm_gains.shape[1]
    ssm_items = [item.reshape(2 * states, own_channels) for item in (ssm_param, first_ssm, second_ssm)]
    small_items = [norm_gains, first_gain, second_gain, *ssm_items]
    *small_new, small_sums = call(
        functools.partial(small_moments_kernel, (6, 8)),
        (small_grads.reshape(2 * states + 2, own_channels), *small_items),
        (*[shaped(item.shape, f32) for item in small_items], shaped((2, LANES), f32)),
    )
    all_sums = everywhere(hidden_sums + head_sums + small_sums, ALL)
    masters = (w_qkv, w_out, w_up, w_down, norm_gains, ssm_items[0])
    news = (*heads_new, *hidden_new, small_new[:3], small_new[3:])
    *weights, norms = call(
        functools.partial(update_kernel, ((0, 1, 2), (3,), (4,), (5,), (6, 7), (8, 9))),
        (all_sums, *masters, *[group[2] for group in news]),
        (*[shaped(item.shape, f32) for item in masters], shaped((2, LANES), f32)),
        time=3.2,
    )
    outputs = [layer_out, input_grad]
    for index, (weight, (first_new, second_new, unused)) in enumerate(zip(weights, news)):
        if index == 4:
            outputs += [weight, first_new, second_new[0], second_new[1]]
        else:
            kept_shape = ssm_param.shape if index == 5 else weight.shape
            outputs += [item.reshape(kept_shape) for item in (weight, first_new, second_new)]
    outputs.append(norms[:, :10])
    return tuple(outputs)


def solution(mesh):
    seq_count, model_count = mesh.shape["seq"], mesh.shape["mp"]
    halves = 2 if HEADS // model_count >= 2 else 1
    sizes = (seq_count // halves, halves, SEQS, halves, model_count // (SEQS * halves))
    fine = Mesh(mesh.devices.reshape(sizes), ALL)
    seq, model = ("sh", "sl"), ("mb", "mq", "ml")
    rows_cols, cols_rows = P(seq, model), P(model, seq)
    token = P(None, seq, None)
    stack = P(None, seq, model)
    gains = P(None, ALL)
    ssm = P(None, None, ALL)
    return jax.shard_map(
        on_device,
        mesh=fine,
        in_specs=(token, token, stack, cols_rows, rows_cols, cols_rows, gains, ssm)
        + (stack,) * 2
        + (cols_rows,) * 2
        + (rows_cols,) * 2
        + (cols_rows,) * 2
        + (gains,) * 2
        + (ssm,) * 2,
        out_specs=(token, token)
        + (stack,) * 3
        + (cols_rows,) * 3
        + (rows_cols,) * 3
        + (cols_rows,) * 3
        + (gains, gains, P(ALL), P(ALL))
        + (ssm,) * 3
        + (P(),),
        check_vma=False,
    )
```

```python
import functools
import math

import jax
import jax.numpy as jnp
from jax import lax
from jax.experimental import pallas as pl
from jax.experimental.pallas import tpu as pltpu
from jax.sharding import Mesh
from jax.sharding import PartitionSpec as P

HD = 128
HEADS = 8
BLK = 512
STEP = 10
SEQS = 2
LANES = 128
SUBS = 8
GROUP = 8

norm_eps = 1e-05
beta_first = 0.9
beta_second = 0.999
lamb_eps = 1e-06
weight_decay = 0.01
learn_rate = 0.5
score_scale = HD ** (-0.5)

f32 = jnp.float32
bf16 = jnp.bfloat16
VMEM_BYTES = 56 * 1024 * 1024

ALL = ("sh", "sl", "mb", "mq", "ml")
MODEL = ("mb", "mq", "ml")
COLS = ("mb", "mq")
TEAM = ("sl", "ml")


def dot(left, right):
    return lax.dot_general(left, right, (((1,), (0,)), ((), ())), preferred_element_type=f32)


def dot_t(left, right):
    return lax.dot_general(left, right, (((1,), (1,)), ((), ())), preferred_element_type=f32)


def normalise(values):
    centred = values - jnp.mean(values, axis=-1, keepdims=True)
    inverse = lax.rsqrt(jnp.mean(centred * centred, axis=-1, keepdims=True) + norm_eps)
    return centred * inverse, inverse


def normalise_back(unit, inverse, grad_unit):
    mean_one = jnp.mean(grad_unit, axis=-1, keepdims=True)
    mean_two = jnp.mean(grad_unit * unit, axis=-1, keepdims=True)
    return inverse * (grad_unit - mean_one - unit * mean_two)


def sub_index():
    return lax.broadcasted_iota(jnp.int32, (SUBS, LANES), 0)


def spread(row):
    return jnp.broadcast_to(row, (SUBS, LANES))


def lane_tile(index):
    return slice(index * LANES, (index + 1) * LANES)


def no_state(tiles):
    rows = tiles[0, :SUBS, :]
    return rows - rows


def in_steps(steps, tile, rows):
    span = rows.shape[0] // SUBS

    def move(i, unused):
        steps[tile, pl.ds(pl.multiple_of(i * SUBS, SUBS), SUBS), :] = rows[
            pl.ds(i, SUBS, stride=span), :
        ]
        return unused

    lax.fori_loop(0, span, move, 0, unroll=8)


def from_steps(rows, steps, tile):
    span = rows.shape[0] // SUBS

    def move(i, unused):
        rows[pl.ds(i, SUBS, stride=span), :] = steps[
            tile, pl.ds(pl.multiple_of(i * SUBS, SUBS), SUBS), :
        ]
        return unused

    lax.fori_loop(0, span, move, 0, unroll=8)


def step_rows(i):
    return pl.ds(pl.multiple_of(i * SUBS, SUBS), SUBS)


def norm_kernel(
    place, x_ref, gain_ref, logr_ref, normed_ref, turned_ref, u_tiles, ends_ref, total_ref, rows
):
    unit, unused = normalise(x_ref[...].astype(f32))
    normed_ref[...] = (unit * gain_ref[...]).astype(bf16)
    turned_ref[...] = normed_ref[...].T
    tiles, length, unused = u_tiles.shape
    states = logr_ref.shape[0]
    span = length // SUBS
    for tile in range(tiles):
        start = place[0] * (tiles * LANES) + tile * LANES
        rows[...] = normed_ref[:, pl.ds(pl.multiple_of(start, LANES), LANES)].astype(f32)
        in_steps(u_tiles, tile, rows)
    left = ((SUBS - 1 - sub_index()) * span).astype(f32)
    for tile in range(tiles):
        rate = jnp.exp(logr_ref[:, lane_tile(tile)])
        decay = jnp.exp(-rate)
        decays = [spread(decay[n : n + 1]) for n in range(states)]

        def step(i, held):
            u = u_tiles[tile, step_rows(i), :]
            return tuple(d * h + u for d, h in zip(decays, held))

        zero = no_state(u_tiles)
        held = lax.fori_loop(0, span, step, (zero,) * states, unroll=4)
        for n in range(states):
            ends_ref[n, :, lane_tile(tile)] = held[n]
            total_ref[n : n + 1, lane_tile(tile)] = jnp.sum(
                held[n] * jnp.exp(-left * rate[n : n + 1]), axis=0, keepdims=True
            )


def context_kernel(
    place, u_tiles, ends_ref, all_ref, logr_ref, coef_ref, context_ref, y_tiles, rows
):
    tiles, length, unused = u_tiles.shape
    states = logr_ref.shape[0]
    span = length // SUBS
    index = sub_index()
    before = (index * span).astype(f32)
    for tile in range(tiles):
        rate = jnp.exp(logr_ref[:, lane_tile(tile)])
        decay = jnp.exp(-rate)
        scale = coef_ref[:, lane_tile(tile)] * jnp.sqrt(2.0 * rate)
        incoming = jnp.zeros((states, LANES), f32)
        for j in range(all_ref.shape[0]):
            gap = place[1] - 1 - j
            distance = (jnp.maximum(gap, 0) * length).astype(f32)
            term = jnp.exp(-distance * rate) * all_ref[j, :, lane_tile(tile)].astype(f32)
            incoming = incoming + jnp.where(gap >= 0, term, 0.0)
        for first in range(0, states, GROUP):
            chosen = range(first, first + GROUP)
            starts = []
            for n in chosen:
                row = rate[n : n + 1]
                run = ends_ref[n, :, lane_tile(tile)]
                for d in (1, 2, 4):
                    moved = jnp.exp(-(d * span) * row) * pltpu.roll(run, d, 0)
                    run = run + jnp.where(index >= d, moved, 0.0)
                run = jnp.where(index >= 1, pltpu.roll(run, 1, 0), 0.0)
                starts.append(run + jnp.exp(-before * row) * incoming[n : n + 1])
            decays = [spread(decay[n : n + 1]) for n in chosen]
            scales = [spread(scale[n : n + 1]) for n in chosen]

            def step(i, held):
                at = step_rows(i)
                u = u_tiles[tile, at, :]
                held = tuple(d * h + u for d, h in zip(decays, held))
                parts = [s * h for s, h in zip(scales, held)]
                if first > 0:
                    parts[0] = parts[0] + y_tiles[tile, at, :]
                while len(parts) > 1:
                    parts = [a + b for a, b in zip(parts[::2], parts[1::2])]
                y_tiles[tile, at, :] = parts[0]
                return held

            lax.fori_loop(0, span, step, tuple(starts), unroll=4)
        from_steps(rows, y_tiles, tile)
        context_ref[:, lane_tile(tile)] = rows[...].astype(bf16)


def whole_rows(block):
    return block.reshape(block.shape[0] * block.shape[1], block.shape[2])


def head(index):
    return slice(index * HD, (index + 1) * HD)


def weight_copies(near, far, buffer, place, sems, act):
    count = sems.shape[0]
    half = count // 2
    for k in range(count):
        owner = lax.rem(place[6] + count - k, count)
        for stacks, low in ((near, 0), (far, half)):

            @pl.when((owner >= low) & (owner < low + half))
            def move():
                for r, stack in enumerate(stacks):
                    inner = buffer.at[k, place[2] ^ r]
                    act(pltpu.make_async_copy(stack.at[owner - low], inner, sems.at[k, r]))


def of_heads(buffer, i):
    return jnp.concatenate([whole_rows(buffer[k, :, :, head(i)]) for k in range(buffer.shape[0])], axis=1)


def gradient_slot(row_parts, order, r):
    position = 0
    for bit in reversed(order):
        position = 2 * position + (1 if r & bit else 0)
    return position // (row_parts // 2), position % (row_parts // 2)


def round_orders(row_parts):
    bits = [1 << i for i in range(row_parts.bit_length() - 1)]
    return bits, bits[::-1]


def gradient_pieces(stacks, row_parts, far, slot):
    found = []
    for r in range(row_parts):
        sent, at = gradient_slot(row_parts, round_orders(row_parts)[far], r)
        found.append(stacks[2 * far + sent].at[at, slot])
    return found


def project_kernel(team, col_parts, row_parts, place, normed_ref, cot_ref, *refs):
    contexts, refs = refs[:team], refs[team:]
    near, far, refs = refs[:row_parts], refs[row_parts : 2 * row_parts], refs[2 * row_parts :]
    context_t_ref, cot_t_ref, kept_ref = refs[:3]
    context_ref, weights, sems = refs[3:]
    weight_copies(near, far, weights, place, sems, lambda copy: copy.start())
    width = contexts[0].shape[1]
    for k in range(team):
        lanes = pl.ds(pl.multiple_of((place[0] ^ k) * width, LANES), width)
        context_ref[:, lanes] = contexts[k][...]
    context_t_ref[...] = context_ref[...].T
    cot_t_ref[...] = cot_ref[...].T
    weight_copies(near, far, weights, place, sems, lambda copy: copy.wait())
    kept_ref[0] = dot(normed_ref[...], of_heads(weights, 0)).astype(bf16)
    kept_ref[1] = dot(context_ref[...], of_heads(weights, 1)).astype(bf16)
    kept_ref[2] = dot(context_ref[...], of_heads(weights, 2)).astype(bf16)


def attend_kernel(team, col_parts, row_parts, place, kept_ref, *refs):
    near, far, refs = refs[:row_parts], refs[row_parts : 2 * row_parts], refs[2 * row_parts :]
    part_ref, attended_ref, probs_ref, probs_t_ref, weights, sems = refs
    weight_copies(near, far, weights, place, sems, lambda copy: copy.start())
    length = kept_ref.shape[1]
    rows = lax.broadcasted_iota(jnp.int32, (length, length), 0)
    cols = lax.broadcasted_iota(jnp.int32, (length, length), 1)
    for h in range(col_parts):
        scores = dot_t(kept_ref[0, :, head(h)], kept_ref[1, :, head(h)]) * score_scale
        scores = jnp.where(rows >= cols, scores, -1e30)
        shifted = jnp.exp(scores - jnp.max(scores, axis=-1, keepdims=True))
        inverse = 1.0 / jnp.sum(shifted, axis=-1, keepdims=True)
        probs = (shifted * inverse).astype(bf16)
        probs_ref[h] = probs
        probs_t_ref[h] = probs.T
        attended_ref[:, head(h)] = dot(probs, kept_ref[2, :, head(h)]).astype(bf16)
    weight_copies(near, far, weights, place, sems, lambda copy: copy.wait())
    part_ref[...] = dot_t(attended_ref[...], of_heads(weights, 3)).astype(bf16)


def gelu_parts(hidden, grad_act):
    density = jnp.exp(-0.5 * hidden * hidden)
    t = 1.0 / (1.0 + (0.3275911 * math.sqrt(0.5)) * jnp.abs(hidden))
    series = 0.5 * 1.061405429
    for factor in (-1.453152027, 1.421413741, -0.284496736, 0.254829592):
        series = series * t + 0.5 * factor
    tail = series * t * density
    cdf = jnp.where(hidden >= 0.0, 1.0 - tail, tail)
    slope = cdf + hidden * density * (1.0 / math.sqrt(2.0 * math.pi))
    return (hidden * cdf).astype(bf16), (grad_act * slope).astype(bf16)


def middle_kernel(team, x_ref, gain_ref, *refs):
    parts, (middle_ref, normed_ref, normed_t_ref) = refs[:team], refs[team:]
    attn = parts[0][...].astype(f32)
    for part in parts[1:]:
        attn = attn + part[...].astype(f32)
    middle = x_ref[...].astype(f32) + attn
    middle_ref[...] = middle
    unit, unused = normalise(middle)
    normed_ref[...] = (unit * gain_ref[...]).astype(bf16)
    normed_t_ref[...] = normed_ref[...].T


def feed_kernel(team, col_parts, row_parts, place, normed_ref, normed_t_ref, cot_ref, cot_t_ref, *refs):
    count = col_parts * row_parts
    pieces, refs = refs[:count], refs[count:]
    outs, two_ref, refs = refs[:team], refs[team], refs[team + 1 :]
    stacks, refs = (refs[:4], refs[4:8]), refs[8:]
    up_all, down_all, grad_up, grad_down, activated_all, grad_all, sems = refs
    z = pl.program_id(0)
    half = col_parts // 2
    hidden_cols = grad_up.shape[3]

    def copies(k):
        found = []
        for r in range(row_parts):
            for which, buffer in enumerate((up_all, down_all)):
                outside = pieces[k * row_parts + r].at[:, pl.ds(which * hidden_cols, hidden_cols)]
                inside = buffer.at[place[2] ^ r, :, pl.ds(k * hidden_cols, hidden_cols)]
                found.append(pltpu.make_async_copy(outside, inside, sems.at[which, k, r]))
        return found

    def each_leaving(k, act):
        for which, buffer in enumerate((grad_up, grad_down)):
            for r, piece in enumerate(gradient_pieces(stacks[which], row_parts, k // half, k % half)):
                inner = buffer.at[k, place[2] ^ r]
                act(pltpu.make_async_copy(inner, piece, sems.at[2 + which, k, r]))

    @pl.when(z == 0)
    def start():
        for k in range(col_parts):
            for copy in copies(k):
                copy.start()

    for k in range(col_parts):

        @pl.when(z == k)
        def arrive():
            for copy in copies(k):
                copy.wait()

    at = pl.ds(pl.multiple_of(z * hidden_cols, hidden_cols), hidden_cols)
    hidden = dot(normed_ref[...], whole_rows(up_all[:, :, at]))
    grad_act = dot(cot_ref[...], whole_rows(down_all[:, :, at]))
    activated, grad_pre = gelu_parts(hidden, grad_act)
    activated_all[:, at] = activated
    grad_all[:, at] = grad_pre
    shape = grad_up.shape[1:]
    grad_up[z] = dot(normed_t_ref[...], grad_pre).astype(bf16).reshape(shape)
    grad_down[z] = dot(cot_t_ref[...], activated).astype(bf16).reshape(shape)

    for k in range(col_parts):

        @pl.when(z == k)
        def leave():
            each_leaving(k, lambda copy: copy.start())

    @pl.when(z == col_parts - 1)
    def finish():
        two_ref[...] = dot_t(grad_all[...], whole_rows(up_all[...])).astype(bf16)
        rows = outs[0].shape[0]
        for k in range(team):
            at_rows = pl.ds(pl.multiple_of((place[0] ^ k) * rows, rows), rows)
            outs[k][...] = dot_t(activated_all[at_rows, :], whole_rows(down_all[...])).astype(bf16)
        for k in range(col_parts):
            each_leaving(k, lambda copy: copy.wait())


def attend_back_kernel(team, col_parts, row_parts, place, middle_ref, gain_ref, cot_ref, *refs):
    parts, refs = refs[:team], refs[team:]
    late, refs = refs[:3], refs[3:]
    near, far, refs = refs[:row_parts], refs[row_parts : 2 * row_parts], refs[2 * row_parts :]
    middle_grad_ref, gain_grad_ref, one_ref, low = refs[:4]
    grad_q, grad_k, grad_v = refs[4:7]
    context_grads, refs = refs[7 : 7 + team], refs[7 + team :]
    weights, grad_out, total_low = refs[:3]
    held, (sems, late_sems) = refs[3:6], refs[6:]
    kept_ref, probs_ref, probs_t_ref = held
    weight_copies(near, far, weights, place, sems, lambda copy: copy.start())
    late_copies = [
        pltpu.make_async_copy(outside, inside, late_sems.at[i])
        for i, (outside, inside) in enumerate(zip(late, held))
    ]
    for copy in late_copies:
        copy.start()
    own_rows = middle_ref.shape[0] // team
    grad_two = parts[0][...].astype(f32)
    for part in parts[1:]:
        grad_two = grad_two + part[...].astype(f32)
    unit, inverse = normalise(middle_ref[...])
    grad_gain = grad_two * unit
    rows = lax.broadcasted_iota(jnp.int32, grad_gain.shape, 0)
    first = place[0] * own_rows
    mine = (rows >= first) & (rows < first + own_rows)
    gain_grad_ref[...] = jnp.sum(jnp.where(mine, grad_gain, 0.0), axis=0, keepdims=True)
    grad = cot_ref[...].astype(f32) + normalise_back(unit, inverse, grad_two * gain_ref[...])
    low[...] = grad.astype(bf16)
    for k in range(team):

        @pl.when(place[0] == k)
        def own():
            middle_grad_ref[...] = grad[k * own_rows : (k + 1) * own_rows, :]

    weight_copies(near, far, weights, place, sems, lambda copy: copy.wait())
    for copy in late_copies:
        copy.wait()
    grad_out[...] = dot(low[...], of_heads(weights, 3)).astype(bf16)
    for h in range(col_parts):
        q, k, v = (kept_ref[i, :, head(h)] for i in range(3))
        grad_heads = grad_out[:, head(h)]
        grad_v[:, head(h)] = dot(probs_t_ref[h], grad_heads).astype(bf16)
        probs = probs_ref[h].astype(f32)
        grad_probs = dot_t(grad_heads, v)
        inner = jnp.sum(grad_probs * probs, axis=-1, keepdims=True)
        grad_scores = (probs * (grad_probs - inner)).astype(bf16)
        grad_q[:, head(h)] = (dot(grad_scores, k) * score_scale).astype(bf16)
        turned = dot_t(v, grad_heads) - inner.T
        turned = (probs_t_ref[h].astype(f32) * turned).astype(bf16)
        grad_k[:, head(h)] = (dot(turned, q) * score_scale).astype(bf16)
    total = dot_t(grad_k[...], of_heads(weights, 1)) + dot_t(grad_v[...], of_heads(weights, 2))
    total_low[...] = total.astype(bf16)
    width = context_grads[0].shape[1]
    for k in range(team):
        lanes = pl.ds(pl.multiple_of((place[0] ^ k) * width, LANES), width)
        context_grads[k][...] = total_low[:, lanes]
    one_ref[...] = dot_t(grad_q[...], of_heads(weights, 0)).astype(bf16)


def head_grads_kernel(col_parts, row_parts, place, low, attended_ref, *refs):
    normed_t_ref, context_t_ref, grad_q, grad_k, grad_v = refs[:5]
    stacks, (grads, out_sems) = refs[5:9], refs[9:]
    half = col_parts // 2
    shape = (*grads.shape[1:3], HD)

    def put(i, grad):
        for h in range(col_parts):
            grads[h, :, :, head(i)] = grad[:, head(h)].astype(bf16).reshape(shape)

    put(0, dot(normed_t_ref[...], grad_q[...]))
    put(1, dot(context_t_ref[...], grad_k[...]))
    put(2, dot(context_t_ref[...], grad_v[...]))
    put(3, dot(low[...].T, attended_ref[...]))
    copies = []
    for k in range(col_parts):
        for r, piece in enumerate(gradient_pieces(stacks, row_parts, k // half, k % half)):
            copies.append(pltpu.make_async_copy(grads.at[k, place[2] ^ r], piece, out_sems.at[k, r]))
    for copy in copies:
        copy.start()
    for copy in copies:
        copy.wait()


def adjoint_kernel(team, logr_ref, *refs):
    parts = refs[:team]
    g_tiles, ends_ref, total_ref, rows = refs[team:]
    grad = parts[0][...].astype(f32)
    for part in parts[1:]:
        grad = grad + part[...].astype(f32)
    grad = grad.astype(bf16).astype(f32)
    tiles, length, unused = g_tiles.shape
    states = logr_ref.shape[0]
    span = length // SUBS
    for tile in range(tiles):
        rows[...] = grad[:, lane_tile(tile)]
        in_steps(g_tiles, tile, rows)
    before = (sub_index() * span).astype(f32)
    for tile in range(tiles):
        rate = jnp.exp(logr_ref[:, lane_tile(tile)])
        decay = jnp.exp(-rate)
        for first in range(0, states, GROUP):
            chosen = range(first, first + GROUP)
            decays = [spread(decay[n : n + 1]) for n in chosen]

            def step(i, held):
                g = g_tiles[tile, step_rows(span - 1 - i), :]
                later = []
                for d, (b, w) in zip(decays, held):
                    shrunk = d * b
                    later.append((g + shrunk, d * w + shrunk))
                return tuple(later)

            zero = no_state(g_tiles)
            held = lax.fori_loop(0, span, step, ((zero, zero),) * GROUP, unroll=4)
            for n, (b, w) in zip(chosen, held):
                ends_ref[0, n, :, lane_tile(tile)] = b
                ends_ref[1, n, :, lane_tile(tile)] = w
                shrink = jnp.exp(-before * rate[n : n + 1])
                total_ref[0, n : n + 1, lane_tile(tile)] = jnp.sum(
                    shrink * b, axis=0, keepdims=True
                )
                total_ref[1, n : n + 1, lane_tile(tile)] = jnp.sum(
                    shrink * (w + before * b), axis=0, keepdims=True
                )


def context_back_kernel(
    team, place, g_tiles, u_tiles, ends_ref, all_ref, logr_ref, coef_ref, one_ref, *refs
):
    pieces = refs[:team]
    grad_ssm_ref, y_tiles, full, rows = refs[team:]
    tiles, length, unused = u_tiles.shape
    states = logr_ref.shape[0]
    span = length // SUBS
    width = tiles * LANES
    index = sub_index()
    after = ((SUBS - 1 - index) * span).astype(f32)
    full[...] = one_ref[...].astype(f32)
    group = GROUP
    for tile in range(tiles):
        lanes = lane_tile(tile)
        rate = jnp.exp(logr_ref[:, lanes])
        decay = jnp.exp(-rate)
        root = jnp.sqrt(2.0 * rate)
        scale = coef_ref[:, lanes] * root
        in_b = jnp.zeros((states, LANES), f32)
        in_w = jnp.zeros((states, LANES), f32)
        for j in range(all_ref.shape[0]):
            gap = j - place[1] - 1
            distance = (jnp.maximum(gap, 0) * length).astype(f32)
            shrink = jnp.exp(-distance * rate)
            b, w = all_ref[j, 0, :, lanes].astype(f32), all_ref[j, 1, :, lanes].astype(f32)
            in_b = in_b + jnp.where(gap >= 0, shrink * b, 0.0)
            in_w = in_w + jnp.where(gap >= 0, shrink * (w + distance * b), 0.0)
        for first in range(0, states, group):
            chosen = range(first, first + group)
            starts = []
            for n in chosen:
                row = rate[n : n + 1]
                b, w = ends_ref[0, n, :, lanes], ends_ref[1, n, :, lanes]
                for d in (1, 2, 4):
                    shrink = jnp.exp(-(d * span) * row)
                    next_b = pltpu.roll(b, SUBS - d, 0)
                    next_w = pltpu.roll(w, SUBS - d, 0)
                    inside = index < SUBS - d
                    b, w = (
                        b + jnp.where(inside, shrink * next_b, 0.0),
                        w + jnp.where(inside, shrink * (next_w + (d * span) * next_b), 0.0),
                    )
                inside = index < SUBS - 1
                b = jnp.where(inside, pltpu.roll(b, SUBS - 1, 0), 0.0)
                w = jnp.where(inside, pltpu.roll(w, SUBS - 1, 0), 0.0)
                shrink = jnp.exp(-after * row)
                b_row, w_row = in_b[n : n + 1], in_w[n : n + 1]
                b = b + shrink * b_row
                w = w + shrink * (w_row + after * b_row)
                zero = no_state(u_tiles)
                starts.append((b, w, zero, zero))
            decays = [spread(decay[n : n + 1]) for n in chosen]
            scales = [spread(scale[n : n + 1]) for n in chosen]

            def step(i, held):
                at = step_rows(span - 1 - i)
                g = g_tiles[tile, at, :]
                u = u_tiles[tile, at, :]
                later, parts = [], []
                for d, s, (b, w, sum_b, sum_w) in zip(decays, scales, held):
                    shrunk = d * b
                    w = d * w + shrunk
                    b = g + shrunk
                    later.append((b, w, sum_b + u * b, sum_w + u * w))
                    parts.append(s * b)
                while len(parts) > 1:
                    parts = [p + q for p, q in zip(parts[::2], parts[1::2])]
                if first > 0:
                    parts[0] = parts[0] + y_tiles[tile, at, :]
                y_tiles[tile, at, :] = parts[0]
                return tuple(later)

            held = lax.fori_loop(0, span, step, tuple(starts), unroll=2)
            for n, (unused_b, unused_w, sum_b, sum_w) in zip(chosen, held):
                sum_b = jnp.sum(sum_b, axis=0, keepdims=True)
                sum_w = jnp.sum(sum_w, axis=0, keepdims=True)
                row = slice(n, n + 1)
                grad_ssm_ref[0, row, lanes] = root[row] * sum_b
                grad_ssm_ref[1, row, lanes] = scale[row] * (0.5 * sum_b - rate[row] * sum_w)
        at_lanes = pl.ds(pl.multiple_of(place[0] * width + tile * LANES, LANES), LANES)
        from_steps(rows, y_tiles, tile)
        full[:, at_lanes] += rows[...].astype(bf16).astype(f32)
    count = pieces[0].shape[0]
    for k in range(team):
        at_rows = pl.ds(pl.multiple_of((place[0] ^ k) * count, count), count)
        pieces[k][...] = full[at_rows, :].astype(bf16)


def input_grad_kernel(team, place, x_ref, gain_ref, middle_grad_ref, *refs):
    parts, (out_ref, gain_grad_ref) = refs[:team], refs[team:]
    rows = out_ref.shape[0]
    at_rows = pl.ds(pl.multiple_of(place[0] * rows, rows), rows)
    grad_one = parts[0][...].astype(f32)
    for part in parts[1:]:
        grad_one = grad_one + part[...].astype(f32)
    unit, inverse = normalise(x_ref[at_rows, :].astype(f32))
    gain_grad_ref[...] = jnp.sum(grad_one * unit, axis=0, keepdims=True)
    back = normalise_back(unit, inverse, grad_one * gain_ref[...])
    out_ref[...] = (middle_grad_ref[...] + back).astype(bf16)


def assemble_kernel(halves, low_count, place, own_ref, *refs):
    others, out_ref = refs[:-1], refs[-1]
    count, rows, unused = own_ref.shape
    half = place[4]

    def put(value, sequence, which, member):
        at_rows = pl.ds(pl.multiple_of((which * low_count + member) * rows, rows), rows)
        out_ref[sequence, at_rows, :] = value.astype(out_ref.dtype)

    for sequence in range(count // (halves * low_count)):
        if halves == 1:
            for member in range(low_count):
                put(own_ref[sequence * low_count + member], sequence, 0, member)
        else:
            put(own_ref[sequence * halves + half], sequence, half, 0)
            put(others[0][sequence], sequence, 1 - half, 0)


def pack_kernel(halves, place, qkv_ref, out_ref, up_ref, down_ref, *refs):
    rows = up_ref.shape[0]
    heads, hidden = out_ref.shape[0] // halves, up_ref.shape[1] // halves
    for which in range(halves):
        side = place[4] if which == 0 else 1 - place[4]
        at_heads = pl.ds(pl.multiple_of(side * heads, LANES), heads)
        at_hidden = pl.ds(pl.multiple_of(side * hidden, LANES), hidden)
        if which == 0:
            head_ref = refs[0]
            wide_ref, deep_ref = refs[1].at[:, :hidden], refs[1].at[:, hidden:]
        else:
            packed = refs[2]
            head_ref = packed.at[:, : 4 * heads]
            wide_ref = packed.at[:, 4 * heads : 4 * heads + hidden]
            deep_ref = packed.at[:, 4 * heads + hidden :]
        for i in range(3):
            head_ref[:, i * heads : (i + 1) * heads] = qkv_ref[i, :, at_heads].astype(bf16)
        head_ref[:, 3 * heads :] = out_ref[at_heads, :].T.astype(bf16)
        wide_ref[...] = up_ref[:, at_hidden].astype(bf16)
        deep_ref[...] = down_ref[at_hidden, :].T.astype(bf16)


def small_kernel(ssm_ref, gains_ref, out_ref):
    count = ssm_ref.shape[0]
    out_ref[:count, :] = ssm_ref[...]
    out_ref[count:, :] = gains_ref[...]


def lamb_moments(weight, grad_item, first_old, second_old):
    first_new = beta_first * first_old + (1.0 - beta_first) * grad_item
    second_new = beta_second * second_old + (1.0 - beta_second) * grad_item * grad_item
    direction = (
        first_new
        / (1.0 - beta_first**STEP)
        / (jnp.sqrt(second_new / (1.0 - beta_second**STEP)) + lamb_eps)
        + weight_decay * weight
    )
    return (first_new, second_new, direction)


def place_sums(sums_ref, sums):
    rows = lax.broadcasted_iota(jnp.int32, sums_ref.shape, 0)
    lanes = lax.broadcasted_iota(jnp.int32, sums_ref.shape, 1)
    found = jnp.zeros(sums_ref.shape, f32)
    for index, pair in sums.items():
        for row, value in enumerate(pair):
            found = jnp.where((rows == row) & (lanes == index), value, found)
    sums_ref[...] = found


def moments_kernel(halves, matrices, place, *refs):
    count = 1 + max(item[1] for item in matrices)
    grads, refs = [refs[halves * i : halves * (i + 1)] for i in range(count)], refs[halves * count :]
    arrays = len({(item[1], item[4] is None) for item in matrices})
    ins = [refs[3 * i : 3 * i + 3] for i in range(arrays)]
    outs = [refs[3 * (arrays + i) : 3 * (arrays + i) + 3] for i in range(arrays)]
    sums_ref = refs[6 * arrays]
    keys = []
    sums = {}
    for number, source, column, turned, stacked in matrices:
        key = (source, stacked is None)
        if key not in keys:
            keys.append(key)
        pick = (lambda ref: ref) if stacked is None else (lambda ref, i=stacked: ref.at[i])
        weight, first, second = (pick(ref) for ref in ins[keys.index(key)])
        news = [pick(ref) for ref in outs[keys.index(key)]]
        width = weight.shape[0 if turned else 1] // halves
        rows = weight.shape[1 if turned else 0]
        cols = slice(column * width, (column + 1) * width)
        total_weight = total_update = 0.0
        for which, grad_ref in enumerate(grads[source]):
            side = place[4] if which == 0 else 1 - place[4]
            at = pl.ds(pl.multiple_of(side * width, width), width)
            if which == 0:
                grad = grad_ref[pl.ds(pl.multiple_of(side * rows, rows), rows), cols].astype(f32)
            else:
                grad = grad_ref[:, cols].astype(f32)
            at = (at, slice(None)) if turned else (slice(None), at)
            grad = grad.T if turned else grad
            old = weight[at]
            found = lamb_moments(old, grad, first[at], second[at])
            for ref, value in zip(news, found):
                ref[at] = value
            total_weight = total_weight + jnp.sum(old * old)
            total_update = total_update + jnp.sum(found[2] * found[2])
        sums[number] = (total_weight, total_update)
    place_sums(sums_ref, sums)


def small_moments_kernel(numbers, grads_ref, *refs):
    ins, outs, sums_ref = (refs[:3], refs[3:6]), (refs[6:9], refs[9:12]), refs[12]
    states = (grads_ref.shape[0] - 2) // 2
    sums = {}
    for (weight, first, second), news, start, rows, first_number in (
        (ins[0], outs[0], 2 * states, 1, numbers[0]),
        (ins[1], outs[1], 0, states, numbers[1]),
    ):
        for i in range(2):
            grad = grads_ref[start + i * rows : start + (i + 1) * rows, :]
            at = slice(i * rows, (i + 1) * rows)
            found = lamb_moments(weight[at, :], grad, first[at, :], second[at, :])
            for ref, value in zip(news, found):
                ref[at, :] = value
            sums[first_number + i] = (
                jnp.sum(weight[at, :] * weight[at, :]),
                jnp.sum(found[2] * found[2]),
            )
    place_sums(sums_ref, sums)


def update_kernel(stacks, sums_ref, *refs):
    count = len(stacks)
    weights, directions, news = refs[:count], refs[count : 2 * count], refs[2 * count : 3 * count]
    norms = jnp.sqrt(jnp.sum(sums_ref[...], axis=0))
    refs[3 * count][...] = norms
    ratios = norms[0:1] / norms[1:2]
    lanes = lax.broadcasted_iota(jnp.int32, ratios.shape, 1)
    for numbers, weight, direction, new in zip(stacks, weights, directions, news):
        step = weight.shape[0] // len(numbers)
        for i, number in enumerate(numbers):
            ratio = jnp.sum(jnp.where(lanes == number, ratios, 0.0), axis=1, keepdims=True)
            at = slice(i * step, (i + 1) * step)
            scale = learn_rate * ratio.reshape((1,) * weight.ndim)
            new[at] = weight[at] - scale * direction[at]


def call(
    body, ins, outs, scratch=(), grid=None, in_specs=None, out_specs=None, time=1.0, after=(), token=False
):
    moved = sum(a.size * a.dtype.itemsize for a in list(ins) + list(outs))
    params = pltpu.CompilerParams(vmem_limit_bytes=VMEM_BYTES)
    cost = pl.CostEstimate(flops=int(time * 1.15e9), bytes_accessed=moved, transcendentals=0)
    whole = pl.BlockSpec(memory_space=pltpu.VMEM)
    anywhere = pl.BlockSpec(memory_space=pl.ANY)
    in_specs = list(in_specs or [whole] * len(ins)) + [anywhere] * len(after)
    out_specs = list(out_specs or [whole] * len(outs))
    outs = list(outs)
    first_out = len(ins) + len(after)
    last_out = first_out + len(outs)
    if token:
        outs.append(jax.ShapeDtypeStruct((SUBS, LANES), f32))
        out_specs.append(whole)

    def run(*refs):
        refs = list(refs)
        if token:
            refs[last_out][...] = jnp.zeros((SUBS, LANES), f32)
            del refs[last_out]
        body(*refs[: len(ins)], *refs[first_out:])

    return pl.pallas_call(
        run,
        out_shape=tuple(outs),
        in_specs=in_specs,
        out_specs=tuple(out_specs),
        scratch_shapes=list(scratch),
        compiler_params=params,
        cost_estimate=cost,
        **({} if grid is None else {"grid": grid}),
    )(*ins, *after)


def shaped(shape, kind):
    return jax.ShapeDtypeStruct(tuple(shape), kind)


def on_device(
    tokens,
    cotangent,
    w_qkv,
    w_out,
    w_up,
    w_down,
    norm_gains,
    ssm_param,
    first_qkv,
    second_qkv,
    first_out,
    second_out,
    first_up,
    second_up,
    first_down,
    second_down,
    first_gain,
    second_gain,
    first_ssm,
    second_ssm,
):
    halves = lax.axis_size("sl")
    low_count = lax.axis_size("ml")
    row_parts = lax.axis_size("sh")
    col_parts = lax.axis_size("mb") * lax.axis_size("mq")
    team = halves * low_count
    sl, ml, mb, mq = (lax.axis_index(name) for name in ("sl", "ml", "mb", "mq"))
    rank = sl * low_count + ml
    block_index = lax.axis_index("sh") * halves + mq
    seq_total, length, width = tokens.shape
    assert length == BLK and seq_total == lax.axis_size("mb")
    states = ssm_param.shape[1]
    channels = width // team
    tiles = channels // LANES
    row_count = width // row_parts
    own_rows = length // team
    place = [rank, block_index, lax.axis_index("sh"), lax.axis_index(MODEL), sl, sl ^ mq]
    place.append(lax.axis_index(COLS))
    place = jnp.stack(place).astype(jnp.int32)
    smem = pl.BlockSpec(memory_space=pltpu.SMEM)
    vmem = pl.BlockSpec(memory_space=pltpu.VMEM)

    def permute(value, axes, moves):
        return lax.ppermute(value, axes, moves)

    def swap(value):
        return permute(value, "sl", [(0, 1), (1, 0)])

    def in_order(own, other, axis):
        return jnp.where(
            sl == 0, jnp.concatenate([own, other], axis), jnp.concatenate([other, own], axis)
        )

    def team_send(pieces):
        moved = [pieces[0]]
        for k in range(1, team):
            moved.append(permute(pieces[k], TEAM, [(i, i ^ k) for i in range(team)]))
        return moved

    def pick_block(array):
        own = lax.dynamic_index_in_dim(array, mb, 0, keepdims=False)
        if halves == 1:
            return own, ()
        other = swap(own)
        return jnp.where(sl == mq, own, other), (other,)

    def across(value, bit):
        return permute(value, "sh", [(i, i ^ bit) for i in range(row_parts)])

    def along(value, axes, step):
        count = lax.axis_size(axes)
        return permute(value, axes, [(i, (i + step) % count) for i in range(count)])

    bits = [1 << i for i in range(row_parts.bit_length() - 1)]

    def bit_order(k):
        return bits if k % 2 == 0 else bits[::-1]

    def double_rows(value, order):
        found = {0: value}
        for bit in order:
            for r in list(found):
                found[r | bit] = across(found[r], bit)
        return [found[r] for r in range(row_parts)]

    def add(*items, zero=None):
        total = sum(item.astype(f32) for item in items)
        return (total if zero is None else total + zero[0, 0]).astype(bf16)

    def first_messages(stacks):
        return across(stacks[1], bits[-1]), across(stacks[3], bits[0])

    def second_messages(stacks, first, zero):
        count = first[0].shape[0] // 2
        return [add(stacks[2 * i][count:], first[i][count:], zero=zero) for i in range(2)]

    def halve_rows(keep, arrived, order, send):
        items = [keep, arrived]
        for bit in order[-2::-1]:
            count = arrived.shape[0] // 2
            if send is None:
                send = add(*[item[count:] for item in items])
            arrived = across(send, bit)
            items = [item[:count] for item in items] + [arrived]
            send = None
        return [item[0] for item in items]

    def halve_both(stacks, first, send):
        near = halve_rows(stacks[0], first[0], bits, send[0])
        return near, halve_rows(stacks[2], first[1], bits[::-1], send[1])

    def hold(arrays, after):
        anywhere = pl.BlockSpec(memory_space=pl.ANY)
        return pl.pallas_call(
            lambda *refs: None,
            out_shape=tuple(shaped(item.shape, item.dtype) for item in arrays),
            in_specs=[anywhere] * (len(arrays) + len(after)),
            out_specs=(anywhere,) * len(arrays),
            input_output_aliases={i: i for i in range(len(arrays))},
        )(*arrays, *after)

    def gather_pieces(shard):
        pieces = []
        for k in range(col_parts):
            held = along(held, COLS, 1) if k > 0 else shard
            pieces.append(double_rows(held, bits if k % 2 == 0 else bits[::-1]))
        return pieces

    def sum_over_z(near, far, ring=True):
        if not ring:
            pieces = [stack[k] for stack in (near, far) for k in range(col_parts // 2)]
            moved = [along(piece, COLS, -k) for k, piece in enumerate(pieces) if k > 0]
            return add(pieces[0], *moved)
        held = None
        for stack in (far, near):
            for k in reversed(range(stack.shape[0])):
                held = stack[k] if held is None else add(stack[k], along(held, COLS, -1))
        return held

    def everywhere(value, axes):
        count = lax.axis_size(axes)
        copies = jnp.broadcast_to(value[None], (count, *value.shape))
        return lax.all_to_all(copies, axes, 0, 0, tiled=True)

    rows_dev = w_up.shape[0]
    hidden_cols = w_up.shape[1] // halves
    head_cols = 4 * w_out.shape[0] // halves
    packed_cols = head_cols + 2 * hidden_cols
    sides = [shaped((rows_dev, cols), bf16) for cols in (head_cols, 2 * hidden_cols)]
    shards = call(
        functools.partial(pack_kernel, halves),
        (place, w_qkv, w_out, w_up, w_down),
        sides + [shaped((rows_dev, packed_cols), bf16)] * (halves - 1),
        time=2.4,
        in_specs=[smem] + [vmem] * 4,
    )
    if halves == 2:
        other = swap(shards[2])
        cuts = (0, head_cols, packed_cols)
        shards = [
            in_order(own, other[:, first:last], 0)
            for own, first, last in zip(shards, cuts, cuts[1:])
        ]
    head_shard, hidden_shard = shards[:2]
    attn_full = lax.all_gather(head_shard, COLS, axis=0, tiled=False)
    hidden_w = gather_pieces(hidden_shard)
    hidden_flat = [piece for group in hidden_w for piece in group]

    small, = call(
        small_kernel,
        (ssm_param.reshape(2 * states, -1), norm_gains),
        (shaped((2 * states + 2, norm_gains.shape[1]), f32),),
        after=hidden_w[0][1:-1],
    )
    small = jnp.transpose(everywhere(small, ALL), (1, 0, 2)).reshape(2 * states + 2, width)
    own_ssm = lax.dynamic_slice_in_dim(
        small[: 2 * states].reshape(2, states, width), rank * channels, channels, 2
    )
    coef, logr = own_ssm[0], own_ssm[1]
    gain_one = small[2 * states : 2 * states + 1]
    gain_two = small[2 * states + 1 : 2 * states + 2]

    x, unused = pick_block(tokens)
    cot, cot_other = pick_block(cotangent)

    anywhere = [pl.BlockSpec(memory_space=pl.ANY)]

    def fixed(*shape):
        return pl.BlockSpec(shape, lambda z: (0,) * len(shape))

    wide = fixed(length, width)
    row = fixed(1, width)

    normed_one, normed_t, u_steps, ends, total = call(
        norm_kernel,
        (place, x, gain_one, logr),
        (
            shaped((length, width), bf16),
            shaped((width, length), bf16),
            shaped((tiles, length, LANES), f32),
            shaped((states, SUBS, channels), f32),
            shaped((states, channels), f32),
        ),
        scratch=[pltpu.VMEM((length, LANES), f32)],
        in_specs=[smem, vmem, vmem, vmem],
        after=(hidden_w[1][0], *cot_other),
        time=5,
    )
    (attn_full,) = hold((attn_full,), (total,))
    attn_w = [
        *double_rows(attn_full[: col_parts // 2], bits),
        *double_rows(attn_full[col_parts // 2 :], bits[::-1]),
    ]
    totals = everywhere(total.astype(bf16), ("sh", "mq"))
    (context_own,) = call(
        context_kernel,
        (place, u_steps, ends, totals, logr, coef),
        (shaped((length, channels), bf16),),
        after=(hidden_w[0][-1], *hidden_w[1][1:-1], hidden_w[-1][0], *attn_w[1 : row_parts - 1]),
        scratch=[pltpu.VMEM((tiles, length, LANES), f32), pltpu.VMEM((length, LANES), f32)],
        in_specs=[smem] + [vmem] * 5,
        time=7,
    )
    contexts = team_send([context_own] * team)

    stack_shape = (row_parts // 2, col_parts // 2, row_count)
    head_stacks = [shaped((*stack_shape, head_cols), bf16)] * 4
    hidden_stacks = [shaped((*stack_shape, hidden_cols), bf16)] * 8
    sizes = (team, col_parts, row_parts)
    head_buffer = pltpu.VMEM((col_parts, row_parts, row_count, 4 * HD), bf16)
    head_sems = pltpu.SemaphoreType.DMA((col_parts, row_parts))
    kept_shape = shaped((3, length, col_parts * HD), bf16)
    flat_shape = shaped((length, col_parts * HD), bf16)
    context_t, cot_t, kept = call(
        functools.partial(project_kernel, *sizes),
        (place, normed_one, cot, *contexts, *attn_w),
        (shaped((width, length), bf16), shaped((width, length), bf16), kept_shape),
        scratch=[pltpu.VMEM((length, width), bf16), head_buffer, head_sems],
        time=1,
        in_specs=[smem] + [vmem] * (2 + team) + anywhere * len(attn_w),
        after=(hidden_w[1][-1], *[piece for group in hidden_w[2:3] for piece in group[1:]]),
    )
    attn_part, attended, probs, probs_t = call(
        functools.partial(attend_kernel, *sizes),
        (place, kept, *attn_w),
        (
            shaped((length, width), bf16),
            flat_shape,
            *[shaped((col_parts, length, length), bf16)] * 2,
        ),
        scratch=[head_buffer, head_sems],
        time=1,
        in_specs=[smem, vmem] + anywhere * len(attn_w),
        after=[piece for group in hidden_w[3:] for piece in group[1:-1]],
    )
    attn_parts = team_send([attn_part] * team)

    middle, normed_two, normed_two_t = call(
        functools.partial(middle_kernel, team),
        (x, gain_two, *attn_parts),
        (shaped((length, width), f32), shaped((length, width), bf16), shaped((width, length), bf16)),
        time=1,
    )
    weight_buffer = pltpu.VMEM((row_parts, row_count, col_parts * hidden_cols), bf16)
    grad_buffer = pltpu.VMEM((col_parts, row_parts, row_count, hidden_cols), bf16)
    fed = call(
        functools.partial(feed_kernel, team, col_parts, row_parts),
        (place, normed_two, normed_two_t, cot, cot_t, *hidden_flat),
        (
            *[shaped((own_rows, width), bf16)] * team,
            shaped((length, width), bf16),
            *hidden_stacks,
        ),
        scratch=[
            *[weight_buffer] * 2,
            *[grad_buffer] * 2,
            *[pltpu.VMEM((length, col_parts * hidden_cols), bf16)] * 2,
            pltpu.SemaphoreType.DMA((4, col_parts, row_parts)),
        ],
        time=18,
        grid=(col_parts,),
        in_specs=[smem, wide, fixed(width, length), wide, fixed(width, length)]
        + anywhere * len(hidden_flat),
        out_specs=[fixed(own_rows, width)] * team + [wide] + anywhere * 8,
    )
    out_pieces, two_part, hidden_grads = fed[:team], fed[team], fed[team + 1 :]
    two_parts = team_send([two_part] * team)

    def rows_of(array, member):
        return lax.dynamic_slice_in_dim(array, member * own_rows, own_rows, 0)

    def share_rows(pieces, kind):
        others = []
        if halves == 2:
            pairs = pieces.reshape(seq_total, halves, own_rows, width)
            others = [swap(lax.dynamic_index_in_dim(pairs, 1 - sl, 1, keepdims=False))]
        (blocks,) = call(
            functools.partial(assemble_kernel, halves, low_count),
            (place, pieces, *others),
            (shaped((seq_total, length, width), kind),),
            time=3.5,
            in_specs=[smem, vmem] + [vmem] * len(others),
        )
        return blocks

    out_pieces = team_send(list(out_pieces))
    result = rows_of(middle, rank) + sum(item.astype(f32) for item in out_pieces)
    result = result.astype(bf16)
    layer_pieces = lax.all_gather(result, MODEL, axis=0, tiled=False)
    layer_out = share_rows(layer_pieces, bf16)

    def both_halves(own):
        if halves == 1:
            return [own]
        return [own, swap(lax.dynamic_slice_in_dim(own, (1 - sl) * rows_dev, rows_dev, 0))]

    middle_grad, gain_two_grad, one_part, low_grad, *rest = call(
        functools.partial(attend_back_kernel, *sizes),
        (place, middle, gain_two, cot, *two_parts, kept, probs, probs_t, *attn_w),
        (
            shaped((own_rows, width), f32),
            shaped((1, width), f32),
            shaped((length, width), bf16),
            shaped((length, width), bf16),
            *[flat_shape] * 3,
            *[shaped((length, channels), bf16)] * team,
        ),
        scratch=[
            head_buffer,
            pltpu.VMEM(flat_shape.shape, bf16),
            pltpu.VMEM((length, width), bf16),
            pltpu.VMEM(kept_shape.shape, bf16),
            *[pltpu.VMEM((col_parts, length, length), bf16)] * 2,
            head_sems,
            pltpu.SemaphoreType.DMA((3,)),
        ],
        time=1,
        in_specs=[smem] + [vmem] * (3 + team) + anywhere * (3 + len(attn_w)),
        after=(result,),
    )
    head_grads, context_grads = rest[:3], rest[3:]
    context_grads = team_send(context_grads)
    head_stacks = call(
        functools.partial(head_grads_kernel, col_parts, row_parts),
        (place, low_grad, attended, normed_t, context_t, *head_grads),
        head_stacks,
        scratch=[head_buffer, head_sems],
        time=1,
        in_specs=[smem] + [vmem] * 7,
        out_specs=anywhere * 4,
    )
    down_first = first_messages(hidden_grads[4:])
    g_steps, adjoint_ends, adjoint_total, adjoint_done = call(
        functools.partial(adjoint_kernel, team),
        (logr, *context_grads),
        (
            shaped((tiles, length, LANES), f32),
            shaped((2, states, SUBS, channels), f32),
            shaped((2, states, channels), f32),
        ),
        scratch=[pltpu.VMEM((length, LANES), f32)],
        time=1,
        after=(*down_first, head_stacks[0]),
        token=True,
    )
    adjoint_totals = everywhere(adjoint_total.astype(bf16), ("sh", "mq"))
    down_second = second_messages(hidden_grads[4:], down_first, adjoint_done)
    down_second = hold(down_second, (adjoint_totals,))
    up_stacks = list(hidden_grads[:4])
    up_stacks[1::2] = hold(up_stacks[1::2], (adjoint_totals,))
    up_first = first_messages(up_stacks)
    *one_pieces, grad_ssm = call(
        functools.partial(context_back_kernel, team),
        (place, g_steps, u_steps, adjoint_ends, adjoint_totals, logr, coef, one_part),
        (
            *[shaped((own_rows, width), bf16)] * team,
            shaped((2, states, channels), f32),
        ),
        scratch=[
            pltpu.VMEM((tiles, length, LANES), f32),
            pltpu.VMEM((length, width), f32),
            pltpu.VMEM((length, LANES), f32),
        ],
        in_specs=[smem] + [vmem] * 7,
        time=1,
        after=(*down_second, *up_stacks[1::2]),
    )
    one_pieces = team_send(one_pieces)
    down_parts = halve_both(hidden_grads[4:], down_first, down_second)
    grad_rows, gain_one_grad, rows_done = call(
        functools.partial(input_grad_kernel, team),
        (place, x, gain_one, middle_grad, *one_pieces),
        (shaped((own_rows, width), bf16), shaped((1, width), f32)),
        in_specs=[smem] + [vmem] * (3 + team),
        time=1,
        after=(layer_pieces, *[parts[-1] for parts in down_parts]),
        token=True,
    )
    down_sums = [add(*parts, zero=rows_done) for parts in down_parts]
    up_second = second_messages(up_stacks, up_first, rows_done)
    up_sums = [add(*parts) for parts in halve_both(up_stacks, up_first, up_second)]
    head_stacks = list(head_stacks)
    head_stacks[1::2] = hold(head_stacks[1::2], (grad_rows,))
    head_first = first_messages(head_stacks)
    head_second = second_messages(head_stacks, head_first, rows_done)
    head_sums = [add(*parts) for parts in halve_both(head_stacks, head_first, head_second)]
    grad_down = sum_over_z(*down_sums)
    grad_up = sum_over_z(*up_sums)
    grad_heads = sum_over_z(*head_sums)
    input_grad = share_rows(lax.all_gather(grad_rows, MODEL, axis=0, tiled=False), f32)

    placed_ssm = lax.dynamic_update_slice_in_dim(
        jnp.zeros((2 * states, width), f32),
        grad_ssm.reshape(2 * states, channels),
        rank * channels,
        1,
    )
    small_grads = jnp.concatenate([placed_ssm, gain_one_grad, gain_two_grad], 0)
    (small_grads,) = hold((small_grads,), head_sums)
    small_grads = small_grads.reshape(2 * states + 2, lax.axis_size(ALL), -1)
    small_grads = lax.all_to_all(jnp.transpose(small_grads, (1, 0, 2)), ALL, 0, 0, tiled=True)
    small_grads = jnp.sum(small_grads, axis=0)

    def moments(matrices, grads, arrays, after=()):
        changed = [shaped(old.shape, f32) for group in arrays for old in group]
        grad_parts = [part for grad in grads for part in both_halves(grad)]
        ins = [item for group in arrays for item in group]
        *found, sums = call(
            functools.partial(moments_kernel, halves, matrices),
            (place, *grad_parts, *ins),
            (*changed, shaped((2, LANES), f32)),
            in_specs=[smem] + [vmem] * (len(grad_parts) + len(ins)),
            after=after,
            time=4,
        )
        return [found[3 * i : 3 * i + 3] for i in range(len(arrays))], sums

    hidden_new, hidden_sums = moments(
        ((4, 0, 0, False, None), (5, 1, 0, True, None)),
        (grad_up, grad_down),
        ((w_up, first_up, second_up), (w_down, first_down, second_down)),
    )
    heads_new, head_sums = moments(
        tuple((i, 0, i, False, i) for i in range(3)) + ((3, 0, 3, True, None),),
        (grad_heads,),
        ((w_qkv, first_qkv, second_qkv), (w_out, first_out, second_out)),
        (layer_out, input_grad),
    )
    own_channels = norm_gains.shape[1]
    ssm_items = [item.reshape(2 * states, own_channels) for item in (ssm_param, first_ssm, second_ssm)]
    small_items = [norm_gains, first_gain, second_gain, *ssm_items]
    *small_new, small_sums = call(
        functools.partial(small_moments_kernel, (6, 8)),
        (small_grads.reshape(2 * states + 2, own_channels), *small_items),
        (*[shaped(item.shape, f32) for item in small_items], shaped((2, LANES), f32)),
    )
    all_sums = everywhere(hidden_sums + head_sums + small_sums, ALL)
    masters = (w_qkv, w_out, w_up, w_down, norm_gains, ssm_items[0])
    news = (*heads_new, *hidden_new, small_new[:3], small_new[3:])
    *weights, norms = call(
        functools.partial(update_kernel, ((0, 1, 2), (3,), (4,), (5,), (6, 7), (8, 9))),
        (all_sums, *masters, *[group[2] for group in news]),
        (*[shaped(item.shape, f32) for item in masters], shaped((2, LANES), f32)),
        time=3.2,
    )
    outputs = [layer_out, input_grad]
    for index, (weight, (first_new, second_new, unused)) in enumerate(zip(weights, news)):
        if index == 4:
            outputs += [weight, first_new, second_new[0], second_new[1]]
        else:
            kept_shape = ssm_param.shape if index == 5 else weight.shape
            outputs += [item.reshape(kept_shape) for item in (weight, first_new, second_new)]
    outputs.append(norms[:, :10])
    return tuple(outputs)


def solution(mesh):
    seq_count, model_count = mesh.shape["seq"], mesh.shape["mp"]
    halves = 2 if HEADS // model_count >= 2 else 1
    sizes = (seq_count // halves, halves, SEQS, halves, model_count // (SEQS * halves))
    fine = Mesh(mesh.devices.reshape(sizes), ALL)
    seq, model = ("sh", "sl"), ("mb", "mq", "ml")
    rows_cols, cols_rows = P(seq, model), P(model, seq)
    token = P(None, seq, None)
    stack = P(None, seq, model)
    gains = P(None, ALL)
    ssm = P(None, None, ALL)
    return jax.shard_map(
        on_device,
        mesh=fine,
        in_specs=(token, token, stack, cols_rows, rows_cols, cols_rows, gains, ssm)
        + (stack,) * 2
        + (cols_rows,) * 2
        + (rows_cols,) * 2
        + (cols_rows,) * 2
        + (gains,) * 2
        + (ssm,) * 2,
        out_specs=(token, token)
        + (stack,) * 3
        + (cols_rows,) * 3
        + (rows_cols,) * 3
        + (cols_rows,) * 3
        + (gains, gains, P(ALL), P(ALL))
        + (ssm,) * 3
        + (P(),),
        check_vma=False,
    )
```

```python
import functools
import math

import jax
import jax.numpy as jnp
from jax import lax
from jax.experimental import pallas as pl
from jax.experimental.pallas import tpu as pltpu
from jax.sharding import Mesh
from jax.sharding import PartitionSpec as P

HD = 128
HEADS = 8
BLK = 512
STEP = 10
SEQS = 2
LANES = 128
SUBS = 8
GROUP = 8

norm_eps = 1e-05
beta_first = 0.9
beta_second = 0.999
lamb_eps = 1e-06
weight_decay = 0.01
learn_rate = 0.5
score_scale = HD ** (-0.5)

f32 = jnp.float32
bf16 = jnp.bfloat16
VMEM_BYTES = 56 * 1024 * 1024

ALL = ("sh", "sl", "mb", "mq", "ml")
MODEL = ("mb", "mq", "ml")
COLS = ("mb", "mq")
TEAM = ("sl", "ml")


def dot(left, right):
    return lax.dot_general(left, right, (((1,), (0,)), ((), ())), preferred_element_type=f32)


def dot_t(left, right):
    return lax.dot_general(left, right, (((1,), (1,)), ((), ())), preferred_element_type=f32)


def normalise(values):
    centred = values - jnp.mean(values, axis=-1, keepdims=True)
    inverse = lax.rsqrt(jnp.mean(centred * centred, axis=-1, keepdims=True) + norm_eps)
    return centred * inverse, inverse


def normalise_back(unit, inverse, grad_unit):
    mean_one = jnp.mean(grad_unit, axis=-1, keepdims=True)
    mean_two = jnp.mean(grad_unit * unit, axis=-1, keepdims=True)
    return inverse * (grad_unit - mean_one - unit * mean_two)


def sub_index():
    return lax.broadcasted_iota(jnp.int32, (SUBS, LANES), 0)


def spread(row):
    return jnp.broadcast_to(row, (SUBS, LANES))


def lane_tile(index):
    return slice(index * LANES, (index + 1) * LANES)


def no_state(tiles):
    rows = tiles[0, :SUBS, :]
    return rows - rows


def in_steps(steps, tile, rows):
    span = rows.shape[0] // SUBS

    def move(i, unused):
        steps[tile, pl.ds(pl.multiple_of(i * SUBS, SUBS), SUBS), :] = rows[
            pl.ds(i, SUBS, stride=span), :
        ]
        return unused

    lax.fori_loop(0, span, move, 0, unroll=8)


def from_steps(rows, steps, tile):
    span = rows.shape[0] // SUBS

    def move(i, unused):
        rows[pl.ds(i, SUBS, stride=span), :] = steps[
            tile, pl.ds(pl.multiple_of(i * SUBS, SUBS), SUBS), :
        ]
        return unused

    lax.fori_loop(0, span, move, 0, unroll=8)


def step_rows(i):
    return pl.ds(pl.multiple_of(i * SUBS, SUBS), SUBS)


def norm_kernel(
    place, x_ref, gain_ref, logr_ref, normed_ref, turned_ref, u_tiles, ends_ref, total_ref, rows
):
    unit, unused = normalise(x_ref[...].astype(f32))
    normed_ref[...] = (unit * gain_ref[...]).astype(bf16)
    turned_ref[...] = normed_ref[...].T
    tiles, length, unused = u_tiles.shape
    states = logr_ref.shape[0]
    span = length // SUBS
    for tile in range(tiles):
        start = place[0] * (tiles * LANES) + tile * LANES
        rows[...] = normed_ref[:, pl.ds(pl.multiple_of(start, LANES), LANES)].astype(f32)
        in_steps(u_tiles, tile, rows)
    left = ((SUBS - 1 - sub_index()) * span).astype(f32)
    for tile in range(tiles):
        rate = jnp.exp(logr_ref[:, lane_tile(tile)])
        decay = jnp.exp(-rate)
        decays = [spread(decay[n : n + 1]) for n in range(states)]

        def step(i, held):
            u = u_tiles[tile, step_rows(i), :]
            return tuple(d * h + u for d, h in zip(decays, held))

        zero = no_state(u_tiles)
        held = lax.fori_loop(0, span, step, (zero,) * states, unroll=4)
        for n in range(states):
            ends_ref[n, :, lane_tile(tile)] = held[n]
            total_ref[n : n + 1, lane_tile(tile)] = jnp.sum(
                held[n] * jnp.exp(-left * rate[n : n + 1]), axis=0, keepdims=True
            )


def context_kernel(
    place, u_tiles, ends_ref, all_ref, logr_ref, coef_ref, context_ref, y_tiles, rows
):
    tiles, length, unused = u_tiles.shape
    states = logr_ref.shape[0]
    span = length // SUBS
    index = sub_index()
    before = (index * span).astype(f32)
    for tile in range(tiles):
        rate = jnp.exp(logr_ref[:, lane_tile(tile)])
        decay = jnp.exp(-rate)
        scale = coef_ref[:, lane_tile(tile)] * jnp.sqrt(2.0 * rate)
        incoming = jnp.zeros((states, LANES), f32)
        for j in range(all_ref.shape[0]):
            gap = place[1] - 1 - j
            distance = (jnp.maximum(gap, 0) * length).astype(f32)
            term = jnp.exp(-distance * rate) * all_ref[j, :, lane_tile(tile)].astype(f32)
            incoming = incoming + jnp.where(gap >= 0, term, 0.0)
        for first in range(0, states, GROUP):
            chosen = range(first, first + GROUP)
            starts = []
            for n in chosen:
                row = rate[n : n + 1]
                run = ends_ref[n, :, lane_tile(tile)]
                for d in (1, 2, 4):
                    moved = jnp.exp(-(d * span) * row) * pltpu.roll(run, d, 0)
                    run = run + jnp.where(index >= d, moved, 0.0)
                run = jnp.where(index >= 1, pltpu.roll(run, 1, 0), 0.0)
                starts.append(run + jnp.exp(-before * row) * incoming[n : n + 1])
            decays = [spread(decay[n : n + 1]) for n in chosen]
            scales = [spread(scale[n : n + 1]) for n in chosen]

            def step(i, held):
                at = step_rows(i)
                u = u_tiles[tile, at, :]
                held = tuple(d * h + u for d, h in zip(decays, held))
                parts = [s * h for s, h in zip(scales, held)]
                if first > 0:
                    parts[0] = parts[0] + y_tiles[tile, at, :]
                while len(parts) > 1:
                    parts = [a + b for a, b in zip(parts[::2], parts[1::2])]
                y_tiles[tile, at, :] = parts[0]
                return held

            lax.fori_loop(0, span, step, tuple(starts), unroll=4)
        from_steps(rows, y_tiles, tile)
        context_ref[:, lane_tile(tile)] = rows[...].astype(bf16)


def whole_rows(block):
    return block.reshape(block.shape[0] * block.shape[1], block.shape[2])


def head(index):
    return slice(index * HD, (index + 1) * HD)


def weight_copies(near, far, buffer, place, sems, act):
    count = sems.shape[0]
    half = count // 2
    for k in range(count):
        owner = lax.rem(place[6] + count - k, count)
        for stacks, low in ((near, 0), (far, half)):

            @pl.when((owner >= low) & (owner < low + half))
            def move():
                for r, stack in enumerate(stacks):
                    inner = buffer.at[k, place[2] ^ r]
                    act(pltpu.make_async_copy(stack.at[owner - low], inner, sems.at[k, r]))


def of_heads(buffer, i):
    return jnp.concatenate([whole_rows(buffer[k, :, :, head(i)]) for k in range(buffer.shape[0])], axis=1)


def gradient_slot(row_parts, order, r):
    position = 0
    for bit in reversed(order):
        position = 2 * position + (1 if r & bit else 0)
    return position // (row_parts // 2), position % (row_parts // 2)


def round_orders(row_parts):
    bits = [1 << i for i in range(row_parts.bit_length() - 1)]
    return bits, bits[::-1]


def gradient_pieces(stacks, row_parts, far, slot):
    found = []
    for r in range(row_parts):
        sent, at = gradient_slot(row_parts, round_orders(row_parts)[far], r)
        found.append(stacks[2 * far + sent].at[at, slot])
    return found


def project_kernel(team, col_parts, row_parts, place, normed_ref, cot_ref, *refs):
    contexts, refs = refs[:team], refs[team:]
    near, far, refs = refs[:row_parts], refs[row_parts : 2 * row_parts], refs[2 * row_parts :]
    context_t_ref, cot_t_ref, kept_ref = refs[:3]
    context_ref, weights, sems = refs[3:]
    weight_copies(near, far, weights, place, sems, lambda copy: copy.start())
    width = contexts[0].shape[1]
    for k in range(team):
        lanes = pl.ds(pl.multiple_of((place[0] ^ k) * width, LANES), width)
        context_ref[:, lanes] = contexts[k][...]
    context_t_ref[...] = context_ref[...].T
    cot_t_ref[...] = cot_ref[...].T
    weight_copies(near, far, weights, place, sems, lambda copy: copy.wait())
    kept_ref[0] = dot(normed_ref[...], of_heads(weights, 0)).astype(bf16)
    kept_ref[1] = dot(context_ref[...], of_heads(weights, 1)).astype(bf16)
    kept_ref[2] = dot(context_ref[...], of_heads(weights, 2)).astype(bf16)


def attend_kernel(team, col_parts, row_parts, place, kept_ref, *refs):
    near, far, refs = refs[:row_parts], refs[row_parts : 2 * row_parts], refs[2 * row_parts :]
    part_ref, attended_ref, probs_ref, probs_t_ref, weights, sems = refs
    weight_copies(near, far, weights, place, sems, lambda copy: copy.start())
    length = kept_ref.shape[1]
    rows = lax.broadcasted_iota(jnp.int32, (length, length), 0)
    cols = lax.broadcasted_iota(jnp.int32, (length, length), 1)
    for h in range(col_parts):
        scores = dot_t(kept_ref[0, :, head(h)], kept_ref[1, :, head(h)]) * score_scale
        scores = jnp.where(rows >= cols, scores, -1e30)
        shifted = jnp.exp(scores - jnp.max(scores, axis=-1, keepdims=True))
        inverse = 1.0 / jnp.sum(shifted, axis=-1, keepdims=True)
        probs = (shifted * inverse).astype(bf16)
        probs_ref[h] = probs
        probs_t_ref[h] = probs.T
        attended_ref[:, head(h)] = dot(probs, kept_ref[2, :, head(h)]).astype(bf16)
    weight_copies(near, far, weights, place, sems, lambda copy: copy.wait())
    part_ref[...] = dot_t(attended_ref[...], of_heads(weights, 3)).astype(bf16)


def gelu_parts(hidden, grad_act):
    density = jnp.exp(-0.5 * hidden * hidden)
    t = 1.0 / (1.0 + (0.3275911 * math.sqrt(0.5)) * jnp.abs(hidden))
    series = 0.5 * 1.061405429
    for factor in (-1.453152027, 1.421413741, -0.284496736, 0.254829592):
        series = series * t + 0.5 * factor
    tail = series * t * density
    cdf = jnp.where(hidden >= 0.0, 1.0 - tail, tail)
    slope = cdf + hidden * density * (1.0 / math.sqrt(2.0 * math.pi))
    return (hidden * cdf).astype(bf16), (grad_act * slope).astype(bf16)


def middle_kernel(team, x_ref, gain_ref, *refs):
    parts, (middle_ref, normed_ref, normed_t_ref) = refs[:team], refs[team:]
    attn = parts[0][...].astype(f32)
    for part in parts[1:]:
        attn = attn + part[...].astype(f32)
    middle = x_ref[...].astype(f32) + attn
    middle_ref[...] = middle
    unit, unused = normalise(middle)
    normed_ref[...] = (unit * gain_ref[...]).astype(bf16)
    normed_t_ref[...] = normed_ref[...].T


def feed_kernel(team, col_parts, row_parts, place, normed_ref, normed_t_ref, cot_ref, cot_t_ref, *refs):
    count = col_parts * row_parts
    pieces, refs = refs[:count], refs[count:]
    outs, two_ref, refs = refs[:team], refs[team], refs[team + 1 :]
    stacks, refs = (refs[:4], refs[4:8]), refs[8:]
    up_all, down_all, grad_up, grad_down, activated_all, grad_all, sems = refs
    z = pl.program_id(0)
    half = col_parts // 2
    hidden_cols = grad_up.shape[3]

    def copies(k):
        found = []
        for r in range(row_parts):
            for which, buffer in enumerate((up_all, down_all)):
                outside = pieces[k * row_parts + r].at[:, pl.ds(which * hidden_cols, hidden_cols)]
                inside = buffer.at[place[2] ^ r, :, pl.ds(k * hidden_cols, hidden_cols)]
                found.append(pltpu.make_async_copy(outside, inside, sems.at[which, k, r]))
        return found

    def each_leaving(k, act):
        for which, buffer in enumerate((grad_up, grad_down)):
            steps = k if which == 0 else lax.rem(place[6] + col_parts - k, col_parts)
            for far in range(2):

                @pl.when(steps // half == far)
                def leaves():
                    slot = lax.rem(steps, half)
                    for r, piece in enumerate(gradient_pieces(stacks[which], row_parts, far, slot)):
                        inner = buffer.at[k, place[2] ^ r]
                        act(pltpu.make_async_copy(inner, piece, sems.at[2 + which, k, r]))

    @pl.when(z == 0)
    def start():
        for k in range(col_parts):
            for copy in copies(k):
                copy.start()

    for k in range(col_parts):

        @pl.when(z == k)
        def arrive():
            for copy in copies(k):
                copy.wait()

    at = pl.ds(pl.multiple_of(z * hidden_cols, hidden_cols), hidden_cols)
    hidden = dot(normed_ref[...], whole_rows(up_all[:, :, at]))
    grad_act = dot(cot_ref[...], whole_rows(down_all[:, :, at]))
    activated, grad_pre = gelu_parts(hidden, grad_act)
    activated_all[:, at] = activated
    grad_all[:, at] = grad_pre
    shape = grad_up.shape[1:]
    grad_up[z] = dot(normed_t_ref[...], grad_pre).astype(bf16).reshape(shape)
    grad_down[z] = dot(cot_t_ref[...], activated).astype(bf16).reshape(shape)

    for k in range(col_parts):

        @pl.when(z == k)
        def leave():
            each_leaving(k, lambda copy: copy.start())

    @pl.when(z == col_parts - 1)
    def finish():
        two_ref[...] = dot_t(grad_all[...], whole_rows(up_all[...])).astype(bf16)
        rows = outs[0].shape[0]
        for k in range(team):
            at_rows = pl.ds(pl.multiple_of((place[0] ^ k) * rows, rows), rows)
            outs[k][...] = dot_t(activated_all[at_rows, :], whole_rows(down_all[...])).astype(bf16)
        for k in range(col_parts):
            each_leaving(k, lambda copy: copy.wait())


def attend_back_kernel(team, col_parts, row_parts, place, middle_ref, gain_ref, cot_ref, *refs):
    parts, refs = refs[:team], refs[team:]
    late, refs = refs[:3], refs[3:]
    near, far, refs = refs[:row_parts], refs[row_parts : 2 * row_parts], refs[2 * row_parts :]
    middle_grad_ref, gain_grad_ref, one_ref, low = refs[:4]
    grad_q, grad_k, grad_v = refs[4:7]
    context_grads, refs = refs[7 : 7 + team], refs[7 + team :]
    weights, grad_out, total_low = refs[:3]
    held, (sems, late_sems) = refs[3:6], refs[6:]
    kept_ref, probs_ref, probs_t_ref = held
    weight_copies(near, far, weights, place, sems, lambda copy: copy.start())
    late_copies = [
        pltpu.make_async_copy(outside, inside, late_sems.at[i])
        for i, (outside, inside) in enumerate(zip(late, held))
    ]
    for copy in late_copies:
        copy.start()
    own_rows = middle_ref.shape[0] // team
    grad_two = parts[0][...].astype(f32)
    for part in parts[1:]:
        grad_two = grad_two + part[...].astype(f32)
    unit, inverse = normalise(middle_ref[...])
    grad_gain = grad_two * unit
    rows = lax.broadcasted_iota(jnp.int32, grad_gain.shape, 0)
    first = place[0] * own_rows
    mine = (rows >= first) & (rows < first + own_rows)
    gain_grad_ref[...] = jnp.sum(jnp.where(mine, grad_gain, 0.0), axis=0, keepdims=True)
    grad = cot_ref[...].astype(f32) + normalise_back(unit, inverse, grad_two * gain_ref[...])
    low[...] = grad.astype(bf16)
    for k in range(team):

        @pl.when(place[0] == k)
        def own():
            middle_grad_ref[...] = grad[k * own_rows : (k + 1) * own_rows, :]

    weight_copies(near, far, weights, place, sems, lambda copy: copy.wait())
    for copy in late_copies:
        copy.wait()
    grad_out[...] = dot(low[...], of_heads(weights, 3)).astype(bf16)
    for h in range(col_parts):
        q, k, v = (kept_ref[i, :, head(h)] for i in range(3))
        grad_heads = grad_out[:, head(h)]
        grad_v[:, head(h)] = dot(probs_t_ref[h], grad_heads).astype(bf16)
        probs = probs_ref[h].astype(f32)
        grad_probs = dot_t(grad_heads, v)
        inner = jnp.sum(grad_probs * probs, axis=-1, keepdims=True)
        grad_scores = (probs * (grad_probs - inner)).astype(bf16)
        grad_q[:, head(h)] = (dot(grad_scores, k) * score_scale).astype(bf16)
        turned = dot_t(v, grad_heads) - inner.T
        turned = (probs_t_ref[h].astype(f32) * turned).astype(bf16)
        grad_k[:, head(h)] = (dot(turned, q) * score_scale).astype(bf16)
    total = dot_t(grad_k[...], of_heads(weights, 1)) + dot_t(grad_v[...], of_heads(weights, 2))
    total_low[...] = total.astype(bf16)
    width = context_grads[0].shape[1]
    for k in range(team):
        lanes = pl.ds(pl.multiple_of((place[0] ^ k) * width, LANES), width)
        context_grads[k][...] = total_low[:, lanes]
    one_ref[...] = dot_t(grad_q[...], of_heads(weights, 0)).astype(bf16)


def head_grads_kernel(col_parts, row_parts, place, low, attended_ref, *refs):
    normed_t_ref, context_t_ref, grad_q, grad_k, grad_v = refs[:5]
    stacks, (grads, out_sems) = refs[5:9], refs[9:]
    half = col_parts // 2
    shape = (*grads.shape[1:3], HD)

    def put(i, grad):
        for h in range(col_parts):
            grads[h, :, :, head(i)] = grad[:, head(h)].astype(bf16).reshape(shape)

    put(0, dot(normed_t_ref[...], grad_q[...]))
    put(1, dot(context_t_ref[...], grad_k[...]))
    put(2, dot(context_t_ref[...], grad_v[...]))
    put(3, dot(low[...].T, attended_ref[...]))
    copies = []
    for k in range(col_parts):
        for r, piece in enumerate(gradient_pieces(stacks, row_parts, k // half, k % half)):
            copies.append(pltpu.make_async_copy(grads.at[k, place[2] ^ r], piece, out_sems.at[k, r]))
    for copy in copies:
        copy.start()
    for copy in copies:
        copy.wait()


def adjoint_kernel(team, logr_ref, *refs):
    parts = refs[:team]
    g_tiles, ends_ref, total_ref, rows = refs[team:]
    grad = parts[0][...].astype(f32)
    for part in parts[1:]:
        grad = grad + part[...].astype(f32)
    grad = grad.astype(bf16).astype(f32)
    tiles, length, unused = g_tiles.shape
    states = logr_ref.shape[0]
    span = length // SUBS
    for tile in range(tiles):
        rows[...] = grad[:, lane_tile(tile)]
        in_steps(g_tiles, tile, rows)
    before = (sub_index() * span).astype(f32)
    for tile in range(tiles):
        rate = jnp.exp(logr_ref[:, lane_tile(tile)])
        decay = jnp.exp(-rate)
        for first in range(0, states, GROUP):
            chosen = range(first, first + GROUP)
            decays = [spread(decay[n : n + 1]) for n in chosen]

            def step(i, held):
                g = g_tiles[tile, step_rows(span - 1 - i), :]
                later = []
                for d, (b, w) in zip(decays, held):
                    shrunk = d * b
                    later.append((g + shrunk, d * w + shrunk))
                return tuple(later)

            zero = no_state(g_tiles)
            held = lax.fori_loop(0, span, step, ((zero, zero),) * GROUP, unroll=4)
            for n, (b, w) in zip(chosen, held):
                ends_ref[0, n, :, lane_tile(tile)] = b
                ends_ref[1, n, :, lane_tile(tile)] = w
                shrink = jnp.exp(-before * rate[n : n + 1])
                total_ref[0, n : n + 1, lane_tile(tile)] = jnp.sum(
                    shrink * b, axis=0, keepdims=True
                )
                total_ref[1, n : n + 1, lane_tile(tile)] = jnp.sum(
                    shrink * (w + before * b), axis=0, keepdims=True
                )


def context_back_kernel(
    team, place, g_tiles, u_tiles, ends_ref, all_ref, logr_ref, coef_ref, one_ref, *refs
):
    pieces = refs[:team]
    grad_ssm_ref, y_tiles, full, rows = refs[team:]
    tiles, length, unused = u_tiles.shape
    states = logr_ref.shape[0]
    span = length // SUBS
    width = tiles * LANES
    index = sub_index()
    after = ((SUBS - 1 - index) * span).astype(f32)
    full[...] = one_ref[...].astype(f32)
    group = GROUP
    for tile in range(tiles):
        lanes = lane_tile(tile)
        rate = jnp.exp(logr_ref[:, lanes])
        decay = jnp.exp(-rate)
        root = jnp.sqrt(2.0 * rate)
        scale = coef_ref[:, lanes] * root
        in_b = jnp.zeros((states, LANES), f32)
        in_w = jnp.zeros((states, LANES), f32)
        for j in range(all_ref.shape[0]):
            gap = j - place[1] - 1
            distance = (jnp.maximum(gap, 0) * length).astype(f32)
            shrink = jnp.exp(-distance * rate)
            b, w = all_ref[j, 0, :, lanes].astype(f32), all_ref[j, 1, :, lanes].astype(f32)
            in_b = in_b + jnp.where(gap >= 0, shrink * b, 0.0)
            in_w = in_w + jnp.where(gap >= 0, shrink * (w + distance * b), 0.0)
        for first in range(0, states, group):
            chosen = range(first, first + group)
            starts = []
            for n in chosen:
                row = rate[n : n + 1]
                b, w = ends_ref[0, n, :, lanes], ends_ref[1, n, :, lanes]
                for d in (1, 2, 4):
                    shrink = jnp.exp(-(d * span) * row)
                    next_b = pltpu.roll(b, SUBS - d, 0)
                    next_w = pltpu.roll(w, SUBS - d, 0)
                    inside = index < SUBS - d
                    b, w = (
                        b + jnp.where(inside, shrink * next_b, 0.0),
                        w + jnp.where(inside, shrink * (next_w + (d * span) * next_b), 0.0),
                    )
                inside = index < SUBS - 1
                b = jnp.where(inside, pltpu.roll(b, SUBS - 1, 0), 0.0)
                w = jnp.where(inside, pltpu.roll(w, SUBS - 1, 0), 0.0)
                shrink = jnp.exp(-after * row)
                b_row, w_row = in_b[n : n + 1], in_w[n : n + 1]
                b = b + shrink * b_row
                w = w + shrink * (w_row + after * b_row)
                zero = no_state(u_tiles)
                starts.append((b, w, zero, zero))
            decays = [spread(decay[n : n + 1]) for n in chosen]
            scales = [spread(scale[n : n + 1]) for n in chosen]

            def step(i, held):
                at = step_rows(span - 1 - i)
                g = g_tiles[tile, at, :]
                u = u_tiles[tile, at, :]
                later, parts = [], []
                for d, s, (b, w, sum_b, sum_w) in zip(decays, scales, held):
                    shrunk = d * b
                    w = d * w + shrunk
                    b = g + shrunk
                    later.append((b, w, sum_b + u * b, sum_w + u * w))
                    parts.append(s * b)
                while len(parts) > 1:
                    parts = [p + q for p, q in zip(parts[::2], parts[1::2])]
                if first > 0:
                    parts[0] = parts[0] + y_tiles[tile, at, :]
                y_tiles[tile, at, :] = parts[0]
                return tuple(later)

            held = lax.fori_loop(0, span, step, tuple(starts), unroll=2)
            for n, (unused_b, unused_w, sum_b, sum_w) in zip(chosen, held):
                sum_b = jnp.sum(sum_b, axis=0, keepdims=True)
                sum_w = jnp.sum(sum_w, axis=0, keepdims=True)
                row = slice(n, n + 1)
                grad_ssm_ref[0, row, lanes] = root[row] * sum_b
                grad_ssm_ref[1, row, lanes] = scale[row] * (0.5 * sum_b - rate[row] * sum_w)
        at_lanes = pl.ds(pl.multiple_of(place[0] * width + tile * LANES, LANES), LANES)
        from_steps(rows, y_tiles, tile)
        full[:, at_lanes] += rows[...].astype(bf16).astype(f32)
    count = pieces[0].shape[0]
    for k in range(team):
        at_rows = pl.ds(pl.multiple_of((place[0] ^ k) * count, count), count)
        pieces[k][...] = full[at_rows, :].astype(bf16)


def input_grad_kernel(team, place, x_ref, gain_ref, middle_grad_ref, *refs):
    parts, (out_ref, gain_grad_ref) = refs[:team], refs[team:]
    rows = out_ref.shape[0]
    at_rows = pl.ds(pl.multiple_of(place[0] * rows, rows), rows)
    grad_one = parts[0][...].astype(f32)
    for part in parts[1:]:
        grad_one = grad_one + part[...].astype(f32)
    unit, inverse = normalise(x_ref[at_rows, :].astype(f32))
    gain_grad_ref[...] = jnp.sum(grad_one * unit, axis=0, keepdims=True)
    back = normalise_back(unit, inverse, grad_one * gain_ref[...])
    out_ref[...] = (middle_grad_ref[...] + back).astype(bf16)


def assemble_kernel(halves, low_count, place, own_ref, *refs):
    others, out_ref = refs[:-1], refs[-1]
    count, rows, unused = own_ref.shape
    half = place[4]

    def put(value, sequence, which, member):
        at_rows = pl.ds(pl.multiple_of((which * low_count + member) * rows, rows), rows)
        out_ref[sequence, at_rows, :] = value.astype(out_ref.dtype)

    for sequence in range(count // (halves * low_count)):
        if halves == 1:
            for member in range(low_count):
                put(own_ref[sequence * low_count + member], sequence, 0, member)
        else:
            put(own_ref[sequence * halves + half], sequence, half, 0)
            put(others[0][sequence], sequence, 1 - half, 0)


def pack_kernel(halves, place, qkv_ref, out_ref, up_ref, down_ref, *refs):
    rows = up_ref.shape[0]
    heads, hidden = out_ref.shape[0] // halves, up_ref.shape[1] // halves
    for which in range(halves):
        side = place[4] if which == 0 else 1 - place[4]
        at_heads = pl.ds(pl.multiple_of(side * heads, LANES), heads)
        at_hidden = pl.ds(pl.multiple_of(side * hidden, LANES), hidden)
        if which == 0:
            head_ref = refs[0]
            wide_ref, deep_ref = refs[1].at[:, :hidden], refs[1].at[:, hidden:]
        else:
            packed = refs[2]
            head_ref = packed.at[:, : 4 * heads]
            wide_ref = packed.at[:, 4 * heads : 4 * heads + hidden]
            deep_ref = packed.at[:, 4 * heads + hidden :]
        for i in range(3):
            head_ref[:, i * heads : (i + 1) * heads] = qkv_ref[i, :, at_heads].astype(bf16)
        head_ref[:, 3 * heads :] = out_ref[at_heads, :].T.astype(bf16)
        wide_ref[...] = up_ref[:, at_hidden].astype(bf16)
        deep_ref[...] = down_ref[at_hidden, :].T.astype(bf16)


def small_kernel(ssm_ref, gains_ref, out_ref):
    count = ssm_ref.shape[0]
    out_ref[:count, :] = ssm_ref[...]
    out_ref[count:, :] = gains_ref[...]


def lamb_moments(weight, grad_item, first_old, second_old):
    first_new = beta_first * first_old + (1.0 - beta_first) * grad_item
    second_new = beta_second * second_old + (1.0 - beta_second) * grad_item * grad_item
    direction = (
        first_new
        / (1.0 - beta_first**STEP)
        / (jnp.sqrt(second_new / (1.0 - beta_second**STEP)) + lamb_eps)
        + weight_decay * weight
    )
    return (first_new, second_new, direction)


def place_sums(sums_ref, sums):
    rows = lax.broadcasted_iota(jnp.int32, sums_ref.shape, 0)
    lanes = lax.broadcasted_iota(jnp.int32, sums_ref.shape, 1)
    found = jnp.zeros(sums_ref.shape, f32)
    for index, pair in sums.items():
        for row, value in enumerate(pair):
            found = jnp.where((rows == row) & (lanes == index), value, found)
    sums_ref[...] = found


def moments_kernel(halves, matrices, place, *refs):
    count = 1 + max(item[1] for item in matrices)
    grads, refs = [refs[halves * i : halves * (i + 1)] for i in range(count)], refs[halves * count :]
    arrays = len({(item[1], item[4] is None) for item in matrices})
    ins = [refs[3 * i : 3 * i + 3] for i in range(arrays)]
    outs = [refs[3 * (arrays + i) : 3 * (arrays + i) + 3] for i in range(arrays)]
    sums_ref = refs[6 * arrays]
    keys = []
    sums = {}
    for number, source, column, turned, stacked in matrices:
        key = (source, stacked is None)
        if key not in keys:
            keys.append(key)
        pick = (lambda ref: ref) if stacked is None else (lambda ref, i=stacked: ref.at[i])
        weight, first, second = (pick(ref) for ref in ins[keys.index(key)])
        news = [pick(ref) for ref in outs[keys.index(key)]]
        width = weight.shape[0 if turned else 1] // halves
        rows = weight.shape[1 if turned else 0]
        cols = slice(column * width, (column + 1) * width)
        total_weight = total_update = 0.0
        for which, grad_ref in enumerate(grads[source]):
            side = place[4] if which == 0 else 1 - place[4]
            at = pl.ds(pl.multiple_of(side * width, width), width)
            if which == 0:
                grad = grad_ref[pl.ds(pl.multiple_of(side * rows, rows), rows), cols].astype(f32)
            else:
                grad = grad_ref[:, cols].astype(f32)
            at = (at, slice(None)) if turned else (slice(None), at)
            grad = grad.T if turned else grad
            old = weight[at]
            found = lamb_moments(old, grad, first[at], second[at])
            for ref, value in zip(news, found):
                ref[at] = value
            total_weight = total_weight + jnp.sum(old * old)
            total_update = total_update + jnp.sum(found[2] * found[2])
        sums[number] = (total_weight, total_update)
    place_sums(sums_ref, sums)


def small_moments_kernel(numbers, grads_ref, *refs):
    ins, outs, sums_ref = (refs[:3], refs[3:6]), (refs[6:9], refs[9:12]), refs[12]
    states = (grads_ref.shape[0] - 2) // 2
    sums = {}
    for (weight, first, second), news, start, rows, first_number in (
        (ins[0], outs[0], 2 * states, 1, numbers[0]),
        (ins[1], outs[1], 0, states, numbers[1]),
    ):
        for i in range(2):
            grad = grads_ref[start + i * rows : start + (i + 1) * rows, :]
            at = slice(i * rows, (i + 1) * rows)
            found = lamb_moments(weight[at, :], grad, first[at, :], second[at, :])
            for ref, value in zip(news, found):
                ref[at, :] = value
            sums[first_number + i] = (
                jnp.sum(weight[at, :] * weight[at, :]),
                jnp.sum(found[2] * found[2]),
            )
    place_sums(sums_ref, sums)


def update_kernel(stacks, sums_ref, *refs):
    count = len(stacks)
    weights, directions, news = refs[:count], refs[count : 2 * count], refs[2 * count : 3 * count]
    norms = jnp.sqrt(jnp.sum(sums_ref[...], axis=0))
    refs[3 * count][...] = norms
    ratios = norms[0:1] / norms[1:2]
    lanes = lax.broadcasted_iota(jnp.int32, ratios.shape, 1)
    for numbers, weight, direction, new in zip(stacks, weights, directions, news):
        step = weight.shape[0] // len(numbers)
        for i, number in enumerate(numbers):
            ratio = jnp.sum(jnp.where(lanes == number, ratios, 0.0), axis=1, keepdims=True)
            at = slice(i * step, (i + 1) * step)
            scale = learn_rate * ratio.reshape((1,) * weight.ndim)
            new[at] = weight[at] - scale * direction[at]


def call(
    body, ins, outs, scratch=(), grid=None, in_specs=None, out_specs=None, time=1.0, after=(), token=False
):
    moved = sum(a.size * a.dtype.itemsize for a in list(ins) + list(outs))
    params = pltpu.CompilerParams(vmem_limit_bytes=VMEM_BYTES)
    cost = pl.CostEstimate(flops=int(time * 1.15e9), bytes_accessed=moved, transcendentals=0)
    whole = pl.BlockSpec(memory_space=pltpu.VMEM)
    anywhere = pl.BlockSpec(memory_space=pl.ANY)
    in_specs = list(in_specs or [whole] * len(ins)) + [anywhere] * len(after)
    out_specs = list(out_specs or [whole] * len(outs))
    outs = list(outs)
    first_out = len(ins) + len(after)
    last_out = first_out + len(outs)
    if token:
        outs.append(jax.ShapeDtypeStruct((SUBS, LANES), f32))
        out_specs.append(whole)

    def run(*refs):
        refs = list(refs)
        if token:
            refs[last_out][...] = jnp.zeros((SUBS, LANES), f32)
            del refs[last_out]
        body(*refs[: len(ins)], *refs[first_out:])

    return pl.pallas_call(
        run,
        out_shape=tuple(outs),
        in_specs=in_specs,
        out_specs=tuple(out_specs),
        scratch_shapes=list(scratch),
        compiler_params=params,
        cost_estimate=cost,
        **({} if grid is None else {"grid": grid}),
    )(*ins, *after)


def shaped(shape, kind):
    return jax.ShapeDtypeStruct(tuple(shape), kind)


def on_device(
    tokens,
    cotangent,
    w_qkv,
    w_out,
    w_up,
    w_down,
    norm_gains,
    ssm_param,
    first_qkv,
    second_qkv,
    first_out,
    second_out,
    first_up,
    second_up,
    first_down,
    second_down,
    first_gain,
    second_gain,
    first_ssm,
    second_ssm,
):
    halves = lax.axis_size("sl")
    low_count = lax.axis_size("ml")
    row_parts = lax.axis_size("sh")
    col_parts = lax.axis_size("mb") * lax.axis_size("mq")
    team = halves * low_count
    sl, ml, mb, mq = (lax.axis_index(name) for name in ("sl", "ml", "mb", "mq"))
    rank = sl * low_count + ml
    block_index = lax.axis_index("sh") * halves + mq
    seq_total, length, width = tokens.shape
    assert length == BLK and seq_total == lax.axis_size("mb")
    states = ssm_param.shape[1]
    channels = width // team
    tiles = channels // LANES
    row_count = width // row_parts
    own_rows = length // team
    place = [rank, block_index, lax.axis_index("sh"), lax.axis_index(MODEL), sl, sl ^ mq]
    place.append(lax.axis_index(COLS))
    place = jnp.stack(place).astype(jnp.int32)
    smem = pl.BlockSpec(memory_space=pltpu.SMEM)
    vmem = pl.BlockSpec(memory_space=pltpu.VMEM)

    def permute(value, axes, moves):
        return lax.ppermute(value, axes, moves)

    def swap(value):
        return permute(value, "sl", [(0, 1), (1, 0)])

    def in_order(own, other, axis):
        return jnp.where(
            sl == 0, jnp.concatenate([own, other], axis), jnp.concatenate([other, own], axis)
        )

    def team_send(pieces):
        moved = [pieces[0]]
        for k in range(1, team):
            moved.append(permute(pieces[k], TEAM, [(i, i ^ k) for i in range(team)]))
        return moved

    def pick_block(array):
        own = lax.dynamic_index_in_dim(array, mb, 0, keepdims=False)
        if halves == 1:
            return own, ()
        other = swap(own)
        return jnp.where(sl == mq, own, other), (other,)

    def across(value, bit):
        return permute(value, "sh", [(i, i ^ bit) for i in range(row_parts)])

    def along(value, axes, step):
        count = lax.axis_size(axes)
        return permute(value, axes, [(i, (i + step) % count) for i in range(count)])

    bits = [1 << i for i in range(row_parts.bit_length() - 1)]

    def bit_order(k):
        return bits if k % 2 == 0 else bits[::-1]

    def double_rows(value, order):
        found = {0: value}
        for bit in order:
            for r in list(found):
                found[r | bit] = across(found[r], bit)
        return [found[r] for r in range(row_parts)]

    def add(*items, zero=None):
        total = sum(item.astype(f32) for item in items)
        return (total if zero is None else total + zero[0, 0]).astype(bf16)

    def first_messages(stacks):
        return across(stacks[1], bits[-1]), across(stacks[3], bits[0])

    def second_messages(stacks, first, zero):
        count = first[0].shape[0] // 2
        return [add(stacks[2 * i][count:], first[i][count:], zero=zero) for i in range(2)]

    def halve_rows(keep, arrived, order, send):
        items = [keep, arrived]
        for bit in order[-2::-1]:
            count = arrived.shape[0] // 2
            if send is None:
                send = add(*[item[count:] for item in items])
            arrived = across(send, bit)
            items = [item[:count] for item in items] + [arrived]
            send = None
        return [item[0] for item in items]

    def halve_both(stacks, first, send):
        near = halve_rows(stacks[0], first[0], bits, send[0])
        return near, halve_rows(stacks[2], first[1], bits[::-1], send[1])

    def hold(arrays, after):
        anywhere = pl.BlockSpec(memory_space=pl.ANY)
        return pl.pallas_call(
            lambda *refs: None,
            out_shape=tuple(shaped(item.shape, item.dtype) for item in arrays),
            in_specs=[anywhere] * (len(arrays) + len(after)),
            out_specs=(anywhere,) * len(arrays),
            input_output_aliases={i: i for i in range(len(arrays))},
        )(*arrays, *after)

    def gather_pieces(shard):
        pieces = []
        for k in range(col_parts):
            held = along(held, COLS, 1) if k > 0 else shard
            pieces.append(double_rows(held, bits if k % 2 == 0 else bits[::-1]))
        return pieces

    def sum_over_z(near, far, ring=True):
        if not ring:
            pieces = [stack[k] for stack in (near, far) for k in range(col_parts // 2)]
            moved = [along(piece, COLS, -k) for k, piece in enumerate(pieces) if k > 0]
            return add(pieces[0], *moved)
        held = None
        for stack in (far, near):
            for k in reversed(range(stack.shape[0])):
                held = stack[k] if held is None else add(stack[k], along(held, COLS, -1))
        return held

    def everywhere(value, axes):
        count = lax.axis_size(axes)
        copies = jnp.broadcast_to(value[None], (count, *value.shape))
        return lax.all_to_all(copies, axes, 0, 0, tiled=True)

    rows_dev = w_up.shape[0]
    hidden_cols = w_up.shape[1] // halves
    head_cols = 4 * w_out.shape[0] // halves
    packed_cols = head_cols + 2 * hidden_cols
    sides = [shaped((rows_dev, cols), bf16) for cols in (head_cols, 2 * hidden_cols)]
    shards = call(
        functools.partial(pack_kernel, halves),
        (place, w_qkv, w_out, w_up, w_down),
        sides + [shaped((rows_dev, packed_cols), bf16)] * (halves - 1),
        time=2.4,
        in_specs=[smem] + [vmem] * 4,
    )
    if halves == 2:
        other = swap(shards[2])
        cuts = (0, head_cols, packed_cols)
        shards = [
            in_order(own, other[:, first:last], 0)
            for own, first, last in zip(shards, cuts, cuts[1:])
        ]
    head_shard, hidden_shard = shards[:2]
    attn_full = lax.all_gather(head_shard, COLS, axis=0, tiled=False)
    hidden_w = gather_pieces(hidden_shard)
    hidden_flat = [piece for group in hidden_w for piece in group]

    small, = call(
        small_kernel,
        (ssm_param.reshape(2 * states, -1), norm_gains),
        (shaped((2 * states + 2, norm_gains.shape[1]), f32),),
        after=hidden_w[0][1:-1],
    )
    small = jnp.transpose(everywhere(small, ALL), (1, 0, 2)).reshape(2 * states + 2, width)
    own_ssm = lax.dynamic_slice_in_dim(
        small[: 2 * states].reshape(2, states, width), rank * channels, channels, 2
    )
    coef, logr = own_ssm[0], own_ssm[1]
    gain_one = small[2 * states : 2 * states + 1]
    gain_two = small[2 * states + 1 : 2 * states + 2]

    x, unused = pick_block(tokens)
    cot, cot_other = pick_block(cotangent)

    anywhere = [pl.BlockSpec(memory_space=pl.ANY)]

    def fixed(*shape):
        return pl.BlockSpec(shape, lambda z: (0,) * len(shape))

    wide = fixed(length, width)
    row = fixed(1, width)

    normed_one, normed_t, u_steps, ends, total = call(
        norm_kernel,
        (place, x, gain_one, logr),
        (
            shaped((length, width), bf16),
            shaped((width, length), bf16),
            shaped((tiles, length, LANES), f32),
            shaped((states, SUBS, channels), f32),
            shaped((states, channels), f32),
        ),
        scratch=[pltpu.VMEM((length, LANES), f32)],
        in_specs=[smem, vmem, vmem, vmem],
        after=(hidden_w[1][0], *cot_other),
        time=5,
    )
    (attn_full,) = hold((attn_full,), (total,))
    attn_w = [
        *double_rows(attn_full[: col_parts // 2], bits),
        *double_rows(attn_full[col_parts // 2 :], bits[::-1]),
    ]
    totals = everywhere(total.astype(bf16), ("sh", "mq"))
    (context_own,) = call(
        context_kernel,
        (place, u_steps, ends, totals, logr, coef),
        (shaped((length, channels), bf16),),
        after=(hidden_w[0][-1], *hidden_w[1][1:-1], hidden_w[-1][0], *attn_w[1 : row_parts - 1]),
        scratch=[pltpu.VMEM((tiles, length, LANES), f32), pltpu.VMEM((length, LANES), f32)],
        in_specs=[smem] + [vmem] * 5,
        time=7,
    )
    contexts = team_send([context_own] * team)

    stack_shape = (row_parts // 2, col_parts // 2, row_count)
    head_stacks = [shaped((*stack_shape, head_cols), bf16)] * 4
    hidden_stacks = [shaped((*stack_shape, hidden_cols), bf16)] * 8
    sizes = (team, col_parts, row_parts)
    head_buffer = pltpu.VMEM((col_parts, row_parts, row_count, 4 * HD), bf16)
    head_sems = pltpu.SemaphoreType.DMA((col_parts, row_parts))
    kept_shape = shaped((3, length, col_parts * HD), bf16)
    flat_shape = shaped((length, col_parts * HD), bf16)
    context_t, cot_t, kept = call(
        functools.partial(project_kernel, *sizes),
        (place, normed_one, cot, *contexts, *attn_w),
        (shaped((width, length), bf16), shaped((width, length), bf16), kept_shape),
        scratch=[pltpu.VMEM((length, width), bf16), head_buffer, head_sems],
        time=1,
        in_specs=[smem] + [vmem] * (2 + team) + anywhere * len(attn_w),
        after=(hidden_w[1][-1], *[piece for group in hidden_w[2:3] for piece in group[1:]]),
    )
    attn_part, attended, probs, probs_t = call(
        functools.partial(attend_kernel, *sizes),
        (place, kept, *attn_w),
        (
            shaped((length, width), bf16),
            flat_shape,
            *[shaped((col_parts, length, length), bf16)] * 2,
        ),
        scratch=[head_buffer, head_sems],
        time=1,
        in_specs=[smem, vmem] + anywhere * len(attn_w),
        after=[piece for group in hidden_w[3:] for piece in group[1:-1]],
    )
    attn_parts = team_send([attn_part] * team)

    middle, normed_two, normed_two_t = call(
        functools.partial(middle_kernel, team),
        (x, gain_two, *attn_parts),
        (shaped((length, width), f32), shaped((length, width), bf16), shaped((width, length), bf16)),
        time=1,
    )
    weight_buffer = pltpu.VMEM((row_parts, row_count, col_parts * hidden_cols), bf16)
    grad_buffer = pltpu.VMEM((col_parts, row_parts, row_count, hidden_cols), bf16)
    fed = call(
        functools.partial(feed_kernel, team, col_parts, row_parts),
        (place, normed_two, normed_two_t, cot, cot_t, *hidden_flat),
        (
            *[shaped((own_rows, width), bf16)] * team,
            shaped((length, width), bf16),
            *hidden_stacks,
        ),
        scratch=[
            *[weight_buffer] * 2,
            *[grad_buffer] * 2,
            *[pltpu.VMEM((length, col_parts * hidden_cols), bf16)] * 2,
            pltpu.SemaphoreType.DMA((4, col_parts, row_parts)),
        ],
        time=18,
        grid=(col_parts,),
        in_specs=[smem, wide, fixed(width, length), wide, fixed(width, length)]
        + anywhere * len(hidden_flat),
        out_specs=[fixed(own_rows, width)] * team + [wide] + anywhere * 8,
    )
    out_pieces, two_part, hidden_grads = fed[:team], fed[team], fed[team + 1 :]
    two_parts = team_send([two_part] * team)

    def rows_of(array, member):
        return lax.dynamic_slice_in_dim(array, member * own_rows, own_rows, 0)

    def from_other_core(pieces):
        if halves == 1:
            return []
        pairs = pieces.reshape(seq_total, halves, own_rows, width)
        return [swap(lax.dynamic_index_in_dim(pairs, 1 - sl, 1, keepdims=False))]

    def share_rows(pieces, others, kind):
        (blocks,) = call(
            functools.partial(assemble_kernel, halves, low_count),
            (place, pieces, *others),
            (shaped((seq_total, length, width), kind),),
            time=3.5,
            in_specs=[smem, vmem] + [vmem] * len(others),
        )
        return blocks

    out_pieces = team_send(list(out_pieces))
    result = rows_of(middle, rank) + sum(item.astype(f32) for item in out_pieces)
    result = result.astype(bf16)
    layer_pieces = lax.all_gather(result, MODEL, axis=0, tiled=False)
    layer_others = from_other_core(layer_pieces)
    layer_out = share_rows(layer_pieces, layer_others, bf16)

    def both_halves(own):
        if halves == 1:
            return [own]
        return [own, swap(lax.dynamic_slice_in_dim(own, (1 - sl) * rows_dev, rows_dev, 0))]

    middle_grad, gain_two_grad, one_part, low_grad, *rest = call(
        functools.partial(attend_back_kernel, *sizes),
        (place, middle, gain_two, cot, *two_parts, kept, probs, probs_t, *attn_w),
        (
            shaped((own_rows, width), f32),
            shaped((1, width), f32),
            shaped((length, width), bf16),
            shaped((length, width), bf16),
            *[flat_shape] * 3,
            *[shaped((length, channels), bf16)] * team,
        ),
        scratch=[
            head_buffer,
            pltpu.VMEM(flat_shape.shape, bf16),
            pltpu.VMEM((length, width), bf16),
            pltpu.VMEM(kept_shape.shape, bf16),
            *[pltpu.VMEM((col_parts, length, length), bf16)] * 2,
            head_sems,
            pltpu.SemaphoreType.DMA((3,)),
        ],
        time=1,
        in_specs=[smem] + [vmem] * (3 + team) + anywhere * (3 + len(attn_w)),
        after=(result,),
    )
    head_grads, context_grads = rest[:3], rest[3:]
    context_grads = team_send(context_grads)
    head_stacks = call(
        functools.partial(head_grads_kernel, col_parts, row_parts),
        (place, low_grad, attended, normed_t, context_t, *head_grads),
        head_stacks,
        scratch=[head_buffer, head_sems],
        time=1,
        in_specs=[smem] + [vmem] * 7,
        out_specs=anywhere * 4,
    )
    down_first = first_messages(hidden_grads[4:])
    g_steps, adjoint_ends, adjoint_total, adjoint_done = call(
        functools.partial(adjoint_kernel, team),
        (logr, *context_grads),
        (
            shaped((tiles, length, LANES), f32),
            shaped((2, states, SUBS, channels), f32),
            shaped((2, states, channels), f32),
        ),
        scratch=[pltpu.VMEM((length, LANES), f32)],
        time=1,
        after=(*down_first, head_stacks[0]),
        token=True,
    )
    adjoint_totals = everywhere(adjoint_total.astype(bf16), ("sh", "mq"))
    down_second = second_messages(hidden_grads[4:], down_first, adjoint_done)
    down_second = hold(down_second, (adjoint_totals,))
    up_stacks = list(hidden_grads[:4])
    up_stacks[1::2] = hold(up_stacks[1::2], (adjoint_totals,))
    up_first = first_messages(up_stacks)
    *one_pieces, grad_ssm = call(
        functools.partial(context_back_kernel, team),
        (place, g_steps, u_steps, adjoint_ends, adjoint_totals, logr, coef, one_part),
        (
            *[shaped((own_rows, width), bf16)] * team,
            shaped((2, states, channels), f32),
        ),
        scratch=[
            pltpu.VMEM((tiles, length, LANES), f32),
            pltpu.VMEM((length, width), f32),
            pltpu.VMEM((length, LANES), f32),
        ],
        in_specs=[smem] + [vmem] * 7,
        time=1,
        after=(*down_second, *up_stacks[1::2], layer_pieces, *layer_others),
    )
    one_pieces = team_send(one_pieces)
    down_parts = halve_both(hidden_grads[4:], down_first, down_second)
    grad_rows, gain_one_grad, rows_done = call(
        functools.partial(input_grad_kernel, team),
        (place, x, gain_one, middle_grad, *one_pieces),
        (shaped((own_rows, width), bf16), shaped((1, width), f32)),
        in_specs=[smem] + [vmem] * (3 + team),
        time=1,
        after=[parts[-1] for parts in down_parts],
        token=True,
    )
    down_sums = [add(*parts, zero=rows_done) for parts in down_parts]
    up_second = second_messages(up_stacks, up_first, rows_done)
    up_sums = [add(*parts) for parts in halve_both(up_stacks, up_first, up_second)]
    head_stacks = list(head_stacks)
    head_stacks[1::2] = hold(head_stacks[1::2], (grad_rows,))
    head_first = first_messages(head_stacks)
    head_second = second_messages(head_stacks, head_first, rows_done)
    head_sums = [add(*parts) for parts in halve_both(head_stacks, head_first, head_second)]
    grad_down = lax.psum_scatter(
        jnp.concatenate(down_sums, 0), COLS, scatter_dimension=0, tiled=False
    )
    grad_up = sum_over_z(*up_sums)
    grad_heads = sum_over_z(*head_sums)
    grad_pieces = lax.all_gather(grad_rows, MODEL, axis=0, tiled=False)
    input_grad = share_rows(grad_pieces, from_other_core(grad_pieces), f32)

    placed_ssm = lax.dynamic_update_slice_in_dim(
        jnp.zeros((2 * states, width), f32),
        grad_ssm.reshape(2 * states, channels),
        rank * channels,
        1,
    )
    small_grads = jnp.concatenate([placed_ssm, gain_one_grad, gain_two_grad], 0)
    (small_grads,) = hold((small_grads,), head_sums)
    small_grads = small_grads.reshape(2 * states + 2, lax.axis_size(ALL), -1)
    small_grads = lax.all_to_all(jnp.transpose(small_grads, (1, 0, 2)), ALL, 0, 0, tiled=True)
    small_grads = jnp.sum(small_grads, axis=0)

    def moments(matrices, grads, arrays, after=()):
        changed = [shaped(old.shape, f32) for group in arrays for old in group]
        grad_parts = [part for grad in grads for part in both_halves(grad)]
        ins = [item for group in arrays for item in group]
        *found, sums = call(
            functools.partial(moments_kernel, halves, matrices),
            (place, *grad_parts, *ins),
            (*changed, shaped((2, LANES), f32)),
            in_specs=[smem] + [vmem] * (len(grad_parts) + len(ins)),
            after=after,
            time=4,
        )
        return [found[3 * i : 3 * i + 3] for i in range(len(arrays))], sums

    hidden_new, hidden_sums = moments(
        ((4, 0, 0, False, None), (5, 1, 0, True, None)),
        (grad_up, grad_down),
        ((w_up, first_up, second_up), (w_down, first_down, second_down)),
    )
    heads_new, head_sums = moments(
        tuple((i, 0, i, False, i) for i in range(3)) + ((3, 0, 3, True, None),),
        (grad_heads,),
        ((w_qkv, first_qkv, second_qkv), (w_out, first_out, second_out)),
        (layer_out, input_grad),
    )
    own_channels = norm_gains.shape[1]
    ssm_items = [item.reshape(2 * states, own_channels) for item in (ssm_param, first_ssm, second_ssm)]
    small_items = [norm_gains, first_gain, second_gain, *ssm_items]
    *small_new, small_sums = call(
        functools.partial(small_moments_kernel, (6, 8)),
        (small_grads.reshape(2 * states + 2, own_channels), *small_items),
        (*[shaped(item.shape, f32) for item in small_items], shaped((2, LANES), f32)),
    )
    all_sums = everywhere(hidden_sums + head_sums + small_sums, ALL)
    masters = (w_qkv, w_out, w_up, w_down, norm_gains, ssm_items[0])
    news = (*heads_new, *hidden_new, small_new[:3], small_new[3:])
    *weights, norms = call(
        functools.partial(update_kernel, ((0, 1, 2), (3,), (4,), (5,), (6, 7), (8, 9))),
        (all_sums, *masters, *[group[2] for group in news]),
        (*[shaped(item.shape, f32) for item in masters], shaped((2, LANES), f32)),
        time=3.2,
    )
    outputs = [layer_out, input_grad]
    for index, (weight, (first_new, second_new, unused)) in enumerate(zip(weights, news)):
        if index == 4:
            outputs += [weight, first_new, second_new[0], second_new[1]]
        else:
            kept_shape = ssm_param.shape if index == 5 else weight.shape
            outputs += [item.reshape(kept_shape) for item in (weight, first_new, second_new)]
    outputs.append(norms[:, :10])
    return tuple(outputs)


def solution(mesh):
    seq_count, model_count = mesh.shape["seq"], mesh.shape["mp"]
    halves = 2 if HEADS // model_count >= 2 else 1
    sizes = (seq_count // halves, halves, SEQS, halves, model_count // (SEQS * halves))
    fine = Mesh(mesh.devices.reshape(sizes), ALL)
    seq, model = ("sh", "sl"), ("mb", "mq", "ml")
    rows_cols, cols_rows = P(seq, model), P(model, seq)
    token = P(None, seq, None)
    stack = P(None, seq, model)
    gains = P(None, ALL)
    ssm = P(None, None, ALL)
    return jax.shard_map(
        on_device,
        mesh=fine,
        in_specs=(token, token, stack, cols_rows, rows_cols, cols_rows, gains, ssm)
        + (stack,) * 2
        + (cols_rows,) * 2
        + (rows_cols,) * 2
        + (cols_rows,) * 2
        + (gains,) * 2
        + (ssm,) * 2,
        out_specs=(token, token)
        + (stack,) * 3
        + (cols_rows,) * 3
        + (rows_cols,) * 3
        + (cols_rows,) * 3
        + (gains, gains, P(ALL), P(ALL))
        + (ssm,) * 3
        + (P(),),
        check_vma=False,
    )
```

```python
import functools
import math

import jax
import jax.numpy as jnp
from jax import lax
from jax.experimental import pallas as pl
from jax.experimental.pallas import tpu as pltpu
from jax.sharding import Mesh
from jax.sharding import PartitionSpec as P

HD = 128
HEADS = 8
BLK = 512
STEP = 10
SEQS = 2
LANES = 128
SUBS = 8
GROUP = 8

norm_eps = 1e-05
beta_first = 0.9
beta_second = 0.999
lamb_eps = 1e-06
weight_decay = 0.01
learn_rate = 0.5
score_scale = HD ** (-0.5)

f32 = jnp.float32
bf16 = jnp.bfloat16
VMEM_BYTES = 56 * 1024 * 1024

ALL = ("sh", "sl", "mb", "mq", "ml")
MODEL = ("mb", "mq", "ml")
COLS = ("mb", "mq")
TEAM = ("sl", "ml")


def dot(left, right):
    return lax.dot_general(left, right, (((1,), (0,)), ((), ())), preferred_element_type=f32)


def dot_t(left, right):
    return lax.dot_general(left, right, (((1,), (1,)), ((), ())), preferred_element_type=f32)


def normalise(values):
    centred = values - jnp.mean(values, axis=-1, keepdims=True)
    inverse = lax.rsqrt(jnp.mean(centred * centred, axis=-1, keepdims=True) + norm_eps)
    return centred * inverse, inverse


def normalise_back(unit, inverse, grad_unit):
    mean_one = jnp.mean(grad_unit, axis=-1, keepdims=True)
    mean_two = jnp.mean(grad_unit * unit, axis=-1, keepdims=True)
    return inverse * (grad_unit - mean_one - unit * mean_two)


def sub_index():
    return lax.broadcasted_iota(jnp.int32, (SUBS, LANES), 0)


def spread(row):
    return jnp.broadcast_to(row, (SUBS, LANES))


def lane_tile(index):
    return slice(index * LANES, (index + 1) * LANES)


def no_state(tiles):
    rows = tiles[0, :SUBS, :]
    return rows - rows


def in_steps(steps, tile, rows):
    span = rows.shape[0] // SUBS

    def move(i, unused):
        steps[tile, pl.ds(pl.multiple_of(i * SUBS, SUBS), SUBS), :] = rows[
            pl.ds(i, SUBS, stride=span), :
        ]
        return unused

    lax.fori_loop(0, span, move, 0, unroll=8)


def from_steps(rows, steps, tile):
    span = rows.shape[0] // SUBS

    def move(i, unused):
        rows[pl.ds(i, SUBS, stride=span), :] = steps[
            tile, pl.ds(pl.multiple_of(i * SUBS, SUBS), SUBS), :
        ]
        return unused

    lax.fori_loop(0, span, move, 0, unroll=8)


def step_rows(i):
    return pl.ds(pl.multiple_of(i * SUBS, SUBS), SUBS)


def norm_kernel(
    place, x_ref, gain_ref, logr_ref, normed_ref, turned_ref, u_tiles, ends_ref, total_ref, rows
):
    unit, unused = normalise(x_ref[...].astype(f32))
    normed_ref[...] = (unit * gain_ref[...]).astype(bf16)
    turned_ref[...] = normed_ref[...].T
    tiles, length, unused = u_tiles.shape
    states = logr_ref.shape[0]
    span = length // SUBS
    for tile in range(tiles):
        start = place[0] * (tiles * LANES) + tile * LANES
        rows[...] = normed_ref[:, pl.ds(pl.multiple_of(start, LANES), LANES)].astype(f32)
        in_steps(u_tiles, tile, rows)
    left = ((SUBS - 1 - sub_index()) * span).astype(f32)
    for tile in range(tiles):
        rate = jnp.exp(logr_ref[:, lane_tile(tile)])
        decay = jnp.exp(-rate)
        decays = [spread(decay[n : n + 1]) for n in range(states)]

        def step(i, held):
            u = u_tiles[tile, step_rows(i), :]
            return tuple(d * h + u for d, h in zip(decays, held))

        zero = no_state(u_tiles)
        held = lax.fori_loop(0, span, step, (zero,) * states, unroll=4)
        for n in range(states):
            ends_ref[n, :, lane_tile(tile)] = held[n]
            total_ref[n : n + 1, lane_tile(tile)] = jnp.sum(
                held[n] * jnp.exp(-left * rate[n : n + 1]), axis=0, keepdims=True
            )


def context_kernel(
    place, u_tiles, ends_ref, all_ref, logr_ref, coef_ref, context_ref, y_tiles, rows
):
    tiles, length, unused = u_tiles.shape
    states = logr_ref.shape[0]
    span = length // SUBS
    index = sub_index()
    before = (index * span).astype(f32)
    for tile in range(tiles):
        rate = jnp.exp(logr_ref[:, lane_tile(tile)])
        decay = jnp.exp(-rate)
        scale = coef_ref[:, lane_tile(tile)] * jnp.sqrt(2.0 * rate)
        incoming = jnp.zeros((states, LANES), f32)
        for j in range(all_ref.shape[0]):
            gap = place[1] - 1 - j
            distance = (jnp.maximum(gap, 0) * length).astype(f32)
            term = jnp.exp(-distance * rate) * all_ref[j, :, lane_tile(tile)].astype(f32)
            incoming = incoming + jnp.where(gap >= 0, term, 0.0)
        for first in range(0, states, GROUP):
            chosen = range(first, first + GROUP)
            starts = []
            for n in chosen:
                row = rate[n : n + 1]
                run = ends_ref[n, :, lane_tile(tile)]
                for d in (1, 2, 4):
                    moved = jnp.exp(-(d * span) * row) * pltpu.roll(run, d, 0)
                    run = run + jnp.where(index >= d, moved, 0.0)
                run = jnp.where(index >= 1, pltpu.roll(run, 1, 0), 0.0)
                starts.append(run + jnp.exp(-before * row) * incoming[n : n + 1])
            decays = [spread(decay[n : n + 1]) for n in chosen]
            scales = [spread(scale[n : n + 1]) for n in chosen]

            def step(i, held):
                at = step_rows(i)
                u = u_tiles[tile, at, :]
                held = tuple(d * h + u for d, h in zip(decays, held))
                parts = [s * h for s, h in zip(scales, held)]
                if first > 0:
                    parts[0] = parts[0] + y_tiles[tile, at, :]
                while len(parts) > 1:
                    parts = [a + b for a, b in zip(parts[::2], parts[1::2])]
                y_tiles[tile, at, :] = parts[0]
                return held

            lax.fori_loop(0, span, step, tuple(starts), unroll=4)
        from_steps(rows, y_tiles, tile)
        context_ref[:, lane_tile(tile)] = rows[...].astype(bf16)


def whole_rows(block):
    return block.reshape(block.shape[0] * block.shape[1], block.shape[2])


def head(index):
    return slice(index * HD, (index + 1) * HD)


def weight_copies(near, far, buffer, place, sems, act):
    count = sems.shape[0]
    half = count // 2
    for k in range(count):
        owner = lax.rem(place[6] + count - k, count)
        for stacks, low in ((near, 0), (far, half)):

            @pl.when((owner >= low) & (owner < low + half))
            def move():
                for r, stack in enumerate(stacks):
                    inner = buffer.at[k, place[2] ^ r]
                    act(pltpu.make_async_copy(stack.at[owner - low], inner, sems.at[k, r]))


def of_heads(buffer, i):
    return jnp.concatenate([whole_rows(buffer[k, :, :, head(i)]) for k in range(buffer.shape[0])], axis=1)


def gradient_slot(row_parts, order, r):
    position = 0
    for bit in reversed(order):
        position = 2 * position + (1 if r & bit else 0)
    return position // (row_parts // 2), position % (row_parts // 2)


def round_orders(row_parts):
    bits = [1 << i for i in range(row_parts.bit_length() - 1)]
    return bits, bits[::-1]


def gradient_pieces(stacks, row_parts, far, slot):
    found = []
    for r in range(row_parts):
        sent, at = gradient_slot(row_parts, round_orders(row_parts)[far], r)
        found.append(stacks[2 * far + sent].at[at, slot])
    return found


def project_kernel(team, col_parts, row_parts, place, normed_ref, cot_ref, *refs):
    contexts, refs = refs[:team], refs[team:]
    near, far, refs = refs[:row_parts], refs[row_parts : 2 * row_parts], refs[2 * row_parts :]
    context_t_ref, cot_t_ref, kept_ref = refs[:3]
    context_ref, weights, sems = refs[3:]
    weight_copies(near, far, weights, place, sems, lambda copy: copy.start())
    width = contexts[0].shape[1]
    for k in range(team):
        lanes = pl.ds(pl.multiple_of((place[0] ^ k) * width, LANES), width)
        context_ref[:, lanes] = contexts[k][...]
    context_t_ref[...] = context_ref[...].T
    cot_t_ref[...] = cot_ref[...].T
    weight_copies(near, far, weights, place, sems, lambda copy: copy.wait())
    kept_ref[0] = dot(normed_ref[...], of_heads(weights, 0)).astype(bf16)
    kept_ref[1] = dot(context_ref[...], of_heads(weights, 1)).astype(bf16)
    kept_ref[2] = dot(context_ref[...], of_heads(weights, 2)).astype(bf16)


def attend_kernel(team, col_parts, row_parts, place, kept_ref, *refs):
    near, far, refs = refs[:row_parts], refs[row_parts : 2 * row_parts], refs[2 * row_parts :]
    part_ref, attended_ref, probs_ref, probs_t_ref, weights, sems = refs
    weight_copies(near, far, weights, place, sems, lambda copy: copy.start())
    length = kept_ref.shape[1]
    rows = lax.broadcasted_iota(jnp.int32, (length, length), 0)
    cols = lax.broadcasted_iota(jnp.int32, (length, length), 1)
    for h in range(col_parts):
        scores = dot_t(kept_ref[0, :, head(h)], kept_ref[1, :, head(h)]) * score_scale
        scores = jnp.where(rows >= cols, scores, -1e30)
        shifted = jnp.exp(scores - jnp.max(scores, axis=-1, keepdims=True))
        inverse = 1.0 / jnp.sum(shifted, axis=-1, keepdims=True)
        probs = (shifted * inverse).astype(bf16)
        probs_ref[h] = probs
        probs_t_ref[h] = probs.T
        attended_ref[:, head(h)] = dot(probs, kept_ref[2, :, head(h)]).astype(bf16)
    weight_copies(near, far, weights, place, sems, lambda copy: copy.wait())
    part_ref[...] = dot_t(attended_ref[...], of_heads(weights, 3)).astype(bf16)


def gelu_parts(hidden, grad_act):
    density = jnp.exp(-0.5 * hidden * hidden)
    t = 1.0 / (1.0 + (0.3275911 * math.sqrt(0.5)) * jnp.abs(hidden))
    series = 0.5 * 1.061405429
    for factor in (-1.453152027, 1.421413741, -0.284496736, 0.254829592):
        series = series * t + 0.5 * factor
    tail = series * t * density
    cdf = jnp.where(hidden >= 0.0, 1.0 - tail, tail)
    slope = cdf + hidden * density * (1.0 / math.sqrt(2.0 * math.pi))
    return (hidden * cdf).astype(bf16), (grad_act * slope).astype(bf16)


def middle_kernel(team, x_ref, gain_ref, *refs):
    parts, (middle_ref, normed_ref, normed_t_ref) = refs[:team], refs[team:]
    attn = parts[0][...].astype(f32)
    for part in parts[1:]:
        attn = attn + part[...].astype(f32)
    middle = x_ref[...].astype(f32) + attn
    middle_ref[...] = middle
    unit, unused = normalise(middle)
    normed_ref[...] = (unit * gain_ref[...]).astype(bf16)
    normed_t_ref[...] = normed_ref[...].T


def feed_kernel(team, col_parts, row_parts, place, normed_ref, normed_t_ref, cot_ref, cot_t_ref, *refs):
    count = col_parts * row_parts
    pieces, refs = refs[:count], refs[count:]
    outs, two_ref, refs = refs[:team], refs[team], refs[team + 1 :]
    stacks, refs = (refs[:4], refs[4:8]), refs[8:]
    up_all, down_all, grad_up, grad_down, activated_all, grad_all, sems = refs
    z = pl.program_id(0)
    half = col_parts // 2
    hidden_cols = grad_up.shape[3]

    def copies(k):
        found = []
        for r in range(row_parts):
            for which, buffer in enumerate((up_all, down_all)):
                outside = pieces[k * row_parts + r].at[:, pl.ds(which * hidden_cols, hidden_cols)]
                inside = buffer.at[place[2] ^ r, :, pl.ds(k * hidden_cols, hidden_cols)]
                found.append(pltpu.make_async_copy(outside, inside, sems.at[which, k, r]))
        return found

    def each_leaving(k, act):
        for which, buffer in enumerate((grad_up, grad_down)):
            steps = k if which == 0 else lax.rem(place[6] + col_parts - k, col_parts)
            for far in range(2):

                @pl.when(steps // half == far)
                def leaves():
                    slot = lax.rem(steps, half)
                    for r, piece in enumerate(gradient_pieces(stacks[which], row_parts, far, slot)):
                        inner = buffer.at[k, place[2] ^ r]
                        act(pltpu.make_async_copy(inner, piece, sems.at[2 + which, k, r]))

    @pl.when(z == 0)
    def start():
        for k in range(col_parts):
            for copy in copies(k):
                copy.start()

    for k in range(col_parts):

        @pl.when(z == k)
        def arrive():
            for copy in copies(k):
                copy.wait()

    at = pl.ds(pl.multiple_of(z * hidden_cols, hidden_cols), hidden_cols)
    hidden = dot(normed_ref[...], whole_rows(up_all[:, :, at]))
    grad_act = dot(cot_ref[...], whole_rows(down_all[:, :, at]))
    activated, grad_pre = gelu_parts(hidden, grad_act)
    activated_all[:, at] = activated
    grad_all[:, at] = grad_pre
    shape = grad_up.shape[1:]
    grad_up[z] = dot(normed_t_ref[...], grad_pre).astype(bf16).reshape(shape)
    grad_down[z] = dot(cot_t_ref[...], activated).astype(bf16).reshape(shape)

    for k in range(col_parts):

        @pl.when(z == k)
        def leave():
            each_leaving(k, lambda copy: copy.start())

    @pl.when(z == col_parts - 1)
    def finish():
        two_ref[...] = dot_t(grad_all[...], whole_rows(up_all[...])).astype(bf16)
        rows = outs[0].shape[0]
        for k in range(team):
            at_rows = pl.ds(pl.multiple_of((place[0] ^ k) * rows, rows), rows)
            outs[k][...] = dot_t(activated_all[at_rows, :], whole_rows(down_all[...])).astype(bf16)
        for k in range(col_parts):
            each_leaving(k, lambda copy: copy.wait())


def attend_back_kernel(team, col_parts, row_parts, place, middle_ref, gain_ref, cot_ref, *refs):
    parts, refs = refs[:team], refs[team:]
    late, refs = refs[:3], refs[3:]
    near, far, refs = refs[:row_parts], refs[row_parts : 2 * row_parts], refs[2 * row_parts :]
    middle_grad_ref, gain_grad_ref, one_ref, low = refs[:4]
    grad_q, grad_k, grad_v = refs[4:7]
    context_grads, refs = refs[7 : 7 + team], refs[7 + team :]
    weights, grad_out, total_low = refs[:3]
    held, (sems, late_sems) = refs[3:6], refs[6:]
    kept_ref, probs_ref, probs_t_ref = held
    weight_copies(near, far, weights, place, sems, lambda copy: copy.start())
    late_copies = [
        pltpu.make_async_copy(outside, inside, late_sems.at[i])
        for i, (outside, inside) in enumerate(zip(late, held))
    ]
    for copy in late_copies:
        copy.start()
    own_rows = middle_ref.shape[0] // team
    grad_two = parts[0][...].astype(f32)
    for part in parts[1:]:
        grad_two = grad_two + part[...].astype(f32)
    unit, inverse = normalise(middle_ref[...])
    grad_gain = grad_two * unit
    rows = lax.broadcasted_iota(jnp.int32, grad_gain.shape, 0)
    first = place[0] * own_rows
    mine = (rows >= first) & (rows < first + own_rows)
    gain_grad_ref[...] = jnp.sum(jnp.where(mine, grad_gain, 0.0), axis=0, keepdims=True)
    grad = cot_ref[...].astype(f32) + normalise_back(unit, inverse, grad_two * gain_ref[...])
    low[...] = grad.astype(bf16)
    for k in range(team):

        @pl.when(place[0] == k)
        def own():
            middle_grad_ref[...] = grad[k * own_rows : (k + 1) * own_rows, :]

    weight_copies(near, far, weights, place, sems, lambda copy: copy.wait())
    for copy in late_copies:
        copy.wait()
    grad_out[...] = dot(low[...], of_heads(weights, 3)).astype(bf16)
    for h in range(col_parts):
        q, k, v = (kept_ref[i, :, head(h)] for i in range(3))
        grad_heads = grad_out[:, head(h)]
        grad_v[:, head(h)] = dot(probs_t_ref[h], grad_heads).astype(bf16)
        probs = probs_ref[h].astype(f32)
        grad_probs = dot_t(grad_heads, v)
        inner = jnp.sum(grad_probs * probs, axis=-1, keepdims=True)
        grad_scores = (probs * (grad_probs - inner)).astype(bf16)
        grad_q[:, head(h)] = (dot(grad_scores, k) * score_scale).astype(bf16)
        turned = dot_t(v, grad_heads) - inner.T
        turned = (probs_t_ref[h].astype(f32) * turned).astype(bf16)
        grad_k[:, head(h)] = (dot(turned, q) * score_scale).astype(bf16)
    total = dot_t(grad_k[...], of_heads(weights, 1)) + dot_t(grad_v[...], of_heads(weights, 2))
    total_low[...] = total.astype(bf16)
    width = context_grads[0].shape[1]
    for k in range(team):
        lanes = pl.ds(pl.multiple_of((place[0] ^ k) * width, LANES), width)
        context_grads[k][...] = total_low[:, lanes]
    one_ref[...] = dot_t(grad_q[...], of_heads(weights, 0)).astype(bf16)


def head_grads_kernel(col_parts, row_parts, place, low, attended_ref, *refs):
    normed_t_ref, context_t_ref, grad_q, grad_k, grad_v = refs[:5]
    stacks, (grads, out_sems) = refs[5:9], refs[9:]
    half = col_parts // 2
    shape = (*grads.shape[1:3], HD)

    def put(i, grad):
        for h in range(col_parts):
            grads[h, :, :, head(i)] = grad[:, head(h)].astype(bf16).reshape(shape)

    put(0, dot(normed_t_ref[...], grad_q[...]))
    put(1, dot(context_t_ref[...], grad_k[...]))
    put(2, dot(context_t_ref[...], grad_v[...]))
    put(3, dot(low[...].T, attended_ref[...]))
    copies = []
    for k in range(col_parts):
        for r, piece in enumerate(gradient_pieces(stacks, row_parts, k // half, k % half)):
            copies.append(pltpu.make_async_copy(grads.at[k, place[2] ^ r], piece, out_sems.at[k, r]))
    for copy in copies:
        copy.start()
    for copy in copies:
        copy.wait()


def adjoint_kernel(team, logr_ref, *refs):
    parts = refs[:team]
    g_tiles, ends_ref, total_ref, rows = refs[team:]
    grad = parts[0][...].astype(f32)
    for part in parts[1:]:
        grad = grad + part[...].astype(f32)
    grad = grad.astype(bf16).astype(f32)
    tiles, length, unused = g_tiles.shape
    states = logr_ref.shape[0]
    span = length // SUBS
    for tile in range(tiles):
        rows[...] = grad[:, lane_tile(tile)]
        in_steps(g_tiles, tile, rows)
    before = (sub_index() * span).astype(f32)
    for tile in range(tiles):
        rate = jnp.exp(logr_ref[:, lane_tile(tile)])
        decay = jnp.exp(-rate)
        for first in range(0, states, GROUP):
            chosen = range(first, first + GROUP)
            decays = [spread(decay[n : n + 1]) for n in chosen]

            def step(i, held):
                g = g_tiles[tile, step_rows(span - 1 - i), :]
                later = []
                for d, (b, w) in zip(decays, held):
                    shrunk = d * b
                    later.append((g + shrunk, d * w + shrunk))
                return tuple(later)

            zero = no_state(g_tiles)
            held = lax.fori_loop(0, span, step, ((zero, zero),) * GROUP, unroll=4)
            for n, (b, w) in zip(chosen, held):
                ends_ref[0, n, :, lane_tile(tile)] = b
                ends_ref[1, n, :, lane_tile(tile)] = w
                shrink = jnp.exp(-before * rate[n : n + 1])
                total_ref[0, n : n + 1, lane_tile(tile)] = jnp.sum(
                    shrink * b, axis=0, keepdims=True
                )
                total_ref[1, n : n + 1, lane_tile(tile)] = jnp.sum(
                    shrink * (w + before * b), axis=0, keepdims=True
                )


def context_back_kernel(
    team, place, g_tiles, u_tiles, ends_ref, all_ref, logr_ref, coef_ref, one_ref, *refs
):
    pieces = refs[:team]
    grad_ssm_ref, y_tiles, full, rows = refs[team:]
    tiles, length, unused = u_tiles.shape
    states = logr_ref.shape[0]
    span = length // SUBS
    width = tiles * LANES
    index = sub_index()
    after = ((SUBS - 1 - index) * span).astype(f32)
    full[...] = one_ref[...].astype(f32)
    group = GROUP
    for tile in range(tiles):
        lanes = lane_tile(tile)
        rate = jnp.exp(logr_ref[:, lanes])
        decay = jnp.exp(-rate)
        root = jnp.sqrt(2.0 * rate)
        scale = coef_ref[:, lanes] * root
        in_b = jnp.zeros((states, LANES), f32)
        in_w = jnp.zeros((states, LANES), f32)
        for j in range(all_ref.shape[0]):
            gap = j - place[1] - 1
            distance = (jnp.maximum(gap, 0) * length).astype(f32)
            shrink = jnp.exp(-distance * rate)
            b, w = all_ref[j, 0, :, lanes].astype(f32), all_ref[j, 1, :, lanes].astype(f32)
            in_b = in_b + jnp.where(gap >= 0, shrink * b, 0.0)
            in_w = in_w + jnp.where(gap >= 0, shrink * (w + distance * b), 0.0)
        for first in range(0, states, group):
            chosen = range(first, first + group)
            starts = []
            for n in chosen:
                row = rate[n : n + 1]
                b, w = ends_ref[0, n, :, lanes], ends_ref[1, n, :, lanes]
                for d in (1, 2, 4):
                    shrink = jnp.exp(-(d * span) * row)
                    next_b = pltpu.roll(b, SUBS - d, 0)
                    next_w = pltpu.roll(w, SUBS - d, 0)
                    inside = index < SUBS - d
                    b, w = (
                        b + jnp.where(inside, shrink * next_b, 0.0),
                        w + jnp.where(inside, shrink * (next_w + (d * span) * next_b), 0.0),
                    )
                inside = index < SUBS - 1
                b = jnp.where(inside, pltpu.roll(b, SUBS - 1, 0), 0.0)
                w = jnp.where(inside, pltpu.roll(w, SUBS - 1, 0), 0.0)
                shrink = jnp.exp(-after * row)
                b_row, w_row = in_b[n : n + 1], in_w[n : n + 1]
                b = b + shrink * b_row
                w = w + shrink * (w_row + after * b_row)
                zero = no_state(u_tiles)
                starts.append((b, w, zero, zero))
            decays = [spread(decay[n : n + 1]) for n in chosen]
            scales = [spread(scale[n : n + 1]) for n in chosen]

            def step(i, held):
                at = step_rows(span - 1 - i)
                g = g_tiles[tile, at, :]
                u = u_tiles[tile, at, :]
                later, parts = [], []
                for d, s, (b, w, sum_b, sum_w) in zip(decays, scales, held):
                    shrunk = d * b
                    w = d * w + shrunk
                    b = g + shrunk
                    later.append((b, w, sum_b + u * b, sum_w + u * w))
                    parts.append(s * b)
                while len(parts) > 1:
                    parts = [p + q for p, q in zip(parts[::2], parts[1::2])]
                if first > 0:
                    parts[0] = parts[0] + y_tiles[tile, at, :]
                y_tiles[tile, at, :] = parts[0]
                return tuple(later)

            held = lax.fori_loop(0, span, step, tuple(starts), unroll=2)
            for n, (unused_b, unused_w, sum_b, sum_w) in zip(chosen, held):
                sum_b = jnp.sum(sum_b, axis=0, keepdims=True)
                sum_w = jnp.sum(sum_w, axis=0, keepdims=True)
                row = slice(n, n + 1)
                grad_ssm_ref[0, row, lanes] = root[row] * sum_b
                grad_ssm_ref[1, row, lanes] = scale[row] * (0.5 * sum_b - rate[row] * sum_w)
        at_lanes = pl.ds(pl.multiple_of(place[0] * width + tile * LANES, LANES), LANES)
        from_steps(rows, y_tiles, tile)
        full[:, at_lanes] += rows[...].astype(bf16).astype(f32)
    count = pieces[0].shape[0]
    for k in range(team):
        at_rows = pl.ds(pl.multiple_of((place[0] ^ k) * count, count), count)
        pieces[k][...] = full[at_rows, :].astype(bf16)


def input_grad_kernel(team, place, x_ref, gain_ref, middle_grad_ref, *refs):
    parts, (out_ref, gain_grad_ref) = refs[:team], refs[team:]
    rows = out_ref.shape[0]
    at_rows = pl.ds(pl.multiple_of(place[0] * rows, rows), rows)
    grad_one = parts[0][...].astype(f32)
    for part in parts[1:]:
        grad_one = grad_one + part[...].astype(f32)
    unit, inverse = normalise(x_ref[at_rows, :].astype(f32))
    gain_grad_ref[...] = jnp.sum(grad_one * unit, axis=0, keepdims=True)
    back = normalise_back(unit, inverse, grad_one * gain_ref[...])
    out_ref[...] = (middle_grad_ref[...] + back).astype(bf16)


def assemble_kernel(halves, low_count, place, own_ref, *refs):
    others, out_ref = refs[:-1], refs[-1]
    count, rows, unused = own_ref.shape
    half = place[4]

    def put(value, sequence, which, member):
        at_rows = pl.ds(pl.multiple_of((which * low_count + member) * rows, rows), rows)
        out_ref[sequence, at_rows, :] = value.astype(out_ref.dtype)

    for sequence in range(count // (halves * low_count)):
        if halves == 1:
            for member in range(low_count):
                put(own_ref[sequence * low_count + member], sequence, 0, member)
        else:
            put(own_ref[sequence * halves + half], sequence, half, 0)
            put(others[0][sequence], sequence, 1 - half, 0)


def pack_kernel(halves, place, qkv_ref, out_ref, up_ref, down_ref, *refs):
    rows = up_ref.shape[0]
    heads, hidden = out_ref.shape[0] // halves, up_ref.shape[1] // halves
    for which in range(halves):
        side = place[4] if which == 0 else 1 - place[4]
        at_heads = pl.ds(pl.multiple_of(side * heads, LANES), heads)
        at_hidden = pl.ds(pl.multiple_of(side * hidden, LANES), hidden)
        if which == 0:
            head_ref = refs[0]
            wide_ref, deep_ref = refs[1].at[:, :hidden], refs[1].at[:, hidden:]
        else:
            packed = refs[2]
            head_ref = packed.at[:, : 4 * heads]
            wide_ref = packed.at[:, 4 * heads : 4 * heads + hidden]
            deep_ref = packed.at[:, 4 * heads + hidden :]
        for i in range(3):
            head_ref[:, i * heads : (i + 1) * heads] = qkv_ref[i, :, at_heads].astype(bf16)
        head_ref[:, 3 * heads :] = out_ref[at_heads, :].T.astype(bf16)
        wide_ref[...] = up_ref[:, at_hidden].astype(bf16)
        deep_ref[...] = down_ref[at_hidden, :].T.astype(bf16)


def small_kernel(ssm_ref, gains_ref, out_ref):
    count = ssm_ref.shape[0]
    out_ref[:count, :] = ssm_ref[...]
    out_ref[count:, :] = gains_ref[...]


def lamb_moments(weight, grad_item, first_old, second_old):
    first_new = beta_first * first_old + (1.0 - beta_first) * grad_item
    second_new = beta_second * second_old + (1.0 - beta_second) * grad_item * grad_item
    direction = (
        first_new
        / (1.0 - beta_first**STEP)
        / (jnp.sqrt(second_new / (1.0 - beta_second**STEP)) + lamb_eps)
        + weight_decay * weight
    )
    return (first_new, second_new, direction)


def place_sums(sums_ref, sums):
    rows = lax.broadcasted_iota(jnp.int32, sums_ref.shape, 0)
    lanes = lax.broadcasted_iota(jnp.int32, sums_ref.shape, 1)
    found = jnp.zeros(sums_ref.shape, f32)
    for index, pair in sums.items():
        for row, value in enumerate(pair):
            found = jnp.where((rows == row) & (lanes == index), value, found)
    sums_ref[...] = found


def moments_kernel(halves, matrices, place, *refs):
    count = 1 + max(item[1] for item in matrices)
    grads, refs = [refs[halves * i : halves * (i + 1)] for i in range(count)], refs[halves * count :]
    arrays = len({(item[1], item[4] is None) for item in matrices})
    ins = [refs[3 * i : 3 * i + 3] for i in range(arrays)]
    outs = [refs[3 * (arrays + i) : 3 * (arrays + i) + 3] for i in range(arrays)]
    sums_ref = refs[6 * arrays]
    keys = []
    sums = {}
    for number, source, column, turned, stacked in matrices:
        key = (source, stacked is None)
        if key not in keys:
            keys.append(key)
        pick = (lambda ref: ref) if stacked is None else (lambda ref, i=stacked: ref.at[i])
        weight, first, second = (pick(ref) for ref in ins[keys.index(key)])
        news = [pick(ref) for ref in outs[keys.index(key)]]
        width = weight.shape[0 if turned else 1] // halves
        rows = weight.shape[1 if turned else 0]
        cols = slice(column * width, (column + 1) * width)
        total_weight = total_update = 0.0
        for which, grad_ref in enumerate(grads[source]):
            side = place[4] if which == 0 else 1 - place[4]
            at = pl.ds(pl.multiple_of(side * width, width), width)
            if which == 0:
                grad = grad_ref[pl.ds(pl.multiple_of(side * rows, rows), rows), cols].astype(f32)
            else:
                grad = grad_ref[:, cols].astype(f32)
            at = (at, slice(None)) if turned else (slice(None), at)
            grad = grad.T if turned else grad
            old = weight[at]
            found = lamb_moments(old, grad, first[at], second[at])
            for ref, value in zip(news, found):
                ref[at] = value
            total_weight = total_weight + jnp.sum(old * old)
            total_update = total_update + jnp.sum(found[2] * found[2])
        sums[number] = (total_weight, total_update)
    place_sums(sums_ref, sums)


def small_moments_kernel(numbers, grads_ref, *refs):
    ins, outs, sums_ref = (refs[:3], refs[3:6]), (refs[6:9], refs[9:12]), refs[12]
    states = (grads_ref.shape[0] - 2) // 2
    sums = {}
    for (weight, first, second), news, start, rows, first_number in (
        (ins[0], outs[0], 2 * states, 1, numbers[0]),
        (ins[1], outs[1], 0, states, numbers[1]),
    ):
        for i in range(2):
            grad = grads_ref[start + i * rows : start + (i + 1) * rows, :]
            at = slice(i * rows, (i + 1) * rows)
            found = lamb_moments(weight[at, :], grad, first[at, :], second[at, :])
            for ref, value in zip(news, found):
                ref[at, :] = value
            sums[first_number + i] = (
                jnp.sum(weight[at, :] * weight[at, :]),
                jnp.sum(found[2] * found[2]),
            )
    place_sums(sums_ref, sums)


def update_kernel(stacks, sums_ref, *refs):
    count = len(stacks)
    weights, directions, news = refs[:count], refs[count : 2 * count], refs[2 * count : 3 * count]
    norms = jnp.sqrt(jnp.sum(sums_ref[...], axis=0))
    refs[3 * count][...] = norms
    ratios = norms[0:1] / norms[1:2]
    lanes = lax.broadcasted_iota(jnp.int32, ratios.shape, 1)
    for numbers, weight, direction, new in zip(stacks, weights, directions, news):
        step = weight.shape[0] // len(numbers)
        for i, number in enumerate(numbers):
            ratio = jnp.sum(jnp.where(lanes == number, ratios, 0.0), axis=1, keepdims=True)
            at = slice(i * step, (i + 1) * step)
            scale = learn_rate * ratio.reshape((1,) * weight.ndim)
            new[at] = weight[at] - scale * direction[at]


def call(
    body, ins, outs, scratch=(), grid=None, in_specs=None, out_specs=None, time=1.0, after=(), token=False
):
    moved = sum(a.size * a.dtype.itemsize for a in list(ins) + list(outs))
    params = pltpu.CompilerParams(vmem_limit_bytes=VMEM_BYTES)
    cost = pl.CostEstimate(flops=int(time * 1.15e9), bytes_accessed=moved, transcendentals=0)
    whole = pl.BlockSpec(memory_space=pltpu.VMEM)
    anywhere = pl.BlockSpec(memory_space=pl.ANY)
    in_specs = list(in_specs or [whole] * len(ins)) + [anywhere] * len(after)
    out_specs = list(out_specs or [whole] * len(outs))
    outs = list(outs)
    first_out = len(ins) + len(after)
    last_out = first_out + len(outs)
    if token:
        outs.append(jax.ShapeDtypeStruct((SUBS, LANES), f32))
        out_specs.append(whole)

    def run(*refs):
        refs = list(refs)
        if token:
            refs[last_out][...] = jnp.zeros((SUBS, LANES), f32)
            del refs[last_out]
        body(*refs[: len(ins)], *refs[first_out:])

    return pl.pallas_call(
        run,
        out_shape=tuple(outs),
        in_specs=in_specs,
        out_specs=tuple(out_specs),
        scratch_shapes=list(scratch),
        compiler_params=params,
        cost_estimate=cost,
        **({} if grid is None else {"grid": grid}),
    )(*ins, *after)


def shaped(shape, kind):
    return jax.ShapeDtypeStruct(tuple(shape), kind)


def on_device(
    tokens,
    cotangent,
    w_qkv,
    w_out,
    w_up,
    w_down,
    norm_gains,
    ssm_param,
    first_qkv,
    second_qkv,
    first_out,
    second_out,
    first_up,
    second_up,
    first_down,
    second_down,
    first_gain,
    second_gain,
    first_ssm,
    second_ssm,
):
    halves = lax.axis_size("sl")
    low_count = lax.axis_size("ml")
    row_parts = lax.axis_size("sh")
    col_parts = lax.axis_size("mb") * lax.axis_size("mq")
    team = halves * low_count
    sl, ml, mb, mq = (lax.axis_index(name) for name in ("sl", "ml", "mb", "mq"))
    rank = sl * low_count + ml
    block_index = lax.axis_index("sh") * halves + mq
    seq_total, length, width = tokens.shape
    assert length == BLK and seq_total == lax.axis_size("mb")
    states = ssm_param.shape[1]
    channels = width // team
    tiles = channels // LANES
    row_count = width // row_parts
    own_rows = length // team
    place = [rank, block_index, lax.axis_index("sh"), lax.axis_index(MODEL), sl, sl ^ mq]
    place.append(lax.axis_index(COLS))
    place = jnp.stack(place).astype(jnp.int32)
    smem = pl.BlockSpec(memory_space=pltpu.SMEM)
    vmem = pl.BlockSpec(memory_space=pltpu.VMEM)

    def permute(value, axes, moves):
        return lax.ppermute(value, axes, moves)

    def swap(value):
        return permute(value, "sl", [(0, 1), (1, 0)])

    def in_order(own, other, axis):
        return jnp.where(
            sl == 0, jnp.concatenate([own, other], axis), jnp.concatenate([other, own], axis)
        )

    def team_send(pieces):
        moved = [pieces[0]]
        for k in range(1, team):
            moved.append(permute(pieces[k], TEAM, [(i, i ^ k) for i in range(team)]))
        return moved

    def pick_block(array):
        own = lax.dynamic_index_in_dim(array, mb, 0, keepdims=False)
        if halves == 1:
            return own, ()
        other = swap(own)
        return jnp.where(sl == mq, own, other), (other,)

    def across(value, bit):
        return permute(value, "sh", [(i, i ^ bit) for i in range(row_parts)])

    def along(value, axes, step):
        count = lax.axis_size(axes)
        return permute(value, axes, [(i, (i + step) % count) for i in range(count)])

    bits = [1 << i for i in range(row_parts.bit_length() - 1)]

    def bit_order(k):
        return bits if k % 2 == 0 else bits[::-1]

    def double_rows(value, order):
        found = {0: value}
        for bit in order:
            for r in list(found):
                found[r | bit] = across(found[r], bit)
        return [found[r] for r in range(row_parts)]

    def add(*items, zero=None):
        total = sum(item.astype(f32) for item in items)
        return (total if zero is None else total + zero[0, 0]).astype(bf16)

    def first_messages(stacks):
        return across(stacks[1], bits[-1]), across(stacks[3], bits[0])

    def second_messages(stacks, first, zero):
        count = first[0].shape[0] // 2
        return [add(stacks[2 * i][count:], first[i][count:], zero=zero) for i in range(2)]

    def halve_rows(keep, arrived, order, send):
        items = [keep, arrived]
        for bit in order[-2::-1]:
            count = arrived.shape[0] // 2
            if send is None:
                send = add(*[item[count:] for item in items])
            arrived = across(send, bit)
            items = [item[:count] for item in items] + [arrived]
            send = None
        return [item[0] for item in items]

    def halve_both(stacks, first, send):
        near = halve_rows(stacks[0], first[0], bits, send[0])
        return near, halve_rows(stacks[2], first[1], bits[::-1], send[1])

    def hold(arrays, after):
        anywhere = pl.BlockSpec(memory_space=pl.ANY)
        return pl.pallas_call(
            lambda *refs: None,
            out_shape=tuple(shaped(item.shape, item.dtype) for item in arrays),
            in_specs=[anywhere] * (len(arrays) + len(after)),
            out_specs=(anywhere,) * len(arrays),
            input_output_aliases={i: i for i in range(len(arrays))},
        )(*arrays, *after)

    def gather_pieces(shard):
        pieces = []
        for k in range(col_parts):
            held = along(held, COLS, 1) if k > 0 else shard
            pieces.append(double_rows(held, bits if k % 2 == 0 else bits[::-1]))
        return pieces

    def sum_over_z(near, far, ring=True):
        if not ring:
            pieces = [stack[k] for stack in (near, far) for k in range(col_parts // 2)]
            moved = [along(piece, COLS, -k) for k, piece in enumerate(pieces) if k > 0]
            return add(pieces[0], *moved)
        held = None
        for stack in (far, near):
            for k in reversed(range(stack.shape[0])):
                held = stack[k] if held is None else add(stack[k], along(held, COLS, -1))
        return held

    def everywhere(value, axes):
        count = lax.axis_size(axes)
        copies = jnp.broadcast_to(value[None], (count, *value.shape))
        return lax.all_to_all(copies, axes, 0, 0, tiled=True)

    rows_dev = w_up.shape[0]
    hidden_cols = w_up.shape[1] // halves
    head_cols = 4 * w_out.shape[0] // halves
    packed_cols = head_cols + 2 * hidden_cols
    sides = [shaped((rows_dev, cols), bf16) for cols in (head_cols, 2 * hidden_cols)]
    shards = call(
        functools.partial(pack_kernel, halves),
        (place, w_qkv, w_out, w_up, w_down),
        sides + [shaped((rows_dev, packed_cols), bf16)] * (halves - 1),
        time=2.4,
        in_specs=[smem] + [vmem] * 4,
    )
    if halves == 2:
        other = swap(shards[2])
        cuts = (0, head_cols, packed_cols)
        shards = [
            in_order(own, other[:, first:last], 0)
            for own, first, last in zip(shards, cuts, cuts[1:])
        ]
    head_shard, hidden_shard = shards[:2]
    attn_full = lax.all_gather(head_shard, COLS, axis=0, tiled=False)
    hidden_w = gather_pieces(hidden_shard)
    hidden_flat = [piece for group in hidden_w for piece in group]

    small, = call(
        small_kernel,
        (ssm_param.reshape(2 * states, -1), norm_gains),
        (shaped((2 * states + 2, norm_gains.shape[1]), f32),),
        after=hidden_w[0][1:-1],
    )
    small = jnp.transpose(everywhere(small, ALL), (1, 0, 2)).reshape(2 * states + 2, width)
    own_ssm = lax.dynamic_slice_in_dim(
        small[: 2 * states].reshape(2, states, width), rank * channels, channels, 2
    )
    coef, logr = own_ssm[0], own_ssm[1]
    gain_one = small[2 * states : 2 * states + 1]
    gain_two = small[2 * states + 1 : 2 * states + 2]

    x, unused = pick_block(tokens)
    cot, cot_other = pick_block(cotangent)

    anywhere = [pl.BlockSpec(memory_space=pl.ANY)]

    def fixed(*shape):
        return pl.BlockSpec(shape, lambda z: (0,) * len(shape))

    wide = fixed(length, width)
    row = fixed(1, width)

    normed_one, normed_t, u_steps, ends, total = call(
        norm_kernel,
        (place, x, gain_one, logr),
        (
            shaped((length, width), bf16),
            shaped((width, length), bf16),
            shaped((tiles, length, LANES), f32),
            shaped((states, SUBS, channels), f32),
            shaped((states, channels), f32),
        ),
        scratch=[pltpu.VMEM((length, LANES), f32)],
        in_specs=[smem, vmem, vmem, vmem],
        after=(hidden_w[1][0], *cot_other),
        time=5,
    )
    (attn_full,) = hold((attn_full,), (total,))
    attn_w = [
        *double_rows(attn_full[: col_parts // 2], bits),
        *double_rows(attn_full[col_parts // 2 :], bits[::-1]),
    ]
    totals = everywhere(total.astype(bf16), ("sh", "mq"))
    (context_own,) = call(
        context_kernel,
        (place, u_steps, ends, totals, logr, coef),
        (shaped((length, channels), bf16),),
        after=(hidden_w[0][-1], *hidden_w[1][1:-1], hidden_w[-1][0], *attn_w[1 : row_parts - 1]),
        scratch=[pltpu.VMEM((tiles, length, LANES), f32), pltpu.VMEM((length, LANES), f32)],
        in_specs=[smem] + [vmem] * 5,
        time=7,
    )
    contexts = team_send([context_own] * team)

    stack_shape = (row_parts // 2, col_parts // 2, row_count)
    head_stacks = [shaped((*stack_shape, head_cols), bf16)] * 4
    hidden_stacks = [shaped((*stack_shape, hidden_cols), bf16)] * 8
    sizes = (team, col_parts, row_parts)
    head_buffer = pltpu.VMEM((col_parts, row_parts, row_count, 4 * HD), bf16)
    head_sems = pltpu.SemaphoreType.DMA((col_parts, row_parts))
    kept_shape = shaped((3, length, col_parts * HD), bf16)
    flat_shape = shaped((length, col_parts * HD), bf16)
    context_t, cot_t, kept = call(
        functools.partial(project_kernel, *sizes),
        (place, normed_one, cot, *contexts, *attn_w),
        (shaped((width, length), bf16), shaped((width, length), bf16), kept_shape),
        scratch=[pltpu.VMEM((length, width), bf16), head_buffer, head_sems],
        time=1,
        in_specs=[smem] + [vmem] * (2 + team) + anywhere * len(attn_w),
        after=(hidden_w[1][-1], *[piece for group in hidden_w[2:3] for piece in group[1:]]),
    )
    attn_part, attended, probs, probs_t = call(
        functools.partial(attend_kernel, *sizes),
        (place, kept, *attn_w),
        (
            shaped((length, width), bf16),
            flat_shape,
            *[shaped((col_parts, length, length), bf16)] * 2,
        ),
        scratch=[head_buffer, head_sems],
        time=1,
        in_specs=[smem, vmem] + anywhere * len(attn_w),
        after=[piece for group in hidden_w[3:] for piece in group[1:-1]],
    )
    attn_parts = team_send([attn_part] * team)

    middle, normed_two, normed_two_t = call(
        functools.partial(middle_kernel, team),
        (x, gain_two, *attn_parts),
        (shaped((length, width), f32), shaped((length, width), bf16), shaped((width, length), bf16)),
        time=1,
    )
    weight_buffer = pltpu.VMEM((row_parts, row_count, col_parts * hidden_cols), bf16)
    grad_buffer = pltpu.VMEM((col_parts, row_parts, row_count, hidden_cols), bf16)
    fed = call(
        functools.partial(feed_kernel, team, col_parts, row_parts),
        (place, normed_two, normed_two_t, cot, cot_t, *hidden_flat),
        (
            *[shaped((own_rows, width), bf16)] * team,
            shaped((length, width), bf16),
            *hidden_stacks,
        ),
        scratch=[
            *[weight_buffer] * 2,
            *[grad_buffer] * 2,
            *[pltpu.VMEM((length, col_parts * hidden_cols), bf16)] * 2,
            pltpu.SemaphoreType.DMA((4, col_parts, row_parts)),
        ],
        time=18,
        grid=(col_parts,),
        in_specs=[smem, wide, fixed(width, length), wide, fixed(width, length)]
        + anywhere * len(hidden_flat),
        out_specs=[fixed(own_rows, width)] * team + [wide] + anywhere * 8,
    )
    out_pieces, two_part, hidden_grads = fed[:team], fed[team], fed[team + 1 :]
    two_parts = team_send([two_part] * team)

    def rows_of(array, member):
        return lax.dynamic_slice_in_dim(array, member * own_rows, own_rows, 0)

    def from_other_core(pieces):
        if halves == 1:
            return []
        pairs = pieces.reshape(seq_total, halves, own_rows, width)
        return [swap(lax.dynamic_index_in_dim(pairs, 1 - sl, 1, keepdims=False))]

    def share_rows(pieces, others, kind):
        (blocks,) = call(
            functools.partial(assemble_kernel, halves, low_count),
            (place, pieces, *others),
            (shaped((seq_total, length, width), kind),),
            time=3.5,
            in_specs=[smem, vmem] + [vmem] * len(others),
        )
        return blocks

    out_pieces = team_send(list(out_pieces))
    result = rows_of(middle, rank) + sum(item.astype(f32) for item in out_pieces)
    result = result.astype(bf16)
    layer_pieces = lax.all_gather(result, MODEL, axis=0, tiled=False)
    layer_others = from_other_core(layer_pieces)
    layer_out = share_rows(layer_pieces, layer_others, bf16)

    def both_halves(own):
        if halves == 1:
            return [own]
        return [own, swap(lax.dynamic_slice_in_dim(own, (1 - sl) * rows_dev, rows_dev, 0))]

    middle_grad, gain_two_grad, one_part, low_grad, *rest = call(
        functools.partial(attend_back_kernel, *sizes),
        (place, middle, gain_two, cot, *two_parts, kept, probs, probs_t, *attn_w),
        (
            shaped((own_rows, width), f32),
            shaped((1, width), f32),
            shaped((length, width), bf16),
            shaped((length, width), bf16),
            *[flat_shape] * 3,
            *[shaped((length, channels), bf16)] * team,
        ),
        scratch=[
            head_buffer,
            pltpu.VMEM(flat_shape.shape, bf16),
            pltpu.VMEM((length, width), bf16),
            pltpu.VMEM(kept_shape.shape, bf16),
            *[pltpu.VMEM((col_parts, length, length), bf16)] * 2,
            head_sems,
            pltpu.SemaphoreType.DMA((3,)),
        ],
        time=1,
        in_specs=[smem] + [vmem] * (3 + team) + anywhere * (3 + len(attn_w)),
        after=(result,),
    )
    head_grads, context_grads = rest[:3], rest[3:]
    context_grads = team_send(context_grads)
    head_stacks = call(
        functools.partial(head_grads_kernel, col_parts, row_parts),
        (place, low_grad, attended, normed_t, context_t, *head_grads),
        head_stacks,
        scratch=[head_buffer, head_sems],
        time=1,
        in_specs=[smem] + [vmem] * 7,
        out_specs=anywhere * 4,
    )
    down_first = first_messages(hidden_grads[4:])
    g_steps, adjoint_ends, adjoint_total, adjoint_done = call(
        functools.partial(adjoint_kernel, team),
        (logr, *context_grads),
        (
            shaped((tiles, length, LANES), f32),
            shaped((2, states, SUBS, channels), f32),
            shaped((2, states, channels), f32),
        ),
        scratch=[pltpu.VMEM((length, LANES), f32)],
        time=1,
        after=(*down_first, head_stacks[0]),
        token=True,
    )
    adjoint_totals = everywhere(adjoint_total.astype(bf16), ("sh", "mq"))
    down_second = second_messages(hidden_grads[4:], down_first, adjoint_done)
    down_second = hold(down_second, (adjoint_totals,))
    up_stacks = list(hidden_grads[:4])
    up_stacks[1::2] = hold(up_stacks[1::2], (adjoint_totals,))
    up_first = first_messages(up_stacks)
    *one_pieces, grad_ssm = call(
        functools.partial(context_back_kernel, team),
        (place, g_steps, u_steps, adjoint_ends, adjoint_totals, logr, coef, one_part),
        (
            *[shaped((own_rows, width), bf16)] * team,
            shaped((2, states, channels), f32),
        ),
        scratch=[
            pltpu.VMEM((tiles, length, LANES), f32),
            pltpu.VMEM((length, width), f32),
            pltpu.VMEM((length, LANES), f32),
        ],
        in_specs=[smem] + [vmem] * 7,
        time=1,
        after=(*down_second, *up_stacks[1::2]),
    )
    one_pieces = team_send(one_pieces)
    down_parts = halve_both(hidden_grads[4:], down_first, down_second)
    grad_rows, gain_one_grad, rows_done = call(
        functools.partial(input_grad_kernel, team),
        (place, x, gain_one, middle_grad, *one_pieces),
        (shaped((own_rows, width), bf16), shaped((1, width), f32)),
        in_specs=[smem] + [vmem] * (3 + team),
        time=1,
        after=(layer_pieces, *[parts[-1] for parts in down_parts]),
        token=True,
    )
    down_sums = [add(*parts, zero=rows_done) for parts in down_parts]
    up_second = second_messages(up_stacks, up_first, rows_done)
    if layer_others:
        up_second = hold(up_second, layer_others)
    up_sums = [add(*parts) for parts in halve_both(up_stacks, up_first, up_second)]
    head_stacks = list(head_stacks)
    head_stacks[1::2] = hold(head_stacks[1::2], (grad_rows,))
    head_first = first_messages(head_stacks)
    head_second = second_messages(head_stacks, head_first, rows_done)
    head_sums = [add(*parts) for parts in halve_both(head_stacks, head_first, head_second)]
    grad_down = lax.psum_scatter(
        jnp.concatenate(down_sums, 0), COLS, scatter_dimension=0, tiled=False
    )
    grad_up = sum_over_z(*up_sums)
    grad_heads = sum_over_z(*head_sums)
    grad_pieces = lax.all_gather(grad_rows, MODEL, axis=0, tiled=False)
    input_grad = share_rows(grad_pieces, from_other_core(grad_pieces), f32)

    placed_ssm = lax.dynamic_update_slice_in_dim(
        jnp.zeros((2 * states, width), f32),
        grad_ssm.reshape(2 * states, channels),
        rank * channels,
        1,
    )
    small_grads = jnp.concatenate([placed_ssm, gain_one_grad, gain_two_grad], 0)
    (small_grads,) = hold((small_grads,), head_sums)
    small_grads = small_grads.reshape(2 * states + 2, lax.axis_size(ALL), -1)
    small_grads = lax.all_to_all(jnp.transpose(small_grads, (1, 0, 2)), ALL, 0, 0, tiled=True)
    small_grads = jnp.sum(small_grads, axis=0)

    def moments(matrices, grads, arrays, after=()):
        changed = [shaped(old.shape, f32) for group in arrays for old in group]
        grad_parts = [part for grad in grads for part in both_halves(grad)]
        ins = [item for group in arrays for item in group]
        *found, sums = call(
            functools.partial(moments_kernel, halves, matrices),
            (place, *grad_parts, *ins),
            (*changed, shaped((2, LANES), f32)),
            in_specs=[smem] + [vmem] * (len(grad_parts) + len(ins)),
            after=after,
            time=4,
        )
        return [found[3 * i : 3 * i + 3] for i in range(len(arrays))], sums

    hidden_new, hidden_sums = moments(
        ((4, 0, 0, False, None), (5, 1, 0, True, None)),
        (grad_up, grad_down),
        ((w_up, first_up, second_up), (w_down, first_down, second_down)),
    )
    heads_new, head_sums = moments(
        tuple((i, 0, i, False, i) for i in range(3)) + ((3, 0, 3, True, None),),
        (grad_heads,),
        ((w_qkv, first_qkv, second_qkv), (w_out, first_out, second_out)),
        (layer_out, input_grad),
    )
    own_channels = norm_gains.shape[1]
    ssm_items = [item.reshape(2 * states, own_channels) for item in (ssm_param, first_ssm, second_ssm)]
    small_items = [norm_gains, first_gain, second_gain, *ssm_items]
    *small_new, small_sums = call(
        functools.partial(small_moments_kernel, (6, 8)),
        (small_grads.reshape(2 * states + 2, own_channels), *small_items),
        (*[shaped(item.shape, f32) for item in small_items], shaped((2, LANES), f32)),
    )
    all_sums = everywhere(hidden_sums + head_sums + small_sums, ALL)
    masters = (w_qkv, w_out, w_up, w_down, norm_gains, ssm_items[0])
    news = (*heads_new, *hidden_new, small_new[:3], small_new[3:])
    *weights, norms = call(
        functools.partial(update_kernel, ((0, 1, 2), (3,), (4,), (5,), (6, 7), (8, 9))),
        (all_sums, *masters, *[group[2] for group in news]),
        (*[shaped(item.shape, f32) for item in masters], shaped((2, LANES), f32)),
        time=3.2,
    )
    outputs = [layer_out, input_grad]
    for index, (weight, (first_new, second_new, unused)) in enumerate(zip(weights, news)):
        if index == 4:
            outputs += [weight, first_new, second_new[0], second_new[1]]
        else:
            kept_shape = ssm_param.shape if index == 5 else weight.shape
            outputs += [item.reshape(kept_shape) for item in (weight, first_new, second_new)]
    outputs.append(norms[:, :10])
    return tuple(outputs)


def solution(mesh):
    seq_count, model_count = mesh.shape["seq"], mesh.shape["mp"]
    halves = 2 if HEADS // model_count >= 2 else 1
    sizes = (seq_count // halves, halves, SEQS, halves, model_count // (SEQS * halves))
    fine = Mesh(mesh.devices.reshape(sizes), ALL)
    seq, model = ("sh", "sl"), ("mb", "mq", "ml")
    rows_cols, cols_rows = P(seq, model), P(model, seq)
    token = P(None, seq, None)
    stack = P(None, seq, model)
    gains = P(None, ALL)
    ssm = P(None, None, ALL)
    return jax.shard_map(
        on_device,
        mesh=fine,
        in_specs=(token, token, stack, cols_rows, rows_cols, cols_rows, gains, ssm)
        + (stack,) * 2
        + (cols_rows,) * 2
        + (rows_cols,) * 2
        + (cols_rows,) * 2
        + (gains,) * 2
        + (ssm,) * 2,
        out_specs=(token, token)
        + (stack,) * 3
        + (cols_rows,) * 3
        + (rows_cols,) * 3
        + (cols_rows,) * 3
        + (gains, gains, P(ALL), P(ALL))
        + (ssm,) * 3
        + (P(),),
        check_vma=False,
    )
```

```python
import functools
import math

import jax
import jax.numpy as jnp
from jax import lax
from jax.experimental import pallas as pl
from jax.experimental.pallas import tpu as pltpu
from jax.sharding import Mesh
from jax.sharding import PartitionSpec as P

HD = 128
HEADS = 8
BLK = 512
STEP = 10
SEQS = 2
LANES = 128
SUBS = 8
GROUP = 8

norm_eps = 1e-05
beta_first = 0.9
beta_second = 0.999
lamb_eps = 1e-06
weight_decay = 0.01
learn_rate = 0.5
score_scale = HD ** (-0.5)

f32 = jnp.float32
bf16 = jnp.bfloat16
VMEM_BYTES = 56 * 1024 * 1024

ALL = ("sh", "sl", "mb", "mq", "ml")
MODEL = ("mb", "mq", "ml")
COLS = ("mb", "mq")
TEAM = ("sl", "ml")


def dot(left, right):
    return lax.dot_general(left, right, (((1,), (0,)), ((), ())), preferred_element_type=f32)


def dot_t(left, right):
    return lax.dot_general(left, right, (((1,), (1,)), ((), ())), preferred_element_type=f32)


def normalise(values):
    centred = values - jnp.mean(values, axis=-1, keepdims=True)
    inverse = lax.rsqrt(jnp.mean(centred * centred, axis=-1, keepdims=True) + norm_eps)
    return centred * inverse, inverse


def normalise_back(unit, inverse, grad_unit):
    mean_one = jnp.mean(grad_unit, axis=-1, keepdims=True)
    mean_two = jnp.mean(grad_unit * unit, axis=-1, keepdims=True)
    return inverse * (grad_unit - mean_one - unit * mean_two)


def sub_index():
    return lax.broadcasted_iota(jnp.int32, (SUBS, LANES), 0)


def spread(row):
    return jnp.broadcast_to(row, (SUBS, LANES))


def lane_tile(index):
    return slice(index * LANES, (index + 1) * LANES)


def no_state(tiles):
    rows = tiles[0, :SUBS, :]
    return rows - rows


def in_steps(steps, tile, rows):
    span = rows.shape[0] // SUBS

    def move(i, unused):
        steps[tile, pl.ds(pl.multiple_of(i * SUBS, SUBS), SUBS), :] = rows[
            pl.ds(i, SUBS, stride=span), :
        ]
        return unused

    lax.fori_loop(0, span, move, 0, unroll=8)


def from_steps(rows, steps, tile):
    span = rows.shape[0] // SUBS

    def move(i, unused):
        rows[pl.ds(i, SUBS, stride=span), :] = steps[
            tile, pl.ds(pl.multiple_of(i * SUBS, SUBS), SUBS), :
        ]
        return unused

    lax.fori_loop(0, span, move, 0, unroll=8)


def step_rows(i):
    return pl.ds(pl.multiple_of(i * SUBS, SUBS), SUBS)


def norm_kernel(
    place, x_ref, gain_ref, logr_ref, normed_ref, turned_ref, u_tiles, ends_ref, total_ref, rows
):
    unit, unused = normalise(x_ref[...].astype(f32))
    normed_ref[...] = (unit * gain_ref[...]).astype(bf16)
    turned_ref[...] = normed_ref[...].T
    tiles, length, unused = u_tiles.shape
    states = logr_ref.shape[0]
    span = length // SUBS
    for tile in range(tiles):
        start = place[0] * (tiles * LANES) + tile * LANES
        rows[...] = normed_ref[:, pl.ds(pl.multiple_of(start, LANES), LANES)].astype(f32)
        in_steps(u_tiles, tile, rows)
    left = ((SUBS - 1 - sub_index()) * span).astype(f32)
    for tile in range(tiles):
        rate = jnp.exp(logr_ref[:, lane_tile(tile)])
        decay = jnp.exp(-rate)
        decays = [spread(decay[n : n + 1]) for n in range(states)]

        def step(i, held):
            u = u_tiles[tile, step_rows(i), :]
            return tuple(d * h + u for d, h in zip(decays, held))

        zero = no_state(u_tiles)
        held = lax.fori_loop(0, span, step, (zero,) * states, unroll=4)
        for n in range(states):
            ends_ref[n, :, lane_tile(tile)] = held[n]
            total_ref[n : n + 1, lane_tile(tile)] = jnp.sum(
                held[n] * jnp.exp(-left * rate[n : n + 1]), axis=0, keepdims=True
            )


def context_kernel(
    place, u_tiles, ends_ref, all_ref, logr_ref, coef_ref, context_ref, y_tiles, rows
):
    tiles, length, unused = u_tiles.shape
    states = logr_ref.shape[0]
    span = length // SUBS
    index = sub_index()
    before = (index * span).astype(f32)
    for tile in range(tiles):
        rate = jnp.exp(logr_ref[:, lane_tile(tile)])
        decay = jnp.exp(-rate)
        scale = coef_ref[:, lane_tile(tile)] * jnp.sqrt(2.0 * rate)
        incoming = jnp.zeros((states, LANES), f32)
        for j in range(all_ref.shape[0]):
            gap = place[1] - 1 - j
            distance = (jnp.maximum(gap, 0) * length).astype(f32)
            term = jnp.exp(-distance * rate) * all_ref[j, :, lane_tile(tile)].astype(f32)
            incoming = incoming + jnp.where(gap >= 0, term, 0.0)
        for first in range(0, states, GROUP):
            chosen = range(first, first + GROUP)
            starts = []
            for n in chosen:
                row = rate[n : n + 1]
                run = ends_ref[n, :, lane_tile(tile)]
                for d in (1, 2, 4):
                    moved = jnp.exp(-(d * span) * row) * pltpu.roll(run, d, 0)
                    run = run + jnp.where(index >= d, moved, 0.0)
                run = jnp.where(index >= 1, pltpu.roll(run, 1, 0), 0.0)
                starts.append(run + jnp.exp(-before * row) * incoming[n : n + 1])
            decays = [spread(decay[n : n + 1]) for n in chosen]
            scales = [spread(scale[n : n + 1]) for n in chosen]

            def step(i, held):
                at = step_rows(i)
                u = u_tiles[tile, at, :]
                held = tuple(d * h + u for d, h in zip(decays, held))
                parts = [s * h for s, h in zip(scales, held)]
                if first > 0:
                    parts[0] = parts[0] + y_tiles[tile, at, :]
                while len(parts) > 1:
                    parts = [a + b for a, b in zip(parts[::2], parts[1::2])]
                y_tiles[tile, at, :] = parts[0]
                return held

            lax.fori_loop(0, span, step, tuple(starts), unroll=4)
        from_steps(rows, y_tiles, tile)
        context_ref[:, lane_tile(tile)] = rows[...].astype(bf16)


def whole_rows(block):
    return block.reshape(block.shape[0] * block.shape[1], block.shape[2])


def head(index):
    return slice(index * HD, (index + 1) * HD)


def weight_copies(near, far, buffer, place, sems, act):
    count = sems.shape[0]
    half = count // 2
    for k in range(count):
        owner = lax.rem(place[6] + count - k, count)
        for stacks, low in ((near, 0), (far, half)):

            @pl.when((owner >= low) & (owner < low + half))
            def move():
                for r, stack in enumerate(stacks):
                    inner = buffer.at[k, place[2] ^ r]
                    act(pltpu.make_async_copy(stack.at[owner - low], inner, sems.at[k, r]))


def of_heads(buffer, i):
    return jnp.concatenate([whole_rows(buffer[k, :, :, head(i)]) for k in range(buffer.shape[0])], axis=1)


def gradient_slot(row_parts, order, r):
    position = 0
    for bit in reversed(order):
        position = 2 * position + (1 if r & bit else 0)
    return position // (row_parts // 2), position % (row_parts // 2)


def round_orders(row_parts):
    bits = [1 << i for i in range(row_parts.bit_length() - 1)]
    return bits, bits[::-1]


def gradient_pieces(stacks, row_parts, far, slot):
    found = []
    for r in range(row_parts):
        sent, at = gradient_slot(row_parts, round_orders(row_parts)[far], r)
        found.append(stacks[2 * far + sent].at[at, slot])
    return found


def project_kernel(team, col_parts, row_parts, place, normed_ref, cot_ref, *refs):
    contexts, refs = refs[:team], refs[team:]
    near, far, refs = refs[:row_parts], refs[row_parts : 2 * row_parts], refs[2 * row_parts :]
    context_t_ref, cot_t_ref, kept_ref = refs[:3]
    context_ref, weights, sems = refs[3:]
    weight_copies(near, far, weights, place, sems, lambda copy: copy.start())
    width = contexts[0].shape[1]
    for k in range(team):
        lanes = pl.ds(pl.multiple_of((place[0] ^ k) * width, LANES), width)
        context_ref[:, lanes] = contexts[k][...]
    context_t_ref[...] = context_ref[...].T
    cot_t_ref[...] = cot_ref[...].T
    weight_copies(near, far, weights, place, sems, lambda copy: copy.wait())
    kept_ref[0] = dot(normed_ref[...], of_heads(weights, 0)).astype(bf16)
    kept_ref[1] = dot(context_ref[...], of_heads(weights, 1)).astype(bf16)
    kept_ref[2] = dot(context_ref[...], of_heads(weights, 2)).astype(bf16)


def attend_kernel(team, col_parts, row_parts, place, kept_ref, *refs):
    near, far, refs = refs[:row_parts], refs[row_parts : 2 * row_parts], refs[2 * row_parts :]
    part_ref, attended_ref, probs_ref, probs_t_ref, weights, sems = refs
    weight_copies(near, far, weights, place, sems, lambda copy: copy.start())
    length = kept_ref.shape[1]
    rows = lax.broadcasted_iota(jnp.int32, (length, length), 0)
    cols = lax.broadcasted_iota(jnp.int32, (length, length), 1)
    for h in range(col_parts):
        scores = dot_t(kept_ref[0, :, head(h)], kept_ref[1, :, head(h)]) * score_scale
        scores = jnp.where(rows >= cols, scores, -1e30)
        shifted = jnp.exp(scores - jnp.max(scores, axis=-1, keepdims=True))
        inverse = 1.0 / jnp.sum(shifted, axis=-1, keepdims=True)
        probs = (shifted * inverse).astype(bf16)
        probs_ref[h] = probs
        probs_t_ref[h] = probs.T
        attended_ref[:, head(h)] = dot(probs, kept_ref[2, :, head(h)]).astype(bf16)
    weight_copies(near, far, weights, place, sems, lambda copy: copy.wait())
    part_ref[...] = dot_t(attended_ref[...], of_heads(weights, 3)).astype(bf16)


def gelu_parts(hidden, grad_act):
    density = jnp.exp(-0.5 * hidden * hidden)
    t = 1.0 / (1.0 + (0.3275911 * math.sqrt(0.5)) * jnp.abs(hidden))
    series = 0.5 * 1.061405429
    for factor in (-1.453152027, 1.421413741, -0.284496736, 0.254829592):
        series = series * t + 0.5 * factor
    tail = series * t * density
    cdf = jnp.where(hidden >= 0.0, 1.0 - tail, tail)
    slope = cdf + hidden * density * (1.0 / math.sqrt(2.0 * math.pi))
    return (hidden * cdf).astype(bf16), (grad_act * slope).astype(bf16)


def middle_kernel(team, x_ref, gain_ref, *refs):
    parts, (middle_ref, normed_ref, normed_t_ref) = refs[:team], refs[team:]
    attn = parts[0][...].astype(f32)
    for part in parts[1:]:
        attn = attn + part[...].astype(f32)
    middle = x_ref[...].astype(f32) + attn
    middle_ref[...] = middle
    unit, unused = normalise(middle)
    normed_ref[...] = (unit * gain_ref[...]).astype(bf16)
    normed_t_ref[...] = normed_ref[...].T


def feed_kernel(team, col_parts, row_parts, place, normed_ref, normed_t_ref, cot_ref, cot_t_ref, *refs):
    count = col_parts * row_parts
    pieces, refs = refs[:count], refs[count:]
    outs, two_ref, refs = refs[:team], refs[team], refs[team + 1 :]
    stacks, refs = (refs[:4], refs[4:8]), refs[8:]
    up_all, down_all, grad_up, grad_down, activated_all, grad_all, sems = refs
    z = pl.program_id(0)
    half = col_parts // 2
    hidden_cols = grad_up.shape[3]

    def copies(k):
        found = []
        for r in range(row_parts):
            for which, buffer in enumerate((up_all, down_all)):
                outside = pieces[k * row_parts + r].at[:, pl.ds(which * hidden_cols, hidden_cols)]
                inside = buffer.at[place[2] ^ r, :, pl.ds(k * hidden_cols, hidden_cols)]
                found.append(pltpu.make_async_copy(outside, inside, sems.at[which, k, r]))
        return found

    def each_leaving(k, act):
        for which, buffer in enumerate((grad_up, grad_down)):
            for r, piece in enumerate(gradient_pieces(stacks[which], row_parts, k // half, k % half)):
                inner = buffer.at[k, place[2] ^ r]
                act(pltpu.make_async_copy(inner, piece, sems.at[2 + which, k, r]))

    @pl.when(z == 0)
    def start():
        for k in range(col_parts):
            for copy in copies(k):
                copy.start()

    for k in range(col_parts):

        @pl.when(z == k)
        def arrive():
            for copy in copies(k):
                copy.wait()

    at = pl.ds(pl.multiple_of(z * hidden_cols, hidden_cols), hidden_cols)
    hidden = dot(normed_ref[...], whole_rows(up_all[:, :, at]))
    grad_act = dot(cot_ref[...], whole_rows(down_all[:, :, at]))
    activated, grad_pre = gelu_parts(hidden, grad_act)
    activated_all[:, at] = activated
    grad_all[:, at] = grad_pre
    shape = grad_up.shape[1:]
    grad_up[z] = dot(normed_t_ref[...], grad_pre).astype(bf16).reshape(shape)
    grad_down[z] = dot(cot_t_ref[...], activated).astype(bf16).reshape(shape)

    for k in range(col_parts):

        @pl.when(z == k)
        def leave():
            each_leaving(k, lambda copy: copy.start())

    @pl.when(z == col_parts - 1)
    def finish():
        two_ref[...] = dot_t(grad_all[...], whole_rows(up_all[...])).astype(bf16)
        rows = outs[0].shape[0]
        for k in range(team):
            at_rows = pl.ds(pl.multiple_of((place[0] ^ k) * rows, rows), rows)
            outs[k][...] = dot_t(activated_all[at_rows, :], whole_rows(down_all[...])).astype(bf16)
        for k in range(col_parts):
            each_leaving(k, lambda copy: copy.wait())


def attend_back_kernel(team, col_parts, row_parts, place, middle_ref, gain_ref, cot_ref, *refs):
    parts, refs = refs[:team], refs[team:]
    late, refs = refs[:3], refs[3:]
    near, far, refs = refs[:row_parts], refs[row_parts : 2 * row_parts], refs[2 * row_parts :]
    middle_grad_ref, gain_grad_ref, one_ref, low = refs[:4]
    grad_q, grad_k, grad_v = refs[4:7]
    context_grads, refs = refs[7 : 7 + team], refs[7 + team :]
    weights, grad_out, total_low = refs[:3]
    held, (sems, late_sems) = refs[3:6], refs[6:]
    kept_ref, probs_ref, probs_t_ref = held
    weight_copies(near, far, weights, place, sems, lambda copy: copy.start())
    late_copies = [
        pltpu.make_async_copy(outside, inside, late_sems.at[i])
        for i, (outside, inside) in enumerate(zip(late, held))
    ]
    for copy in late_copies:
        copy.start()
    own_rows = middle_ref.shape[0] // team
    grad_two = parts[0][...].astype(f32)
    for part in parts[1:]:
        grad_two = grad_two + part[...].astype(f32)
    unit, inverse = normalise(middle_ref[...])
    grad_gain = grad_two * unit
    rows = lax.broadcasted_iota(jnp.int32, grad_gain.shape, 0)
    first = place[0] * own_rows
    mine = (rows >= first) & (rows < first + own_rows)
    gain_grad_ref[...] = jnp.sum(jnp.where(mine, grad_gain, 0.0), axis=0, keepdims=True)
    grad = cot_ref[...].astype(f32) + normalise_back(unit, inverse, grad_two * gain_ref[...])
    low[...] = grad.astype(bf16)
    for k in range(team):

        @pl.when(place[0] == k)
        def own():
            middle_grad_ref[...] = grad[k * own_rows : (k + 1) * own_rows, :]

    weight_copies(near, far, weights, place, sems, lambda copy: copy.wait())
    for copy in late_copies:
        copy.wait()
    grad_out[...] = dot(low[...], of_heads(weights, 3)).astype(bf16)
    for h in range(col_parts):
        q, k, v = (kept_ref[i, :, head(h)] for i in range(3))
        grad_heads = grad_out[:, head(h)]
        grad_v[:, head(h)] = dot(probs_t_ref[h], grad_heads).astype(bf16)
        probs = probs_ref[h].astype(f32)
        grad_probs = dot_t(grad_heads, v)
        inner = jnp.sum(grad_probs * probs, axis=-1, keepdims=True)
        grad_scores = (probs * (grad_probs - inner)).astype(bf16)
        grad_q[:, head(h)] = (dot(grad_scores, k) * score_scale).astype(bf16)
        turned = dot_t(v, grad_heads) - inner.T
        turned = (probs_t_ref[h].astype(f32) * turned).astype(bf16)
        grad_k[:, head(h)] = (dot(turned, q) * score_scale).astype(bf16)
    total = dot_t(grad_k[...], of_heads(weights, 1)) + dot_t(grad_v[...], of_heads(weights, 2))
    total_low[...] = total.astype(bf16)
    width = context_grads[0].shape[1]
    for k in range(team):
        lanes = pl.ds(pl.multiple_of((place[0] ^ k) * width, LANES), width)
        context_grads[k][...] = total_low[:, lanes]
    one_ref[...] = dot_t(grad_q[...], of_heads(weights, 0)).astype(bf16)


def head_grads_kernel(col_parts, row_parts, place, low, attended_ref, *refs):
    normed_t_ref, context_t_ref, grad_q, grad_k, grad_v = refs[:5]
    stacks, (grads, out_sems) = refs[5:9], refs[9:]
    half = col_parts // 2
    shape = (*grads.shape[1:3], HD)

    def put(i, grad):
        for h in range(col_parts):
            grads[h, :, :, head(i)] = grad[:, head(h)].astype(bf16).reshape(shape)

    put(0, dot(normed_t_ref[...], grad_q[...]))
    put(1, dot(context_t_ref[...], grad_k[...]))
    put(2, dot(context_t_ref[...], grad_v[...]))
    put(3, dot(low[...].T, attended_ref[...]))
    copies = []
    for k in range(col_parts):
        for r, piece in enumerate(gradient_pieces(stacks, row_parts, k // half, k % half)):
            copies.append(pltpu.make_async_copy(grads.at[k, place[2] ^ r], piece, out_sems.at[k, r]))
    for copy in copies:
        copy.start()
    for copy in copies:
        copy.wait()


def adjoint_kernel(team, logr_ref, *refs):
    parts = refs[:team]
    g_tiles, ends_ref, total_ref, rows = refs[team:]
    grad = parts[0][...].astype(f32)
    for part in parts[1:]:
        grad = grad + part[...].astype(f32)
    grad = grad.astype(bf16).astype(f32)
    tiles, length, unused = g_tiles.shape
    states = logr_ref.shape[0]
    span = length // SUBS
    for tile in range(tiles):
        rows[...] = grad[:, lane_tile(tile)]
        in_steps(g_tiles, tile, rows)
    before = (sub_index() * span).astype(f32)
    for tile in range(tiles):
        rate = jnp.exp(logr_ref[:, lane_tile(tile)])
        decay = jnp.exp(-rate)
        for first in range(0, states, GROUP):
            chosen = range(first, first + GROUP)
            decays = [spread(decay[n : n + 1]) for n in chosen]

            def step(i, held):
                g = g_tiles[tile, step_rows(span - 1 - i), :]
                later = []
                for d, (b, w) in zip(decays, held):
                    shrunk = d * b
                    later.append((g + shrunk, d * w + shrunk))
                return tuple(later)

            zero = no_state(g_tiles)
            held = lax.fori_loop(0, span, step, ((zero, zero),) * GROUP, unroll=4)
            for n, (b, w) in zip(chosen, held):
                ends_ref[0, n, :, lane_tile(tile)] = b
                ends_ref[1, n, :, lane_tile(tile)] = w
                shrink = jnp.exp(-before * rate[n : n + 1])
                total_ref[0, n : n + 1, lane_tile(tile)] = jnp.sum(
                    shrink * b, axis=0, keepdims=True
                )
                total_ref[1, n : n + 1, lane_tile(tile)] = jnp.sum(
                    shrink * (w + before * b), axis=0, keepdims=True
                )


def context_back_kernel(
    team, place, g_tiles, u_tiles, ends_ref, all_ref, logr_ref, coef_ref, one_ref, *refs
):
    pieces = refs[:team]
    grad_ssm_ref, y_tiles, full, rows = refs[team:]
    tiles, length, unused = u_tiles.shape
    states = logr_ref.shape[0]
    span = length // SUBS
    width = tiles * LANES
    index = sub_index()
    after = ((SUBS - 1 - index) * span).astype(f32)
    full[...] = one_ref[...].astype(f32)
    group = GROUP
    for tile in range(tiles):
        lanes = lane_tile(tile)
        rate = jnp.exp(logr_ref[:, lanes])
        decay = jnp.exp(-rate)
        root = jnp.sqrt(2.0 * rate)
        scale = coef_ref[:, lanes] * root
        in_b = jnp.zeros((states, LANES), f32)
        in_w = jnp.zeros((states, LANES), f32)
        for j in range(all_ref.shape[0]):
            gap = j - place[1] - 1
            distance = (jnp.maximum(gap, 0) * length).astype(f32)
            shrink = jnp.exp(-distance * rate)
            b, w = all_ref[j, 0, :, lanes].astype(f32), all_ref[j, 1, :, lanes].astype(f32)
            in_b = in_b + jnp.where(gap >= 0, shrink * b, 0.0)
            in_w = in_w + jnp.where(gap >= 0, shrink * (w + distance * b), 0.0)
        for first in range(0, states, group):
            chosen = range(first, first + group)
            starts = []
            for n in chosen:
                row = rate[n : n + 1]
                b, w = ends_ref[0, n, :, lanes], ends_ref[1, n, :, lanes]
                for d in (1, 2, 4):
                    shrink = jnp.exp(-(d * span) * row)
                    next_b = pltpu.roll(b, SUBS - d, 0)
                    next_w = pltpu.roll(w, SUBS - d, 0)
                    inside = index < SUBS - d
                    b, w = (
                        b + jnp.where(inside, shrink * next_b, 0.0),
                        w + jnp.where(inside, shrink * (next_w + (d * span) * next_b), 0.0),
                    )
                inside = index < SUBS - 1
                b = jnp.where(inside, pltpu.roll(b, SUBS - 1, 0), 0.0)
                w = jnp.where(inside, pltpu.roll(w, SUBS - 1, 0), 0.0)
                shrink = jnp.exp(-after * row)
                b_row, w_row = in_b[n : n + 1], in_w[n : n + 1]
                b = b + shrink * b_row
                w = w + shrink * (w_row + after * b_row)
                zero = no_state(u_tiles)
                starts.append((b, w, zero, zero))
            decays = [spread(decay[n : n + 1]) for n in chosen]
            scales = [spread(scale[n : n + 1]) for n in chosen]

            def step(i, held):
                at = step_rows(span - 1 - i)
                g = g_tiles[tile, at, :]
                u = u_tiles[tile, at, :]
                later, parts = [], []
                for d, s, (b, w, sum_b, sum_w) in zip(decays, scales, held):
                    shrunk = d * b
                    w = d * w + shrunk
                    b = g + shrunk
                    later.append((b, w, sum_b + u * b, sum_w + u * w))
                    parts.append(s * b)
                while len(parts) > 1:
                    parts = [p + q for p, q in zip(parts[::2], parts[1::2])]
                if first > 0:
                    parts[0] = parts[0] + y_tiles[tile, at, :]
                y_tiles[tile, at, :] = parts[0]
                return tuple(later)

            held = lax.fori_loop(0, span, step, tuple(starts), unroll=2)
            for n, (unused_b, unused_w, sum_b, sum_w) in zip(chosen, held):
                sum_b = jnp.sum(sum_b, axis=0, keepdims=True)
                sum_w = jnp.sum(sum_w, axis=0, keepdims=True)
                row = slice(n, n + 1)
                grad_ssm_ref[0, row, lanes] = root[row] * sum_b
                grad_ssm_ref[1, row, lanes] = scale[row] * (0.5 * sum_b - rate[row] * sum_w)
        at_lanes = pl.ds(pl.multiple_of(place[0] * width + tile * LANES, LANES), LANES)
        from_steps(rows, y_tiles, tile)
        full[:, at_lanes] += rows[...].astype(bf16).astype(f32)
    count = pieces[0].shape[0]
    for k in range(team):
        at_rows = pl.ds(pl.multiple_of((place[0] ^ k) * count, count), count)
        pieces[k][...] = full[at_rows, :].astype(bf16)


def input_grad_kernel(team, place, x_ref, gain_ref, middle_grad_ref, *refs):
    parts, (out_ref, gain_grad_ref) = refs[:team], refs[team:]
    rows = out_ref.shape[0]
    at_rows = pl.ds(pl.multiple_of(place[0] * rows, rows), rows)
    grad_one = parts[0][...].astype(f32)
    for part in parts[1:]:
        grad_one = grad_one + part[...].astype(f32)
    unit, inverse = normalise(x_ref[at_rows, :].astype(f32))
    gain_grad_ref[...] = jnp.sum(grad_one * unit, axis=0, keepdims=True)
    back = normalise_back(unit, inverse, grad_one * gain_ref[...])
    out_ref[...] = (middle_grad_ref[...] + back).astype(bf16)


def assemble_kernel(halves, low_count, place, own_ref, *refs):
    others, out_ref = refs[:-1], refs[-1]
    count, rows, unused = own_ref.shape
    half = place[4]

    def put(value, sequence, which, member):
        at_rows = pl.ds(pl.multiple_of((which * low_count + member) * rows, rows), rows)
        out_ref[sequence, at_rows, :] = value.astype(out_ref.dtype)

    for sequence in range(count // (halves * low_count)):
        if halves == 1:
            for member in range(low_count):
                put(own_ref[sequence * low_count + member], sequence, 0, member)
        else:
            put(own_ref[sequence * halves + half], sequence, half, 0)
            put(others[0][sequence], sequence, 1 - half, 0)


def pack_kernel(halves, place, qkv_ref, out_ref, up_ref, down_ref, *refs):
    rows = up_ref.shape[0]
    heads, hidden = out_ref.shape[0] // halves, up_ref.shape[1] // halves
    for which in range(halves):
        side = place[4] if which == 0 else 1 - place[4]
        at_heads = pl.ds(pl.multiple_of(side * heads, LANES), heads)
        at_hidden = pl.ds(pl.multiple_of(side * hidden, LANES), hidden)
        if which == 0:
            head_ref = refs[0]
            wide_ref, deep_ref = refs[1].at[:, :hidden], refs[1].at[:, hidden:]
        else:
            packed = refs[2]
            head_ref = packed.at[:, : 4 * heads]
            wide_ref = packed.at[:, 4 * heads : 4 * heads + hidden]
            deep_ref = packed.at[:, 4 * heads + hidden :]
        for i in range(3):
            head_ref[:, i * heads : (i + 1) * heads] = qkv_ref[i, :, at_heads].astype(bf16)
        head_ref[:, 3 * heads :] = out_ref[at_heads, :].T.astype(bf16)
        wide_ref[...] = up_ref[:, at_hidden].astype(bf16)
        deep_ref[...] = down_ref[at_hidden, :].T.astype(bf16)


def small_kernel(ssm_ref, gains_ref, out_ref):
    count = ssm_ref.shape[0]
    out_ref[:count, :] = ssm_ref[...]
    out_ref[count:, :] = gains_ref[...]


def lamb_moments(weight, grad_item, first_old, second_old):
    first_new = beta_first * first_old + (1.0 - beta_first) * grad_item
    second_new = beta_second * second_old + (1.0 - beta_second) * grad_item * grad_item
    direction = (
        first_new
        / (1.0 - beta_first**STEP)
        / (jnp.sqrt(second_new / (1.0 - beta_second**STEP)) + lamb_eps)
        + weight_decay * weight
    )
    return (first_new, second_new, direction)


def place_sums(sums_ref, sums):
    rows = lax.broadcasted_iota(jnp.int32, sums_ref.shape, 0)
    lanes = lax.broadcasted_iota(jnp.int32, sums_ref.shape, 1)
    found = jnp.zeros(sums_ref.shape, f32)
    for index, pair in sums.items():
        for row, value in enumerate(pair):
            found = jnp.where((rows == row) & (lanes == index), value, found)
    sums_ref[...] = found


def moments_kernel(halves, matrices, place, *refs):
    count = 1 + max(item[1] for item in matrices)
    grads, refs = [refs[halves * i : halves * (i + 1)] for i in range(count)], refs[halves * count :]
    arrays = len({(item[1], item[4] is None) for item in matrices})
    ins = [refs[3 * i : 3 * i + 3] for i in range(arrays)]
    outs = [refs[3 * (arrays + i) : 3 * (arrays + i) + 3] for i in range(arrays)]
    sums_ref = refs[6 * arrays]
    keys = []
    sums = {}
    for number, source, column, turned, stacked in matrices:
        key = (source, stacked is None)
        if key not in keys:
            keys.append(key)
        pick = (lambda ref: ref) if stacked is None else (lambda ref, i=stacked: ref.at[i])
        weight, first, second = (pick(ref) for ref in ins[keys.index(key)])
        news = [pick(ref) for ref in outs[keys.index(key)]]
        width = weight.shape[0 if turned else 1] // halves
        rows = weight.shape[1 if turned else 0]
        cols = slice(column * width, (column + 1) * width)
        total_weight = total_update = 0.0
        for which, grad_ref in enumerate(grads[source]):
            side = place[4] if which == 0 else 1 - place[4]
            at = pl.ds(pl.multiple_of(side * width, width), width)
            if which == 0:
                grad = grad_ref[pl.ds(pl.multiple_of(side * rows, rows), rows), cols].astype(f32)
            else:
                grad = grad_ref[:, cols].astype(f32)
            at = (at, slice(None)) if turned else (slice(None), at)
            grad = grad.T if turned else grad
            old = weight[at]
            found = lamb_moments(old, grad, first[at], second[at])
            for ref, value in zip(news, found):
                ref[at] = value
            total_weight = total_weight + jnp.sum(old * old)
            total_update = total_update + jnp.sum(found[2] * found[2])
        sums[number] = (total_weight, total_update)
    place_sums(sums_ref, sums)


def small_moments_kernel(numbers, grads_ref, *refs):
    ins, outs, sums_ref = (refs[:3], refs[3:6]), (refs[6:9], refs[9:12]), refs[12]
    states = (grads_ref.shape[0] - 2) // 2
    sums = {}
    for (weight, first, second), news, start, rows, first_number in (
        (ins[0], outs[0], 2 * states, 1, numbers[0]),
        (ins[1], outs[1], 0, states, numbers[1]),
    ):
        for i in range(2):
            grad = grads_ref[start + i * rows : start + (i + 1) * rows, :]
            at = slice(i * rows, (i + 1) * rows)
            found = lamb_moments(weight[at, :], grad, first[at, :], second[at, :])
            for ref, value in zip(news, found):
                ref[at, :] = value
            sums[first_number + i] = (
                jnp.sum(weight[at, :] * weight[at, :]),
                jnp.sum(found[2] * found[2]),
            )
    place_sums(sums_ref, sums)


def update_kernel(stacks, sums_ref, *refs):
    count = len(stacks)
    weights, directions, news = refs[:count], refs[count : 2 * count], refs[2 * count : 3 * count]
    norms = jnp.sqrt(jnp.sum(sums_ref[...], axis=0))
    refs[3 * count][...] = norms
    ratios = norms[0:1] / norms[1:2]
    lanes = lax.broadcasted_iota(jnp.int32, ratios.shape, 1)
    for numbers, weight, direction, new in zip(stacks, weights, directions, news):
        step = weight.shape[0] // len(numbers)
        for i, number in enumerate(numbers):
            ratio = jnp.sum(jnp.where(lanes == number, ratios, 0.0), axis=1, keepdims=True)
            at = slice(i * step, (i + 1) * step)
            scale = learn_rate * ratio.reshape((1,) * weight.ndim)
            new[at] = weight[at] - scale * direction[at]


def call(
    body, ins, outs, scratch=(), grid=None, in_specs=None, out_specs=None, time=1.0, after=(), token=False
):
    moved = sum(a.size * a.dtype.itemsize for a in list(ins) + list(outs))
    params = pltpu.CompilerParams(vmem_limit_bytes=VMEM_BYTES)
    cost = pl.CostEstimate(flops=int(time * 1.15e9), bytes_accessed=moved, transcendentals=0)
    whole = pl.BlockSpec(memory_space=pltpu.VMEM)
    anywhere = pl.BlockSpec(memory_space=pl.ANY)
    in_specs = list(in_specs or [whole] * len(ins)) + [anywhere] * len(after)
    out_specs = list(out_specs or [whole] * len(outs))
    outs = list(outs)
    first_out = len(ins) + len(after)
    last_out = first_out + len(outs)
    if token:
        outs.append(jax.ShapeDtypeStruct((SUBS, LANES), f32))
        out_specs.append(whole)

    def run(*refs):
        refs = list(refs)
        if token:
            refs[last_out][...] = jnp.zeros((SUBS, LANES), f32)
            del refs[last_out]
        body(*refs[: len(ins)], *refs[first_out:])

    return pl.pallas_call(
        run,
        out_shape=tuple(outs),
        in_specs=in_specs,
        out_specs=tuple(out_specs),
        scratch_shapes=list(scratch),
        compiler_params=params,
        cost_estimate=cost,
        **({} if grid is None else {"grid": grid}),
    )(*ins, *after)


def shaped(shape, kind):
    return jax.ShapeDtypeStruct(tuple(shape), kind)


def on_device(
    tokens,
    cotangent,
    w_qkv,
    w_out,
    w_up,
    w_down,
    norm_gains,
    ssm_param,
    first_qkv,
    second_qkv,
    first_out,
    second_out,
    first_up,
    second_up,
    first_down,
    second_down,
    first_gain,
    second_gain,
    first_ssm,
    second_ssm,
):
    halves = lax.axis_size("sl")
    low_count = lax.axis_size("ml")
    row_parts = lax.axis_size("sh")
    col_parts = lax.axis_size("mb") * lax.axis_size("mq")
    team = halves * low_count
    sl, ml, mb, mq = (lax.axis_index(name) for name in ("sl", "ml", "mb", "mq"))
    rank = sl * low_count + ml
    block_index = lax.axis_index("sh") * halves + mq
    seq_total, length, width = tokens.shape
    assert length == BLK and seq_total == lax.axis_size("mb")
    states = ssm_param.shape[1]
    channels = width // team
    tiles = channels // LANES
    row_count = width // row_parts
    own_rows = length // team
    place = [rank, block_index, lax.axis_index("sh"), lax.axis_index(MODEL), sl, sl ^ mq]
    place.append(lax.axis_index(COLS))
    place = jnp.stack(place).astype(jnp.int32)
    smem = pl.BlockSpec(memory_space=pltpu.SMEM)
    vmem = pl.BlockSpec(memory_space=pltpu.VMEM)

    def permute(value, axes, moves):
        return lax.ppermute(value, axes, moves)

    def swap(value):
        return permute(value, "sl", [(0, 1), (1, 0)])

    def in_order(own, other, axis):
        return jnp.where(
            sl == 0, jnp.concatenate([own, other], axis), jnp.concatenate([other, own], axis)
        )

    def team_send(pieces):
        moved = [pieces[0]]
        for k in range(1, team):
            moved.append(permute(pieces[k], TEAM, [(i, i ^ k) for i in range(team)]))
        return moved

    def pick_block(array):
        own = lax.dynamic_index_in_dim(array, mb, 0, keepdims=False)
        if halves == 1:
            return own, ()
        other = swap(own)
        return jnp.where(sl == mq, own, other), (other,)

    def across(value, bit):
        return permute(value, "sh", [(i, i ^ bit) for i in range(row_parts)])

    def along(value, axes, step):
        count = lax.axis_size(axes)
        return permute(value, axes, [(i, (i + step) % count) for i in range(count)])

    bits = [1 << i for i in range(row_parts.bit_length() - 1)]

    def bit_order(k):
        return bits if k % 2 == 0 else bits[::-1]

    def double_rows(value, order):
        found = {0: value}
        for bit in order:
            for r in list(found):
                found[r | bit] = across(found[r], bit)
        return [found[r] for r in range(row_parts)]

    def add(*items, zero=None):
        total = sum(item.astype(f32) for item in items)
        return (total if zero is None else total + zero[0, 0]).astype(bf16)

    def first_messages(stacks):
        return across(stacks[1], bits[-1]), across(stacks[3], bits[0])

    def second_messages(stacks, first, zero):
        count = first[0].shape[0] // 2
        return [add(stacks[2 * i][count:], first[i][count:], zero=zero) for i in range(2)]

    def halve_rows(keep, arrived, order, send):
        items = [keep, arrived]
        for bit in order[-2::-1]:
            count = arrived.shape[0] // 2
            if send is None:
                send = add(*[item[count:] for item in items])
            arrived = across(send, bit)
            items = [item[:count] for item in items] + [arrived]
            send = None
        return [item[0] for item in items]

    def halve_both(stacks, first, send):
        near = halve_rows(stacks[0], first[0], bits, send[0])
        return near, halve_rows(stacks[2], first[1], bits[::-1], send[1])

    def hold(arrays, after):
        anywhere = pl.BlockSpec(memory_space=pl.ANY)
        return pl.pallas_call(
            lambda *refs: None,
            out_shape=tuple(shaped(item.shape, item.dtype) for item in arrays),
            in_specs=[anywhere] * (len(arrays) + len(after)),
            out_specs=(anywhere,) * len(arrays),
            input_output_aliases={i: i for i in range(len(arrays))},
        )(*arrays, *after)

    def gather_pieces(shard):
        pieces = []
        for k in range(col_parts):
            held = along(held, COLS, 1) if k > 0 else shard
            pieces.append(double_rows(held, bits if k % 2 == 0 else bits[::-1]))
        return pieces

    def sum_over_z(near, far, ring=True):
        if not ring:
            pieces = [stack[k] for stack in (near, far) for k in range(col_parts // 2)]
            moved = [along(piece, COLS, -k) for k, piece in enumerate(pieces) if k > 0]
            return add(pieces[0], *moved)
        held = None
        for stack in (far, near):
            for k in reversed(range(stack.shape[0])):
                held = stack[k] if held is None else add(stack[k], along(held, COLS, -1))
        return held

    def everywhere(value, axes):
        count = lax.axis_size(axes)
        copies = jnp.broadcast_to(value[None], (count, *value.shape))
        return lax.all_to_all(copies, axes, 0, 0, tiled=True)

    rows_dev = w_up.shape[0]
    hidden_cols = w_up.shape[1] // halves
    head_cols = 4 * w_out.shape[0] // halves
    packed_cols = head_cols + 2 * hidden_cols
    sides = [shaped((rows_dev, cols), bf16) for cols in (head_cols, 2 * hidden_cols)]
    shards = call(
        functools.partial(pack_kernel, halves),
        (place, w_qkv, w_out, w_up, w_down),
        sides + [shaped((rows_dev, packed_cols), bf16)] * (halves - 1),
        time=2.4,
        in_specs=[smem] + [vmem] * 4,
    )
    if halves == 2:
        other = swap(shards[2])
        cuts = (0, head_cols, packed_cols)
        shards = [
            in_order(own, other[:, first:last], 0)
            for own, first, last in zip(shards, cuts, cuts[1:])
        ]
    head_shard, hidden_shard = shards[:2]
    attn_full = lax.all_gather(head_shard, COLS, axis=0, tiled=False)
    hidden_w = gather_pieces(hidden_shard)
    hidden_flat = [piece for group in hidden_w for piece in group]

    small, = call(
        small_kernel,
        (ssm_param.reshape(2 * states, -1), norm_gains),
        (shaped((2 * states + 2, norm_gains.shape[1]), f32),),
        after=hidden_w[0][1:-1],
    )
    small = jnp.transpose(everywhere(small, ALL), (1, 0, 2)).reshape(2 * states + 2, width)
    own_ssm = lax.dynamic_slice_in_dim(
        small[: 2 * states].reshape(2, states, width), rank * channels, channels, 2
    )
    coef, logr = own_ssm[0], own_ssm[1]
    gain_one = small[2 * states : 2 * states + 1]
    gain_two = small[2 * states + 1 : 2 * states + 2]

    x, unused = pick_block(tokens)
    cot, cot_other = pick_block(cotangent)

    anywhere = [pl.BlockSpec(memory_space=pl.ANY)]

    def fixed(*shape):
        return pl.BlockSpec(shape, lambda z: (0,) * len(shape))

    wide = fixed(length, width)
    row = fixed(1, width)

    normed_one, normed_t, u_steps, ends, total = call(
        norm_kernel,
        (place, x, gain_one, logr),
        (
            shaped((length, width), bf16),
            shaped((width, length), bf16),
            shaped((tiles, length, LANES), f32),
            shaped((states, SUBS, channels), f32),
            shaped((states, channels), f32),
        ),
        scratch=[pltpu.VMEM((length, LANES), f32)],
        in_specs=[smem, vmem, vmem, vmem],
        after=(hidden_w[1][0], *cot_other),
        time=5,
    )
    (attn_full,) = hold((attn_full,), (total,))
    attn_w = [
        *double_rows(attn_full[: col_parts // 2], bits),
        *double_rows(attn_full[col_parts // 2 :], bits[::-1]),
    ]
    totals = everywhere(total.astype(bf16), ("sh", "mq"))
    (context_own,) = call(
        context_kernel,
        (place, u_steps, ends, totals, logr, coef),
        (shaped((length, channels), bf16),),
        after=(hidden_w[0][-1], *hidden_w[1][1:-1], hidden_w[-1][0], *attn_w[1 : row_parts - 1]),
        scratch=[pltpu.VMEM((tiles, length, LANES), f32), pltpu.VMEM((length, LANES), f32)],
        in_specs=[smem] + [vmem] * 5,
        time=7,
    )
    contexts = team_send([context_own] * team)

    stack_shape = (row_parts // 2, col_parts // 2, row_count)
    head_stacks = [shaped((*stack_shape, head_cols), bf16)] * 4
    hidden_stacks = [shaped((*stack_shape, hidden_cols), bf16)] * 8
    sizes = (team, col_parts, row_parts)
    head_buffer = pltpu.VMEM((col_parts, row_parts, row_count, 4 * HD), bf16)
    head_sems = pltpu.SemaphoreType.DMA((col_parts, row_parts))
    kept_shape = shaped((3, length, col_parts * HD), bf16)
    flat_shape = shaped((length, col_parts * HD), bf16)
    context_t, cot_t, kept = call(
        functools.partial(project_kernel, *sizes),
        (place, normed_one, cot, *contexts, *attn_w),
        (shaped((width, length), bf16), shaped((width, length), bf16), kept_shape),
        scratch=[pltpu.VMEM((length, width), bf16), head_buffer, head_sems],
        time=1,
        in_specs=[smem] + [vmem] * (2 + team) + anywhere * len(attn_w),
        after=(hidden_w[1][-1], *[piece for group in hidden_w[2:3] for piece in group[1:]]),
    )
    attn_part, attended, probs, probs_t = call(
        functools.partial(attend_kernel, *sizes),
        (place, kept, *attn_w),
        (
            shaped((length, width), bf16),
            flat_shape,
            *[shaped((col_parts, length, length), bf16)] * 2,
        ),
        scratch=[head_buffer, head_sems],
        time=1,
        in_specs=[smem, vmem] + anywhere * len(attn_w),
        after=[piece for group in hidden_w[3:] for piece in group[1:-1]],
    )
    attn_parts = team_send([attn_part] * team)

    middle, normed_two, normed_two_t = call(
        functools.partial(middle_kernel, team),
        (x, gain_two, *attn_parts),
        (shaped((length, width), f32), shaped((length, width), bf16), shaped((width, length), bf16)),
        time=1,
    )
    weight_buffer = pltpu.VMEM((row_parts, row_count, col_parts * hidden_cols), bf16)
    grad_buffer = pltpu.VMEM((col_parts, row_parts, row_count, hidden_cols), bf16)
    fed = call(
        functools.partial(feed_kernel, team, col_parts, row_parts),
        (place, normed_two, normed_two_t, cot, cot_t, *hidden_flat),
        (
            *[shaped((own_rows, width), bf16)] * team,
            shaped((length, width), bf16),
            *hidden_stacks,
        ),
        scratch=[
            *[weight_buffer] * 2,
            *[grad_buffer] * 2,
            *[pltpu.VMEM((length, col_parts * hidden_cols), bf16)] * 2,
            pltpu.SemaphoreType.DMA((4, col_parts, row_parts)),
        ],
        time=18,
        grid=(col_parts,),
        in_specs=[smem, wide, fixed(width, length), wide, fixed(width, length)]
        + anywhere * len(hidden_flat),
        out_specs=[fixed(own_rows, width)] * team + [wide] + anywhere * 8,
    )
    out_pieces, two_part, hidden_grads = fed[:team], fed[team], fed[team + 1 :]
    two_parts = team_send([two_part] * team)

    def rows_of(array, member):
        return lax.dynamic_slice_in_dim(array, member * own_rows, own_rows, 0)

    def share_rows(pieces, kind):
        others = []
        if halves == 2:
            pairs = pieces.reshape(seq_total, halves, own_rows, width)
            others = [swap(lax.dynamic_index_in_dim(pairs, 1 - sl, 1, keepdims=False))]
        (blocks,) = call(
            functools.partial(assemble_kernel, halves, low_count),
            (place, pieces, *others),
            (shaped((seq_total, length, width), kind),),
            time=3.5,
            in_specs=[smem, vmem] + [vmem] * len(others),
        )
        return blocks

    out_pieces = team_send(list(out_pieces))
    result = rows_of(middle, rank) + sum(item.astype(f32) for item in out_pieces)
    result = result.astype(bf16)
    layer_pieces = lax.all_gather(result, MODEL, axis=0, tiled=False)
    layer_out = share_rows(layer_pieces, bf16)

    def both_halves(own):
        if halves == 1:
            return [own]
        return [own, swap(lax.dynamic_slice_in_dim(own, (1 - sl) * rows_dev, rows_dev, 0))]

    middle_grad, gain_two_grad, one_part, low_grad, *rest = call(
        functools.partial(attend_back_kernel, *sizes),
        (place, middle, gain_two, cot, *two_parts, kept, probs, probs_t, *attn_w),
        (
            shaped((own_rows, width), f32),
            shaped((1, width), f32),
            shaped((length, width), bf16),
            shaped((length, width), bf16),
            *[flat_shape] * 3,
            *[shaped((length, channels), bf16)] * team,
        ),
        scratch=[
            head_buffer,
            pltpu.VMEM(flat_shape.shape, bf16),
            pltpu.VMEM((length, width), bf16),
            pltpu.VMEM(kept_shape.shape, bf16),
            *[pltpu.VMEM((col_parts, length, length), bf16)] * 2,
            head_sems,
            pltpu.SemaphoreType.DMA((3,)),
        ],
        time=1,
        in_specs=[smem] + [vmem] * (3 + team) + anywhere * (3 + len(attn_w)),
        after=(result,),
    )
    head_grads, context_grads = rest[:3], rest[3:]
    context_grads = team_send(context_grads)
    head_stacks = call(
        functools.partial(head_grads_kernel, col_parts, row_parts),
        (place, low_grad, attended, normed_t, context_t, *head_grads),
        head_stacks,
        scratch=[head_buffer, head_sems],
        time=1,
        in_specs=[smem] + [vmem] * 7,
        out_specs=anywhere * 4,
    )
    down_first = first_messages(hidden_grads[4:])
    g_steps, adjoint_ends, adjoint_total, adjoint_done = call(
        functools.partial(adjoint_kernel, team),
        (logr, *context_grads),
        (
            shaped((tiles, length, LANES), f32),
            shaped((2, states, SUBS, channels), f32),
            shaped((2, states, channels), f32),
        ),
        scratch=[pltpu.VMEM((length, LANES), f32)],
        time=1,
        after=(*down_first, head_stacks[0]),
        token=True,
    )
    adjoint_totals = everywhere(adjoint_total.astype(bf16), ("sh", "mq"))
    down_second = second_messages(hidden_grads[4:], down_first, adjoint_done)
    down_second = hold(down_second, (adjoint_totals,))
    up_stacks = list(hidden_grads[:4])
    up_stacks[1::2] = hold(up_stacks[1::2], (adjoint_totals,))
    up_first = first_messages(up_stacks)
    *one_pieces, grad_ssm = call(
        functools.partial(context_back_kernel, team),
        (place, g_steps, u_steps, adjoint_ends, adjoint_totals, logr, coef, one_part),
        (
            *[shaped((own_rows, width), bf16)] * team,
            shaped((2, states, channels), f32),
        ),
        scratch=[
            pltpu.VMEM((tiles, length, LANES), f32),
            pltpu.VMEM((length, width), f32),
            pltpu.VMEM((length, LANES), f32),
        ],
        in_specs=[smem] + [vmem] * 7,
        time=1,
        after=(*down_second, *up_stacks[1::2]),
    )
    one_pieces = team_send(one_pieces)
    down_parts = halve_both(hidden_grads[4:], down_first, down_second)
    grad_rows, gain_one_grad, rows_done = call(
        functools.partial(input_grad_kernel, team),
        (place, x, gain_one, middle_grad, *one_pieces),
        (shaped((own_rows, width), bf16), shaped((1, width), f32)),
        in_specs=[smem] + [vmem] * (3 + team),
        time=1,
        after=(layer_pieces, *[parts[-1] for parts in down_parts]),
        token=True,
    )
    down_sums = [add(*parts, zero=rows_done) for parts in down_parts]
    up_second = second_messages(up_stacks, up_first, rows_done)
    up_sums = [add(*parts) for parts in halve_both(up_stacks, up_first, up_second)]
    head_stacks = list(head_stacks)
    head_stacks[1::2] = hold(head_stacks[1::2], (grad_rows,))
    head_first = first_messages(head_stacks)
    head_second = second_messages(head_stacks, head_first, rows_done)
    down_sums = hold(down_sums, head_second)
    up_sums = hold(up_sums, head_second)
    grad_down = sum_over_z(*down_sums)
    grad_up = sum_over_z(*up_sums)
    head_sums = [add(*parts) for parts in halve_both(head_stacks, head_first, head_second)]
    grad_heads = sum_over_z(*head_sums)
    input_grad = share_rows(lax.all_gather(grad_rows, MODEL, axis=0, tiled=False), f32)

    placed_ssm = lax.dynamic_update_slice_in_dim(
        jnp.zeros((2 * states, width), f32),
        grad_ssm.reshape(2 * states, channels),
        rank * channels,
        1,
    )
    small_grads = jnp.concatenate([placed_ssm, gain_one_grad, gain_two_grad], 0)
    (small_grads,) = hold((small_grads,), head_sums)
    small_grads = small_grads.reshape(2 * states + 2, lax.axis_size(ALL), -1)
    small_grads = lax.all_to_all(jnp.transpose(small_grads, (1, 0, 2)), ALL, 0, 0, tiled=True)
    small_grads = jnp.sum(small_grads, axis=0)

    def moments(matrices, grads, arrays, after=()):
        changed = [shaped(old.shape, f32) for group in arrays for old in group]
        grad_parts = [part for grad in grads for part in both_halves(grad)]
        ins = [item for group in arrays for item in group]
        *found, sums = call(
            functools.partial(moments_kernel, halves, matrices),
            (place, *grad_parts, *ins),
            (*changed, shaped((2, LANES), f32)),
            in_specs=[smem] + [vmem] * (len(grad_parts) + len(ins)),
            after=after,
            time=4,
        )
        return [found[3 * i : 3 * i + 3] for i in range(len(arrays))], sums

    hidden_new, hidden_sums = moments(
        ((4, 0, 0, False, None), (5, 1, 0, True, None)),
        (grad_up, grad_down),
        ((w_up, first_up, second_up), (w_down, first_down, second_down)),
    )
    heads_new, head_sums = moments(
        tuple((i, 0, i, False, i) for i in range(3)) + ((3, 0, 3, True, None),),
        (grad_heads,),
        ((w_qkv, first_qkv, second_qkv), (w_out, first_out, second_out)),
        (layer_out, input_grad),
    )
    own_channels = norm_gains.shape[1]
    ssm_items = [item.reshape(2 * states, own_channels) for item in (ssm_param, first_ssm, second_ssm)]
    small_items = [norm_gains, first_gain, second_gain, *ssm_items]
    *small_new, small_sums = call(
        functools.partial(small_moments_kernel, (6, 8)),
        (small_grads.reshape(2 * states + 2, own_channels), *small_items),
        (*[shaped(item.shape, f32) for item in small_items], shaped((2, LANES), f32)),
    )
    all_sums = everywhere(hidden_sums + head_sums + small_sums, ALL)
    masters = (w_qkv, w_out, w_up, w_down, norm_gains, ssm_items[0])
    news = (*heads_new, *hidden_new, small_new[:3], small_new[3:])
    *weights, norms = call(
        functools.partial(update_kernel, ((0, 1, 2), (3,), (4,), (5,), (6, 7), (8, 9))),
        (all_sums, *masters, *[group[2] for group in news]),
        (*[shaped(item.shape, f32) for item in masters], shaped((2, LANES), f32)),
        time=3.2,
    )
    outputs = [layer_out, input_grad]
    for index, (weight, (first_new, second_new, unused)) in enumerate(zip(weights, news)):
        if index == 4:
            outputs += [weight, first_new, second_new[0], second_new[1]]
        else:
            kept_shape = ssm_param.shape if index == 5 else weight.shape
            outputs += [item.reshape(kept_shape) for item in (weight, first_new, second_new)]
    outputs.append(norms[:, :10])
    return tuple(outputs)


def solution(mesh):
    seq_count, model_count = mesh.shape["seq"], mesh.shape["mp"]
    halves = 2 if HEADS // model_count >= 2 else 1
    sizes = (seq_count // halves, halves, SEQS, halves, model_count // (SEQS * halves))
    fine = Mesh(mesh.devices.reshape(sizes), ALL)
    seq, model = ("sh", "sl"), ("mb", "mq", "ml")
    rows_cols, cols_rows = P(seq, model), P(model, seq)
    token = P(None, seq, None)
    stack = P(None, seq, model)
    gains = P(None, ALL)
    ssm = P(None, None, ALL)
    return jax.shard_map(
        on_device,
        mesh=fine,
        in_specs=(token, token, stack, cols_rows, rows_cols, cols_rows, gains, ssm)
        + (stack,) * 2
        + (cols_rows,) * 2
        + (rows_cols,) * 2
        + (cols_rows,) * 2
        + (gains,) * 2
        + (ssm,) * 2,
        out_specs=(token, token)
        + (stack,) * 3
        + (cols_rows,) * 3
        + (rows_cols,) * 3
        + (cols_rows,) * 3
        + (gains, gains, P(ALL), P(ALL))
        + (ssm,) * 3
        + (P(),),
        check_vma=False,
    )
```
